32 devices in a mesh: dp: 8 (over y, x, core), head: 4 (over z).
Axes of the slice: x: 2, y: 2, z: 4, core: 2. Of those that a mesh axis runs over, the one named last changes fastest.
Arguments:
- hidden_in: bfloat16 [32, 512, 768], P('dp', 'head'), may hold values from -6 to 6
- cotangent: bfloat16 [32, 512, 768], P('dp', 'head'), may hold values from -6 to 6
- box_coords: int32 [32, 512, 4], P('dp'), may hold values from 0 to 1023
- doc_lengths: int32 [32, 4], P('dp'), may hold values from 1 to 509, as said below
- params: float32 [7700480], P(('dp', 'head')), may hold values from -3 to 3
- moment_one: float32 [7700480], P(('dp', 'head')), may hold values from -60 to 60
- moment_two: float32 [7700480], P(('dp', 'head')), may hold values from 1 to 10000
Outputs:
- output: bfloat16 [32, 512, 768], P('dp', 'head')
- grad_hidden: bfloat16 [32, 512, 768], P('dp', 'head')
- grad_params: float32 [7700480], P(('dp', 'head'))
- param_step: float32 [7700480], P(('dp', 'head'))
- new_moment_one: float32 [7700480], P(('dp', 'head'))
The draws below stay inside these ranges and needn't reach their ends.
Inputs may be any that keep to these rules, and one draw needn't show every extreme that they name: `doc_lengths`: each row holds the lengths of the 4 documents of one window, summing to 512; the second document starts within the first quarter of the window and ends within its last quarter.
All inputs are finite; a program needn't handle non-finite values.
Results may differ from the reference program's by a relative error of at most 0.019.
Values may be sent and summed in bfloat16 or wider, within the bound.
A program may use at most 192 MiB of HBM per device.

```python
import math
import jax
import jax.numpy as jnp
from jax import lax

D = 768
HEADS = 12
FF = 3072
BUCKETS = 32
WINLEN = 512
WINDOWS = 32
HEAD_DIM = 64
NPARAM = 7700480


def draw_doc_lengths(key, part):
    key = jax.random.fold_in(key, 5)
    sub_keys = jax.random.split(key, 4)
    quarter = WINLEN // 4
    lead_len = jax.random.randint(sub_keys[0], (WINDOWS,), 1, quarter)
    long_ends = jax.random.randint(sub_keys[1], (WINDOWS,), 3 * quarter + 1, WINLEN - 1)
    chosen = jax.random.randint(sub_keys[2], (), 0, WINDOWS)
    row_ids = jnp.arange(WINDOWS, dtype=jnp.int32)
    lead_len = jnp.where(row_ids == chosen, 1, lead_len)
    long_ends = jnp.where(row_ids == chosen, WINLEN - 2, long_ends)
    rest_len = WINLEN - long_ends
    third_len = jax.random.randint(sub_keys[3], (WINDOWS,), 1, rest_len)
    return jnp.stack([lead_len, long_ends - lead_len, third_len, rest_len - third_len], axis=1).astype(jnp.int32)


def draw_params(key, part):
    key = jax.random.fold_in(key, 9)
    noise_draw = jnp.clip(jax.random.normal(key, (NPARAM,), jnp.float32), -4.0, 4.0)
    flat_index = jnp.arange(NPARAM, dtype=jnp.int32)
    segments = ((3 * D * D, D ** (-0.5)), (D * D, 8.0 * D ** (-0.5)), (D * D, D ** (-0.5)), (D * FF, D ** (-0.5)), (FF * D, 2.0 * FF ** (-0.5)), (2 * D, 0.5), (D, 0.3), (D, -1.0), (D, 0.3), (FF, 0.5), (D, 0.3), (D, -1.0), (D, 0.3), (3 * HEADS * BUCKETS, 0.7))
    scale_map = jnp.full((NPARAM,), 0.1, jnp.float32)
    gain_mask = flat_index < 0
    offset = 0
    for seg_size, factor in segments:
        inside = (flat_index >= offset) & (flat_index < offset + seg_size)
        if factor < 0:
            gain_mask = gain_mask | inside
        else:
            scale_map = jnp.where(inside, factor, scale_map)
        offset += seg_size
    drawn = jnp.where(gain_mask, 1.0 + 0.2 * noise_draw, scale_map * noise_draw)
    return jnp.clip(drawn, -3.0, 3.0)


def place_ends(values, stream_key, least, top_value):
    index_at = [jax.random.randint(jax.random.fold_in(stream_key, axis), (), 0, length) for axis, length in enumerate(values.shape)]
    main_axis = values.shape.index(max(values.shape))
    beside = index_at[:main_axis] + [(index_at[main_axis] + 1) % values.shape[main_axis]] + index_at[main_axis + 1:]
    return values.at[tuple(index_at)].set(least).at[tuple(beside)].set(top_value)


def block_levels(rng, shape, cuts, smallest, high):
    def one(axis_at, shards_of):
        draws = jax.random.uniform(jax.random.fold_in(jax.random.fold_in(rng, 6), axis_at), (shards_of,), jnp.float32, smallest / len(cuts), high / len(cuts))
        return jnp.repeat(jnp.exp(draws), shape[axis_at] // shards_of).reshape((-1,) + (1,) * (len(shape) - axis_at - 1))

    loudness = one(*cuts[0])
    for cut in cuts[1:]:
        loudness = loudness * one(*cut)
    return loudness


def bell_draw(stream_key, extent, width, limit, cuts=(), kind=jnp.bfloat16):
    result = width * jax.random.normal(stream_key, extent, jnp.float32)
    if cuts:
        result = result * block_levels(stream_key, extent, cuts, -0.22, 0.18)
    return jnp.clip(result, -limit, limit).astype(kind)


def setup_inputs(seed: int = 0) -> dict:
    key_list = jax.random.split(jax.random.key(seed), 8)
    return {
        "hidden_in": bell_draw(key_list[0], (WINDOWS, WINLEN, D), 1.0, 6.0, ((0, 8), (1, 4))),
        "cotangent": bell_draw(key_list[1], (WINDOWS, WINLEN, D), 1.0, 6.0, ((0, 8), (1, 4))),
        "box_coords": place_ends(jax.random.randint(key_list[2], (WINDOWS, WINLEN, 4), 0, 1024), jax.random.fold_in(key_list[2], 1), 0, 1023).astype(jnp.int32),
        "doc_lengths": draw_doc_lengths(jax.random.fold_in(key_list[7], 71), 0),
        "params": draw_params(jax.random.fold_in(key_list[7], 71), 0),
        "moment_one": bell_draw(key_list[5], (NPARAM,), 10.0, 60.0, ((0, 32),), jnp.float32),
        "moment_two": jnp.clip(jnp.exp(math.log(10000.0) - 9.2103404 * jax.random.uniform(key_list[6], (NPARAM,), jnp.float32) ** block_levels(key_list[6], (NPARAM,), ((0, 32),), -0.2, 0.2)), 1.0, 10000.0),
    }


beta_one = 0.9
beta_two = 0.999
adam_eps = 1e-08
norm_eps = 1e-05
base_rate = 0.001
layer_decay = 0.75
decay_weight = 0.01
adam_count = 100
coord_cell = 32
masked_score = -1e+30

@jax.custom_vjp
def low(v):
    return lax.optimization_barrier(v.astype(jnp.bfloat16)).astype(jnp.float32)

@jax.custom_vjp
def low_back(v):
    return v

def low_keep(v):
    return (low(v), None)

def low_pass(kept, grad):
    return (grad,)

def back_keep(v):
    return (v, None)

def back_low(kept, grad):
    return (low(grad),)
low.defvjp(low_keep, low_pass)
low_back.defvjp(back_keep, back_low)

def unpack(flat_params):
    layouts = ((D, 3 * D), (D, D), (D, D), (D, FF), (FF, D), (2, D), (D,), (2, D), (FF,), (D,), (2, D), (3, HEADS, BUCKETS))
    pieces = []
    offset = 0
    for layout in layouts:
        elements = math.prod(layout)
        pieces.append(flat_params[offset:offset + elements].reshape(layout))
        offset += elements
    return pieces

def matmul(left_mat, right_mat):
    return jnp.dot(left_mat, right_mat, precision=lax.Precision.HIGHEST, preferred_element_type=jnp.float32)

def layer_norm(values, gain_bias):
    row_mean = lax.optimization_barrier(jnp.mean(values, axis=-1, keepdims=True))
    centred = values - row_mean
    spread = lax.optimization_barrier(jnp.mean(centred * centred, axis=-1, keepdims=True))
    return centred * lax.rsqrt(spread + norm_eps) * gain_bias[0] + gain_bias[1]

def window_layout(doc_lengths, box_coords):
    doc_ends = jnp.cumsum(doc_lengths, dtype=jnp.int32)
    doc_starts = doc_ends - doc_lengths
    places = jnp.arange(WINLEN, dtype=jnp.int32)
    doc_ids = lax.optimization_barrier(jnp.sum((places[:, None] >= doc_ends[None, :]).astype(jnp.int32), axis=1, dtype=jnp.int32))
    chosen = doc_ids[:, None] == jnp.arange(doc_lengths.shape[0], dtype=jnp.int32)[None, :]
    firsts = lax.optimization_barrier(jnp.sum(jnp.where(chosen, doc_starts[None, :], 0), axis=1, dtype=jnp.int32))
    anchor = jnp.take(box_coords, firsts, axis=0)
    relative = box_coords - jnp.concatenate([anchor[:, :2], anchor[:, :2]], axis=1)
    centre_x = (box_coords[:, 0] + box_coords[:, 2]) // 2
    centre_y = (box_coords[:, 1] + box_coords[:, 3]) // 2
    return (doc_ids, relative, centre_x, centre_y)

def box_features(relative):
    count_freq = D // 8
    steps = jnp.arange(count_freq, dtype=jnp.float32)
    frequency = jnp.exp(steps * (-math.log(1000.0) / count_freq))
    angles = relative.astype(jnp.float32)[:, :, None] * frequency[None, None, :]
    return jnp.concatenate([jnp.sin(angles), jnp.cos(angles)], axis=2).reshape(relative.shape[0], D)

def attend_window(tables, window):
    queries, keys_in, values, doc_ids, centre_x, centre_y = window
    query_heads = queries.reshape(WINLEN, HEADS, HEAD_DIM)
    key_heads = keys_in.reshape(WINLEN, HEADS, HEAD_DIM)
    value_heads = values.reshape(WINLEN, HEADS, HEAD_DIM)
    scores = jnp.einsum('ihd,jhd->ihj', query_heads, key_heads, precision=lax.Precision.HIGHEST) * HEAD_DIM ** (-0.5)
    half_span = BUCKETS // 2
    places = jnp.arange(WINLEN, dtype=jnp.int32)
    along_seq = jnp.clip(places[:, None] - places[None, :], -half_span, half_span - 1) + half_span
    across_x = jnp.clip((centre_x[:, None] - centre_x[None, :]) // coord_cell, -half_span, half_span - 1) + half_span
    across_y = jnp.clip((centre_y[:, None] - centre_y[None, :]) // coord_cell, -half_span, half_span - 1) + half_span
    bias_all = tables[0][:, along_seq] + tables[1][:, across_x] + tables[2][:, across_y]
    scores = low_back(scores + bias_all.transpose(1, 0, 2))
    same_doc = doc_ids[:, None, None] == doc_ids[None, None, :]
    scores = jnp.where(same_doc, scores, masked_score)
    row_max = lax.optimization_barrier(jnp.max(scores, axis=2, keepdims=True))
    weights = jnp.exp(scores - row_max)
    attn_probs = weights / lax.optimization_barrier(jnp.sum(weights, axis=2, keepdims=True))
    context = jnp.einsum('ihj,jhd->ihd', low(attn_probs), value_heads, precision=lax.Precision.HIGHEST)
    return context.reshape(WINLEN, D)

def layer_forward(flat_params, hidden, features, doc_ids, centre_x, centre_y):
    pieces = unpack(low(flat_params))
    proj_qkv, proj_out, proj_box, proj_in, proj_back = pieces[:5]
    qv_bias, out_bias, norm_one, in_bias, back_bias, norm_two, tables = pieces[5:]
    start = hidden + low_back(matmul(low(features), proj_box))
    start_low = low(start)
    queries = low(low_back(matmul(start_low, proj_qkv[:, :D]) + qv_bias[0]))
    keys_in = low(low_back(matmul(start_low, proj_qkv[:, D:2 * D])))
    values = low(low_back(matmul(start_low, proj_qkv[:, 2 * D:]) + qv_bias[1]))
    win_shape = (-1, WINLEN, D)

    def one_window(window):
        return attend_window(tables, window)
    context = lax.map(jax.checkpoint(one_window), (queries.reshape(win_shape), keys_in.reshape(win_shape), values.reshape(win_shape), doc_ids, centre_x, centre_y))
    context = low(low_back(context.reshape(-1, D)))
    attn_out = low_back(matmul(context, proj_out) + out_bias)
    normed = layer_norm(start + attn_out, norm_one)
    inner_act = low_back(matmul(low(normed), proj_in) + in_bias)
    active = low(jax.nn.gelu(inner_act, approximate=False))
    branch = low_back(matmul(active, proj_back) + back_bias)
    return layer_norm(normed + branch, norm_two)

def adam_step(params, moment_one, moment_two, grads, flat_index):
    box_part = (flat_index >= 4 * D * D) & (flat_index < 5 * D * D)
    step_rate = jnp.where(box_part, base_rate * layer_decay ** 12, base_rate * layer_decay)
    decay_mask = jnp.where(flat_index < 5 * D * D + 2 * D * FF, decay_weight, 0.0)
    moment_one = beta_one * moment_one + (1.0 - beta_one) * grads
    moment_two = beta_two * moment_two + (1.0 - beta_two) * grads * grads
    first_hat = moment_one / (1.0 - beta_one ** adam_count)
    second_hat = moment_two / (1.0 - beta_two ** adam_count)
    update = first_hat / (jnp.sqrt(second_hat) + adam_eps) + decay_mask * params
    return (-step_rate * update, moment_one)

def reference(hidden_in, cotangent, box_coords, doc_lengths, params, moment_one, moment_two):
    windows = doc_lengths.shape[0]
    blocks = windows // 8
    doc_ids, relative, centre_x, centre_y = jax.vmap(window_layout)(doc_lengths, box_coords)

    def one_block(running, block_inputs):
        hidden_b, cot_b, relative_b, ids_b, x_b, y_b = block_inputs
        features = box_features(relative_b.reshape(-1, 4))

        def forward(flat_params, hidden):
            return layer_forward(flat_params, hidden, features, ids_b, x_b, y_b)
        output, backward = jax.vjp(forward, params, hidden_b.reshape(-1, D).astype(jnp.float32))
        grad_flat, grad_hidden = backward(cot_b.reshape(-1, D).astype(jnp.float32))
        return (running + grad_flat, (output.astype(jnp.bfloat16), grad_hidden.astype(jnp.bfloat16)))
    block_inputs = (hidden_in.reshape(blocks, 8, WINLEN, D), cotangent.reshape(blocks, 8, WINLEN, D), relative.reshape(blocks, 8, WINLEN, 4), doc_ids.reshape(blocks, 8, WINLEN), centre_x.reshape(blocks, 8, WINLEN), centre_y.reshape(blocks, 8, WINLEN))
    grad_params, (outputs, grads_hidden) = lax.scan(one_block, jnp.zeros_like(params), block_inputs)
    param_step, new_one = adam_step(params, moment_one, moment_two, grad_params, jnp.arange(params.shape[0], dtype=jnp.int32))
    return (outputs.reshape(windows, WINLEN, D), grads_hidden.reshape(windows, WINLEN, D), grad_params, param_step, new_one)
```

```python
import functools
import math

import jax
import jax.numpy as jnp
import numpy as np
from jax import lax
from jax.experimental import pallas as pl
from jax.experimental.pallas import tpu as pltpu
from jax.sharding import PartitionSpec as P

D = 768
HEADS = 12
FF = 3072
BUCKETS = 32
WINLEN = 512
HEAD_DIM = 64
PAIRS = HEADS // 2
LANES = 128
BLOCKS = WINLEN // LANES

beta_one = 0.9
beta_two = 0.999
adam_eps = 1e-08
norm_eps = 1e-05
base_rate = 0.001
layer_decay = 0.75
decay_weight = 0.01
adam_count = 100
coord_cell = 32
masked_score = -1e30

F32 = jnp.float32
BF16 = jnp.bfloat16


def layouts_list():
    return (
        (D, 3 * D),
        (D, D),
        (D, D),
        (D, FF),
        (FF, D),
        (2, D),
        (D,),
        (2, D),
        (FF,),
        (D,),
        (2, D),
        (3, HEADS, BUCKETS),
    )


def unpack(flat_params):
    pieces = []
    offset = 0
    for layout in layouts_list():
        elements = math.prod(layout)
        pieces.append(flat_params[offset : offset + elements].reshape(layout))
        offset += elements
    return pieces


def matmul(left_mat, right_mat):
    return jnp.dot(left_mat, right_mat, preferred_element_type=F32)


def rows_inner(left_mat, right_mat):
    return lax.dot_general(left_mat, right_mat, (((0,), (0,)), ((), ())), preferred_element_type=F32)


def times_transposed(left_mat, right_mat):
    return lax.dot_general(left_mat, right_mat, (((1,), (1,)), ((), ())), preferred_element_type=F32)


def layer_norm(values, gain_bias):
    row_mean = jnp.mean(values, axis=-1, keepdims=True)
    centred = values - row_mean
    spread = jnp.mean(centred * centred, axis=-1, keepdims=True)
    return centred * lax.rsqrt(spread + norm_eps) * gain_bias[0] + gain_bias[1]


def gelu_exact(values):
    return jax.nn.gelu(values, approximate=False)


def hot(index, count):
    return (np.asarray(index)[..., None] == np.arange(count)).astype(np.float32)


def clipped(steps):
    return np.clip(steps, -(BUCKETS // 2), BUCKETS // 2 - 1) + BUCKETS // 2


CELLS = np.arange(BUCKETS)
HOT_SAME = hot(clipped(CELLS[:, None] - CELLS[None, :]), BUCKETS)
HOT_LESS = hot(clipped(CELLS[:, None] - CELLS[None, :] - 1), BUCKETS)
WIDE = 6 * LANES
_U = np.arange(WIDE)
BAND_HOT = hot(np.where(_U < 5 * LANES, clipped(_U - 2 * LANES), 0), BUCKETS)
_V = np.arange(4 * LANES)
DIAG_HOT = np.concatenate(
    [
        hot(np.zeros(LANES, np.int64), BUCKETS),
        hot(np.where(_V < 3 * LANES, clipped(_V - LANES), 0), BUCKETS),
        hot(np.full(LANES, BUCKETS - 1), BUCKETS),
    ]
)


def window_layout(doc_lengths, box_coords):
    doc_ends = jnp.cumsum(doc_lengths, dtype=jnp.int32)
    doc_starts = doc_ends - doc_lengths
    places = jnp.arange(WINLEN, dtype=jnp.int32)
    doc_ids = jnp.sum(
        (places[:, None] >= doc_ends[None, :]).astype(jnp.int32), axis=1, dtype=jnp.int32
    )
    docs = jnp.arange(doc_lengths.shape[0], dtype=jnp.int32)
    chosen = doc_ids[:, None] == docs[None, :]
    first_hot = places[:, None] == doc_starts[None, :]
    first_box = jnp.sum(
        jnp.where(first_hot[:, :, None], box_coords[:, None, :], 0), axis=0, dtype=jnp.int32
    )
    anchor = jnp.sum(
        jnp.where(chosen[:, :, None], first_box[None, :, :], 0), axis=1, dtype=jnp.int32
    )
    relative = box_coords - jnp.concatenate([anchor[:, :2], anchor[:, :2]], axis=1)
    centre_x = (box_coords[:, 0] + box_coords[:, 2]) // 2
    centre_y = (box_coords[:, 1] + box_coords[:, 3]) // 2
    return chosen, relative, centre_x, centre_y


def box_features(relative):
    count_freq = D // 8
    steps = jnp.arange(count_freq, dtype=F32)
    frequency = jnp.exp(steps * (-math.log(1000.0) / count_freq))
    angles = relative.astype(F32)[:, :, None] * frequency[None, None, :]
    return jnp.concatenate([jnp.sin(angles), jnp.cos(angles)], axis=2).reshape(relative.shape[0], D)


def bias_operands(tables, chosen, centre_x, centre_y):
    cell_x, cell_y = centre_x // coord_cell, centre_y // coord_cell
    rest_x, rest_y = centre_x % coord_cell, centre_y % coord_cell
    cells = jnp.arange(BUCKETS, dtype=jnp.int32)
    hot_x = (cell_x[:, None] == cells[None, :]).astype(BF16)
    hot_y = (cell_y[:, None] == cells[None, :]).astype(BF16)
    none = jnp.zeros_like(hot_x)
    hot_two = jnp.concatenate([hot_x, hot_y, hot_x, hot_y], axis=1)
    key_x = jnp.stack(
        [
            jnp.concatenate([hot_x, -hot_x, none, none], axis=1),
            jnp.concatenate([none, none, hot_x, -hot_x], axis=1),
        ]
    )
    key_y = jnp.stack(
        [
            jnp.concatenate([hot_y, -hot_y, none, none], axis=1),
            jnp.concatenate([none, none, hot_y, -hot_y], axis=1),
        ]
    )
    same = jnp.einsum("qcb,thb->thqc", HOT_SAME.astype(BF16), tables[1:], preferred_element_type=F32)
    less = jnp.einsum("qcb,thb->thqc", HOT_LESS.astype(BF16), tables[1:], preferred_element_type=F32)
    zero = jnp.zeros_like(same[0])
    base = jnp.concatenate(
        [jnp.concatenate([same[0], zero], axis=2), jnp.concatenate([zero, same[1]], axis=2)], axis=1
    )
    base = base.reshape(PAIRS, 2, 64, 64)[:, ::-1].reshape(HEADS, 64, 64)
    diff_x = jnp.concatenate([jnp.concatenate([less[0], same[0]], axis=2), jnp.zeros((HEADS, 32, 64), F32)], axis=1)
    diff_y = jnp.concatenate([jnp.zeros((HEADS, 32, 64), F32), jnp.concatenate([less[1], same[1]], axis=2)], axis=1)
    rows = jnp.concatenate([base, diff_x, diff_y], axis=0).astype(BF16)
    rows = rows.transpose(1, 0, 2).reshape(64, 3 * D)
    met = matmul(hot_two[:, :64], rows).astype(BF16)
    band = matmul(tables[0], jnp.asarray(BAND_HOT.T, BF16)).reshape(HEADS, 1, WIDE)
    rest_cols = jnp.stack([rest_x, rest_y], axis=1).astype(F32)
    rest_rows = rest_cols.T
    pad = jnp.zeros((WINLEN, LANES - chosen.shape[1]), BF16)
    marks = chosen.astype(BF16)
    mark_keys = jnp.concatenate([marks, pad], axis=1)
    mark_queries = jnp.concatenate([(1 - marks) * jnp.asarray(masked_score, BF16), pad], axis=1)
    return dict(
        hot_two=hot_two,
        key_x=key_x,
        key_y=key_y,
        met=met,
        band=band,
        rest_cols=rest_cols,
        rest_rows=rest_rows,
        mark_keys=mark_keys,
        mark_queries=mark_queries,
    )


def half_masks():
    lane = lax.broadcasted_iota(jnp.int32, (1, LANES), 1)
    low = (lane < HEAD_DIM).astype(F32)
    return low.astype(BF16), (1.0 - low).astype(BF16)


def less_masks(rest_cols, rest_rows, less_x, less_y):
    for part in range(BLOCKS):
        rows = slice(part * LANES, (part + 1) * LANES)
        for axis, less in ((0, less_x), (1, less_y)):
            column = rest_cols[rows, axis : axis + 1]
            row = rest_rows[axis : axis + 1, :]
            less[rows, :] = jnp.where(row < column, 1.0, 0.0).astype(less.dtype)


def attention_forward_kernel(
    q_ref, k_ref, v_ref, hot_ref, keyx_ref, keyy_ref, met_ref, band_ref, cols_ref, rows_ref,
    mkey_ref, mquery_ref, probs_ref, context_ref,
    kaug, qaug, less_x, less_y, wide, scores,
):
    low, high = half_masks()
    less_masks(cols_ref, rows_ref, less_x, less_y)
    kaug[:, LANES:] = mkey_ref[...]
    qaug[:, LANES:] = mquery_ref[...]
    half = 2 * LANES

    def one_pair(pair, carry):
        at = pl.multiple_of(pair * LANES, LANES)
        lanes = pl.ds(at, LANES)
        lanes_x = pl.ds(pl.multiple_of(at + D, LANES), LANES)
        lanes_y = pl.ds(pl.multiple_of(at + 2 * D, LANES), LANES)
        values_t = v_ref[:, lanes].T
        for odd in range(2):
            own, other = (low, high) if odd == 0 else (high, low)
            head = 2 * pair + odd
            kaug[:, :LANES] = k_ref[:, lanes] * own + hot_ref[...] * other
            qaug[:, :LANES] = q_ref[:, lanes] * own + met_ref[:, lanes] * other
            skew_band(band_ref[head], wide)
            for side in range(2):
                cols = slice(side * half, (side + 1) * half)
                top = None
                for part in range(BLOCKS):
                    rows = slice(part * LANES, (part + 1) * LANES)
                    s = times_transposed(kaug[rows, :], qaug[cols, :])
                    dx = times_transposed(keyx_ref[odd, rows, :], met_ref[cols, lanes_x])
                    dy = times_transposed(keyy_ref[odd, rows, :], met_ref[cols, lanes_y])
                    bias = []
                    for block in range(2 * side, 2 * side + 2):
                        step = max(-2, min(2, block - part)) + 2
                        bias.append(wide[:, step * LANES : (step + 1) * LANES])
                    s = s + jnp.concatenate(bias, axis=1)
                    s = s + dx * less_x[rows, cols] + dy * less_y[rows, cols]
                    scores[rows, :] = s
                    best = jnp.max(s, axis=0, keepdims=True)
                    top = best if top is None else jnp.maximum(top, best)
                total = None
                for part in range(BLOCKS):
                    rows = slice(part * LANES, (part + 1) * LANES)
                    e = jnp.exp(scores[rows, :] - top)
                    scores[rows, :] = e
                    add = jnp.sum(e, axis=0, keepdims=True)
                    total = add if total is None else total + add
                share = 1.0 / total
                for part in range(BLOCKS):
                    rows = slice(part * LANES, (part + 1) * LANES)
                    probs_ref[head, rows, cols] = (scores[rows, :] * share).astype(BF16)
                got = matmul(
                    values_t[odd * HEAD_DIM : (odd + 1) * HEAD_DIM, :], probs_ref[head, :, cols]
                )
                context_ref[pl.ds(pl.multiple_of(head * HEAD_DIM, HEAD_DIM), HEAD_DIM), cols] = (
                    got.astype(BF16)
                )
        return carry

    lax.fori_loop(0, PAIRS, one_pair, 0)


def skew_band(row, wide):
    x = jnp.broadcast_to(row, (8, WIDE))
    sub = lax.broadcasted_iota(jnp.int32, (8, WIDE), 0)
    for bit in (1, 2, 4):
        x = jnp.where((sub & bit) != 0, pltpu.roll(x, bit, 1), x)
    for group in range(LANES // 8):
        y = x if group == 0 else pltpu.roll(x, 8 * group, 1)
        wide[8 * group : 8 * group + 8, :] = y[:, : 5 * LANES]


def diagonal_sums(parts):
    total = None
    for group in range(LANES // 8):
        x = jnp.concatenate(
            [parts[8 * group : 8 * group + 8, LANES : 4 * LANES], jnp.zeros((8, LANES), F32)], axis=1
        )
        y = x if group == 0 else pltpu.roll(x, 4 * LANES - 8 * group, 1)
        total = y if total is None else total + y
    sub = lax.broadcasted_iota(jnp.int32, (8, 4 * LANES), 0)
    for bit in (1, 2, 4):
        total = jnp.where((sub & bit) != 0, pltpu.roll(total, 4 * LANES - bit, 1), total)
    return jnp.sum(total, axis=0, keepdims=True)


def attention_backward_kernel(
    q_ref, k_ref, v_ref, dctx_ref, probs_ref, hot_ref, cols_ref, rows_ref,
    dq_ref, dk_ref, dv_ref, cells_ref, diag_ref,
    qaug, less_x, less_y, scores, dscores, band, kept, hot_t,
):
    low, high = half_masks()
    less_masks(cols_ref, rows_ref, less_x, less_y)
    hot_t[...] = hot_ref[...].T
    lane = lax.broadcasted_iota(jnp.int32, (1, LANES), 1)
    scale = HEAD_DIM ** (-0.5)
    of_x = jnp.where((lane // BUCKETS) % 2 == 0, 1.0, 0.0)
    cells_x = hot_ref[...] * of_x.astype(BF16)
    cells_y = hot_ref[...] * (1.0 - of_x).astype(BF16)

    def one_pair(pair, carry):
        at = pl.multiple_of(pair * LANES, LANES)
        lanes = pl.ds(at, LANES)
        keys_t = k_ref[:, lanes].T
        for odd in range(2):
            own, other = (low, high) if odd == 0 else (high, low)
            head = 2 * pair + odd
            qaug[...] = q_ref[:, lanes] * own + hot_ref[...] * other
            dctx = dctx_ref[:, lanes]
            dot = None
            for part in range(BLOCKS):
                rows = slice(part * LANES, (part + 1) * LANES)
                dp = times_transposed(v_ref[rows, lanes] * own, dctx)
                scores[rows, :] = dp
                add = jnp.sum(dp * probs_ref[head, rows, :].astype(F32), axis=0, keepdims=True)
                dot = add if dot is None else dot + add
            band[...] = jnp.zeros_like(band)
            for part in range(BLOCKS):
                rows = slice(part * LANES, (part + 1) * LANES)
                probs = probs_ref[head, rows, :]
                ds = probs.astype(F32) * (scores[rows, :] - dot)
                for block in range(BLOCKS):
                    step = max(-2, min(2, block - part)) + 2
                    where = slice(step * LANES, (step + 1) * LANES)
                    band[:, where] = band[:, where] + ds[:, block * LANES : (block + 1) * LANES]
                ds = ds.astype(BF16)
                dscores[rows, :] = ds
                both = matmul(ds, qaug[...])
                less = matmul(ds * less_x[rows, :], cells_x) + matmul(ds * less_y[rows, :], cells_y)
                dv = matmul(probs, dctx)
                kept[odd, 0, rows, :] = both
                kept[odd, 1, rows, :] = less
                kept[odd, 2, rows, :] = dv
            got = matmul(keys_t[odd * HEAD_DIM : (odd + 1) * HEAD_DIM, :], dscores[...])
            dq_ref[pl.ds(pl.multiple_of(head * HEAD_DIM, HEAD_DIM), HEAD_DIM), :] = (
                got * scale
            ).astype(BF16)
            diag_ref[head, :, LANES : 5 * LANES] = diagonal_sums(band)
            diag_ref[head, :, :LANES] = jnp.sum(band[:, :LANES], axis=0, keepdims=True)
            diag_ref[head, :, 5 * LANES :] = jnp.sum(band[:, 4 * LANES :], axis=0, keepdims=True)
            for which in range(2):
                summed = kept[odd, which]
                first = summed.astype(BF16)
                rest = (summed - first.astype(F32)).astype(BF16)
                cells_ref[head, which] = matmul(hot_t[:64, :], first) + matmul(hot_t[:64, :], rest)
        dk_ref[:, lanes] = jnp.where(lane < HEAD_DIM, kept[0, 0], kept[1, 0]).astype(BF16)
        dv_ref[:, lanes] = jnp.where(lane < HEAD_DIM, kept[0, 2], kept[1, 2]).astype(BF16)
        return carry

    lax.fori_loop(0, PAIRS, one_pair, 0)


def attention_forward(queries, keys, values, ops):
    return pl.pallas_call(
        attention_forward_kernel,
        out_shape=(
            jax.ShapeDtypeStruct((HEADS, WINLEN, WINLEN), BF16),
            jax.ShapeDtypeStruct((D, WINLEN), BF16),
        ),
        scratch_shapes=[
            pltpu.VMEM((WINLEN, 2 * LANES), BF16),
            pltpu.VMEM((WINLEN, 2 * LANES), BF16),
            pltpu.VMEM((WINLEN, WINLEN), F32),
            pltpu.VMEM((WINLEN, WINLEN), F32),
            pltpu.VMEM((LANES, 5 * LANES), F32),
            pltpu.VMEM((WINLEN, 2 * LANES), F32),
        ],
        compiler_params=pltpu.CompilerParams(vmem_limit_bytes=48 * 2**20),
        name="attention_forward",
    )(
        queries, keys, values, ops["hot_two"], ops["key_x"], ops["key_y"], ops["met"], ops["band"],
        ops["rest_cols"], ops["rest_rows"], ops["mark_keys"], ops["mark_queries"],
    )


def attention_backward(queries, keys, values, grad_context, probs, ops):
    return pl.pallas_call(
        attention_backward_kernel,
        out_shape=(
            jax.ShapeDtypeStruct((D, WINLEN), BF16),
            jax.ShapeDtypeStruct((WINLEN, D), BF16),
            jax.ShapeDtypeStruct((WINLEN, D), BF16),
            jax.ShapeDtypeStruct((HEADS, 2, 64, LANES), F32),
            jax.ShapeDtypeStruct((HEADS, 1, WIDE), F32),
        ),
        scratch_shapes=[
            pltpu.VMEM((WINLEN, LANES), BF16),
            pltpu.VMEM((WINLEN, WINLEN), BF16),
            pltpu.VMEM((WINLEN, WINLEN), BF16),
            pltpu.VMEM((WINLEN, WINLEN), F32),
            pltpu.VMEM((WINLEN, WINLEN), BF16),
            pltpu.VMEM((LANES, 5 * LANES), F32),
            pltpu.VMEM((2, 3, WINLEN, LANES), F32),
            pltpu.VMEM((LANES, WINLEN), BF16),
        ],
        compiler_params=pltpu.CompilerParams(vmem_limit_bytes=48 * 2**20),
        name="attention_backward",
    )(
        queries, keys, values, grad_context, probs, ops["hot_two"], ops["rest_cols"],
        ops["rest_rows"],
    )


def table_grads(cells, diag):
    exact = lax.Precision.HIGHEST
    pairs = cells.reshape(PAIRS, 2, 2, 64, LANES)
    every = jnp.stack([pairs[:, 0, 0, :, 64:], pairs[:, 1, 0, :, :64]], axis=1).reshape(HEADS, 64, 64)
    less = cells[:, 1]
    less_x, less_y = less[:, :32, :32], less[:, 32:, 32:64]
    all_x, all_y = every[:, :32, :32], every[:, 32:, 32:]
    same = jnp.stack([all_x - less_x, all_y - less_y]).reshape(2 * HEADS, -1)
    below = jnp.stack([less_x, less_y]).reshape(2 * HEADS, -1)
    same_hot = jnp.asarray(HOT_SAME.transpose(1, 0, 2).reshape(-1, BUCKETS))
    less_hot = jnp.asarray(HOT_LESS.transpose(1, 0, 2).reshape(-1, BUCKETS))
    moved = jnp.dot(same, same_hot, precision=exact) + jnp.dot(below, less_hot, precision=exact)
    along = jnp.dot(diag.reshape(HEADS, WIDE), jnp.asarray(DIAG_HOT), precision=exact)
    return jnp.concatenate([along[None], moved.reshape(2, HEADS, BUCKETS)], axis=0)


def adam_step(params, moment_one, moment_two, grads, flat_index):
    box_part = (flat_index >= 4 * D * D) & (flat_index < 5 * D * D)
    step_rate = jnp.where(box_part, base_rate * layer_decay**12, base_rate * layer_decay)
    decay_mask = jnp.where(flat_index < 5 * D * D + 2 * D * FF, decay_weight, 0.0)
    moment_one = beta_one * moment_one + (1.0 - beta_one) * grads
    moment_two = beta_two * moment_two + (1.0 - beta_two) * grads * grads
    first_hat = moment_one / (1.0 - beta_one**adam_count)
    second_hat = moment_two / (1.0 - beta_two**adam_count)
    update = first_hat / (jnp.sqrt(second_hat) + adam_eps) + decay_mask * params
    return (-step_rate * update, moment_one)


def to_windows(shard):
    return lax.all_to_all(shard, "head", split_axis=0, concat_axis=1, tiled=True)


def to_positions(window):
    return lax.all_to_all(window, "head", split_axis=1, concat_axis=0, tiled=True)


def shards(hidden_in, cotangent, box_coords, doc_lengths, params, moment_one, moment_two):
    head_pos = lax.axis_index("head")
    groups = lax.axis_size("head")
    flat_params = lax.all_gather(params.astype(BF16), ("dp", "head"), axis=0, tiled=True)
    hidden = to_windows(hidden_in).reshape(WINLEN, D)
    cot = to_windows(cotangent).reshape(WINLEN, D)
    own_box = lax.dynamic_index_in_dim(box_coords, head_pos, 0, keepdims=False)
    own_lengths = lax.dynamic_index_in_dim(doc_lengths, head_pos, 0, keepdims=False)
    chosen, relative, centre_x, centre_y = window_layout(own_lengths, own_box)
    features = box_features(relative).astype(BF16)

    pieces = unpack(flat_params)
    proj_qkv, proj_out, proj_box, proj_in, proj_back = pieces[:5]
    qv_bias, out_bias, norm_one, in_bias, back_bias, norm_two, tables = pieces[5:]
    ops = bias_operands(tables, chosen, centre_x, centre_y)
    start_state = hidden.astype(F32) + matmul(features, proj_box)
    start_low = start_state.astype(BF16)
    qv_float = qv_bias.astype(F32)
    mixed = matmul(start_low, proj_qkv)
    queries = (mixed[:, :D] + qv_float[0]).astype(BF16) * jnp.asarray(HEAD_DIM ** (-0.5), BF16)
    keys = mixed[:, D : 2 * D].astype(BF16)
    values = (mixed[:, 2 * D :] + qv_float[1]).astype(BF16)

    probs, context_t = attention_forward(queries, keys, values, ops)
    first_sum = start_state + rows_inner(context_t, proj_out) + out_bias.astype(F32)
    normed, norm_one_back = jax.vjp(layer_norm, first_sum, norm_one.astype(F32))
    normed_low = normed.astype(BF16)
    inner_act = matmul(normed_low, proj_in) + in_bias.astype(F32)
    active, gelu_back = jax.vjp(gelu_exact, inner_act)
    active_low = active.astype(BF16)
    second_sum = normed + matmul(active_low, proj_back) + back_bias.astype(F32)
    output, norm_two_back = jax.vjp(layer_norm, second_sum, norm_two.astype(F32))
    output_low = to_positions(output.astype(BF16).reshape(1, WINLEN, D))

    grad_second, grad_norm_two = norm_two_back(cot.astype(F32))
    grad_branch = grad_second.astype(BF16)
    grad_proj_back = rows_inner(active_low, grad_branch)
    grad_back_bias = jnp.sum(grad_branch.astype(F32), axis=0)
    (grad_inner_f,) = gelu_back(times_transposed(grad_branch, proj_back))
    grad_inner = grad_inner_f.astype(BF16)
    grad_proj_in = rows_inner(normed_low, grad_inner)
    grad_in_bias = jnp.sum(grad_inner.astype(F32), axis=0)
    grad_first, grad_norm_one = norm_one_back(grad_second + times_transposed(grad_inner, proj_in))
    grad_attn = grad_first.astype(BF16)
    grad_proj_out = matmul(context_t, grad_attn)
    grad_out_bias = jnp.sum(grad_attn.astype(F32), axis=0)
    grad_context = times_transposed(grad_attn, proj_out).astype(BF16)
    grad_queries_t, grad_keys, grad_values, cells, diag = attention_backward(
        queries, keys, values, grad_context, probs, ops
    )
    table_grad = table_grads(cells, diag)
    grad_mixed = jnp.concatenate([grad_queries_t.T, grad_keys, grad_values], axis=1)
    grad_proj_qkv = rows_inner(start_low, grad_mixed)
    summed = jnp.sum(grad_mixed.astype(F32), axis=0)
    grad_qv_bias = jnp.stack([summed[:D], summed[2 * D :]])
    grad_start = grad_first + times_transposed(grad_mixed, proj_qkv)
    grad_start_low = grad_start.astype(BF16)
    grad_hidden = to_positions(grad_start_low.reshape(1, WINLEN, D))
    grad_proj_box = rows_inner(features, grad_start_low)
    grad_list = (
        grad_proj_qkv,
        grad_proj_out,
        grad_proj_box,
        grad_proj_in,
        grad_proj_back,
        grad_qv_bias,
        grad_out_bias,
        grad_norm_one,
        grad_in_bias,
        grad_back_bias,
        grad_norm_two,
        table_grad,
    )
    used = sum((math.prod(layout) for layout in layouts_list()))
    padding = jnp.zeros((flat_params.shape[0] - used,), BF16)
    grads_flat = jnp.concatenate([piece.astype(BF16).reshape(-1) for piece in grad_list] + [padding])
    grad_share = lax.psum_scatter(
        grads_flat, ("dp", "head"), scatter_dimension=0, tiled=True
    ).astype(F32)
    shard_len = params.shape[0]
    flat_index = (lax.axis_index("dp") * groups + head_pos) * shard_len + jnp.arange(
        shard_len, dtype=jnp.int32
    )
    param_step, new_one = adam_step(params, moment_one, moment_two, grad_share, flat_index)
    return (output_low, grad_hidden, grad_share, param_step, new_one)


def solution(mesh):
    placed = (
        P("dp", "head", None),
        P("dp", "head", None),
        P("dp", None, None),
        P("dp", None),
        P(("dp", "head")),
        P(("dp", "head")),
        P(("dp", "head")),
    )
    return jax.shard_map(
        shards,
        mesh=mesh,
        in_specs=placed,
        out_specs=(
            P("dp", "head", None),
            P("dp", "head", None),
            P(("dp", "head")),
            P(("dp", "head")),
            P(("dp", "head")),
        ),
        check_vma=False,
    )
```

```python
import functools
import math

import jax
import jax.numpy as jnp
import numpy as np
from jax import lax
from jax.experimental import pallas as pl
from jax.experimental.pallas import tpu as pltpu
from jax.sharding import PartitionSpec as P

D = 768
HEADS = 12
FF = 3072
BUCKETS = 32
WINLEN = 512
HEAD_DIM = 64
PAIRS = HEADS // 2
LANES = 128
BLOCKS = WINLEN // LANES

beta_one = 0.9
beta_two = 0.999
adam_eps = 1e-08
norm_eps = 1e-05
base_rate = 0.001
layer_decay = 0.75
decay_weight = 0.01
adam_count = 100
coord_cell = 32
masked_score = -1e30

F32 = jnp.float32
BF16 = jnp.bfloat16


def layouts_list():
    return (
        (D, 3 * D),
        (D, D),
        (D, D),
        (D, FF),
        (FF, D),
        (2, D),
        (D,),
        (2, D),
        (FF,),
        (D,),
        (2, D),
        (3, HEADS, BUCKETS),
    )


def unpack(flat_params):
    pieces = []
    offset = 0
    for layout in layouts_list():
        elements = math.prod(layout)
        pieces.append(flat_params[offset : offset + elements].reshape(layout))
        offset += elements
    return pieces


def matmul(left_mat, right_mat):
    return jnp.dot(left_mat, right_mat, preferred_element_type=F32)


def rows_inner(left_mat, right_mat):
    return lax.dot_general(left_mat, right_mat, (((0,), (0,)), ((), ())), preferred_element_type=F32)


def times_transposed(left_mat, right_mat):
    return lax.dot_general(left_mat, right_mat, (((1,), (1,)), ((), ())), preferred_element_type=F32)


def layer_norm(values, gain_bias):
    row_mean = jnp.mean(values, axis=-1, keepdims=True)
    centred = values - row_mean
    spread = jnp.mean(centred * centred, axis=-1, keepdims=True)
    return centred * lax.rsqrt(spread + norm_eps) * gain_bias[0] + gain_bias[1]


def gelu_exact(values):
    return jax.nn.gelu(values, approximate=False)


def hot(index, count):
    return (np.asarray(index)[..., None] == np.arange(count)).astype(np.float32)


def clipped(steps):
    return np.clip(steps, -(BUCKETS // 2), BUCKETS // 2 - 1) + BUCKETS // 2


CELLS = np.arange(BUCKETS)
HOT_SAME = hot(clipped(CELLS[:, None] - CELLS[None, :]), BUCKETS)
HOT_LESS = hot(clipped(CELLS[:, None] - CELLS[None, :] - 1), BUCKETS)
WIDE = 6 * LANES
_U = np.arange(WIDE)
BAND_HOT = hot(np.where(_U < 5 * LANES, clipped(_U - 2 * LANES), 0), BUCKETS)
_V = np.arange(4 * LANES)
DIAG_HOT = np.concatenate(
    [
        hot(np.zeros(LANES, np.int64), BUCKETS),
        hot(np.where(_V < 3 * LANES, clipped(_V - LANES), 0), BUCKETS),
        hot(np.full(LANES, BUCKETS - 1), BUCKETS),
    ]
)


def window_layout(doc_lengths, box_coords):
    doc_ends = jnp.cumsum(doc_lengths, dtype=jnp.int32)
    doc_starts = doc_ends - doc_lengths
    places = jnp.arange(WINLEN, dtype=jnp.int32)
    doc_ids = jnp.sum(
        (places[:, None] >= doc_ends[None, :]).astype(jnp.int32), axis=1, dtype=jnp.int32
    )
    docs = jnp.arange(doc_lengths.shape[0], dtype=jnp.int32)
    chosen = doc_ids[:, None] == docs[None, :]
    first_hot = places[:, None] == doc_starts[None, :]
    first_box = jnp.sum(
        jnp.where(first_hot[:, :, None], box_coords[:, None, :], 0), axis=0, dtype=jnp.int32
    )
    anchor = jnp.sum(
        jnp.where(chosen[:, :, None], first_box[None, :, :], 0), axis=1, dtype=jnp.int32
    )
    relative = box_coords - jnp.concatenate([anchor[:, :2], anchor[:, :2]], axis=1)
    centre_x = (box_coords[:, 0] + box_coords[:, 2]) // 2
    centre_y = (box_coords[:, 1] + box_coords[:, 3]) // 2
    return chosen, relative, centre_x, centre_y


def box_features(relative):
    count_freq = D // 8
    steps = jnp.arange(count_freq, dtype=F32)
    frequency = jnp.exp(steps * (-math.log(1000.0) / count_freq))
    angles = relative.astype(F32)[:, :, None] * frequency[None, None, :]
    return jnp.concatenate([jnp.sin(angles), jnp.cos(angles)], axis=2).reshape(relative.shape[0], D)


def bias_operands(tables, chosen, centre_x, centre_y):
    cell_x, cell_y = centre_x // coord_cell, centre_y // coord_cell
    rest_x, rest_y = centre_x % coord_cell, centre_y % coord_cell
    cells = jnp.arange(BUCKETS, dtype=jnp.int32)
    hot_x = (cell_x[:, None] == cells[None, :]).astype(BF16)
    hot_y = (cell_y[:, None] == cells[None, :]).astype(BF16)
    none = jnp.zeros_like(hot_x)
    hot_two = jnp.concatenate([hot_x, hot_y, hot_x, hot_y], axis=1)
    key_x = jnp.stack(
        [
            jnp.concatenate([hot_x, -hot_x, none, none], axis=1),
            jnp.concatenate([none, none, hot_x, -hot_x], axis=1),
        ]
    )
    key_y = jnp.stack(
        [
            jnp.concatenate([hot_y, -hot_y, none, none], axis=1),
            jnp.concatenate([none, none, hot_y, -hot_y], axis=1),
        ]
    )
    same = jnp.einsum("qcb,thb->thqc", HOT_SAME.astype(BF16), tables[1:], preferred_element_type=F32)
    less = jnp.einsum("qcb,thb->thqc", HOT_LESS.astype(BF16), tables[1:], preferred_element_type=F32)
    zero = jnp.zeros_like(same[0])
    base = jnp.concatenate(
        [jnp.concatenate([same[0], zero], axis=2), jnp.concatenate([zero, same[1]], axis=2)], axis=1
    )
    base = base.reshape(PAIRS, 2, 64, 64)[:, ::-1].reshape(HEADS, 64, 64)
    diff_x = jnp.concatenate([jnp.concatenate([less[0], same[0]], axis=2), jnp.zeros((HEADS, 32, 64), F32)], axis=1)
    diff_y = jnp.concatenate([jnp.zeros((HEADS, 32, 64), F32), jnp.concatenate([less[1], same[1]], axis=2)], axis=1)
    rows = jnp.concatenate([base, diff_x, diff_y], axis=0).astype(BF16)
    rows = rows.transpose(1, 0, 2).reshape(64, 3 * D)
    met = matmul(hot_two[:, :64], rows).astype(BF16)
    band = matmul(tables[0], jnp.asarray(BAND_HOT.T, BF16)).reshape(HEADS, 1, WIDE)
    rest_cols = jnp.stack([rest_x, rest_y], axis=1).astype(F32)
    rest_rows = rest_cols.T
    pad = jnp.zeros((WINLEN, LANES - chosen.shape[1]), BF16)
    marks = chosen.astype(BF16)
    mark_keys = jnp.concatenate([marks, pad], axis=1)
    mark_queries = jnp.concatenate([(1 - marks) * jnp.asarray(masked_score, BF16), pad], axis=1)
    return dict(
        hot_two=hot_two,
        key_x=key_x,
        key_y=key_y,
        met=met,
        band=band,
        rest_cols=rest_cols,
        rest_rows=rest_rows,
        mark_keys=mark_keys,
        mark_queries=mark_queries,
    )


def half_masks():
    lane = lax.broadcasted_iota(jnp.int32, (1, LANES), 1)
    low = (lane < HEAD_DIM).astype(F32)
    return low.astype(BF16), (1.0 - low).astype(BF16)


def less_masks(rest_cols, rest_rows, less_x, less_y):
    for part in range(BLOCKS):
        rows = slice(part * LANES, (part + 1) * LANES)
        for axis, less in ((0, less_x), (1, less_y)):
            column = rest_cols[rows, axis : axis + 1]
            row = rest_rows[axis : axis + 1, :]
            less[rows, :] = jnp.where(row < column, 1.0, 0.0).astype(less.dtype)


def attention_forward_kernel(
    q_ref, k_ref, v_ref, hot_ref, keyx_ref, keyy_ref, met_ref, band_ref, cols_ref, rows_ref,
    mkey_ref, mquery_ref, probs_ref, context_ref,
    kaug, qaug, less_x, less_y, wide, scores,
):
    low, high = half_masks()
    less_masks(cols_ref, rows_ref, less_x, less_y)
    kaug[:, LANES:] = mkey_ref[...]
    qaug[:, LANES:] = mquery_ref[...]
    half = 2 * LANES

    def one_pair(pair, carry):
        at = pl.multiple_of(pair * LANES, LANES)
        lanes = pl.ds(at, LANES)
        lanes_x = pl.ds(pl.multiple_of(at + D, LANES), LANES)
        lanes_y = pl.ds(pl.multiple_of(at + 2 * D, LANES), LANES)
        values_t = v_ref[:, lanes].T
        for odd in range(2):
            own, other = (low, high) if odd == 0 else (high, low)
            head = 2 * pair + odd
            kaug[:, :LANES] = k_ref[:, lanes] * own + hot_ref[...] * other
            qaug[:, :LANES] = q_ref[:, lanes] * own + met_ref[:, lanes] * other
            skew_band(band_ref[head], wide)
            for side in range(2):
                cols = slice(side * half, (side + 1) * half)
                top = None
                for part in range(BLOCKS):
                    rows = slice(part * LANES, (part + 1) * LANES)
                    s = times_transposed(kaug[rows, :], qaug[cols, :])
                    dx = times_transposed(keyx_ref[odd, rows, :], met_ref[cols, lanes_x])
                    dy = times_transposed(keyy_ref[odd, rows, :], met_ref[cols, lanes_y])
                    bias = []
                    for block in range(2 * side, 2 * side + 2):
                        step = max(-2, min(2, block - part)) + 2
                        bias.append(wide[:, step * LANES : (step + 1) * LANES])
                    s = s + jnp.concatenate(bias, axis=1)
                    s = s + dx * less_x[rows, cols] + dy * less_y[rows, cols]
                    scores[rows, :] = s
                    best = jnp.max(s, axis=0, keepdims=True)
                    top = best if top is None else jnp.maximum(top, best)
                total = None
                for part in range(BLOCKS):
                    rows = slice(part * LANES, (part + 1) * LANES)
                    e = jnp.exp(scores[rows, :] - top)
                    scores[rows, :] = e
                    add = jnp.sum(e, axis=0, keepdims=True)
                    total = add if total is None else total + add
                share = 1.0 / total
                for part in range(BLOCKS):
                    rows = slice(part * LANES, (part + 1) * LANES)
                    probs_ref[head, rows, cols] = (scores[rows, :] * share).astype(BF16)
                got = matmul(
                    values_t[odd * HEAD_DIM : (odd + 1) * HEAD_DIM, :], probs_ref[head, :, cols]
                )
                context_ref[pl.ds(pl.multiple_of(head * HEAD_DIM, HEAD_DIM), HEAD_DIM), cols] = (
                    got.astype(BF16)
                )
        return carry

    lax.fori_loop(0, PAIRS, one_pair, 0)


def skew_band(row, wide):
    x = jnp.broadcast_to(row, (8, WIDE))
    sub = lax.broadcasted_iota(jnp.int32, (8, WIDE), 0)
    for bit in (1, 2, 4):
        x = jnp.where((sub & bit) != 0, pltpu.roll(x, bit, 1), x)
    for group in range(LANES // 8):
        y = x if group == 0 else pltpu.roll(x, 8 * group, 1)
        wide[8 * group : 8 * group + 8, :] = y[:, : 5 * LANES]


def diagonal_sums(parts):
    total = None
    for group in range(LANES // 8):
        x = jnp.concatenate(
            [parts[8 * group : 8 * group + 8, LANES : 4 * LANES], jnp.zeros((8, LANES), F32)], axis=1
        )
        y = x if group == 0 else pltpu.roll(x, 4 * LANES - 8 * group, 1)
        total = y if total is None else total + y
    sub = lax.broadcasted_iota(jnp.int32, (8, 4 * LANES), 0)
    for bit in (1, 2, 4):
        total = jnp.where((sub & bit) != 0, pltpu.roll(total, 4 * LANES - bit, 1), total)
    return jnp.sum(total, axis=0, keepdims=True)


def attention_backward_kernel(
    q_ref, k_ref, v_ref, dctx_ref, probs_ref, hot_ref, cols_ref, rows_ref,
    dq_ref, dk_ref, dv_ref, cells_ref, diag_ref,
    qaug, less_x, less_y, scores, dscores, band, kept, hot_t,
):
    low, high = half_masks()
    less_masks(cols_ref, rows_ref, less_x, less_y)
    hot_t[...] = hot_ref[...].T
    lane = lax.broadcasted_iota(jnp.int32, (1, LANES), 1)
    scale = HEAD_DIM ** (-0.5)
    of_x = jnp.where((lane // BUCKETS) % 2 == 0, 1.0, 0.0)
    cells_x = hot_ref[...] * of_x.astype(BF16)
    cells_y = hot_ref[...] * (1.0 - of_x).astype(BF16)

    def one_pair(pair, carry):
        at = pl.multiple_of(pair * LANES, LANES)
        lanes = pl.ds(at, LANES)
        keys_t = k_ref[:, lanes].T
        for odd in range(2):
            own, other = (low, high) if odd == 0 else (high, low)
            head = 2 * pair + odd
            qaug[...] = q_ref[:, lanes] * own + hot_ref[...] * other
            dctx = dctx_ref[:, lanes]
            dot = None
            for part in range(BLOCKS):
                rows = slice(part * LANES, (part + 1) * LANES)
                dp = times_transposed(v_ref[rows, lanes] * own, dctx)
                scores[rows, :] = dp
                add = jnp.sum(dp * probs_ref[head, rows, :].astype(F32), axis=0, keepdims=True)
                dot = add if dot is None else dot + add
            band[...] = jnp.zeros_like(band)
            for part in range(BLOCKS):
                rows = slice(part * LANES, (part + 1) * LANES)
                probs = probs_ref[head, rows, :]
                ds = probs.astype(F32) * (scores[rows, :] - dot)
                for block in range(BLOCKS):
                    step = max(-2, min(2, block - part)) + 2
                    where = slice(step * LANES, (step + 1) * LANES)
                    band[:, where] = band[:, where] + ds[:, block * LANES : (block + 1) * LANES]
                ds = ds.astype(BF16)
                dscores[rows, :] = ds
                both = matmul(ds, qaug[...])
                less = matmul(ds * less_x[rows, :], cells_x) + matmul(ds * less_y[rows, :], cells_y)
                dv = matmul(probs, dctx)
                kept[odd, 0, rows, :] = both
                kept[odd, 1, rows, :] = less
                kept[odd, 2, rows, :] = dv
            got = matmul(keys_t[odd * HEAD_DIM : (odd + 1) * HEAD_DIM, :], dscores[...])
            dq_ref[pl.ds(pl.multiple_of(head * HEAD_DIM, HEAD_DIM), HEAD_DIM), :] = (
                got * scale
            ).astype(BF16)
            diag_ref[head, :, LANES : 5 * LANES] = diagonal_sums(band)
            diag_ref[head, :, :LANES] = jnp.sum(band[:, :LANES], axis=0, keepdims=True)
            diag_ref[head, :, 5 * LANES :] = jnp.sum(band[:, 4 * LANES :], axis=0, keepdims=True)
            for which in range(2):
                summed = kept[odd, which]
                first = summed.astype(BF16)
                rest = (summed - first.astype(F32)).astype(BF16)
                cells_ref[head, which] = matmul(hot_t[:64, :], first) + matmul(hot_t[:64, :], rest)
        dk_ref[:, lanes] = jnp.where(lane < HEAD_DIM, kept[0, 0], kept[1, 0]).astype(BF16)
        dv_ref[:, lanes] = jnp.where(lane < HEAD_DIM, kept[0, 2], kept[1, 2]).astype(BF16)
        return carry

    lax.fori_loop(0, PAIRS, one_pair, 0)


def attention_forward(queries, keys, values, ops):
    return pl.pallas_call(
        attention_forward_kernel,
        out_shape=(
            jax.ShapeDtypeStruct((HEADS, WINLEN, WINLEN), BF16),
            jax.ShapeDtypeStruct((D, WINLEN), BF16),
        ),
        scratch_shapes=[
            pltpu.VMEM((WINLEN, 2 * LANES), BF16),
            pltpu.VMEM((WINLEN, 2 * LANES), BF16),
            pltpu.VMEM((WINLEN, WINLEN), F32),
            pltpu.VMEM((WINLEN, WINLEN), F32),
            pltpu.VMEM((LANES, 5 * LANES), F32),
            pltpu.VMEM((WINLEN, 2 * LANES), F32),
        ],
        compiler_params=pltpu.CompilerParams(vmem_limit_bytes=48 * 2**20),
        name="attention_forward",
    )(
        queries, keys, values, ops["hot_two"], ops["key_x"], ops["key_y"], ops["met"], ops["band"],
        ops["rest_cols"], ops["rest_rows"], ops["mark_keys"], ops["mark_queries"],
    )


def attention_backward(queries, keys, values, grad_context, probs, ops):
    return pl.pallas_call(
        attention_backward_kernel,
        out_shape=(
            jax.ShapeDtypeStruct((D, WINLEN), BF16),
            jax.ShapeDtypeStruct((WINLEN, D), BF16),
            jax.ShapeDtypeStruct((WINLEN, D), BF16),
            jax.ShapeDtypeStruct((HEADS, 2, 64, LANES), F32),
            jax.ShapeDtypeStruct((HEADS, 1, WIDE), F32),
        ),
        scratch_shapes=[
            pltpu.VMEM((WINLEN, LANES), BF16),
            pltpu.VMEM((WINLEN, WINLEN), BF16),
            pltpu.VMEM((WINLEN, WINLEN), BF16),
            pltpu.VMEM((WINLEN, WINLEN), F32),
            pltpu.VMEM((WINLEN, WINLEN), BF16),
            pltpu.VMEM((LANES, 5 * LANES), F32),
            pltpu.VMEM((2, 3, WINLEN, LANES), F32),
            pltpu.VMEM((LANES, WINLEN), BF16),
        ],
        compiler_params=pltpu.CompilerParams(vmem_limit_bytes=48 * 2**20),
        name="attention_backward",
    )(
        queries, keys, values, grad_context, probs, ops["hot_two"], ops["rest_cols"],
        ops["rest_rows"],
    )


def table_grads(cells, diag):
    exact = lax.Precision.HIGHEST
    pairs = cells.reshape(PAIRS, 2, 2, 64, LANES)
    every = jnp.stack([pairs[:, 0, 0, :, 64:], pairs[:, 1, 0, :, :64]], axis=1).reshape(HEADS, 64, 64)
    less = cells[:, 1]
    less_x, less_y = less[:, :32, :32], less[:, 32:, 32:64]
    all_x, all_y = every[:, :32, :32], every[:, 32:, 32:]
    same = jnp.stack([all_x - less_x, all_y - less_y]).reshape(2 * HEADS, -1)
    below = jnp.stack([less_x, less_y]).reshape(2 * HEADS, -1)
    same_hot = jnp.asarray(HOT_SAME.transpose(1, 0, 2).reshape(-1, BUCKETS))
    less_hot = jnp.asarray(HOT_LESS.transpose(1, 0, 2).reshape(-1, BUCKETS))
    moved = jnp.dot(same, same_hot, precision=exact) + jnp.dot(below, less_hot, precision=exact)
    along = jnp.dot(diag.reshape(HEADS, WIDE), jnp.asarray(DIAG_HOT), precision=exact)
    return jnp.concatenate([along[None], moved.reshape(2, HEADS, BUCKETS)], axis=0)


COLUMNS = 4
CORES = 2
DEPTH = 4
USED = sum(math.prod(layout) for layout in layouts_list())
MATRICES = layouts_list()[:5]
MISC = sum(math.prod(layout) for layout in layouts_list()[5:])
MISC_ROWS = -(-MISC // (8 * LANES)) * 8


class Plan:
    def __init__(self, shard_len):
        self.rows = shard_len // LANES
        self.quarter = -(-self.rows // (16 * COLUMNS)) * 16
        self.padded = COLUMNS * self.quarter
        self.per_column = CORES * DEPTH * self.rows
        self.carry = 128
        self.half = 2 * self.per_column
        self.staged = self.carry + self.half + 3 * LANES
        starts = []
        offset = 0
        for depth, width in MATRICES:
            starts.append(offset // LANES)
            offset += depth * width
        self.starts = starts
        self.misc_start = offset // LANES


def fits(mesh):
    return mesh.shape["dp"] == COLUMNS * CORES and mesh.shape["head"] == DEPTH


MESH = pl.DeviceIdType.MESH


class Place:
    def __init__(self):
        dp = lax.axis_index("dp")
        self.z = lax.axis_index("head")
        self.core = dp % CORES
        self.column = dp // CORES
        self.x = self.column % 2
        self.y = self.column // 2
        self.col_x = 2 * self.y + (1 - self.x)
        self.col_y = 2 * (1 - self.y) + self.x
        self.col_d = 2 * (1 - self.y) + (1 - self.x)
        self.peer_x = self.at(self.col_x, self.core, self.z)
        self.peer_y = self.at(self.col_y, self.core, self.z)
        self.peer_d = self.at(self.col_d, self.core, self.z)
        self.peer_core = self.at(self.column, 1 - self.core, self.z)
        self.far = [lax.rem(self.z + d, DEPTH) for d in range(1, DEPTH)]
        self.from_far = [lax.rem(self.z + DEPTH - d, DEPTH) for d in range(1, DEPTH)]
        self.peers_z = [self.at(self.column, self.core, f) for f in self.far]

    def at(self, column, core, z):
        return {"dp": column * CORES + core, "head": z}

    def greet(self):
        barrier = pltpu.get_barrier_semaphore()
        peers = [self.peer_x, self.peer_y, self.peer_d, self.peer_core] + self.peers_z
        for peer in peers:
            pl.semaphore_signal(barrier, inc=1, device_id=peer, device_id_type=MESH)
        pl.semaphore_wait(barrier, len(peers))


def remote(src, dst, send_sem, recv_sem, peer):
    return pltpu.make_async_remote_copy(
        src_ref=src, dst_ref=dst, send_sem=send_sem, recv_sem=recv_sem, device_id=peer,
        device_id_type=MESH,
    )


class Gathering:
    def __init__(self, place, flat, sems):
        self.place = place
        self.flat = flat
        self.sems = sems
        self.sent = []

    def send(self, src, dst, kind, index, peer):
        copy = remote(src, dst, self.sems[kind].at[0, index], self.sems[kind].at[1, index], peer)
        copy.start()
        self.sent.append(copy)

    def got(self, dst, kind, index):
        remote(
            dst, dst, self.sems[kind].at[0, index], self.sems[kind].at[1, index], self.place.peer_x
        ).wait_recv()

    def spread(self, own):
        p = self.place
        for index, (column, peer) in enumerate(
            ((p.col_x, p.peer_x), (p.col_y, p.peer_y), (p.col_d, p.peer_d))
        ):
            self.send(
                own.at[column], self.flat.at[p.column, p.core, p.z, column], "spread", index, peer
            )
        self.flat[p.column, p.core, p.z, p.column] = own[p.column]

    def spread_done(self):
        p = self.place
        for index, column in enumerate((p.col_x, p.col_y, p.col_d)):
            self.got(self.flat.at[column, p.core, p.z, p.column], "spread", index)

    def along_z(self, k):
        p = self.place
        piece = self.flat.at[k, p.core, p.z, p.column]
        for d in range(DEPTH - 1):
            self.send(piece, piece, "z", 3 * k + d, p.peers_z[d])

    def first(self, k):
        p = self.place
        for d in range(DEPTH - 1):
            self.got(self.flat.at[k, p.core, p.from_far[d], p.column], "z", 3 * k + d)
        piece = self.flat.at[k, p.core, :, p.column]
        self.send(piece, piece, "one", 2 * k, p.peer_x)
        self.send(piece, piece, "one", 2 * k + 1, p.peer_y)
        self.send(piece, piece, "core", 5 * k, p.peer_core)

    def second(self, k):
        p = self.place
        from_x = self.flat.at[k, p.core, :, p.col_x]
        self.got(from_x, "one", 2 * k)
        part = self.flat.at[k, p.core, 0:2, p.col_x]
        self.send(part, part, "two", 2 * k, p.peer_y)
        self.send(from_x, from_x, "core", 5 * k + 1, p.peer_core)
        from_y = self.flat.at[k, p.core, :, p.col_y]
        self.got(from_y, "one", 2 * k + 1)
        part = self.flat.at[k, p.core, 2:4, p.col_y]
        self.send(part, part, "two", 2 * k + 1, p.peer_x)
        self.send(from_y, from_y, "core", 5 * k + 2, p.peer_core)

    def third(self, k):
        p = self.place
        part = self.flat.at[k, p.core, 0:2, p.col_d]
        self.got(part, "two", 2 * k)
        self.send(part, part, "core", 5 * k + 3, p.peer_core)
        part = self.flat.at[k, p.core, 2:4, p.col_d]
        self.got(part, "two", 2 * k + 1)
        self.send(part, part, "core", 5 * k + 4, p.peer_core)

    def complete(self, k):
        p = self.place
        other = 1 - p.core
        for index, column in enumerate((p.column, p.col_x, p.col_y)):
            self.got(self.flat.at[k, other, :, column], "core", 5 * k + index)
        self.got(self.flat.at[k, other, 0:2, p.col_d], "core", 5 * k + 3)
        self.got(self.flat.at[k, other, 2:4, p.col_d], "core", 5 * k + 4)

    def finish(self):
        for copy in self.sent:
            copy.wait_send()


GATHER_SEMS = {"spread": 3, "z": 12, "one": 8, "two": 8, "core": 20}


def sem_shapes(counts):
    return [pltpu.SemaphoreType.DMA((2, count)) for count in counts.values()]


def stage_columns(plan, flat, staged, half):
    def one(step, carry):
        column = step // (CORES * DEPTH * COLUMNS)
        shard = step // COLUMNS
        quarter = step % COLUMNS
        core = (shard // DEPTH) % CORES
        base = plan.carry + shard * plan.rows + quarter * plan.quarter
        piece = flat[2 * half + column, core, shard % DEPTH, quarter]
        staged[pl.ds(pl.multiple_of(base, 8), plan.quarter), :] = piece.astype(F32)
        return carry

    lax.fori_loop(0, 2 * CORES * DEPTH * COLUMNS, one, 0)


ROW_STEP = 48


def rows_in_half(plan, half):
    low, high = half * plan.half, (half + 1) * plan.half
    taken = []
    for index, (depth, width) in enumerate(MATRICES):
        blocks = width // LANES

        def groups_until(end):
            rows = (end - plan.starts[index]) // (16 * blocks) * 16
            return max(0, min(depth, rows))

        begin, end = groups_until(low), groups_until(high)
        if end > begin:
            taken.append((index, begin, end))
    return taken


def staged_at(plan, half, row):
    return plan.carry + row - half * plan.half


def form_matrices(plan, staged, matrices, half):
    for index, begin, end in rows_in_half(plan, half):
        blocks = MATRICES[index][1] // LANES
        base = staged_at(plan, half, plan.starts[index] + begin * blocks)
        assert base >= 0
        target = matrices[index]
        for step_rows, first, count in row_loops(end - begin):

            def one(step, carry, step_rows=step_rows, first=first, blocks=blocks, base=base,
                    begin=begin, target=target):
                row = first + step * step_rows
                for block in range(blocks):
                    got = staged[pl.ds(base + row * blocks + block, step_rows, stride=blocks), :]
                    target[
                        pl.ds(pl.multiple_of(begin + row, 16), step_rows),
                        block * LANES : (block + 1) * LANES,
                    ] = got.astype(BF16)
                return carry

            lax.fori_loop(0, count, one, 0)


def row_loops(rows):
    whole = rows // ROW_STEP
    loops = [(ROW_STEP, 0, whole)] if whole else []
    if rows % ROW_STEP:
        loops.append((16, whole * ROW_STEP, (rows % ROW_STEP) // 16))
    return loops


def gather_kernel(plan, own, *refs):
    outs, refs = refs[:6], refs[6:]
    flat, staged, refs = refs[0], refs[1], refs[2:]
    held, refs = refs[:5], refs[5:]
    out_sems, refs = refs[0], refs[1:]
    place = Place()
    gathering = Gathering(place, flat, dict(zip(GATHER_SEMS, refs)))
    place.greet()
    gathering.spread(own)
    gathering.spread_done()
    gathering.along_z(0)
    gathering.along_z(1)
    gathering.first(0)
    gathering.along_z(2)
    gathering.first(1)
    gathering.along_z(3)
    gathering.second(0)
    gathering.third(0)
    gathering.first(2)
    gathering.second(1)
    gathering.third(1)
    gathering.first(3)
    gathering.second(2)
    gathering.complete(0)
    gathering.complete(1)
    stage_columns(plan, flat, staged, 0)
    gathering.third(2)
    gathering.second(3)
    form_matrices(plan, staged, held, 0)
    gathering.third(3)
    written = []
    for index in range(3):
        copy = pltpu.make_async_copy(held[index], outs[index], out_sems.at[index])
        copy.start()
        written.append(copy)
    staged[: plan.carry, :] = staged[plan.half : plan.half + plan.carry, :]
    gathering.complete(2)
    gathering.complete(3)
    stage_columns(plan, flat, staged, 1)
    form_matrices(plan, staged, held, 1)
    misc = staged_at(plan, 1, plan.misc_start)
    outs[5][...] = staged[misc : misc + MISC_ROWS, :]
    for index in range(3, 5):
        copy = pltpu.make_async_copy(held[index], outs[index], out_sems.at[index])
        copy.start()
        written.append(copy)
    for copy in written:
        copy.wait()
    gathering.finish()


def gather_weights(plan, own):
    anywhere = pl.BlockSpec(memory_space=pl.ANY)
    vmem = pl.BlockSpec(memory_space=pltpu.VMEM)
    return pl.pallas_call(
        functools.partial(gather_kernel, plan),
        out_shape=[jax.ShapeDtypeStruct(layout, BF16) for layout in MATRICES]
        + [jax.ShapeDtypeStruct((MISC_ROWS, LANES), F32)],
        in_specs=[vmem],
        out_specs=[anywhere] * 5 + [vmem],
        scratch_shapes=[
            pltpu.VMEM((COLUMNS, CORES, DEPTH, COLUMNS, plan.quarter, LANES), BF16),
            pltpu.VMEM((plan.staged, LANES), F32),
        ]
        + [pltpu.VMEM(layout, BF16) for layout in MATRICES]
        + [pltpu.SemaphoreType.DMA((5,))]
        + sem_shapes(GATHER_SEMS),
        compiler_params=pltpu.CompilerParams(
            collective_id=0, has_side_effects=True, vmem_limit_bytes=60 * 2**20
        ),
        name="gather_weights",
    )(own)


class Reducing:
    def __init__(self, place, flat, swapped, one, two, deep, piece, result, sems):
        self.place = place
        self.flat = flat
        self.swapped = swapped
        self.one = one
        self.two = two
        self.deep = deep
        self.piece = piece
        self.result = result
        self.sems = sems
        self.sent = []

    send = Gathering.send
    got = Gathering.got
    finish = Gathering.finish

    def swap(self, k):
        p = self.place
        self.send(self.flat.at[k, 1 - p.core], self.swapped.at[k], "core", k, p.peer_core)

    def first(self, k):
        p = self.place
        self.got(self.swapped.at[k], "core", k)

        def one(step, carry):
            z, quarter = step // COLUMNS, step % COLUMNS
            total = self.flat[k, p.core, z, quarter].astype(F32)
            total = total + self.swapped[k, z, quarter].astype(F32)
            self.flat[k, p.core, z, quarter] = total.astype(BF16)
            return carry

        lax.fori_loop(0, DEPTH * COLUMNS, one, 0)
        self.send(self.flat.at[k, p.core, 0:2, p.col_d], self.one.at[k, 0], "one", 2 * k, p.peer_y)
        self.send(
            self.flat.at[k, p.core, 2:4, p.col_d], self.one.at[k, 1], "one", 2 * k + 1, p.peer_x
        )

    def second(self, k):
        p = self.place
        for side, column in ((0, p.col_x), (1, p.col_y)):
            self.got(self.one.at[k, side], "one", 2 * k + side)

            def one(step, carry, side=side, column=column):
                z = 2 * side + step
                total = self.flat[k, p.core, z, column].astype(F32)
                total = total + self.one[k, side, step].astype(F32)
                self.flat[k, p.core, z, column] = total.astype(BF16)
                return carry

            lax.fori_loop(0, 2, one, 0)
        self.send(self.flat.at[k, p.core, :, p.col_x], self.two.at[k, 0], "two", 2 * k, p.peer_x)
        self.send(self.flat.at[k, p.core, :, p.col_y], self.two.at[k, 1], "two", 2 * k + 1, p.peer_y)

    def third(self, k):
        p = self.place
        for side in range(2):
            self.got(self.two.at[k, side], "two", 2 * k + side)

        def one(z, carry):
            total = self.flat[k, p.core, z, p.column].astype(F32)
            total = total + self.two[k, 0, z].astype(F32) + self.two[k, 1, z].astype(F32)
            self.flat[k, p.core, z, p.column] = total.astype(BF16)
            return carry

        lax.fori_loop(0, DEPTH, one, 0)
        for d in range(DEPTH - 1):
            self.send(
                self.flat.at[k, p.core, p.far[d], p.column], self.deep.at[k, d], "z", 3 * k + d,
                p.peers_z[d],
            )

    def fourth(self, k):
        p = self.place
        for d in range(DEPTH - 1):
            self.got(self.deep.at[k, d], "z", 3 * k + d)
        total = self.flat[k, p.core, p.z, p.column].astype(F32)
        for d in range(DEPTH - 1):
            total = total + self.deep[k, d].astype(F32)
        self.piece[k] = total.astype(BF16)

    def give_back(self):
        p = self.place
        for index, (column, peer) in enumerate(
            ((p.col_x, p.peer_x), (p.col_y, p.peer_y), (p.col_d, p.peer_d))
        ):
            self.send(self.piece.at[column], self.result.at[index], "spread", index, peer)

    def receive(self, out):
        p = self.place
        out[p.column] = self.piece[p.column].astype(F32)
        for index, column in enumerate((p.col_x, p.col_y, p.col_d)):
            self.got(self.result.at[index], "spread", index)
            out[column] = self.result[index].astype(F32)


REDUCE_SEMS = {"spread": 3, "z": 12, "one": 8, "two": 8, "core": 4}


def flatten_matrices(plan, staged, matrices, half):
    for index, begin, end in rows_touching_half(plan, half):
        blocks = MATRICES[index][1] // LANES
        base = staged_at(plan, half, plan.starts[index] + begin * blocks)
        source = matrices[index]
        for step_rows, first, count in row_loops(end - begin):

            def one(step, carry, step_rows=step_rows, first=first, blocks=blocks, base=base,
                    begin=begin, source=source):
                row = first + step * step_rows
                for block in range(blocks):
                    got = source[
                        pl.ds(pl.multiple_of(begin + row, 16), step_rows),
                        block * LANES : (block + 1) * LANES,
                    ]
                    staged[pl.ds(base + row * blocks + block, step_rows, stride=blocks), :] = (
                        got.astype(F32)
                    )
                return carry

            lax.fori_loop(0, count, one, 0)


def rows_touching_half(plan, half):
    low, high = half * plan.half, (half + 1) * plan.half
    taken = []
    for index, (depth, width) in enumerate(MATRICES):
        blocks = width // LANES
        begin = max(0, (low - plan.starts[index]) // (16 * blocks) * 16)
        end = min(depth, -(-(high - plan.starts[index]) // (16 * blocks)) * 16)
        if end > begin:
            taken.append((index, begin, end))
    return taken


def unstage_columns(plan, flat, staged, half):
    def one(step, carry):
        column = step // (CORES * DEPTH * COLUMNS)
        shard = step // COLUMNS
        quarter = step % COLUMNS
        core = (shard // DEPTH) % CORES
        base = plan.carry + shard * plan.rows + quarter * plan.quarter
        piece = staged[pl.ds(pl.multiple_of(base, 8), plan.quarter), :]
        flat[2 * half + column, core, shard % DEPTH, quarter] = piece.astype(BF16)
        return carry

    lax.fori_loop(0, 2 * CORES * DEPTH * COLUMNS, one, 0)


def reduce_kernel(plan, *refs):
    grads, misc, refs = refs[:5], refs[5], refs[6:]
    out, refs = refs[0], refs[1:]
    flat, staged, refs = refs[0], refs[1], refs[2:]
    buffers, refs = refs[:6], refs[6:]
    place = Place()
    reducing = Reducing(place, flat, *buffers, dict(zip(REDUCE_SEMS, refs)))
    end = plan.carry + plan.half
    staged[end:, :] = jnp.zeros((plan.staged - end, LANES), F32)
    flatten_matrices(plan, staged, grads, 1)
    at = staged_at(plan, 1, plan.misc_start)
    staged[at : at + MISC_ROWS, :] = misc[...]
    staged[at + MISC_ROWS : end, :] = jnp.zeros((end - at - MISC_ROWS, LANES), F32)
    unstage_columns(plan, flat, staged, 1)
    place.greet()
    reducing.swap(3)
    reducing.swap(2)
    flatten_matrices(plan, staged, grads, 0)
    unstage_columns(plan, flat, staged, 0)
    reducing.first(3)
    reducing.swap(1)
    reducing.first(2)
    reducing.swap(0)
    reducing.second(3)
    reducing.first(1)
    reducing.second(2)
    reducing.third(3)
    reducing.first(0)
    reducing.second(1)
    reducing.third(2)
    reducing.fourth(3)
    reducing.second(0)
    reducing.third(1)
    reducing.fourth(2)
    reducing.third(0)
    reducing.fourth(1)
    reducing.fourth(0)
    reducing.give_back()
    reducing.receive(out)
    reducing.finish()


def reduce_grads(plan, grads, misc):
    vmem = pl.BlockSpec(memory_space=pltpu.VMEM)
    block = (plan.quarter, LANES)
    return pl.pallas_call(
        functools.partial(reduce_kernel, plan),
        out_shape=jax.ShapeDtypeStruct((COLUMNS,) + block, F32),
        in_specs=[vmem] * 6,
        out_specs=vmem,
        scratch_shapes=[
            pltpu.VMEM((COLUMNS, CORES, DEPTH, COLUMNS) + block, BF16),
            pltpu.VMEM((plan.staged, LANES), F32),
            pltpu.VMEM((COLUMNS, DEPTH, COLUMNS) + block, BF16),
            pltpu.VMEM((COLUMNS, 2, 2) + block, BF16),
            pltpu.VMEM((COLUMNS, 2, DEPTH) + block, BF16),
            pltpu.VMEM((COLUMNS, DEPTH - 1) + block, BF16),
            pltpu.VMEM((COLUMNS,) + block, BF16),
            pltpu.VMEM((3,) + block, BF16),
        ]
        + sem_shapes(REDUCE_SEMS),
        compiler_params=pltpu.CompilerParams(
            collective_id=1, has_side_effects=True, vmem_limit_bytes=62 * 2**20
        ),
        name="reduce_grads",
    )(*grads, misc)


def adam_step(params, moment_one, moment_two, grads, flat_index):
    box_part = (flat_index >= 4 * D * D) & (flat_index < 5 * D * D)
    step_rate = jnp.where(box_part, base_rate * layer_decay**12, base_rate * layer_decay)
    decay_mask = jnp.where(flat_index < 5 * D * D + 2 * D * FF, decay_weight, 0.0)
    moment_one = beta_one * moment_one + (1.0 - beta_one) * grads
    moment_two = beta_two * moment_two + (1.0 - beta_two) * grads * grads
    first_hat = moment_one / (1.0 - beta_one**adam_count)
    second_hat = moment_two / (1.0 - beta_two**adam_count)
    update = first_hat / (jnp.sqrt(second_hat) + adam_eps) + decay_mask * params
    return (-step_rate * update, moment_one)


def to_windows(shard):
    return lax.all_to_all(shard, "head", split_axis=0, concat_axis=1, tiled=True)


def to_positions(window):
    return lax.all_to_all(window, "head", split_axis=1, concat_axis=0, tiled=True)


def shards(fast, hidden_in, cotangent, box_coords, doc_lengths, params, moment_one, moment_two):
    head_pos = lax.axis_index("head")
    groups = lax.axis_size("head")
    shard_len = params.shape[0]
    plan = Plan(shard_len) if fast else None
    if plan is None:
        flat_params = lax.all_gather(params.astype(BF16), ("dp", "head"), axis=0, tiled=True)
        pieces = unpack(flat_params)
    else:
        own = params.astype(BF16).reshape(plan.rows, LANES)
        own = jnp.pad(own, ((0, plan.padded - plan.rows), (0, 0)))
        own = own.reshape(COLUMNS, plan.quarter, LANES)
        *pieces, misc = gather_weights(plan, own)
        misc = misc.reshape(-1).astype(BF16)
        offset = 0
        for layout in layouts_list()[5:]:
            elements = math.prod(layout)
            pieces.append(misc[offset : offset + elements].reshape(layout))
            offset += elements
    hidden = to_windows(hidden_in).reshape(WINLEN, D)
    cot = to_windows(cotangent).reshape(WINLEN, D)
    own_box = lax.dynamic_index_in_dim(box_coords, head_pos, 0, keepdims=False)
    own_lengths = lax.dynamic_index_in_dim(doc_lengths, head_pos, 0, keepdims=False)
    chosen, relative, centre_x, centre_y = window_layout(own_lengths, own_box)
    features = box_features(relative).astype(BF16)

    proj_qkv, proj_out, proj_box, proj_in, proj_back = pieces[:5]
    qv_bias, out_bias, norm_one, in_bias, back_bias, norm_two, tables = pieces[5:]
    ops = bias_operands(tables, chosen, centre_x, centre_y)
    start_state = hidden.astype(F32) + matmul(features, proj_box)
    start_low = start_state.astype(BF16)
    qv_float = qv_bias.astype(F32)
    mixed = matmul(start_low, proj_qkv)
    queries = (mixed[:, :D] + qv_float[0]).astype(BF16) * jnp.asarray(HEAD_DIM ** (-0.5), BF16)
    keys = mixed[:, D : 2 * D].astype(BF16)
    values = (mixed[:, 2 * D :] + qv_float[1]).astype(BF16)

    probs, context_t = attention_forward(queries, keys, values, ops)
    first_sum = start_state + rows_inner(context_t, proj_out) + out_bias.astype(F32)
    normed, norm_one_back = jax.vjp(layer_norm, first_sum, norm_one.astype(F32))
    normed_low = normed.astype(BF16)
    inner_act = matmul(normed_low, proj_in) + in_bias.astype(F32)
    active, gelu_back = jax.vjp(gelu_exact, inner_act)
    active_low = active.astype(BF16)
    second_sum = normed + matmul(active_low, proj_back) + back_bias.astype(F32)
    output, norm_two_back = jax.vjp(layer_norm, second_sum, norm_two.astype(F32))
    output_low = to_positions(output.astype(BF16).reshape(1, WINLEN, D))

    grad_second, grad_norm_two = norm_two_back(cot.astype(F32))
    grad_branch = grad_second.astype(BF16)
    grad_proj_back = rows_inner(active_low, grad_branch)
    grad_back_bias = jnp.sum(grad_branch.astype(F32), axis=0)
    (grad_inner_f,) = gelu_back(times_transposed(grad_branch, proj_back))
    grad_inner = grad_inner_f.astype(BF16)
    grad_proj_in = rows_inner(normed_low, grad_inner)
    grad_in_bias = jnp.sum(grad_inner.astype(F32), axis=0)
    grad_first, grad_norm_one = norm_one_back(grad_second + times_transposed(grad_inner, proj_in))
    grad_attn = grad_first.astype(BF16)
    grad_proj_out = matmul(context_t, grad_attn)
    grad_out_bias = jnp.sum(grad_attn.astype(F32), axis=0)
    grad_context = times_transposed(grad_attn, proj_out).astype(BF16)
    grad_queries_t, grad_keys, grad_values, cells, diag = attention_backward(
        queries, keys, values, grad_context, probs, ops
    )
    table_grad = table_grads(cells, diag)
    grad_mixed = jnp.concatenate([grad_queries_t.T, grad_keys, grad_values], axis=1)
    grad_proj_qkv = rows_inner(start_low, grad_mixed)
    summed = jnp.sum(grad_mixed.astype(F32), axis=0)
    grad_qv_bias = jnp.stack([summed[:D], summed[2 * D :]])
    grad_start = grad_first + times_transposed(grad_mixed, proj_qkv)
    grad_start_low = grad_start.astype(BF16)
    grad_hidden = to_positions(grad_start_low.reshape(1, WINLEN, D))
    grad_proj_box = rows_inner(features, grad_start_low)
    grad_list = (
        grad_proj_qkv,
        grad_proj_out,
        grad_proj_box,
        grad_proj_in,
        grad_proj_back,
        grad_qv_bias,
        grad_out_bias,
        grad_norm_one,
        grad_in_bias,
        grad_back_bias,
        grad_norm_two,
        table_grad,
    )
    if plan is None:
        padding = jnp.zeros((shard_len * groups * lax.axis_size("dp") - USED,), BF16)
        grads_flat = jnp.concatenate(
            [piece.astype(BF16).reshape(-1) for piece in grad_list] + [padding]
        )
        grad_share = lax.psum_scatter(
            grads_flat, ("dp", "head"), scatter_dimension=0, tiled=True
        ).astype(F32)
    else:
        misc = jnp.concatenate([piece.reshape(-1) for piece in grad_list[5:]])
        misc = jnp.pad(misc, (0, MISC_ROWS * LANES - MISC)).reshape(MISC_ROWS, LANES)
        summed = reduce_grads(plan, [piece.astype(BF16) for piece in grad_list[:5]], misc)
        grad_share = summed.reshape(plan.padded, LANES)[: plan.rows].reshape(-1)
    flat_index = (lax.axis_index("dp") * groups + head_pos) * shard_len + jnp.arange(
        shard_len, dtype=jnp.int32
    )
    param_step, new_one = adam_step(params, moment_one, moment_two, grad_share, flat_index)
    return (output_low, grad_hidden, grad_share, param_step, new_one)


def solution(mesh):
    placed = (
        P("dp", "head", None),
        P("dp", "head", None),
        P("dp", None, None),
        P("dp", None),
        P(("dp", "head")),
        P(("dp", "head")),
        P(("dp", "head")),
    )
    fast = fits(mesh)
    return jax.shard_map(
        functools.partial(shards, fast),
        mesh=mesh,
        in_specs=placed,
        out_specs=(
            P("dp", "head", None),
            P("dp", "head", None),
            P(("dp", "head")),
            P(("dp", "head")),
            P(("dp", "head")),
        ),
        check_vma=False,
    )
```

```python
import functools
import math

import jax
import jax.numpy as jnp
import numpy as np
from jax import lax
from jax.experimental import pallas as pl
from jax.experimental.pallas import tpu as pltpu
from jax.sharding import PartitionSpec as P

D = 768
HEADS = 12
FF = 3072
BUCKETS = 32
WINLEN = 512
HEAD_DIM = 64
PAIRS = HEADS // 2
LANES = 128
BLOCKS = WINLEN // LANES

beta_one = 0.9
beta_two = 0.999
adam_eps = 1e-08
norm_eps = 1e-05
base_rate = 0.001
layer_decay = 0.75
decay_weight = 0.01
adam_count = 100
coord_cell = 32
masked_score = -1e30

F32 = jnp.float32
BF16 = jnp.bfloat16


def layouts_list():
    return (
        (D, 3 * D),
        (D, D),
        (D, D),
        (D, FF),
        (FF, D),
        (2, D),
        (D,),
        (2, D),
        (FF,),
        (D,),
        (2, D),
        (3, HEADS, BUCKETS),
    )


def unpack(flat_params):
    pieces = []
    offset = 0
    for layout in layouts_list():
        elements = math.prod(layout)
        pieces.append(flat_params[offset : offset + elements].reshape(layout))
        offset += elements
    return pieces


def matmul(left_mat, right_mat):
    return jnp.dot(left_mat, right_mat, preferred_element_type=F32)


def rows_inner(left_mat, right_mat):
    return lax.dot_general(left_mat, right_mat, (((0,), (0,)), ((), ())), preferred_element_type=F32)


def times_transposed(left_mat, right_mat):
    return lax.dot_general(left_mat, right_mat, (((1,), (1,)), ((), ())), preferred_element_type=F32)


def layer_norm(values, gain_bias):
    row_mean = jnp.mean(values, axis=-1, keepdims=True)
    centred = values - row_mean
    spread = jnp.mean(centred * centred, axis=-1, keepdims=True)
    return centred * lax.rsqrt(spread + norm_eps) * gain_bias[0] + gain_bias[1]


def gelu_exact(values):
    return jax.nn.gelu(values, approximate=False)


def hot(index, count):
    return (np.asarray(index)[..., None] == np.arange(count)).astype(np.float32)


def clipped(steps):
    return np.clip(steps, -(BUCKETS // 2), BUCKETS // 2 - 1) + BUCKETS // 2


CELLS = np.arange(BUCKETS)
HOT_SAME = hot(clipped(CELLS[:, None] - CELLS[None, :]), BUCKETS)
HOT_LESS = hot(clipped(CELLS[:, None] - CELLS[None, :] - 1), BUCKETS)
WIDE = 6 * LANES
_U = np.arange(WIDE)
BAND_HOT = hot(np.where(_U < 5 * LANES, clipped(_U - 2 * LANES), 0), BUCKETS)
_V = np.arange(4 * LANES)
DIAG_HOT = np.concatenate(
    [
        hot(np.zeros(LANES, np.int64), BUCKETS),
        hot(np.where(_V < 3 * LANES, clipped(_V - LANES), 0), BUCKETS),
        hot(np.full(LANES, BUCKETS - 1), BUCKETS),
    ]
)


def window_layout(doc_lengths, box_coords):
    doc_ends = jnp.cumsum(doc_lengths, dtype=jnp.int32)
    doc_starts = doc_ends - doc_lengths
    places = jnp.arange(WINLEN, dtype=jnp.int32)
    doc_ids = jnp.sum(
        (places[:, None] >= doc_ends[None, :]).astype(jnp.int32), axis=1, dtype=jnp.int32
    )
    docs = jnp.arange(doc_lengths.shape[0], dtype=jnp.int32)
    chosen = doc_ids[:, None] == docs[None, :]
    first_hot = places[:, None] == doc_starts[None, :]
    first_box = jnp.sum(
        jnp.where(first_hot[:, :, None], box_coords[:, None, :], 0), axis=0, dtype=jnp.int32
    )
    anchor = jnp.sum(
        jnp.where(chosen[:, :, None], first_box[None, :, :], 0), axis=1, dtype=jnp.int32
    )
    relative = box_coords - jnp.concatenate([anchor[:, :2], anchor[:, :2]], axis=1)
    centre_x = (box_coords[:, 0] + box_coords[:, 2]) // 2
    centre_y = (box_coords[:, 1] + box_coords[:, 3]) // 2
    return chosen, relative, centre_x, centre_y


def box_features(relative):
    count_freq = D // 8
    steps = jnp.arange(count_freq, dtype=F32)
    frequency = jnp.exp(steps * (-math.log(1000.0) / count_freq))
    angles = relative.astype(F32)[:, :, None] * frequency[None, None, :]
    return jnp.concatenate([jnp.sin(angles), jnp.cos(angles)], axis=2).reshape(relative.shape[0], D)


def bias_operands(tables, chosen, centre_x, centre_y):
    cell_x, cell_y = centre_x // coord_cell, centre_y // coord_cell
    rest_x, rest_y = centre_x % coord_cell, centre_y % coord_cell
    cells = jnp.arange(BUCKETS, dtype=jnp.int32)
    hot_x = (cell_x[:, None] == cells[None, :]).astype(BF16)
    hot_y = (cell_y[:, None] == cells[None, :]).astype(BF16)
    none = jnp.zeros_like(hot_x)
    hot_two = jnp.concatenate([hot_x, hot_y, hot_x, hot_y], axis=1)
    key_x = jnp.stack(
        [
            jnp.concatenate([hot_x, -hot_x, none, none], axis=1),
            jnp.concatenate([none, none, hot_x, -hot_x], axis=1),
        ]
    )
    key_y = jnp.stack(
        [
            jnp.concatenate([hot_y, -hot_y, none, none], axis=1),
            jnp.concatenate([none, none, hot_y, -hot_y], axis=1),
        ]
    )
    same = jnp.einsum("qcb,thb->thqc", HOT_SAME.astype(BF16), tables[1:], preferred_element_type=F32)
    less = jnp.einsum("qcb,thb->thqc", HOT_LESS.astype(BF16), tables[1:], preferred_element_type=F32)
    zero = jnp.zeros_like(same[0])
    base = jnp.concatenate(
        [jnp.concatenate([same[0], zero], axis=2), jnp.concatenate([zero, same[1]], axis=2)], axis=1
    )
    base = base.reshape(PAIRS, 2, 64, 64)[:, ::-1].reshape(HEADS, 64, 64)
    diff_x = jnp.concatenate([jnp.concatenate([less[0], same[0]], axis=2), jnp.zeros((HEADS, 32, 64), F32)], axis=1)
    diff_y = jnp.concatenate([jnp.zeros((HEADS, 32, 64), F32), jnp.concatenate([less[1], same[1]], axis=2)], axis=1)
    rows = jnp.concatenate([base, diff_x, diff_y], axis=0).astype(BF16)
    rows = rows.transpose(1, 0, 2).reshape(64, 3 * D)
    met = matmul(hot_two[:, :64], rows).astype(BF16)
    band = matmul(tables[0], jnp.asarray(BAND_HOT.T, BF16)).reshape(HEADS, 1, WIDE)
    rest_cols = jnp.stack([rest_x, rest_y], axis=1).astype(F32)
    rest_rows = rest_cols.T
    pad = jnp.zeros((WINLEN, LANES - chosen.shape[1]), BF16)
    marks = chosen.astype(BF16)
    mark_keys = jnp.concatenate([marks, pad], axis=1)
    mark_queries = jnp.concatenate([(1 - marks) * jnp.asarray(masked_score, BF16), pad], axis=1)
    return dict(
        hot_two=hot_two,
        key_x=key_x,
        key_y=key_y,
        met=met,
        band=band,
        rest_cols=rest_cols,
        rest_rows=rest_rows,
        mark_keys=mark_keys,
        mark_queries=mark_queries,
    )


def half_masks():
    lane = lax.broadcasted_iota(jnp.int32, (1, LANES), 1)
    low = (lane < HEAD_DIM).astype(F32)
    return low.astype(BF16), (1.0 - low).astype(BF16)


def less_masks(rest_cols, rest_rows, less_x, less_y):
    for part in range(BLOCKS):
        rows = slice(part * LANES, (part + 1) * LANES)
        for axis, less in ((0, less_x), (1, less_y)):
            column = rest_cols[rows, axis : axis + 1]
            row = rest_rows[axis : axis + 1, :]
            less[rows, :] = jnp.where(row < column, 1.0, 0.0).astype(less.dtype)


def attention_forward_kernel(
    q_ref, k_ref, v_ref, hot_ref, keyx_ref, keyy_ref, met_ref, band_ref, cols_ref, rows_ref,
    mkey_ref, mquery_ref, probs_ref, context_ref,
    kaug, qaug, less_x, less_y, wide, scores,
):
    low, high = half_masks()
    less_masks(cols_ref, rows_ref, less_x, less_y)
    kaug[:, LANES:] = mkey_ref[...]
    qaug[:, LANES:] = mquery_ref[...]
    half = 2 * LANES

    def one_pair(pair, carry):
        at = pl.multiple_of(pair * LANES, LANES)
        lanes = pl.ds(at, LANES)
        lanes_x = pl.ds(pl.multiple_of(at + D, LANES), LANES)
        lanes_y = pl.ds(pl.multiple_of(at + 2 * D, LANES), LANES)
        values_t = v_ref[:, lanes].T
        for odd in range(2):
            own, other = (low, high) if odd == 0 else (high, low)
            head = 2 * pair + odd
            kaug[:, :LANES] = k_ref[:, lanes] * own + hot_ref[...] * other
            qaug[:, :LANES] = q_ref[:, lanes] * own + met_ref[:, lanes] * other
            skew_band(band_ref[head], wide)
            for side in range(2):
                cols = slice(side * half, (side + 1) * half)
                top = None
                for part in range(BLOCKS):
                    rows = slice(part * LANES, (part + 1) * LANES)
                    s = times_transposed(kaug[rows, :], qaug[cols, :])
                    dx = times_transposed(keyx_ref[odd, rows, :], met_ref[cols, lanes_x])
                    dy = times_transposed(keyy_ref[odd, rows, :], met_ref[cols, lanes_y])
                    bias = []
                    for block in range(2 * side, 2 * side + 2):
                        step = max(-2, min(2, block - part)) + 2
                        bias.append(wide[:, step * LANES : (step + 1) * LANES])
                    s = s + jnp.concatenate(bias, axis=1)
                    s = s + dx * less_x[rows, cols] + dy * less_y[rows, cols]
                    scores[rows, :] = s
                    best = jnp.max(s, axis=0, keepdims=True)
                    top = best if top is None else jnp.maximum(top, best)
                total = None
                for part in range(BLOCKS):
                    rows = slice(part * LANES, (part + 1) * LANES)
                    e = jnp.exp(scores[rows, :] - top)
                    scores[rows, :] = e
                    add = jnp.sum(e, axis=0, keepdims=True)
                    total = add if total is None else total + add
                share = 1.0 / total
                for part in range(BLOCKS):
                    rows = slice(part * LANES, (part + 1) * LANES)
                    probs_ref[head, rows, cols] = (scores[rows, :] * share).astype(BF16)
                got = matmul(
                    values_t[odd * HEAD_DIM : (odd + 1) * HEAD_DIM, :], probs_ref[head, :, cols]
                )
                context_ref[pl.ds(pl.multiple_of(head * HEAD_DIM, HEAD_DIM), HEAD_DIM), cols] = (
                    got.astype(BF16)
                )
        return carry

    lax.fori_loop(0, PAIRS, one_pair, 0)


def skew_band(row, wide):
    x = jnp.broadcast_to(row, (8, WIDE))
    sub = lax.broadcasted_iota(jnp.int32, (8, WIDE), 0)
    for bit in (1, 2, 4):
        x = jnp.where((sub & bit) != 0, pltpu.roll(x, bit, 1), x)
    for group in range(LANES // 8):
        y = x if group == 0 else pltpu.roll(x, 8 * group, 1)
        wide[8 * group : 8 * group + 8, :] = y[:, : 5 * LANES]


def diagonal_sums(parts):
    total = None
    for group in range(LANES // 8):
        x = jnp.concatenate(
            [parts[8 * group : 8 * group + 8, LANES : 4 * LANES], jnp.zeros((8, LANES), F32)], axis=1
        )
        y = x if group == 0 else pltpu.roll(x, 4 * LANES - 8 * group, 1)
        total = y if total is None else total + y
    sub = lax.broadcasted_iota(jnp.int32, (8, 4 * LANES), 0)
    for bit in (1, 2, 4):
        total = jnp.where((sub & bit) != 0, pltpu.roll(total, 4 * LANES - bit, 1), total)
    return jnp.sum(total, axis=0, keepdims=True)


def attention_backward_kernel(
    q_ref, k_ref, v_ref, dctx_ref, probs_ref, hot_ref, cols_ref, rows_ref,
    dq_ref, dk_ref, dv_ref, cells_ref, diag_ref,
    qaug, less_x, less_y, scores, dscores, band, kept, hot_t,
):
    low, high = half_masks()
    less_masks(cols_ref, rows_ref, less_x, less_y)
    hot_t[...] = hot_ref[...].T
    lane = lax.broadcasted_iota(jnp.int32, (1, LANES), 1)
    scale = HEAD_DIM ** (-0.5)
    of_x = jnp.where((lane // BUCKETS) % 2 == 0, 1.0, 0.0)
    cells_x = hot_ref[...] * of_x.astype(BF16)
    cells_y = hot_ref[...] * (1.0 - of_x).astype(BF16)

    def one_pair(pair, carry):
        at = pl.multiple_of(pair * LANES, LANES)
        lanes = pl.ds(at, LANES)
        keys_t = k_ref[:, lanes].T
        for odd in range(2):
            own, other = (low, high) if odd == 0 else (high, low)
            head = 2 * pair + odd
            qaug[...] = q_ref[:, lanes] * own + hot_ref[...] * other
            dctx = dctx_ref[:, lanes]
            dot = None
            for part in range(BLOCKS):
                rows = slice(part * LANES, (part + 1) * LANES)
                dp = times_transposed(v_ref[rows, lanes] * own, dctx)
                scores[rows, :] = dp
                add = jnp.sum(dp * probs_ref[head, rows, :].astype(F32), axis=0, keepdims=True)
                dot = add if dot is None else dot + add
            band[...] = jnp.zeros_like(band)
            for part in range(BLOCKS):
                rows = slice(part * LANES, (part + 1) * LANES)
                probs = probs_ref[head, rows, :]
                ds = probs.astype(F32) * (scores[rows, :] - dot)
                for block in range(BLOCKS):
                    step = max(-2, min(2, block - part)) + 2
                    where = slice(step * LANES, (step + 1) * LANES)
                    band[:, where] = band[:, where] + ds[:, block * LANES : (block + 1) * LANES]
                ds = ds.astype(BF16)
                dscores[rows, :] = ds
                both = matmul(ds, qaug[...])
                less = matmul(ds * less_x[rows, :], cells_x) + matmul(ds * less_y[rows, :], cells_y)
                dv = matmul(probs, dctx)
                kept[odd, 0, rows, :] = both
                kept[odd, 1, rows, :] = less
                kept[odd, 2, rows, :] = dv
            got = matmul(keys_t[odd * HEAD_DIM : (odd + 1) * HEAD_DIM, :], dscores[...])
            dq_ref[pl.ds(pl.multiple_of(head * HEAD_DIM, HEAD_DIM), HEAD_DIM), :] = (
                got * scale
            ).astype(BF16)
            diag_ref[head, :, LANES : 5 * LANES] = diagonal_sums(band)
            diag_ref[head, :, :LANES] = jnp.sum(band[:, :LANES], axis=0, keepdims=True)
            diag_ref[head, :, 5 * LANES :] = jnp.sum(band[:, 4 * LANES :], axis=0, keepdims=True)
            for which in range(2):
                summed = kept[odd, which]
                first = summed.astype(BF16)
                rest = (summed - first.astype(F32)).astype(BF16)
                cells_ref[head, which] = matmul(hot_t[:64, :], first) + matmul(hot_t[:64, :], rest)
        dk_ref[:, lanes] = jnp.where(lane < HEAD_DIM, kept[0, 0], kept[1, 0]).astype(BF16)
        dv_ref[:, lanes] = jnp.where(lane < HEAD_DIM, kept[0, 2], kept[1, 2]).astype(BF16)
        return carry

    lax.fori_loop(0, PAIRS, one_pair, 0)


def attention_forward(queries, keys, values, ops):
    return pl.pallas_call(
        attention_forward_kernel,
        out_shape=(
            jax.ShapeDtypeStruct((HEADS, WINLEN, WINLEN), BF16),
            jax.ShapeDtypeStruct((D, WINLEN), BF16),
        ),
        scratch_shapes=[
            pltpu.VMEM((WINLEN, 2 * LANES), BF16),
            pltpu.VMEM((WINLEN, 2 * LANES), BF16),
            pltpu.VMEM((WINLEN, WINLEN), F32),
            pltpu.VMEM((WINLEN, WINLEN), F32),
            pltpu.VMEM((LANES, 5 * LANES), F32),
            pltpu.VMEM((WINLEN, 2 * LANES), F32),
        ],
        compiler_params=pltpu.CompilerParams(vmem_limit_bytes=48 * 2**20),
        name="attention_forward",
    )(
        queries, keys, values, ops["hot_two"], ops["key_x"], ops["key_y"], ops["met"], ops["band"],
        ops["rest_cols"], ops["rest_rows"], ops["mark_keys"], ops["mark_queries"],
    )


def attention_backward(queries, keys, values, grad_context, probs, ops):
    return pl.pallas_call(
        attention_backward_kernel,
        out_shape=(
            jax.ShapeDtypeStruct((D, WINLEN), BF16),
            jax.ShapeDtypeStruct((WINLEN, D), BF16),
            jax.ShapeDtypeStruct((WINLEN, D), BF16),
            jax.ShapeDtypeStruct((HEADS, 2, 64, LANES), F32),
            jax.ShapeDtypeStruct((HEADS, 1, WIDE), F32),
        ),
        scratch_shapes=[
            pltpu.VMEM((WINLEN, LANES), BF16),
            pltpu.VMEM((WINLEN, WINLEN), BF16),
            pltpu.VMEM((WINLEN, WINLEN), BF16),
            pltpu.VMEM((WINLEN, WINLEN), F32),
            pltpu.VMEM((WINLEN, WINLEN), BF16),
            pltpu.VMEM((LANES, 5 * LANES), F32),
            pltpu.VMEM((2, 3, WINLEN, LANES), F32),
            pltpu.VMEM((LANES, WINLEN), BF16),
        ],
        compiler_params=pltpu.CompilerParams(vmem_limit_bytes=48 * 2**20),
        name="attention_backward",
    )(
        queries, keys, values, grad_context, probs, ops["hot_two"], ops["rest_cols"],
        ops["rest_rows"],
    )


def table_grads(cells, diag):
    exact = lax.Precision.HIGHEST
    pairs = cells.reshape(PAIRS, 2, 2, 64, LANES)
    every = jnp.stack([pairs[:, 0, 0, :, 64:], pairs[:, 1, 0, :, :64]], axis=1).reshape(HEADS, 64, 64)
    less = cells[:, 1]
    less_x, less_y = less[:, :32, :32], less[:, 32:, 32:64]
    all_x, all_y = every[:, :32, :32], every[:, 32:, 32:]
    same = jnp.stack([all_x - less_x, all_y - less_y]).reshape(2 * HEADS, -1)
    below = jnp.stack([less_x, less_y]).reshape(2 * HEADS, -1)
    same_hot = jnp.asarray(HOT_SAME.transpose(1, 0, 2).reshape(-1, BUCKETS))
    less_hot = jnp.asarray(HOT_LESS.transpose(1, 0, 2).reshape(-1, BUCKETS))
    moved = jnp.dot(same, same_hot, precision=exact) + jnp.dot(below, less_hot, precision=exact)
    along = jnp.dot(diag.reshape(HEADS, WIDE), jnp.asarray(DIAG_HOT), precision=exact)
    return jnp.concatenate([along[None], moved.reshape(2, HEADS, BUCKETS)], axis=0)


COLUMNS = 4
CORES = 2
DEPTH = 4
USED = sum(math.prod(layout) for layout in layouts_list())
MATRICES = layouts_list()[:5]
MISC = sum(math.prod(layout) for layout in layouts_list()[5:])
MISC_ROWS = -(-MISC // (8 * LANES)) * 8


class Plan:
    def __init__(self, shard_len):
        self.rows = shard_len // LANES
        self.quarter = -(-self.rows // (16 * COLUMNS)) * 16
        self.padded = COLUMNS * self.quarter
        self.per_column = CORES * DEPTH * self.rows
        self.carry = 3 * LANES
        self.staged = self.carry + self.per_column + 3 * LANES
        starts = []
        offset = 0
        for depth, width in MATRICES:
            starts.append(offset // LANES)
            offset += depth * width
        self.starts = starts
        self.misc_start = offset // LANES


def fits(mesh):
    return mesh.shape["dp"] == COLUMNS * CORES and mesh.shape["head"] == DEPTH


MESH = pl.DeviceIdType.MESH


class Place:
    def __init__(self):
        dp = lax.axis_index("dp")
        self.z = lax.axis_index("head")
        self.core = dp % CORES
        self.column = dp // CORES
        self.x = self.column % 2
        self.y = self.column // 2
        self.col_x = 2 * self.y + (1 - self.x)
        self.col_y = 2 * (1 - self.y) + self.x
        self.col_d = 2 * (1 - self.y) + (1 - self.x)
        self.peer_x = self.at(self.col_x, self.core, self.z)
        self.peer_y = self.at(self.col_y, self.core, self.z)
        self.peer_d = self.at(self.col_d, self.core, self.z)
        self.peer_core = self.at(self.column, 1 - self.core, self.z)
        self.far = [lax.rem(self.z + d, DEPTH) for d in range(1, DEPTH)]
        self.from_far = [lax.rem(self.z + DEPTH - d, DEPTH) for d in range(1, DEPTH)]
        self.peers_z = [self.at(self.column, self.core, f) for f in self.far]

    def at(self, column, core, z):
        return {"dp": column * CORES + core, "head": z}

    def greet(self):
        barrier = pltpu.get_barrier_semaphore()
        peers = [self.peer_x, self.peer_y, self.peer_d, self.peer_core] + self.peers_z
        for peer in peers:
            pl.semaphore_signal(barrier, inc=1, device_id=peer, device_id_type=MESH)
        pl.semaphore_wait(barrier, len(peers))


def remote(src, dst, send_sem, recv_sem, peer):
    return pltpu.make_async_remote_copy(
        src_ref=src, dst_ref=dst, send_sem=send_sem, recv_sem=recv_sem, device_id=peer,
        device_id_type=MESH,
    )


class Gathering:
    def __init__(self, place, flat, sems):
        self.place = place
        self.flat = flat
        self.sems = sems
        self.sent = []

    def send(self, src, dst, kind, index, peer):
        copy = remote(src, dst, self.sems[kind].at[0, index], self.sems[kind].at[1, index], peer)
        copy.start()
        self.sent.append(copy)

    def got(self, dst, kind, index):
        remote(
            dst, dst, self.sems[kind].at[0, index], self.sems[kind].at[1, index], self.place.peer_x
        ).wait_recv()

    def spread(self, own):
        p = self.place
        for index, (column, peer) in enumerate(
            ((p.col_x, p.peer_x), (p.col_y, p.peer_y), (p.col_d, p.peer_d))
        ):
            self.send(
                own.at[column], self.flat.at[p.column, p.core, p.z, column], "spread", index, peer
            )
        self.flat[p.column, p.core, p.z, p.column] = own[p.column]

    def spread_done(self):
        p = self.place
        for index, column in enumerate((p.col_x, p.col_y, p.col_d)):
            self.got(self.flat.at[column, p.core, p.z, p.column], "spread", index)

    def along_z(self, k):
        p = self.place
        piece = self.flat.at[k, p.core, p.z, p.column]
        for d in range(DEPTH - 1):
            self.send(piece, piece, "z", 3 * k + d, p.peers_z[d])

    def first(self, k):
        p = self.place
        for d in range(DEPTH - 1):
            self.got(self.flat.at[k, p.core, p.from_far[d], p.column], "z", 3 * k + d)
        piece = self.flat.at[k, p.core, :, p.column]
        self.send(piece, piece, "one", 2 * k, p.peer_x)
        self.send(piece, piece, "one", 2 * k + 1, p.peer_y)
        self.send(piece, piece, "core", 5 * k, p.peer_core)

    def second(self, k):
        p = self.place
        from_x = self.flat.at[k, p.core, :, p.col_x]
        self.got(from_x, "one", 2 * k)
        part = self.flat.at[k, p.core, 0:2, p.col_x]
        self.send(part, part, "two", 2 * k, p.peer_y)
        self.send(from_x, from_x, "core", 5 * k + 1, p.peer_core)
        from_y = self.flat.at[k, p.core, :, p.col_y]
        self.got(from_y, "one", 2 * k + 1)
        part = self.flat.at[k, p.core, 2:4, p.col_y]
        self.send(part, part, "two", 2 * k + 1, p.peer_x)
        self.send(from_y, from_y, "core", 5 * k + 2, p.peer_core)

    def third(self, k):
        p = self.place
        part = self.flat.at[k, p.core, 0:2, p.col_d]
        self.got(part, "two", 2 * k)
        self.send(part, part, "core", 5 * k + 3, p.peer_core)
        part = self.flat.at[k, p.core, 2:4, p.col_d]
        self.got(part, "two", 2 * k + 1)
        self.send(part, part, "core", 5 * k + 4, p.peer_core)

    def complete(self, k):
        p = self.place
        other = 1 - p.core
        for index, column in enumerate((p.column, p.col_x, p.col_y)):
            self.got(self.flat.at[k, other, :, column], "core", 5 * k + index)
        self.got(self.flat.at[k, other, 0:2, p.col_d], "core", 5 * k + 3)
        self.got(self.flat.at[k, other, 2:4, p.col_d], "core", 5 * k + 4)

    def finish(self):
        for copy in self.sent:
            copy.wait_send()


GATHER_SEMS = {"spread": 3, "z": 12, "one": 8, "two": 8, "core": 20}


def sem_shapes(counts):
    return [pltpu.SemaphoreType.DMA((2, count)) for count in counts.values()]


def stage_column(plan, flat, staged, k):
    def one(shard, carry):
        core, z = shard // DEPTH, shard % DEPTH
        for quarter in range(COLUMNS):
            base = plan.carry + shard * plan.rows + quarter * plan.quarter
            staged[pl.ds(pl.multiple_of(base, 8), plan.quarter), :] = flat[k, core, z, quarter].astype(F32)
        return carry

    lax.fori_loop(0, CORES * DEPTH, one, 0)


def keep_carry(plan, staged):
    end = plan.carry + plan.per_column
    staged[: plan.carry, :] = staged[end - plan.carry : end, :]


ROW_STEP = 48


def column_rows(plan, k, touching):
    low, high = k * plan.per_column, (k + 1) * plan.per_column
    taken = []
    for index, (depth, width) in enumerate(MATRICES):
        group = 16 * (width // LANES)
        from_low, from_high = low - plan.starts[index], high - plan.starts[index]
        begin = max(0, min(depth, from_low // group * 16))
        if touching:
            end = max(0, min(depth, -(-from_high // group) * 16))
        else:
            end = max(0, min(depth, from_high // group * 16))
        if end > begin:
            taken.append((index, begin, end))
    return taken


def staged_at(plan, k, row):
    return plan.carry + row - k * plan.per_column


def row_loops(rows):
    whole = rows // ROW_STEP
    loops = [(ROW_STEP, 0, whole)] if whole else []
    if rows % ROW_STEP:
        loops.append((16, whole * ROW_STEP, (rows % ROW_STEP) // 16))
    return loops


def form_matrices(plan, staged, matrices, k):
    for index, begin, end in column_rows(plan, k, False):
        blocks = MATRICES[index][1] // LANES
        base = staged_at(plan, k, plan.starts[index] + begin * blocks)
        assert 0 <= base
        target = matrices[index]
        for step_rows, first, count in row_loops(end - begin):

            def one(step, carry, step_rows=step_rows, first=first, blocks=blocks, base=base,
                    begin=begin, target=target):
                row = first + step * step_rows
                for block in range(blocks):
                    got = staged[pl.ds(base + row * blocks + block, step_rows, stride=blocks), :]
                    target[
                        pl.ds(pl.multiple_of(begin + row, 16), step_rows),
                        block * LANES : (block + 1) * LANES,
                    ] = got.astype(BF16)
                return carry

            lax.fori_loop(0, count, one, 0)


class Reducing:
    def __init__(self, place, flat, swapped, one, two, deep, piece, result, sems):
        self.place = place
        self.flat = flat
        self.swapped = swapped
        self.one = one
        self.two = two
        self.deep = deep
        self.piece = piece
        self.result = result
        self.sems = sems
        self.sent = []

    send = Gathering.send
    got = Gathering.got
    finish = Gathering.finish

    def swap(self, k):
        p = self.place
        self.send(self.flat.at[k, 1 - p.core], self.swapped.at[k], "core", k, p.peer_core)

    def first(self, k):
        p = self.place
        self.got(self.swapped.at[k], "core", k)

        def one(step, carry):
            z, quarter = step // COLUMNS, step % COLUMNS
            total = self.flat[k, p.core, z, quarter].astype(F32)
            total = total + self.swapped[k, z, quarter].astype(F32)
            self.flat[k, p.core, z, quarter] = total.astype(BF16)
            return carry

        lax.fori_loop(0, DEPTH * COLUMNS, one, 0)
        self.send(self.flat.at[k, p.core, 0:2, p.col_d], self.one.at[k, 0], "one", 2 * k, p.peer_y)
        self.send(
            self.flat.at[k, p.core, 2:4, p.col_d], self.one.at[k, 1], "one", 2 * k + 1, p.peer_x
        )

    def second(self, k):
        p = self.place
        for side, column in ((0, p.col_x), (1, p.col_y)):
            self.got(self.one.at[k, side], "one", 2 * k + side)

            def one(step, carry, side=side, column=column):
                z = 2 * side + step
                total = self.flat[k, p.core, z, column].astype(F32)
                total = total + self.one[k, side, step].astype(F32)
                self.flat[k, p.core, z, column] = total.astype(BF16)
                return carry

            lax.fori_loop(0, 2, one, 0)
        self.send(self.flat.at[k, p.core, :, p.col_x], self.two.at[k, 0], "two", 2 * k, p.peer_x)
        self.send(self.flat.at[k, p.core, :, p.col_y], self.two.at[k, 1], "two", 2 * k + 1, p.peer_y)

    def third(self, k):
        p = self.place
        for side in range(2):
            self.got(self.two.at[k, side], "two", 2 * k + side)

        def one(z, carry):
            total = self.flat[k, p.core, z, p.column].astype(F32)
            total = total + self.two[k, 0, z].astype(F32) + self.two[k, 1, z].astype(F32)
            self.flat[k, p.core, z, p.column] = total.astype(BF16)
            return carry

        lax.fori_loop(0, DEPTH, one, 0)
        for d in range(DEPTH - 1):
            self.send(
                self.flat.at[k, p.core, p.far[d], p.column], self.deep.at[k, d], "z", 3 * k + d,
                p.peers_z[d],
            )

    def fourth(self, k):
        p = self.place
        for d in range(DEPTH - 1):
            self.got(self.deep.at[k, d], "z", 3 * k + d)
        total = self.flat[k, p.core, p.z, p.column].astype(F32)
        for d in range(DEPTH - 1):
            total = total + self.deep[k, d].astype(F32)
        self.piece[k] = total.astype(BF16)

    def give_back(self):
        p = self.place
        for index, (column, peer) in enumerate(
            ((p.col_x, p.peer_x), (p.col_y, p.peer_y), (p.col_d, p.peer_d))
        ):
            self.send(self.piece.at[column], self.result.at[index], "spread", index, peer)

    def receive(self, out):
        p = self.place
        out[p.column] = self.piece[p.column].astype(F32)
        for index, column in enumerate((p.col_x, p.col_y, p.col_d)):
            self.got(self.result.at[index], "spread", index)
            out[column] = self.result[index].astype(F32)


REDUCE_SEMS = {"spread": 3, "z": 12, "one": 8, "two": 8, "core": 4}


def flatten_matrices(plan, staged, matrices, k):
    for index, begin, end in column_rows(plan, k, True):
        blocks = MATRICES[index][1] // LANES
        base = staged_at(plan, k, plan.starts[index] + begin * blocks)
        source = matrices[index]
        for step_rows, first, count in row_loops(end - begin):

            def one(step, carry, step_rows=step_rows, first=first, blocks=blocks, base=base,
                    begin=begin, source=source):
                row = first + step * step_rows
                for block in range(blocks):
                    got = source[
                        pl.ds(pl.multiple_of(begin + row, 16), step_rows),
                        block * LANES : (block + 1) * LANES,
                    ]
                    staged[pl.ds(base + row * blocks + block, step_rows, stride=blocks), :] = (
                        got.astype(F32)
                    )
                return carry

            lax.fori_loop(0, count, one, 0)


def unstage_column(plan, flat, staged, k):
    def one(step, carry):
        shard, quarter = step // COLUMNS, step % COLUMNS
        base = plan.carry + shard * plan.rows + quarter * plan.quarter
        piece = staged[pl.ds(pl.multiple_of(base, 8), plan.quarter), :]
        flat[k, shard // DEPTH, shard % DEPTH, quarter] = piece.astype(BF16)
        return carry

    lax.fori_loop(0, CORES * DEPTH * COLUMNS, one, 0)


def reduce_kernel(plan, *refs):
    grads, misc, refs = refs[:5], refs[5], refs[6:]
    out, refs = refs[0], refs[1:]
    flat, staged, refs = refs[0], refs[1], refs[2:]
    buffers, refs = refs[:6], refs[6:]
    place = Place()
    reducing = Reducing(place, flat, *buffers, dict(zip(REDUCE_SEMS, refs)))
    end = plan.carry + plan.per_column
    staged[end:, :] = jnp.zeros((plan.staged - end, LANES), F32)
    flatten_matrices(plan, staged, grads, 3)
    at = staged_at(plan, 3, plan.misc_start)
    staged[at : at + MISC_ROWS, :] = misc[...]
    staged[at + MISC_ROWS : end, :] = jnp.zeros((end - at - MISC_ROWS, LANES), F32)
    unstage_column(plan, flat, staged, 3)
    place.greet()
    reducing.swap(3)
    flatten_matrices(plan, staged, grads, 2)
    unstage_column(plan, flat, staged, 2)
    reducing.swap(2)
    flatten_matrices(plan, staged, grads, 1)
    unstage_column(plan, flat, staged, 1)
    flatten_matrices(plan, staged, grads, 0)
    unstage_column(plan, flat, staged, 0)
    reducing.first(3)
    reducing.swap(1)
    reducing.first(2)
    reducing.swap(0)
    reducing.second(3)
    reducing.first(1)
    reducing.second(2)
    reducing.third(3)
    reducing.first(0)
    reducing.second(1)
    reducing.third(2)
    reducing.fourth(3)
    reducing.second(0)
    reducing.third(1)
    reducing.fourth(2)
    reducing.third(0)
    reducing.fourth(1)
    reducing.fourth(0)
    reducing.give_back()
    reducing.receive(out)
    reducing.finish()


def reduce_grads(plan, grads, misc):
    vmem = pl.BlockSpec(memory_space=pltpu.VMEM)
    block = (plan.quarter, LANES)
    return pl.pallas_call(
        functools.partial(reduce_kernel, plan),
        out_shape=jax.ShapeDtypeStruct((COLUMNS,) + block, F32),
        in_specs=[vmem] * 6,
        out_specs=vmem,
        scratch_shapes=[
            pltpu.VMEM((COLUMNS, CORES, DEPTH, COLUMNS) + block, BF16),
            pltpu.VMEM((plan.staged, LANES), F32),
            pltpu.VMEM((COLUMNS, DEPTH, COLUMNS) + block, BF16),
            pltpu.VMEM((COLUMNS, 2, 2) + block, BF16),
            pltpu.VMEM((COLUMNS, 2, DEPTH) + block, BF16),
            pltpu.VMEM((COLUMNS, DEPTH - 1) + block, BF16),
            pltpu.VMEM((COLUMNS,) + block, BF16),
            pltpu.VMEM((3,) + block, BF16),
        ]
        + sem_shapes(REDUCE_SEMS),
        compiler_params=pltpu.CompilerParams(
            collective_id=1, has_side_effects=True, vmem_limit_bytes=62 * 2**20
        ),
        name="reduce_grads",
    )(*grads, misc)


def adam_step(params, moment_one, moment_two, grads, flat_index):
    box_part = (flat_index >= 4 * D * D) & (flat_index < 5 * D * D)
    step_rate = jnp.where(box_part, base_rate * layer_decay**12, base_rate * layer_decay)
    decay_mask = jnp.where(flat_index < 5 * D * D + 2 * D * FF, decay_weight, 0.0)
    moment_one = beta_one * moment_one + (1.0 - beta_one) * grads
    moment_two = beta_two * moment_two + (1.0 - beta_two) * grads * grads
    first_hat = moment_one / (1.0 - beta_one**adam_count)
    second_hat = moment_two / (1.0 - beta_two**adam_count)
    update = first_hat / (jnp.sqrt(second_hat) + adam_eps) + decay_mask * params
    return (-step_rate * update, moment_one)


VEC = {}
_at = 0
for _name, _rows in (
    ("q_bias", 6), ("v_bias", 6), ("out_bias", 6), ("gain_one", 6), ("shift_one", 6), ("in_bias", 24),
    ("back_bias", 6), ("gain_two", 6), ("shift_two", 6), ("tables", 9),
):
    VEC[_name] = _at * LANES
    _at += _rows
VEC_ROWS = _at
NOTE_ROWS = 96
NBLOCK = 2 * LANES


def note_place(plan):
    row = plan.misc_start - (CORES * DEPTH * COLUMNS - 1) * plan.rows
    quarter, row = row // plan.quarter, row % plan.quarter
    first = row // 16 * 16
    assert first + NOTE_ROWS <= plan.quarter and row - first + VEC_ROWS <= NOTE_ROWS
    return quarter, first, row - first


def spread_notes(place, own, notes, sems, plan):
    quarter, first, _ = note_place(plan)
    source = own.at[quarter, first : first + NOTE_ROWS]
    home = (place.column == COLUMNS - 1) & (place.core == CORES - 1)
    root = home & (place.z == DEPTH - 1)

    def copy(src, index, peer):
        return remote(src, notes, sems.at[0, index], sems.at[1, 0], peer)

    def arrived():
        copy(notes, 0, place.peer_core).wait_recv()

    @pl.when(root)
    def _():
        notes[...] = own[quarter, first : first + NOTE_ROWS]
        for index, peer in enumerate(place.peers_z):
            copy(source, index, peer).start()

    @pl.when(home & (place.z != DEPTH - 1))
    def _():
        arrived()

    @pl.when(home)
    def _():
        for index, peer in enumerate((place.peer_x, place.peer_y, place.peer_d)):
            copy(notes, 3 + index, peer).start()

    @pl.when((place.core == CORES - 1) & (place.column != COLUMNS - 1))
    def _():
        arrived()

    @pl.when(place.core == CORES - 1)
    def _():
        copy(notes, 6, place.peer_core).start()

    @pl.when(place.core != CORES - 1)
    def _():
        arrived()

    def finish():
        @pl.when(root)
        def _():
            for index, peer in enumerate(place.peers_z):
                copy(source, index, peer).wait_send()

        @pl.when(home)
        def _():
            for index, peer in enumerate((place.peer_x, place.peer_y, place.peer_d)):
                copy(notes, 3 + index, peer).wait_send()

        @pl.when(place.core == CORES - 1)
        def _():
            copy(notes, 6, place.peer_core).wait_send()

    return finish


def turns_table():
    count_freq = D // 8
    freq = np.exp(np.arange(count_freq) * (-math.log(1000.0) / count_freq)) / (2 * math.pi)
    per = np.concatenate([freq, freq])
    phase = np.concatenate([np.zeros(count_freq), np.full(count_freq, 0.25)])
    return np.stack([np.tile(per, 4), np.tile(phase, 4)]).astype(np.float32)


def sin_turns(t):
    t = t - jnp.floor(t + 0.5)
    a = jnp.abs(t)
    m = jnp.minimum(a, 0.5 - a) * (2 * math.pi)
    u = m * m
    poly = -1.0 / 39916800.0
    for term in (1.0 / 362880.0, -1.0 / 5040.0, 1.0 / 120.0, -1.0 / 6.0, 1.0):
        poly = poly * u + term
    s = m * poly
    return jnp.where(t < 0, -s, s)


def token_columns(info):
    coords = info[0:4, :]
    doc, first = info[4:5, :], info[5:6, :]
    anchor = jnp.zeros_like(coords)
    for d in range(4):
        mine = jnp.where(doc == float(d), 1.0, 0.0)
        value = jnp.sum(coords * (mine * first), axis=1, keepdims=True)
        anchor = anchor + value * mine
    anchor = jnp.concatenate([anchor[0:2], anchor[0:2]], axis=0)
    relative = coords - anchor
    centre = jnp.floor((coords[0:2] + coords[2:4]) * 0.5)
    cell = jnp.floor(centre * (1.0 / coord_cell))
    rest = centre - cell * coord_cell
    rows = jnp.concatenate(
        [relative, cell, rest, doc, jnp.zeros((LANES - 9, WINLEN), F32)], axis=0
    )
    return rest, rows.T


def form_features(columns, turns_ref, features):
    lane = lax.broadcasted_iota(jnp.int32, (1, LANES), 1)
    for block in range(D // LANES):
        lanes = slice(block * LANES, (block + 1) * LANES)
        low, high = block * LANES // (D // 4), ((block + 1) * LANES - 1) // (D // 4)
        value = columns[:, low : low + 1]
        if high != low:
            value = jnp.where(
                lane + block * LANES < high * (D // 4), value, columns[:, high : high + 1]
            )
        t = value * turns_ref[0:1, lanes] + turns_ref[1:2, lanes]
        features[:, lanes] = sin_turns(t).astype(BF16)


def form_hots(columns, hot_ref, keyx_ref, keyy_ref, mkey, mquery):
    lane = lax.broadcasted_iota(jnp.int32, (1, LANES), 1)
    part = lane // BUCKETS
    cell = (lane % BUCKETS).astype(F32)
    is_x = jnp.where(columns[:, 4:5] == cell, 1.0, 0.0)
    is_y = jnp.where(columns[:, 5:6] == cell, 1.0, 0.0)
    hot_ref[...] = jnp.where(part % 2 == 0, is_x, is_y).astype(BF16)
    sign = jnp.where(part % 2 == 0, 1.0, -1.0)
    for odd in range(2):
        here = jnp.where(part // 2 == odd, sign, 0.0)
        keyx_ref[odd] = (is_x * here).astype(BF16)
        keyy_ref[odd] = (is_y * here).astype(BF16)
    doc = jnp.where(columns[:, 8:9] == lane.astype(F32), 1.0, 0.0)
    mkey[...] = doc.astype(BF16)
    mquery[...] = (jnp.where(lane < 4, 1.0 - doc, 0.0) * masked_score).astype(BF16)


def form_tables(tables, bands, tilted):
    row = lax.broadcasted_iota(jnp.int32, (LANES, 1), 0)
    half = BUCKETS // 2
    sub = lax.broadcasted_iota(jnp.int32, (8, LANES), 0)
    place = lax.broadcasted_iota(jnp.int32, (1, WIDE), 1)
    wanted = jnp.where(place < 5 * LANES, jnp.clip(place - 2 * LANES, -half, half - 1) + half, 0)
    lane = lax.broadcasted_iota(jnp.int32, (1, LANES), 1)
    turned = jnp.clip(64 - lane, -half, half - 1) + half
    for m in range(4):
        hot_band = jnp.where(row == wanted + m * BUCKETS, 1.0, 0.0).astype(BF16)
        got = matmul(tables, hot_band)
        for n in range(3):
            bands[4 * n + m] = got[n : n + 1, :]
        hot_turn = jnp.where(row == turned + m * BUCKETS, 1.0, 0.0).astype(BF16)
        got = matmul(tables, hot_turn)
        for t in (1, 2):
            for n in range(3):
                x = jnp.broadcast_to(got[3 * t + n : 3 * t + n + 1, :], (8, LANES))
                for bit in (1, 2, 4):
                    x = jnp.where((sub & bit) != 0, pltpu.roll(x, bit, 1), x)
                for group in range(BUCKETS // 8):
                    y = x if group == 0 else pltpu.roll(x, 8 * group, 1)
                    tilted[(t - 1) * HEADS + 4 * n + m, 8 * group : 8 * group + 8, :] = y


def pair_rows(tilted, pair):
    lane = lax.broadcasted_iota(jnp.int32, (1, LANES), 1)
    part = lane // BUCKETS
    x0, x1 = tilted[2 * pair], tilted[2 * pair + 1]
    y0, y1 = tilted[HEADS + 2 * pair], tilted[HEADS + 2 * pair + 1]

    def same(value, to):
        return value if to == 64 else pltpu.roll(value, (to - 64) % LANES, 1)

    def less(value, to):
        return pltpu.roll(value, (to - 65) % LANES, 1)

    zero = jnp.zeros_like(x0)
    base_x = jnp.where(part == 0, same(x1, 0), jnp.where(part == 2, same(x0, 64), zero))
    base_y = jnp.where(part == 1, same(y1, 32), jnp.where(part == 3, same(y0, 96), zero))

    def steps(even, odd):
        return jnp.where(
            part < 2,
            jnp.where(part == 0, less(even, 0), same(even, 32)),
            jnp.where(part == 2, less(odd, 64), same(odd, 96)),
        )

    rows = [
        jnp.concatenate([base_x, base_y], axis=0),
        jnp.concatenate([steps(x0, x1), zero], axis=0),
        jnp.concatenate([zero, steps(y0, y1)], axis=0),
    ]
    return jnp.concatenate(rows, axis=1).astype(BF16)


def gelu_and_slope(z):
    a = jnp.abs(z)
    t = 1.0 / (1.0 + (0.3275911 / math.sqrt(2.0)) * a)
    poly = 1.061405429 * 0.5
    for term in (-1.453152027, 1.421413741, -0.284496736, 0.254829592):
        poly = poly * t + 0.5 * term
    e = jnp.exp(-0.5 * z * z)
    tail = poly * t * e
    cdf = jnp.where(z < 0, tail, 1.0 - tail)
    return z * cdf, cdf + z * (e * (1.0 / math.sqrt(2.0 * math.pi)))


def forward_kernel(plan, own, hidden_in, cot_in, info, turns, *refs):
    (w_qkv_out, w_out_out, w_in_out, w_back_out, features_out, low_out, q_out, k_out, v_out, probs_out,
     context_out, hat_out, normed_out, active_out, slope_out, second_out, vec_out, rstd_out, gain_grads,
     output_ref, cot_ref, hot_out, rest_out) = refs[:23]
    refs = refs[23:]
    (flat, staged, w_qkv, w_out, w_box, w_in, w_back, notes, features, hidden, start, start_low, q_ref,
     k_ref, v_ref, hot_ref, key_x, key_y, less_x, less_y, bands, tilted, met, kaug, qaug, wide, scores,
     probs, context_t, pair_t, hat, active, slope, vec) = refs[:34]
    note_sems, swap_sems, copy_sems, probs_sems = refs[34:38]
    place = Place()
    normed_low = hidden
    context = features
    gathering = Gathering(place, flat, dict(zip(GATHER_SEMS, refs[38:])))
    matrices = (w_qkv, w_out, w_box, w_in, w_back)
    written = []

    def write_out(src, dst):
        copy = pltpu.make_async_copy(src, dst, copy_sems.at[len(written)])
        copy.start()
        written.append(copy)

    place.greet()
    finish_notes = None
    gathering.spread(own)

    quarter = WINLEN // DEPTH

    def exchange(source, target, kind):
        rows = pl.ds(pl.multiple_of(place.z * quarter, quarter), quarter)
        for d in range(DEPTH - 1):
            gathering_send(source.at[place.far[d]], target.at[rows], kind, d, place.peers_z[d])

    def gathering_send(src, dst, kind, d, peer):
        copy = remote(src, dst, swap_sems.at[kind, 0, d], swap_sems.at[kind, 1, d], peer)
        copy.start()
        gathering.sent.append(copy)

    def exchanged(target, kind):
        for d in range(DEPTH - 1):
            rows = pl.ds(pl.multiple_of(place.from_far[d] * quarter, quarter), quarter)
            remote(
                target.at[rows], target.at[rows], swap_sems.at[kind, 0, d], swap_sems.at[kind, 1, d],
                place.peer_x,
            ).wait_recv()

    exchange(hidden_in, hidden, 0)
    finish_notes = spread_notes(place, own, notes, note_sems, plan)
    own_rows = pl.ds(pl.multiple_of(place.z * quarter, quarter), quarter)
    own_hidden = pltpu.make_async_copy(
        hidden_in.at[place.z], hidden.at[own_rows], swap_sems.at[0, 0, DEPTH - 1]
    )
    own_hidden.start()
    own_cot = pltpu.make_async_copy(
        cot_in.at[place.z], cot_ref.at[own_rows], swap_sems.at[1, 0, DEPTH - 1]
    )
    own_cot.start()
    gathering.spread_done()
    gathering.along_z(0)
    gathering.along_z(1)

    rest, columns = token_columns(info[...])
    for part in range(BLOCKS):
        rows = slice(part * LANES, (part + 1) * LANES)
        for axis, less in ((0, less_x), (1, less_y)):
            less[rows, :] = jnp.where(
                rest[axis : axis + 1, :] < columns[rows, 6 + axis : 7 + axis], 1.0, 0.0
            ).astype(BF16)
    rest_out[...] = rest
    form_hots(columns, hot_ref, key_x, key_y, kaug.at[:, LANES:], qaug.at[:, LANES:])
    hot_out[...] = hot_ref[...]
    form_features(columns, turns, features)
    write_out(features, features_out)
    _, _, note_row = note_place(plan)
    for row in range(VEC_ROWS):
        at = note_row + row
        vec[0:1, row * LANES : (row + 1) * LANES] = notes[at // 16 * 16 : at // 16 * 16 + 16, :].astype(
            F32
        )[at % 16 : at % 16 + 1, :]
    vec_out[...] = vec[...]
    table_row = note_row + VEC["tables"] // LANES
    assert table_row % 16 == 0
    form_tables(notes[table_row : table_row + 16, :], bands, tilted)

    gathering.first(0)
    gathering.along_z(2)
    gathering.first(1)
    gathering.along_z(3)
    exchange(cot_in, cot_ref, 1)
    gathering.second(0)
    gathering.first(2)
    gathering.third(0)
    gathering.second(1)
    gathering.complete(0)
    stage_column(plan, flat, staged, 0)
    form_matrices(plan, staged, matrices, 0)
    keep_carry(plan, staged)
    gathering.first(3)
    gathering.third(1)
    gathering.second(2)
    gathering.complete(1)
    stage_column(plan, flat, staged, 1)
    form_matrices(plan, staged, matrices, 1)
    keep_carry(plan, staged)
    write_out(w_qkv, w_qkv_out)
    write_out(w_out, w_out_out)

    exchanged(hidden, 0)
    own_hidden.wait()
    for n in range(D // NBLOCK):
        lanes = slice(n * NBLOCK, (n + 1) * NBLOCK)
        value = hidden[:, lanes].astype(F32) + matmul(features[...], w_box[:, lanes])
        start[:, lanes] = value
        start_low[:, lanes] = value.astype(BF16)
    write_out(start_low, low_out)
    written[0].wait()

    def project(n, carry):
        at = pl.multiple_of(n * NBLOCK, NBLOCK)
        lanes = pl.ds(at, NBLOCK)
        low = start_low[...]
        bias = vec[0:1, pl.ds(pl.multiple_of(VEC["q_bias"] + at, LANES), NBLOCK)]
        got = matmul(low, w_qkv[:, lanes]) + bias
        q_ref[:, lanes] = (got.astype(BF16).astype(F32) * HEAD_DIM ** (-0.5)).astype(BF16)
        k_ref[:, lanes] = matmul(low, w_qkv[:, pl.ds(pl.multiple_of(at + D, LANES), NBLOCK)]).astype(BF16)
        bias = vec[0:1, pl.ds(pl.multiple_of(VEC["v_bias"] + at, LANES), NBLOCK)]
        got = matmul(low, w_qkv[:, pl.ds(pl.multiple_of(at + 2 * D, LANES), NBLOCK)]) + bias
        v_ref[:, lanes] = got.astype(BF16)
        return carry

    lax.fori_loop(0, D // NBLOCK, project, 0)
    write_out(q_ref, q_out)
    write_out(k_ref, k_out)
    write_out(v_ref, v_out)
    gathering.third(2)
    gathering.second(3)

    low, high = half_masks()
    half = 2 * LANES

    def probs_copy(head, odd):
        return pltpu.make_async_copy(probs.at[odd], probs_out.at[head], probs_sems.at[odd])

    def one_pair(pair, carry):
        at = pl.multiple_of(pair * LANES, LANES)
        lanes = pl.ds(at, LANES)
        values_t = v_ref[:, lanes].T
        met[...] = matmul(hot_ref[:, :64], pair_rows(tilted, pair)).astype(BF16)
        for odd in range(2):
            mine, other = (low, high) if odd == 0 else (high, low)
            head = 2 * pair + odd
            kaug[:, :LANES] = k_ref[:, lanes] * mine + hot_ref[...] * other
            qaug[:, :LANES] = q_ref[:, lanes] * mine + met[:, :LANES] * other
            skew_band(bands[head], wide)

            @pl.when(pair > 0)
            def _():
                probs_copy(head, odd).wait()

            for side in range(2):
                cols = slice(side * half, (side + 1) * half)
                top = None
                for part in range(BLOCKS):
                    rows = slice(part * LANES, (part + 1) * LANES)
                    s = times_transposed(kaug[rows, :], qaug[cols, :])
                    dx = times_transposed(key_x[odd, rows, :], met[cols, LANES : 2 * LANES])
                    dy = times_transposed(key_y[odd, rows, :], met[cols, 2 * LANES :])
                    bias = []
                    for block in range(2 * side, 2 * side + 2):
                        step = max(-2, min(2, block - part)) + 2
                        bias.append(wide[:, step * LANES : (step + 1) * LANES])
                    s = s + jnp.concatenate(bias, axis=1)
                    s = s + dx * less_x[rows, cols].astype(F32) + dy * less_y[rows, cols].astype(F32)
                    scores[rows, :] = s
                    best = jnp.max(s, axis=0, keepdims=True)
                    top = best if top is None else jnp.maximum(top, best)
                total = None
                for part in range(BLOCKS):
                    rows = slice(part * LANES, (part + 1) * LANES)
                    e = jnp.exp(scores[rows, :] - top)
                    scores[rows, :] = e
                    add = jnp.sum(e, axis=0, keepdims=True)
                    total = add if total is None else total + add
                share = 1.0 / total
                for part in range(BLOCKS):
                    rows = slice(part * LANES, (part + 1) * LANES)
                    probs[odd, rows, cols] = (scores[rows, :] * share).astype(BF16)
                got = matmul(values_t[odd * HEAD_DIM : (odd + 1) * HEAD_DIM, :], probs[odd, :, cols])
                pair_t[odd * HEAD_DIM : (odd + 1) * HEAD_DIM, cols] = got
            probs_copy(head, odd).start()
        both = pair_t[...]
        context_t[lanes, :] = both.astype(BF16)
        context[:, lanes] = both.T.astype(BF16)
        return carry

    lax.fori_loop(0, 2, one_pair, 0)
    gathering.third(3)
    gathering.complete(2)
    stage_column(plan, flat, staged, 2)
    form_matrices(plan, staged, matrices, 2)
    keep_carry(plan, staged)
    write_out(w_in, w_in_out)
    lax.fori_loop(2, PAIRS, one_pair, 0)
    write_out(context_t, context_out)
    gathering.complete(3)
    stage_column(plan, flat, staged, 3)
    form_matrices(plan, staged, matrices, 3)
    write_out(w_back, w_back_out)

    def vector(name):
        return vec[0:1, VEC[name] : VEC[name] + D]

    for n in range(D // NBLOCK):
        lanes = slice(n * NBLOCK, (n + 1) * NBLOCK)
        bias = vec[0:1, VEC["out_bias"] + n * NBLOCK : VEC["out_bias"] + (n + 1) * NBLOCK]
        start[:, lanes] = start[:, lanes] + matmul(context[...], w_out[:, lanes]) + bias

    step_rows = 64

    def norm_first(n, carry):
        rows = pl.ds(pl.multiple_of(n * step_rows, step_rows), step_rows)
        x = start[rows, :]
        centred = x - jnp.mean(x, axis=1, keepdims=True)
        rstd = lax.rsqrt(jnp.mean(centred * centred, axis=1, keepdims=True) + norm_eps)
        xhat = centred * rstd
        hat[rows, :] = xhat
        rstd_out[rows, :] = jnp.broadcast_to(rstd, (step_rows, LANES))
        normed = xhat * vector("gain_one") + vector("shift_one")
        start[rows, :] = normed
        normed_low[rows, :] = normed.astype(BF16)
        return carry

    lax.fori_loop(0, WINLEN // step_rows, norm_first, 0)
    write_out(hat, hat_out)
    write_out(normed_low, normed_out)

    def widen(n, carry):
        at = pl.multiple_of(n * NBLOCK, NBLOCK)
        lanes = pl.ds(at, NBLOCK)
        bias = vec[0:1, pl.ds(pl.multiple_of(VEC["in_bias"] + at, LANES), NBLOCK)]
        value, change = gelu_and_slope(matmul(normed_low[...], w_in[:, lanes]) + bias)
        active[:, lanes] = value.astype(BF16)
        slope[:, lanes] = change.astype(BF16)
        return carry

    lax.fori_loop(0, FF // NBLOCK, widen, 0)
    write_out(active, active_out)
    write_out(slope, slope_out)
    for n in range(D // NBLOCK):
        lanes = slice(n * NBLOCK, (n + 1) * NBLOCK)
        bias = vec[0:1, VEC["back_bias"] + n * NBLOCK : VEC["back_bias"] + (n + 1) * NBLOCK]
        start[:, lanes] = start[:, lanes] + matmul(active[...], w_back[:, lanes]) + bias

    exchanged(cot_ref, 1)
    own_cot.wait()
    gain_grads[...] = jnp.zeros_like(gain_grads)

    def norm_second(n, carry):
        rows = pl.ds(pl.multiple_of(n * step_rows, step_rows), step_rows)
        x = start[rows, :]
        centred = x - jnp.mean(x, axis=1, keepdims=True)
        rstd = lax.rsqrt(jnp.mean(centred * centred, axis=1, keepdims=True) + norm_eps)
        xhat = centred * rstd
        output_ref[rows, :] = (xhat * vector("gain_two") + vector("shift_two")).astype(BF16)
        cot = cot_ref[rows, :].astype(F32)
        prod = cot * xhat
        gain_grads[0:1, :] = gain_grads[0:1, :] + jnp.sum(prod, axis=0, keepdims=True)
        gain_grads[1:2, :] = gain_grads[1:2, :] + jnp.sum(cot, axis=0, keepdims=True)
        gain = vector("gain_two")
        gc = cot * gain
        mean_one = jnp.mean(gc, axis=1, keepdims=True)
        mean_two = jnp.mean(prod * gain, axis=1, keepdims=True)
        second_out[rows, :] = rstd * (gc - mean_one - xhat * mean_two)
        return carry

    lax.fori_loop(0, WINLEN // step_rows, norm_second, 0)
    for odd in range(2):
        probs_copy(0, odd).wait()
    for copy in written[1:]:
        copy.wait()
    finish_notes()
    gathering.finish()


def forward_pass(plan, own, hidden_in, cotangent, info):
    anywhere = pl.BlockSpec(memory_space=pl.ANY)
    vmem = pl.BlockSpec(memory_space=pltpu.VMEM)
    token = (WINLEN, D)

    def hbm(shape, dtype=BF16):
        return jax.ShapeDtypeStruct(shape, dtype), anywhere

    def near(shape, dtype=F32):
        return jax.ShapeDtypeStruct(shape, dtype), vmem

    outs = [
        hbm(MATRICES[0]), hbm(MATRICES[1]), hbm(MATRICES[3]), hbm(MATRICES[4]), hbm(token), hbm(token),
        hbm(token), hbm(token), hbm(token), hbm((HEADS, WINLEN, WINLEN)), hbm((D, WINLEN)),
        hbm(token, F32), hbm(token), hbm((WINLEN, FF)), hbm((WINLEN, FF)), near(token),
        near((1, VEC_ROWS * LANES)), near((WINLEN, LANES)), near((2, D)), near(token, BF16),
        near(token, BF16), near((WINLEN, LANES), BF16), near((2, WINLEN)),
    ]
    scratch = [
        pltpu.VMEM((COLUMNS, CORES, DEPTH, COLUMNS, plan.quarter, LANES), BF16),
        pltpu.VMEM((plan.staged, LANES), F32),
    ]
    scratch += [pltpu.VMEM(layout, BF16) for layout in MATRICES]
    scratch += [
        pltpu.VMEM((NOTE_ROWS, LANES), BF16),
        pltpu.VMEM(token, BF16),
        pltpu.VMEM(token, BF16),
        pltpu.VMEM(token, F32),
        pltpu.VMEM(token, BF16),
        pltpu.VMEM(token, BF16),
        pltpu.VMEM(token, BF16),
        pltpu.VMEM(token, BF16),
        pltpu.VMEM((WINLEN, LANES), BF16),
        pltpu.VMEM((2, WINLEN, LANES), BF16),
        pltpu.VMEM((2, WINLEN, LANES), BF16),
        pltpu.VMEM((WINLEN, WINLEN), BF16),
        pltpu.VMEM((WINLEN, WINLEN), BF16),
        pltpu.VMEM((HEADS, 1, WIDE), F32),
        pltpu.VMEM((2 * HEADS, BUCKETS, LANES), F32),
        pltpu.VMEM((WINLEN, 3 * LANES), BF16),
        pltpu.VMEM((WINLEN, 2 * LANES), BF16),
        pltpu.VMEM((WINLEN, 2 * LANES), BF16),
        pltpu.VMEM((LANES, 5 * LANES), F32),
        pltpu.VMEM((WINLEN, 2 * LANES), F32),
        pltpu.VMEM((2, WINLEN, WINLEN), BF16),
        pltpu.VMEM((D, WINLEN), BF16),
        pltpu.VMEM((LANES, WINLEN), F32),
        pltpu.VMEM(token, F32),
        pltpu.VMEM((WINLEN, FF), BF16),
        pltpu.VMEM((WINLEN, FF), BF16),
        pltpu.VMEM((1, VEC_ROWS * LANES), F32),
        pltpu.SemaphoreType.DMA((2, 7)),
        pltpu.SemaphoreType.DMA((2, 2, DEPTH)),
        pltpu.SemaphoreType.DMA((16,)),
        pltpu.SemaphoreType.DMA((2,)),
    ]
    return pl.pallas_call(
        functools.partial(forward_kernel, plan),
        out_shape=[shape for shape, _ in outs],
        in_specs=[vmem, anywhere, anywhere, vmem, vmem],
        out_specs=[spec for _, spec in outs],
        scratch_shapes=scratch + sem_shapes(GATHER_SEMS),
        compiler_params=pltpu.CompilerParams(
            collective_id=0, has_side_effects=True, vmem_limit_bytes=62 * 2**20
        ),
        name="forward_pass",
    )(own, hidden_in, cotangent, info, jnp.asarray(turns_table()))


def token_info(doc_lengths, box_coords):
    places = jnp.arange(WINLEN, dtype=jnp.int32)
    first = places == 0
    doc = jnp.zeros((WINLEN,), jnp.int32)
    end = 0
    for d in range(3):
        end = end + doc_lengths[d]
        doc = doc + (places >= end).astype(jnp.int32)
        first = first | (places == end)
    rows = [box_coords[:, c] for c in range(4)] + [doc, first.astype(jnp.int32)]
    return jnp.stack(rows + [jnp.zeros_like(doc)] * 2).astype(F32)


def norm_back(grad, xhat, rstd, gain):
    gc = grad * gain
    prod = gc * xhat
    inner = gc - jnp.mean(gc, axis=1, keepdims=True) - xhat * jnp.mean(prod, axis=1, keepdims=True)
    return rstd * inner


def fast_shards(hidden_in, cotangent, box_coords, doc_lengths, params, moment_one, moment_two):
    head_pos = lax.axis_index("head")
    shard_len = params.shape[0]
    plan = Plan(shard_len)
    own = params.astype(BF16).reshape(plan.rows, LANES)
    own = jnp.pad(own, ((0, plan.padded - plan.rows), (0, 0))).reshape(COLUMNS, plan.quarter, LANES)
    own_box = lax.dynamic_index_in_dim(box_coords, head_pos, 0, keepdims=False)
    own_lengths = lax.dynamic_index_in_dim(doc_lengths, head_pos, 0, keepdims=False)
    info = token_info(own_lengths, own_box)
    (proj_qkv, proj_out, proj_in, proj_back, features, start_low, queries, keys, values, probs, context_t,
     xhat, normed_low, active, slope, grad_second, vec, rstd, grad_norm_two, output, cot, hot_two,
     rest_rows) = forward_pass(plan, own, hidden_in, cotangent, info)
    output_low = to_positions(output.reshape(1, WINLEN, D))

    grad_branch = grad_second.astype(BF16)
    grad_proj_back = rows_inner(active, grad_branch)
    grad_back_bias = jnp.sum(grad_branch.astype(F32), axis=0)
    grad_inner = (times_transposed(grad_branch, proj_back) * slope.astype(F32)).astype(BF16)
    grad_proj_in = rows_inner(normed_low, grad_inner)
    grad_in_bias = jnp.sum(grad_inner.astype(F32), axis=0)
    grad_normed = grad_second + times_transposed(grad_inner, proj_in)
    grad_norm_one = jnp.stack([jnp.sum(grad_normed * xhat, axis=0), jnp.sum(grad_normed, axis=0)])
    gain = vec[0, VEC["gain_one"] : VEC["gain_one"] + D]
    grad_first = norm_back(grad_normed, xhat, rstd[:, :1], gain)
    grad_attn = grad_first.astype(BF16)
    grad_proj_out = matmul(context_t, grad_attn)
    grad_out_bias = jnp.sum(grad_attn.astype(F32), axis=0)
    grad_context = times_transposed(grad_attn, proj_out).astype(BF16)
    ops = dict(hot_two=hot_two, rest_cols=rest_rows.T, rest_rows=rest_rows)
    grad_queries_t, grad_keys, grad_values, cells, diag = attention_backward(
        queries, keys, values, grad_context, probs, ops
    )
    table_grad = table_grads(cells, diag)
    grad_mixed = jnp.concatenate([grad_queries_t.T, grad_keys, grad_values], axis=1)
    grad_proj_qkv = rows_inner(start_low, grad_mixed)
    summed = jnp.sum(grad_mixed.astype(F32), axis=0)
    grad_qv_bias = jnp.stack([summed[:D], summed[2 * D :]])
    grad_start_low = (grad_first + times_transposed(grad_mixed, proj_qkv)).astype(BF16)
    grad_hidden = to_positions(grad_start_low.reshape(1, WINLEN, D))
    grad_proj_box = rows_inner(features, grad_start_low)
    small = (
        grad_qv_bias, grad_out_bias, grad_norm_one, grad_in_bias, grad_back_bias, grad_norm_two, table_grad,
    )
    misc = jnp.concatenate([piece.reshape(-1) for piece in small])
    misc = jnp.pad(misc, (0, MISC_ROWS * LANES - MISC)).reshape(MISC_ROWS, LANES)
    large = (grad_proj_qkv, grad_proj_out, grad_proj_box, grad_proj_in, grad_proj_back)
    summed = reduce_grads(plan, [piece.astype(BF16) for piece in large], misc)
    grad_share = summed.reshape(plan.padded, LANES)[: plan.rows].reshape(-1)
    return finish_step(output_low, grad_hidden, grad_share, params, moment_one, moment_two)


def finish_step(output_low, grad_hidden, grad_share, params, moment_one, moment_two):
    shard_len = params.shape[0]
    index = lax.axis_index("dp") * lax.axis_size("head") + lax.axis_index("head")
    flat_index = index * shard_len + jnp.arange(shard_len, dtype=jnp.int32)
    param_step, new_one = adam_step(params, moment_one, moment_two, grad_share, flat_index)
    return (output_low, grad_hidden, grad_share, param_step, new_one)


def to_windows(shard):
    return lax.all_to_all(shard, "head", split_axis=0, concat_axis=1, tiled=True)


def to_positions(window):
    return lax.all_to_all(window, "head", split_axis=1, concat_axis=0, tiled=True)


def plain_shards(hidden_in, cotangent, box_coords, doc_lengths, params, moment_one, moment_two):
    head_pos = lax.axis_index("head")
    groups = lax.axis_size("head")
    shard_len = params.shape[0]
    flat_params = lax.all_gather(params.astype(BF16), ("dp", "head"), axis=0, tiled=True)
    pieces = unpack(flat_params)
    hidden = to_windows(hidden_in).reshape(WINLEN, D)
    cot = to_windows(cotangent).reshape(WINLEN, D)
    own_box = lax.dynamic_index_in_dim(box_coords, head_pos, 0, keepdims=False)
    own_lengths = lax.dynamic_index_in_dim(doc_lengths, head_pos, 0, keepdims=False)
    chosen, relative, centre_x, centre_y = window_layout(own_lengths, own_box)
    features = box_features(relative).astype(BF16)

    proj_qkv, proj_out, proj_box, proj_in, proj_back = pieces[:5]
    qv_bias, out_bias, norm_one, in_bias, back_bias, norm_two, tables = pieces[5:]
    ops = bias_operands(tables, chosen, centre_x, centre_y)
    start_state = hidden.astype(F32) + matmul(features, proj_box)
    start_low = start_state.astype(BF16)
    qv_float = qv_bias.astype(F32)
    mixed = matmul(start_low, proj_qkv)
    queries = (mixed[:, :D] + qv_float[0]).astype(BF16) * jnp.asarray(HEAD_DIM ** (-0.5), BF16)
    keys = mixed[:, D : 2 * D].astype(BF16)
    values = (mixed[:, 2 * D :] + qv_float[1]).astype(BF16)

    probs, context_t = attention_forward(queries, keys, values, ops)
    first_sum = start_state + rows_inner(context_t, proj_out) + out_bias.astype(F32)
    normed, norm_one_back = jax.vjp(layer_norm, first_sum, norm_one.astype(F32))
    normed_low = normed.astype(BF16)
    inner_act = matmul(normed_low, proj_in) + in_bias.astype(F32)
    active, gelu_back = jax.vjp(gelu_exact, inner_act)
    active_low = active.astype(BF16)
    second_sum = normed + matmul(active_low, proj_back) + back_bias.astype(F32)
    output, norm_two_back = jax.vjp(layer_norm, second_sum, norm_two.astype(F32))
    output_low = to_positions(output.astype(BF16).reshape(1, WINLEN, D))

    grad_second, grad_norm_two = norm_two_back(cot.astype(F32))
    grad_branch = grad_second.astype(BF16)
    grad_proj_back = rows_inner(active_low, grad_branch)
    grad_back_bias = jnp.sum(grad_branch.astype(F32), axis=0)
    (grad_inner_f,) = gelu_back(times_transposed(grad_branch, proj_back))
    grad_inner = grad_inner_f.astype(BF16)
    grad_proj_in = rows_inner(normed_low, grad_inner)
    grad_in_bias = jnp.sum(grad_inner.astype(F32), axis=0)
    grad_first, grad_norm_one = norm_one_back(grad_second + times_transposed(grad_inner, proj_in))
    grad_attn = grad_first.astype(BF16)
    grad_proj_out = matmul(context_t, grad_attn)
    grad_out_bias = jnp.sum(grad_attn.astype(F32), axis=0)
    grad_context = times_transposed(grad_attn, proj_out).astype(BF16)
    grad_queries_t, grad_keys, grad_values, cells, diag = attention_backward(
        queries, keys, values, grad_context, probs, ops
    )
    table_grad = table_grads(cells, diag)
    grad_mixed = jnp.concatenate([grad_queries_t.T, grad_keys, grad_values], axis=1)
    grad_proj_qkv = rows_inner(start_low, grad_mixed)
    summed = jnp.sum(grad_mixed.astype(F32), axis=0)
    grad_qv_bias = jnp.stack([summed[:D], summed[2 * D :]])
    grad_start = grad_first + times_transposed(grad_mixed, proj_qkv)
    grad_start_low = grad_start.astype(BF16)
    grad_hidden = to_positions(grad_start_low.reshape(1, WINLEN, D))
    grad_proj_box = rows_inner(features, grad_start_low)
    grad_list = (
        grad_proj_qkv,
        grad_proj_out,
        grad_proj_box,
        grad_proj_in,
        grad_proj_back,
        grad_qv_bias,
        grad_out_bias,
        grad_norm_one,
        grad_in_bias,
        grad_back_bias,
        grad_norm_two,
        table_grad,
    )
    padding = jnp.zeros((shard_len * groups * lax.axis_size("dp") - USED,), BF16)
    grads_flat = jnp.concatenate([piece.astype(BF16).reshape(-1) for piece in grad_list] + [padding])
    grad_share = lax.psum_scatter(
        grads_flat, ("dp", "head"), scatter_dimension=0, tiled=True
    ).astype(F32)
    return finish_step(output_low, grad_hidden, grad_share, params, moment_one, moment_two)


def solution(mesh):
    placed = (
        P("dp", "head", None),
        P("dp", "head", None),
        P("dp", None, None),
        P("dp", None),
        P(("dp", "head")),
        P(("dp", "head")),
        P(("dp", "head")),
    )
    return jax.shard_map(
        fast_shards if fits(mesh) else plain_shards,
        mesh=mesh,
        in_specs=placed,
        out_specs=(
            P("dp", "head", None),
            P("dp", "head", None),
            P(("dp", "head")),
            P(("dp", "head")),
            P(("dp", "head")),
        ),
        check_vma=False,
    )
```

```python
import functools
import math

import jax
import jax.numpy as jnp
import numpy as np
from jax import lax
from jax.experimental import pallas as pl
from jax.experimental.pallas import tpu as pltpu
from jax.sharding import PartitionSpec as P

D = 768
HEADS = 12
FF = 3072
BUCKETS = 32
WINLEN = 512
HEAD_DIM = 64
PAIRS = HEADS // 2
LANES = 128
BLOCKS = WINLEN // LANES

beta_one = 0.9
beta_two = 0.999
adam_eps = 1e-08
norm_eps = 1e-05
base_rate = 0.001
layer_decay = 0.75
decay_weight = 0.01
adam_count = 100
coord_cell = 32
masked_score = -1e30

F32 = jnp.float32
BF16 = jnp.bfloat16


def layouts_list():
    return (
        (D, 3 * D),
        (D, D),
        (D, D),
        (D, FF),
        (FF, D),
        (2, D),
        (D,),
        (2, D),
        (FF,),
        (D,),
        (2, D),
        (3, HEADS, BUCKETS),
    )


def unpack(flat_params):
    pieces = []
    offset = 0
    for layout in layouts_list():
        elements = math.prod(layout)
        pieces.append(flat_params[offset : offset + elements].reshape(layout))
        offset += elements
    return pieces


def matmul(left_mat, right_mat):
    return jnp.dot(left_mat, right_mat, preferred_element_type=F32)


def rows_inner(left_mat, right_mat):
    return lax.dot_general(left_mat, right_mat, (((0,), (0,)), ((), ())), preferred_element_type=F32)


def times_transposed(left_mat, right_mat):
    return lax.dot_general(left_mat, right_mat, (((1,), (1,)), ((), ())), preferred_element_type=F32)


def layer_norm(values, gain_bias):
    row_mean = jnp.mean(values, axis=-1, keepdims=True)
    centred = values - row_mean
    spread = jnp.mean(centred * centred, axis=-1, keepdims=True)
    return centred * lax.rsqrt(spread + norm_eps) * gain_bias[0] + gain_bias[1]


def gelu_exact(values):
    return jax.nn.gelu(values, approximate=False)


def hot(index, count):
    return (np.asarray(index)[..., None] == np.arange(count)).astype(np.float32)


def clipped(steps):
    return np.clip(steps, -(BUCKETS // 2), BUCKETS // 2 - 1) + BUCKETS // 2


CELLS = np.arange(BUCKETS)
HOT_SAME = hot(clipped(CELLS[:, None] - CELLS[None, :]), BUCKETS)
HOT_LESS = hot(clipped(CELLS[:, None] - CELLS[None, :] - 1), BUCKETS)
WIDE = 6 * LANES
_U = np.arange(WIDE)
BAND_HOT = hot(np.where(_U < 5 * LANES, clipped(_U - 2 * LANES), 0), BUCKETS)
_V = np.arange(4 * LANES)
DIAG_HOT = np.concatenate(
    [
        hot(np.zeros(LANES, np.int64), BUCKETS),
        hot(np.where(_V < 3 * LANES, clipped(_V - LANES), 0), BUCKETS),
        hot(np.full(LANES, BUCKETS - 1), BUCKETS),
    ]
)


def window_layout(doc_lengths, box_coords):
    doc_ends = jnp.cumsum(doc_lengths, dtype=jnp.int32)
    doc_starts = doc_ends - doc_lengths
    places = jnp.arange(WINLEN, dtype=jnp.int32)
    doc_ids = jnp.sum(
        (places[:, None] >= doc_ends[None, :]).astype(jnp.int32), axis=1, dtype=jnp.int32
    )
    docs = jnp.arange(doc_lengths.shape[0], dtype=jnp.int32)
    chosen = doc_ids[:, None] == docs[None, :]
    first_hot = places[:, None] == doc_starts[None, :]
    first_box = jnp.sum(
        jnp.where(first_hot[:, :, None], box_coords[:, None, :], 0), axis=0, dtype=jnp.int32
    )
    anchor = jnp.sum(
        jnp.where(chosen[:, :, None], first_box[None, :, :], 0), axis=1, dtype=jnp.int32
    )
    relative = box_coords - jnp.concatenate([anchor[:, :2], anchor[:, :2]], axis=1)
    centre_x = (box_coords[:, 0] + box_coords[:, 2]) // 2
    centre_y = (box_coords[:, 1] + box_coords[:, 3]) // 2
    return chosen, relative, centre_x, centre_y


def box_features(relative):
    count_freq = D // 8
    steps = jnp.arange(count_freq, dtype=F32)
    frequency = jnp.exp(steps * (-math.log(1000.0) / count_freq))
    angles = relative.astype(F32)[:, :, None] * frequency[None, None, :]
    return jnp.concatenate([jnp.sin(angles), jnp.cos(angles)], axis=2).reshape(relative.shape[0], D)


def bias_operands(tables, chosen, centre_x, centre_y):
    cell_x, cell_y = centre_x // coord_cell, centre_y // coord_cell
    rest_x, rest_y = centre_x % coord_cell, centre_y % coord_cell
    cells = jnp.arange(BUCKETS, dtype=jnp.int32)
    hot_x = (cell_x[:, None] == cells[None, :]).astype(BF16)
    hot_y = (cell_y[:, None] == cells[None, :]).astype(BF16)
    none = jnp.zeros_like(hot_x)
    hot_two = jnp.concatenate([hot_x, hot_y, hot_x, hot_y], axis=1)
    key_x = jnp.stack(
        [
            jnp.concatenate([hot_x, -hot_x, none, none], axis=1),
            jnp.concatenate([none, none, hot_x, -hot_x], axis=1),
        ]
    )
    key_y = jnp.stack(
        [
            jnp.concatenate([hot_y, -hot_y, none, none], axis=1),
            jnp.concatenate([none, none, hot_y, -hot_y], axis=1),
        ]
    )
    same = jnp.einsum("qcb,thb->thqc", HOT_SAME.astype(BF16), tables[1:], preferred_element_type=F32)
    less = jnp.einsum("qcb,thb->thqc", HOT_LESS.astype(BF16), tables[1:], preferred_element_type=F32)
    zero = jnp.zeros_like(same[0])
    base = jnp.concatenate(
        [jnp.concatenate([same[0], zero], axis=2), jnp.concatenate([zero, same[1]], axis=2)], axis=1
    )
    base = base.reshape(PAIRS, 2, 64, 64)[:, ::-1].reshape(HEADS, 64, 64)
    diff_x = jnp.concatenate([jnp.concatenate([less[0], same[0]], axis=2), jnp.zeros((HEADS, 32, 64), F32)], axis=1)
    diff_y = jnp.concatenate([jnp.zeros((HEADS, 32, 64), F32), jnp.concatenate([less[1], same[1]], axis=2)], axis=1)
    rows = jnp.concatenate([base, diff_x, diff_y], axis=0).astype(BF16)
    rows = rows.transpose(1, 0, 2).reshape(64, 3 * D)
    met = matmul(hot_two[:, :64], rows).astype(BF16)
    band = matmul(tables[0], jnp.asarray(BAND_HOT.T, BF16)).reshape(HEADS, 1, WIDE)
    rest_cols = jnp.stack([rest_x, rest_y], axis=1).astype(F32)
    rest_rows = rest_cols.T
    pad = jnp.zeros((WINLEN, LANES - chosen.shape[1]), BF16)
    marks = chosen.astype(BF16)
    mark_keys = jnp.concatenate([marks, pad], axis=1)
    mark_queries = jnp.concatenate([(1 - marks) * jnp.asarray(masked_score, BF16), pad], axis=1)
    return dict(
        hot_two=hot_two,
        key_x=key_x,
        key_y=key_y,
        met=met,
        band=band,
        rest_cols=rest_cols,
        rest_rows=rest_rows,
        mark_keys=mark_keys,
        mark_queries=mark_queries,
    )


def half_masks():
    lane = lax.broadcasted_iota(jnp.int32, (1, LANES), 1)
    low = (lane < HEAD_DIM).astype(F32)
    return low.astype(BF16), (1.0 - low).astype(BF16)


def less_masks(rest_cols, rest_rows, less_x, less_y):
    for part in range(BLOCKS):
        rows = slice(part * LANES, (part + 1) * LANES)
        for axis, less in ((0, less_x), (1, less_y)):
            column = rest_cols[rows, axis : axis + 1]
            row = rest_rows[axis : axis + 1, :]
            less[rows, :] = jnp.where(row < column, 1.0, 0.0).astype(less.dtype)


def attention_forward_kernel(
    q_ref, k_ref, v_ref, hot_ref, keyx_ref, keyy_ref, met_ref, band_ref, cols_ref, rows_ref,
    mkey_ref, mquery_ref, probs_ref, context_ref,
    kaug, qaug, less_x, less_y, wide, scores,
):
    low, high = half_masks()
    less_masks(cols_ref, rows_ref, less_x, less_y)
    kaug[:, LANES:] = mkey_ref[...]
    qaug[:, LANES:] = mquery_ref[...]
    half = 2 * LANES

    def one_pair(pair, carry):
        at = pl.multiple_of(pair * LANES, LANES)
        lanes = pl.ds(at, LANES)
        lanes_x = pl.ds(pl.multiple_of(at + D, LANES), LANES)
        lanes_y = pl.ds(pl.multiple_of(at + 2 * D, LANES), LANES)
        values_t = v_ref[:, lanes].T
        for odd in range(2):
            own, other = (low, high) if odd == 0 else (high, low)
            head = 2 * pair + odd
            kaug[:, :LANES] = k_ref[:, lanes] * own + hot_ref[...] * other
            qaug[:, :LANES] = q_ref[:, lanes] * own + met_ref[:, lanes] * other
            skew_band(band_ref[head], wide)
            for side in range(2):
                cols = slice(side * half, (side + 1) * half)
                top = None
                for part in range(BLOCKS):
                    rows = slice(part * LANES, (part + 1) * LANES)
                    s = times_transposed(kaug[rows, :], qaug[cols, :])
                    dx = times_transposed(keyx_ref[odd, rows, :], met_ref[cols, lanes_x])
                    dy = times_transposed(keyy_ref[odd, rows, :], met_ref[cols, lanes_y])
                    bias = []
                    for block in range(2 * side, 2 * side + 2):
                        step = max(-2, min(2, block - part)) + 2
                        bias.append(wide[:, step * LANES : (step + 1) * LANES])
                    s = s + jnp.concatenate(bias, axis=1)
                    s = s + dx * less_x[rows, cols] + dy * less_y[rows, cols]
                    scores[rows, :] = s
                    best = jnp.max(s, axis=0, keepdims=True)
                    top = best if top is None else jnp.maximum(top, best)
                total = None
                for part in range(BLOCKS):
                    rows = slice(part * LANES, (part + 1) * LANES)
                    e = jnp.exp(scores[rows, :] - top)
                    scores[rows, :] = e
                    add = jnp.sum(e, axis=0, keepdims=True)
                    total = add if total is None else total + add
                share = 1.0 / total
                for part in range(BLOCKS):
                    rows = slice(part * LANES, (part + 1) * LANES)
                    probs_ref[head, rows, cols] = (scores[rows, :] * share).astype(BF16)
                got = matmul(
                    values_t[odd * HEAD_DIM : (odd + 1) * HEAD_DIM, :], probs_ref[head, :, cols]
                )
                context_ref[pl.ds(pl.multiple_of(head * HEAD_DIM, HEAD_DIM), HEAD_DIM), cols] = (
                    got.astype(BF16)
                )
        return carry

    lax.fori_loop(0, PAIRS, one_pair, 0)


def skew_band(row, wide):
    x = jnp.broadcast_to(row, (8, WIDE))
    sub = lax.broadcasted_iota(jnp.int32, (8, WIDE), 0)
    for bit in (1, 2, 4):
        x = jnp.where((sub & bit) != 0, pltpu.roll(x, bit, 1), x)
    for group in range(LANES // 8):
        y = x if group == 0 else pltpu.roll(x, 8 * group, 1)
        wide[8 * group : 8 * group + 8, :] = y[:, : 5 * LANES]


def diagonal_sums(parts):
    total = None
    for group in range(LANES // 8):
        x = jnp.concatenate(
            [parts[8 * group : 8 * group + 8, LANES : 4 * LANES], jnp.zeros((8, LANES), F32)], axis=1
        )
        y = x if group == 0 else pltpu.roll(x, 4 * LANES - 8 * group, 1)
        total = y if total is None else total + y
    sub = lax.broadcasted_iota(jnp.int32, (8, 4 * LANES), 0)
    for bit in (1, 2, 4):
        total = jnp.where((sub & bit) != 0, pltpu.roll(total, 4 * LANES - bit, 1), total)
    return jnp.sum(total, axis=0, keepdims=True)


def attention_backward_kernel(
    q_ref, k_ref, v_ref, dctx_ref, probs_ref, hot_ref, cols_ref, rows_ref,
    dq_ref, dk_ref, dv_ref, cells_ref, diag_ref,
    qaug, less_x, less_y, scores, dscores, band, kept, hot_t,
):
    low, high = half_masks()
    less_masks(cols_ref, rows_ref, less_x, less_y)
    hot_t[...] = hot_ref[...].T
    lane = lax.broadcasted_iota(jnp.int32, (1, LANES), 1)
    scale = HEAD_DIM ** (-0.5)
    of_x = jnp.where((lane // BUCKETS) % 2 == 0, 1.0, 0.0)
    cells_x = hot_ref[...] * of_x.astype(BF16)
    cells_y = hot_ref[...] * (1.0 - of_x).astype(BF16)

    def one_pair(pair, carry):
        at = pl.multiple_of(pair * LANES, LANES)
        lanes = pl.ds(at, LANES)
        keys_t = k_ref[:, lanes].T
        for odd in range(2):
            own, other = (low, high) if odd == 0 else (high, low)
            head = 2 * pair + odd
            qaug[...] = q_ref[:, lanes] * own + hot_ref[...] * other
            dctx = dctx_ref[:, lanes]
            dot = None
            for part in range(BLOCKS):
                rows = slice(part * LANES, (part + 1) * LANES)
                dp = times_transposed(v_ref[rows, lanes] * own, dctx)
                scores[rows, :] = dp
                add = jnp.sum(dp * probs_ref[head, rows, :].astype(F32), axis=0, keepdims=True)
                dot = add if dot is None else dot + add
            band[...] = jnp.zeros_like(band)
            for part in range(BLOCKS):
                rows = slice(part * LANES, (part + 1) * LANES)
                probs = probs_ref[head, rows, :]
                ds = probs.astype(F32) * (scores[rows, :] - dot)
                for block in range(BLOCKS):
                    step = max(-2, min(2, block - part)) + 2
                    where = slice(step * LANES, (step + 1) * LANES)
                    band[:, where] = band[:, where] + ds[:, block * LANES : (block + 1) * LANES]
                ds = ds.astype(BF16)
                dscores[rows, :] = ds
                both = matmul(ds, qaug[...])
                less = matmul(ds * less_x[rows, :], cells_x) + matmul(ds * less_y[rows, :], cells_y)
                dv = matmul(probs, dctx)
                kept[odd, 0, rows, :] = both
                kept[odd, 1, rows, :] = less
                kept[odd, 2, rows, :] = dv
            got = matmul(keys_t[odd * HEAD_DIM : (odd + 1) * HEAD_DIM, :], dscores[...])
            dq_ref[pl.ds(pl.multiple_of(head * HEAD_DIM, HEAD_DIM), HEAD_DIM), :] = (
                got * scale
            ).astype(BF16)
            diag_ref[head, :, LANES : 5 * LANES] = diagonal_sums(band)
            diag_ref[head, :, :LANES] = jnp.sum(band[:, :LANES], axis=0, keepdims=True)
            diag_ref[head, :, 5 * LANES :] = jnp.sum(band[:, 4 * LANES :], axis=0, keepdims=True)
            for which in range(2):
                summed = kept[odd, which]
                first = summed.astype(BF16)
                rest = (summed - first.astype(F32)).astype(BF16)
                cells_ref[head, which] = matmul(hot_t[:64, :], first) + matmul(hot_t[:64, :], rest)
        dk_ref[:, lanes] = jnp.where(lane < HEAD_DIM, kept[0, 0], kept[1, 0]).astype(BF16)
        dv_ref[:, lanes] = jnp.where(lane < HEAD_DIM, kept[0, 2], kept[1, 2]).astype(BF16)
        return carry

    lax.fori_loop(0, PAIRS, one_pair, 0)


def attention_forward(queries, keys, values, ops):
    return pl.pallas_call(
        attention_forward_kernel,
        out_shape=(
            jax.ShapeDtypeStruct((HEADS, WINLEN, WINLEN), BF16),
            jax.ShapeDtypeStruct((D, WINLEN), BF16),
        ),
        scratch_shapes=[
            pltpu.VMEM((WINLEN, 2 * LANES), BF16),
            pltpu.VMEM((WINLEN, 2 * LANES), BF16),
            pltpu.VMEM((WINLEN, WINLEN), F32),
            pltpu.VMEM((WINLEN, WINLEN), F32),
            pltpu.VMEM((LANES, 5 * LANES), F32),
            pltpu.VMEM((WINLEN, 2 * LANES), F32),
        ],
        compiler_params=pltpu.CompilerParams(vmem_limit_bytes=48 * 2**20),
        name="attention_forward",
    )(
        queries, keys, values, ops["hot_two"], ops["key_x"], ops["key_y"], ops["met"], ops["band"],
        ops["rest_cols"], ops["rest_rows"], ops["mark_keys"], ops["mark_queries"],
    )


def attention_backward(queries, keys, values, grad_context, probs, ops):
    return pl.pallas_call(
        attention_backward_kernel,
        out_shape=(
            jax.ShapeDtypeStruct((D, WINLEN), BF16),
            jax.ShapeDtypeStruct((WINLEN, D), BF16),
            jax.ShapeDtypeStruct((WINLEN, D), BF16),
            jax.ShapeDtypeStruct((HEADS, 2, 64, LANES), F32),
            jax.ShapeDtypeStruct((HEADS, 1, WIDE), F32),
        ),
        scratch_shapes=[
            pltpu.VMEM((WINLEN, LANES), BF16),
            pltpu.VMEM((WINLEN, WINLEN), BF16),
            pltpu.VMEM((WINLEN, WINLEN), BF16),
            pltpu.VMEM((WINLEN, WINLEN), F32),
            pltpu.VMEM((WINLEN, WINLEN), BF16),
            pltpu.VMEM((LANES, 5 * LANES), F32),
            pltpu.VMEM((2, 3, WINLEN, LANES), F32),
            pltpu.VMEM((LANES, WINLEN), BF16),
        ],
        compiler_params=pltpu.CompilerParams(vmem_limit_bytes=48 * 2**20),
        name="attention_backward",
    )(
        queries, keys, values, grad_context, probs, ops["hot_two"], ops["rest_cols"],
        ops["rest_rows"],
    )


def table_grads(cells, diag):
    exact = lax.Precision.HIGHEST
    pairs = cells.reshape(PAIRS, 2, 2, 64, LANES)
    every = jnp.stack([pairs[:, 0, 0, :, 64:], pairs[:, 1, 0, :, :64]], axis=1).reshape(HEADS, 64, 64)
    less = cells[:, 1]
    less_x, less_y = less[:, :32, :32], less[:, 32:, 32:64]
    all_x, all_y = every[:, :32, :32], every[:, 32:, 32:]
    same = jnp.stack([all_x - less_x, all_y - less_y]).reshape(2 * HEADS, -1)
    below = jnp.stack([less_x, less_y]).reshape(2 * HEADS, -1)
    same_hot = jnp.asarray(HOT_SAME.transpose(1, 0, 2).reshape(-1, BUCKETS))
    less_hot = jnp.asarray(HOT_LESS.transpose(1, 0, 2).reshape(-1, BUCKETS))
    moved = jnp.dot(same, same_hot, precision=exact) + jnp.dot(below, less_hot, precision=exact)
    along = jnp.dot(diag.reshape(HEADS, WIDE), jnp.asarray(DIAG_HOT), precision=exact)
    return jnp.concatenate([along[None], moved.reshape(2, HEADS, BUCKETS)], axis=0)


COLUMNS = 4
CORES = 2
DEPTH = 4
USED = sum(math.prod(layout) for layout in layouts_list())
MATRICES = layouts_list()[:5]
MISC = sum(math.prod(layout) for layout in layouts_list()[5:])
MISC_ROWS = -(-MISC // (8 * LANES)) * 8


class Plan:
    def __init__(self, shard_len, carry=3 * LANES):
        self.rows = shard_len // LANES
        self.quarter = -(-self.rows // (16 * COLUMNS)) * 16
        self.padded = COLUMNS * self.quarter
        self.per_column = CORES * DEPTH * self.rows
        self.carry = carry
        self.staged = self.carry + self.per_column + 3 * LANES
        starts = []
        offset = 0
        for depth, width in MATRICES:
            starts.append(offset // LANES)
            offset += depth * width
        self.starts = starts
        self.misc_start = offset // LANES


def fits(mesh):
    return mesh.shape["dp"] == COLUMNS * CORES and mesh.shape["head"] == DEPTH


MESH = pl.DeviceIdType.MESH


class Place:
    def __init__(self):
        dp = lax.axis_index("dp")
        self.z = lax.axis_index("head")
        self.core = dp % CORES
        self.column = dp // CORES
        self.x = self.column % 2
        self.y = self.column // 2
        self.col_x = 2 * self.y + (1 - self.x)
        self.col_y = 2 * (1 - self.y) + self.x
        self.col_d = 2 * (1 - self.y) + (1 - self.x)
        self.peer_x = self.at(self.col_x, self.core, self.z)
        self.peer_y = self.at(self.col_y, self.core, self.z)
        self.peer_d = self.at(self.col_d, self.core, self.z)
        self.peer_core = self.at(self.column, 1 - self.core, self.z)
        self.far = [lax.rem(self.z + d, DEPTH) for d in range(1, DEPTH)]
        self.from_far = [lax.rem(self.z + DEPTH - d, DEPTH) for d in range(1, DEPTH)]
        self.peers_z = [self.at(self.column, self.core, f) for f in self.far]

    def at(self, column, core, z):
        return {"dp": column * CORES + core, "head": z}

    def greet(self):
        barrier = pltpu.get_barrier_semaphore()
        peers = [self.peer_x, self.peer_y, self.peer_d, self.peer_core] + self.peers_z
        for peer in peers:
            pl.semaphore_signal(barrier, inc=1, device_id=peer, device_id_type=MESH)
        pl.semaphore_wait(barrier, len(peers))


def remote(src, dst, send_sem, recv_sem, peer):
    return pltpu.make_async_remote_copy(
        src_ref=src, dst_ref=dst, send_sem=send_sem, recv_sem=recv_sem, device_id=peer,
        device_id_type=MESH,
    )


class Gathering:
    def __init__(self, place, flat, sems):
        self.place = place
        self.flat = flat
        self.sems = sems
        self.sent = []

    def send(self, src, dst, kind, index, peer):
        copy = remote(src, dst, self.sems[kind].at[0, index], self.sems[kind].at[1, index], peer)
        copy.start()
        self.sent.append(copy)

    def got(self, dst, kind, index):
        remote(
            dst, dst, self.sems[kind].at[0, index], self.sems[kind].at[1, index], self.place.peer_x
        ).wait_recv()

    def spread(self, own):
        p = self.place
        for index, (column, peer) in enumerate(
            ((p.col_x, p.peer_x), (p.col_y, p.peer_y), (p.col_d, p.peer_d))
        ):
            self.send(
                own.at[column], self.flat.at[p.column, p.core, p.z, column], "spread", index, peer
            )
        self.flat[p.column, p.core, p.z, p.column] = own[p.column]

    def spread_done(self):
        p = self.place
        for index, column in enumerate((p.col_x, p.col_y, p.col_d)):
            self.got(self.flat.at[column, p.core, p.z, p.column], "spread", index)

    def along_z(self, k):
        p = self.place
        piece = self.flat.at[k, p.core, p.z, p.column]
        for d in range(DEPTH - 1):
            self.send(piece, piece, "z", 3 * k + d, p.peers_z[d])

    def first(self, k):
        p = self.place
        for d in range(DEPTH - 1):
            self.got(self.flat.at[k, p.core, p.from_far[d], p.column], "z", 3 * k + d)
        piece = self.flat.at[k, p.core, :, p.column]
        self.send(piece, piece, "one", 2 * k, p.peer_x)
        self.send(piece, piece, "one", 2 * k + 1, p.peer_y)
        self.send(piece, piece, "core", 5 * k, p.peer_core)

    def second(self, k):
        p = self.place
        from_x = self.flat.at[k, p.core, :, p.col_x]
        self.got(from_x, "one", 2 * k)
        part = self.flat.at[k, p.core, 0:2, p.col_x]
        self.send(part, part, "two", 2 * k, p.peer_y)
        self.send(from_x, from_x, "core", 5 * k + 1, p.peer_core)
        from_y = self.flat.at[k, p.core, :, p.col_y]
        self.got(from_y, "one", 2 * k + 1)
        part = self.flat.at[k, p.core, 2:4, p.col_y]
        self.send(part, part, "two", 2 * k + 1, p.peer_x)
        self.send(from_y, from_y, "core", 5 * k + 2, p.peer_core)

    def third(self, k):
        p = self.place
        part = self.flat.at[k, p.core, 0:2, p.col_d]
        self.got(part, "two", 2 * k)
        self.send(part, part, "core", 5 * k + 3, p.peer_core)
        part = self.flat.at[k, p.core, 2:4, p.col_d]
        self.got(part, "two", 2 * k + 1)
        self.send(part, part, "core", 5 * k + 4, p.peer_core)

    def complete(self, k):
        p = self.place
        other = 1 - p.core
        for index, column in enumerate((p.column, p.col_x, p.col_y)):
            self.got(self.flat.at[k, other, :, column], "core", 5 * k + index)
        self.got(self.flat.at[k, other, 0:2, p.col_d], "core", 5 * k + 3)
        self.got(self.flat.at[k, other, 2:4, p.col_d], "core", 5 * k + 4)

    def finish(self):
        for copy in self.sent:
            copy.wait_send()


GATHER_SEMS = {"spread": 3, "z": 12, "one": 8, "two": 8, "core": 20}


def sem_shapes(counts):
    return [pltpu.SemaphoreType.DMA((2, count)) for count in counts.values()]


def stage_column(plan, flat, staged, k):
    def one(shard, carry):
        core, z = shard // DEPTH, shard % DEPTH
        for quarter in range(COLUMNS):
            base = plan.carry + shard * plan.rows + quarter * plan.quarter
            staged[pl.ds(pl.multiple_of(base, 8), plan.quarter), :] = flat[k, core, z, quarter].astype(F32)
        return carry

    lax.fori_loop(0, CORES * DEPTH, one, 0)


def keep_carry(plan, staged):
    end = plan.carry + plan.per_column
    staged[: plan.carry, :] = staged[end - plan.carry : end, :]


ROW_STEP = 48


def column_rows(plan, k, touching):
    low, high = k * plan.per_column, (k + 1) * plan.per_column
    taken = []
    for index, (depth, width) in enumerate(MATRICES):
        group = 16 * (width // LANES)
        from_low, from_high = low - plan.starts[index], high - plan.starts[index]
        begin = max(0, min(depth, from_low // group * 16))
        if touching:
            end = max(0, min(depth, -(-from_high // group) * 16))
        else:
            end = max(0, min(depth, from_high // group * 16))
        if end > begin:
            taken.append((index, begin, end))
    return taken


def staged_at(plan, k, row):
    return plan.carry + row - k * plan.per_column


def row_loops(rows):
    whole = rows // ROW_STEP
    loops = [(ROW_STEP, 0, whole)] if whole else []
    if rows % ROW_STEP:
        loops.append((16, whole * ROW_STEP, (rows % ROW_STEP) // 16))
    return loops


def form_matrices(plan, staged, matrices, k):
    for index, begin, end in column_rows(plan, k, False):
        blocks = MATRICES[index][1] // LANES
        base = staged_at(plan, k, plan.starts[index] + begin * blocks)
        assert 0 <= base
        target = matrices[index]
        for step_rows, first, count in row_loops(end - begin):

            def one(step, carry, step_rows=step_rows, first=first, blocks=blocks, base=base,
                    begin=begin, target=target):
                row = first + step * step_rows
                for block in range(blocks):
                    got = staged[pl.ds(base + row * blocks + block, step_rows, stride=blocks), :]
                    target[
                        pl.ds(pl.multiple_of(begin + row, 16), step_rows),
                        block * LANES : (block + 1) * LANES,
                    ] = got.astype(BF16)
                return carry

            lax.fori_loop(0, count, one, 0)


def adam_step(params, moment_one, moment_two, grads, flat_index):
    box_part = (flat_index >= 4 * D * D) & (flat_index < 5 * D * D)
    step_rate = jnp.where(box_part, base_rate * layer_decay**12, base_rate * layer_decay)
    decay_mask = jnp.where(flat_index < 5 * D * D + 2 * D * FF, decay_weight, 0.0)
    moment_one = beta_one * moment_one + (1.0 - beta_one) * grads
    moment_two = beta_two * moment_two + (1.0 - beta_two) * grads * grads
    first_hat = moment_one / (1.0 - beta_one**adam_count)
    second_hat = moment_two / (1.0 - beta_two**adam_count)
    update = first_hat / (jnp.sqrt(second_hat) + adam_eps) + decay_mask * params
    return (-step_rate * update, moment_one)


VEC = {}
_at = 0
for _name, _rows in (
    ("q_bias", 6), ("v_bias", 6), ("out_bias", 6), ("gain_one", 6), ("shift_one", 6), ("in_bias", 24),
    ("back_bias", 6), ("gain_two", 6), ("shift_two", 6), ("tables", 9),
):
    VEC[_name] = _at * LANES
    _at += _rows
VEC_ROWS = _at
NOTE_ROWS = 96
NBLOCK = 2 * LANES


def note_place(plan):
    row = plan.misc_start - (CORES * DEPTH * COLUMNS - 1) * plan.rows
    quarter, row = row // plan.quarter, row % plan.quarter
    first = row // 16 * 16
    assert first + NOTE_ROWS <= plan.quarter and row - first + VEC_ROWS <= NOTE_ROWS
    return quarter, first, row - first


def spread_notes(place, own, notes, sems, plan):
    quarter, first, _ = note_place(plan)
    source = own.at[quarter, first : first + NOTE_ROWS]
    home = (place.column == COLUMNS - 1) & (place.core == CORES - 1)
    root = home & (place.z == DEPTH - 1)

    def copy(src, index, peer):
        return remote(src, notes, sems.at[0, index], sems.at[1, 0], peer)

    def arrived():
        copy(notes, 0, place.peer_core).wait_recv()

    @pl.when(root)
    def _():
        notes[...] = own[quarter, first : first + NOTE_ROWS]
        for index, peer in enumerate(place.peers_z):
            copy(source, index, peer).start()

    @pl.when(home & (place.z != DEPTH - 1))
    def _():
        arrived()

    @pl.when(home)
    def _():
        for index, peer in enumerate((place.peer_x, place.peer_y, place.peer_d)):
            copy(notes, 3 + index, peer).start()

    @pl.when((place.core == CORES - 1) & (place.column != COLUMNS - 1))
    def _():
        arrived()

    @pl.when(place.core == CORES - 1)
    def _():
        copy(notes, 6, place.peer_core).start()

    @pl.when(place.core != CORES - 1)
    def _():
        arrived()

    def finish():
        @pl.when(root)
        def _():
            for index, peer in enumerate(place.peers_z):
                copy(source, index, peer).wait_send()

        @pl.when(home)
        def _():
            for index, peer in enumerate((place.peer_x, place.peer_y, place.peer_d)):
                copy(notes, 3 + index, peer).wait_send()

        @pl.when(place.core == CORES - 1)
        def _():
            copy(notes, 6, place.peer_core).wait_send()

    return finish


def turns_table():
    count_freq = D // 8
    freq = np.exp(np.arange(count_freq) * (-math.log(1000.0) / count_freq)) / (2 * math.pi)
    per = np.concatenate([freq, freq])
    phase = np.concatenate([np.zeros(count_freq), np.full(count_freq, 0.25)])
    return np.stack([np.tile(per, 4), np.tile(phase, 4)]).astype(np.float32)


def sin_turns(t):
    t = t - jnp.floor(t + 0.5)
    a = jnp.abs(t)
    m = jnp.minimum(a, 0.5 - a) * (2 * math.pi)
    u = m * m
    poly = -1.0 / 39916800.0
    for term in (1.0 / 362880.0, -1.0 / 5040.0, 1.0 / 120.0, -1.0 / 6.0, 1.0):
        poly = poly * u + term
    s = m * poly
    return jnp.where(t < 0, -s, s)


def token_columns(info):
    coords = info[0:4, :]
    doc, first = info[4:5, :], info[5:6, :]
    anchor = jnp.zeros_like(coords)
    for d in range(4):
        mine = jnp.where(doc == float(d), 1.0, 0.0)
        value = jnp.sum(coords * (mine * first), axis=1, keepdims=True)
        anchor = anchor + value * mine
    anchor = jnp.concatenate([anchor[0:2], anchor[0:2]], axis=0)
    relative = coords - anchor
    centre = jnp.floor((coords[0:2] + coords[2:4]) * 0.5)
    cell = jnp.floor(centre * (1.0 / coord_cell))
    rest = centre - cell * coord_cell
    rows = jnp.concatenate(
        [relative, cell, rest, doc, jnp.zeros((LANES - 9, WINLEN), F32)], axis=0
    )
    return rest, rows.T


def form_features(columns, turns_ref, features):
    lane = lax.broadcasted_iota(jnp.int32, (1, LANES), 1)
    for block in range(D // LANES):
        lanes = slice(block * LANES, (block + 1) * LANES)
        low, high = block * LANES // (D // 4), ((block + 1) * LANES - 1) // (D // 4)
        value = columns[:, low : low + 1]
        if high != low:
            value = jnp.where(
                lane + block * LANES < high * (D // 4), value, columns[:, high : high + 1]
            )
        t = value * turns_ref[0:1, lanes] + turns_ref[1:2, lanes]
        features[:, lanes] = sin_turns(t).astype(BF16)


def form_hots(columns, hot_ref, keyx_ref, keyy_ref, mkey, mquery):
    lane = lax.broadcasted_iota(jnp.int32, (1, LANES), 1)
    part = lane // BUCKETS
    cell = (lane % BUCKETS).astype(F32)
    is_x = jnp.where(columns[:, 4:5] == cell, 1.0, 0.0)
    is_y = jnp.where(columns[:, 5:6] == cell, 1.0, 0.0)
    hot_ref[...] = jnp.where(part % 2 == 0, is_x, is_y).astype(BF16)
    sign = jnp.where(part % 2 == 0, 1.0, -1.0)
    for odd in range(2):
        here = jnp.where(part // 2 == odd, sign, 0.0)
        keyx_ref[odd] = (is_x * here).astype(BF16)
        keyy_ref[odd] = (is_y * here).astype(BF16)
    doc = jnp.where(columns[:, 8:9] == lane.astype(F32), 1.0, 0.0)
    mkey[...] = doc.astype(BF16)
    mquery[...] = (jnp.where(lane < 4, 1.0 - doc, 0.0) * masked_score).astype(BF16)


def form_tables(tables, bands, tilted):
    row = lax.broadcasted_iota(jnp.int32, (LANES, 1), 0)
    half = BUCKETS // 2
    sub = lax.broadcasted_iota(jnp.int32, (8, LANES), 0)
    place = lax.broadcasted_iota(jnp.int32, (1, WIDE), 1)
    wanted = jnp.where(place < 5 * LANES, jnp.clip(place - 2 * LANES, -half, half - 1) + half, 0)
    lane = lax.broadcasted_iota(jnp.int32, (1, LANES), 1)
    turned = jnp.clip(64 - lane, -half, half - 1) + half
    for m in range(4):
        hot_band = jnp.where(row == wanted + m * BUCKETS, 1.0, 0.0).astype(BF16)
        got = matmul(tables, hot_band)
        for n in range(3):
            bands[4 * n + m] = got[n : n + 1, :]
        hot_turn = jnp.where(row == turned + m * BUCKETS, 1.0, 0.0).astype(BF16)
        got = matmul(tables, hot_turn)
        for t in (1, 2):
            for n in range(3):
                x = jnp.broadcast_to(got[3 * t + n : 3 * t + n + 1, :], (8, LANES))
                for bit in (1, 2, 4):
                    x = jnp.where((sub & bit) != 0, pltpu.roll(x, bit, 1), x)
                for group in range(BUCKETS // 8):
                    y = x if group == 0 else pltpu.roll(x, 8 * group, 1)
                    tilted[(t - 1) * HEADS + 4 * n + m, 8 * group : 8 * group + 8, :] = y


def pair_rows(tilted, pair):
    lane = lax.broadcasted_iota(jnp.int32, (1, LANES), 1)
    part = lane // BUCKETS
    x0, x1 = tilted[2 * pair], tilted[2 * pair + 1]
    y0, y1 = tilted[HEADS + 2 * pair], tilted[HEADS + 2 * pair + 1]

    def same(value, to):
        return value if to == 64 else pltpu.roll(value, (to - 64) % LANES, 1)

    def less(value, to):
        return pltpu.roll(value, (to - 65) % LANES, 1)

    zero = jnp.zeros_like(x0)
    base_x = jnp.where(part == 0, same(x1, 0), jnp.where(part == 2, same(x0, 64), zero))
    base_y = jnp.where(part == 1, same(y1, 32), jnp.where(part == 3, same(y0, 96), zero))

    def steps(even, odd):
        return jnp.where(
            part < 2,
            jnp.where(part == 0, less(even, 0), same(even, 32)),
            jnp.where(part == 2, less(odd, 64), same(odd, 96)),
        )

    rows = [
        jnp.concatenate([base_x, base_y], axis=0),
        jnp.concatenate([steps(x0, x1), zero], axis=0),
        jnp.concatenate([zero, steps(y0, y1)], axis=0),
    ]
    return jnp.concatenate(rows, axis=1).astype(BF16)


def gelu_and_slope(z):
    a = jnp.abs(z)
    t = 1.0 / (1.0 + (0.3275911 / math.sqrt(2.0)) * a)
    poly = 1.061405429 * 0.5
    for term in (-1.453152027, 1.421413741, -0.284496736, 0.254829592):
        poly = poly * t + 0.5 * term
    e = jnp.exp(-0.5 * z * z)
    tail = poly * t * e
    cdf = jnp.where(z < 0, tail, 1.0 - tail)
    return z * cdf, cdf + z * (e * (1.0 / math.sqrt(2.0 * math.pi)))


def forward_kernel(plan, own, hidden_in, cot_in, info, turns, *refs):
    (w_qkv_out, w_out_out, w_in_out, w_back_out, features_out, low_out, q_out, k_out, v_out, probs_out,
     context_out, hat_out, normed_out, active_out, slope_out, second_out, vec_out, rstd_out, gain_grads,
     output_ref, cot_ref, hot_out, rest_out) = refs[:23]
    refs = refs[23:]
    (flat, staged, w_qkv, w_out, w_box, w_in, w_back, notes, features, hidden, start, start_low, q_ref,
     k_ref, v_ref, hot_ref, key_x, key_y, less_x, less_y, bands, tilted, met, kaug, qaug, wide, scores,
     probs, context_t, pair_t, hat, active, slope, vec) = refs[:34]
    note_sems, swap_sems, copy_sems, probs_sems = refs[34:38]
    place = Place()
    normed_low = hidden
    context = features
    gathering = Gathering(place, flat, dict(zip(GATHER_SEMS, refs[38:])))
    matrices = (w_qkv, w_out, w_box, w_in, w_back)
    written = []

    def write_out(src, dst):
        copy = pltpu.make_async_copy(src, dst, copy_sems.at[len(written)])
        copy.start()
        written.append(copy)

    place.greet()
    finish_notes = None
    gathering.spread(own)

    quarter = WINLEN // DEPTH

    def exchange(source, target, kind):
        rows = pl.ds(pl.multiple_of(place.z * quarter, quarter), quarter)
        for d in range(DEPTH - 1):
            gathering_send(source.at[place.far[d]], target.at[rows], kind, d, place.peers_z[d])

    def gathering_send(src, dst, kind, d, peer):
        copy = remote(src, dst, swap_sems.at[kind, 0, d], swap_sems.at[kind, 1, d], peer)
        copy.start()
        gathering.sent.append(copy)

    def exchanged(target, kind):
        for d in range(DEPTH - 1):
            rows = pl.ds(pl.multiple_of(place.from_far[d] * quarter, quarter), quarter)
            remote(
                target.at[rows], target.at[rows], swap_sems.at[kind, 0, d], swap_sems.at[kind, 1, d],
                place.peer_x,
            ).wait_recv()

    exchange(hidden_in, hidden, 0)
    finish_notes = spread_notes(place, own, notes, note_sems, plan)
    own_rows = pl.ds(pl.multiple_of(place.z * quarter, quarter), quarter)
    own_hidden = pltpu.make_async_copy(
        hidden_in.at[place.z], hidden.at[own_rows], swap_sems.at[0, 0, DEPTH - 1]
    )
    own_hidden.start()
    own_cot = pltpu.make_async_copy(
        cot_in.at[place.z], cot_ref.at[own_rows], swap_sems.at[1, 0, DEPTH - 1]
    )
    own_cot.start()
    gathering.spread_done()
    gathering.along_z(0)
    gathering.along_z(1)

    rest, columns = token_columns(info[...])
    for part in range(BLOCKS):
        rows = slice(part * LANES, (part + 1) * LANES)
        for axis, less in ((0, less_x), (1, less_y)):
            less[rows, :] = jnp.where(
                rest[axis : axis + 1, :] < columns[rows, 6 + axis : 7 + axis], 1.0, 0.0
            ).astype(BF16)
    rest_out[...] = rest
    form_hots(columns, hot_ref, key_x, key_y, kaug.at[:, LANES:], qaug.at[:, LANES:])
    hot_out[...] = hot_ref[...]
    form_features(columns, turns, features)
    for n in range(D // LANES):
        rows = slice(n * LANES, (n + 1) * LANES)
        context_t[rows, :] = features[:, rows].T
    write_out(context_t, features_out)
    _, _, note_row = note_place(plan)
    for row in range(VEC_ROWS):
        at = note_row + row
        vec[0:1, row * LANES : (row + 1) * LANES] = notes[at // 16 * 16 : at // 16 * 16 + 16, :].astype(
            F32
        )[at % 16 : at % 16 + 1, :]
    vec_out[...] = vec[...]
    table_row = note_row + VEC["tables"] // LANES
    assert table_row % 16 == 0
    form_tables(notes[table_row : table_row + 16, :], bands, tilted)

    gathering.first(0)
    gathering.along_z(2)
    gathering.first(1)
    gathering.along_z(3)
    exchange(cot_in, cot_ref, 1)
    gathering.second(0)
    gathering.first(2)
    gathering.third(0)
    gathering.second(1)
    gathering.complete(0)
    stage_column(plan, flat, staged, 0)
    form_matrices(plan, staged, matrices, 0)
    keep_carry(plan, staged)
    gathering.first(3)
    gathering.third(1)
    gathering.second(2)
    gathering.complete(1)
    stage_column(plan, flat, staged, 1)
    form_matrices(plan, staged, matrices, 1)
    keep_carry(plan, staged)
    write_out(w_qkv, w_qkv_out)
    write_out(w_out, w_out_out)

    exchanged(hidden, 0)
    own_hidden.wait()
    for n in range(D // NBLOCK):
        lanes = slice(n * NBLOCK, (n + 1) * NBLOCK)
        value = hidden[:, lanes].astype(F32) + matmul(features[...], w_box[:, lanes])
        start[:, lanes] = value
        start_low[:, lanes] = value.astype(BF16)
    write_out(start_low, low_out)
    written[0].wait()

    def project(n, carry):
        at = pl.multiple_of(n * NBLOCK, NBLOCK)
        lanes = pl.ds(at, NBLOCK)
        low = start_low[...]
        bias = vec[0:1, pl.ds(pl.multiple_of(VEC["q_bias"] + at, LANES), NBLOCK)]
        got = matmul(low, w_qkv[:, lanes]) + bias
        q_ref[:, lanes] = (got.astype(BF16).astype(F32) * HEAD_DIM ** (-0.5)).astype(BF16)
        k_ref[:, lanes] = matmul(low, w_qkv[:, pl.ds(pl.multiple_of(at + D, LANES), NBLOCK)]).astype(BF16)
        bias = vec[0:1, pl.ds(pl.multiple_of(VEC["v_bias"] + at, LANES), NBLOCK)]
        got = matmul(low, w_qkv[:, pl.ds(pl.multiple_of(at + 2 * D, LANES), NBLOCK)]) + bias
        v_ref[:, lanes] = got.astype(BF16)
        return carry

    lax.fori_loop(0, D // NBLOCK, project, 0)
    write_out(q_ref, q_out)
    write_out(k_ref, k_out)
    write_out(v_ref, v_out)
    gathering.third(2)
    gathering.second(3)

    low, high = half_masks()
    half = 2 * LANES

    def probs_copy(head, odd):
        return pltpu.make_async_copy(probs.at[odd], probs_out.at[head], probs_sems.at[odd])

    def one_pair(pair, carry):
        at = pl.multiple_of(pair * LANES, LANES)
        lanes = pl.ds(at, LANES)
        values_t = v_ref[:, lanes].T
        met[...] = matmul(hot_ref[:, :64], pair_rows(tilted, pair)).astype(BF16)
        for odd in range(2):
            mine, other = (low, high) if odd == 0 else (high, low)
            head = 2 * pair + odd
            kaug[:, :LANES] = k_ref[:, lanes] * mine + hot_ref[...] * other
            qaug[:, :LANES] = q_ref[:, lanes] * mine + met[:, :LANES] * other
            skew_band(bands[head], wide)

            @pl.when(pair > 0)
            def _():
                probs_copy(head, odd).wait()

            for side in range(2):
                cols = slice(side * half, (side + 1) * half)
                top = None
                for part in range(BLOCKS):
                    rows = slice(part * LANES, (part + 1) * LANES)
                    s = times_transposed(kaug[rows, :], qaug[cols, :])
                    dx = times_transposed(key_x[odd, rows, :], met[cols, LANES : 2 * LANES])
                    dy = times_transposed(key_y[odd, rows, :], met[cols, 2 * LANES :])
                    bias = []
                    for block in range(2 * side, 2 * side + 2):
                        step = max(-2, min(2, block - part)) + 2
                        bias.append(wide[:, step * LANES : (step + 1) * LANES])
                    s = s + jnp.concatenate(bias, axis=1)
                    s = s + dx * less_x[rows, cols].astype(F32) + dy * less_y[rows, cols].astype(F32)
                    scores[rows, :] = s
                    best = jnp.max(s, axis=0, keepdims=True)
                    top = best if top is None else jnp.maximum(top, best)
                total = None
                for part in range(BLOCKS):
                    rows = slice(part * LANES, (part + 1) * LANES)
                    e = jnp.exp(scores[rows, :] - top)
                    scores[rows, :] = e
                    add = jnp.sum(e, axis=0, keepdims=True)
                    total = add if total is None else total + add
                share = 1.0 / total
                for part in range(BLOCKS):
                    rows = slice(part * LANES, (part + 1) * LANES)
                    probs[odd, rows, cols] = (scores[rows, :] * share).astype(BF16)
                got = matmul(values_t[odd * HEAD_DIM : (odd + 1) * HEAD_DIM, :], probs[odd, :, cols])
                pair_t[odd * HEAD_DIM : (odd + 1) * HEAD_DIM, cols] = got
            probs_copy(head, odd).start()
        both = pair_t[...]
        context_t[lanes, :] = both.astype(BF16)
        context[:, lanes] = both.T.astype(BF16)
        return carry

    lax.fori_loop(0, 2, one_pair, 0)
    gathering.third(3)
    gathering.complete(2)
    stage_column(plan, flat, staged, 2)
    form_matrices(plan, staged, matrices, 2)
    keep_carry(plan, staged)
    write_out(w_in, w_in_out)
    lax.fori_loop(2, PAIRS, one_pair, 0)
    write_out(context_t, context_out)
    gathering.complete(3)
    stage_column(plan, flat, staged, 3)
    form_matrices(plan, staged, matrices, 3)
    write_out(w_back, w_back_out)

    def vector(name):
        return vec[0:1, VEC[name] : VEC[name] + D]

    for n in range(D // NBLOCK):
        lanes = slice(n * NBLOCK, (n + 1) * NBLOCK)
        bias = vec[0:1, VEC["out_bias"] + n * NBLOCK : VEC["out_bias"] + (n + 1) * NBLOCK]
        start[:, lanes] = start[:, lanes] + matmul(context[...], w_out[:, lanes]) + bias

    step_rows = 64

    def norm_first(n, carry):
        rows = pl.ds(pl.multiple_of(n * step_rows, step_rows), step_rows)
        x = start[rows, :]
        centred = x - jnp.mean(x, axis=1, keepdims=True)
        rstd = lax.rsqrt(jnp.mean(centred * centred, axis=1, keepdims=True) + norm_eps)
        xhat = centred * rstd
        hat[rows, :] = xhat
        rstd_out[rows, :] = jnp.broadcast_to(rstd, (step_rows, LANES))
        normed = xhat * vector("gain_one") + vector("shift_one")
        start[rows, :] = normed
        normed_low[rows, :] = normed.astype(BF16)
        return carry

    lax.fori_loop(0, WINLEN // step_rows, norm_first, 0)
    write_out(hat, hat_out)
    write_out(normed_low, normed_out)

    def widen(n, carry):
        at = pl.multiple_of(n * NBLOCK, NBLOCK)
        lanes = pl.ds(at, NBLOCK)
        bias = vec[0:1, pl.ds(pl.multiple_of(VEC["in_bias"] + at, LANES), NBLOCK)]
        value, change = gelu_and_slope(matmul(normed_low[...], w_in[:, lanes]) + bias)
        active[:, lanes] = value.astype(BF16)
        slope[:, lanes] = change.astype(BF16)
        return carry

    lax.fori_loop(0, FF // NBLOCK, widen, 0)
    write_out(active, active_out)
    write_out(slope, slope_out)
    for n in range(D // NBLOCK):
        lanes = slice(n * NBLOCK, (n + 1) * NBLOCK)
        bias = vec[0:1, VEC["back_bias"] + n * NBLOCK : VEC["back_bias"] + (n + 1) * NBLOCK]
        start[:, lanes] = start[:, lanes] + matmul(active[...], w_back[:, lanes]) + bias

    exchanged(cot_ref, 1)
    own_cot.wait()
    gain_grads[...] = jnp.zeros_like(gain_grads)

    def norm_second(n, carry):
        rows = pl.ds(pl.multiple_of(n * step_rows, step_rows), step_rows)
        x = start[rows, :]
        centred = x - jnp.mean(x, axis=1, keepdims=True)
        rstd = lax.rsqrt(jnp.mean(centred * centred, axis=1, keepdims=True) + norm_eps)
        xhat = centred * rstd
        output_ref[rows, :] = (xhat * vector("gain_two") + vector("shift_two")).astype(BF16)
        cot = cot_ref[rows, :].astype(F32)
        prod = cot * xhat
        gain_grads[0:1, :] = gain_grads[0:1, :] + jnp.sum(prod, axis=0, keepdims=True)
        gain_grads[1:2, :] = gain_grads[1:2, :] + jnp.sum(cot, axis=0, keepdims=True)
        gain = vector("gain_two")
        gc = cot * gain
        mean_one = jnp.mean(gc, axis=1, keepdims=True)
        mean_two = jnp.mean(prod * gain, axis=1, keepdims=True)
        second_out[rows, :] = rstd * (gc - mean_one - xhat * mean_two)
        return carry

    lax.fori_loop(0, WINLEN // step_rows, norm_second, 0)
    for odd in range(2):
        probs_copy(0, odd).wait()
    for copy in written[1:]:
        copy.wait()
    finish_notes()
    gathering.finish()


def forward_pass(plan, own, hidden_in, cotangent, info):
    anywhere = pl.BlockSpec(memory_space=pl.ANY)
    vmem = pl.BlockSpec(memory_space=pltpu.VMEM)
    token = (WINLEN, D)

    def hbm(shape, dtype=BF16):
        return jax.ShapeDtypeStruct(shape, dtype), anywhere

    def near(shape, dtype=F32):
        return jax.ShapeDtypeStruct(shape, dtype), vmem

    outs = [
        hbm(MATRICES[0]), hbm(MATRICES[1]), hbm(MATRICES[3]), hbm(MATRICES[4]), hbm((D, WINLEN)), hbm(token),
        hbm(token), hbm(token), hbm(token), hbm((HEADS, WINLEN, WINLEN)), hbm((D, WINLEN)),
        hbm(token, F32), hbm(token), hbm((WINLEN, FF)), hbm((WINLEN, FF)), near(token),
        near((1, VEC_ROWS * LANES)), near((WINLEN, LANES)), near((2, D)), near(token, BF16),
        near(token, BF16), near((WINLEN, LANES), BF16), near((2, WINLEN)),
    ]
    scratch = [
        pltpu.VMEM((COLUMNS, CORES, DEPTH, COLUMNS, plan.quarter, LANES), BF16),
        pltpu.VMEM((plan.staged, LANES), F32),
    ]
    scratch += [pltpu.VMEM(layout, BF16) for layout in MATRICES]
    scratch += [
        pltpu.VMEM((NOTE_ROWS, LANES), BF16),
        pltpu.VMEM(token, BF16),
        pltpu.VMEM(token, BF16),
        pltpu.VMEM(token, F32),
        pltpu.VMEM(token, BF16),
        pltpu.VMEM(token, BF16),
        pltpu.VMEM(token, BF16),
        pltpu.VMEM(token, BF16),
        pltpu.VMEM((WINLEN, LANES), BF16),
        pltpu.VMEM((2, WINLEN, LANES), BF16),
        pltpu.VMEM((2, WINLEN, LANES), BF16),
        pltpu.VMEM((WINLEN, WINLEN), BF16),
        pltpu.VMEM((WINLEN, WINLEN), BF16),
        pltpu.VMEM((HEADS, 1, WIDE), F32),
        pltpu.VMEM((2 * HEADS, BUCKETS, LANES), F32),
        pltpu.VMEM((WINLEN, 3 * LANES), BF16),
        pltpu.VMEM((WINLEN, 2 * LANES), BF16),
        pltpu.VMEM((WINLEN, 2 * LANES), BF16),
        pltpu.VMEM((LANES, 5 * LANES), F32),
        pltpu.VMEM((WINLEN, 2 * LANES), F32),
        pltpu.VMEM((2, WINLEN, WINLEN), BF16),
        pltpu.VMEM((D, WINLEN), BF16),
        pltpu.VMEM((LANES, WINLEN), F32),
        pltpu.VMEM(token, F32),
        pltpu.VMEM((WINLEN, FF), BF16),
        pltpu.VMEM((WINLEN, FF), BF16),
        pltpu.VMEM((1, VEC_ROWS * LANES), F32),
        pltpu.SemaphoreType.DMA((2, 7)),
        pltpu.SemaphoreType.DMA((2, 2, DEPTH)),
        pltpu.SemaphoreType.DMA((16,)),
        pltpu.SemaphoreType.DMA((2,)),
    ]
    return pl.pallas_call(
        functools.partial(forward_kernel, plan),
        out_shape=[shape for shape, _ in outs],
        in_specs=[vmem, anywhere, anywhere, vmem, vmem],
        out_specs=[spec for _, spec in outs],
        scratch_shapes=scratch + sem_shapes(GATHER_SEMS),
        compiler_params=pltpu.CompilerParams(
            collective_id=0, has_side_effects=True, vmem_limit_bytes=62 * 2**20
        ),
        name="forward_pass",
    )(own, hidden_in, cotangent, info, jnp.asarray(turns_table()))


class Reducing:
    def __init__(self, place, flat, swapped, one, two, deep, piece, result, sems, free):
        self.place = place
        self.flat = flat
        self.swapped = swapped
        self.one = one
        self.two = two
        self.deep = deep
        self.piece = piece
        self.result = result
        self.sems = sems
        self.free = free
        self.sent = {k: [] for k in range(COLUMNS)}

    def send(self, k, src, dst, kind, index, peer):
        copy = remote(src, dst, self.sems[kind].at[0, index], self.sems[kind].at[1, index], peer)
        copy.start()
        self.sent[k].append(copy)

    got = Gathering.got

    def settle(self, k):
        for copy in self.sent.pop(k):
            copy.wait_send()

    def swap(self, k):
        p = self.place
        slot = k % 2
        if k < 2:
            pl.semaphore_wait(self.free.at[slot], 1)
        self.send(k, self.flat.at[slot, 1 - p.core], self.swapped.at[slot], "core", k, p.peer_core)

    def first(self, k):
        p = self.place
        slot = k % 2
        self.got(self.swapped.at[slot], "core", k)

        def one(step, carry):
            z, quarter = step // COLUMNS, step % COLUMNS
            total = self.flat[slot, p.core, z, quarter].astype(F32)
            total = total + self.swapped[slot, z, quarter].astype(F32)
            self.flat[slot, p.core, z, quarter] = total.astype(BF16)
            return carry

        lax.fori_loop(0, DEPTH * COLUMNS, one, 0)
        flat = self.flat
        self.send(k, flat.at[slot, p.core, 0:2, p.col_d], self.one.at[k, 0], "one", 2 * k, p.peer_y)
        self.send(k, flat.at[slot, p.core, 2:4, p.col_d], self.one.at[k, 1], "one", 2 * k + 1, p.peer_x)
        if k >= 2:
            pl.semaphore_signal(
                self.free.at[slot], inc=1, device_id=p.peer_core, device_id_type=MESH
            )

    def second(self, k):
        p = self.place
        slot = k % 2
        for side, column in ((0, p.col_x), (1, p.col_y)):
            self.got(self.one.at[k, side], "one", 2 * k + side)

            def one(step, carry, side=side, column=column):
                z = 2 * side + step
                total = self.flat[slot, p.core, z, column].astype(F32)
                total = total + self.one[k, side, step].astype(F32)
                self.flat[slot, p.core, z, column] = total.astype(BF16)
                return carry

            lax.fori_loop(0, 2, one, 0)
        flat = self.flat
        self.send(k, flat.at[slot, p.core, :, p.col_x], self.two.at[k, 0], "two", 2 * k, p.peer_x)
        self.send(k, flat.at[slot, p.core, :, p.col_y], self.two.at[k, 1], "two", 2 * k + 1, p.peer_y)

    def third(self, k):
        p = self.place
        slot = k % 2
        for side in range(2):
            self.got(self.two.at[k, side], "two", 2 * k + side)

        def one(z, carry):
            total = self.flat[slot, p.core, z, p.column].astype(F32)
            total = total + self.two[k, 0, z].astype(F32) + self.two[k, 1, z].astype(F32)
            self.flat[slot, p.core, z, p.column] = total.astype(BF16)
            return carry

        lax.fori_loop(0, DEPTH, one, 0)
        for d in range(DEPTH - 1):
            self.send(
                k, self.flat.at[slot, p.core, p.far[d], p.column], self.deep.at[k, d], "z", 3 * k + d,
                p.peers_z[d],
            )

    def fourth(self, k):
        p = self.place
        for d in range(DEPTH - 1):
            self.got(self.deep.at[k, d], "z", 3 * k + d)
        total = self.flat[k % 2, p.core, p.z, p.column].astype(F32)
        for d in range(DEPTH - 1):
            total = total + self.deep[k, d].astype(F32)
        self.piece[k] = total.astype(BF16)

    def giving(self, k):
        p = self.place
        sems = self.sems["spread"]
        return remote(
            self.piece.at[k], self.result.at[p.column], sems.at[0, k], sems.at[1, p.column],
            p.at(k, p.core, p.z),
        )

    def give(self, k):
        @pl.when(self.place.column != k)
        def _():
            self.giving(k).start()

    def given(self, k):
        @pl.when(self.place.column != k)
        def _():
            self.giving(k).wait_send()

    def receive(self, out):
        p = self.place
        out[p.column] = self.piece[p.column].astype(F32)
        for column in (p.col_x, p.col_y, p.col_d):
            self.got(self.result.at[column], "spread", column)
            out[column] = self.result[column].astype(F32)


REDUCE_SEMS = {"spread": 4, "z": 12, "one": 8, "two": 8, "core": 4}


def unstage_column(plan, flat, staged, k):
    def one(step, carry):
        shard, quarter = step // COLUMNS, step % COLUMNS
        base = plan.carry + shard * plan.rows + quarter * plan.quarter
        piece = staged[pl.ds(pl.multiple_of(base, 8), plan.quarter), :]
        flat[k % 2, shard // DEPTH, shard % DEPTH, quarter] = piece.astype(BF16)
        return carry

    lax.fori_loop(0, CORES * DEPTH * COLUMNS, one, 0)


class Notes:
    def __init__(self, place, notes, slots, sems):
        self.place, self.notes, self.slots, self.sems = place, notes, slots, sems
        p = place
        self.home = (p.column == COLUMNS - 1) & (p.core == CORES - 1)
        self.root = self.home & (p.z == DEPTH - 1)

    def copy(self, slot, peer):
        return remote(
            self.notes, self.slots.at[slot], self.sems.at[0, 0], self.sems.at[1, slot], peer
        )

    def take(self, slot):
        self.copy(slot, self.place.peer_core).wait_recv()
        self.notes[...] = self.notes[...] + self.slots[slot]

    def start(self):
        p = self.place

        @pl.when(p.core != CORES - 1)
        def _():
            self.copy(0, p.peer_core).start()

    def rise(self):
        p = self.place

        @pl.when(p.core == CORES - 1)
        def _():
            self.take(0)

        @pl.when((p.core == CORES - 1) & (p.column != COLUMNS - 1))
        def _():
            self.copy(1 + p.column, p.at(COLUMNS - 1, p.core, p.z)).start()

    def end(self):
        p = self.place

        @pl.when(self.home)
        def _():
            for slot in range(1, 4):
                self.take(slot)

        @pl.when(self.home & (p.z != DEPTH - 1))
        def _():
            self.copy(4 + p.z, p.at(p.column, p.core, DEPTH - 1)).start()

        @pl.when(self.root)
        def _():
            for slot in range(4, 7):
                self.take(slot)

        @pl.when(jnp.logical_not(self.root))
        def _():
            self.copy(0, p.peer_core).wait_send()


def cell_sums(whole, less, odd):
    lane = lax.broadcasted_iota(jnp.int32, (1, LANES), 1)
    sub = lax.broadcasted_iota(jnp.int32, (8, LANES), 0)
    sums = []
    for axis in range(2):
        rows = slice(axis * BUCKETS, (axis + 1) * BUCKETS)
        start = axis * BUCKETS + (0 if odd else 64)
        every = pltpu.roll(whole[rows], (BUCKETS - start) % LANES, 1)
        below = pltpu.roll(less[rows], (BUCKETS - axis * BUCKETS) % LANES, 1)
        inside = (lane >= BUCKETS) & (lane < 2 * BUCKETS)
        every = jnp.where(inside, every, 0.0)
        below = jnp.where(inside, below, 0.0)
        x = every - below + pltpu.roll(below, LANES - 1, 1)
        total = None
        for group in range(BUCKETS // 8):
            y = x[8 * group : 8 * group + 8]
            y = y if group == 0 else pltpu.roll(y, LANES - 8 * group, 1)
            total = y if total is None else total + y
        for bit in (1, 2, 4):
            total = jnp.where((sub & bit) != 0, pltpu.roll(total, LANES - bit, 1), total)
        sums.append(jnp.sum(total, axis=0, keepdims=True))
    return sums


def exact_dot(a, b):
    return jnp.dot(a, b, preferred_element_type=F32, precision=lax.Precision.HIGHEST)


def bucket_rows(cell_ref, diag_ref):
    half = BUCKETS // 2
    column = lax.broadcasted_iota(jnp.int32, (1, LANES), 1)
    row = lax.broadcasted_iota(jnp.int32, (LANES, 1), 0)
    to = jnp.clip(row - BUCKETS, -half, half - 1) + half
    place = lax.broadcasted_iota(jnp.int32, (WIDE, 1), 0)
    along = place - LANES
    far = jnp.where(place < LANES, 0, jnp.where(place < 5 * LANES, 0, BUCKETS - 1))
    along = jnp.where(
        (place >= LANES) & (place < 4 * LANES),
        jnp.clip(along - LANES, -half, half - 1) + half,
        far,
    )
    first, rest = None, None
    zero = jnp.zeros((5, WIDE), F32)
    for m in range(4):
        hot_along = jnp.where(along + m * BUCKETS == column, 1.0, 0.0)
        got = exact_dot(
            jnp.concatenate([diag_ref[4 * n + m] for n in range(3)] + [zero], axis=0), hot_along
        )
        first = got if first is None else first + got
        hot_cell = jnp.where(to + m * BUCKETS == column, 1.0, 0.0)
        rows = [cell_ref[t * HEADS + 4 * n + m] for t in range(2) for n in range(3)]
        got = exact_dot(jnp.concatenate(rows + [zero[:2, :LANES]], axis=0), hot_cell)
        rest = got if rest is None else rest + got
    return jnp.concatenate([first[:3], rest[:6]], axis=0)


def backward_kernel(
    plan, active_in, slope_in, w_back_in, w_in_in, w_out_in, w_qkv_in, normed_in, low_in, features_in,
    context_in, q_in, k_in, v_in, probs_in, hat_in, second_in, rstd_ref, vec, gain_two, hot_ref, rest_ref,
    output_in, *refs,
):
    out, output_pos, hidden_pos = refs[:3]
    (flat, staged, swapped, one_buf, two_buf, deep, piece, result, active, slope, w_back, w_in, w_out,
     turned, low_t, features_t, context_t, q_ref, k_ref, v_ref, hat, second, branch, dctx, probs, less_x,
     less_y, scores, dscores, band, kept, hot_t, qaug, pair_t, vecg, cell_rows, diag_rows, notes, slots,
     ) = refs[3:42]
    load_sems, probs_sems, free, pos_sems, note_sems = refs[42:47]
    place = Place()
    reducing = Reducing(
        place, flat, swapped, one_buf, two_buf, deep, piece, result,
        dict(zip(REDUCE_SEMS, refs[47:])), free,
    )
    climbing = Notes(place, notes, slots, note_sems)
    loads = {}

    def load(name, src, dst):
        loads[name] = pltpu.make_async_copy(src, dst, load_sems.at[len(loads)])
        loads[name].start()

    mixed = active.at[:, : 3 * D]
    grad_attn = branch
    w_qkv = w_in.at[:, : 3 * D]
    hidden_low = dctx

    load("second", second_in, second)
    load("active", active_in, active)
    load("w_back", w_back_in, w_back)
    load("slope", slope_in, slope)
    load("normed", normed_in, dctx)
    load("w_in", w_in_in, w_in)
    load("hat", hat_in, hat)
    load("w_out", w_out_in, w_out)
    load("context", context_in, context_t)
    load("q", q_in, q_ref)
    load("k", k_in, k_ref)
    load("v", v_in, v_ref)
    for odd in range(2):
        pltpu.make_async_copy(probs_in.at[odd], probs.at[odd], probs_sems.at[odd]).start()
    load("features", features_in, features_t)
    load("low", low_in, low_t)

    at = staged_at(plan, COLUMNS - 1, plan.misc_start)
    staged[at:, :] = jnp.zeros((plan.staged - at, LANES), F32)
    place.greet()

    quarter = WINLEN // DEPTH
    positions = []

    def to_pos(source, target, kind):
        for d in range(DEPTH - 1):
            rows = pl.ds(pl.multiple_of(place.far[d] * quarter, quarter), quarter)
            copy = remote(
                source.at[rows], target.at[place.z], pos_sems.at[kind, 0, d], pos_sems.at[kind, 1, d],
                place.peers_z[d],
            )
            copy.start()
            positions.append(copy)
        rows = pl.ds(pl.multiple_of(place.z * quarter, quarter), quarter)
        copy = pltpu.make_async_copy(
            source.at[rows], target.at[place.z], pos_sems.at[kind, 0, DEPTH - 1]
        )
        copy.start()
        return copy

    def in_pos(target, kind):
        for d in range(DEPTH - 1):
            there = target.at[place.from_far[d]]
            remote(
                there, there, pos_sems.at[kind, 0, d], pos_sems.at[kind, 1, d], place.peer_x
            ).wait_recv()

    own_output = to_pos(output_in, output_pos, 0)

    def store(k, index, row, value, first_block=0):
        blocks = MATRICES[index][1] // LANES
        base = staged_at(plan, k, plan.starts[index]) + row * blocks + first_block
        for block in range(value.shape[1] // LANES):
            staged[pl.ds(base + block, value.shape[0], stride=blocks), :] = value[
                :, block * LANES : (block + 1) * LANES
            ]

    def column_sum(value):
        return jnp.sum(value, axis=0, keepdims=True)

    def keep_vector(name, lanes_at, value):
        at = pl.multiple_of(VEC[name] + lanes_at, LANES)
        vecg[0:1, pl.ds(at, value.shape[1])] = value

    loads["second"].wait()
    for n in range(D // NBLOCK):
        lanes = slice(n * NBLOCK, (n + 1) * NBLOCK)
        value = second[:, lanes].astype(BF16)
        branch[:, lanes] = value
        keep_vector("back_bias", n * NBLOCK, column_sum(value.astype(F32)))
    loads["active"].wait()

    def back_rows(k, size, begin, count):
        def body(n, carry):
            row = pl.multiple_of(begin + n * size, LANES)
            turned[:size, :] = active[:, pl.ds(row, size)].T
            store(k, 4, row, matmul(turned[:size, :], branch[...]))
            return carry

        lax.fori_loop(0, count, body, 0)

    back_rows(3, NBLOCK, 512, (FF - 512) // NBLOCK)
    unstage_column(plan, flat, staged, 3)
    reducing.swap(3)

    back_rows(2, NBLOCK, 0, 2)
    back_rows(2, LANES, 512, 1)
    loads["w_back"].wait()
    loads["slope"].wait()

    def inner(n, carry):
        at = pl.multiple_of(n * NBLOCK, NBLOCK)
        lanes = pl.ds(at, NBLOCK)
        value = times_transposed(branch[...], w_back[lanes, :]) * slope[:, lanes].astype(F32)
        value = value.astype(BF16)
        slope[:, lanes] = value
        keep_vector("in_bias", at, column_sum(value.astype(F32)))
        return carry

    lax.fori_loop(0, FF // NBLOCK, inner, 0)
    grad_inner = slope
    reducing.first(3)

    loads["normed"].wait()
    for n in range(D // NBLOCK):
        rows = slice(n * NBLOCK, (n + 1) * NBLOCK)
        turned[rows, :] = dctx[:, rows].T

    def in_rows(k, begin, end):
        def body(n, carry):
            lanes = pl.ds(pl.multiple_of(n * NBLOCK, NBLOCK), NBLOCK)
            got = matmul(turned[begin:end, :], grad_inner[:, lanes])
            store(k, 3, begin, got, n * (NBLOCK // LANES))
            return carry

        lax.fori_loop(0, FF // NBLOCK, body, 0)

    in_rows(2, 288, D)
    unstage_column(plan, flat, staged, 2)
    reducing.swap(2)
    reducing.second(3)

    loads["w_in"].wait()
    for n in range(D // NBLOCK):
        lanes = slice(n * NBLOCK, (n + 1) * NBLOCK)
        second[:, lanes] = second[:, lanes] + times_transposed(grad_inner[...], w_in[lanes, :])
    load("w_qkv", w_qkv_in, w_qkv)
    reducing.first(2)

    loads["hat"].wait()
    step_rows = 64
    for name in ("gain_one", "shift_one", "out_bias"):
        keep_vector(name, 0, jnp.zeros((1, D), F32))

    def norm_first(n, carry):
        rows = pl.ds(pl.multiple_of(n * step_rows, step_rows), step_rows)
        grad = second[rows, :]
        xhat = hat[rows, :]
        prod = grad * xhat
        gain = vec[0:1, VEC["gain_one"] : VEC["gain_one"] + D]
        gc = grad * gain
        mean_one = jnp.mean(gc, axis=1, keepdims=True)
        mean_two = jnp.mean(prod * gain, axis=1, keepdims=True)
        value = rstd_ref[rows, 0:1] * (gc - mean_one - xhat * mean_two)
        second[rows, :] = value
        value = value.astype(BF16)
        grad_attn[rows, :] = value
        for name, term in (
            ("gain_one", prod), ("shift_one", grad), ("out_bias", value.astype(F32)),
        ):
            lanes = slice(VEC[name], VEC[name] + D)
            vecg[0:1, lanes] = vecg[0:1, lanes] + column_sum(term)
        return carry

    lax.fori_loop(0, WINLEN // step_rows, norm_first, 0)
    reducing.third(3)
    loads["w_out"].wait()
    for n in range(D // NBLOCK):
        lanes = slice(n * NBLOCK, (n + 1) * NBLOCK)
        dctx[:, lanes] = times_transposed(grad_attn[...], w_out[lanes, :]).astype(BF16)
    loads["context"].wait()
    in_rows(1, 0, 304)
    reducing.second(2)

    def out_rows(k, begin, end):
        for n in range(D // NBLOCK):
            lanes = slice(n * NBLOCK, (n + 1) * NBLOCK)
            got = matmul(context_t[begin:end, :], grad_attn[:, lanes])
            store(k, 1, begin, got, n * (NBLOCK // LANES))

    out_rows(1, 192, D)
    reducing.fourth(3)
    reducing.give(3)

    low, high = half_masks()
    rest = rest_ref[...]
    columns = jnp.concatenate([rest, jnp.zeros((LANES - 2, WINLEN), F32)], axis=0).T
    for part in range(BLOCKS):
        rows = slice(part * LANES, (part + 1) * LANES)
        for axis, less in ((0, less_x), (1, less_y)):
            less[rows, :] = jnp.where(
                rest[axis : axis + 1, :] < columns[rows, axis : axis + 1], 1.0, 0.0
            ).astype(BF16)
    hot_t[...] = hot_ref[...].T
    lane = lax.broadcasted_iota(jnp.int32, (1, LANES), 1)
    scale = HEAD_DIM ** (-0.5)
    of_x = jnp.where((lane // BUCKETS) % 2 == 0, 1.0, 0.0)
    for name in ("q", "k", "v"):
        loads[name].wait()

    def probs_copy(head, odd):
        return pltpu.make_async_copy(probs_in.at[head], probs.at[odd], probs_sems.at[odd])

    def one_pair(pair, carry):
        at = pl.multiple_of(pair * LANES, LANES)
        lanes = pl.ds(at, LANES)
        keys_t = k_ref[:, lanes].T
        cells_x = hot_ref[...] * of_x.astype(BF16)
        cells_y = hot_ref[...] * (1.0 - of_x).astype(BF16)
        for odd in range(2):
            mine, other = (low, high) if odd == 0 else (high, low)
            head = 2 * pair + odd
            probs_copy(head, odd).wait()
            qaug[...] = q_ref[:, lanes] * mine + hot_ref[...] * other
            grad_context = dctx[:, lanes]
            dot = None
            for part in range(BLOCKS):
                rows = slice(part * LANES, (part + 1) * LANES)
                dp = times_transposed(v_ref[rows, lanes] * mine, grad_context)
                scores[rows, :] = dp
                add = column_sum(dp * probs[odd, rows, :].astype(F32))
                dot = add if dot is None else dot + add
            band[...] = jnp.zeros_like(band)
            for part in range(BLOCKS):
                rows = slice(part * LANES, (part + 1) * LANES)
                share = probs[odd, rows, :]
                ds = share.astype(F32) * (scores[rows, :] - dot)
                for block in range(BLOCKS):
                    step = max(-2, min(2, block - part)) + 2
                    where = slice(step * LANES, (step + 1) * LANES)
                    band[:, where] = band[:, where] + ds[:, block * LANES : (block + 1) * LANES]
                ds = ds.astype(BF16)
                dscores[rows, :] = ds
                kept[odd, 0, rows, :] = matmul(ds, qaug[...])
                kept[odd, 1, rows, :] = matmul(ds * less_x[rows, :], cells_x) + matmul(
                    ds * less_y[rows, :], cells_y
                )
                kept[odd, 2, rows, :] = matmul(share, grad_context)

            @pl.when(pair < PAIRS - 1)
            def _():
                probs_copy(head + 2, odd).start()

            pair_t[odd * HEAD_DIM : (odd + 1) * HEAD_DIM, :] = matmul(
                keys_t[odd * HEAD_DIM : (odd + 1) * HEAD_DIM, :], dscores[...]
            )
            diag_rows[head, :, LANES : 5 * LANES] = diagonal_sums(band)
            diag_rows[head, :, :LANES] = column_sum(band[:, :LANES])
            diag_rows[head, :, 5 * LANES :] = column_sum(band[:, 4 * LANES :])
            sums = []
            for which in range(2):
                summed = kept[odd, which]
                first = summed.astype(BF16)
                remainder = (summed - first.astype(F32)).astype(BF16)
                sums.append(matmul(hot_t[:64, :], first) + matmul(hot_t[:64, :], remainder))
            for axis, value in enumerate(cell_sums(sums[0], sums[1], odd)):
                cell_rows[axis * HEADS + head] = value
        for which, value in (
            (0, pair_t[...].T * scale),
            (1, jnp.where(lane < HEAD_DIM, kept[0, 0], kept[1, 0])),
            (2, jnp.where(lane < HEAD_DIM, kept[0, 2], kept[1, 2])),
        ):
            value = value.astype(BF16)
            mixed[:, pl.ds(pl.multiple_of(at + which * D, LANES), LANES)] = value
            if which != 1:
                keep_vector("q_bias" if which == 0 else "v_bias", at, column_sum(value.astype(F32)))
        return carry

    lax.fori_loop(0, 2, one_pair, 0)
    reducing.third(2)
    lax.fori_loop(2, 4, one_pair, 0)
    reducing.fourth(2)
    reducing.give(2)
    lax.fori_loop(4, PAIRS, one_pair, 0)

    keep_vector("gain_two", 0, gain_two[0:1, :])
    keep_vector("shift_two", 0, gain_two[1:2, :])
    notes[...] = jnp.zeros_like(notes)
    table = VEC["tables"] // LANES
    for row in range(table):
        notes[row : row + 1, :] = vecg[0:1, row * LANES : (row + 1) * LANES]
    notes[table : table + 9, :] = bucket_rows(cell_rows, diag_rows)
    climbing.start()

    loads["w_qkv"].wait()
    for n in range(D // NBLOCK):
        lanes = slice(n * NBLOCK, (n + 1) * NBLOCK)
        value = second[:, lanes] + times_transposed(mixed[...], w_qkv[lanes, :])
        hidden_low[:, lanes] = value.astype(BF16)
    own_hidden = to_pos(hidden_low, hidden_pos, 1)
    loads["features"].wait()
    for n in range(D // NBLOCK):
        lanes = slice(n * NBLOCK, (n + 1) * NBLOCK)
        store(1, 2, 0, matmul(features_t[...], hidden_low[:, lanes]), n * (NBLOCK // LANES))
    reducing.settle(3)
    unstage_column(plan, flat, staged, 1)
    reducing.swap(1)
    climbing.rise()

    loads["low"].wait()
    for n in range(D // NBLOCK):
        rows = slice(n * NBLOCK, (n + 1) * NBLOCK)
        turned[rows, :] = low_t[:, rows].T

    def qkv_rows(n, carry):
        lanes = pl.ds(pl.multiple_of(n * NBLOCK, NBLOCK), NBLOCK)
        store(0, 0, 0, matmul(turned[...], mixed[:, lanes]), n * (NBLOCK // LANES))
        return carry

    lax.fori_loop(0, 3 * D // NBLOCK, qkv_rows, 0)
    out_rows(0, 0, 208)
    reducing.settle(2)
    unstage_column(plan, flat, staged, 0)
    reducing.swap(0)
    reducing.first(1)
    climbing.end()
    reducing.first(0)
    reducing.second(1)
    reducing.second(0)
    reducing.third(1)
    reducing.third(0)
    reducing.fourth(1)
    reducing.give(1)
    reducing.fourth(0)
    reducing.give(0)
    reducing.receive(out)
    note_quarter, note_first, note_row = note_place(plan)
    base = note_first + note_row

    @pl.when(climbing.root)
    def _():
        out[note_quarter, base : base + MISC_ROWS, :] = (
            out[note_quarter, base : base + MISC_ROWS, :] + notes[:MISC_ROWS, :]
        )

    in_pos(output_pos, 0)
    in_pos(hidden_pos, 1)
    own_output.wait()
    own_hidden.wait()
    for copy in positions:
        copy.wait_send()
    for k in range(COLUMNS):
        reducing.given(k)
    reducing.settle(1)
    reducing.settle(0)


def backward_pass(plan, operands):
    anywhere = pl.BlockSpec(memory_space=pl.ANY)
    vmem = pl.BlockSpec(memory_space=pltpu.VMEM)
    token = (WINLEN, D)
    block = (plan.quarter, LANES)
    positions = jax.ShapeDtypeStruct((DEPTH, WINLEN // DEPTH, D), BF16)
    scratch = [
        pltpu.VMEM((2, CORES, DEPTH, COLUMNS) + block, BF16),
        pltpu.VMEM((plan.staged, LANES), F32),
        pltpu.VMEM((2, DEPTH, COLUMNS) + block, BF16),
        pltpu.VMEM((COLUMNS, 2, 2) + block, BF16),
        pltpu.VMEM((COLUMNS, 2, DEPTH) + block, BF16),
        pltpu.VMEM((COLUMNS, DEPTH - 1) + block, BF16),
        pltpu.VMEM((COLUMNS,) + block, BF16),
        pltpu.VMEM((COLUMNS,) + block, BF16),
        pltpu.VMEM((WINLEN, FF), BF16),
        pltpu.VMEM((WINLEN, FF), BF16),
        pltpu.VMEM((FF, D), BF16),
        pltpu.VMEM((D, FF), BF16),
        pltpu.VMEM((D, D), BF16),
        pltpu.VMEM((D, WINLEN), BF16),
        pltpu.VMEM(token, BF16),
        pltpu.VMEM((D, WINLEN), BF16),
        pltpu.VMEM((D, WINLEN), BF16),
        pltpu.VMEM(token, BF16),
        pltpu.VMEM(token, BF16),
        pltpu.VMEM(token, BF16),
        pltpu.VMEM(token, F32),
        pltpu.VMEM(token, F32),
        pltpu.VMEM(token, BF16),
        pltpu.VMEM(token, BF16),
        pltpu.VMEM((2, WINLEN, WINLEN), BF16),
        pltpu.VMEM((WINLEN, WINLEN), BF16),
        pltpu.VMEM((WINLEN, WINLEN), BF16),
        pltpu.VMEM((WINLEN, WINLEN), F32),
        pltpu.VMEM((WINLEN, WINLEN), BF16),
        pltpu.VMEM((LANES, 5 * LANES), F32),
        pltpu.VMEM((2, 3, WINLEN, LANES), F32),
        pltpu.VMEM((LANES, WINLEN), BF16),
        pltpu.VMEM((WINLEN, LANES), BF16),
        pltpu.VMEM((LANES, WINLEN), F32),
        pltpu.VMEM((1, VEC_ROWS * LANES), F32),
        pltpu.VMEM((2 * HEADS, 1, LANES), F32),
        pltpu.VMEM((HEADS, 1, WIDE), F32),
        pltpu.VMEM((NOTE_ROWS, LANES), F32),
        pltpu.VMEM((7, NOTE_ROWS, LANES), F32),
        pltpu.SemaphoreType.DMA((16,)),
        pltpu.SemaphoreType.DMA((2,)),
        pltpu.SemaphoreType.REGULAR((2,)),
        pltpu.SemaphoreType.DMA((2, 2, DEPTH)),
        pltpu.SemaphoreType.DMA((2, 7)),
    ]
    return pl.pallas_call(
        functools.partial(backward_kernel, plan),
        out_shape=[jax.ShapeDtypeStruct((COLUMNS,) + block, F32), positions, positions],
        in_specs=[anywhere] * 16 + [vmem] * 5 + [anywhere],
        out_specs=[vmem, anywhere, anywhere],
        scratch_shapes=scratch + sem_shapes(REDUCE_SEMS),
        compiler_params=pltpu.CompilerParams(
            collective_id=1, has_side_effects=True, vmem_limit_bytes=62 * 2**20
        ),
        name="backward_pass",
    )(*operands)


def token_info(doc_lengths, box_coords):
    places = jnp.arange(WINLEN, dtype=jnp.int32)
    first = places == 0
    doc = jnp.zeros((WINLEN,), jnp.int32)
    end = 0
    for d in range(3):
        end = end + doc_lengths[d]
        doc = doc + (places >= end).astype(jnp.int32)
        first = first | (places == end)
    rows = [box_coords[:, c] for c in range(4)] + [doc, first.astype(jnp.int32)]
    return jnp.stack(rows + [jnp.zeros_like(doc)] * 2).astype(F32)


def fast_shards(hidden_in, cotangent, box_coords, doc_lengths, params, moment_one, moment_two):
    head_pos = lax.axis_index("head")
    shard_len = params.shape[0]
    plan = Plan(shard_len)
    own = params.astype(BF16).reshape(plan.rows, LANES)
    own = jnp.pad(own, ((0, plan.padded - plan.rows), (0, 0))).reshape(COLUMNS, plan.quarter, LANES)
    own_box = lax.dynamic_index_in_dim(box_coords, head_pos, 0, keepdims=False)
    own_lengths = lax.dynamic_index_in_dim(doc_lengths, head_pos, 0, keepdims=False)
    info = token_info(own_lengths, own_box)
    (proj_qkv, proj_out, proj_in, proj_back, features_t, start_low, queries, keys, values, probs, context_t,
     xhat, normed_low, active, slope, grad_second, vec, rstd, grad_norm_two, output, _, hot_two,
     rest_rows) = forward_pass(plan, own, hidden_in, cotangent, info)
    summed, output_low, grad_hidden = backward_pass(
        Plan(shard_len, carry=5 * LANES),
        (active, slope, proj_back, proj_in, proj_out, proj_qkv, normed_low, start_low, features_t, context_t,
         queries, keys, values, probs, xhat, grad_second, rstd, vec, grad_norm_two, hot_two, rest_rows,
         output),
    )
    grad_share = summed.reshape(plan.padded, LANES)[: plan.rows].reshape(-1)
    return finish_step(output_low, grad_hidden, grad_share, params, moment_one, moment_two)


def finish_step(output_low, grad_hidden, grad_share, params, moment_one, moment_two):
    shard_len = params.shape[0]
    index = lax.axis_index("dp") * lax.axis_size("head") + lax.axis_index("head")
    flat_index = index * shard_len + jnp.arange(shard_len, dtype=jnp.int32)
    param_step, new_one = adam_step(params, moment_one, moment_two, grad_share, flat_index)
    return (output_low, grad_hidden, grad_share, param_step, new_one)


def to_windows(shard):
    return lax.all_to_all(shard, "head", split_axis=0, concat_axis=1, tiled=True)


def to_positions(window):
    return lax.all_to_all(window, "head", split_axis=1, concat_axis=0, tiled=True)


def plain_shards(hidden_in, cotangent, box_coords, doc_lengths, params, moment_one, moment_two):
    head_pos = lax.axis_index("head")
    groups = lax.axis_size("head")
    shard_len = params.shape[0]
    flat_params = lax.all_gather(params.astype(BF16), ("dp", "head"), axis=0, tiled=True)
    pieces = unpack(flat_params)
    hidden = to_windows(hidden_in).reshape(WINLEN, D)
    cot = to_windows(cotangent).reshape(WINLEN, D)
    own_box = lax.dynamic_index_in_dim(box_coords, head_pos, 0, keepdims=False)
    own_lengths = lax.dynamic_index_in_dim(doc_lengths, head_pos, 0, keepdims=False)
    chosen, relative, centre_x, centre_y = window_layout(own_lengths, own_box)
    features = box_features(relative).astype(BF16)

    proj_qkv, proj_out, proj_box, proj_in, proj_back = pieces[:5]
    qv_bias, out_bias, norm_one, in_bias, back_bias, norm_two, tables = pieces[5:]
    ops = bias_operands(tables, chosen, centre_x, centre_y)
    start_state = hidden.astype(F32) + matmul(features, proj_box)
    start_low = start_state.astype(BF16)
    qv_float = qv_bias.astype(F32)
    mixed = matmul(start_low, proj_qkv)
    queries = (mixed[:, :D] + qv_float[0]).astype(BF16) * jnp.asarray(HEAD_DIM ** (-0.5), BF16)
    keys = mixed[:, D : 2 * D].astype(BF16)
    values = (mixed[:, 2 * D :] + qv_float[1]).astype(BF16)

    probs, context_t = attention_forward(queries, keys, values, ops)
    first_sum = start_state + rows_inner(context_t, proj_out) + out_bias.astype(F32)
    normed, norm_one_back = jax.vjp(layer_norm, first_sum, norm_one.astype(F32))
    normed_low = normed.astype(BF16)
    inner_act = matmul(normed_low, proj_in) + in_bias.astype(F32)
    active, gelu_back = jax.vjp(gelu_exact, inner_act)
    active_low = active.astype(BF16)
    second_sum = normed + matmul(active_low, proj_back) + back_bias.astype(F32)
    output, norm_two_back = jax.vjp(layer_norm, second_sum, norm_two.astype(F32))
    output_low = to_positions(output.astype(BF16).reshape(1, WINLEN, D))

    grad_second, grad_norm_two = norm_two_back(cot.astype(F32))
    grad_branch = grad_second.astype(BF16)
    grad_proj_back = rows_inner(active_low, grad_branch)
    grad_back_bias = jnp.sum(grad_branch.astype(F32), axis=0)
    (grad_inner_f,) = gelu_back(times_transposed(grad_branch, proj_back))
    grad_inner = grad_inner_f.astype(BF16)
    grad_proj_in = rows_inner(normed_low, grad_inner)
    grad_in_bias = jnp.sum(grad_inner.astype(F32), axis=0)
    grad_first, grad_norm_one = norm_one_back(grad_second + times_transposed(grad_inner, proj_in))
    grad_attn = grad_first.astype(BF16)
    grad_proj_out = matmul(context_t, grad_attn)
    grad_out_bias = jnp.sum(grad_attn.astype(F32), axis=0)
    grad_context = times_transposed(grad_attn, proj_out).astype(BF16)
    grad_queries_t, grad_keys, grad_values, cells, diag = attention_backward(
        queries, keys, values, grad_context, probs, ops
    )
    table_grad = table_grads(cells, diag)
    grad_mixed = jnp.concatenate([grad_queries_t.T, grad_keys, grad_values], axis=1)
    grad_proj_qkv = rows_inner(start_low, grad_mixed)
    summed = jnp.sum(grad_mixed.astype(F32), axis=0)
    grad_qv_bias = jnp.stack([summed[:D], summed[2 * D :]])
    grad_start = grad_first + times_transposed(grad_mixed, proj_qkv)
    grad_start_low = grad_start.astype(BF16)
    grad_hidden = to_positions(grad_start_low.reshape(1, WINLEN, D))
    grad_proj_box = rows_inner(features, grad_start_low)
    grad_list = (
        grad_proj_qkv,
        grad_proj_out,
        grad_proj_box,
        grad_proj_in,
        grad_proj_back,
        grad_qv_bias,
        grad_out_bias,
        grad_norm_one,
        grad_in_bias,
        grad_back_bias,
        grad_norm_two,
        table_grad,
    )
    padding = jnp.zeros((shard_len * groups * lax.axis_size("dp") - USED,), BF16)
    grads_flat = jnp.concatenate([piece.astype(BF16).reshape(-1) for piece in grad_list] + [padding])
    grad_share = lax.psum_scatter(
        grads_flat, ("dp", "head"), scatter_dimension=0, tiled=True
    ).astype(F32)
    return finish_step(output_low, grad_hidden, grad_share, params, moment_one, moment_two)


def solution(mesh):
    placed = (
        P("dp", "head", None),
        P("dp", "head", None),
        P("dp", None, None),
        P("dp", None),
        P(("dp", "head")),
        P(("dp", "head")),
        P(("dp", "head")),
    )
    return jax.shard_map(
        fast_shards if fits(mesh) else plain_shards,
        mesh=mesh,
        in_specs=placed,
        out_specs=(
            P("dp", "head", None),
            P("dp", "head", None),
            P(("dp", "head")),
            P(("dp", "head")),
            P(("dp", "head")),
        ),
        check_vma=False,
    )
```

```python
import functools
import math

import jax
import jax.numpy as jnp
import numpy as np
from jax import lax
from jax.experimental import pallas as pl
from jax.experimental.pallas import tpu as pltpu
from jax.sharding import PartitionSpec as P

D = 768
HEADS = 12
FF = 3072
BUCKETS = 32
WINLEN = 512
HEAD_DIM = 64
PAIRS = HEADS // 2
LANES = 128
BLOCKS = WINLEN // LANES

beta_one = 0.9
beta_two = 0.999
adam_eps = 1e-08
norm_eps = 1e-05
base_rate = 0.001
layer_decay = 0.75
decay_weight = 0.01
adam_count = 100
coord_cell = 32
masked_score = -1e30

F32 = jnp.float32
BF16 = jnp.bfloat16


def layouts_list():
    return (
        (D, 3 * D),
        (D, D),
        (D, D),
        (D, FF),
        (FF, D),
        (2, D),
        (D,),
        (2, D),
        (FF,),
        (D,),
        (2, D),
        (3, HEADS, BUCKETS),
    )


def unpack(flat_params):
    pieces = []
    offset = 0
    for layout in layouts_list():
        elements = math.prod(layout)
        pieces.append(flat_params[offset : offset + elements].reshape(layout))
        offset += elements
    return pieces


def matmul(left_mat, right_mat):
    return jnp.dot(left_mat, right_mat, preferred_element_type=F32)


def rows_inner(left_mat, right_mat):
    return lax.dot_general(left_mat, right_mat, (((0,), (0,)), ((), ())), preferred_element_type=F32)


def times_transposed(left_mat, right_mat):
    return lax.dot_general(left_mat, right_mat, (((1,), (1,)), ((), ())), preferred_element_type=F32)


def layer_norm(values, gain_bias):
    row_mean = jnp.mean(values, axis=-1, keepdims=True)
    centred = values - row_mean
    spread = jnp.mean(centred * centred, axis=-1, keepdims=True)
    return centred * lax.rsqrt(spread + norm_eps) * gain_bias[0] + gain_bias[1]


def gelu_exact(values):
    return jax.nn.gelu(values, approximate=False)


def hot(index, count):
    return (np.asarray(index)[..., None] == np.arange(count)).astype(np.float32)


def clipped(steps):
    return np.clip(steps, -(BUCKETS // 2), BUCKETS // 2 - 1) + BUCKETS // 2


CELLS = np.arange(BUCKETS)
HOT_SAME = hot(clipped(CELLS[:, None] - CELLS[None, :]), BUCKETS)
HOT_LESS = hot(clipped(CELLS[:, None] - CELLS[None, :] - 1), BUCKETS)
WIDE = 6 * LANES
_U = np.arange(WIDE)
BAND_HOT = hot(np.where(_U < 5 * LANES, clipped(_U - 2 * LANES), 0), BUCKETS)
_V = np.arange(4 * LANES)
DIAG_HOT = np.concatenate(
    [
        hot(np.zeros(LANES, np.int64), BUCKETS),
        hot(np.where(_V < 3 * LANES, clipped(_V - LANES), 0), BUCKETS),
        hot(np.full(LANES, BUCKETS - 1), BUCKETS),
    ]
)


def window_layout(doc_lengths, box_coords):
    doc_ends = jnp.cumsum(doc_lengths, dtype=jnp.int32)
    doc_starts = doc_ends - doc_lengths
    places = jnp.arange(WINLEN, dtype=jnp.int32)
    doc_ids = jnp.sum(
        (places[:, None] >= doc_ends[None, :]).astype(jnp.int32), axis=1, dtype=jnp.int32
    )
    docs = jnp.arange(doc_lengths.shape[0], dtype=jnp.int32)
    chosen = doc_ids[:, None] == docs[None, :]
    first_hot = places[:, None] == doc_starts[None, :]
    first_box = jnp.sum(
        jnp.where(first_hot[:, :, None], box_coords[:, None, :], 0), axis=0, dtype=jnp.int32
    )
    anchor = jnp.sum(
        jnp.where(chosen[:, :, None], first_box[None, :, :], 0), axis=1, dtype=jnp.int32
    )
    relative = box_coords - jnp.concatenate([anchor[:, :2], anchor[:, :2]], axis=1)
    centre_x = (box_coords[:, 0] + box_coords[:, 2]) // 2
    centre_y = (box_coords[:, 1] + box_coords[:, 3]) // 2
    return chosen, relative, centre_x, centre_y


def box_features(relative):
    count_freq = D // 8
    steps = jnp.arange(count_freq, dtype=F32)
    frequency = jnp.exp(steps * (-math.log(1000.0) / count_freq))
    angles = relative.astype(F32)[:, :, None] * frequency[None, None, :]
    return jnp.concatenate([jnp.sin(angles), jnp.cos(angles)], axis=2).reshape(relative.shape[0], D)


def bias_operands(tables, chosen, centre_x, centre_y):
    cell_x, cell_y = centre_x // coord_cell, centre_y // coord_cell
    rest_x, rest_y = centre_x % coord_cell, centre_y % coord_cell
    cells = jnp.arange(BUCKETS, dtype=jnp.int32)
    hot_x = (cell_x[:, None] == cells[None, :]).astype(BF16)
    hot_y = (cell_y[:, None] == cells[None, :]).astype(BF16)
    none = jnp.zeros_like(hot_x)
    hot_two = jnp.concatenate([hot_x, hot_y, hot_x, hot_y], axis=1)
    key_x = jnp.stack(
        [
            jnp.concatenate([hot_x, -hot_x, none, none], axis=1),
            jnp.concatenate([none, none, hot_x, -hot_x], axis=1),
        ]
    )
    key_y = jnp.stack(
        [
            jnp.concatenate([hot_y, -hot_y, none, none], axis=1),
            jnp.concatenate([none, none, hot_y, -hot_y], axis=1),
        ]
    )
    same = jnp.einsum("qcb,thb->thqc", HOT_SAME.astype(BF16), tables[1:], preferred_element_type=F32)
    less = jnp.einsum("qcb,thb->thqc", HOT_LESS.astype(BF16), tables[1:], preferred_element_type=F32)
    zero = jnp.zeros_like(same[0])
    base = jnp.concatenate(
        [jnp.concatenate([same[0], zero], axis=2), jnp.concatenate([zero, same[1]], axis=2)], axis=1
    )
    base = base.reshape(PAIRS, 2, 64, 64)[:, ::-1].reshape(HEADS, 64, 64)
    diff_x = jnp.concatenate([jnp.concatenate([less[0], same[0]], axis=2), jnp.zeros((HEADS, 32, 64), F32)], axis=1)
    diff_y = jnp.concatenate([jnp.zeros((HEADS, 32, 64), F32), jnp.concatenate([less[1], same[1]], axis=2)], axis=1)
    rows = jnp.concatenate([base, diff_x, diff_y], axis=0).astype(BF16)
    rows = rows.transpose(1, 0, 2).reshape(64, 3 * D)
    met = matmul(hot_two[:, :64], rows).astype(BF16)
    band = matmul(tables[0], jnp.asarray(BAND_HOT.T, BF16)).reshape(HEADS, 1, WIDE)
    rest_cols = jnp.stack([rest_x, rest_y], axis=1).astype(F32)
    rest_rows = rest_cols.T
    pad = jnp.zeros((WINLEN, LANES - chosen.shape[1]), BF16)
    marks = chosen.astype(BF16)
    mark_keys = jnp.concatenate([marks, pad], axis=1)
    mark_queries = jnp.concatenate([(1 - marks) * jnp.asarray(masked_score, BF16), pad], axis=1)
    return dict(
        hot_two=hot_two,
        key_x=key_x,
        key_y=key_y,
        met=met,
        band=band,
        rest_cols=rest_cols,
        rest_rows=rest_rows,
        mark_keys=mark_keys,
        mark_queries=mark_queries,
    )


def half_masks():
    lane = lax.broadcasted_iota(jnp.int32, (1, LANES), 1)
    low = (lane < HEAD_DIM).astype(F32)
    return low.astype(BF16), (1.0 - low).astype(BF16)


def less_masks(rest_cols, rest_rows, less_x, less_y):
    for part in range(BLOCKS):
        rows = slice(part * LANES, (part + 1) * LANES)
        for axis, less in ((0, less_x), (1, less_y)):
            column = rest_cols[rows, axis : axis + 1]
            row = rest_rows[axis : axis + 1, :]
            less[rows, :] = jnp.where(row < column, 1.0, 0.0).astype(less.dtype)


def attention_forward_kernel(
    q_ref, k_ref, v_ref, hot_ref, keyx_ref, keyy_ref, met_ref, band_ref, cols_ref, rows_ref,
    mkey_ref, mquery_ref, probs_ref, context_ref,
    kaug, qaug, less_x, less_y, wide, scores,
):
    low, high = half_masks()
    less_masks(cols_ref, rows_ref, less_x, less_y)
    kaug[:, LANES:] = mkey_ref[...]
    qaug[:, LANES:] = mquery_ref[...]
    half = 2 * LANES

    def one_pair(pair, carry):
        at = pl.multiple_of(pair * LANES, LANES)
        lanes = pl.ds(at, LANES)
        lanes_x = pl.ds(pl.multiple_of(at + D, LANES), LANES)
        lanes_y = pl.ds(pl.multiple_of(at + 2 * D, LANES), LANES)
        values_t = v_ref[:, lanes].T
        for odd in range(2):
            own, other = (low, high) if odd == 0 else (high, low)
            head = 2 * pair + odd
            kaug[:, :LANES] = k_ref[:, lanes] * own + hot_ref[...] * other
            qaug[:, :LANES] = q_ref[:, lanes] * own + met_ref[:, lanes] * other
            skew_band(band_ref[head], wide)
            for side in range(2):
                cols = slice(side * half, (side + 1) * half)
                top = None
                for part in range(BLOCKS):
                    rows = slice(part * LANES, (part + 1) * LANES)
                    s = times_transposed(kaug[rows, :], qaug[cols, :])
                    dx = times_transposed(keyx_ref[odd, rows, :], met_ref[cols, lanes_x])
                    dy = times_transposed(keyy_ref[odd, rows, :], met_ref[cols, lanes_y])
                    bias = []
                    for block in range(2 * side, 2 * side + 2):
                        step = max(-2, min(2, block - part)) + 2
                        bias.append(wide[:, step * LANES : (step + 1) * LANES])
                    s = s + jnp.concatenate(bias, axis=1)
                    s = s + dx * less_x[rows, cols] + dy * less_y[rows, cols]
                    scores[rows, :] = s
                    best = jnp.max(s, axis=0, keepdims=True)
                    top = best if top is None else jnp.maximum(top, best)
                total = None
                for part in range(BLOCKS):
                    rows = slice(part * LANES, (part + 1) * LANES)
                    e = jnp.exp(scores[rows, :] - top)
                    scores[rows, :] = e
                    add = jnp.sum(e, axis=0, keepdims=True)
                    total = add if total is None else total + add
                share = 1.0 / total
                for part in range(BLOCKS):
                    rows = slice(part * LANES, (part + 1) * LANES)
                    probs_ref[head, rows, cols] = (scores[rows, :] * share).astype(BF16)
                got = matmul(
                    values_t[odd * HEAD_DIM : (odd + 1) * HEAD_DIM, :], probs_ref[head, :, cols]
                )
                context_ref[pl.ds(pl.multiple_of(head * HEAD_DIM, HEAD_DIM), HEAD_DIM), cols] = (
                    got.astype(BF16)
                )
        return carry

    lax.fori_loop(0, PAIRS, one_pair, 0)


def skew_band(row, wide):
    x = jnp.broadcast_to(row, (8, WIDE))
    sub = lax.broadcasted_iota(jnp.int32, (8, WIDE), 0)
    for bit in (1, 2, 4):
        x = jnp.where((sub & bit) != 0, pltpu.roll(x, bit, 1), x)
    for group in range(LANES // 8):
        y = x if group == 0 else pltpu.roll(x, 8 * group, 1)
        wide[8 * group : 8 * group + 8, :] = y[:, : 5 * LANES]


def diagonal_sums(parts):
    total = None
    for group in range(LANES // 8):
        x = jnp.concatenate(
            [parts[8 * group : 8 * group + 8, LANES : 4 * LANES], jnp.zeros((8, LANES), F32)], axis=1
        )
        y = x if group == 0 else pltpu.roll(x, 4 * LANES - 8 * group, 1)
        total = y if total is None else total + y
    sub = lax.broadcasted_iota(jnp.int32, (8, 4 * LANES), 0)
    for bit in (1, 2, 4):
        total = jnp.where((sub & bit) != 0, pltpu.roll(total, 4 * LANES - bit, 1), total)
    return jnp.sum(total, axis=0, keepdims=True)


def attention_backward_kernel(
    q_ref, k_ref, v_ref, dctx_ref, probs_ref, hot_ref, cols_ref, rows_ref,
    dq_ref, dk_ref, dv_ref, cells_ref, diag_ref,
    qaug, less_x, less_y, scores, dscores, band, kept, hot_t,
):
    low, high = half_masks()
    less_masks(cols_ref, rows_ref, less_x, less_y)
    hot_t[...] = hot_ref[...].T
    lane = lax.broadcasted_iota(jnp.int32, (1, LANES), 1)
    scale = HEAD_DIM ** (-0.5)
    of_x = jnp.where((lane // BUCKETS) % 2 == 0, 1.0, 0.0)
    cells_x = hot_ref[...] * of_x.astype(BF16)
    cells_y = hot_ref[...] * (1.0 - of_x).astype(BF16)

    def one_pair(pair, carry):
        at = pl.multiple_of(pair * LANES, LANES)
        lanes = pl.ds(at, LANES)
        keys_t = k_ref[:, lanes].T
        for odd in range(2):
            own, other = (low, high) if odd == 0 else (high, low)
            head = 2 * pair + odd
            qaug[...] = q_ref[:, lanes] * own + hot_ref[...] * other
            dctx = dctx_ref[:, lanes]
            dot = None
            for part in range(BLOCKS):
                rows = slice(part * LANES, (part + 1) * LANES)
                dp = times_transposed(v_ref[rows, lanes] * own, dctx)
                scores[rows, :] = dp
                add = jnp.sum(dp * probs_ref[head, rows, :].astype(F32), axis=0, keepdims=True)
                dot = add if dot is None else dot + add
            band[...] = jnp.zeros_like(band)
            for part in range(BLOCKS):
                rows = slice(part * LANES, (part + 1) * LANES)
                probs = probs_ref[head, rows, :]
                ds = probs.astype(F32) * (scores[rows, :] - dot)
                for block in range(BLOCKS):
                    step = max(-2, min(2, block - part)) + 2
                    where = slice(step * LANES, (step + 1) * LANES)
                    band[:, where] = band[:, where] + ds[:, block * LANES : (block + 1) * LANES]
                ds = ds.astype(BF16)
                dscores[rows, :] = ds
                both = matmul(ds, qaug[...])
                less = matmul(ds * less_x[rows, :], cells_x) + matmul(ds * less_y[rows, :], cells_y)
                dv = matmul(probs, dctx)
                kept[odd, 0, rows, :] = both
                kept[odd, 1, rows, :] = less
                kept[odd, 2, rows, :] = dv
            got = matmul(keys_t[odd * HEAD_DIM : (odd + 1) * HEAD_DIM, :], dscores[...])
            dq_ref[pl.ds(pl.multiple_of(head * HEAD_DIM, HEAD_DIM), HEAD_DIM), :] = (
                got * scale
            ).astype(BF16)
            diag_ref[head, :, LANES : 5 * LANES] = diagonal_sums(band)
            diag_ref[head, :, :LANES] = jnp.sum(band[:, :LANES], axis=0, keepdims=True)
            diag_ref[head, :, 5 * LANES :] = jnp.sum(band[:, 4 * LANES :], axis=0, keepdims=True)
            for which in range(2):
                summed = kept[odd, which]
                first = summed.astype(BF16)
                rest = (summed - first.astype(F32)).astype(BF16)
                cells_ref[head, which] = matmul(hot_t[:64, :], first) + matmul(hot_t[:64, :], rest)
        dk_ref[:, lanes] = jnp.where(lane < HEAD_DIM, kept[0, 0], kept[1, 0]).astype(BF16)
        dv_ref[:, lanes] = jnp.where(lane < HEAD_DIM, kept[0, 2], kept[1, 2]).astype(BF16)
        return carry

    lax.fori_loop(0, PAIRS, one_pair, 0)


def attention_forward(queries, keys, values, ops):
    return pl.pallas_call(
        attention_forward_kernel,
        out_shape=(
            jax.ShapeDtypeStruct((HEADS, WINLEN, WINLEN), BF16),
            jax.ShapeDtypeStruct((D, WINLEN), BF16),
        ),
        scratch_shapes=[
            pltpu.VMEM((WINLEN, 2 * LANES), BF16),
            pltpu.VMEM((WINLEN, 2 * LANES), BF16),
            pltpu.VMEM((WINLEN, WINLEN), F32),
            pltpu.VMEM((WINLEN, WINLEN), F32),
            pltpu.VMEM((LANES, 5 * LANES), F32),
            pltpu.VMEM((WINLEN, 2 * LANES), F32),
        ],
        compiler_params=pltpu.CompilerParams(vmem_limit_bytes=48 * 2**20),
        name="attention_forward",
    )(
        queries, keys, values, ops["hot_two"], ops["key_x"], ops["key_y"], ops["met"], ops["band"],
        ops["rest_cols"], ops["rest_rows"], ops["mark_keys"], ops["mark_queries"],
    )


def attention_backward(queries, keys, values, grad_context, probs, ops):
    return pl.pallas_call(
        attention_backward_kernel,
        out_shape=(
            jax.ShapeDtypeStruct((D, WINLEN), BF16),
            jax.ShapeDtypeStruct((WINLEN, D), BF16),
            jax.ShapeDtypeStruct((WINLEN, D), BF16),
            jax.ShapeDtypeStruct((HEADS, 2, 64, LANES), F32),
            jax.ShapeDtypeStruct((HEADS, 1, WIDE), F32),
        ),
        scratch_shapes=[
            pltpu.VMEM((WINLEN, LANES), BF16),
            pltpu.VMEM((WINLEN, WINLEN), BF16),
            pltpu.VMEM((WINLEN, WINLEN), BF16),
            pltpu.VMEM((WINLEN, WINLEN), F32),
            pltpu.VMEM((WINLEN, WINLEN), BF16),
            pltpu.VMEM((LANES, 5 * LANES), F32),
            pltpu.VMEM((2, 3, WINLEN, LANES), F32),
            pltpu.VMEM((LANES, WINLEN), BF16),
        ],
        compiler_params=pltpu.CompilerParams(vmem_limit_bytes=48 * 2**20),
        name="attention_backward",
    )(
        queries, keys, values, grad_context, probs, ops["hot_two"], ops["rest_cols"],
        ops["rest_rows"],
    )


def table_grads(cells, diag):
    exact = lax.Precision.HIGHEST
    pairs = cells.reshape(PAIRS, 2, 2, 64, LANES)
    every = jnp.stack([pairs[:, 0, 0, :, 64:], pairs[:, 1, 0, :, :64]], axis=1).reshape(HEADS, 64, 64)
    less = cells[:, 1]
    less_x, less_y = less[:, :32, :32], less[:, 32:, 32:64]
    all_x, all_y = every[:, :32, :32], every[:, 32:, 32:]
    same = jnp.stack([all_x - less_x, all_y - less_y]).reshape(2 * HEADS, -1)
    below = jnp.stack([less_x, less_y]).reshape(2 * HEADS, -1)
    same_hot = jnp.asarray(HOT_SAME.transpose(1, 0, 2).reshape(-1, BUCKETS))
    less_hot = jnp.asarray(HOT_LESS.transpose(1, 0, 2).reshape(-1, BUCKETS))
    moved = jnp.dot(same, same_hot, precision=exact) + jnp.dot(below, less_hot, precision=exact)
    along = jnp.dot(diag.reshape(HEADS, WIDE), jnp.asarray(DIAG_HOT), precision=exact)
    return jnp.concatenate([along[None], moved.reshape(2, HEADS, BUCKETS)], axis=0)


COLUMNS = 4
CORES = 2
DEPTH = 4
USED = sum(math.prod(layout) for layout in layouts_list())
MATRICES = layouts_list()[:5]
MISC = sum(math.prod(layout) for layout in layouts_list()[5:])
MISC_ROWS = -(-MISC // (8 * LANES)) * 8


class Plan:
    def __init__(self, shard_len, carry=3 * LANES):
        self.rows = shard_len // LANES
        self.quarter = -(-self.rows // (16 * COLUMNS)) * 16
        self.padded = COLUMNS * self.quarter
        self.per_column = CORES * DEPTH * self.rows
        self.carry = carry
        self.staged = self.carry + self.per_column + 3 * LANES
        starts = []
        offset = 0
        for depth, width in MATRICES:
            starts.append(offset // LANES)
            offset += depth * width
        self.starts = starts
        self.misc_start = offset // LANES


def fits(mesh):
    return mesh.shape["dp"] == COLUMNS * CORES and mesh.shape["head"] == DEPTH


MESH = pl.DeviceIdType.MESH


class Place:
    def __init__(self):
        dp = lax.axis_index("dp")
        self.z = lax.axis_index("head")
        self.core = dp % CORES
        self.column = dp // CORES
        self.x = self.column % 2
        self.y = self.column // 2
        self.col_x = 2 * self.y + (1 - self.x)
        self.col_y = 2 * (1 - self.y) + self.x
        self.col_d = 2 * (1 - self.y) + (1 - self.x)
        self.peer_x = self.at(self.col_x, self.core, self.z)
        self.peer_y = self.at(self.col_y, self.core, self.z)
        self.peer_d = self.at(self.col_d, self.core, self.z)
        self.peer_core = self.at(self.column, 1 - self.core, self.z)
        self.far = [lax.rem(self.z + d, DEPTH) for d in range(1, DEPTH)]
        self.from_far = [lax.rem(self.z + DEPTH - d, DEPTH) for d in range(1, DEPTH)]
        self.peers_z = [self.at(self.column, self.core, f) for f in self.far]

    def at(self, column, core, z):
        return {"dp": column * CORES + core, "head": z}

    def greet(self):
        barrier = pltpu.get_barrier_semaphore()
        peers = [self.peer_x, self.peer_y, self.peer_d, self.peer_core] + self.peers_z
        for peer in peers:
            pl.semaphore_signal(barrier, inc=1, device_id=peer, device_id_type=MESH)
        pl.semaphore_wait(barrier, len(peers))


def remote(src, dst, send_sem, recv_sem, peer):
    return pltpu.make_async_remote_copy(
        src_ref=src, dst_ref=dst, send_sem=send_sem, recv_sem=recv_sem, device_id=peer,
        device_id_type=MESH,
    )


class Gathering:
    def __init__(self, place, flat, sems):
        self.place = place
        self.flat = flat
        self.sems = sems
        self.sent = []

    def send(self, src, dst, kind, index, peer):
        copy = remote(src, dst, self.sems[kind].at[0, index], self.sems[kind].at[1, index], peer)
        copy.start()
        self.sent.append(copy)

    def got(self, dst, kind, index):
        remote(
            dst, dst, self.sems[kind].at[0, index], self.sems[kind].at[1, index], self.place.peer_x
        ).wait_recv()

    def spread(self, own):
        p = self.place
        for index, (column, peer) in enumerate(
            ((p.col_x, p.peer_x), (p.col_y, p.peer_y), (p.col_d, p.peer_d))
        ):
            self.send(
                own.at[column], self.flat.at[p.column, p.core, p.z, column], "spread", index, peer
            )
        self.flat[p.column, p.core, p.z, p.column] = own[p.column]

    def spread_done(self):
        p = self.place
        for index, column in enumerate((p.col_x, p.col_y, p.col_d)):
            self.got(self.flat.at[column, p.core, p.z, p.column], "spread", index)

    def along_z(self, k):
        p = self.place
        piece = self.flat.at[k, p.core, p.z, p.column]
        for d in range(DEPTH - 1):
            self.send(piece, piece, "z", 3 * k + d, p.peers_z[d])

    def first(self, k):
        p = self.place
        for d in range(DEPTH - 1):
            self.got(self.flat.at[k, p.core, p.from_far[d], p.column], "z", 3 * k + d)
        piece = self.flat.at[k, p.core, :, p.column]
        self.send(piece, piece, "one", 2 * k, p.peer_x)
        self.send(piece, piece, "one", 2 * k + 1, p.peer_y)
        self.send(piece, piece, "core", 5 * k, p.peer_core)

    def second(self, k):
        p = self.place
        from_x = self.flat.at[k, p.core, :, p.col_x]
        self.got(from_x, "one", 2 * k)
        part = self.flat.at[k, p.core, 0:2, p.col_x]
        self.send(part, part, "two", 2 * k, p.peer_y)
        self.send(from_x, from_x, "core", 5 * k + 1, p.peer_core)
        from_y = self.flat.at[k, p.core, :, p.col_y]
        self.got(from_y, "one", 2 * k + 1)
        part = self.flat.at[k, p.core, 2:4, p.col_y]
        self.send(part, part, "two", 2 * k + 1, p.peer_x)
        self.send(from_y, from_y, "core", 5 * k + 2, p.peer_core)

    def third(self, k):
        p = self.place
        part = self.flat.at[k, p.core, 0:2, p.col_d]
        self.got(part, "two", 2 * k)
        self.send(part, part, "core", 5 * k + 3, p.peer_core)
        part = self.flat.at[k, p.core, 2:4, p.col_d]
        self.got(part, "two", 2 * k + 1)
        self.send(part, part, "core", 5 * k + 4, p.peer_core)

    def complete(self, k):
        p = self.place
        other = 1 - p.core
        for index, column in enumerate((p.column, p.col_x, p.col_y)):
            self.got(self.flat.at[k, other, :, column], "core", 5 * k + index)
        self.got(self.flat.at[k, other, 0:2, p.col_d], "core", 5 * k + 3)
        self.got(self.flat.at[k, other, 2:4, p.col_d], "core", 5 * k + 4)

    def finish(self):
        for copy in self.sent:
            copy.wait_send()


GATHER_SEMS = {"spread": 3, "z": 12, "one": 8, "two": 8, "core": 20}


def sem_shapes(counts):
    return [pltpu.SemaphoreType.DMA((2, count)) for count in counts.values()]


def stage_column(plan, flat, staged, k):
    def one(shard, carry):
        core, z = shard // DEPTH, shard % DEPTH
        for quarter in range(COLUMNS):
            base = plan.carry + shard * plan.rows + quarter * plan.quarter
            staged[pl.ds(pl.multiple_of(base, 8), plan.quarter), :] = flat[k, core, z, quarter].astype(F32)
        return carry

    lax.fori_loop(0, CORES * DEPTH, one, 0)


def keep_carry(plan, staged):
    end = plan.carry + plan.per_column
    staged[: plan.carry, :] = staged[end - plan.carry : end, :]


ROW_STEP = 48


def column_rows(plan, k, touching):
    low, high = k * plan.per_column, (k + 1) * plan.per_column
    taken = []
    for index, (depth, width) in enumerate(MATRICES):
        group = 16 * (width // LANES)
        from_low, from_high = low - plan.starts[index], high - plan.starts[index]
        begin = max(0, min(depth, from_low // group * 16))
        if touching:
            end = max(0, min(depth, -(-from_high // group) * 16))
        else:
            end = max(0, min(depth, from_high // group * 16))
        if end > begin:
            taken.append((index, begin, end))
    return taken


def staged_at(plan, k, row):
    return plan.carry + row - k * plan.per_column


def row_loops(rows):
    whole = rows // ROW_STEP
    loops = [(ROW_STEP, 0, whole)] if whole else []
    if rows % ROW_STEP:
        loops.append((16, whole * ROW_STEP, (rows % ROW_STEP) // 16))
    return loops


def form_matrices(plan, staged, matrices, k):
    for index, begin, end in column_rows(plan, k, False):
        blocks = MATRICES[index][1] // LANES
        base = staged_at(plan, k, plan.starts[index] + begin * blocks)
        assert 0 <= base
        target = matrices[index]
        for step_rows, first, count in row_loops(end - begin):

            def one(step, carry, step_rows=step_rows, first=first, blocks=blocks, base=base,
                    begin=begin, target=target):
                row = first + step * step_rows
                for block in range(blocks):
                    got = staged[pl.ds(base + row * blocks + block, step_rows, stride=blocks), :]
                    target[
                        pl.ds(pl.multiple_of(begin + row, 16), step_rows),
                        block * LANES : (block + 1) * LANES,
                    ] = got.astype(BF16)
                return carry

            lax.fori_loop(0, count, one, 0)


def adam_step(params, moment_one, moment_two, grads, flat_index):
    box_part = (flat_index >= 4 * D * D) & (flat_index < 5 * D * D)
    step_rate = jnp.where(box_part, base_rate * layer_decay**12, base_rate * layer_decay)
    decay_mask = jnp.where(flat_index < 5 * D * D + 2 * D * FF, decay_weight, 0.0)
    moment_one = beta_one * moment_one + (1.0 - beta_one) * grads
    moment_two = beta_two * moment_two + (1.0 - beta_two) * grads * grads
    first_hat = moment_one / (1.0 - beta_one**adam_count)
    second_hat = moment_two / (1.0 - beta_two**adam_count)
    update = first_hat / (jnp.sqrt(second_hat) + adam_eps) + decay_mask * params
    return (-step_rate * update, moment_one)


VEC = {}
_at = 0
for _name, _rows in (
    ("q_bias", 6), ("v_bias", 6), ("out_bias", 6), ("gain_one", 6), ("shift_one", 6), ("in_bias", 24),
    ("back_bias", 6), ("gain_two", 6), ("shift_two", 6), ("tables", 9),
):
    VEC[_name] = _at * LANES
    _at += _rows
VEC_ROWS = _at
NOTE_ROWS = 96
NBLOCK = 2 * LANES


def note_place(plan):
    row = plan.misc_start - (CORES * DEPTH * COLUMNS - 1) * plan.rows
    quarter, row = row // plan.quarter, row % plan.quarter
    first = row // 16 * 16
    assert first + NOTE_ROWS <= plan.quarter and row - first + VEC_ROWS <= NOTE_ROWS
    return quarter, first, row - first


def spread_notes(place, own, notes, sems, plan):
    quarter, first, _ = note_place(plan)
    source = own.at[quarter, first : first + NOTE_ROWS]
    home = (place.column == COLUMNS - 1) & (place.core == CORES - 1)
    root = home & (place.z == DEPTH - 1)

    def copy(src, index, peer):
        return remote(src, notes, sems.at[0, index], sems.at[1, 0], peer)

    def arrived():
        copy(notes, 0, place.peer_core).wait_recv()

    @pl.when(root)
    def _():
        notes[...] = own[quarter, first : first + NOTE_ROWS]
        for index, peer in enumerate(place.peers_z):
            copy(source, index, peer).start()

    @pl.when(home & (place.z != DEPTH - 1))
    def _():
        arrived()

    @pl.when(home)
    def _():
        for index, peer in enumerate((place.peer_x, place.peer_y, place.peer_d)):
            copy(notes, 3 + index, peer).start()

    @pl.when((place.core == CORES - 1) & (place.column != COLUMNS - 1))
    def _():
        arrived()

    @pl.when(place.core == CORES - 1)
    def _():
        copy(notes, 6, place.peer_core).start()

    @pl.when(place.core != CORES - 1)
    def _():
        arrived()

    def finish():
        @pl.when(root)
        def _():
            for index, peer in enumerate(place.peers_z):
                copy(source, index, peer).wait_send()

        @pl.when(home)
        def _():
            for index, peer in enumerate((place.peer_x, place.peer_y, place.peer_d)):
                copy(notes, 3 + index, peer).wait_send()

        @pl.when(place.core == CORES - 1)
        def _():
            copy(notes, 6, place.peer_core).wait_send()

    return finish


def turns_table():
    count_freq = D // 8
    freq = np.exp(np.arange(count_freq) * (-math.log(1000.0) / count_freq)) / (2 * math.pi)
    per = np.concatenate([freq, freq])
    phase = np.concatenate([np.zeros(count_freq), np.full(count_freq, 0.25)])
    return np.stack([np.tile(per, 4), np.tile(phase, 4)]).astype(np.float32)


def sin_turns(t):
    t = t - jnp.floor(t + 0.5)
    a = jnp.abs(t)
    m = jnp.minimum(a, 0.5 - a) * (2 * math.pi)
    u = m * m
    poly = -1.0 / 39916800.0
    for term in (1.0 / 362880.0, -1.0 / 5040.0, 1.0 / 120.0, -1.0 / 6.0, 1.0):
        poly = poly * u + term
    s = m * poly
    return jnp.where(t < 0, -s, s)


def token_columns(info):
    coords = info[0:4, :]
    doc, first = info[4:5, :], info[5:6, :]
    anchor = jnp.zeros_like(coords)
    for d in range(4):
        mine = jnp.where(doc == float(d), 1.0, 0.0)
        value = jnp.sum(coords * (mine * first), axis=1, keepdims=True)
        anchor = anchor + value * mine
    anchor = jnp.concatenate([anchor[0:2], anchor[0:2]], axis=0)
    relative = coords - anchor
    centre = jnp.floor((coords[0:2] + coords[2:4]) * 0.5)
    cell = jnp.floor(centre * (1.0 / coord_cell))
    rest = centre - cell * coord_cell
    rows = jnp.concatenate(
        [relative, cell, rest, doc, jnp.zeros((LANES - 9, WINLEN), F32)], axis=0
    )
    return rest, rows.T


def form_features(columns, turns_ref, features):
    lane = lax.broadcasted_iota(jnp.int32, (1, LANES), 1)
    for block in range(D // LANES):
        lanes = slice(block * LANES, (block + 1) * LANES)
        low, high = block * LANES // (D // 4), ((block + 1) * LANES - 1) // (D // 4)
        value = columns[:, low : low + 1]
        if high != low:
            value = jnp.where(
                lane + block * LANES < high * (D // 4), value, columns[:, high : high + 1]
            )
        t = value * turns_ref[0:1, lanes] + turns_ref[1:2, lanes]
        features[:, lanes] = sin_turns(t).astype(BF16)


def form_hots(columns, hot_ref, keyx_ref, keyy_ref, mkey, mquery):
    lane = lax.broadcasted_iota(jnp.int32, (1, LANES), 1)
    part = lane // BUCKETS
    cell = (lane % BUCKETS).astype(F32)
    is_x = jnp.where(columns[:, 4:5] == cell, 1.0, 0.0)
    is_y = jnp.where(columns[:, 5:6] == cell, 1.0, 0.0)
    hot_ref[...] = jnp.where(part % 2 == 0, is_x, is_y).astype(BF16)
    sign = jnp.where(part % 2 == 0, 1.0, -1.0)
    for odd in range(2):
        here = jnp.where(part // 2 == odd, sign, 0.0)
        keyx_ref[odd] = (is_x * here).astype(BF16)
        keyy_ref[odd] = (is_y * here).astype(BF16)
    doc = jnp.where(columns[:, 8:9] == lane.astype(F32), 1.0, 0.0)
    mkey[...] = doc.astype(BF16)
    mquery[...] = (jnp.where(lane < 4, 1.0 - doc, 0.0) * masked_score).astype(BF16)


def form_tables(tables, bands, tilted):
    row = lax.broadcasted_iota(jnp.int32, (LANES, 1), 0)
    half = BUCKETS // 2
    sub = lax.broadcasted_iota(jnp.int32, (8, LANES), 0)
    place = lax.broadcasted_iota(jnp.int32, (1, WIDE), 1)
    wanted = jnp.where(place < 5 * LANES, jnp.clip(place - 2 * LANES, -half, half - 1) + half, 0)
    lane = lax.broadcasted_iota(jnp.int32, (1, LANES), 1)
    turned = jnp.clip(64 - lane, -half, half - 1) + half
    for m in range(4):
        hot_band = jnp.where(row == wanted + m * BUCKETS, 1.0, 0.0).astype(BF16)
        got = matmul(tables, hot_band)
        for n in range(3):
            bands[4 * n + m] = got[n : n + 1, :]
        hot_turn = jnp.where(row == turned + m * BUCKETS, 1.0, 0.0).astype(BF16)
        got = matmul(tables, hot_turn)
        for t in (1, 2):
            for n in range(3):
                x = jnp.broadcast_to(got[3 * t + n : 3 * t + n + 1, :], (8, LANES))
                for bit in (1, 2, 4):
                    x = jnp.where((sub & bit) != 0, pltpu.roll(x, bit, 1), x)
                for group in range(BUCKETS // 8):
                    y = x if group == 0 else pltpu.roll(x, 8 * group, 1)
                    tilted[(t - 1) * HEADS + 4 * n + m, 8 * group : 8 * group + 8, :] = y


def pair_rows(tilted, pair):
    lane = lax.broadcasted_iota(jnp.int32, (1, LANES), 1)
    part = lane // BUCKETS
    x0, x1 = tilted[2 * pair], tilted[2 * pair + 1]
    y0, y1 = tilted[HEADS + 2 * pair], tilted[HEADS + 2 * pair + 1]

    def same(value, to):
        return value if to == 64 else pltpu.roll(value, (to - 64) % LANES, 1)

    def less(value, to):
        return pltpu.roll(value, (to - 65) % LANES, 1)

    zero = jnp.zeros_like(x0)
    base_x = jnp.where(part == 0, same(x1, 0), jnp.where(part == 2, same(x0, 64), zero))
    base_y = jnp.where(part == 1, same(y1, 32), jnp.where(part == 3, same(y0, 96), zero))

    def steps(even, odd):
        return jnp.where(
            part < 2,
            jnp.where(part == 0, less(even, 0), same(even, 32)),
            jnp.where(part == 2, less(odd, 64), same(odd, 96)),
        )

    rows = [
        jnp.concatenate([base_x, base_y], axis=0),
        jnp.concatenate([steps(x0, x1), zero], axis=0),
        jnp.concatenate([zero, steps(y0, y1)], axis=0),
    ]
    return jnp.concatenate(rows, axis=1).astype(BF16)


def gelu_and_slope(z):
    a = jnp.abs(z)
    t = 1.0 / (1.0 + (0.3275911 / math.sqrt(2.0)) * a)
    poly = 1.061405429 * 0.5
    for term in (-1.453152027, 1.421413741, -0.284496736, 0.254829592):
        poly = poly * t + 0.5 * term
    e = jnp.exp(-0.5 * z * z)
    tail = poly * t * e
    cdf = jnp.where(z < 0, tail, 1.0 - tail)
    return z * cdf, cdf + z * (e * (1.0 / math.sqrt(2.0 * math.pi)))


def forward_kernel(plan, own, hidden_in, cot_in, info, turns, *refs):
    (w_qkv_out, w_out_out, w_in_out, w_back_out, features_out, low_out, q_out, k_out, v_out, probs_out,
     context_out, hat_out, normed_out, active_out, slope_out, second_out, vec_out, rstd_out, gain_grads,
     output_ref, cot_ref, hot_out, rest_out, share_out) = refs[:24]
    refs = refs[24:]
    (flat, staged, w_qkv, w_out, w_box, w_in, w_back, notes, features, hidden, start, start_low, q_ref,
     k_ref, v_ref, hot_ref, key_x, key_y, less_x, less_y, bands, tilted, met, kaug, qaug, wide, scores,
     probs, context_t, pair_t, hat, active, slope, vec) = refs[:34]
    note_sems, swap_sems, copy_sems, probs_sems = refs[34:38]
    place = Place()
    normed_low = hidden
    context = features
    gathering = Gathering(place, flat, dict(zip(GATHER_SEMS, refs[38:])))
    matrices = (w_qkv, w_out, w_box, w_in, w_back)
    written = []

    def write_out(src, dst):
        copy = pltpu.make_async_copy(src, dst, copy_sems.at[len(written)])
        copy.start()
        written.append(copy)

    place.greet()
    finish_notes = None
    gathering.spread(own)

    quarter = WINLEN // DEPTH

    def exchange(source, target, kind):
        rows = pl.ds(pl.multiple_of(place.z * quarter, quarter), quarter)
        for d in range(DEPTH - 1):
            gathering_send(source.at[place.far[d]], target.at[rows], kind, d, place.peers_z[d])

    def gathering_send(src, dst, kind, d, peer):
        copy = remote(src, dst, swap_sems.at[kind, 0, d], swap_sems.at[kind, 1, d], peer)
        copy.start()
        gathering.sent.append(copy)

    def exchanged(target, kind):
        for d in range(DEPTH - 1):
            rows = pl.ds(pl.multiple_of(place.from_far[d] * quarter, quarter), quarter)
            remote(
                target.at[rows], target.at[rows], swap_sems.at[kind, 0, d], swap_sems.at[kind, 1, d],
                place.peer_x,
            ).wait_recv()

    exchange(hidden_in, hidden, 0)
    finish_notes = spread_notes(place, own, notes, note_sems, plan)
    own_rows = pl.ds(pl.multiple_of(place.z * quarter, quarter), quarter)
    own_hidden = pltpu.make_async_copy(
        hidden_in.at[place.z], hidden.at[own_rows], swap_sems.at[0, 0, DEPTH - 1]
    )
    own_hidden.start()
    own_cot = pltpu.make_async_copy(
        cot_in.at[place.z], cot_ref.at[own_rows], swap_sems.at[1, 0, DEPTH - 1]
    )
    own_cot.start()
    gathering.spread_done()
    gathering.along_z(0)
    gathering.along_z(1)

    rest, columns = token_columns(info[...])
    for part in range(BLOCKS):
        rows = slice(part * LANES, (part + 1) * LANES)
        for axis, less in ((0, less_x), (1, less_y)):
            less[rows, :] = jnp.where(
                rest[axis : axis + 1, :] < columns[rows, 6 + axis : 7 + axis], 1.0, 0.0
            ).astype(BF16)
    rest_out[...] = rest
    form_hots(columns, hot_ref, key_x, key_y, kaug.at[:, LANES:], qaug.at[:, LANES:])
    hot_out[...] = hot_ref[...]
    form_features(columns, turns, features)
    for n in range(D // LANES):
        rows = slice(n * LANES, (n + 1) * LANES)
        context_t[rows, :] = features[:, rows].T
    write_out(context_t, features_out)
    _, _, note_row = note_place(plan)
    for row in range(VEC_ROWS):
        at = note_row + row
        vec[0:1, row * LANES : (row + 1) * LANES] = notes[at // 16 * 16 : at // 16 * 16 + 16, :].astype(
            F32
        )[at % 16 : at % 16 + 1, :]
    vec_out[...] = vec[...]
    table_row = note_row + VEC["tables"] // LANES
    assert table_row % 16 == 0
    form_tables(notes[table_row : table_row + 16, :], bands, tilted)

    gathering.first(0)
    gathering.along_z(2)
    gathering.first(1)
    gathering.along_z(3)
    exchange(cot_in, cot_ref, 1)
    gathering.second(0)
    gathering.second(1)
    gathering.first(2)
    gathering.third(0)
    gathering.complete(0)
    stage_column(plan, flat, staged, 0)
    form_matrices(plan, staged, matrices, 0)
    keep_carry(plan, staged)
    gathering.third(1)
    gathering.first(3)
    gathering.complete(1)
    stage_column(plan, flat, staged, 1)
    form_matrices(plan, staged, matrices, 1)
    keep_carry(plan, staged)
    write_out(w_qkv, w_qkv_out)
    write_out(w_out, w_out_out)

    exchanged(hidden, 0)
    own_hidden.wait()
    for n in range(D // NBLOCK):
        lanes = slice(n * NBLOCK, (n + 1) * NBLOCK)
        value = hidden[:, lanes].astype(F32) + matmul(features[...], w_box[:, lanes])
        start[:, lanes] = value
        start_low[:, lanes] = value.astype(BF16)
    write_out(start_low, low_out)
    written[0].wait()

    def project(n, carry):
        at = pl.multiple_of(n * NBLOCK, NBLOCK)
        lanes = pl.ds(at, NBLOCK)
        low = start_low[...]
        bias = vec[0:1, pl.ds(pl.multiple_of(VEC["q_bias"] + at, LANES), NBLOCK)]
        got = matmul(low, w_qkv[:, lanes]) + bias
        q_ref[:, lanes] = (got.astype(BF16).astype(F32) * HEAD_DIM ** (-0.5)).astype(BF16)
        k_ref[:, lanes] = matmul(low, w_qkv[:, pl.ds(pl.multiple_of(at + D, LANES), NBLOCK)]).astype(BF16)
        bias = vec[0:1, pl.ds(pl.multiple_of(VEC["v_bias"] + at, LANES), NBLOCK)]
        got = matmul(low, w_qkv[:, pl.ds(pl.multiple_of(at + 2 * D, LANES), NBLOCK)]) + bias
        v_ref[:, lanes] = got.astype(BF16)
        return carry

    lax.fori_loop(0, D // NBLOCK, project, 0)
    write_out(q_ref, q_out)
    write_out(k_ref, k_out)
    write_out(v_ref, v_out)
    gathering.second(2)

    low, high = half_masks()
    half = 2 * LANES

    def probs_copy(head, odd):
        return pltpu.make_async_copy(probs.at[odd], probs_out.at[head], probs_sems.at[odd])

    def one_pair(pair, carry):
        at = pl.multiple_of(pair * LANES, LANES)
        lanes = pl.ds(at, LANES)
        values_t = v_ref[:, lanes].T
        met[...] = matmul(hot_ref[:, :64], pair_rows(tilted, pair)).astype(BF16)
        for odd in range(2):
            mine, other = (low, high) if odd == 0 else (high, low)
            head = 2 * pair + odd
            kaug[:, :LANES] = k_ref[:, lanes] * mine + hot_ref[...] * other
            qaug[:, :LANES] = q_ref[:, lanes] * mine + met[:, :LANES] * other
            skew_band(bands[head], wide)

            @pl.when(pair > 0)
            def _():
                probs_copy(head, odd).wait()

            for side in range(2):
                cols = slice(side * half, (side + 1) * half)
                whole = times_transposed(kaug[...], qaug[cols, :])
                steps_x = times_transposed(key_x[odd], met[cols, LANES : 2 * LANES])
                steps_y = times_transposed(key_y[odd], met[cols, 2 * LANES :])
                top = None
                for part in range(BLOCKS):
                    rows = slice(part * LANES, (part + 1) * LANES)
                    bias = []
                    for block in range(2 * side, 2 * side + 2):
                        step = max(-2, min(2, block - part)) + 2
                        bias.append(wide[:, step * LANES : (step + 1) * LANES])
                    s = whole[rows] + jnp.concatenate(bias, axis=1)
                    s = s + steps_x[rows] * less_x[rows, cols].astype(F32)
                    s = s + steps_y[rows] * less_y[rows, cols].astype(F32)
                    scores[rows, :] = s
                    best = jnp.max(s, axis=0, keepdims=True)
                    top = best if top is None else jnp.maximum(top, best)
                total = None
                for part in range(BLOCKS):
                    rows = slice(part * LANES, (part + 1) * LANES)
                    e = jnp.exp(scores[rows, :] - top)
                    probs[odd, rows, cols] = e.astype(BF16)
                    add = jnp.sum(e, axis=0, keepdims=True)
                    total = add if total is None else total + add
                share = 1.0 / total
                share_out[head, :, cols] = share
                got = matmul(values_t[odd * HEAD_DIM : (odd + 1) * HEAD_DIM, :], probs[odd, :, cols])
                pair_t[odd * HEAD_DIM : (odd + 1) * HEAD_DIM, cols] = got * share
            probs_copy(head, odd).start()
        both = pair_t[...]
        context_t[lanes, :] = both.astype(BF16)
        context[:, lanes] = both.T.astype(BF16)
        return carry

    lax.fori_loop(0, 2, one_pair, 0)
    gathering.third(2)
    gathering.second(3)
    lax.fori_loop(2, 4, one_pair, 0)
    gathering.third(3)
    gathering.complete(2)
    stage_column(plan, flat, staged, 2)
    form_matrices(plan, staged, matrices, 2)
    keep_carry(plan, staged)
    write_out(w_in, w_in_out)
    lax.fori_loop(4, PAIRS, one_pair, 0)
    write_out(context_t, context_out)
    gathering.complete(3)
    stage_column(plan, flat, staged, 3)
    form_matrices(plan, staged, matrices, 3)
    write_out(w_back, w_back_out)

    def vector(name):
        return vec[0:1, VEC[name] : VEC[name] + D]

    for n in range(D // NBLOCK):
        lanes = slice(n * NBLOCK, (n + 1) * NBLOCK)
        bias = vec[0:1, VEC["out_bias"] + n * NBLOCK : VEC["out_bias"] + (n + 1) * NBLOCK]
        start[:, lanes] = start[:, lanes] + matmul(context[...], w_out[:, lanes]) + bias

    step_rows = 64

    def norm_first(n, carry):
        rows = pl.ds(pl.multiple_of(n * step_rows, step_rows), step_rows)
        x = start[rows, :]
        centred = x - jnp.mean(x, axis=1, keepdims=True)
        rstd = lax.rsqrt(jnp.mean(centred * centred, axis=1, keepdims=True) + norm_eps)
        xhat = centred * rstd
        hat[rows, :] = xhat
        rstd_out[rows, :] = jnp.broadcast_to(rstd, (step_rows, LANES))
        normed = xhat * vector("gain_one") + vector("shift_one")
        start[rows, :] = normed
        normed_low[rows, :] = normed.astype(BF16)
        return carry

    lax.fori_loop(0, WINLEN // step_rows, norm_first, 0)
    write_out(hat, hat_out)
    write_out(normed_low, normed_out)

    def widen(n, carry):
        at = pl.multiple_of(n * NBLOCK, NBLOCK)
        lanes = pl.ds(at, NBLOCK)
        bias = vec[0:1, pl.ds(pl.multiple_of(VEC["in_bias"] + at, LANES), NBLOCK)]
        value, change = gelu_and_slope(matmul(normed_low[...], w_in[:, lanes]) + bias)
        active[:, lanes] = value.astype(BF16)
        slope[:, lanes] = change.astype(BF16)
        return carry

    lax.fori_loop(0, FF // NBLOCK, widen, 0)
    write_out(active, active_out)
    write_out(slope, slope_out)
    for n in range(D // NBLOCK):
        lanes = slice(n * NBLOCK, (n + 1) * NBLOCK)
        bias = vec[0:1, VEC["back_bias"] + n * NBLOCK : VEC["back_bias"] + (n + 1) * NBLOCK]
        start[:, lanes] = start[:, lanes] + matmul(active[...], w_back[:, lanes]) + bias

    exchanged(cot_ref, 1)
    own_cot.wait()
    gain_grads[...] = jnp.zeros_like(gain_grads)

    def norm_second(n, carry):
        rows = pl.ds(pl.multiple_of(n * step_rows, step_rows), step_rows)
        x = start[rows, :]
        centred = x - jnp.mean(x, axis=1, keepdims=True)
        rstd = lax.rsqrt(jnp.mean(centred * centred, axis=1, keepdims=True) + norm_eps)
        xhat = centred * rstd
        output_ref[rows, :] = (xhat * vector("gain_two") + vector("shift_two")).astype(BF16)
        cot = cot_ref[rows, :].astype(F32)
        prod = cot * xhat
        gain_grads[0:1, :] = gain_grads[0:1, :] + jnp.sum(prod, axis=0, keepdims=True)
        gain_grads[1:2, :] = gain_grads[1:2, :] + jnp.sum(cot, axis=0, keepdims=True)
        gain = vector("gain_two")
        gc = cot * gain
        mean_one = jnp.mean(gc, axis=1, keepdims=True)
        mean_two = jnp.mean(prod * gain, axis=1, keepdims=True)
        second_out[rows, :] = rstd * (gc - mean_one - xhat * mean_two)
        return carry

    lax.fori_loop(0, WINLEN // step_rows, norm_second, 0)
    for odd in range(2):
        probs_copy(0, odd).wait()
    for copy in written[1:]:
        copy.wait()
    finish_notes()
    gathering.finish()


def forward_pass(plan, own, hidden_in, cotangent, info):
    anywhere = pl.BlockSpec(memory_space=pl.ANY)
    vmem = pl.BlockSpec(memory_space=pltpu.VMEM)
    token = (WINLEN, D)

    def hbm(shape, dtype=BF16):
        return jax.ShapeDtypeStruct(shape, dtype), anywhere

    def near(shape, dtype=F32):
        return jax.ShapeDtypeStruct(shape, dtype), vmem

    outs = [
        hbm(MATRICES[0]), hbm(MATRICES[1]), hbm(MATRICES[3]), hbm(MATRICES[4]), hbm((D, WINLEN)), hbm(token),
        hbm(token), hbm(token), hbm(token), hbm((HEADS, WINLEN, WINLEN)), hbm((D, WINLEN)),
        hbm(token, F32), hbm(token), hbm((WINLEN, FF)), hbm((WINLEN, FF)), near(token),
        near((1, VEC_ROWS * LANES)), near((WINLEN, LANES)), near((2, D)), near(token, BF16),
        near(token, BF16), near((WINLEN, LANES), BF16), near((2, WINLEN)),
        near((HEADS, 1, WINLEN)),
    ]
    scratch = [
        pltpu.VMEM((COLUMNS, CORES, DEPTH, COLUMNS, plan.quarter, LANES), BF16),
        pltpu.VMEM((plan.staged, LANES), F32),
    ]
    scratch += [pltpu.VMEM(layout, BF16) for layout in MATRICES]
    scratch += [
        pltpu.VMEM((NOTE_ROWS, LANES), BF16),
        pltpu.VMEM(token, BF16),
        pltpu.VMEM(token, BF16),
        pltpu.VMEM(token, F32),
        pltpu.VMEM(token, BF16),
        pltpu.VMEM(token, BF16),
        pltpu.VMEM(token, BF16),
        pltpu.VMEM(token, BF16),
        pltpu.VMEM((WINLEN, LANES), BF16),
        pltpu.VMEM((2, WINLEN, LANES), BF16),
        pltpu.VMEM((2, WINLEN, LANES), BF16),
        pltpu.VMEM((WINLEN, WINLEN), BF16),
        pltpu.VMEM((WINLEN, WINLEN), BF16),
        pltpu.VMEM((HEADS, 1, WIDE), F32),
        pltpu.VMEM((2 * HEADS, BUCKETS, LANES), F32),
        pltpu.VMEM((WINLEN, 3 * LANES), BF16),
        pltpu.VMEM((WINLEN, 2 * LANES), BF16),
        pltpu.VMEM((WINLEN, 2 * LANES), BF16),
        pltpu.VMEM((LANES, 5 * LANES), F32),
        pltpu.VMEM((WINLEN, 2 * LANES), F32),
        pltpu.VMEM((2, WINLEN, WINLEN), BF16),
        pltpu.VMEM((D, WINLEN), BF16),
        pltpu.VMEM((LANES, WINLEN), F32),
        pltpu.VMEM(token, F32),
        pltpu.VMEM((WINLEN, FF), BF16),
        pltpu.VMEM((WINLEN, FF), BF16),
        pltpu.VMEM((1, VEC_ROWS * LANES), F32),
        pltpu.SemaphoreType.DMA((2, 7)),
        pltpu.SemaphoreType.DMA((2, 2, DEPTH)),
        pltpu.SemaphoreType.DMA((16,)),
        pltpu.SemaphoreType.DMA((2,)),
    ]
    return pl.pallas_call(
        functools.partial(forward_kernel, plan),
        out_shape=[shape for shape, _ in outs],
        in_specs=[vmem, anywhere, anywhere, vmem, vmem],
        out_specs=[spec for _, spec in outs],
        scratch_shapes=scratch + sem_shapes(GATHER_SEMS),
        compiler_params=pltpu.CompilerParams(
            collective_id=0, has_side_effects=True, vmem_limit_bytes=62 * 2**20
        ),
        name="forward_pass",
    )(own, hidden_in, cotangent, info, jnp.asarray(turns_table()))


class Reducing:
    def __init__(self, place, flat, swapped, one, two, deep, piece, result, sems, free):
        self.place = place
        self.flat = flat
        self.swapped = swapped
        self.one = one
        self.two = two
        self.deep = deep
        self.piece = piece
        self.result = result
        self.sems = sems
        self.free = free
        self.sent = {k: [] for k in range(COLUMNS)}

    def send(self, k, src, dst, kind, index, peer):
        copy = remote(src, dst, self.sems[kind].at[0, index], self.sems[kind].at[1, index], peer)
        copy.start()
        self.sent[k].append(copy)

    got = Gathering.got

    def settle(self, k):
        for copy in self.sent.pop(k):
            copy.wait_send()

    def swap(self, k):
        p = self.place
        slot = k % 2
        if k < 2:
            pl.semaphore_wait(self.free.at[slot], 1)
        self.send(k, self.flat.at[slot, 1 - p.core], self.swapped.at[slot], "core", k, p.peer_core)

    def first(self, k):
        p = self.place
        slot = k % 2
        self.got(self.swapped.at[slot], "core", k)

        def one(step, carry):
            z, quarter = step // COLUMNS, step % COLUMNS
            total = self.flat[slot, p.core, z, quarter].astype(F32)
            total = total + self.swapped[slot, z, quarter].astype(F32)
            self.flat[slot, p.core, z, quarter] = total.astype(BF16)
            return carry

        lax.fori_loop(0, DEPTH * COLUMNS, one, 0)
        flat = self.flat
        self.send(k, flat.at[slot, p.core, 0:2, p.col_d], self.one.at[k, 0], "one", 2 * k, p.peer_y)
        self.send(k, flat.at[slot, p.core, 2:4, p.col_d], self.one.at[k, 1], "one", 2 * k + 1, p.peer_x)
        if k >= 2:
            pl.semaphore_signal(
                self.free.at[slot], inc=1, device_id=p.peer_core, device_id_type=MESH
            )

    def second(self, k):
        p = self.place
        slot = k % 2
        for side, column in ((0, p.col_x), (1, p.col_y)):
            self.got(self.one.at[k, side], "one", 2 * k + side)

            def one(step, carry, side=side, column=column):
                z = 2 * side + step
                total = self.flat[slot, p.core, z, column].astype(F32)
                total = total + self.one[k, side, step].astype(F32)
                self.flat[slot, p.core, z, column] = total.astype(BF16)
                return carry

            lax.fori_loop(0, 2, one, 0)
        flat = self.flat
        self.send(k, flat.at[slot, p.core, :, p.col_x], self.two.at[k, 0], "two", 2 * k, p.peer_x)
        self.send(k, flat.at[slot, p.core, :, p.col_y], self.two.at[k, 1], "two", 2 * k + 1, p.peer_y)

    def third(self, k):
        p = self.place
        slot = k % 2
        for side in range(2):
            self.got(self.two.at[k, side], "two", 2 * k + side)

        def one(z, carry):
            total = self.flat[slot, p.core, z, p.column].astype(F32)
            total = total + self.two[k, 0, z].astype(F32) + self.two[k, 1, z].astype(F32)
            self.flat[slot, p.core, z, p.column] = total.astype(BF16)
            return carry

        lax.fori_loop(0, DEPTH, one, 0)
        for d in range(DEPTH - 1):
            self.send(
                k, self.flat.at[slot, p.core, p.far[d], p.column], self.deep.at[k, d], "z", 3 * k + d,
                p.peers_z[d],
            )

    def fourth(self, k):
        p = self.place
        for d in range(DEPTH - 1):
            self.got(self.deep.at[k, d], "z", 3 * k + d)
        total = self.flat[k % 2, p.core, p.z, p.column].astype(F32)
        for d in range(DEPTH - 1):
            total = total + self.deep[k, d].astype(F32)
        self.piece[k] = total.astype(BF16)

    def giving(self, k):
        p = self.place
        sems = self.sems["spread"]
        return remote(
            self.piece.at[k], self.result.at[p.column], sems.at[0, k], sems.at[1, p.column],
            p.at(k, p.core, p.z),
        )

    def give(self, k):
        @pl.when(self.place.column != k)
        def _():
            self.giving(k).start()

    def given(self, k):
        @pl.when(self.place.column != k)
        def _():
            self.giving(k).wait_send()

    def receive(self, out):
        p = self.place
        out[p.column] = self.piece[p.column].astype(F32)
        for column in (p.col_x, p.col_y, p.col_d):
            self.got(self.result.at[column], "spread", column)
            out[column] = self.result[column].astype(F32)


REDUCE_SEMS = {"spread": 4, "z": 12, "one": 8, "two": 8, "core": 4}


def unstage_column(plan, flat, staged, k):
    def one(step, carry):
        shard, quarter = step // COLUMNS, step % COLUMNS
        base = plan.carry + shard * plan.rows + quarter * plan.quarter
        piece = staged[pl.ds(pl.multiple_of(base, 8), plan.quarter), :]
        flat[k % 2, shard // DEPTH, shard % DEPTH, quarter] = piece.astype(BF16)
        return carry

    lax.fori_loop(0, CORES * DEPTH * COLUMNS, one, 0)


class Notes:
    def __init__(self, place, notes, slots, sems):
        self.place, self.notes, self.slots, self.sems = place, notes, slots, sems
        p = place
        self.home = (p.column == COLUMNS - 1) & (p.core == CORES - 1)
        self.root = self.home & (p.z == DEPTH - 1)

    def copy(self, slot, peer):
        return remote(
            self.notes, self.slots.at[slot], self.sems.at[0, 0], self.sems.at[1, slot], peer
        )

    def take(self, slot):
        self.copy(slot, self.place.peer_core).wait_recv()
        self.notes[...] = self.notes[...] + self.slots[slot]

    def start(self):
        p = self.place

        @pl.when(p.core != CORES - 1)
        def _():
            self.copy(0, p.peer_core).start()

    def rise(self):
        p = self.place

        @pl.when(p.core == CORES - 1)
        def _():
            self.take(0)

        @pl.when((p.core == CORES - 1) & (p.column != COLUMNS - 1))
        def _():
            self.copy(1 + p.column, p.at(COLUMNS - 1, p.core, p.z)).start()

    def end(self):
        p = self.place

        @pl.when(self.home)
        def _():
            for slot in range(1, 4):
                self.take(slot)

        @pl.when(self.home & (p.z != DEPTH - 1))
        def _():
            self.copy(4 + p.z, p.at(p.column, p.core, DEPTH - 1)).start()

        @pl.when(self.root)
        def _():
            for slot in range(4, 7):
                self.take(slot)

        @pl.when(jnp.logical_not(self.root))
        def _():
            self.copy(0, p.peer_core).wait_send()


def cell_sums(whole, less, odd):
    lane = lax.broadcasted_iota(jnp.int32, (1, LANES), 1)
    sub = lax.broadcasted_iota(jnp.int32, (8, LANES), 0)
    sums = []
    for axis in range(2):
        rows = slice(axis * BUCKETS, (axis + 1) * BUCKETS)
        start = axis * BUCKETS + (0 if odd else 64)
        every = pltpu.roll(whole[rows], (BUCKETS - start) % LANES, 1)
        below = pltpu.roll(less[rows], (BUCKETS - axis * BUCKETS) % LANES, 1)
        inside = (lane >= BUCKETS) & (lane < 2 * BUCKETS)
        every = jnp.where(inside, every, 0.0)
        below = jnp.where(inside, below, 0.0)
        x = every - below + pltpu.roll(below, LANES - 1, 1)
        total = None
        for group in range(BUCKETS // 8):
            y = x[8 * group : 8 * group + 8]
            y = y if group == 0 else pltpu.roll(y, LANES - 8 * group, 1)
            total = y if total is None else total + y
        for bit in (1, 2, 4):
            total = jnp.where((sub & bit) != 0, pltpu.roll(total, LANES - bit, 1), total)
        sums.append(jnp.sum(total, axis=0, keepdims=True))
    return sums


def exact_dot(a, b):
    return jnp.dot(a, b, preferred_element_type=F32, precision=lax.Precision.HIGHEST)


def bucket_rows(cell_ref, diag_ref):
    half = BUCKETS // 2
    column = lax.broadcasted_iota(jnp.int32, (1, LANES), 1)
    row = lax.broadcasted_iota(jnp.int32, (LANES, 1), 0)
    to = jnp.clip(row - BUCKETS, -half, half - 1) + half
    place = lax.broadcasted_iota(jnp.int32, (WIDE, 1), 0)
    along = place - LANES
    far = jnp.where(place < LANES, 0, jnp.where(place < 5 * LANES, 0, BUCKETS - 1))
    along = jnp.where(
        (place >= LANES) & (place < 4 * LANES),
        jnp.clip(along - LANES, -half, half - 1) + half,
        far,
    )
    first, rest = None, None
    zero = jnp.zeros((5, WIDE), F32)
    for m in range(4):
        hot_along = jnp.where(along + m * BUCKETS == column, 1.0, 0.0)
        got = exact_dot(
            jnp.concatenate([diag_ref[4 * n + m] for n in range(3)] + [zero], axis=0), hot_along
        )
        first = got if first is None else first + got
        hot_cell = jnp.where(to + m * BUCKETS == column, 1.0, 0.0)
        rows = [cell_ref[t * HEADS + 4 * n + m] for t in range(2) for n in range(3)]
        got = exact_dot(jnp.concatenate(rows + [zero[:2, :LANES]], axis=0), hot_cell)
        rest = got if rest is None else rest + got
    return jnp.concatenate([first[:3], rest[:6]], axis=0)


def backward_kernel(
    plan, active_in, slope_in, w_back_in, w_in_in, w_out_in, w_qkv_in, normed_in, low_in, features_in,
    context_in, q_in, k_in, v_in, probs_in, hat_in, second_in, rstd_ref, vec, gain_two, hot_ref, rest_ref,
    share_ref, output_in, *refs,
):
    out, output_pos, hidden_pos = refs[:3]
    (flat, staged, swapped, one_buf, two_buf, deep, piece, result, active, slope, w_back, w_in, w_out,
     turned, low_t, features_t, context_t, q_ref, k_ref, v_ref, hat, second, branch, dctx, probs, less_x,
     less_y, dscores, dscores_x, dscores_y, band, hot_t, qaug, pair_t, scaled, share_cols, vecg, cell_rows, diag_rows, notes, slots,
     ) = refs[3:44]
    load_sems, probs_sems, free, pos_sems, note_sems = refs[44:49]
    place = Place()
    reducing = Reducing(
        place, flat, swapped, one_buf, two_buf, deep, piece, result,
        dict(zip(REDUCE_SEMS, refs[49:])), free,
    )
    climbing = Notes(place, notes, slots, note_sems)
    loads = {}

    def load(name, src, dst):
        loads[name] = pltpu.make_async_copy(src, dst, load_sems.at[len(loads)])
        loads[name].start()

    mixed = active.at[:, : 3 * D]
    grad_attn = branch
    w_qkv = w_in.at[:, : 3 * D]
    hidden_low = dctx
    scores = hat.at[:, :WINLEN]

    load("second", second_in, second)
    load("active", active_in, active)

    at = staged_at(plan, COLUMNS - 1, plan.misc_start)
    staged[at:, :] = jnp.zeros((plan.staged - at, LANES), F32)
    place.greet()

    quarter = WINLEN // DEPTH
    positions = []

    def to_pos(source, target, kind):
        for d in range(DEPTH - 1):
            rows = pl.ds(pl.multiple_of(place.far[d] * quarter, quarter), quarter)
            copy = remote(
                source.at[rows], target.at[place.z], pos_sems.at[kind, 0, d], pos_sems.at[kind, 1, d],
                place.peers_z[d],
            )
            copy.start()
            positions.append(copy)
        rows = pl.ds(pl.multiple_of(place.z * quarter, quarter), quarter)
        copy = pltpu.make_async_copy(
            source.at[rows], target.at[place.z], pos_sems.at[kind, 0, DEPTH - 1]
        )
        copy.start()
        return copy

    def in_pos(target, kind):
        for d in range(DEPTH - 1):
            there = target.at[place.from_far[d]]
            remote(
                there, there, pos_sems.at[kind, 0, d], pos_sems.at[kind, 1, d], place.peer_x
            ).wait_recv()

    own_output = to_pos(output_in, output_pos, 0)

    def store(k, index, row, value, first_block=0):
        blocks = MATRICES[index][1] // LANES
        base = staged_at(plan, k, plan.starts[index]) + row * blocks + first_block
        for block in range(value.shape[1] // LANES):
            staged[pl.ds(base + block, value.shape[0], stride=blocks), :] = value[
                :, block * LANES : (block + 1) * LANES
            ]

    def column_sum(value):
        return jnp.sum(value, axis=0, keepdims=True)

    def keep_vector(name, lanes_at, value):
        at = pl.multiple_of(VEC[name] + lanes_at, LANES)
        vecg[0:1, pl.ds(at, value.shape[1])] = value

    loads["second"].wait()
    for n in range(D // NBLOCK):
        lanes = slice(n * NBLOCK, (n + 1) * NBLOCK)
        value = second[:, lanes].astype(BF16)
        branch[:, lanes] = value
        keep_vector("back_bias", n * NBLOCK, column_sum(value.astype(F32)))
    loads["active"].wait()
    load("slope", slope_in, slope)
    load("w_back", w_back_in, w_back)
    load("normed", normed_in, dctx)

    def back_rows(k, size, begin, count):
        def body(n, carry):
            row = pl.multiple_of(begin + n * size, LANES)
            turned[:size, :] = active[:, pl.ds(row, size)].T
            store(k, 4, row, matmul(turned[:size, :], branch[...]))
            return carry

        lax.fori_loop(0, count, body, 0)

    back_rows(3, WINLEN, 512, FF // WINLEN - 1)
    unstage_column(plan, flat, staged, 3)
    reducing.swap(3)

    back_rows(2, WINLEN, 0, 1)
    back_rows(2, LANES, 512, 1)
    loads["w_back"].wait()
    loads["slope"].wait()
    load("w_in", w_in_in, w_in)
    load("hat", hat_in, hat)
    load("w_out", w_out_in, w_out)

    def inner(n, carry):
        at = pl.multiple_of(n * NBLOCK, NBLOCK)
        lanes = pl.ds(at, NBLOCK)
        value = times_transposed(branch[...], w_back[lanes, :]) * slope[:, lanes].astype(F32)
        value = value.astype(BF16)
        slope[:, lanes] = value
        keep_vector("in_bias", at, column_sum(value.astype(F32)))
        return carry

    lax.fori_loop(0, FF // NBLOCK, inner, 0)
    grad_inner = slope
    reducing.first(3)

    loads["normed"].wait()
    for n in range(D // NBLOCK):
        rows = slice(n * NBLOCK, (n + 1) * NBLOCK)
        turned[rows, :] = dctx[:, rows].T

    def in_rows(k, begin, end):
        def body(n, carry):
            lanes = pl.ds(pl.multiple_of(n * NBLOCK, NBLOCK), NBLOCK)
            got = matmul(turned[begin:end, :], grad_inner[:, lanes])
            store(k, 3, begin, got, n * (NBLOCK // LANES))
            return carry

        lax.fori_loop(0, FF // NBLOCK, body, 0)

    in_rows(2, 288, D)
    unstage_column(plan, flat, staged, 2)
    reducing.swap(2)
    reducing.second(3)

    loads["w_in"].wait()
    load("context", context_in, context_t)
    load("q", q_in, q_ref)
    load("k", k_in, k_ref)
    load("v", v_in, v_ref)
    for odd in range(2):
        pltpu.make_async_copy(probs_in.at[odd], probs.at[odd], probs_sems.at[odd]).start()
    for n in range(D // NBLOCK):
        lanes = slice(n * NBLOCK, (n + 1) * NBLOCK)
        second[:, lanes] = second[:, lanes] + times_transposed(grad_inner[...], w_in[lanes, :])
    load("w_qkv", w_qkv_in, w_qkv)
    load("features", features_in, features_t)
    load("low", low_in, low_t)
    reducing.first(2)

    loads["hat"].wait()
    step_rows = 64
    for name in ("gain_one", "shift_one", "out_bias"):
        keep_vector(name, 0, jnp.zeros((1, D), F32))

    def norm_first(n, carry):
        rows = pl.ds(pl.multiple_of(n * step_rows, step_rows), step_rows)
        grad = second[rows, :]
        xhat = hat[rows, :]
        prod = grad * xhat
        gain = vec[0:1, VEC["gain_one"] : VEC["gain_one"] + D]
        gc = grad * gain
        mean_one = jnp.mean(gc, axis=1, keepdims=True)
        mean_two = jnp.mean(prod * gain, axis=1, keepdims=True)
        value = rstd_ref[rows, 0:1] * (gc - mean_one - xhat * mean_two)
        second[rows, :] = value
        value = value.astype(BF16)
        grad_attn[rows, :] = value
        for name, term in (
            ("gain_one", prod), ("shift_one", grad), ("out_bias", value.astype(F32)),
        ):
            lanes = slice(VEC[name], VEC[name] + D)
            vecg[0:1, lanes] = vecg[0:1, lanes] + column_sum(term)
        return carry

    lax.fori_loop(0, WINLEN // step_rows, norm_first, 0)
    reducing.third(3)
    loads["w_out"].wait()
    for n in range(D // NBLOCK):
        lanes = slice(n * NBLOCK, (n + 1) * NBLOCK)
        dctx[:, lanes] = times_transposed(grad_attn[...], w_out[lanes, :]).astype(BF16)
    loads["context"].wait()
    in_rows(1, 0, 304)
    reducing.second(2)

    def out_rows(k, begin, end):
        for n in range(D // NBLOCK):
            lanes = slice(n * NBLOCK, (n + 1) * NBLOCK)
            got = matmul(context_t[begin:end, :], grad_attn[:, lanes])
            store(k, 1, begin, got, n * (NBLOCK // LANES))

    out_rows(1, 192, D)
    reducing.fourth(3)
    reducing.give(3)

    low, high = half_masks()
    rest = rest_ref[...]
    columns = jnp.concatenate([rest, jnp.zeros((LANES - 2, WINLEN), F32)], axis=0).T
    for part in range(BLOCKS):
        rows = slice(part * LANES, (part + 1) * LANES)
        for axis, less in ((0, less_x), (1, less_y)):
            less[rows, :] = jnp.where(
                rest[axis : axis + 1, :] < columns[rows, axis : axis + 1], 1.0, 0.0
            ).astype(BF16)
    hot_t[...] = hot_ref[...].T
    lane = lax.broadcasted_iota(jnp.int32, (1, LANES), 1)
    scale = HEAD_DIM ** (-0.5)
    of_x = jnp.where((lane // BUCKETS) % 2 == 0, 1.0, 0.0)
    share_cols[...] = jnp.concatenate(
        [share_ref[head] for head in range(HEADS)] + [jnp.zeros((LANES - HEADS, WINLEN), F32)], axis=0
    ).T
    for name in ("q", "k", "v"):
        loads[name].wait()

    def probs_copy(head, odd):
        return pltpu.make_async_copy(probs_in.at[head], probs.at[odd], probs_sems.at[odd])

    def one_pair(pair, carry):
        at = pl.multiple_of(pair * LANES, LANES)
        lanes = pl.ds(at, LANES)
        keys_t = k_ref[:, lanes].T
        cells_x = hot_ref[...] * of_x.astype(BF16)
        cells_y = hot_ref[...] * (1.0 - of_x).astype(BF16)
        both = pltpu.roll(share_cols[...], lax.rem(LANES - 2 * pair, LANES), 1)
        both = jnp.where(lane < HEAD_DIM, both[:, 0:1], both[:, 1:2])
        scaled[...] = (dctx[:, lanes].astype(F32) * both).astype(BF16)
        for odd in range(2):
            mine, other = (low, high) if odd == 0 else (high, low)
            head = 2 * pair + odd
            probs_copy(head, odd).wait()
            qaug[...] = q_ref[:, lanes] * mine + hot_ref[...] * other
            grad_context = dctx[:, lanes]
            share = share_ref[head]
            products = times_transposed(v_ref[:, lanes] * mine, grad_context)
            dot = None
            for part in range(BLOCKS):
                rows = slice(part * LANES, (part + 1) * LANES)
                dp = products[rows]
                scores[rows, :] = dp
                add = column_sum(dp * probs[odd, rows, :].astype(F32))
                dot = add if dot is None else dot + add
            dot = dot * share
            band[...] = jnp.zeros_like(band)
            for part in range(BLOCKS):
                rows = slice(part * LANES, (part + 1) * LANES)
                ds = probs[odd, rows, :].astype(F32) * ((scores[rows, :] - dot) * share)
                for block in range(BLOCKS):
                    step = max(-2, min(2, block - part)) + 2
                    where = slice(step * LANES, (step + 1) * LANES)
                    band[:, where] = band[:, where] + ds[:, block * LANES : (block + 1) * LANES]
                ds = ds.astype(BF16)
                dscores[rows, :] = ds
                dscores_x[rows, :] = ds * less_x[rows, :]
                dscores_y[rows, :] = ds * less_y[rows, :]
            keys_cells = matmul(dscores[...], qaug[...])
            less = matmul(dscores_x[...], cells_x) + matmul(dscores_y[...], cells_y)
            values_grad = matmul(probs[odd], scaled[...])

            @pl.when(pair < PAIRS - 1)
            def _():
                probs_copy(head + 2, odd).start()

            pair_t[odd * HEAD_DIM : (odd + 1) * HEAD_DIM, :] = matmul(
                keys_t[odd * HEAD_DIM : (odd + 1) * HEAD_DIM, :], dscores[...]
            )
            diag_rows[head, :, LANES : 5 * LANES] = diagonal_sums(band)
            diag_rows[head, :, :LANES] = column_sum(band[:, :LANES])
            diag_rows[head, :, 5 * LANES :] = column_sum(band[:, 4 * LANES :])
            sums = []
            for summed in (keys_cells, less):
                first = summed.astype(BF16)
                remainder = (summed - first.astype(F32)).astype(BF16)
                sums.append(matmul(hot_t[:64, :], first) + matmul(hot_t[:64, :], remainder))
            for axis, value in enumerate(cell_sums(sums[0], sums[1], odd)):
                cell_rows[axis * HEADS + head] = value
            for which, value in ((1, keys_cells), (2, values_grad)):
                there = pl.ds(pl.multiple_of(at + which * D, LANES), LANES)
                value = value.astype(BF16)
                if odd:
                    value = mixed[:, there] * low + value * high
                mixed[:, there] = value
        value = (pair_t[...].T * scale).astype(BF16)
        mixed[:, lanes] = value
        keep_vector("q_bias", at, column_sum(value.astype(F32)))
        there = pl.ds(pl.multiple_of(at + 2 * D, LANES), LANES)
        keep_vector("v_bias", at, column_sum(mixed[:, there].astype(F32)))
        return carry

    lax.fori_loop(0, 2, one_pair, 0)
    reducing.third(2)
    lax.fori_loop(2, 4, one_pair, 0)
    reducing.fourth(2)
    reducing.give(2)
    lax.fori_loop(4, PAIRS, one_pair, 0)

    keep_vector("gain_two", 0, gain_two[0:1, :])
    keep_vector("shift_two", 0, gain_two[1:2, :])
    notes[...] = jnp.zeros_like(notes)
    table = VEC["tables"] // LANES
    for row in range(table):
        notes[row : row + 1, :] = vecg[0:1, row * LANES : (row + 1) * LANES]
    notes[table : table + 9, :] = bucket_rows(cell_rows, diag_rows)
    climbing.start()

    loads["w_qkv"].wait()
    for n in range(D // NBLOCK):
        lanes = slice(n * NBLOCK, (n + 1) * NBLOCK)
        value = second[:, lanes] + times_transposed(mixed[...], w_qkv[lanes, :])
        hidden_low[:, lanes] = value.astype(BF16)
    own_hidden = to_pos(hidden_low, hidden_pos, 1)
    loads["features"].wait()
    for n in range(D // NBLOCK):
        lanes = slice(n * NBLOCK, (n + 1) * NBLOCK)
        store(1, 2, 0, matmul(features_t[...], hidden_low[:, lanes]), n * (NBLOCK // LANES))
    reducing.settle(3)
    unstage_column(plan, flat, staged, 1)
    reducing.swap(1)
    climbing.rise()

    loads["low"].wait()
    for n in range(D // NBLOCK):
        rows = slice(n * NBLOCK, (n + 1) * NBLOCK)
        turned[rows, :] = low_t[:, rows].T

    def qkv_rows(n, carry):
        lanes = pl.ds(pl.multiple_of(n * NBLOCK, NBLOCK), NBLOCK)
        store(0, 0, 0, matmul(turned[...], mixed[:, lanes]), n * (NBLOCK // LANES))
        return carry

    lax.fori_loop(0, 3 * D // NBLOCK, qkv_rows, 0)
    out_rows(0, 0, 208)
    reducing.settle(2)
    unstage_column(plan, flat, staged, 0)
    reducing.swap(0)
    reducing.first(1)
    climbing.end()
    reducing.first(0)
    reducing.second(1)
    reducing.second(0)
    reducing.third(1)
    reducing.third(0)
    reducing.fourth(1)
    reducing.give(1)
    reducing.fourth(0)
    reducing.give(0)
    reducing.receive(out)
    note_quarter, note_first, note_row = note_place(plan)
    base = note_first + note_row

    @pl.when(climbing.root)
    def _():
        out[note_quarter, base : base + MISC_ROWS, :] = (
            out[note_quarter, base : base + MISC_ROWS, :] + notes[:MISC_ROWS, :]
        )

    in_pos(output_pos, 0)
    in_pos(hidden_pos, 1)
    own_output.wait()
    own_hidden.wait()
    for copy in positions:
        copy.wait_send()
    for k in range(COLUMNS):
        reducing.given(k)
    reducing.settle(1)
    reducing.settle(0)


def backward_pass(plan, operands):
    anywhere = pl.BlockSpec(memory_space=pl.ANY)
    vmem = pl.BlockSpec(memory_space=pltpu.VMEM)
    token = (WINLEN, D)
    block = (plan.quarter, LANES)
    positions = jax.ShapeDtypeStruct((DEPTH, WINLEN // DEPTH, D), BF16)
    scratch = [
        pltpu.VMEM((2, CORES, DEPTH, COLUMNS) + block, BF16),
        pltpu.VMEM((plan.staged, LANES), F32),
        pltpu.VMEM((2, DEPTH, COLUMNS) + block, BF16),
        pltpu.VMEM((COLUMNS, 2, 2) + block, BF16),
        pltpu.VMEM((COLUMNS, 2, DEPTH) + block, BF16),
        pltpu.VMEM((COLUMNS, DEPTH - 1) + block, BF16),
        pltpu.VMEM((COLUMNS,) + block, BF16),
        pltpu.VMEM((COLUMNS,) + block, BF16),
        pltpu.VMEM((WINLEN, FF), BF16),
        pltpu.VMEM((WINLEN, FF), BF16),
        pltpu.VMEM((FF, D), BF16),
        pltpu.VMEM((D, FF), BF16),
        pltpu.VMEM((D, D), BF16),
        pltpu.VMEM((D, WINLEN), BF16),
        pltpu.VMEM(token, BF16),
        pltpu.VMEM((D, WINLEN), BF16),
        pltpu.VMEM((D, WINLEN), BF16),
        pltpu.VMEM(token, BF16),
        pltpu.VMEM(token, BF16),
        pltpu.VMEM(token, BF16),
        pltpu.VMEM(token, F32),
        pltpu.VMEM(token, F32),
        pltpu.VMEM(token, BF16),
        pltpu.VMEM(token, BF16),
        pltpu.VMEM((2, WINLEN, WINLEN), BF16),
        pltpu.VMEM((WINLEN, WINLEN), BF16),
        pltpu.VMEM((WINLEN, WINLEN), BF16),
        pltpu.VMEM((WINLEN, WINLEN), BF16),
        pltpu.VMEM((WINLEN, WINLEN), BF16),
        pltpu.VMEM((WINLEN, WINLEN), BF16),
        pltpu.VMEM((LANES, 5 * LANES), F32),
        pltpu.VMEM((LANES, WINLEN), BF16),
        pltpu.VMEM((WINLEN, LANES), BF16),
        pltpu.VMEM((LANES, WINLEN), F32),
        pltpu.VMEM((WINLEN, LANES), BF16),
        pltpu.VMEM((WINLEN, LANES), F32),
        pltpu.VMEM((1, VEC_ROWS * LANES), F32),
        pltpu.VMEM((2 * HEADS, 1, LANES), F32),
        pltpu.VMEM((HEADS, 1, WIDE), F32),
        pltpu.VMEM((NOTE_ROWS, LANES), F32),
        pltpu.VMEM((7, NOTE_ROWS, LANES), F32),
        pltpu.SemaphoreType.DMA((16,)),
        pltpu.SemaphoreType.DMA((2,)),
        pltpu.SemaphoreType.REGULAR((2,)),
        pltpu.SemaphoreType.DMA((2, 2, DEPTH)),
        pltpu.SemaphoreType.DMA((2, 7)),
    ]
    return pl.pallas_call(
        functools.partial(backward_kernel, plan),
        out_shape=[jax.ShapeDtypeStruct((COLUMNS,) + block, F32), positions, positions],
        in_specs=[anywhere] * 16 + [vmem] * 6 + [anywhere],
        out_specs=[vmem, anywhere, anywhere],
        scratch_shapes=scratch + sem_shapes(REDUCE_SEMS),
        compiler_params=pltpu.CompilerParams(
            collective_id=1, has_side_effects=True, vmem_limit_bytes=62 * 2**20
        ),
        name="backward_pass",
    )(*operands)


def token_info(doc_lengths, box_coords):
    places = jnp.arange(WINLEN, dtype=jnp.int32)
    first = places == 0
    doc = jnp.zeros((WINLEN,), jnp.int32)
    end = 0
    for d in range(3):
        end = end + doc_lengths[d]
        doc = doc + (places >= end).astype(jnp.int32)
        first = first | (places == end)
    rows = [box_coords[:, c] for c in range(4)] + [doc, first.astype(jnp.int32)]
    return jnp.stack(rows + [jnp.zeros_like(doc)] * 2).astype(F32)


def fast_shards(hidden_in, cotangent, box_coords, doc_lengths, params, moment_one, moment_two):
    head_pos = lax.axis_index("head")
    shard_len = params.shape[0]
    plan = Plan(shard_len)
    own = params.astype(BF16).reshape(plan.rows, LANES)
    own = jnp.pad(own, ((0, plan.padded - plan.rows), (0, 0))).reshape(COLUMNS, plan.quarter, LANES)
    own_box = lax.dynamic_index_in_dim(box_coords, head_pos, 0, keepdims=False)
    own_lengths = lax.dynamic_index_in_dim(doc_lengths, head_pos, 0, keepdims=False)
    info = token_info(own_lengths, own_box)
    (proj_qkv, proj_out, proj_in, proj_back, features_t, start_low, queries, keys, values, probs, context_t,
     xhat, normed_low, active, slope, grad_second, vec, rstd, grad_norm_two, output, _, hot_two,
     rest_rows, share) = forward_pass(plan, own, hidden_in, cotangent, info)
    summed, output_low, grad_hidden = backward_pass(
        Plan(shard_len, carry=5 * LANES),
        (active, slope, proj_back, proj_in, proj_out, proj_qkv, normed_low, start_low, features_t, context_t,
         queries, keys, values, probs, xhat, grad_second, rstd, vec, grad_norm_two, hot_two, rest_rows,
         share, output),
    )
    grad_share = summed.reshape(plan.padded, LANES)[: plan.rows].reshape(-1)
    return finish_step(output_low, grad_hidden, grad_share, params, moment_one, moment_two)


def finish_step(output_low, grad_hidden, grad_share, params, moment_one, moment_two):
    shard_len = params.shape[0]
    index = lax.axis_index("dp") * lax.axis_size("head") + lax.axis_index("head")
    flat_index = index * shard_len + jnp.arange(shard_len, dtype=jnp.int32)
    param_step, new_one = adam_step(params, moment_one, moment_two, grad_share, flat_index)
    return (output_low, grad_hidden, grad_share, param_step, new_one)


def to_windows(shard):
    return lax.all_to_all(shard, "head", split_axis=0, concat_axis=1, tiled=True)


def to_positions(window):
    return lax.all_to_all(window, "head", split_axis=1, concat_axis=0, tiled=True)


def plain_shards(hidden_in, cotangent, box_coords, doc_lengths, params, moment_one, moment_two):
    head_pos = lax.axis_index("head")
    groups = lax.axis_size("head")
    shard_len = params.shape[0]
    flat_params = lax.all_gather(params.astype(BF16), ("dp", "head"), axis=0, tiled=True)
    pieces = unpack(flat_params)
    hidden = to_windows(hidden_in).reshape(WINLEN, D)
    cot = to_windows(cotangent).reshape(WINLEN, D)
    own_box = lax.dynamic_index_in_dim(box_coords, head_pos, 0, keepdims=False)
    own_lengths = lax.dynamic_index_in_dim(doc_lengths, head_pos, 0, keepdims=False)
    chosen, relative, centre_x, centre_y = window_layout(own_lengths, own_box)
    features = box_features(relative).astype(BF16)

    proj_qkv, proj_out, proj_box, proj_in, proj_back = pieces[:5]
    qv_bias, out_bias, norm_one, in_bias, back_bias, norm_two, tables = pieces[5:]
    ops = bias_operands(tables, chosen, centre_x, centre_y)
    start_state = hidden.astype(F32) + matmul(features, proj_box)
    start_low = start_state.astype(BF16)
    qv_float = qv_bias.astype(F32)
    mixed = matmul(start_low, proj_qkv)
    queries = (mixed[:, :D] + qv_float[0]).astype(BF16) * jnp.asarray(HEAD_DIM ** (-0.5), BF16)
    keys = mixed[:, D : 2 * D].astype(BF16)
    values = (mixed[:, 2 * D :] + qv_float[1]).astype(BF16)

    probs, context_t = attention_forward(queries, keys, values, ops)
    first_sum = start_state + rows_inner(context_t, proj_out) + out_bias.astype(F32)
    normed, norm_one_back = jax.vjp(layer_norm, first_sum, norm_one.astype(F32))
    normed_low = normed.astype(BF16)
    inner_act = matmul(normed_low, proj_in) + in_bias.astype(F32)
    active, gelu_back = jax.vjp(gelu_exact, inner_act)
    active_low = active.astype(BF16)
    second_sum = normed + matmul(active_low, proj_back) + back_bias.astype(F32)
    output, norm_two_back = jax.vjp(layer_norm, second_sum, norm_two.astype(F32))
    output_low = to_positions(output.astype(BF16).reshape(1, WINLEN, D))

    grad_second, grad_norm_two = norm_two_back(cot.astype(F32))
    grad_branch = grad_second.astype(BF16)
    grad_proj_back = rows_inner(active_low, grad_branch)
    grad_back_bias = jnp.sum(grad_branch.astype(F32), axis=0)
    (grad_inner_f,) = gelu_back(times_transposed(grad_branch, proj_back))
    grad_inner = grad_inner_f.astype(BF16)
    grad_proj_in = rows_inner(normed_low, grad_inner)
    grad_in_bias = jnp.sum(grad_inner.astype(F32), axis=0)
    grad_first, grad_norm_one = norm_one_back(grad_second + times_transposed(grad_inner, proj_in))
    grad_attn = grad_first.astype(BF16)
    grad_proj_out = matmul(context_t, grad_attn)
    grad_out_bias = jnp.sum(grad_attn.astype(F32), axis=0)
    grad_context = times_transposed(grad_attn, proj_out).astype(BF16)
    grad_queries_t, grad_keys, grad_values, cells, diag = attention_backward(
        queries, keys, values, grad_context, probs, ops
    )
    table_grad = table_grads(cells, diag)
    grad_mixed = jnp.concatenate([grad_queries_t.T, grad_keys, grad_values], axis=1)
    grad_proj_qkv = rows_inner(start_low, grad_mixed)
    summed = jnp.sum(grad_mixed.astype(F32), axis=0)
    grad_qv_bias = jnp.stack([summed[:D], summed[2 * D :]])
    grad_start = grad_first + times_transposed(grad_mixed, proj_qkv)
    grad_start_low = grad_start.astype(BF16)
    grad_hidden = to_positions(grad_start_low.reshape(1, WINLEN, D))
    grad_proj_box = rows_inner(features, grad_start_low)
    grad_list = (
        grad_proj_qkv,
        grad_proj_out,
        grad_proj_box,
        grad_proj_in,
        grad_proj_back,
        grad_qv_bias,
        grad_out_bias,
        grad_norm_one,
        grad_in_bias,
        grad_back_bias,
        grad_norm_two,
        table_grad,
    )
    padding = jnp.zeros((shard_len * groups * lax.axis_size("dp") - USED,), BF16)
    grads_flat = jnp.concatenate([piece.astype(BF16).reshape(-1) for piece in grad_list] + [padding])
    grad_share = lax.psum_scatter(
        grads_flat, ("dp", "head"), scatter_dimension=0, tiled=True
    ).astype(F32)
    return finish_step(output_low, grad_hidden, grad_share, params, moment_one, moment_two)


def solution(mesh):
    placed = (
        P("dp", "head", None),
        P("dp", "head", None),
        P("dp", None, None),
        P("dp", None),
        P(("dp", "head")),
        P(("dp", "head")),
        P(("dp", "head")),
    )
    return jax.shard_map(
        fast_shards if fits(mesh) else plain_shards,
        mesh=mesh,
        in_specs=placed,
        out_specs=(
            P("dp", "head", None),
            P("dp", "head", None),
            P(("dp", "head")),
            P(("dp", "head")),
            P(("dp", "head")),
        ),
        check_vma=False,
    )
```

```python
import functools
import math

import jax
import jax.numpy as jnp
import numpy as np
from jax import lax
from jax.experimental import pallas as pl
from jax.experimental.pallas import tpu as pltpu
from jax.sharding import PartitionSpec as P

D = 768
HEADS = 12
FF = 3072
BUCKETS = 32
WINLEN = 512
HEAD_DIM = 64
PAIRS = HEADS // 2
LANES = 128
BLOCKS = WINLEN // LANES

beta_one = 0.9
beta_two = 0.999
adam_eps = 1e-08
norm_eps = 1e-05
base_rate = 0.001
layer_decay = 0.75
decay_weight = 0.01
adam_count = 100
coord_cell = 32
masked_score = -1e30

F32 = jnp.float32
BF16 = jnp.bfloat16


def layouts_list():
    return (
        (D, 3 * D),
        (D, D),
        (D, D),
        (D, FF),
        (FF, D),
        (2, D),
        (D,),
        (2, D),
        (FF,),
        (D,),
        (2, D),
        (3, HEADS, BUCKETS),
    )


def unpack(flat_params):
    pieces = []
    offset = 0
    for layout in layouts_list():
        elements = math.prod(layout)
        pieces.append(flat_params[offset : offset + elements].reshape(layout))
        offset += elements
    return pieces


def matmul(left_mat, right_mat):
    return jnp.dot(left_mat, right_mat, preferred_element_type=F32)


def rows_inner(left_mat, right_mat):
    return lax.dot_general(left_mat, right_mat, (((0,), (0,)), ((), ())), preferred_element_type=F32)


def times_transposed(left_mat, right_mat):
    return lax.dot_general(left_mat, right_mat, (((1,), (1,)), ((), ())), preferred_element_type=F32)


def layer_norm(values, gain_bias):
    row_mean = jnp.mean(values, axis=-1, keepdims=True)
    centred = values - row_mean
    spread = jnp.mean(centred * centred, axis=-1, keepdims=True)
    return centred * lax.rsqrt(spread + norm_eps) * gain_bias[0] + gain_bias[1]


def gelu_exact(values):
    return jax.nn.gelu(values, approximate=False)


def hot(index, count):
    return (np.asarray(index)[..., None] == np.arange(count)).astype(np.float32)


def clipped(steps):
    return np.clip(steps, -(BUCKETS // 2), BUCKETS // 2 - 1) + BUCKETS // 2


CELLS = np.arange(BUCKETS)
HOT_SAME = hot(clipped(CELLS[:, None] - CELLS[None, :]), BUCKETS)
HOT_LESS = hot(clipped(CELLS[:, None] - CELLS[None, :] - 1), BUCKETS)
WIDE = 6 * LANES
_U = np.arange(WIDE)
BAND_HOT = hot(np.where(_U < 5 * LANES, clipped(_U - 2 * LANES), 0), BUCKETS)
_V = np.arange(4 * LANES)
DIAG_HOT = np.concatenate(
    [
        hot(np.zeros(LANES, np.int64), BUCKETS),
        hot(np.where(_V < 3 * LANES, clipped(_V - LANES), 0), BUCKETS),
        hot(np.full(LANES, BUCKETS - 1), BUCKETS),
    ]
)


def window_layout(doc_lengths, box_coords):
    doc_ends = jnp.cumsum(doc_lengths, dtype=jnp.int32)
    doc_starts = doc_ends - doc_lengths
    places = jnp.arange(WINLEN, dtype=jnp.int32)
    doc_ids = jnp.sum(
        (places[:, None] >= doc_ends[None, :]).astype(jnp.int32), axis=1, dtype=jnp.int32
    )
    docs = jnp.arange(doc_lengths.shape[0], dtype=jnp.int32)
    chosen = doc_ids[:, None] == docs[None, :]
    first_hot = places[:, None] == doc_starts[None, :]
    first_box = jnp.sum(
        jnp.where(first_hot[:, :, None], box_coords[:, None, :], 0), axis=0, dtype=jnp.int32
    )
    anchor = jnp.sum(
        jnp.where(chosen[:, :, None], first_box[None, :, :], 0), axis=1, dtype=jnp.int32
    )
    relative = box_coords - jnp.concatenate([anchor[:, :2], anchor[:, :2]], axis=1)
    centre_x = (box_coords[:, 0] + box_coords[:, 2]) // 2
    centre_y = (box_coords[:, 1] + box_coords[:, 3]) // 2
    return chosen, relative, centre_x, centre_y


def box_features(relative):
    count_freq = D // 8
    steps = jnp.arange(count_freq, dtype=F32)
    frequency = jnp.exp(steps * (-math.log(1000.0) / count_freq))
    angles = relative.astype(F32)[:, :, None] * frequency[None, None, :]
    return jnp.concatenate([jnp.sin(angles), jnp.cos(angles)], axis=2).reshape(relative.shape[0], D)


def bias_operands(tables, chosen, centre_x, centre_y):
    cell_x, cell_y = centre_x // coord_cell, centre_y // coord_cell
    rest_x, rest_y = centre_x % coord_cell, centre_y % coord_cell
    cells = jnp.arange(BUCKETS, dtype=jnp.int32)
    hot_x = (cell_x[:, None] == cells[None, :]).astype(BF16)
    hot_y = (cell_y[:, None] == cells[None, :]).astype(BF16)
    none = jnp.zeros_like(hot_x)
    hot_two = jnp.concatenate([hot_x, hot_y, hot_x, hot_y], axis=1)
    key_x = jnp.stack(
        [
            jnp.concatenate([hot_x, -hot_x, none, none], axis=1),
            jnp.concatenate([none, none, hot_x, -hot_x], axis=1),
        ]
    )
    key_y = jnp.stack(
        [
            jnp.concatenate([hot_y, -hot_y, none, none], axis=1),
            jnp.concatenate([none, none, hot_y, -hot_y], axis=1),
        ]
    )
    same = jnp.einsum("qcb,thb->thqc", HOT_SAME.astype(BF16), tables[1:], preferred_element_type=F32)
    less = jnp.einsum("qcb,thb->thqc", HOT_LESS.astype(BF16), tables[1:], preferred_element_type=F32)
    zero = jnp.zeros_like(same[0])
    base = jnp.concatenate(
        [jnp.concatenate([same[0], zero], axis=2), jnp.concatenate([zero, same[1]], axis=2)], axis=1
    )
    base = base.reshape(PAIRS, 2, 64, 64)[:, ::-1].reshape(HEADS, 64, 64)
    diff_x = jnp.concatenate([jnp.concatenate([less[0], same[0]], axis=2), jnp.zeros((HEADS, 32, 64), F32)], axis=1)
    diff_y = jnp.concatenate([jnp.zeros((HEADS, 32, 64), F32), jnp.concatenate([less[1], same[1]], axis=2)], axis=1)
    rows = jnp.concatenate([base, diff_x, diff_y], axis=0).astype(BF16)
    rows = rows.transpose(1, 0, 2).reshape(64, 3 * D)
    met = matmul(hot_two[:, :64], rows).astype(BF16)
    band = matmul(tables[0], jnp.asarray(BAND_HOT.T, BF16)).reshape(HEADS, 1, WIDE)
    rest_cols = jnp.stack([rest_x, rest_y], axis=1).astype(F32)
    rest_rows = rest_cols.T
    pad = jnp.zeros((WINLEN, LANES - chosen.shape[1]), BF16)
    marks = chosen.astype(BF16)
    mark_keys = jnp.concatenate([marks, pad], axis=1)
    mark_queries = jnp.concatenate([(1 - marks) * jnp.asarray(masked_score, BF16), pad], axis=1)
    return dict(
        hot_two=hot_two,
        key_x=key_x,
        key_y=key_y,
        met=met,
        band=band,
        rest_cols=rest_cols,
        rest_rows=rest_rows,
        mark_keys=mark_keys,
        mark_queries=mark_queries,
    )


def half_masks():
    lane = lax.broadcasted_iota(jnp.int32, (1, LANES), 1)
    low = (lane < HEAD_DIM).astype(F32)
    return low.astype(BF16), (1.0 - low).astype(BF16)


def less_masks(rest_cols, rest_rows, less_x, less_y):
    for part in range(BLOCKS):
        rows = slice(part * LANES, (part + 1) * LANES)
        for axis, less in ((0, less_x), (1, less_y)):
            column = rest_cols[rows, axis : axis + 1]
            row = rest_rows[axis : axis + 1, :]
            less[rows, :] = jnp.where(row < column, 1.0, 0.0).astype(less.dtype)


def attention_forward_kernel(
    q_ref, k_ref, v_ref, hot_ref, keyx_ref, keyy_ref, met_ref, band_ref, cols_ref, rows_ref,
    mkey_ref, mquery_ref, probs_ref, context_ref,
    kaug, qaug, less_x, less_y, wide, scores,
):
    low, high = half_masks()
    less_masks(cols_ref, rows_ref, less_x, less_y)
    kaug[:, LANES:] = mkey_ref[...]
    qaug[:, LANES:] = mquery_ref[...]
    half = 2 * LANES

    def one_pair(pair, carry):
        at = pl.multiple_of(pair * LANES, LANES)
        lanes = pl.ds(at, LANES)
        lanes_x = pl.ds(pl.multiple_of(at + D, LANES), LANES)
        lanes_y = pl.ds(pl.multiple_of(at + 2 * D, LANES), LANES)
        values_t = v_ref[:, lanes].T
        for odd in range(2):
            own, other = (low, high) if odd == 0 else (high, low)
            head = 2 * pair + odd
            kaug[:, :LANES] = k_ref[:, lanes] * own + hot_ref[...] * other
            qaug[:, :LANES] = q_ref[:, lanes] * own + met_ref[:, lanes] * other
            skew_band(band_ref[head], wide)
            for side in range(2):
                cols = slice(side * half, (side + 1) * half)
                top = None
                for part in range(BLOCKS):
                    rows = slice(part * LANES, (part + 1) * LANES)
                    s = times_transposed(kaug[rows, :], qaug[cols, :])
                    dx = times_transposed(keyx_ref[odd, rows, :], met_ref[cols, lanes_x])
                    dy = times_transposed(keyy_ref[odd, rows, :], met_ref[cols, lanes_y])
                    bias = []
                    for block in range(2 * side, 2 * side + 2):
                        step = max(-2, min(2, block - part)) + 2
                        bias.append(wide[:, step * LANES : (step + 1) * LANES])
                    s = s + jnp.concatenate(bias, axis=1)
                    s = s + dx * less_x[rows, cols] + dy * less_y[rows, cols]
                    scores[rows, :] = s
                    best = jnp.max(s, axis=0, keepdims=True)
                    top = best if top is None else jnp.maximum(top, best)
                total = None
                for part in range(BLOCKS):
                    rows = slice(part * LANES, (part + 1) * LANES)
                    e = jnp.exp(scores[rows, :] - top)
                    scores[rows, :] = e
                    add = jnp.sum(e, axis=0, keepdims=True)
                    total = add if total is None else total + add
                share = 1.0 / total
                for part in range(BLOCKS):
                    rows = slice(part * LANES, (part + 1) * LANES)
                    probs_ref[head, rows, cols] = (scores[rows, :] * share).astype(BF16)
                got = matmul(
                    values_t[odd * HEAD_DIM : (odd + 1) * HEAD_DIM, :], probs_ref[head, :, cols]
                )
                context_ref[pl.ds(pl.multiple_of(head * HEAD_DIM, HEAD_DIM), HEAD_DIM), cols] = (
                    got.astype(BF16)
                )
        return carry

    lax.fori_loop(0, PAIRS, one_pair, 0)


def skew_band(row, wide):
    x = jnp.broadcast_to(row, (8, WIDE))
    sub = lax.broadcasted_iota(jnp.int32, (8, WIDE), 0)
    for bit in (1, 2, 4):
        x = jnp.where((sub & bit) != 0, pltpu.roll(x, bit, 1), x)
    for group in range(LANES // 8):
        y = x if group == 0 else pltpu.roll(x, 8 * group, 1)
        wide[8 * group : 8 * group + 8, :] = y[:, : 5 * LANES]


def diagonal_sums(parts):
    total = None
    for group in range(LANES // 8):
        x = jnp.concatenate(
            [parts[8 * group : 8 * group + 8, LANES : 4 * LANES], jnp.zeros((8, LANES), F32)], axis=1
        )
        y = x if group == 0 else pltpu.roll(x, 4 * LANES - 8 * group, 1)
        total = y if total is None else total + y
    sub = lax.broadcasted_iota(jnp.int32, (8, 4 * LANES), 0)
    for bit in (1, 2, 4):
        total = jnp.where((sub & bit) != 0, pltpu.roll(total, 4 * LANES - bit, 1), total)
    return jnp.sum(total, axis=0, keepdims=True)


def attention_backward_kernel(
    q_ref, k_ref, v_ref, dctx_ref, probs_ref, hot_ref, cols_ref, rows_ref,
    dq_ref, dk_ref, dv_ref, cells_ref, diag_ref,
    qaug, less_x, less_y, scores, dscores, band, kept, hot_t,
):
    low, high = half_masks()
    less_masks(cols_ref, rows_ref, less_x, less_y)
    hot_t[...] = hot_ref[...].T
    lane = lax.broadcasted_iota(jnp.int32, (1, LANES), 1)
    scale = HEAD_DIM ** (-0.5)
    of_x = jnp.where((lane // BUCKETS) % 2 == 0, 1.0, 0.0)
    cells_x = hot_ref[...] * of_x.astype(BF16)
    cells_y = hot_ref[...] * (1.0 - of_x).astype(BF16)

    def one_pair(pair, carry):
        at = pl.multiple_of(pair * LANES, LANES)
        lanes = pl.ds(at, LANES)
        keys_t = k_ref[:, lanes].T
        for odd in range(2):
            own, other = (low, high) if odd == 0 else (high, low)
            head = 2 * pair + odd
            qaug[...] = q_ref[:, lanes] * own + hot_ref[...] * other
            dctx = dctx_ref[:, lanes]
            dot = None
            for part in range(BLOCKS):
                rows = slice(part * LANES, (part + 1) * LANES)
                dp = times_transposed(v_ref[rows, lanes] * own, dctx)
                scores[rows, :] = dp
                add = jnp.sum(dp * probs_ref[head, rows, :].astype(F32), axis=0, keepdims=True)
                dot = add if dot is None else dot + add
            band[...] = jnp.zeros_like(band)
            for part in range(BLOCKS):
                rows = slice(part * LANES, (part + 1) * LANES)
                probs = probs_ref[head, rows, :]
                ds = probs.astype(F32) * (scores[rows, :] - dot)
                for block in range(BLOCKS):
                    step = max(-2, min(2, block - part)) + 2
                    where = slice(step * LANES, (step + 1) * LANES)
                    band[:, where] = band[:, where] + ds[:, block * LANES : (block + 1) * LANES]
                ds = ds.astype(BF16)
                dscores[rows, :] = ds
                both = matmul(ds, qaug[...])
                less = matmul(ds * less_x[rows, :], cells_x) + matmul(ds * less_y[rows, :], cells_y)
                dv = matmul(probs, dctx)
                kept[odd, 0, rows, :] = both
                kept[odd, 1, rows, :] = less
                kept[odd, 2, rows, :] = dv
            got = matmul(keys_t[odd * HEAD_DIM : (odd + 1) * HEAD_DIM, :], dscores[...])
            dq_ref[pl.ds(pl.multiple_of(head * HEAD_DIM, HEAD_DIM), HEAD_DIM), :] = (
                got * scale
            ).astype(BF16)
            diag_ref[head, :, LANES : 5 * LANES] = diagonal_sums(band)
            diag_ref[head, :, :LANES] = jnp.sum(band[:, :LANES], axis=0, keepdims=True)
            diag_ref[head, :, 5 * LANES :] = jnp.sum(band[:, 4 * LANES :], axis=0, keepdims=True)
            for which in range(2):
                summed = kept[odd, which]
                first = summed.astype(BF16)
                rest = (summed - first.astype(F32)).astype(BF16)
                cells_ref[head, which] = matmul(hot_t[:64, :], first) + matmul(hot_t[:64, :], rest)
        dk_ref[:, lanes] = jnp.where(lane < HEAD_DIM, kept[0, 0], kept[1, 0]).astype(BF16)
        dv_ref[:, lanes] = jnp.where(lane < HEAD_DIM, kept[0, 2], kept[1, 2]).astype(BF16)
        return carry

    lax.fori_loop(0, PAIRS, one_pair, 0)


def attention_forward(queries, keys, values, ops):
    return pl.pallas_call(
        attention_forward_kernel,
        out_shape=(
            jax.ShapeDtypeStruct((HEADS, WINLEN, WINLEN), BF16),
            jax.ShapeDtypeStruct((D, WINLEN), BF16),
        ),
        scratch_shapes=[
            pltpu.VMEM((WINLEN, 2 * LANES), BF16),
            pltpu.VMEM((WINLEN, 2 * LANES), BF16),
            pltpu.VMEM((WINLEN, WINLEN), F32),
            pltpu.VMEM((WINLEN, WINLEN), F32),
            pltpu.VMEM((LANES, 5 * LANES), F32),
            pltpu.VMEM((WINLEN, 2 * LANES), F32),
        ],
        compiler_params=pltpu.CompilerParams(vmem_limit_bytes=48 * 2**20),
        name="attention_forward",
    )(
        queries, keys, values, ops["hot_two"], ops["key_x"], ops["key_y"], ops["met"], ops["band"],
        ops["rest_cols"], ops["rest_rows"], ops["mark_keys"], ops["mark_queries"],
    )


def attention_backward(queries, keys, values, grad_context, probs, ops):
    return pl.pallas_call(
        attention_backward_kernel,
        out_shape=(
            jax.ShapeDtypeStruct((D, WINLEN), BF16),
            jax.ShapeDtypeStruct((WINLEN, D), BF16),
            jax.ShapeDtypeStruct((WINLEN, D), BF16),
            jax.ShapeDtypeStruct((HEADS, 2, 64, LANES), F32),
            jax.ShapeDtypeStruct((HEADS, 1, WIDE), F32),
        ),
        scratch_shapes=[
            pltpu.VMEM((WINLEN, LANES), BF16),
            pltpu.VMEM((WINLEN, WINLEN), BF16),
            pltpu.VMEM((WINLEN, WINLEN), BF16),
            pltpu.VMEM((WINLEN, WINLEN), F32),
            pltpu.VMEM((WINLEN, WINLEN), BF16),
            pltpu.VMEM((LANES, 5 * LANES), F32),
            pltpu.VMEM((2, 3, WINLEN, LANES), F32),
            pltpu.VMEM((LANES, WINLEN), BF16),
        ],
        compiler_params=pltpu.CompilerParams(vmem_limit_bytes=48 * 2**20),
        name="attention_backward",
    )(
        queries, keys, values, grad_context, probs, ops["hot_two"], ops["rest_cols"],
        ops["rest_rows"],
    )


def table_grads(cells, diag):
    exact = lax.Precision.HIGHEST
    pairs = cells.reshape(PAIRS, 2, 2, 64, LANES)
    every = jnp.stack([pairs[:, 0, 0, :, 64:], pairs[:, 1, 0, :, :64]], axis=1).reshape(HEADS, 64, 64)
    less = cells[:, 1]
    less_x, less_y = less[:, :32, :32], less[:, 32:, 32:64]
    all_x, all_y = every[:, :32, :32], every[:, 32:, 32:]
    same = jnp.stack([all_x - less_x, all_y - less_y]).reshape(2 * HEADS, -1)
    below = jnp.stack([less_x, less_y]).reshape(2 * HEADS, -1)
    same_hot = jnp.asarray(HOT_SAME.transpose(1, 0, 2).reshape(-1, BUCKETS))
    less_hot = jnp.asarray(HOT_LESS.transpose(1, 0, 2).reshape(-1, BUCKETS))
    moved = jnp.dot(same, same_hot, precision=exact) + jnp.dot(below, less_hot, precision=exact)
    along = jnp.dot(diag.reshape(HEADS, WIDE), jnp.asarray(DIAG_HOT), precision=exact)
    return jnp.concatenate([along[None], moved.reshape(2, HEADS, BUCKETS)], axis=0)


COLUMNS = 4
CORES = 2
DEPTH = 4
USED = sum(math.prod(layout) for layout in layouts_list())
MATRICES = layouts_list()[:5]
MISC = sum(math.prod(layout) for layout in layouts_list()[5:])
MISC_ROWS = -(-MISC // (8 * LANES)) * 8

HALO = 5 * LANES
PIECE_TILES = 30
COLUMN_TILES = 936


class Plan:
    def __init__(self, shard_len):
        self.rows = shard_len // LANES
        self.quarter = 16 * PIECE_TILES
        self.column_rows = CORES * DEPTH * COLUMNS * self.quarter
        self.pad = self.column_rows - 16 * COLUMN_TILES
        self.starts, self.tile_starts = [], []
        offset = 0
        for depth, width in MATRICES:
            self.starts.append(offset // LANES)
            self.tile_starts.append(offset // (16 * LANES))
            offset += depth * width
        self.misc_start = offset // LANES
        assert offset == COLUMNS * COLUMN_TILES * 16 * LANES

    def in_column(self, k):
        taken = []
        for index, (depth, width) in enumerate(MATRICES):
            blocks = width // LANES
            begin, end = (
                max(0, min(depth // 16 * blocks, at * COLUMN_TILES - self.tile_starts[index]))
                for at in (k, k + 1)
            )
            assert begin % blocks == 0 and end % blocks == 0
            if end > begin:
                taken.append((index, begin // blocks * 16, end // blocks * 16))
        return taken


def fits(mesh):
    return mesh.shape["dp"] == COLUMNS * CORES and mesh.shape["head"] == DEPTH


MESH = pl.DeviceIdType.MESH


class Place:
    def __init__(self):
        dp = lax.axis_index("dp")
        self.z = lax.axis_index("head")
        self.core = dp % CORES
        self.column = dp // CORES
        self.x = self.column % 2
        self.y = self.column // 2
        self.col_x = 2 * self.y + (1 - self.x)
        self.col_y = 2 * (1 - self.y) + self.x
        self.col_d = 2 * (1 - self.y) + (1 - self.x)
        self.peer_x = self.at(self.col_x, self.core, self.z)
        self.peer_y = self.at(self.col_y, self.core, self.z)
        self.peer_d = self.at(self.col_d, self.core, self.z)
        self.peer_core = self.at(self.column, 1 - self.core, self.z)
        self.far = [lax.rem(self.z + d, DEPTH) for d in range(1, DEPTH)]
        self.from_far = [lax.rem(self.z + DEPTH - d, DEPTH) for d in range(1, DEPTH)]
        self.peers_z = [self.at(self.column, self.core, f) for f in self.far]
        self.index = dp * DEPTH + self.z
        self.count = COLUMNS * CORES * DEPTH
        self.before = {"dp": lax.rem(self.index + self.count - 1, self.count) // DEPTH, "head": lax.rem(self.z + DEPTH - 1, DEPTH)}
        self.after = {"dp": lax.rem(self.index + 1, self.count) // DEPTH, "head": lax.rem(self.z + 1, DEPTH)}

    def at(self, column, core, z):
        return {"dp": column * CORES + core, "head": z}

    def greet(self):
        barrier = pltpu.get_barrier_semaphore()
        peers = [self.peer_x, self.peer_y, self.peer_d, self.peer_core] + self.peers_z
        peers += [self.before, self.after]
        for peer in peers:
            pl.semaphore_signal(barrier, inc=1, device_id=peer, device_id_type=MESH)
        pl.semaphore_wait(barrier, len(peers))


def remote(src, dst, send_sem, recv_sem, peer):
    return pltpu.make_async_remote_copy(
        src_ref=src, dst_ref=dst, send_sem=send_sem, recv_sem=recv_sem, device_id=peer,
        device_id_type=MESH,
    )


class Gathering:
    def __init__(self, place, flat, sems):
        self.place = place
        self.flat = flat
        self.sems = sems
        self.sent = []

    def send(self, src, dst, kind, index, peer):
        copy = remote(src, dst, self.sems[kind].at[0, index], self.sems[kind].at[1, index], peer)
        copy.start()
        self.sent.append(copy)

    def got(self, dst, kind, index):
        remote(
            dst, dst, self.sems[kind].at[0, index], self.sems[kind].at[1, index], self.place.peer_x
        ).wait_recv()

    def spread(self, own):
        p = self.place
        for index, (column, peer) in enumerate(
            ((p.col_x, p.peer_x), (p.col_y, p.peer_y), (p.col_d, p.peer_d))
        ):
            self.send(
                own.at[column], self.flat.at[p.column, p.core, p.z, column], "spread", index, peer
            )
        self.flat[p.column, p.core, p.z, p.column] = own[p.column]

    def spread_done(self):
        p = self.place
        for index, column in enumerate((p.col_x, p.col_y, p.col_d)):
            self.got(self.flat.at[column, p.core, p.z, p.column], "spread", index)

    def along_z(self, k):
        p = self.place
        piece = self.flat.at[k, p.core, p.z, p.column]
        for d in range(DEPTH - 1):
            self.send(piece, piece, "z", 3 * k + d, p.peers_z[d])

    def first(self, k):
        p = self.place
        for d in range(DEPTH - 1):
            self.got(self.flat.at[k, p.core, p.from_far[d], p.column], "z", 3 * k + d)
        piece = self.flat.at[k, p.core, :, p.column]
        self.send(piece, piece, "one", 2 * k, p.peer_x)
        self.send(piece, piece, "one", 2 * k + 1, p.peer_y)
        self.send(piece, piece, "core", 5 * k, p.peer_core)

    def second(self, k):
        p = self.place
        from_x = self.flat.at[k, p.core, :, p.col_x]
        self.got(from_x, "one", 2 * k)
        part = self.flat.at[k, p.core, 0:2, p.col_x]
        self.send(part, part, "two", 2 * k, p.peer_y)
        self.send(from_x, from_x, "core", 5 * k + 1, p.peer_core)
        from_y = self.flat.at[k, p.core, :, p.col_y]
        self.got(from_y, "one", 2 * k + 1)
        part = self.flat.at[k, p.core, 2:4, p.col_y]
        self.send(part, part, "two", 2 * k + 1, p.peer_x)
        self.send(from_y, from_y, "core", 5 * k + 2, p.peer_core)

    def third(self, k):
        p = self.place
        part = self.flat.at[k, p.core, 0:2, p.col_d]
        self.got(part, "two", 2 * k)
        self.send(part, part, "core", 5 * k + 3, p.peer_core)
        part = self.flat.at[k, p.core, 2:4, p.col_d]
        self.got(part, "two", 2 * k + 1)
        self.send(part, part, "core", 5 * k + 4, p.peer_core)

    def complete(self, k):
        p = self.place
        other = 1 - p.core
        for index, column in enumerate((p.column, p.col_x, p.col_y)):
            self.got(self.flat.at[k, other, :, column], "core", 5 * k + index)
        self.got(self.flat.at[k, other, 0:2, p.col_d], "core", 5 * k + 3)
        self.got(self.flat.at[k, other, 2:4, p.col_d], "core", 5 * k + 4)

    def finish(self):
        for copy in self.sent:
            copy.wait_send()


GATHER_SEMS = {"spread": 3, "z": 12, "one": 8, "two": 8, "core": 20}


def sem_shapes(counts):
    return [pltpu.SemaphoreType.DMA((2, count)) for count in counts.values()]


class Halo:
    def __init__(self, place, buffers, sems):
        self.place, self.buffers, self.sems = place, buffers, sems

    def copy(self, side):
        p = self.place
        return remote(
            self.buffers.at[side], self.buffers.at[3 - side], self.sems.at[0, side],
            self.sems.at[1, 1 - side], p.before if side == 0 else p.after,
        )

    def each(self, act):
        p = self.place

        @pl.when(p.index > 0)
        def _():
            act(0)

        @pl.when(p.index < p.count - 1)
        def _():
            act(1)

    def send(self):
        self.each(lambda side: self.copy(side).start())

    def arrived(self):
        self.each(
            lambda side: remote(
                self.buffers.at[2 + side], self.buffers.at[2 + side], self.sems.at[0, side],
                self.sems.at[1, side], self.place.peer_x,
            ).wait_recv()
        )

    def sent(self):
        self.each(lambda side: self.copy(side).wait_send())


def over_tiles(plan, place, act):
    within = (place.core * DEPTH + place.z) * COLUMNS * PIECE_TILES
    first = place.column * COLUMN_TILES + within
    last = jnp.minimum(first + COLUMNS * PIECE_TILES, (place.column + 1) * COLUMN_TILES)
    shift = HALO - place.index * plan.rows
    for index, (depth, width) in enumerate(MATRICES):
        blocks = width // LANES
        start = plan.tile_starts[index]
        begin = jnp.maximum(first, start)
        end = jnp.maximum(begin, jnp.minimum(last, start + depth // 16 * blocks))

        def one(tile, carry, blocks=blocks, start=start, index=index):
            group = (tile - start) // blocks
            block = (tile - start) - group * blocks
            row = plan.starts[index] + group * (16 * blocks) + block + shift
            act(blocks, tile - first, row)
            return carry

        lax.fori_loop(begin, end, one, 0)


def form_tiles(plan, place, extended, own):
    def act(blocks, tile, row):
        quarter = tile // PIECE_TILES
        at = pl.multiple_of((tile - quarter * PIECE_TILES) * 16, 16)
        own[quarter, pl.ds(at, 16), :] = extended[pl.ds(row, 16, stride=blocks), :].astype(BF16)

    over_tiles(plan, place, act)


def spread_tiles(plan, place, sums, extended):
    def act(blocks, tile, row):
        quarter = tile // PIECE_TILES
        at = pl.multiple_of((tile - quarter * PIECE_TILES) * 16, 16)
        extended[pl.ds(row, 16, stride=blocks), :] = sums[quarter, pl.ds(at, 16), :].astype(F32)

    over_tiles(plan, place, act)


def form_matrices(plan, flat, matrices, k):
    tiles = flat.reshape(-1, LANES)
    for index, begin, end in plan.in_column(k):
        blocks = MATRICES[index][1] // LANES
        base = 16 * plan.tile_starts[index] + plan.pad * k
        target = matrices[index]

        def one(group, carry, blocks=blocks, base=base, target=target):
            got = tiles[pl.ds(pl.multiple_of(base + group * (16 * blocks), 16), 16 * blocks), :]
            rows = pl.ds(pl.multiple_of(group * 16, 16), 16)
            for block in range(blocks):
                target[rows, block * LANES : (block + 1) * LANES] = got[16 * block : 16 * block + 16]
            return carry

        lax.fori_loop(begin // 16, end // 16, one, 0)


def adam_step(params, moment_one, moment_two, grads, flat_index):
    box_part = (flat_index >= 4 * D * D) & (flat_index < 5 * D * D)
    step_rate = jnp.where(box_part, base_rate * layer_decay**12, base_rate * layer_decay)
    decay_mask = jnp.where(flat_index < 5 * D * D + 2 * D * FF, decay_weight, 0.0)
    moment_one = beta_one * moment_one + (1.0 - beta_one) * grads
    moment_two = beta_two * moment_two + (1.0 - beta_two) * grads * grads
    first_hat = moment_one / (1.0 - beta_one**adam_count)
    second_hat = moment_two / (1.0 - beta_two**adam_count)
    update = first_hat / (jnp.sqrt(second_hat) + adam_eps) + decay_mask * params
    return (-step_rate * update, moment_one)


VEC = {}
_at = 0
for _name, _rows in (
    ("q_bias", 6), ("v_bias", 6), ("out_bias", 6), ("gain_one", 6), ("shift_one", 6), ("in_bias", 24),
    ("back_bias", 6), ("gain_two", 6), ("shift_two", 6), ("tables", 9),
):
    VEC[_name] = _at * LANES
    _at += _rows
VEC_ROWS = _at
NOTE_ROWS = 96
NBLOCK = 2 * LANES


def note_place(plan):
    row = plan.misc_start - (CORES * DEPTH * COLUMNS - 1) * plan.rows
    first = row // 16 * 16
    assert first + NOTE_ROWS <= plan.rows + HALO and row - first + VEC_ROWS <= NOTE_ROWS
    return first, row - first


def spread_notes(place, source, notes, sems):
    home = (place.column == COLUMNS - 1) & (place.core == CORES - 1)
    root = home & (place.z == DEPTH - 1)

    def copy(src, index, peer):
        return remote(src, notes, sems.at[0, index], sems.at[1, 0], peer)

    def arrived():
        copy(notes, 0, place.peer_core).wait_recv()

    @pl.when(root)
    def _():
        notes[...] = source[...]
        for index, peer in enumerate(place.peers_z):
            copy(source, index, peer).start()

    @pl.when(home & (place.z != DEPTH - 1))
    def _():
        arrived()

    @pl.when(home)
    def _():
        for index, peer in enumerate((place.peer_x, place.peer_y, place.peer_d)):
            copy(notes, 3 + index, peer).start()

    @pl.when((place.core == CORES - 1) & (place.column != COLUMNS - 1))
    def _():
        arrived()

    @pl.when(place.core == CORES - 1)
    def _():
        copy(notes, 6, place.peer_core).start()

    @pl.when(place.core != CORES - 1)
    def _():
        arrived()

    def finish():
        @pl.when(root)
        def _():
            for index, peer in enumerate(place.peers_z):
                copy(source, index, peer).wait_send()

        @pl.when(home)
        def _():
            for index, peer in enumerate((place.peer_x, place.peer_y, place.peer_d)):
                copy(notes, 3 + index, peer).wait_send()

        @pl.when(place.core == CORES - 1)
        def _():
            copy(notes, 6, place.peer_core).wait_send()

    return finish


def turns_table():
    count_freq = D // 8
    freq = np.exp(np.arange(count_freq) * (-math.log(1000.0) / count_freq)) / (2 * math.pi)
    per = np.concatenate([freq, freq])
    phase = np.concatenate([np.zeros(count_freq), np.full(count_freq, 0.25)])
    return np.stack([np.tile(per, 4), np.tile(phase, 4)]).astype(np.float32)


def sin_turns(t):
    t = t - jnp.floor(t + 0.5)
    a = jnp.abs(t)
    m = jnp.minimum(a, 0.5 - a) * (2 * math.pi)
    u = m * m
    poly = -1.0 / 39916800.0
    for term in (1.0 / 362880.0, -1.0 / 5040.0, 1.0 / 120.0, -1.0 / 6.0, 1.0):
        poly = poly * u + term
    s = m * poly
    return jnp.where(t < 0, -s, s)


def token_columns(boxes, lengths, window):
    coords = boxes[window].astype(F32)
    place = lax.broadcasted_iota(jnp.int32, (1, WINLEN), 1)
    doc = jnp.zeros((1, WINLEN), F32)
    anchor = jnp.zeros_like(coords)
    begin = 0
    for d in range(4):
        end = begin + lengths[window, d]
        mine = jnp.where((place >= begin) & (place < end), 1.0, 0.0)
        value = jnp.sum(coords * jnp.where(place == begin, 1.0, 0.0), axis=1, keepdims=True)
        anchor = anchor + value * mine
        doc = doc + mine * float(d)
        begin = end
    anchor = jnp.concatenate([anchor[0:2], anchor[0:2]], axis=0)
    relative = coords - anchor
    centre = jnp.floor((coords[0:2] + coords[2:4]) * 0.5)
    cell = jnp.floor(centre * (1.0 / coord_cell))
    rest = centre - cell * coord_cell
    rows = jnp.concatenate(
        [relative, cell, rest, doc, jnp.zeros((LANES - 9, WINLEN), F32)], axis=0
    )
    return rest, rows.T


def form_features(columns, turns_ref, features):
    lane = lax.broadcasted_iota(jnp.int32, (1, LANES), 1)
    for block in range(D // LANES):
        lanes = slice(block * LANES, (block + 1) * LANES)
        low, high = block * LANES // (D // 4), ((block + 1) * LANES - 1) // (D // 4)
        value = columns[:, low : low + 1]
        if high != low:
            value = jnp.where(
                lane + block * LANES < high * (D // 4), value, columns[:, high : high + 1]
            )
        t = value * turns_ref[0:1, lanes] + turns_ref[1:2, lanes]
        features[:, lanes] = sin_turns(t).astype(BF16)


def form_hots(columns, hot_ref, keyx_ref, keyy_ref, mkey, mquery):
    lane = lax.broadcasted_iota(jnp.int32, (1, LANES), 1)
    part = lane // BUCKETS
    cell = (lane % BUCKETS).astype(F32)
    is_x = jnp.where(columns[:, 4:5] == cell, 1.0, 0.0)
    is_y = jnp.where(columns[:, 5:6] == cell, 1.0, 0.0)
    hot_ref[...] = jnp.where(part % 2 == 0, is_x, is_y).astype(BF16)
    sign = jnp.where(part % 2 == 0, 1.0, -1.0)
    for odd in range(2):
        here = jnp.where(part // 2 == odd, sign, 0.0)
        keyx_ref[odd] = (is_x * here).astype(BF16)
        keyy_ref[odd] = (is_y * here).astype(BF16)
    doc = jnp.where(columns[:, 8:9] == lane.astype(F32), 1.0, 0.0)
    mkey[...] = doc.astype(BF16)
    mquery[...] = (jnp.where(lane < 4, 1.0 - doc, 0.0) * masked_score).astype(BF16)


def form_tables(tables, bands, tilted):
    row = lax.broadcasted_iota(jnp.int32, (LANES, 1), 0)
    half = BUCKETS // 2
    sub = lax.broadcasted_iota(jnp.int32, (8, LANES), 0)
    place = lax.broadcasted_iota(jnp.int32, (1, WIDE), 1)
    wanted = jnp.where(place < 5 * LANES, jnp.clip(place - 2 * LANES, -half, half - 1) + half, 0)
    lane = lax.broadcasted_iota(jnp.int32, (1, LANES), 1)
    turned = jnp.clip(64 - lane, -half, half - 1) + half
    for m in range(4):
        hot_band = jnp.where(row == wanted + m * BUCKETS, 1.0, 0.0).astype(BF16)
        got = matmul(tables, hot_band)
        for n in range(3):
            bands[4 * n + m] = got[n : n + 1, :]
        hot_turn = jnp.where(row == turned + m * BUCKETS, 1.0, 0.0).astype(BF16)
        got = matmul(tables, hot_turn)
        for t in (1, 2):
            for n in range(3):
                x = jnp.broadcast_to(got[3 * t + n : 3 * t + n + 1, :], (8, LANES))
                for bit in (1, 2, 4):
                    x = jnp.where((sub & bit) != 0, pltpu.roll(x, bit, 1), x)
                for group in range(BUCKETS // 8):
                    y = x if group == 0 else pltpu.roll(x, 8 * group, 1)
                    tilted[(t - 1) * HEADS + 4 * n + m, 8 * group : 8 * group + 8, :] = y


def pair_rows(tilted, pair):
    lane = lax.broadcasted_iota(jnp.int32, (1, LANES), 1)
    part = lane // BUCKETS
    x0, x1 = tilted[2 * pair], tilted[2 * pair + 1]
    y0, y1 = tilted[HEADS + 2 * pair], tilted[HEADS + 2 * pair + 1]

    def same(value, to):
        return value if to == 64 else pltpu.roll(value, (to - 64) % LANES, 1)

    def less(value, to):
        return pltpu.roll(value, (to - 65) % LANES, 1)

    zero = jnp.zeros_like(x0)
    base_x = jnp.where(part == 0, same(x1, 0), jnp.where(part == 2, same(x0, 64), zero))
    base_y = jnp.where(part == 1, same(y1, 32), jnp.where(part == 3, same(y0, 96), zero))

    def steps(even, odd):
        return jnp.where(
            part < 2,
            jnp.where(part == 0, less(even, 0), same(even, 32)),
            jnp.where(part == 2, less(odd, 64), same(odd, 96)),
        )

    rows = [
        jnp.concatenate([base_x, base_y], axis=0),
        jnp.concatenate([steps(x0, x1), zero], axis=0),
        jnp.concatenate([zero, steps(y0, y1)], axis=0),
    ]
    return jnp.concatenate(rows, axis=1).astype(BF16)


def gelu_and_slope(z):
    a = jnp.abs(z)
    t = 1.0 / (1.0 + (0.3275911 / math.sqrt(2.0)) * a)
    poly = 1.061405429 * 0.5
    for term in (-1.453152027, 1.421413741, -0.284496736, 0.254829592):
        poly = poly * t + 0.5 * term
    e = jnp.exp(-0.5 * z * z)
    tail = poly * t * e
    cdf = jnp.where(z < 0, tail, 1.0 - tail)
    return z * cdf, cdf + z * (e * (1.0 / math.sqrt(2.0 * math.pi)))


def forward_kernel(plan, params_in, hidden_in, cot_in, boxes, lengths, turns, *refs):
    (w_qkv_out, w_out_out, w_in_out, w_back_out, features_out, low_out, q_out, k_out, v_out, probs_out,
     context_out, hat_out, normed_out, active_out, slope_out, second_out, vec_out, rstd_out, gain_grads,
     output_ref, cot_ref, hot_out, rest_out, share_out) = refs[:24]
    refs = refs[24:]
    (flat, extended, own, note_source, halo, w_qkv, w_out, w_box, w_in, w_back, notes, features, hidden, start, start_low, q_ref,
     k_ref, v_ref, hot_ref, key_x, key_y, less_x, less_y, bands, tilted, met, kaug, qaug, wide, scores,
     probs, context_t, pair_t, hat, active, slope, vec) = refs[:37]
    note_sems, swap_sems, copy_sems, probs_sems, halo_sems = refs[37:42]
    place = Place()
    normed_low = hidden
    context = features
    gathering = Gathering(place, flat, dict(zip(GATHER_SEMS, refs[42:])))
    matrices = (w_qkv, w_out, w_box, w_in, w_back)
    written = []

    def write_out(src, dst):
        copy = pltpu.make_async_copy(src, dst, copy_sems.at[len(written)])
        copy.start()
        written.append(copy)

    own_rows = slice(HALO, HALO + plan.rows)
    fetch = pltpu.make_async_copy(params_in, extended.at[own_rows], halo_sems.at[0, 2])
    fetch.start()
    place.greet()
    fetch.wait()
    halo[0] = extended[HALO : 2 * HALO, :].astype(BF16)
    halo[1] = extended[plan.rows : plan.rows + HALO, :].astype(BF16)
    halos = Halo(place, halo, halo_sems)
    halos.send()
    note_first, note_row = note_place(plan)
    note_source[...] = extended[HALO + note_first : HALO + note_first + NOTE_ROWS, :].astype(BF16)

    quarter = WINLEN // DEPTH

    def exchange(source, target, kind):
        rows = pl.ds(pl.multiple_of(place.z * quarter, quarter), quarter)
        for d in range(DEPTH - 1):
            gathering_send(source.at[place.far[d]], target.at[rows], kind, d, place.peers_z[d])

    def gathering_send(src, dst, kind, d, peer):
        copy = remote(src, dst, swap_sems.at[kind, 0, d], swap_sems.at[kind, 1, d], peer)
        copy.start()
        gathering.sent.append(copy)

    def exchanged(target, kind):
        for d in range(DEPTH - 1):
            rows = pl.ds(pl.multiple_of(place.from_far[d] * quarter, quarter), quarter)
            remote(
                target.at[rows], target.at[rows], swap_sems.at[kind, 0, d], swap_sems.at[kind, 1, d],
                place.peer_x,
            ).wait_recv()

    exchange(hidden_in, hidden, 0)
    finish_notes = spread_notes(place, note_source, notes, note_sems)
    own_places = pl.ds(pl.multiple_of(place.z * quarter, quarter), quarter)
    own_hidden = pltpu.make_async_copy(
        hidden_in.at[place.z], hidden.at[own_places], swap_sems.at[0, 0, DEPTH - 1]
    )
    own_hidden.start()
    own_cot = pltpu.make_async_copy(
        cot_in.at[place.z], cot_ref.at[own_places], swap_sems.at[1, 0, DEPTH - 1]
    )
    own_cot.start()
    halos.arrived()
    extended[:HALO, :] = halo[2].astype(F32)
    extended[HALO + plan.rows :, :] = halo[3].astype(F32)
    form_tiles(plan, place, extended, own)
    gathering.spread(own)
    rest, columns = token_columns(boxes, lengths, place.z)
    for part in range(BLOCKS):
        rows = slice(part * LANES, (part + 1) * LANES)
        for axis, less in ((0, less_x), (1, less_y)):
            less[rows, :] = jnp.where(
                rest[axis : axis + 1, :] < columns[rows, 6 + axis : 7 + axis], 1.0, 0.0
            ).astype(BF16)
    rest_out[...] = rest
    form_hots(columns, hot_ref, key_x, key_y, kaug.at[:, LANES:], qaug.at[:, LANES:])
    hot_out[...] = hot_ref[...]
    gathering.spread_done()
    gathering.along_z(0)
    gathering.along_z(1)

    form_features(columns, turns, features)
    for n in range(D // LANES):
        rows = slice(n * LANES, (n + 1) * LANES)
        context_t[rows, :] = features[:, rows].T
    write_out(context_t, features_out)
    for row in range(VEC_ROWS):
        at = note_row + row
        vec[0:1, row * LANES : (row + 1) * LANES] = notes[at // 16 * 16 : at // 16 * 16 + 16, :].astype(
            F32
        )[at % 16 : at % 16 + 1, :]
    vec_out[...] = vec[...]
    table_row = note_row + VEC["tables"] // LANES
    assert table_row % 16 == 0
    form_tables(notes[table_row : table_row + 16, :], bands, tilted)

    gathering.first(0)
    gathering.along_z(2)
    gathering.first(1)
    gathering.along_z(3)
    exchange(cot_in, cot_ref, 1)
    gathering.second(0)
    gathering.second(1)
    gathering.first(2)
    gathering.third(0)
    gathering.complete(0)
    form_matrices(plan, flat, matrices, 0)
    gathering.third(1)
    gathering.first(3)
    gathering.complete(1)
    form_matrices(plan, flat, matrices, 1)
    write_out(w_qkv, w_qkv_out)
    write_out(w_out, w_out_out)

    exchanged(hidden, 0)
    own_hidden.wait()
    for n in range(D // NBLOCK):
        lanes = slice(n * NBLOCK, (n + 1) * NBLOCK)
        value = hidden[:, lanes].astype(F32) + matmul(features[...], w_box[:, lanes])
        start[:, lanes] = value
        start_low[:, lanes] = value.astype(BF16)
    write_out(start_low, low_out)
    written[0].wait()

    def project(n, carry):
        at = pl.multiple_of(n * NBLOCK, NBLOCK)
        lanes = pl.ds(at, NBLOCK)
        low = start_low[...]
        bias = vec[0:1, pl.ds(pl.multiple_of(VEC["q_bias"] + at, LANES), NBLOCK)]
        got = matmul(low, w_qkv[:, lanes]) + bias
        q_ref[:, lanes] = (got.astype(BF16).astype(F32) * HEAD_DIM ** (-0.5)).astype(BF16)
        k_ref[:, lanes] = matmul(low, w_qkv[:, pl.ds(pl.multiple_of(at + D, LANES), NBLOCK)]).astype(BF16)
        bias = vec[0:1, pl.ds(pl.multiple_of(VEC["v_bias"] + at, LANES), NBLOCK)]
        got = matmul(low, w_qkv[:, pl.ds(pl.multiple_of(at + 2 * D, LANES), NBLOCK)]) + bias
        v_ref[:, lanes] = got.astype(BF16)
        return carry

    lax.fori_loop(0, D // NBLOCK, project, 0)
    write_out(q_ref, q_out)
    write_out(k_ref, k_out)
    write_out(v_ref, v_out)
    gathering.second(2)

    low, high = half_masks()
    half = 2 * LANES

    def probs_copy(head, odd):
        return pltpu.make_async_copy(probs.at[odd], probs_out.at[head], probs_sems.at[odd])

    def one_pair(pair, carry):
        at = pl.multiple_of(pair * LANES, LANES)
        lanes = pl.ds(at, LANES)
        values_t = v_ref[:, lanes].T
        met[...] = matmul(hot_ref[:, :64], pair_rows(tilted, pair)).astype(BF16)
        for odd in range(2):
            mine, other = (low, high) if odd == 0 else (high, low)
            head = 2 * pair + odd
            kaug[:, :LANES] = k_ref[:, lanes] * mine + hot_ref[...] * other
            qaug[:, :LANES] = q_ref[:, lanes] * mine + met[:, :LANES] * other
            skew_band(bands[head], wide)

            @pl.when(pair > 0)
            def _():
                probs_copy(head, odd).wait()

            for side in range(2):
                cols = slice(side * half, (side + 1) * half)
                whole = times_transposed(kaug[...], qaug[cols, :])
                steps_x = times_transposed(key_x[odd], met[cols, LANES : 2 * LANES])
                steps_y = times_transposed(key_y[odd], met[cols, 2 * LANES :])
                top = None
                for part in range(BLOCKS):
                    rows = slice(part * LANES, (part + 1) * LANES)
                    bias = []
                    for block in range(2 * side, 2 * side + 2):
                        step = max(-2, min(2, block - part)) + 2
                        bias.append(wide[:, step * LANES : (step + 1) * LANES])
                    s = whole[rows] + jnp.concatenate(bias, axis=1)
                    s = s + steps_x[rows] * less_x[rows, cols].astype(F32)
                    s = s + steps_y[rows] * less_y[rows, cols].astype(F32)
                    scores[rows, :] = s
                    best = jnp.max(s, axis=0, keepdims=True)
                    top = best if top is None else jnp.maximum(top, best)
                total = None
                for part in range(BLOCKS):
                    rows = slice(part * LANES, (part + 1) * LANES)
                    e = jnp.exp(scores[rows, :] - top)
                    probs[odd, rows, cols] = e.astype(BF16)
                    add = jnp.sum(e, axis=0, keepdims=True)
                    total = add if total is None else total + add
                share = 1.0 / total
                share_out[head, :, cols] = share
                got = matmul(values_t[odd * HEAD_DIM : (odd + 1) * HEAD_DIM, :], probs[odd, :, cols])
                pair_t[odd * HEAD_DIM : (odd + 1) * HEAD_DIM, cols] = got * share
            probs_copy(head, odd).start()
        both = pair_t[...]
        context_t[lanes, :] = both.astype(BF16)
        context[:, lanes] = both.T.astype(BF16)
        return carry

    lax.fori_loop(0, 2, one_pair, 0)
    gathering.third(2)
    gathering.second(3)
    lax.fori_loop(2, 4, one_pair, 0)
    gathering.third(3)
    gathering.complete(2)
    form_matrices(plan, flat, matrices, 2)
    write_out(w_in, w_in_out)
    lax.fori_loop(4, PAIRS, one_pair, 0)
    write_out(context_t, context_out)
    gathering.complete(3)
    form_matrices(plan, flat, matrices, 3)
    write_out(w_back, w_back_out)

    def vector(name):
        return vec[0:1, VEC[name] : VEC[name] + D]

    for n in range(D // NBLOCK):
        lanes = slice(n * NBLOCK, (n + 1) * NBLOCK)
        bias = vec[0:1, VEC["out_bias"] + n * NBLOCK : VEC["out_bias"] + (n + 1) * NBLOCK]
        start[:, lanes] = start[:, lanes] + matmul(context[...], w_out[:, lanes]) + bias

    step_rows = 64

    def norm_first(n, carry):
        rows = pl.ds(pl.multiple_of(n * step_rows, step_rows), step_rows)
        x = start[rows, :]
        centred = x - jnp.mean(x, axis=1, keepdims=True)
        rstd = lax.rsqrt(jnp.mean(centred * centred, axis=1, keepdims=True) + norm_eps)
        xhat = centred * rstd
        hat[rows, :] = xhat
        rstd_out[rows, :] = jnp.broadcast_to(rstd, (step_rows, LANES))
        normed = xhat * vector("gain_one") + vector("shift_one")
        start[rows, :] = normed
        normed_low[rows, :] = normed.astype(BF16)
        return carry

    lax.fori_loop(0, WINLEN // step_rows, norm_first, 0)
    write_out(hat, hat_out)
    write_out(normed_low, normed_out)

    def widen(n, carry):
        at = pl.multiple_of(n * NBLOCK, NBLOCK)
        lanes = pl.ds(at, NBLOCK)
        bias = vec[0:1, pl.ds(pl.multiple_of(VEC["in_bias"] + at, LANES), NBLOCK)]
        value, change = gelu_and_slope(matmul(normed_low[...], w_in[:, lanes]) + bias)
        active[:, lanes] = value.astype(BF16)
        slope[:, lanes] = change.astype(BF16)
        return carry

    lax.fori_loop(0, FF // NBLOCK, widen, 0)
    write_out(active, active_out)
    write_out(slope, slope_out)
    for n in range(D // NBLOCK):
        lanes = slice(n * NBLOCK, (n + 1) * NBLOCK)
        bias = vec[0:1, VEC["back_bias"] + n * NBLOCK : VEC["back_bias"] + (n + 1) * NBLOCK]
        start[:, lanes] = start[:, lanes] + matmul(active[...], w_back[:, lanes]) + bias

    exchanged(cot_ref, 1)
    own_cot.wait()
    gain_grads[...] = jnp.zeros_like(gain_grads)

    def norm_second(n, carry):
        rows = pl.ds(pl.multiple_of(n * step_rows, step_rows), step_rows)
        x = start[rows, :]
        centred = x - jnp.mean(x, axis=1, keepdims=True)
        rstd = lax.rsqrt(jnp.mean(centred * centred, axis=1, keepdims=True) + norm_eps)
        xhat = centred * rstd
        output_ref[rows, :] = (xhat * vector("gain_two") + vector("shift_two")).astype(BF16)
        cot = cot_ref[rows, :].astype(F32)
        prod = cot * xhat
        gain_grads[0:1, :] = gain_grads[0:1, :] + jnp.sum(prod, axis=0, keepdims=True)
        gain_grads[1:2, :] = gain_grads[1:2, :] + jnp.sum(cot, axis=0, keepdims=True)
        gain = vector("gain_two")
        gc = cot * gain
        mean_one = jnp.mean(gc, axis=1, keepdims=True)
        mean_two = jnp.mean(prod * gain, axis=1, keepdims=True)
        second_out[rows, :] = rstd * (gc - mean_one - xhat * mean_two)
        return carry

    lax.fori_loop(0, WINLEN // step_rows, norm_second, 0)
    for odd in range(2):
        probs_copy(0, odd).wait()
    for copy in written[1:]:
        copy.wait()
    finish_notes()
    halos.sent()
    gathering.finish()


def forward_pass(plan, params, hidden_in, cotangent, boxes, lengths):
    anywhere = pl.BlockSpec(memory_space=pl.ANY)
    vmem = pl.BlockSpec(memory_space=pltpu.VMEM)
    token = (WINLEN, D)

    def hbm(shape, dtype=BF16):
        return jax.ShapeDtypeStruct(shape, dtype), anywhere

    def near(shape, dtype=F32):
        return jax.ShapeDtypeStruct(shape, dtype), vmem

    outs = [
        hbm(MATRICES[0]), hbm(MATRICES[1]), hbm(MATRICES[3]), hbm(MATRICES[4]), hbm((D, WINLEN)), hbm(token),
        hbm(token), hbm(token), hbm(token), hbm((HEADS, WINLEN, WINLEN)), hbm((D, WINLEN)),
        hbm(token, F32), hbm(token), hbm((WINLEN, FF)), hbm((WINLEN, FF)), near(token),
        near((1, VEC_ROWS * LANES)), near((WINLEN, LANES)), near((2, D)), near(token, BF16),
        near(token, BF16), near((WINLEN, LANES), BF16), near((2, WINLEN)),
        near((HEADS, 1, WINLEN)),
    ]
    scratch = [
        pltpu.VMEM((COLUMNS, CORES, DEPTH, COLUMNS, plan.quarter, LANES), BF16),
        pltpu.VMEM((plan.rows + 2 * HALO, LANES), F32),
        pltpu.VMEM((COLUMNS, plan.quarter, LANES), BF16),
        pltpu.VMEM((NOTE_ROWS, LANES), BF16),
        pltpu.VMEM((4, HALO, LANES), BF16),
    ]
    scratch += [pltpu.VMEM(layout, BF16) for layout in MATRICES]
    scratch += [
        pltpu.VMEM((NOTE_ROWS, LANES), BF16),
        pltpu.VMEM(token, BF16),
        pltpu.VMEM(token, BF16),
        pltpu.VMEM(token, F32),
        pltpu.VMEM(token, BF16),
        pltpu.VMEM(token, BF16),
        pltpu.VMEM(token, BF16),
        pltpu.VMEM(token, BF16),
        pltpu.VMEM((WINLEN, LANES), BF16),
        pltpu.VMEM((2, WINLEN, LANES), BF16),
        pltpu.VMEM((2, WINLEN, LANES), BF16),
        pltpu.VMEM((WINLEN, WINLEN), BF16),
        pltpu.VMEM((WINLEN, WINLEN), BF16),
        pltpu.VMEM((HEADS, 1, WIDE), F32),
        pltpu.VMEM((2 * HEADS, BUCKETS, LANES), F32),
        pltpu.VMEM((WINLEN, 3 * LANES), BF16),
        pltpu.VMEM((WINLEN, 2 * LANES), BF16),
        pltpu.VMEM((WINLEN, 2 * LANES), BF16),
        pltpu.VMEM((LANES, 5 * LANES), F32),
        pltpu.VMEM((WINLEN, 2 * LANES), F32),
        pltpu.VMEM((2, WINLEN, WINLEN), BF16),
        pltpu.VMEM((D, WINLEN), BF16),
        pltpu.VMEM((LANES, WINLEN), F32),
        pltpu.VMEM(token, F32),
        pltpu.VMEM((WINLEN, FF), BF16),
        pltpu.VMEM((WINLEN, FF), BF16),
        pltpu.VMEM((1, VEC_ROWS * LANES), F32),
        pltpu.SemaphoreType.DMA((2, 7)),
        pltpu.SemaphoreType.DMA((2, 2, DEPTH)),
        pltpu.SemaphoreType.DMA((16,)),
        pltpu.SemaphoreType.DMA((2,)),
        pltpu.SemaphoreType.DMA((2, 3)),
    ]
    return pl.pallas_call(
        functools.partial(forward_kernel, plan),
        out_shape=[shape for shape, _ in outs],
        in_specs=[anywhere] * 3 + [vmem, pl.BlockSpec(memory_space=pltpu.SMEM), vmem],
        out_specs=[spec for _, spec in outs],
        scratch_shapes=scratch + sem_shapes(GATHER_SEMS),
        compiler_params=pltpu.CompilerParams(
            collective_id=0, has_side_effects=True, vmem_limit_bytes=62 * 2**20
        ),
        name="forward_pass",
    )(params, hidden_in, cotangent, boxes, lengths, jnp.asarray(turns_table()))


class Reducing:
    def __init__(self, place, flat, swapped, one, two, deep, piece, result, sems, free):
        self.place = place
        self.flat = flat
        self.swapped = swapped
        self.one = one
        self.two = two
        self.deep = deep
        self.piece = piece
        self.result = result
        self.sems = sems
        self.free = free
        self.sent = {k: [] for k in range(COLUMNS)}

    def send(self, k, src, dst, kind, index, peer):
        copy = remote(src, dst, self.sems[kind].at[0, index], self.sems[kind].at[1, index], peer)
        copy.start()
        self.sent[k].append(copy)

    got = Gathering.got

    def settle(self, k):
        for copy in self.sent.pop(k):
            copy.wait_send()

    def swap(self, k):
        p = self.place
        slot = k % 2
        if k < 2:
            pl.semaphore_wait(self.free.at[slot], 1)
        self.send(k, self.flat.at[k, 1 - p.core], self.swapped.at[slot], "core", k, p.peer_core)

    def first(self, k):
        p = self.place
        slot = k % 2
        self.got(self.swapped.at[slot], "core", k)

        def one(step, carry):
            z, quarter = step // COLUMNS, step % COLUMNS
            total = self.flat[k, p.core, z, quarter].astype(F32)
            total = total + self.swapped[slot, z, quarter].astype(F32)
            self.flat[k, p.core, z, quarter] = total.astype(BF16)
            return carry

        lax.fori_loop(0, DEPTH * COLUMNS, one, 0)
        flat = self.flat
        self.send(k, flat.at[k, p.core, 0:2, p.col_d], self.one.at[k, 0], "one", 2 * k, p.peer_y)
        self.send(k, flat.at[k, p.core, 2:4, p.col_d], self.one.at[k, 1], "one", 2 * k + 1, p.peer_x)
        if k >= 2:
            pl.semaphore_signal(
                self.free.at[slot], inc=1, device_id=p.peer_core, device_id_type=MESH
            )

    def second(self, k):
        p = self.place
        for side, column in ((0, p.col_x), (1, p.col_y)):
            self.got(self.one.at[k, side], "one", 2 * k + side)

            def one(step, carry, side=side, column=column):
                z = 2 * side + step
                total = self.flat[k, p.core, z, column].astype(F32)
                total = total + self.one[k, side, step].astype(F32)
                self.flat[k, p.core, z, column] = total.astype(BF16)
                return carry

            lax.fori_loop(0, 2, one, 0)
        flat = self.flat
        self.send(k, flat.at[k, p.core, :, p.col_x], self.two.at[k, 0], "two", 2 * k, p.peer_x)
        self.send(k, flat.at[k, p.core, :, p.col_y], self.two.at[k, 1], "two", 2 * k + 1, p.peer_y)

    def third(self, k):
        p = self.place
        for side in range(2):
            self.got(self.two.at[k, side], "two", 2 * k + side)

        def one(z, carry):
            total = self.flat[k, p.core, z, p.column].astype(F32)
            total = total + self.two[k, 0, z].astype(F32) + self.two[k, 1, z].astype(F32)
            self.flat[k, p.core, z, p.column] = total.astype(BF16)
            return carry

        lax.fori_loop(0, DEPTH, one, 0)
        for d in range(DEPTH - 1):
            self.send(
                k, self.flat.at[k, p.core, p.far[d], p.column], self.deep.at[k, d], "z", 3 * k + d,
                p.peers_z[d],
            )

    def fourth(self, k):
        p = self.place
        for d in range(DEPTH - 1):
            self.got(self.deep.at[k, d], "z", 3 * k + d)
        total = self.flat[k, p.core, p.z, p.column].astype(F32)
        for d in range(DEPTH - 1):
            total = total + self.deep[k, d].astype(F32)
        self.piece[k] = total.astype(BF16)

    def giving(self, k):
        p = self.place
        sems = self.sems["spread"]
        return remote(
            self.piece.at[k], self.result.at[p.column], sems.at[0, k], sems.at[1, p.column],
            p.at(k, p.core, p.z),
        )

    def give(self, k):
        @pl.when(self.place.column != k)
        def _():
            self.giving(k).start()

    def given(self, k):
        @pl.when(self.place.column != k)
        def _():
            self.giving(k).wait_send()

    def receive(self):
        p = self.place
        self.result[p.column] = self.piece[p.column]
        for column in (p.col_x, p.col_y, p.col_d):
            self.got(self.result.at[column], "spread", column)


REDUCE_SEMS = {"spread": 4, "z": 12, "one": 8, "two": 8, "core": 4}


class Notes:
    def __init__(self, place, notes, slots, sems):
        self.place, self.notes, self.slots, self.sems = place, notes, slots, sems
        p = place
        self.home = (p.column == COLUMNS - 1) & (p.core == CORES - 1)
        self.root = self.home & (p.z == DEPTH - 1)

    def copy(self, slot, peer):
        return remote(
            self.notes, self.slots.at[slot], self.sems.at[0, 0], self.sems.at[1, slot], peer
        )

    def take(self, slot):
        self.copy(slot, self.place.peer_core).wait_recv()
        self.notes[...] = self.notes[...] + self.slots[slot]

    def start(self):
        p = self.place

        @pl.when(p.core != CORES - 1)
        def _():
            self.copy(0, p.peer_core).start()

    def rise(self):
        p = self.place

        @pl.when(p.core == CORES - 1)
        def _():
            self.take(0)

        @pl.when((p.core == CORES - 1) & (p.column != COLUMNS - 1))
        def _():
            self.copy(1 + p.column, p.at(COLUMNS - 1, p.core, p.z)).start()

    def end(self):
        p = self.place

        @pl.when(self.home)
        def _():
            for slot in range(1, 4):
                self.take(slot)

        @pl.when(self.home & (p.z != DEPTH - 1))
        def _():
            self.copy(4 + p.z, p.at(p.column, p.core, DEPTH - 1)).start()

        @pl.when(self.root)
        def _():
            for slot in range(4, 7):
                self.take(slot)

        @pl.when(jnp.logical_not(self.root))
        def _():
            self.copy(0, p.peer_core).wait_send()


def cell_sums(whole, less, odd):
    lane = lax.broadcasted_iota(jnp.int32, (1, LANES), 1)
    sub = lax.broadcasted_iota(jnp.int32, (8, LANES), 0)
    sums = []
    for axis in range(2):
        rows = slice(axis * BUCKETS, (axis + 1) * BUCKETS)
        start = axis * BUCKETS + (0 if odd else 64)
        every = pltpu.roll(whole[rows], (BUCKETS - start) % LANES, 1)
        below = pltpu.roll(less[rows], (BUCKETS - axis * BUCKETS) % LANES, 1)
        inside = (lane >= BUCKETS) & (lane < 2 * BUCKETS)
        every = jnp.where(inside, every, 0.0)
        below = jnp.where(inside, below, 0.0)
        x = every - below + pltpu.roll(below, LANES - 1, 1)
        total = None
        for group in range(BUCKETS // 8):
            y = x[8 * group : 8 * group + 8]
            y = y if group == 0 else pltpu.roll(y, LANES - 8 * group, 1)
            total = y if total is None else total + y
        for bit in (1, 2, 4):
            total = jnp.where((sub & bit) != 0, pltpu.roll(total, LANES - bit, 1), total)
        sums.append(jnp.sum(total, axis=0, keepdims=True))
    return sums


def exact_dot(a, b):
    return jnp.dot(a, b, preferred_element_type=F32, precision=lax.Precision.HIGHEST)


def bucket_rows(cell_ref, diag_ref):
    half = BUCKETS // 2
    column = lax.broadcasted_iota(jnp.int32, (1, LANES), 1)
    row = lax.broadcasted_iota(jnp.int32, (LANES, 1), 0)
    to = jnp.clip(row - BUCKETS, -half, half - 1) + half
    place = lax.broadcasted_iota(jnp.int32, (WIDE, 1), 0)
    along = place - LANES
    far = jnp.where(place < LANES, 0, jnp.where(place < 5 * LANES, 0, BUCKETS - 1))
    along = jnp.where(
        (place >= LANES) & (place < 4 * LANES),
        jnp.clip(along - LANES, -half, half - 1) + half,
        far,
    )
    first, rest = None, None
    zero = jnp.zeros((5, WIDE), F32)
    for m in range(4):
        hot_along = jnp.where(along + m * BUCKETS == column, 1.0, 0.0)
        got = exact_dot(
            jnp.concatenate([diag_ref[4 * n + m] for n in range(3)] + [zero], axis=0), hot_along
        )
        first = got if first is None else first + got
        hot_cell = jnp.where(to + m * BUCKETS == column, 1.0, 0.0)
        rows = [cell_ref[t * HEADS + 4 * n + m] for t in range(2) for n in range(3)]
        got = exact_dot(jnp.concatenate(rows + [zero[:2, :LANES]], axis=0), hot_cell)
        rest = got if rest is None else rest + got
    return jnp.concatenate([first[:3], rest[:6]], axis=0)


def backward_kernel(
    plan, active_in, slope_in, w_back_in, w_in_in, w_out_in, w_qkv_in, normed_in, low_in, features_in,
    context_in, q_in, k_in, v_in, probs_in, hat_in, second_in, rstd_ref, vec, gain_two, hot_ref, rest_ref,
    share_ref, output_in, *refs,
):
    out, output_pos, hidden_pos = refs[:3]
    (flat, extended, halo, swapped, one_buf, two_buf, deep, piece, result, active, slope, w_back, w_in, w_out,
     turned, context_t, q_ref, k_ref, v_ref, hat, second, branch, dctx, probs, less_x,
     less_y, dscores, dscores_x, dscores_y, band, hot_t, qaug, pair_t, scaled, share_cols, vecg, cell_rows, diag_rows, notes, slots,
     ) = refs[3:43]
    load_sems, probs_sems, free, pos_sems, note_sems, halo_sems = refs[43:49]
    place = Place()
    reducing = Reducing(
        place, flat, swapped, one_buf, two_buf, deep, piece, result,
        dict(zip(REDUCE_SEMS, refs[49:])), free,
    )
    climbing = Notes(place, notes, slots, note_sems)
    loads = {}

    def load(name, src, dst):
        loads[name] = pltpu.make_async_copy(src, dst, load_sems.at[len(loads)])
        loads[name].start()

    mixed = active.at[:, : 3 * D]
    grad_attn = branch
    w_qkv = w_in.at[:, : 3 * D]
    hidden_low = dctx
    scores = hat.at[:, :WINLEN]

    load("second", second_in, second)
    load("active", active_in, active)

    extended[...] = jnp.zeros_like(extended)
    place.greet()

    quarter = WINLEN // DEPTH
    positions = []

    def to_pos(source, target, kind):
        for d in range(DEPTH - 1):
            rows = pl.ds(pl.multiple_of(place.far[d] * quarter, quarter), quarter)
            copy = remote(
                source.at[rows], target.at[place.z], pos_sems.at[kind, 0, d], pos_sems.at[kind, 1, d],
                place.peers_z[d],
            )
            copy.start()
            positions.append(copy)
        rows = pl.ds(pl.multiple_of(place.z * quarter, quarter), quarter)
        copy = pltpu.make_async_copy(
            source.at[rows], target.at[place.z], pos_sems.at[kind, 0, DEPTH - 1]
        )
        copy.start()
        return copy

    def in_pos(target, kind):
        for d in range(DEPTH - 1):
            there = target.at[place.from_far[d]]
            remote(
                there, there, pos_sems.at[kind, 0, d], pos_sems.at[kind, 1, d], place.peer_x
            ).wait_recv()

    own_output = to_pos(output_in, output_pos, 0)

    tiles = flat.reshape(-1, LANES)

    def store(index, row, value, first_block=0, column=None):
        blocks = MATRICES[index][1] // LANES
        value = value.astype(BF16)
        for group in range(value.shape[0] // 16):
            first = plan.tile_starts[index] + (row // 16 + group) * blocks
            k = first // COLUMN_TILES if column is None else column
            base = 16 * (first + first_block) + plan.pad * k
            for block in range(value.shape[1] // LANES):
                tiles[pl.ds(pl.multiple_of(base + 16 * block, 16), 16), :] = value[
                    16 * group : 16 * group + 16, block * LANES : (block + 1) * LANES
                ]

    def column_sum(value):
        return jnp.sum(value, axis=0, keepdims=True)

    def keep_vector(name, lanes_at, value):
        at = pl.multiple_of(VEC[name] + lanes_at, LANES)
        vecg[0:1, pl.ds(at, value.shape[1])] = value

    loads["second"].wait()
    for n in range(D // NBLOCK):
        lanes = slice(n * NBLOCK, (n + 1) * NBLOCK)
        value = second[:, lanes].astype(BF16)
        branch[:, lanes] = value
        keep_vector("back_bias", n * NBLOCK, column_sum(value.astype(F32)))
    loads["active"].wait()
    load("slope", slope_in, slope)
    load("w_back", w_back_in, w_back)
    load("normed", normed_in, dctx)

    def back_rows(row, column):
        turned[:WINLEN, :] = active[:, pl.ds(row, WINLEN)].T
        store(4, row, matmul(turned[:WINLEN, :], branch[...]), column=column)

    def far_rows(n, carry):
        back_rows(pl.multiple_of(n * WINLEN, WINLEN), COLUMNS - 1)
        return carry

    lax.fori_loop(2, FF // WINLEN, far_rows, 0)
    back_rows(WINLEN, None)
    reducing.swap(3)
    back_rows(0, None)
    loads["w_back"].wait()
    loads["slope"].wait()
    load("w_in", w_in_in, w_in)
    load("hat", hat_in, hat)
    load("w_out", w_out_in, w_out)

    def inner(n, carry):
        at = pl.multiple_of(n * NBLOCK, NBLOCK)
        lanes = pl.ds(at, NBLOCK)
        value = times_transposed(branch[...], w_back[lanes, :]) * slope[:, lanes].astype(F32)
        value = value.astype(BF16)
        slope[:, lanes] = value
        keep_vector("in_bias", at, column_sum(value.astype(F32)))
        return carry

    lax.fori_loop(0, FF // NBLOCK, inner, 0)
    grad_inner = slope
    reducing.first(3)

    loads["normed"].wait()
    for n in range(D // NBLOCK):
        rows = slice(n * NBLOCK, (n + 1) * NBLOCK)
        turned[rows, :] = dctx[:, rows].T

    def in_rows(n, carry):
        lanes = pl.ds(pl.multiple_of(n * NBLOCK, NBLOCK), NBLOCK)
        store(3, 0, matmul(turned[...], grad_inner[:, lanes]), n * (NBLOCK // LANES))
        return carry

    lax.fori_loop(0, FF // NBLOCK, in_rows, 0)
    reducing.swap(2)
    reducing.second(3)

    loads["w_in"].wait()
    load("context", context_in, context_t)
    load("q", q_in, q_ref)
    load("k", k_in, k_ref)
    load("v", v_in, v_ref)
    for odd in range(2):
        pltpu.make_async_copy(probs_in.at[odd], probs.at[odd], probs_sems.at[odd]).start()
    for n in range(D // NBLOCK):
        lanes = slice(n * NBLOCK, (n + 1) * NBLOCK)
        second[:, lanes] = second[:, lanes] + times_transposed(grad_inner[...], w_in[lanes, :])
    load("w_qkv", w_qkv_in, w_qkv)
    reducing.first(2)

    loads["hat"].wait()
    step_rows = 64
    for name in ("gain_one", "shift_one", "out_bias"):
        keep_vector(name, 0, jnp.zeros((1, D), F32))

    def norm_first(n, carry):
        rows = pl.ds(pl.multiple_of(n * step_rows, step_rows), step_rows)
        grad = second[rows, :]
        xhat = hat[rows, :]
        prod = grad * xhat
        gain = vec[0:1, VEC["gain_one"] : VEC["gain_one"] + D]
        gc = grad * gain
        mean_one = jnp.mean(gc, axis=1, keepdims=True)
        mean_two = jnp.mean(prod * gain, axis=1, keepdims=True)
        value = rstd_ref[rows, 0:1] * (gc - mean_one - xhat * mean_two)
        second[rows, :] = value
        value = value.astype(BF16)
        grad_attn[rows, :] = value
        for name, term in (
            ("gain_one", prod), ("shift_one", grad), ("out_bias", value.astype(F32)),
        ):
            lanes = slice(VEC[name], VEC[name] + D)
            vecg[0:1, lanes] = vecg[0:1, lanes] + column_sum(term)
        return carry

    lax.fori_loop(0, WINLEN // step_rows, norm_first, 0)
    reducing.third(3)
    loads["w_out"].wait()
    for n in range(D // NBLOCK):
        lanes = slice(n * NBLOCK, (n + 1) * NBLOCK)
        dctx[:, lanes] = times_transposed(grad_attn[...], w_out[lanes, :]).astype(BF16)
    loads["context"].wait()
    reducing.second(2)
    for n in range(D // NBLOCK):
        lanes = slice(n * NBLOCK, (n + 1) * NBLOCK)
        store(1, 0, matmul(context_t[...], grad_attn[:, lanes]), n * (NBLOCK // LANES))
    load("low", low_in, branch)
    load("features", features_in, context_t)
    features_t = context_t
    reducing.fourth(3)
    reducing.give(3)

    low, high = half_masks()
    rest = rest_ref[...]
    columns = jnp.concatenate([rest, jnp.zeros((LANES - 2, WINLEN), F32)], axis=0).T
    for part in range(BLOCKS):
        rows = slice(part * LANES, (part + 1) * LANES)
        for axis, less in ((0, less_x), (1, less_y)):
            less[rows, :] = jnp.where(
                rest[axis : axis + 1, :] < columns[rows, axis : axis + 1], 1.0, 0.0
            ).astype(BF16)
    hot_t[...] = hot_ref[...].T
    lane = lax.broadcasted_iota(jnp.int32, (1, LANES), 1)
    scale = HEAD_DIM ** (-0.5)
    of_x = jnp.where((lane // BUCKETS) % 2 == 0, 1.0, 0.0)
    share_cols[...] = jnp.concatenate(
        [share_ref[head] for head in range(HEADS)] + [jnp.zeros((LANES - HEADS, WINLEN), F32)], axis=0
    ).T
    for name in ("q", "k", "v"):
        loads[name].wait()

    def probs_copy(head, odd):
        return pltpu.make_async_copy(probs_in.at[head], probs.at[odd], probs_sems.at[odd])

    def one_pair(pair, carry):
        at = pl.multiple_of(pair * LANES, LANES)
        lanes = pl.ds(at, LANES)
        keys_t = k_ref[:, lanes].T
        cells_x = hot_ref[...] * of_x.astype(BF16)
        cells_y = hot_ref[...] * (1.0 - of_x).astype(BF16)
        both = pltpu.roll(share_cols[...], lax.rem(LANES - 2 * pair, LANES), 1)
        both = jnp.where(lane < HEAD_DIM, both[:, 0:1], both[:, 1:2])
        scaled[...] = (dctx[:, lanes].astype(F32) * both).astype(BF16)
        for odd in range(2):
            mine, other = (low, high) if odd == 0 else (high, low)
            head = 2 * pair + odd
            probs_copy(head, odd).wait()
            qaug[...] = q_ref[:, lanes] * mine + hot_ref[...] * other
            grad_context = dctx[:, lanes]
            share = share_ref[head]
            products = times_transposed(v_ref[:, lanes] * mine, grad_context)
            dot = None
            for part in range(BLOCKS):
                rows = slice(part * LANES, (part + 1) * LANES)
                dp = products[rows]
                scores[rows, :] = dp
                add = column_sum(dp * probs[odd, rows, :].astype(F32))
                dot = add if dot is None else dot + add
            dot = dot * share
            band[...] = jnp.zeros_like(band)
            for part in range(BLOCKS):
                rows = slice(part * LANES, (part + 1) * LANES)
                ds = probs[odd, rows, :].astype(F32) * ((scores[rows, :] - dot) * share)
                for block in range(BLOCKS):
                    step = max(-2, min(2, block - part)) + 2
                    where = slice(step * LANES, (step + 1) * LANES)
                    band[:, where] = band[:, where] + ds[:, block * LANES : (block + 1) * LANES]
                ds = ds.astype(BF16)
                dscores[rows, :] = ds
                dscores_x[rows, :] = ds * less_x[rows, :]
                dscores_y[rows, :] = ds * less_y[rows, :]
            keys_cells = matmul(dscores[...], qaug[...])
            less = matmul(dscores_x[...], cells_x) + matmul(dscores_y[...], cells_y)
            values_grad = matmul(probs[odd], scaled[...])

            @pl.when(pair < PAIRS - 1)
            def _():
                probs_copy(head + 2, odd).start()

            pair_t[odd * HEAD_DIM : (odd + 1) * HEAD_DIM, :] = matmul(
                keys_t[odd * HEAD_DIM : (odd + 1) * HEAD_DIM, :], dscores[...]
            )
            diag_rows[head, :, LANES : 5 * LANES] = diagonal_sums(band)
            diag_rows[head, :, :LANES] = column_sum(band[:, :LANES])
            diag_rows[head, :, 5 * LANES :] = column_sum(band[:, 4 * LANES :])
            sums = []
            for summed in (keys_cells, less):
                first = summed.astype(BF16)
                remainder = (summed - first.astype(F32)).astype(BF16)
                sums.append(matmul(hot_t[:64, :], first) + matmul(hot_t[:64, :], remainder))
            for axis, value in enumerate(cell_sums(sums[0], sums[1], odd)):
                cell_rows[axis * HEADS + head] = value
            for which, value in ((1, keys_cells), (2, values_grad)):
                there = pl.ds(pl.multiple_of(at + which * D, LANES), LANES)
                value = value.astype(BF16)
                if odd:
                    value = mixed[:, there] * low + value * high
                mixed[:, there] = value
        value = (pair_t[...].T * scale).astype(BF16)
        mixed[:, lanes] = value
        keep_vector("q_bias", at, column_sum(value.astype(F32)))
        there = pl.ds(pl.multiple_of(at + 2 * D, LANES), LANES)
        keep_vector("v_bias", at, column_sum(mixed[:, there].astype(F32)))
        return carry

    lax.fori_loop(0, 2, one_pair, 0)
    reducing.third(2)
    lax.fori_loop(2, 4, one_pair, 0)
    reducing.fourth(2)
    reducing.give(2)
    lax.fori_loop(4, PAIRS, one_pair, 0)

    keep_vector("gain_two", 0, gain_two[0:1, :])
    keep_vector("shift_two", 0, gain_two[1:2, :])
    notes[...] = jnp.zeros_like(notes)
    table = VEC["tables"] // LANES
    for row in range(table):
        notes[row : row + 1, :] = vecg[0:1, row * LANES : (row + 1) * LANES]
    notes[table : table + 9, :] = bucket_rows(cell_rows, diag_rows)
    climbing.start()

    loads["w_qkv"].wait()
    for n in range(D // NBLOCK):
        lanes = slice(n * NBLOCK, (n + 1) * NBLOCK)
        value = second[:, lanes] + times_transposed(mixed[...], w_qkv[lanes, :])
        hidden_low[:, lanes] = value.astype(BF16)
    own_hidden = to_pos(hidden_low, hidden_pos, 1)
    loads["features"].wait()
    for n in range(D // NBLOCK):
        lanes = slice(n * NBLOCK, (n + 1) * NBLOCK)
        store(2, 0, matmul(features_t[...], hidden_low[:, lanes]), n * (NBLOCK // LANES))
    reducing.swap(1)
    climbing.rise()

    loads["low"].wait()
    for n in range(D // NBLOCK):
        rows = slice(n * NBLOCK, (n + 1) * NBLOCK)
        turned[rows, :] = branch[:, rows].T

    def qkv_rows(n, carry):
        lanes = pl.ds(pl.multiple_of(n * NBLOCK, NBLOCK), NBLOCK)
        store(0, 0, matmul(turned[...], mixed[:, lanes]), n * (NBLOCK // LANES))
        return carry

    lax.fori_loop(0, 3 * D // NBLOCK, qkv_rows, 0)
    reducing.swap(0)
    reducing.first(1)
    climbing.end()
    reducing.first(0)
    reducing.second(1)
    reducing.second(0)
    reducing.third(1)
    reducing.third(0)
    reducing.fourth(1)
    reducing.give(1)
    reducing.fourth(0)
    reducing.give(0)
    reducing.receive()
    spread_tiles(plan, place, result, extended)
    halo[0] = extended[:HALO, :].astype(BF16)
    halo[1] = extended[HALO + plan.rows :, :].astype(BF16)
    halos = Halo(place, halo, halo_sems)
    halos.send()
    note_first, note_row = note_place(plan)
    base = HALO + note_first + note_row

    @pl.when(climbing.root)
    def _():
        extended[base : base + MISC_ROWS, :] = notes[:MISC_ROWS, :]

    halos.arrived()
    low_rows, high_rows = slice(HALO, 2 * HALO), slice(plan.rows, plan.rows + HALO)

    @pl.when(place.index > 0)
    def _():
        extended[low_rows, :] = extended[low_rows, :] + halo[2].astype(F32)

    @pl.when(place.index < place.count - 1)
    def _():
        extended[high_rows, :] = extended[high_rows, :] + halo[3].astype(F32)

    out[...] = extended[HALO : HALO + plan.rows, :]
    in_pos(output_pos, 0)
    in_pos(hidden_pos, 1)
    own_output.wait()
    own_hidden.wait()
    for copy in positions:
        copy.wait_send()
    for k in range(COLUMNS):
        reducing.given(k)
        reducing.settle(k)
    halos.sent()


def backward_pass(plan, operands):
    anywhere = pl.BlockSpec(memory_space=pl.ANY)
    vmem = pl.BlockSpec(memory_space=pltpu.VMEM)
    token = (WINLEN, D)
    block = (plan.quarter, LANES)
    positions = jax.ShapeDtypeStruct((DEPTH, WINLEN // DEPTH, D), BF16)
    scratch = [
        pltpu.VMEM((COLUMNS, CORES, DEPTH, COLUMNS) + block, BF16),
        pltpu.VMEM((plan.rows + 2 * HALO, LANES), F32),
        pltpu.VMEM((4, HALO, LANES), BF16),
        pltpu.VMEM((2, DEPTH, COLUMNS) + block, BF16),
        pltpu.VMEM((COLUMNS, 2, 2) + block, BF16),
        pltpu.VMEM((COLUMNS, 2, DEPTH) + block, BF16),
        pltpu.VMEM((COLUMNS, DEPTH - 1) + block, BF16),
        pltpu.VMEM((COLUMNS,) + block, BF16),
        pltpu.VMEM((COLUMNS,) + block, BF16),
        pltpu.VMEM((WINLEN, FF), BF16),
        pltpu.VMEM((WINLEN, FF), BF16),
        pltpu.VMEM((FF, D), BF16),
        pltpu.VMEM((D, FF), BF16),
        pltpu.VMEM((D, D), BF16),
        pltpu.VMEM((D, WINLEN), BF16),
        pltpu.VMEM((D, WINLEN), BF16),
        pltpu.VMEM(token, BF16),
        pltpu.VMEM(token, BF16),
        pltpu.VMEM(token, BF16),
        pltpu.VMEM(token, F32),
        pltpu.VMEM(token, F32),
        pltpu.VMEM(token, BF16),
        pltpu.VMEM(token, BF16),
        pltpu.VMEM((2, WINLEN, WINLEN), BF16),
        pltpu.VMEM((WINLEN, WINLEN), BF16),
        pltpu.VMEM((WINLEN, WINLEN), BF16),
        pltpu.VMEM((WINLEN, WINLEN), BF16),
        pltpu.VMEM((WINLEN, WINLEN), BF16),
        pltpu.VMEM((WINLEN, WINLEN), BF16),
        pltpu.VMEM((LANES, 5 * LANES), F32),
        pltpu.VMEM((LANES, WINLEN), BF16),
        pltpu.VMEM((WINLEN, LANES), BF16),
        pltpu.VMEM((LANES, WINLEN), F32),
        pltpu.VMEM((WINLEN, LANES), BF16),
        pltpu.VMEM((WINLEN, LANES), F32),
        pltpu.VMEM((1, VEC_ROWS * LANES), F32),
        pltpu.VMEM((2 * HEADS, 1, LANES), F32),
        pltpu.VMEM((HEADS, 1, WIDE), F32),
        pltpu.VMEM((NOTE_ROWS, LANES), F32),
        pltpu.VMEM((7, NOTE_ROWS, LANES), F32),
        pltpu.SemaphoreType.DMA((16,)),
        pltpu.SemaphoreType.DMA((2,)),
        pltpu.SemaphoreType.REGULAR((2,)),
        pltpu.SemaphoreType.DMA((2, 2, DEPTH)),
        pltpu.SemaphoreType.DMA((2, 7)),
        pltpu.SemaphoreType.DMA((2, 3)),
    ]
    return pl.pallas_call(
        functools.partial(backward_kernel, plan),
        out_shape=[jax.ShapeDtypeStruct((plan.rows, LANES), F32), positions, positions],
        in_specs=[anywhere] * 16 + [vmem] * 6 + [anywhere],
        out_specs=[vmem, anywhere, anywhere],
        scratch_shapes=scratch + sem_shapes(REDUCE_SEMS),
        compiler_params=pltpu.CompilerParams(
            collective_id=1, has_side_effects=True, vmem_limit_bytes=62 * 2**20
        ),
        name="backward_pass",
    )(*operands)


def fast_shards(hidden_in, cotangent, box_coords, doc_lengths, params, moment_one, moment_two):
    plan = Plan(params.shape[0])
    (proj_qkv, proj_out, proj_in, proj_back, features_t, start_low, queries, keys, values, probs, context_t,
     xhat, normed_low, active, slope, grad_second, vec, rstd, grad_norm_two, output, _, hot_two,
     rest_rows, share) = forward_pass(
        plan, params.reshape(plan.rows, LANES), hidden_in, cotangent,
        jnp.transpose(box_coords, (0, 2, 1)), doc_lengths,
    )
    summed, output_low, grad_hidden = backward_pass(
        plan,
        (active, slope, proj_back, proj_in, proj_out, proj_qkv, normed_low, start_low, features_t, context_t,
         queries, keys, values, probs, xhat, grad_second, rstd, vec, grad_norm_two, hot_two, rest_rows,
         share, output),
    )
    grad_share = summed.reshape(-1)
    return finish_step(output_low, grad_hidden, grad_share, params, moment_one, moment_two)


def finish_step(output_low, grad_hidden, grad_share, params, moment_one, moment_two):
    shard_len = params.shape[0]
    index = lax.axis_index("dp") * lax.axis_size("head") + lax.axis_index("head")
    flat_index = index * shard_len + jnp.arange(shard_len, dtype=jnp.int32)
    param_step, new_one = adam_step(params, moment_one, moment_two, grad_share, flat_index)
    return (output_low, grad_hidden, grad_share, param_step, new_one)


def to_windows(shard):
    return lax.all_to_all(shard, "head", split_axis=0, concat_axis=1, tiled=True)


def to_positions(window):
    return lax.all_to_all(window, "head", split_axis=1, concat_axis=0, tiled=True)


def plain_shards(hidden_in, cotangent, box_coords, doc_lengths, params, moment_one, moment_two):
    head_pos = lax.axis_index("head")
    groups = lax.axis_size("head")
    shard_len = params.shape[0]
    flat_params = lax.all_gather(params.astype(BF16), ("dp", "head"), axis=0, tiled=True)
    pieces = unpack(flat_params)
    hidden = to_windows(hidden_in).reshape(WINLEN, D)
    cot = to_windows(cotangent).reshape(WINLEN, D)
    own_box = lax.dynamic_index_in_dim(box_coords, head_pos, 0, keepdims=False)
    own_lengths = lax.dynamic_index_in_dim(doc_lengths, head_pos, 0, keepdims=False)
    chosen, relative, centre_x, centre_y = window_layout(own_lengths, own_box)
    features = box_features(relative).astype(BF16)

    proj_qkv, proj_out, proj_box, proj_in, proj_back = pieces[:5]
    qv_bias, out_bias, norm_one, in_bias, back_bias, norm_two, tables = pieces[5:]
    ops = bias_operands(tables, chosen, centre_x, centre_y)
    start_state = hidden.astype(F32) + matmul(features, proj_box)
    start_low = start_state.astype(BF16)
    qv_float = qv_bias.astype(F32)
    mixed = matmul(start_low, proj_qkv)
    queries = (mixed[:, :D] + qv_float[0]).astype(BF16) * jnp.asarray(HEAD_DIM ** (-0.5), BF16)
    keys = mixed[:, D : 2 * D].astype(BF16)
    values = (mixed[:, 2 * D :] + qv_float[1]).astype(BF16)

    probs, context_t = attention_forward(queries, keys, values, ops)
    first_sum = start_state + rows_inner(context_t, proj_out) + out_bias.astype(F32)
    normed, norm_one_back = jax.vjp(layer_norm, first_sum, norm_one.astype(F32))
    normed_low = normed.astype(BF16)
    inner_act = matmul(normed_low, proj_in) + in_bias.astype(F32)
    active, gelu_back = jax.vjp(gelu_exact, inner_act)
    active_low = active.astype(BF16)
    second_sum = normed + matmul(active_low, proj_back) + back_bias.astype(F32)
    output, norm_two_back = jax.vjp(layer_norm, second_sum, norm_two.astype(F32))
    output_low = to_positions(output.astype(BF16).reshape(1, WINLEN, D))

    grad_second, grad_norm_two = norm_two_back(cot.astype(F32))
    grad_branch = grad_second.astype(BF16)
    grad_proj_back = rows_inner(active_low, grad_branch)
    grad_back_bias = jnp.sum(grad_branch.astype(F32), axis=0)
    (grad_inner_f,) = gelu_back(times_transposed(grad_branch, proj_back))
    grad_inner = grad_inner_f.astype(BF16)
    grad_proj_in = rows_inner(normed_low, grad_inner)
    grad_in_bias = jnp.sum(grad_inner.astype(F32), axis=0)
    grad_first, grad_norm_one = norm_one_back(grad_second + times_transposed(grad_inner, proj_in))
    grad_attn = grad_first.astype(BF16)
    grad_proj_out = matmul(context_t, grad_attn)
    grad_out_bias = jnp.sum(grad_attn.astype(F32), axis=0)
    grad_context = times_transposed(grad_attn, proj_out).astype(BF16)
    grad_queries_t, grad_keys, grad_values, cells, diag = attention_backward(
        queries, keys, values, grad_context, probs, ops
    )
    table_grad = table_grads(cells, diag)
    grad_mixed = jnp.concatenate([grad_queries_t.T, grad_keys, grad_values], axis=1)
    grad_proj_qkv = rows_inner(start_low, grad_mixed)
    summed = jnp.sum(grad_mixed.astype(F32), axis=0)
    grad_qv_bias = jnp.stack([summed[:D], summed[2 * D :]])
    grad_start = grad_first + times_transposed(grad_mixed, proj_qkv)
    grad_start_low = grad_start.astype(BF16)
    grad_hidden = to_positions(grad_start_low.reshape(1, WINLEN, D))
    grad_proj_box = rows_inner(features, grad_start_low)
    grad_list = (
        grad_proj_qkv,
        grad_proj_out,
        grad_proj_box,
        grad_proj_in,
        grad_proj_back,
        grad_qv_bias,
        grad_out_bias,
        grad_norm_one,
        grad_in_bias,
        grad_back_bias,
        grad_norm_two,
        table_grad,
    )
    padding = jnp.zeros((shard_len * groups * lax.axis_size("dp") - USED,), BF16)
    grads_flat = jnp.concatenate([piece.astype(BF16).reshape(-1) for piece in grad_list] + [padding])
    grad_share = lax.psum_scatter(
        grads_flat, ("dp", "head"), scatter_dimension=0, tiled=True
    ).astype(F32)
    return finish_step(output_low, grad_hidden, grad_share, params, moment_one, moment_two)


def solution(mesh):
    placed = (
        P("dp", "head", None),
        P("dp", "head", None),
        P("dp", None, None),
        P("dp", None),
        P(("dp", "head")),
        P(("dp", "head")),
        P(("dp", "head")),
    )
    return jax.shard_map(
        fast_shards if fits(mesh) else plain_shards,
        mesh=mesh,
        in_specs=placed,
        out_specs=(
            P("dp", "head", None),
            P("dp", "head", None),
            P(("dp", "head")),
            P(("dp", "head")),
            P(("dp", "head")),
        ),
        check_vma=False,
    )
```

```python
import functools
import math

import jax
import jax.numpy as jnp
import numpy as np
from jax import lax
from jax.experimental import pallas as pl
from jax.experimental.pallas import tpu as pltpu
from jax.sharding import PartitionSpec as P

D = 768
HEADS = 12
FF = 3072
BUCKETS = 32
WINLEN = 512
HEAD_DIM = 64
PAIRS = HEADS // 2
LANES = 128
BLOCKS = WINLEN // LANES

beta_one = 0.9
beta_two = 0.999
adam_eps = 1e-08
norm_eps = 1e-05
base_rate = 0.001
layer_decay = 0.75
decay_weight = 0.01
adam_count = 100
coord_cell = 32
masked_score = -1e30

F32 = jnp.float32
BF16 = jnp.bfloat16


def layouts_list():
    return (
        (D, 3 * D),
        (D, D),
        (D, D),
        (D, FF),
        (FF, D),
        (2, D),
        (D,),
        (2, D),
        (FF,),
        (D,),
        (2, D),
        (3, HEADS, BUCKETS),
    )


def unpack(flat_params):
    pieces = []
    offset = 0
    for layout in layouts_list():
        elements = math.prod(layout)
        pieces.append(flat_params[offset : offset + elements].reshape(layout))
        offset += elements
    return pieces


def matmul(left_mat, right_mat):
    return jnp.dot(left_mat, right_mat, preferred_element_type=F32)


def rows_inner(left_mat, right_mat):
    return lax.dot_general(left_mat, right_mat, (((0,), (0,)), ((), ())), preferred_element_type=F32)


def times_transposed(left_mat, right_mat):
    return lax.dot_general(left_mat, right_mat, (((1,), (1,)), ((), ())), preferred_element_type=F32)


def layer_norm(values, gain_bias):
    row_mean = jnp.mean(values, axis=-1, keepdims=True)
    centred = values - row_mean
    spread = jnp.mean(centred * centred, axis=-1, keepdims=True)
    return centred * lax.rsqrt(spread + norm_eps) * gain_bias[0] + gain_bias[1]


def gelu_exact(values):
    return jax.nn.gelu(values, approximate=False)


def hot(index, count):
    return (np.asarray(index)[..., None] == np.arange(count)).astype(np.float32)


def clipped(steps):
    return np.clip(steps, -(BUCKETS // 2), BUCKETS // 2 - 1) + BUCKETS // 2


CELLS = np.arange(BUCKETS)
HOT_SAME = hot(clipped(CELLS[:, None] - CELLS[None, :]), BUCKETS)
HOT_LESS = hot(clipped(CELLS[:, None] - CELLS[None, :] - 1), BUCKETS)
WIDE = 6 * LANES
_U = np.arange(WIDE)
BAND_HOT = hot(np.where(_U < 5 * LANES, clipped(_U - 2 * LANES), 0), BUCKETS)
_V = np.arange(4 * LANES)
DIAG_HOT = np.concatenate(
    [
        hot(np.zeros(LANES, np.int64), BUCKETS),
        hot(np.where(_V < 3 * LANES, clipped(_V - LANES), 0), BUCKETS),
        hot(np.full(LANES, BUCKETS - 1), BUCKETS),
    ]
)


def window_layout(doc_lengths, box_coords):
    doc_ends = jnp.cumsum(doc_lengths, dtype=jnp.int32)
    doc_starts = doc_ends - doc_lengths
    places = jnp.arange(WINLEN, dtype=jnp.int32)
    doc_ids = jnp.sum(
        (places[:, None] >= doc_ends[None, :]).astype(jnp.int32), axis=1, dtype=jnp.int32
    )
    docs = jnp.arange(doc_lengths.shape[0], dtype=jnp.int32)
    chosen = doc_ids[:, None] == docs[None, :]
    first_hot = places[:, None] == doc_starts[None, :]
    first_box = jnp.sum(
        jnp.where(first_hot[:, :, None], box_coords[:, None, :], 0), axis=0, dtype=jnp.int32
    )
    anchor = jnp.sum(
        jnp.where(chosen[:, :, None], first_box[None, :, :], 0), axis=1, dtype=jnp.int32
    )
    relative = box_coords - jnp.concatenate([anchor[:, :2], anchor[:, :2]], axis=1)
    centre_x = (box_coords[:, 0] + box_coords[:, 2]) // 2
    centre_y = (box_coords[:, 1] + box_coords[:, 3]) // 2
    return chosen, relative, centre_x, centre_y


def box_features(relative):
    count_freq = D // 8
    steps = jnp.arange(count_freq, dtype=F32)
    frequency = jnp.exp(steps * (-math.log(1000.0) / count_freq))
    angles = relative.astype(F32)[:, :, None] * frequency[None, None, :]
    return jnp.concatenate([jnp.sin(angles), jnp.cos(angles)], axis=2).reshape(relative.shape[0], D)


def bias_operands(tables, chosen, centre_x, centre_y):
    cell_x, cell_y = centre_x // coord_cell, centre_y // coord_cell
    rest_x, rest_y = centre_x % coord_cell, centre_y % coord_cell
    cells = jnp.arange(BUCKETS, dtype=jnp.int32)
    hot_x = (cell_x[:, None] == cells[None, :]).astype(BF16)
    hot_y = (cell_y[:, None] == cells[None, :]).astype(BF16)
    none = jnp.zeros_like(hot_x)
    hot_two = jnp.concatenate([hot_x, hot_y, hot_x, hot_y], axis=1)
    key_x = jnp.stack(
        [
            jnp.concatenate([hot_x, -hot_x, none, none], axis=1),
            jnp.concatenate([none, none, hot_x, -hot_x], axis=1),
        ]
    )
    key_y = jnp.stack(
        [
            jnp.concatenate([hot_y, -hot_y, none, none], axis=1),
            jnp.concatenate([none, none, hot_y, -hot_y], axis=1),
        ]
    )
    same = jnp.einsum("qcb,thb->thqc", HOT_SAME.astype(BF16), tables[1:], preferred_element_type=F32)
    less = jnp.einsum("qcb,thb->thqc", HOT_LESS.astype(BF16), tables[1:], preferred_element_type=F32)
    zero = jnp.zeros_like(same[0])
    base = jnp.concatenate(
        [jnp.concatenate([same[0], zero], axis=2), jnp.concatenate([zero, same[1]], axis=2)], axis=1
    )
    base = base.reshape(PAIRS, 2, 64, 64)[:, ::-1].reshape(HEADS, 64, 64)
    diff_x = jnp.concatenate([jnp.concatenate([less[0], same[0]], axis=2), jnp.zeros((HEADS, 32, 64), F32)], axis=1)
    diff_y = jnp.concatenate([jnp.zeros((HEADS, 32, 64), F32), jnp.concatenate([less[1], same[1]], axis=2)], axis=1)
    rows = jnp.concatenate([base, diff_x, diff_y], axis=0).astype(BF16)
    rows = rows.transpose(1, 0, 2).reshape(64, 3 * D)
    met = matmul(hot_two[:, :64], rows).astype(BF16)
    band = matmul(tables[0], jnp.asarray(BAND_HOT.T, BF16)).reshape(HEADS, 1, WIDE)
    rest_cols = jnp.stack([rest_x, rest_y], axis=1).astype(F32)
    rest_rows = rest_cols.T
    pad = jnp.zeros((WINLEN, LANES - chosen.shape[1]), BF16)
    marks = chosen.astype(BF16)
    mark_keys = jnp.concatenate([marks, pad], axis=1)
    mark_queries = jnp.concatenate([(1 - marks) * jnp.asarray(masked_score, BF16), pad], axis=1)
    return dict(
        hot_two=hot_two,
        key_x=key_x,
        key_y=key_y,
        met=met,
        band=band,
        rest_cols=rest_cols,
        rest_rows=rest_rows,
        mark_keys=mark_keys,
        mark_queries=mark_queries,
    )


def half_masks():
    lane = lax.broadcasted_iota(jnp.int32, (1, LANES), 1)
    low = (lane < HEAD_DIM).astype(F32)
    return low.astype(BF16), (1.0 - low).astype(BF16)


def less_masks(rest_cols, rest_rows, less_x, less_y):
    for part in range(BLOCKS):
        rows = slice(part * LANES, (part + 1) * LANES)
        for axis, less in ((0, less_x), (1, less_y)):
            column = rest_cols[rows, axis : axis + 1]
            row = rest_rows[axis : axis + 1, :]
            less[rows, :] = jnp.where(row < column, 1.0, 0.0).astype(less.dtype)


def attention_forward_kernel(
    q_ref, k_ref, v_ref, hot_ref, keyx_ref, keyy_ref, met_ref, band_ref, cols_ref, rows_ref,
    mkey_ref, mquery_ref, probs_ref, context_ref,
    kaug, qaug, less_x, less_y, wide, scores,
):
    low, high = half_masks()
    less_masks(cols_ref, rows_ref, less_x, less_y)
    kaug[:, LANES:] = mkey_ref[...]
    qaug[:, LANES:] = mquery_ref[...]
    half = 2 * LANES

    def one_pair(pair, carry):
        at = pl.multiple_of(pair * LANES, LANES)
        lanes = pl.ds(at, LANES)
        lanes_x = pl.ds(pl.multiple_of(at + D, LANES), LANES)
        lanes_y = pl.ds(pl.multiple_of(at + 2 * D, LANES), LANES)
        values_t = v_ref[:, lanes].T
        for odd in range(2):
            own, other = (low, high) if odd == 0 else (high, low)
            head = 2 * pair + odd
            kaug[:, :LANES] = k_ref[:, lanes] * own + hot_ref[...] * other
            qaug[:, :LANES] = q_ref[:, lanes] * own + met_ref[:, lanes] * other
            skew_band(band_ref[head], wide)
            for side in range(2):
                cols = slice(side * half, (side + 1) * half)
                top = None
                for part in range(BLOCKS):
                    rows = slice(part * LANES, (part + 1) * LANES)
                    s = times_transposed(kaug[rows, :], qaug[cols, :])
                    dx = times_transposed(keyx_ref[odd, rows, :], met_ref[cols, lanes_x])
                    dy = times_transposed(keyy_ref[odd, rows, :], met_ref[cols, lanes_y])
                    bias = []
                    for block in range(2 * side, 2 * side + 2):
                        step = max(-2, min(2, block - part)) + 2
                        bias.append(wide[:, step * LANES : (step + 1) * LANES])
                    s = s + jnp.concatenate(bias, axis=1)
                    s = s + dx * less_x[rows, cols] + dy * less_y[rows, cols]
                    scores[rows, :] = s
                    best = jnp.max(s, axis=0, keepdims=True)
                    top = best if top is None else jnp.maximum(top, best)
                total = None
                for part in range(BLOCKS):
                    rows = slice(part * LANES, (part + 1) * LANES)
                    e = jnp.exp(scores[rows, :] - top)
                    scores[rows, :] = e
                    add = jnp.sum(e, axis=0, keepdims=True)
                    total = add if total is None else total + add
                share = 1.0 / total
                for part in range(BLOCKS):
                    rows = slice(part * LANES, (part + 1) * LANES)
                    probs_ref[head, rows, cols] = (scores[rows, :] * share).astype(BF16)
                got = matmul(
                    values_t[odd * HEAD_DIM : (odd + 1) * HEAD_DIM, :], probs_ref[head, :, cols]
                )
                context_ref[pl.ds(pl.multiple_of(head * HEAD_DIM, HEAD_DIM), HEAD_DIM), cols] = (
                    got.astype(BF16)
                )
        return carry

    lax.fori_loop(0, PAIRS, one_pair, 0)


def skew_band(row, wide):
    x = jnp.broadcast_to(row, (8, WIDE))
    sub = lax.broadcasted_iota(jnp.int32, (8, WIDE), 0)
    for bit in (1, 2, 4):
        x = jnp.where((sub & bit) != 0, pltpu.roll(x, bit, 1), x)
    for group in range(LANES // 8):
        y = x if group == 0 else pltpu.roll(x, 8 * group, 1)
        wide[8 * group : 8 * group + 8, :] = y[:, : 5 * LANES]


def skew_groups(skewed, wide):
    for group in range(LANES // 8):
        y = skewed if group == 0 else pltpu.roll(skewed, 8 * group, 1)
        wide[8 * group : 8 * group + 8, :] = y[:, : 5 * LANES]


def diagonal_sums(parts):
    total = None
    for group in range(LANES // 8):
        x = jnp.concatenate(
            [parts[8 * group : 8 * group + 8, LANES : 4 * LANES], jnp.zeros((8, LANES), F32)], axis=1
        )
        y = x if group == 0 else pltpu.roll(x, 4 * LANES - 8 * group, 1)
        total = y if total is None else total + y
    sub = lax.broadcasted_iota(jnp.int32, (8, 4 * LANES), 0)
    for bit in (1, 2, 4):
        total = jnp.where((sub & bit) != 0, pltpu.roll(total, 4 * LANES - bit, 1), total)
    return jnp.sum(total, axis=0, keepdims=True)


def attention_backward_kernel(
    q_ref, k_ref, v_ref, dctx_ref, probs_ref, hot_ref, cols_ref, rows_ref,
    dq_ref, dk_ref, dv_ref, cells_ref, diag_ref,
    qaug, less_x, less_y, scores, dscores, band, kept, hot_t,
):
    low, high = half_masks()
    less_masks(cols_ref, rows_ref, less_x, less_y)
    hot_t[...] = hot_ref[...].T
    lane = lax.broadcasted_iota(jnp.int32, (1, LANES), 1)
    scale = HEAD_DIM ** (-0.5)
    of_x = jnp.where((lane // BUCKETS) % 2 == 0, 1.0, 0.0)
    cells_x = hot_ref[...] * of_x.astype(BF16)
    cells_y = hot_ref[...] * (1.0 - of_x).astype(BF16)

    def one_pair(pair, carry):
        at = pl.multiple_of(pair * LANES, LANES)
        lanes = pl.ds(at, LANES)
        keys_t = k_ref[:, lanes].T
        for odd in range(2):
            own, other = (low, high) if odd == 0 else (high, low)
            head = 2 * pair + odd
            qaug[...] = q_ref[:, lanes] * own + hot_ref[...] * other
            dctx = dctx_ref[:, lanes]
            dot = None
            for part in range(BLOCKS):
                rows = slice(part * LANES, (part + 1) * LANES)
                dp = times_transposed(v_ref[rows, lanes] * own, dctx)
                scores[rows, :] = dp
                add = jnp.sum(dp * probs_ref[head, rows, :].astype(F32), axis=0, keepdims=True)
                dot = add if dot is None else dot + add
            band[...] = jnp.zeros_like(band)
            for part in range(BLOCKS):
                rows = slice(part * LANES, (part + 1) * LANES)
                probs = probs_ref[head, rows, :]
                ds = probs.astype(F32) * (scores[rows, :] - dot)
                for block in range(BLOCKS):
                    step = max(-2, min(2, block - part)) + 2
                    where = slice(step * LANES, (step + 1) * LANES)
                    band[:, where] = band[:, where] + ds[:, block * LANES : (block + 1) * LANES]
                ds = ds.astype(BF16)
                dscores[rows, :] = ds
                both = matmul(ds, qaug[...])
                less = matmul(ds * less_x[rows, :], cells_x) + matmul(ds * less_y[rows, :], cells_y)
                dv = matmul(probs, dctx)
                kept[odd, 0, rows, :] = both
                kept[odd, 1, rows, :] = less
                kept[odd, 2, rows, :] = dv
            got = matmul(keys_t[odd * HEAD_DIM : (odd + 1) * HEAD_DIM, :], dscores[...])
            dq_ref[pl.ds(pl.multiple_of(head * HEAD_DIM, HEAD_DIM), HEAD_DIM), :] = (
                got * scale
            ).astype(BF16)
            diag_ref[head, :, LANES : 5 * LANES] = diagonal_sums(band)
            diag_ref[head, :, :LANES] = jnp.sum(band[:, :LANES], axis=0, keepdims=True)
            diag_ref[head, :, 5 * LANES :] = jnp.sum(band[:, 4 * LANES :], axis=0, keepdims=True)
            for which in range(2):
                summed = kept[odd, which]
                first = summed.astype(BF16)
                rest = (summed - first.astype(F32)).astype(BF16)
                cells_ref[head, which] = matmul(hot_t[:64, :], first) + matmul(hot_t[:64, :], rest)
        dk_ref[:, lanes] = jnp.where(lane < HEAD_DIM, kept[0, 0], kept[1, 0]).astype(BF16)
        dv_ref[:, lanes] = jnp.where(lane < HEAD_DIM, kept[0, 2], kept[1, 2]).astype(BF16)
        return carry

    lax.fori_loop(0, PAIRS, one_pair, 0)


def attention_forward(queries, keys, values, ops):
    return pl.pallas_call(
        attention_forward_kernel,
        out_shape=(
            jax.ShapeDtypeStruct((HEADS, WINLEN, WINLEN), BF16),
            jax.ShapeDtypeStruct((D, WINLEN), BF16),
        ),
        scratch_shapes=[
            pltpu.VMEM((WINLEN, 2 * LANES), BF16),
            pltpu.VMEM((WINLEN, 2 * LANES), BF16),
            pltpu.VMEM((WINLEN, WINLEN), F32),
            pltpu.VMEM((WINLEN, WINLEN), F32),
            pltpu.VMEM((LANES, 5 * LANES), F32),
            pltpu.VMEM((WINLEN, 2 * LANES), F32),
        ],
        compiler_params=pltpu.CompilerParams(vmem_limit_bytes=48 * 2**20),
        name="attention_forward",
    )(
        queries, keys, values, ops["hot_two"], ops["key_x"], ops["key_y"], ops["met"], ops["band"],
        ops["rest_cols"], ops["rest_rows"], ops["mark_keys"], ops["mark_queries"],
    )


def attention_backward(queries, keys, values, grad_context, probs, ops):
    return pl.pallas_call(
        attention_backward_kernel,
        out_shape=(
            jax.ShapeDtypeStruct((D, WINLEN), BF16),
            jax.ShapeDtypeStruct((WINLEN, D), BF16),
            jax.ShapeDtypeStruct((WINLEN, D), BF16),
            jax.ShapeDtypeStruct((HEADS, 2, 64, LANES), F32),
            jax.ShapeDtypeStruct((HEADS, 1, WIDE), F32),
        ),
        scratch_shapes=[
            pltpu.VMEM((WINLEN, LANES), BF16),
            pltpu.VMEM((WINLEN, WINLEN), BF16),
            pltpu.VMEM((WINLEN, WINLEN), BF16),
            pltpu.VMEM((WINLEN, WINLEN), F32),
            pltpu.VMEM((WINLEN, WINLEN), BF16),
            pltpu.VMEM((LANES, 5 * LANES), F32),
            pltpu.VMEM((2, 3, WINLEN, LANES), F32),
            pltpu.VMEM((LANES, WINLEN), BF16),
        ],
        compiler_params=pltpu.CompilerParams(vmem_limit_bytes=48 * 2**20),
        name="attention_backward",
    )(
        queries, keys, values, grad_context, probs, ops["hot_two"], ops["rest_cols"],
        ops["rest_rows"],
    )


def table_grads(cells, diag):
    exact = lax.Precision.HIGHEST
    pairs = cells.reshape(PAIRS, 2, 2, 64, LANES)
    every = jnp.stack([pairs[:, 0, 0, :, 64:], pairs[:, 1, 0, :, :64]], axis=1).reshape(HEADS, 64, 64)
    less = cells[:, 1]
    less_x, less_y = less[:, :32, :32], less[:, 32:, 32:64]
    all_x, all_y = every[:, :32, :32], every[:, 32:, 32:]
    same = jnp.stack([all_x - less_x, all_y - less_y]).reshape(2 * HEADS, -1)
    below = jnp.stack([less_x, less_y]).reshape(2 * HEADS, -1)
    same_hot = jnp.asarray(HOT_SAME.transpose(1, 0, 2).reshape(-1, BUCKETS))
    less_hot = jnp.asarray(HOT_LESS.transpose(1, 0, 2).reshape(-1, BUCKETS))
    moved = jnp.dot(same, same_hot, precision=exact) + jnp.dot(below, less_hot, precision=exact)
    along = jnp.dot(diag.reshape(HEADS, WIDE), jnp.asarray(DIAG_HOT), precision=exact)
    return jnp.concatenate([along[None], moved.reshape(2, HEADS, BUCKETS)], axis=0)


COLUMNS = 4
CORES = 2
DEPTH = 4
USED = sum(math.prod(layout) for layout in layouts_list())
MATRICES = layouts_list()[:5]
MISC = sum(math.prod(layout) for layout in layouts_list()[5:])
MISC_ROWS = -(-MISC // (8 * LANES)) * 8


class Plan:
    def __init__(self, shard_len, carry=3 * LANES):
        self.rows = shard_len // LANES
        self.quarter = -(-self.rows // (16 * COLUMNS)) * 16
        self.padded = COLUMNS * self.quarter
        self.per_column = CORES * DEPTH * self.rows
        self.carry = carry
        self.staged = self.carry + self.per_column + 3 * LANES
        starts = []
        offset = 0
        for depth, width in MATRICES:
            starts.append(offset // LANES)
            offset += depth * width
        self.starts = starts
        self.misc_start = offset // LANES


def fits(mesh):
    return mesh.shape["dp"] == COLUMNS * CORES and mesh.shape["head"] == DEPTH


MESH = pl.DeviceIdType.MESH


class Place:
    def __init__(self):
        dp = lax.axis_index("dp")
        self.z = lax.axis_index("head")
        self.core = dp % CORES
        self.column = dp // CORES
        self.x = self.column % 2
        self.y = self.column // 2
        self.col_x = 2 * self.y + (1 - self.x)
        self.col_y = 2 * (1 - self.y) + self.x
        self.col_d = 2 * (1 - self.y) + (1 - self.x)
        self.peer_x = self.at(self.col_x, self.core, self.z)
        self.peer_y = self.at(self.col_y, self.core, self.z)
        self.peer_d = self.at(self.col_d, self.core, self.z)
        self.peer_core = self.at(self.column, 1 - self.core, self.z)
        self.far = [lax.rem(self.z + d, DEPTH) for d in range(1, DEPTH)]
        self.from_far = [lax.rem(self.z + DEPTH - d, DEPTH) for d in range(1, DEPTH)]
        self.peers_z = [self.at(self.column, self.core, f) for f in self.far]

    def at(self, column, core, z):
        return {"dp": column * CORES + core, "head": z}

    def greet(self):
        barrier = pltpu.get_barrier_semaphore()
        peers = [self.peer_x, self.peer_y, self.peer_d, self.peer_core] + self.peers_z
        for peer in peers:
            pl.semaphore_signal(barrier, inc=1, device_id=peer, device_id_type=MESH)
        pl.semaphore_wait(barrier, len(peers))


def remote(src, dst, send_sem, recv_sem, peer):
    return pltpu.make_async_remote_copy(
        src_ref=src, dst_ref=dst, send_sem=send_sem, recv_sem=recv_sem, device_id=peer,
        device_id_type=MESH,
    )


class Gathering:
    def __init__(self, place, flat, sems):
        self.place = place
        self.flat = flat
        self.sems = sems
        self.sent = []

    def send(self, src, dst, kind, index, peer):
        copy = remote(src, dst, self.sems[kind].at[0, index], self.sems[kind].at[1, index], peer)
        copy.start()
        self.sent.append(copy)

    def got(self, dst, kind, index):
        remote(
            dst, dst, self.sems[kind].at[0, index], self.sems[kind].at[1, index], self.place.peer_x
        ).wait_recv()

    def spread(self, own):
        p = self.place
        for index, (column, peer) in enumerate(
            ((p.col_x, p.peer_x), (p.col_y, p.peer_y), (p.col_d, p.peer_d))
        ):
            self.send(
                own.at[column], self.flat.at[p.column, p.core, p.z, column], "spread", index, peer
            )
        self.flat[p.column, p.core, p.z, p.column] = own[p.column]

    def spread_done(self):
        p = self.place
        for index, column in enumerate((p.col_x, p.col_y, p.col_d)):
            self.got(self.flat.at[column, p.core, p.z, p.column], "spread", index)

    def along_z(self, k):
        p = self.place
        piece = self.flat.at[k, p.core, p.z, p.column]
        for d in range(DEPTH - 1):
            self.send(piece, piece, "z", 3 * k + d, p.peers_z[d])

    def first(self, k):
        p = self.place
        for d in range(DEPTH - 1):
            self.got(self.flat.at[k, p.core, p.from_far[d], p.column], "z", 3 * k + d)
        piece = self.flat.at[k, p.core, :, p.column]
        self.send(piece, piece, "one", 2 * k, p.peer_x)
        self.send(piece, piece, "one", 2 * k + 1, p.peer_y)
        self.send(piece, piece, "core", 5 * k, p.peer_core)

    def second(self, k):
        p = self.place
        from_x = self.flat.at[k, p.core, :, p.col_x]
        self.got(from_x, "one", 2 * k)
        part = self.flat.at[k, p.core, 0:2, p.col_x]
        self.send(part, part, "two", 2 * k, p.peer_y)
        self.send(from_x, from_x, "core", 5 * k + 1, p.peer_core)
        from_y = self.flat.at[k, p.core, :, p.col_y]
        self.got(from_y, "one", 2 * k + 1)
        part = self.flat.at[k, p.core, 2:4, p.col_y]
        self.send(part, part, "two", 2 * k + 1, p.peer_x)
        self.send(from_y, from_y, "core", 5 * k + 2, p.peer_core)

    def third(self, k):
        p = self.place
        part = self.flat.at[k, p.core, 0:2, p.col_d]
        self.got(part, "two", 2 * k)
        self.send(part, part, "core", 5 * k + 3, p.peer_core)
        part = self.flat.at[k, p.core, 2:4, p.col_d]
        self.got(part, "two", 2 * k + 1)
        self.send(part, part, "core", 5 * k + 4, p.peer_core)

    def complete(self, k):
        p = self.place
        other = 1 - p.core
        for index, column in enumerate((p.column, p.col_x, p.col_y)):
            self.got(self.flat.at[k, other, :, column], "core", 5 * k + index)
        self.got(self.flat.at[k, other, 0:2, p.col_d], "core", 5 * k + 3)
        self.got(self.flat.at[k, other, 2:4, p.col_d], "core", 5 * k + 4)

    def finish(self):
        for copy in self.sent:
            copy.wait_send()


GATHER_SEMS = {"spread": 3, "z": 12, "one": 8, "two": 8, "core": 20}


def sem_shapes(counts):
    return [pltpu.SemaphoreType.DMA((2, count)) for count in counts.values()]


def stage_column(plan, flat, staged, k):
    def one(shard, carry):
        core, z = shard // DEPTH, shard % DEPTH
        for quarter in range(COLUMNS):
            base = plan.carry + shard * plan.rows + quarter * plan.quarter
            staged[pl.ds(pl.multiple_of(base, 8), plan.quarter), :] = flat[k, core, z, quarter].astype(F32)
        return carry

    lax.fori_loop(0, CORES * DEPTH, one, 0)


def keep_carry(plan, staged):
    end = plan.carry + plan.per_column
    staged[: plan.carry, :] = staged[end - plan.carry : end, :]


ROW_STEP = 48


def column_rows(plan, k, touching):
    low, high = k * plan.per_column, (k + 1) * plan.per_column
    taken = []
    for index, (depth, width) in enumerate(MATRICES):
        group = 16 * (width // LANES)
        from_low, from_high = low - plan.starts[index], high - plan.starts[index]
        begin = max(0, min(depth, from_low // group * 16))
        if touching:
            end = max(0, min(depth, -(-from_high // group) * 16))
        else:
            end = max(0, min(depth, from_high // group * 16))
        if end > begin:
            taken.append((index, begin, end))
    return taken


def staged_at(plan, k, row):
    return plan.carry + row - k * plan.per_column


def row_loops(rows):
    whole = rows // ROW_STEP
    loops = [(ROW_STEP, 0, whole)] if whole else []
    if rows % ROW_STEP:
        loops.append((16, whole * ROW_STEP, (rows % ROW_STEP) // 16))
    return loops


def form_matrices(plan, staged, matrices, k):
    for index, begin, end in column_rows(plan, k, False):
        blocks = MATRICES[index][1] // LANES
        base = staged_at(plan, k, plan.starts[index] + begin * blocks)
        assert 0 <= base
        target = matrices[index]
        for step_rows, first, count in row_loops(end - begin):

            def one(step, carry, step_rows=step_rows, first=first, blocks=blocks, base=base,
                    begin=begin, target=target):
                row = first + step * step_rows
                for block in range(blocks):
                    got = staged[pl.ds(base + row * blocks + block, step_rows, stride=blocks), :]
                    target[
                        pl.ds(pl.multiple_of(begin + row, 16), step_rows),
                        block * LANES : (block + 1) * LANES,
                    ] = got.astype(BF16)
                return carry

            lax.fori_loop(0, count, one, 0)


def adam_step(params, moment_one, moment_two, grads, flat_index):
    box_part = (flat_index >= 4 * D * D) & (flat_index < 5 * D * D)
    step_rate = jnp.where(box_part, base_rate * layer_decay**12, base_rate * layer_decay)
    decay_mask = jnp.where(flat_index < 5 * D * D + 2 * D * FF, decay_weight, 0.0)
    moment_one = beta_one * moment_one + (1.0 - beta_one) * grads
    moment_two = beta_two * moment_two + (1.0 - beta_two) * grads * grads
    first_hat = moment_one / (1.0 - beta_one**adam_count)
    second_hat = moment_two / (1.0 - beta_two**adam_count)
    update = first_hat / (jnp.sqrt(second_hat) + adam_eps) + decay_mask * params
    return (-step_rate * update, moment_one)


VEC = {}
_at = 0
for _name, _rows in (
    ("q_bias", 6), ("v_bias", 6), ("out_bias", 6), ("gain_one", 6), ("shift_one", 6), ("in_bias", 24),
    ("back_bias", 6), ("gain_two", 6), ("shift_two", 6), ("tables", 9),
):
    VEC[_name] = _at * LANES
    _at += _rows
VEC_ROWS = _at
NOTE_ROWS = 96
NBLOCK = 2 * LANES


def note_place(plan):
    row = plan.misc_start - (CORES * DEPTH * COLUMNS - 1) * plan.rows
    quarter, row = row // plan.quarter, row % plan.quarter
    first = row // 16 * 16
    assert first + NOTE_ROWS <= plan.quarter and row - first + VEC_ROWS <= NOTE_ROWS
    return quarter, first, row - first


def spread_notes(place, own, notes, sems, plan):
    quarter, first, _ = note_place(plan)
    source = own.at[quarter, first : first + NOTE_ROWS]
    home = (place.column == COLUMNS - 1) & (place.core == CORES - 1)
    root = home & (place.z == DEPTH - 1)

    def copy(src, index, peer):
        return remote(src, notes, sems.at[0, index], sems.at[1, 0], peer)

    def arrived():
        copy(notes, 0, place.peer_core).wait_recv()

    @pl.when(root)
    def _():
        notes[...] = own[quarter, first : first + NOTE_ROWS]
        for index, peer in enumerate(place.peers_z):
            copy(source, index, peer).start()

    @pl.when(home & (place.z != DEPTH - 1))
    def _():
        arrived()

    @pl.when(home)
    def _():
        for index, peer in enumerate((place.peer_x, place.peer_y, place.peer_d)):
            copy(notes, 3 + index, peer).start()

    @pl.when((place.core == CORES - 1) & (place.column != COLUMNS - 1))
    def _():
        arrived()

    @pl.when(place.core == CORES - 1)
    def _():
        copy(notes, 6, place.peer_core).start()

    @pl.when(place.core != CORES - 1)
    def _():
        arrived()

    def finish():
        @pl.when(root)
        def _():
            for index, peer in enumerate(place.peers_z):
                copy(source, index, peer).wait_send()

        @pl.when(home)
        def _():
            for index, peer in enumerate((place.peer_x, place.peer_y, place.peer_d)):
                copy(notes, 3 + index, peer).wait_send()

        @pl.when(place.core == CORES - 1)
        def _():
            copy(notes, 6, place.peer_core).wait_send()

    return finish


def turns_table():
    count_freq = D // 8
    freq = np.exp(np.arange(count_freq) * (-math.log(1000.0) / count_freq)) / (2 * math.pi)
    per = np.concatenate([freq, freq])
    phase = np.concatenate([np.zeros(count_freq), np.full(count_freq, 0.25)])
    return np.stack([np.tile(per, 4), np.tile(phase, 4)]).astype(np.float32)


def sin_turns(t):
    t = t - jnp.floor(t + 0.5)
    a = jnp.abs(t)
    m = jnp.minimum(a, 0.5 - a) * (2 * math.pi)
    u = m * m
    poly = -1.0 / 39916800.0
    for term in (1.0 / 362880.0, -1.0 / 5040.0, 1.0 / 120.0, -1.0 / 6.0, 1.0):
        poly = poly * u + term
    s = m * poly
    return jnp.where(t < 0, -s, s)


def token_columns(boxes, lengths, window):
    coords = boxes[window].astype(F32)
    place = lax.broadcasted_iota(jnp.int32, (1, WINLEN), 1)
    doc = jnp.zeros((1, WINLEN), F32)
    anchor = jnp.zeros_like(coords)
    begin = 0
    for d in range(4):
        end = begin + lengths[window, d]
        mine = jnp.where((place >= begin) & (place < end), 1.0, 0.0)
        value = jnp.sum(coords * jnp.where(place == begin, 1.0, 0.0), axis=1, keepdims=True)
        anchor = anchor + value * mine
        doc = doc + mine * float(d)
        begin = end
    anchor = jnp.concatenate([anchor[0:2], anchor[0:2]], axis=0)
    relative = coords - anchor
    centre = jnp.floor((coords[0:2] + coords[2:4]) * 0.5)
    cell = jnp.floor(centre * (1.0 / coord_cell))
    rest = centre - cell * coord_cell
    rows = jnp.concatenate(
        [relative, cell, rest, doc, jnp.zeros((LANES - 9, WINLEN), F32)], axis=0
    )
    return rest, rows.T


def form_features(columns, turns_ref, features):
    lane = lax.broadcasted_iota(jnp.int32, (1, LANES), 1)
    for block in range(D // LANES):
        lanes = slice(block * LANES, (block + 1) * LANES)
        low, high = block * LANES // (D // 4), ((block + 1) * LANES - 1) // (D // 4)
        value = columns[:, low : low + 1]
        if high != low:
            value = jnp.where(
                lane + block * LANES < high * (D // 4), value, columns[:, high : high + 1]
            )
        t = value * turns_ref[0:1, lanes] + turns_ref[1:2, lanes]
        features[:, lanes] = sin_turns(t).astype(BF16)


def form_hots(columns, hot_ref, keyx_ref, keyy_ref, mkey, mquery):
    lane = lax.broadcasted_iota(jnp.int32, (1, LANES), 1)
    part = lane // BUCKETS
    cell = (lane % BUCKETS).astype(F32)
    is_x = jnp.where(columns[:, 4:5] == cell, 1.0, 0.0)
    is_y = jnp.where(columns[:, 5:6] == cell, 1.0, 0.0)
    hot_ref[...] = jnp.where(part % 2 == 0, is_x, is_y).astype(BF16)
    sign = jnp.where(part % 2 == 0, 1.0, -1.0)
    for odd in range(2):
        here = jnp.where(part // 2 == odd, sign, 0.0)
        keyx_ref[odd] = (is_x * here).astype(BF16)
        keyy_ref[odd] = (is_y * here).astype(BF16)
    doc = jnp.where(columns[:, 8:9] == lane.astype(F32), 1.0, 0.0)
    mkey[:, LANES:] = doc.astype(BF16)
    mquery[:, LANES:] = (jnp.where(lane < 4, 1.0 - doc, 0.0) * masked_score).astype(BF16)


def form_tables(tables, bands, tilted):
    row = lax.broadcasted_iota(jnp.int32, (LANES, 1), 0)
    half = BUCKETS // 2
    sub = lax.broadcasted_iota(jnp.int32, (8, LANES), 0)
    sub_wide = lax.broadcasted_iota(jnp.int32, (8, WIDE), 0)
    place = lax.broadcasted_iota(jnp.int32, (1, WIDE), 1)
    wanted = jnp.where(place < 5 * LANES, jnp.clip(place - 2 * LANES, -half, half - 1) + half, 0)
    lane = lax.broadcasted_iota(jnp.int32, (1, LANES), 1)
    turned = jnp.clip(64 - lane, -half, half - 1) + half
    for m in range(4):
        hot_band = jnp.where(row == wanted + m * BUCKETS, 1.0, 0.0).astype(BF16)
        got = matmul(tables, hot_band)
        for n in range(3):
            x = jnp.broadcast_to(got[n : n + 1, :], (8, WIDE))
            for bit in (1, 2, 4):
                x = jnp.where((sub_wide & bit) != 0, pltpu.roll(x, bit, 1), x)
            bands[4 * n + m] = x
        hot_turn = jnp.where(row == turned + m * BUCKETS, 1.0, 0.0).astype(BF16)
        got = matmul(tables, hot_turn)
        for t in (1, 2):
            for n in range(3):
                x = jnp.broadcast_to(got[3 * t + n : 3 * t + n + 1, :], (8, LANES))
                for bit in (1, 2, 4):
                    x = jnp.where((sub & bit) != 0, pltpu.roll(x, bit, 1), x)
                for group in range(BUCKETS // 8):
                    y = x if group == 0 else pltpu.roll(x, 8 * group, 1)
                    tilted[(t - 1) * HEADS + 4 * n + m, 8 * group : 8 * group + 8, :] = y


def pair_rows(tilted, pair):
    lane = lax.broadcasted_iota(jnp.int32, (1, LANES), 1)
    part = lane // BUCKETS
    x0, x1 = tilted[2 * pair], tilted[2 * pair + 1]
    y0, y1 = tilted[HEADS + 2 * pair], tilted[HEADS + 2 * pair + 1]

    def same(value, to):
        return value if to == 64 else pltpu.roll(value, (to - 64) % LANES, 1)

    def less(value, to):
        return pltpu.roll(value, (to - 65) % LANES, 1)

    zero = jnp.zeros_like(x0)
    base_x = jnp.where(part == 0, same(x1, 0), jnp.where(part == 2, same(x0, 64), zero))
    base_y = jnp.where(part == 1, same(y1, 32), jnp.where(part == 3, same(y0, 96), zero))

    def steps(even, odd):
        return jnp.where(
            part < 2,
            jnp.where(part == 0, less(even, 0), same(even, 32)),
            jnp.where(part == 2, less(odd, 64), same(odd, 96)),
        )

    rows = [
        jnp.concatenate([base_x, base_y], axis=0),
        jnp.concatenate([steps(x0, x1), zero], axis=0),
        jnp.concatenate([zero, steps(y0, y1)], axis=0),
    ]
    return jnp.concatenate(rows, axis=1).astype(BF16)


def gelu_and_slope(z):
    a = jnp.abs(z)
    t = 1.0 / (1.0 + (0.3275911 / math.sqrt(2.0)) * a)
    poly = 1.061405429 * 0.5
    for term in (-1.453152027, 1.421413741, -0.284496736, 0.254829592):
        poly = poly * t + 0.5 * term
    e = jnp.exp(-0.5 * z * z)
    tail = poly * t * e
    cdf = jnp.where(z < 0, tail, 1.0 - tail)
    return z * cdf, cdf + z * (e * (1.0 / math.sqrt(2.0 * math.pi)))


def forward_kernel(plan, params_in, hidden_in, cot_in, boxes, lengths, turns, *refs):
    (w_qkv_out, w_out_out, w_in_out, w_back_out, features_out, low_out, q_out, k_out, v_out, probs_out,
     context_out, hat_out, normed_out, active_out, slope_out, second_out, vec_out, rstd_out, gain_grads,
     output_ref, cot_ref, hot_out, rest_out, share_out) = refs[:24]
    refs = refs[24:]
    (flat, staged, own, w_qkv, w_out, w_box, w_in, w_back, notes, features, hidden, start, start_low, q_ref,
     k_ref, v_ref, hot_ref, key_x, key_y, bands, tilted, wides, scores, context_t, pair_t, hat, active,
     slope, vec) = refs[:29]
    note_sems, swap_sems, copy_sems, probs_sems = refs[29:33]

    def lend(buffer, slot, lanes):
        return buffer.at[:, slot : slot + lanes]

    less_x, less_y = lend(slope, 0, WINLEN), lend(slope, WINLEN, WINLEN)
    probs = [lend(slope, 2 * WINLEN, WINLEN), lend(slope, 3 * WINLEN, WINLEN)]
    kaugs = [lend(active, 0, 2 * LANES), lend(active, 2 * LANES, 2 * LANES)]
    qaugs = [lend(active, 4 * LANES, 2 * LANES), lend(active, 6 * LANES, 2 * LANES)]
    met = lend(active, 8 * LANES, 3 * LANES)
    place = Place()
    normed_low = hidden
    context = features
    gathering = Gathering(place, flat, dict(zip(GATHER_SEMS, refs[33:])))
    matrices = (w_qkv, w_out, w_box, w_in, w_back)
    written = []

    def write_out(src, dst):
        copy = pltpu.make_async_copy(src, dst, copy_sems.at[len(written)])
        copy.start()
        written.append(copy)

    fetch = pltpu.make_async_copy(params_in, staged.at[: plan.rows], probs_sems.at[0])
    fetch.start()
    place.greet()
    fetch.wait()
    for quarter_at in range(COLUMNS):
        begin = quarter_at * plan.quarter
        own[quarter_at] = staged[begin : begin + plan.quarter, :].astype(BF16)
    gathering.spread(own)

    quarter = WINLEN // DEPTH

    def exchange(source, target, kind):
        rows = pl.ds(pl.multiple_of(place.z * quarter, quarter), quarter)
        for d in range(DEPTH - 1):
            gathering_send(source.at[place.far[d]], target.at[rows], kind, d, place.peers_z[d])

    def gathering_send(src, dst, kind, d, peer):
        copy = remote(src, dst, swap_sems.at[kind, 0, d], swap_sems.at[kind, 1, d], peer)
        copy.start()
        gathering.sent.append(copy)

    def exchanged(target, kind):
        for d in range(DEPTH - 1):
            rows = pl.ds(pl.multiple_of(place.from_far[d] * quarter, quarter), quarter)
            remote(
                target.at[rows], target.at[rows], swap_sems.at[kind, 0, d], swap_sems.at[kind, 1, d],
                place.peer_x,
            ).wait_recv()

    exchange(hidden_in, hidden, 0)
    finish_notes = spread_notes(place, own, notes, note_sems, plan)
    own_rows = pl.ds(pl.multiple_of(place.z * quarter, quarter), quarter)
    own_hidden = pltpu.make_async_copy(
        hidden_in.at[place.z], hidden.at[own_rows], swap_sems.at[0, 0, DEPTH - 1]
    )
    own_hidden.start()
    own_cot = pltpu.make_async_copy(
        cot_in.at[place.z], cot_ref.at[own_rows], swap_sems.at[1, 0, DEPTH - 1]
    )
    own_cot.start()
    gathering.spread_done()
    gathering.along_z(0)
    gathering.along_z(1)

    rest, columns = token_columns(boxes, lengths, place.z)
    for part in range(BLOCKS):
        rows = slice(part * LANES, (part + 1) * LANES)
        for axis, less in ((0, less_x), (1, less_y)):
            less[rows, :] = jnp.where(
                rest[axis : axis + 1, :] < columns[rows, 6 + axis : 7 + axis], 1.0, 0.0
            ).astype(BF16)
    rest_out[...] = rest
    form_hots(columns, hot_ref, key_x, key_y, kaugs[0], qaugs[0])
    kaugs[1][:, LANES:] = kaugs[0][:, LANES:]
    qaugs[1][:, LANES:] = qaugs[0][:, LANES:]
    hot_out[...] = hot_ref[...]
    form_features(columns, turns, features)
    for n in range(D // LANES):
        rows = slice(n * LANES, (n + 1) * LANES)
        context_t[rows, :] = features[:, rows].T
    write_out(context_t, features_out)
    _, _, note_row = note_place(plan)
    for row in range(VEC_ROWS):
        at = note_row + row
        vec[0:1, row * LANES : (row + 1) * LANES] = notes[at // 16 * 16 : at // 16 * 16 + 16, :].astype(
            F32
        )[at % 16 : at % 16 + 1, :]
    vec_out[...] = vec[...]
    table_row = note_row + VEC["tables"] // LANES
    assert table_row % 16 == 0
    form_tables(notes[table_row : table_row + 16, :], bands, tilted)

    gathering.first(0)
    gathering.along_z(2)
    gathering.first(1)
    gathering.along_z(3)
    exchange(cot_in, cot_ref, 1)
    gathering.second(0)
    gathering.second(1)
    gathering.first(2)
    gathering.third(0)
    gathering.complete(0)
    stage_column(plan, flat, staged, 0)
    form_matrices(plan, staged, matrices, 0)
    keep_carry(plan, staged)
    gathering.third(1)
    gathering.first(3)
    gathering.complete(1)
    stage_column(plan, flat, staged, 1)
    form_matrices(plan, staged, matrices, 1)
    keep_carry(plan, staged)
    write_out(w_qkv, w_qkv_out)
    write_out(w_out, w_out_out)

    exchanged(hidden, 0)
    own_hidden.wait()
    for n in range(D // NBLOCK):
        lanes = slice(n * NBLOCK, (n + 1) * NBLOCK)
        value = hidden[:, lanes].astype(F32) + matmul(features[...], w_box[:, lanes])
        start[:, lanes] = value
        start_low[:, lanes] = value.astype(BF16)
    write_out(start_low, low_out)
    written[0].wait()

    def project(n, carry):
        at = pl.multiple_of(n * NBLOCK, NBLOCK)
        lanes = pl.ds(at, NBLOCK)
        low = start_low[...]
        bias = vec[0:1, pl.ds(pl.multiple_of(VEC["q_bias"] + at, LANES), NBLOCK)]
        got = matmul(low, w_qkv[:, lanes]) + bias
        q_ref[:, lanes] = (got.astype(BF16).astype(F32) * HEAD_DIM ** (-0.5)).astype(BF16)
        k_ref[:, lanes] = matmul(low, w_qkv[:, pl.ds(pl.multiple_of(at + D, LANES), NBLOCK)]).astype(BF16)
        bias = vec[0:1, pl.ds(pl.multiple_of(VEC["v_bias"] + at, LANES), NBLOCK)]
        got = matmul(low, w_qkv[:, pl.ds(pl.multiple_of(at + 2 * D, LANES), NBLOCK)]) + bias
        v_ref[:, lanes] = got.astype(BF16)
        return carry

    lax.fori_loop(0, D // NBLOCK, project, 0)
    write_out(q_ref, q_out)
    write_out(k_ref, k_out)
    write_out(v_ref, v_out)
    gathering.second(2)

    low, high = half_masks()
    half = 2 * LANES

    def probs_copy(head, odd):
        return pltpu.make_async_copy(probs[odd], probs_out.at[head], probs_sems.at[odd])

    def one_pair(pair, carry):
        at = pl.multiple_of(pair * LANES, LANES)
        lanes = pl.ds(at, LANES)
        values_t = v_ref[:, lanes].T
        met[...] = matmul(hot_ref[:, :64], pair_rows(tilted, pair)).astype(BF16)
        for odd in range(2):
            mine, other = (low, high) if odd == 0 else (high, low)
            kaugs[odd][:, :LANES] = k_ref[:, lanes] * mine + hot_ref[...] * other
            qaugs[odd][:, :LANES] = q_ref[:, lanes] * mine + met[:, :LANES] * other
            skew_groups(bands[2 * pair + odd], wides.at[odd])

            @pl.when(pair > 0)
            def _():
                probs_copy(2 * pair + odd, odd).wait()

        for side in range(2):
            cols = slice(side * half, (side + 1) * half)
            tops = []
            for odd in range(2):
                whole = times_transposed(kaugs[odd][...], qaugs[odd][cols, :])
                steps_x = times_transposed(key_x[odd], met[cols, LANES : 2 * LANES])
                steps_y = times_transposed(key_y[odd], met[cols, 2 * LANES :])
                top = None
                for part in range(BLOCKS):
                    rows = slice(part * LANES, (part + 1) * LANES)
                    bias = []
                    for block in range(2 * side, 2 * side + 2):
                        step = max(-2, min(2, block - part)) + 2
                        bias.append(wides[odd, :, step * LANES : (step + 1) * LANES])
                    s = whole[rows] + jnp.concatenate(bias, axis=1)
                    s = s + steps_x[rows] * less_x[rows, cols].astype(F32)
                    s = s + steps_y[rows] * less_y[rows, cols].astype(F32)
                    scores[odd, rows, :] = s
                    best = jnp.max(s.reshape(LANES // 8, 8, half), axis=0)
                    top = best if top is None else jnp.maximum(top, best)
                tops.append(jnp.max(top, axis=0, keepdims=True))
            for odd in range(2):
                total = None
                for part in range(BLOCKS):
                    rows = slice(part * LANES, (part + 1) * LANES)
                    e = jnp.exp(scores[odd, rows, :] - tops[odd])
                    probs[odd][rows, cols] = e.astype(BF16)
                    add = jnp.sum(e.reshape(LANES // 8, 8, half), axis=0)
                    total = add if total is None else total + add
                share = 1.0 / jnp.sum(total, axis=0, keepdims=True)
                share_out[2 * pair + odd, :, cols] = share
                got = matmul(values_t[odd * HEAD_DIM : (odd + 1) * HEAD_DIM, :], probs[odd][:, cols])
                pair_t[odd * HEAD_DIM : (odd + 1) * HEAD_DIM, cols] = got * share
        for odd in range(2):
            probs_copy(2 * pair + odd, odd).start()
        both = pair_t[...]
        context_t[lanes, :] = both.astype(BF16)
        context[:, lanes] = both.T.astype(BF16)
        return carry

    lax.fori_loop(0, 2, one_pair, 0)
    gathering.third(2)
    gathering.second(3)
    lax.fori_loop(2, 4, one_pair, 0)
    gathering.third(3)
    gathering.complete(2)
    stage_column(plan, flat, staged, 2)
    form_matrices(plan, staged, matrices, 2)
    keep_carry(plan, staged)
    write_out(w_in, w_in_out)
    lax.fori_loop(4, PAIRS, one_pair, 0)
    write_out(context_t, context_out)
    gathering.complete(3)
    stage_column(plan, flat, staged, 3)
    form_matrices(plan, staged, matrices, 3)
    write_out(w_back, w_back_out)

    def vector(name):
        return vec[0:1, VEC[name] : VEC[name] + D]

    for n in range(D // NBLOCK):
        lanes = slice(n * NBLOCK, (n + 1) * NBLOCK)
        bias = vec[0:1, VEC["out_bias"] + n * NBLOCK : VEC["out_bias"] + (n + 1) * NBLOCK]
        start[:, lanes] = start[:, lanes] + matmul(context[...], w_out[:, lanes]) + bias

    step_rows = 64

    def norm_first(n, carry):
        rows = pl.ds(pl.multiple_of(n * step_rows, step_rows), step_rows)
        x = start[rows, :]
        centred = x - jnp.mean(x, axis=1, keepdims=True)
        rstd = lax.rsqrt(jnp.mean(centred * centred, axis=1, keepdims=True) + norm_eps)
        xhat = centred * rstd
        hat[rows, :] = xhat
        rstd_out[rows, :] = jnp.broadcast_to(rstd, (step_rows, LANES))
        normed = xhat * vector("gain_one") + vector("shift_one")
        start[rows, :] = normed
        normed_low[rows, :] = normed.astype(BF16)
        return carry

    lax.fori_loop(0, WINLEN // step_rows, norm_first, 0)
    write_out(hat, hat_out)
    write_out(normed_low, normed_out)

    for odd in range(2):
        probs_copy(0, odd).wait()

    def widen(n, carry):
        at = pl.multiple_of(n * NBLOCK, NBLOCK)
        lanes = pl.ds(at, NBLOCK)
        bias = vec[0:1, pl.ds(pl.multiple_of(VEC["in_bias"] + at, LANES), NBLOCK)]
        value, change = gelu_and_slope(matmul(normed_low[...], w_in[:, lanes]) + bias)
        active[:, lanes] = value.astype(BF16)
        slope[:, lanes] = change.astype(BF16)
        return carry

    lax.fori_loop(0, FF // NBLOCK, widen, 0, unroll=2)
    write_out(active, active_out)
    write_out(slope, slope_out)
    for n in range(D // NBLOCK):
        lanes = slice(n * NBLOCK, (n + 1) * NBLOCK)
        bias = vec[0:1, VEC["back_bias"] + n * NBLOCK : VEC["back_bias"] + (n + 1) * NBLOCK]
        start[:, lanes] = start[:, lanes] + matmul(active[...], w_back[:, lanes]) + bias

    exchanged(cot_ref, 1)
    own_cot.wait()
    gain_grads[...] = jnp.zeros_like(gain_grads)

    def norm_second(n, carry):
        rows = pl.ds(pl.multiple_of(n * step_rows, step_rows), step_rows)
        x = start[rows, :]
        centred = x - jnp.mean(x, axis=1, keepdims=True)
        rstd = lax.rsqrt(jnp.mean(centred * centred, axis=1, keepdims=True) + norm_eps)
        xhat = centred * rstd
        output_ref[rows, :] = (xhat * vector("gain_two") + vector("shift_two")).astype(BF16)
        cot = cot_ref[rows, :].astype(F32)
        prod = cot * xhat
        gain_grads[0:1, :] = gain_grads[0:1, :] + jnp.sum(prod, axis=0, keepdims=True)
        gain_grads[1:2, :] = gain_grads[1:2, :] + jnp.sum(cot, axis=0, keepdims=True)
        gain = vector("gain_two")
        gc = cot * gain
        mean_one = jnp.mean(gc, axis=1, keepdims=True)
        mean_two = jnp.mean(prod * gain, axis=1, keepdims=True)
        second_out[rows, :] = rstd * (gc - mean_one - xhat * mean_two)
        return carry

    lax.fori_loop(0, WINLEN // step_rows, norm_second, 0)
    for copy in written[1:]:
        copy.wait()
    finish_notes()
    gathering.finish()


def forward_pass(plan, params, hidden_in, cotangent, boxes, lengths):
    anywhere = pl.BlockSpec(memory_space=pl.ANY)
    vmem = pl.BlockSpec(memory_space=pltpu.VMEM)
    token = (WINLEN, D)

    def hbm(shape, dtype=BF16):
        return jax.ShapeDtypeStruct(shape, dtype), anywhere

    def near(shape, dtype=F32):
        return jax.ShapeDtypeStruct(shape, dtype), vmem

    outs = [
        hbm(MATRICES[0]), hbm(MATRICES[1]), hbm(MATRICES[3]), hbm(MATRICES[4]), hbm((D, WINLEN)), hbm(token),
        hbm(token), hbm(token), hbm(token), hbm((HEADS, WINLEN, WINLEN)), hbm((D, WINLEN)),
        hbm(token, F32), hbm(token), hbm((WINLEN, FF)), hbm((WINLEN, FF)), near(token),
        near((1, VEC_ROWS * LANES)), near((WINLEN, LANES)), near((2, D)), near(token, BF16),
        near(token, BF16), near((WINLEN, LANES), BF16), near((2, WINLEN)),
        near((HEADS, 1, WINLEN)),
    ]
    scratch = [
        pltpu.VMEM((COLUMNS, CORES, DEPTH, COLUMNS, plan.quarter, LANES), BF16),
        pltpu.VMEM((plan.staged, LANES), F32),
        pltpu.VMEM((COLUMNS, plan.quarter, LANES), BF16),
    ]
    scratch += [pltpu.VMEM(layout, BF16) for layout in MATRICES]
    scratch += [
        pltpu.VMEM((NOTE_ROWS, LANES), BF16),
        pltpu.VMEM(token, BF16),
        pltpu.VMEM(token, BF16),
        pltpu.VMEM(token, F32),
        pltpu.VMEM(token, BF16),
        pltpu.VMEM(token, BF16),
        pltpu.VMEM(token, BF16),
        pltpu.VMEM(token, BF16),
        pltpu.VMEM((WINLEN, LANES), BF16),
        pltpu.VMEM((2, WINLEN, LANES), BF16),
        pltpu.VMEM((2, WINLEN, LANES), BF16),
        pltpu.VMEM((HEADS, 8, WIDE), F32),
        pltpu.VMEM((2 * HEADS, BUCKETS, LANES), F32),
        pltpu.VMEM((2, LANES, 5 * LANES), F32),
        pltpu.VMEM((2, WINLEN, 2 * LANES), F32),
        pltpu.VMEM((D, WINLEN), BF16),
        pltpu.VMEM((LANES, WINLEN), F32),
        pltpu.VMEM(token, F32),
        pltpu.VMEM((WINLEN, FF), BF16),
        pltpu.VMEM((WINLEN, FF), BF16),
        pltpu.VMEM((1, VEC_ROWS * LANES), F32),
        pltpu.SemaphoreType.DMA((2, 7)),
        pltpu.SemaphoreType.DMA((2, 2, DEPTH)),
        pltpu.SemaphoreType.DMA((16,)),
        pltpu.SemaphoreType.DMA((2,)),
    ]
    return pl.pallas_call(
        functools.partial(forward_kernel, plan),
        out_shape=[shape for shape, _ in outs],
        in_specs=[anywhere] * 3 + [vmem, pl.BlockSpec(memory_space=pltpu.SMEM), vmem],
        out_specs=[spec for _, spec in outs],
        scratch_shapes=scratch + sem_shapes(GATHER_SEMS),
        compiler_params=pltpu.CompilerParams(
            collective_id=0, has_side_effects=True, vmem_limit_bytes=62 * 2**20
        ),
        name="forward_pass",
    )(params, hidden_in, cotangent, boxes, lengths, jnp.asarray(turns_table()))


def token_info(doc_lengths, box_coords):
    places = jnp.arange(WINLEN, dtype=jnp.int32)
    first = places == 0
    doc = jnp.zeros((WINLEN,), jnp.int32)
    end = 0
    for d in range(3):
        end = end + doc_lengths[d]
        doc = doc + (places >= end).astype(jnp.int32)
        first = first | (places == end)
    rows = [box_coords[:, c] for c in range(4)] + [doc, first.astype(jnp.int32)]
    return jnp.stack(rows + [jnp.zeros_like(doc)] * 2).astype(F32)


class Reducing:
    def __init__(self, place, flat, swapped, one, two, deep, piece, result, sems, free):
        self.place = place
        self.flat = flat
        self.swapped = swapped
        self.one = one
        self.two = two
        self.deep = deep
        self.piece = piece
        self.result = result
        self.sems = sems
        self.free = free
        self.sent = {k: [] for k in range(COLUMNS)}

    def send(self, k, src, dst, kind, index, peer):
        copy = remote(src, dst, self.sems[kind].at[0, index], self.sems[kind].at[1, index], peer)
        copy.start()
        self.sent[k].append(copy)

    got = Gathering.got

    def settle(self, k):
        for copy in self.sent.pop(k):
            copy.wait_send()

    def swap(self, k):
        p = self.place
        slot = k % 2
        if k < 2:
            pl.semaphore_wait(self.free.at[slot], 1)
        self.send(k, self.flat.at[slot, 1 - p.core], self.swapped.at[slot], "core", k, p.peer_core)

    def first(self, k):
        p = self.place
        slot = k % 2
        self.got(self.swapped.at[slot], "core", k)

        def one(step, carry):
            z, quarter = step // COLUMNS, step % COLUMNS
            total = self.flat[slot, p.core, z, quarter].astype(F32)
            total = total + self.swapped[slot, z, quarter].astype(F32)
            self.flat[slot, p.core, z, quarter] = total.astype(BF16)
            return carry

        lax.fori_loop(0, DEPTH * COLUMNS, one, 0)
        flat = self.flat
        self.send(k, flat.at[slot, p.core, 0:2, p.col_d], self.one.at[k, 0], "one", 2 * k, p.peer_y)
        self.send(k, flat.at[slot, p.core, 2:4, p.col_d], self.one.at[k, 1], "one", 2 * k + 1, p.peer_x)
        if k >= 2:
            pl.semaphore_signal(
                self.free.at[slot], inc=1, device_id=p.peer_core, device_id_type=MESH
            )

    def second(self, k):
        p = self.place
        slot = k % 2
        for side, column in ((0, p.col_x), (1, p.col_y)):
            self.got(self.one.at[k, side], "one", 2 * k + side)

            def one(step, carry, side=side, column=column):
                z = 2 * side + step
                total = self.flat[slot, p.core, z, column].astype(F32)
                total = total + self.one[k, side, step].astype(F32)
                self.flat[slot, p.core, z, column] = total.astype(BF16)
                return carry

            lax.fori_loop(0, 2, one, 0)
        flat = self.flat
        self.send(k, flat.at[slot, p.core, :, p.col_x], self.two.at[k, 0], "two", 2 * k, p.peer_x)
        self.send(k, flat.at[slot, p.core, :, p.col_y], self.two.at[k, 1], "two", 2 * k + 1, p.peer_y)

    def third(self, k):
        p = self.place
        slot = k % 2
        for side in range(2):
            self.got(self.two.at[k, side], "two", 2 * k + side)

        def one(z, carry):
            total = self.flat[slot, p.core, z, p.column].astype(F32)
            total = total + self.two[k, 0, z].astype(F32) + self.two[k, 1, z].astype(F32)
            self.flat[slot, p.core, z, p.column] = total.astype(BF16)
            return carry

        lax.fori_loop(0, DEPTH, one, 0)
        for d in range(DEPTH - 1):
            self.send(
                k, self.flat.at[slot, p.core, p.far[d], p.column], self.deep.at[k, d], "z", 3 * k + d,
                p.peers_z[d],
            )

    def fourth(self, k):
        p = self.place
        for d in range(DEPTH - 1):
            self.got(self.deep.at[k, d], "z", 3 * k + d)
        total = self.flat[k % 2, p.core, p.z, p.column].astype(F32)
        for d in range(DEPTH - 1):
            total = total + self.deep[k, d].astype(F32)
        self.piece[k] = total.astype(BF16)

    def giving(self, k):
        p = self.place
        sems = self.sems["spread"]
        return remote(
            self.piece.at[k], self.result.at[p.column], sems.at[0, k], sems.at[1, p.column],
            p.at(k, p.core, p.z),
        )

    def give(self, k):
        @pl.when(self.place.column != k)
        def _():
            self.giving(k).start()

    def given(self, k):
        @pl.when(self.place.column != k)
        def _():
            self.giving(k).wait_send()

    def receive(self, out):
        p = self.place
        out[p.column] = self.piece[p.column].astype(F32)
        for column in (p.col_x, p.col_y, p.col_d):
            self.got(self.result.at[column], "spread", column)
            out[column] = self.result[column].astype(F32)


REDUCE_SEMS = {"spread": 4, "z": 12, "one": 8, "two": 8, "core": 4}


def unstage_column(plan, flat, staged, k):
    def one(step, carry):
        shard, quarter = step // COLUMNS, step % COLUMNS
        base = plan.carry + shard * plan.rows + quarter * plan.quarter
        piece = staged[pl.ds(pl.multiple_of(base, 8), plan.quarter), :]
        flat[k % 2, shard // DEPTH, shard % DEPTH, quarter] = piece.astype(BF16)
        return carry

    lax.fori_loop(0, CORES * DEPTH * COLUMNS, one, 0)


class Notes:
    def __init__(self, place, notes, slots, sems):
        self.place, self.notes, self.slots, self.sems = place, notes, slots, sems
        p = place
        self.home = (p.column == COLUMNS - 1) & (p.core == CORES - 1)
        self.root = self.home & (p.z == DEPTH - 1)

    def copy(self, slot, peer):
        return remote(
            self.notes, self.slots.at[slot], self.sems.at[0, 0], self.sems.at[1, slot], peer
        )

    def take(self, slot):
        self.copy(slot, self.place.peer_core).wait_recv()
        self.notes[...] = self.notes[...] + self.slots[slot]

    def start(self):
        p = self.place

        @pl.when(p.core != CORES - 1)
        def _():
            self.copy(0, p.peer_core).start()

    def rise(self):
        p = self.place

        @pl.when(p.core == CORES - 1)
        def _():
            self.take(0)

        @pl.when((p.core == CORES - 1) & (p.column != COLUMNS - 1))
        def _():
            self.copy(1 + p.column, p.at(COLUMNS - 1, p.core, p.z)).start()

    def end(self):
        p = self.place

        @pl.when(self.home)
        def _():
            for slot in range(1, 4):
                self.take(slot)

        @pl.when(self.home & (p.z != DEPTH - 1))
        def _():
            self.copy(4 + p.z, p.at(p.column, p.core, DEPTH - 1)).start()

        @pl.when(self.root)
        def _():
            for slot in range(4, 7):
                self.take(slot)

        @pl.when(jnp.logical_not(self.root))
        def _():
            self.copy(0, p.peer_core).wait_send()


def cell_sums(whole, less, odd):
    lane = lax.broadcasted_iota(jnp.int32, (1, LANES), 1)
    sub = lax.broadcasted_iota(jnp.int32, (8, LANES), 0)
    sums = []
    for axis in range(2):
        rows = slice(axis * BUCKETS, (axis + 1) * BUCKETS)
        start = axis * BUCKETS + (0 if odd else 64)
        every = pltpu.roll(whole[rows], (BUCKETS - start) % LANES, 1)
        below = pltpu.roll(less[rows], (BUCKETS - axis * BUCKETS) % LANES, 1)
        inside = (lane >= BUCKETS) & (lane < 2 * BUCKETS)
        every = jnp.where(inside, every, 0.0)
        below = jnp.where(inside, below, 0.0)
        x = every - below + pltpu.roll(below, LANES - 1, 1)
        total = None
        for group in range(BUCKETS // 8):
            y = x[8 * group : 8 * group + 8]
            y = y if group == 0 else pltpu.roll(y, LANES - 8 * group, 1)
            total = y if total is None else total + y
        for bit in (1, 2, 4):
            total = jnp.where((sub & bit) != 0, pltpu.roll(total, LANES - bit, 1), total)
        sums.append(jnp.sum(total, axis=0, keepdims=True))
    return sums


def exact_dot(a, b):
    return jnp.dot(a, b, preferred_element_type=F32, precision=lax.Precision.HIGHEST)


def bucket_rows(cell_ref, diag_ref):
    half = BUCKETS // 2
    column = lax.broadcasted_iota(jnp.int32, (1, LANES), 1)
    row = lax.broadcasted_iota(jnp.int32, (LANES, 1), 0)
    to = jnp.clip(row - BUCKETS, -half, half - 1) + half
    place = lax.broadcasted_iota(jnp.int32, (WIDE, 1), 0)
    along = place - LANES
    far = jnp.where(place < LANES, 0, jnp.where(place < 5 * LANES, 0, BUCKETS - 1))
    along = jnp.where(
        (place >= LANES) & (place < 4 * LANES),
        jnp.clip(along - LANES, -half, half - 1) + half,
        far,
    )
    first, rest = None, None
    zero = jnp.zeros((5, WIDE), F32)
    for m in range(4):
        hot_along = jnp.where(along + m * BUCKETS == column, 1.0, 0.0)
        got = exact_dot(
            jnp.concatenate([diag_ref[4 * n + m] for n in range(3)] + [zero], axis=0), hot_along
        )
        first = got if first is None else first + got
        hot_cell = jnp.where(to + m * BUCKETS == column, 1.0, 0.0)
        rows = [cell_ref[t * HEADS + 4 * n + m] for t in range(2) for n in range(3)]
        got = exact_dot(jnp.concatenate(rows + [zero[:2, :LANES]], axis=0), hot_cell)
        rest = got if rest is None else rest + got
    return jnp.concatenate([first[:3], rest[:6]], axis=0)


def backward_kernel(
    plan, active_in, slope_in, w_back_in, w_in_in, w_out_in, w_qkv_in, normed_in, low_in, features_in,
    context_in, q_in, k_in, v_in, probs_in, hat_in, second_in, rstd_ref, vec, gain_two, hot_ref, rest_ref,
    share_ref, output_in, *refs,
):
    out, output_pos, hidden_pos = refs[:3]
    (flat, staged, swapped, one_buf, two_buf, deep, piece, result, active, slope, w_back, w_in, w_out,
     turned, context_t, q_ref, k_ref, v_ref, hat, second, branch, dctx, probs, less_x,
     less_y, scores_odd, bands, hot_t, qaugs, pair_t, scaled, share_cols, vecg, cell_rows, diag_rows, notes, slots,
     ) = refs[3:40]
    load_sems, probs_sems, free, pos_sems, note_sems = refs[40:45]
    place = Place()
    reducing = Reducing(
        place, flat, swapped, one_buf, two_buf, deep, piece, result,
        dict(zip(REDUCE_SEMS, refs[45:])), free,
    )
    climbing = Notes(place, notes, slots, note_sems)
    loads = {}

    def load(name, src, dst):
        loads[name] = pltpu.make_async_copy(src, dst, load_sems.at[len(loads)])
        loads[name].start()

    mixed = active.at[:, : 3 * D]
    grad_attn = branch
    w_qkv = w_in.at[:, : 3 * D]
    hidden_low = dctx
    features_t = w_back.at[:D, :WINLEN]
    low_t = w_out.at[:WINLEN]
    scores = [hat.at[:, :WINLEN], scores_odd]
    dscores = [slope.at[:, :WINLEN], slope.at[:, WINLEN : 2 * WINLEN]]
    dscores_x = [slope.at[:, 2 * WINLEN : 3 * WINLEN], slope.at[:, 3 * WINLEN : 4 * WINLEN]]
    dscores_y = [slope.at[:, 4 * WINLEN : 5 * WINLEN], slope.at[:, 5 * WINLEN :]]

    load("second", second_in, second)
    load("active", active_in, active)

    at = staged_at(plan, COLUMNS - 1, plan.misc_start)
    staged[at:, :] = jnp.zeros((plan.staged - at, LANES), F32)
    place.greet()

    quarter = WINLEN // DEPTH
    positions = []

    def to_pos(source, target, kind):
        for d in range(DEPTH - 1):
            rows = pl.ds(pl.multiple_of(place.far[d] * quarter, quarter), quarter)
            copy = remote(
                source.at[rows], target.at[place.z], pos_sems.at[kind, 0, d], pos_sems.at[kind, 1, d],
                place.peers_z[d],
            )
            copy.start()
            positions.append(copy)
        rows = pl.ds(pl.multiple_of(place.z * quarter, quarter), quarter)
        copy = pltpu.make_async_copy(
            source.at[rows], target.at[place.z], pos_sems.at[kind, 0, DEPTH - 1]
        )
        copy.start()
        return copy

    def in_pos(target, kind):
        for d in range(DEPTH - 1):
            there = target.at[place.from_far[d]]
            remote(
                there, there, pos_sems.at[kind, 0, d], pos_sems.at[kind, 1, d], place.peer_x
            ).wait_recv()

    own_output = to_pos(output_in, output_pos, 0)

    def store(k, index, row, value, first_block=0):
        blocks = MATRICES[index][1] // LANES
        base = staged_at(plan, k, plan.starts[index]) + row * blocks + first_block
        for block in range(value.shape[1] // LANES):
            staged[pl.ds(base + block, value.shape[0], stride=blocks), :] = value[
                :, block * LANES : (block + 1) * LANES
            ]

    def column_sum(value):
        return jnp.sum(value, axis=0, keepdims=True)

    def keep_vector(name, lanes_at, value):
        at = pl.multiple_of(VEC[name] + lanes_at, LANES)
        vecg[0:1, pl.ds(at, value.shape[1])] = value

    loads["second"].wait()
    for n in range(D // NBLOCK):
        lanes = slice(n * NBLOCK, (n + 1) * NBLOCK)
        value = second[:, lanes].astype(BF16)
        branch[:, lanes] = value
        keep_vector("back_bias", n * NBLOCK, column_sum(value.astype(F32)))
    loads["active"].wait()
    load("slope", slope_in, slope)
    load("w_back", w_back_in, w_back)
    load("normed", normed_in, dctx)

    def back_rows(k, size, begin, count):
        def body(n, carry):
            row = pl.multiple_of(begin + n * size, LANES)
            turned[:size, :] = active[:, pl.ds(row, size)].T
            store(k, 4, row, matmul(turned[:size, :], branch[...]))
            return carry

        lax.fori_loop(0, count, body, 0)

    back_rows(3, WINLEN, 512, FF // WINLEN - 1)
    unstage_column(plan, flat, staged, 3)
    reducing.swap(3)

    back_rows(2, WINLEN, 0, 1)
    back_rows(2, LANES, 512, 1)
    loads["w_back"].wait()
    loads["slope"].wait()
    load("w_in", w_in_in, w_in)
    load("hat", hat_in, hat)
    load("w_out", w_out_in, w_out)

    def inner(n, carry):
        at = pl.multiple_of(n * NBLOCK, NBLOCK)
        lanes = pl.ds(at, NBLOCK)
        value = times_transposed(branch[...], w_back[lanes, :]) * slope[:, lanes].astype(F32)
        value = value.astype(BF16)
        slope[:, lanes] = value
        keep_vector("in_bias", at, column_sum(value.astype(F32)))
        return carry

    lax.fori_loop(0, FF // NBLOCK, inner, 0, unroll=2)
    grad_inner = slope
    reducing.first(3)

    loads["normed"].wait()
    for n in range(D // NBLOCK):
        rows = slice(n * NBLOCK, (n + 1) * NBLOCK)
        turned[rows, :] = dctx[:, rows].T

    def in_rows(k, begin, end):
        def body(n, carry):
            lanes = pl.ds(pl.multiple_of(n * NBLOCK, NBLOCK), NBLOCK)
            got = matmul(turned[begin:end, :], grad_inner[:, lanes])
            store(k, 3, begin, got, n * (NBLOCK // LANES))
            return carry

        lax.fori_loop(0, FF // NBLOCK, body, 0)

    in_rows(2, 288, D)
    unstage_column(plan, flat, staged, 2)
    reducing.swap(2)
    reducing.second(3)

    loads["w_in"].wait()
    load("context", context_in, context_t)
    load("q", q_in, q_ref)
    load("k", k_in, k_ref)
    load("v", v_in, v_ref)
    for odd in range(2):
        pltpu.make_async_copy(probs_in.at[odd], probs.at[odd], probs_sems.at[odd]).start()
    for n in range(D // NBLOCK):
        lanes = slice(n * NBLOCK, (n + 1) * NBLOCK)
        second[:, lanes] = second[:, lanes] + times_transposed(grad_inner[...], w_in[lanes, :])
    load("w_qkv", w_qkv_in, w_qkv)
    load("features", features_in, features_t)
    reducing.first(2)

    loads["hat"].wait()
    step_rows = 64
    for name in ("gain_one", "shift_one", "out_bias"):
        keep_vector(name, 0, jnp.zeros((1, D), F32))

    def norm_first(n, carry):
        rows = pl.ds(pl.multiple_of(n * step_rows, step_rows), step_rows)
        grad = second[rows, :]
        xhat = hat[rows, :]
        prod = grad * xhat
        gain = vec[0:1, VEC["gain_one"] : VEC["gain_one"] + D]
        gc = grad * gain
        mean_one = jnp.mean(gc, axis=1, keepdims=True)
        mean_two = jnp.mean(prod * gain, axis=1, keepdims=True)
        value = rstd_ref[rows, 0:1] * (gc - mean_one - xhat * mean_two)
        second[rows, :] = value
        value = value.astype(BF16)
        grad_attn[rows, :] = value
        for name, term in (
            ("gain_one", prod), ("shift_one", grad), ("out_bias", value.astype(F32)),
        ):
            lanes = slice(VEC[name], VEC[name] + D)
            vecg[0:1, lanes] = vecg[0:1, lanes] + column_sum(term)
        return carry

    lax.fori_loop(0, WINLEN // step_rows, norm_first, 0)
    reducing.third(3)
    loads["w_out"].wait()
    for n in range(D // NBLOCK):
        lanes = slice(n * NBLOCK, (n + 1) * NBLOCK)
        dctx[:, lanes] = times_transposed(grad_attn[...], w_out[lanes, :]).astype(BF16)
    load("low", low_in, low_t)
    loads["context"].wait()
    in_rows(1, 0, 304)
    reducing.second(2)

    def out_rows(k, begin, end):
        for n in range(D // NBLOCK):
            lanes = slice(n * NBLOCK, (n + 1) * NBLOCK)
            got = matmul(context_t[begin:end, :], grad_attn[:, lanes])
            store(k, 1, begin, got, n * (NBLOCK // LANES))

    out_rows(1, 192, D)
    reducing.fourth(3)
    reducing.give(3)

    low, high = half_masks()
    rest = rest_ref[...]
    columns = jnp.concatenate([rest, jnp.zeros((LANES - 2, WINLEN), F32)], axis=0).T
    for part in range(BLOCKS):
        rows = slice(part * LANES, (part + 1) * LANES)
        for axis, less in ((0, less_x), (1, less_y)):
            less[rows, :] = jnp.where(
                rest[axis : axis + 1, :] < columns[rows, axis : axis + 1], 1.0, 0.0
            ).astype(BF16)
    hot_t[...] = hot_ref[...].T
    lane = lax.broadcasted_iota(jnp.int32, (1, LANES), 1)
    scale = HEAD_DIM ** (-0.5)
    of_x = jnp.where((lane // BUCKETS) % 2 == 0, 1.0, 0.0)
    share_cols[...] = jnp.concatenate(
        [share_ref[head] for head in range(HEADS)] + [jnp.zeros((LANES - HEADS, WINLEN), F32)], axis=0
    ).T
    for name in ("q", "k", "v"):
        loads[name].wait()

    def probs_copy(head, odd):
        return pltpu.make_async_copy(probs_in.at[head], probs.at[odd], probs_sems.at[odd])

    def one_pair(pair, carry):
        at = pl.multiple_of(pair * LANES, LANES)
        lanes = pl.ds(at, LANES)
        keys_t = k_ref[:, lanes].T
        cells_x = hot_ref[...] * of_x.astype(BF16)
        cells_y = hot_ref[...] * (1.0 - of_x).astype(BF16)
        both = pltpu.roll(share_cols[...], lax.rem(LANES - 2 * pair, LANES), 1)
        both = jnp.where(lane < HEAD_DIM, both[:, 0:1], both[:, 1:2])
        scaled[...] = (dctx[:, lanes].astype(F32) * both).astype(BF16)
        grad_context = dctx[:, lanes]
        dots = []
        for odd in range(2):
            mine, other = (low, high) if odd == 0 else (high, low)
            head = 2 * pair + odd
            probs_copy(head, odd).wait()
            qaugs[odd] = q_ref[:, lanes] * mine + hot_ref[...] * other
            products = times_transposed(v_ref[:, lanes] * mine, grad_context)
            dot = None
            for part in range(BLOCKS):
                rows = slice(part * LANES, (part + 1) * LANES)
                dp = products[rows]
                scores[odd][rows, :] = dp
                add = dp * probs[odd, rows, :].astype(F32)
                add = jnp.sum(add.reshape(LANES // 8, 8, WINLEN), axis=0)
                dot = add if dot is None else dot + add
            dots.append(column_sum(dot) * share_ref[head])
            bands[odd] = jnp.zeros_like(bands[odd])
        for odd in range(2):
            head = 2 * pair + odd
            share = share_ref[head]
            for part in range(BLOCKS):
                rows = slice(part * LANES, (part + 1) * LANES)
                ds = probs[odd, rows, :].astype(F32) * ((scores[odd][rows, :] - dots[odd]) * share)
                for block in range(BLOCKS):
                    step = max(-2, min(2, block - part)) + 2
                    where = slice(step * LANES, (step + 1) * LANES)
                    bands[odd, :, where] = (
                        bands[odd, :, where] + ds[:, block * LANES : (block + 1) * LANES]
                    )
                ds = ds.astype(BF16)
                dscores[odd][rows, :] = ds
                dscores_x[odd][rows, :] = ds * less_x[rows, :]
                dscores_y[odd][rows, :] = ds * less_y[rows, :]
        for odd in range(2):
            head = 2 * pair + odd
            keys_cells = matmul(dscores[odd][...], qaugs[odd])
            less = matmul(dscores_x[odd][...], cells_x) + matmul(dscores_y[odd][...], cells_y)
            values_grad = matmul(probs[odd], scaled[...])

            pair_t[odd * HEAD_DIM : (odd + 1) * HEAD_DIM, :] = matmul(
                keys_t[odd * HEAD_DIM : (odd + 1) * HEAD_DIM, :], dscores[odd][...]
            )
            band = bands.at[odd]
            diag_rows[head, :, LANES : 5 * LANES] = diagonal_sums(band)
            diag_rows[head, :, :LANES] = column_sum(band[:, :LANES])
            diag_rows[head, :, 5 * LANES :] = column_sum(band[:, 4 * LANES :])
            sums = []
            for summed in (keys_cells, less):
                first = summed.astype(BF16)
                remainder = (summed - first.astype(F32)).astype(BF16)
                sums.append(matmul(hot_t[:64, :], first) + matmul(hot_t[:64, :], remainder))
            for axis, value in enumerate(cell_sums(sums[0], sums[1], odd)):
                cell_rows[axis * HEADS + head] = value
            for which, value in ((1, keys_cells), (2, values_grad)):
                there = pl.ds(pl.multiple_of(at + which * D, LANES), LANES)
                value = value.astype(BF16)
                if odd:
                    value = mixed[:, there] * low + value * high
                mixed[:, there] = value

        @pl.when(pair < PAIRS - 1)
        def _():
            for odd in range(2):
                probs_copy(2 * pair + odd + 2, odd).start()

        value = (pair_t[...].T * scale).astype(BF16)
        mixed[:, lanes] = value
        keep_vector("q_bias", at, column_sum(value.astype(F32)))
        there = pl.ds(pl.multiple_of(at + 2 * D, LANES), LANES)
        keep_vector("v_bias", at, column_sum(mixed[:, there].astype(F32)))
        return carry

    lax.fori_loop(0, 2, one_pair, 0)
    reducing.third(2)
    lax.fori_loop(2, 4, one_pair, 0)
    reducing.fourth(2)
    reducing.give(2)
    lax.fori_loop(4, PAIRS, one_pair, 0)

    loads["w_qkv"].wait()
    for n in range(D // NBLOCK):
        lanes = slice(n * NBLOCK, (n + 1) * NBLOCK)
        value = second[:, lanes] + times_transposed(mixed[...], w_qkv[lanes, :])
        hidden_low[:, lanes] = value.astype(BF16)
    own_hidden = to_pos(hidden_low, hidden_pos, 1)
    loads["features"].wait()
    for n in range(D // NBLOCK):
        lanes = slice(n * NBLOCK, (n + 1) * NBLOCK)
        store(1, 2, 0, matmul(features_t[...], hidden_low[:, lanes]), n * (NBLOCK // LANES))
    reducing.settle(3)
    unstage_column(plan, flat, staged, 1)
    reducing.swap(1)

    loads["low"].wait()
    for n in range(D // NBLOCK):
        rows = slice(n * NBLOCK, (n + 1) * NBLOCK)
        turned[rows, :] = low_t[:, rows].T

    def qkv_rows(n, carry):
        lanes = pl.ds(pl.multiple_of(n * NBLOCK, NBLOCK), NBLOCK)
        store(0, 0, 0, matmul(turned[...], mixed[:, lanes]), n * (NBLOCK // LANES))
        return carry

    lax.fori_loop(0, 3 * D // NBLOCK, qkv_rows, 0)
    out_rows(0, 0, 208)
    reducing.settle(2)
    unstage_column(plan, flat, staged, 0)
    reducing.swap(0)
    reducing.first(1)
    keep_vector("gain_two", 0, gain_two[0:1, :])
    keep_vector("shift_two", 0, gain_two[1:2, :])
    notes[...] = jnp.zeros_like(notes)
    table = VEC["tables"] // LANES
    for row in range(table):
        notes[row : row + 1, :] = vecg[0:1, row * LANES : (row + 1) * LANES]
    notes[table : table + 9, :] = bucket_rows(cell_rows, diag_rows)
    climbing.start()

    reducing.first(0)
    reducing.second(1)
    climbing.rise()
    reducing.second(0)
    climbing.end()
    reducing.third(1)
    reducing.third(0)
    reducing.fourth(1)
    reducing.give(1)
    reducing.fourth(0)
    reducing.give(0)
    reducing.receive(out)
    note_quarter, note_first, note_row = note_place(plan)
    base = note_first + note_row

    @pl.when(climbing.root)
    def _():
        out[note_quarter, base : base + MISC_ROWS, :] = (
            out[note_quarter, base : base + MISC_ROWS, :] + notes[:MISC_ROWS, :]
        )

    in_pos(output_pos, 0)
    in_pos(hidden_pos, 1)
    own_output.wait()
    own_hidden.wait()
    for copy in positions:
        copy.wait_send()
    for k in range(COLUMNS):
        reducing.given(k)
    reducing.settle(1)
    reducing.settle(0)


def backward_pass(plan, operands):
    anywhere = pl.BlockSpec(memory_space=pl.ANY)
    vmem = pl.BlockSpec(memory_space=pltpu.VMEM)
    token = (WINLEN, D)
    block = (plan.quarter, LANES)
    positions = jax.ShapeDtypeStruct((DEPTH, WINLEN // DEPTH, D), BF16)
    scratch = [
        pltpu.VMEM((2, CORES, DEPTH, COLUMNS) + block, BF16),
        pltpu.VMEM((plan.staged, LANES), F32),
        pltpu.VMEM((2, DEPTH, COLUMNS) + block, BF16),
        pltpu.VMEM((COLUMNS, 2, 2) + block, BF16),
        pltpu.VMEM((COLUMNS, 2, DEPTH) + block, BF16),
        pltpu.VMEM((COLUMNS, DEPTH - 1) + block, BF16),
        pltpu.VMEM((COLUMNS,) + block, BF16),
        pltpu.VMEM((COLUMNS,) + block, BF16),
        pltpu.VMEM((WINLEN, FF), BF16),
        pltpu.VMEM((WINLEN, FF), BF16),
        pltpu.VMEM((FF, D), BF16),
        pltpu.VMEM((D, FF), BF16),
        pltpu.VMEM((D, D), BF16),
        pltpu.VMEM((D, WINLEN), BF16),
        pltpu.VMEM((D, WINLEN), BF16),
        pltpu.VMEM(token, BF16),
        pltpu.VMEM(token, BF16),
        pltpu.VMEM(token, BF16),
        pltpu.VMEM(token, F32),
        pltpu.VMEM(token, F32),
        pltpu.VMEM(token, BF16),
        pltpu.VMEM(token, BF16),
        pltpu.VMEM((2, WINLEN, WINLEN), BF16),
        pltpu.VMEM((WINLEN, WINLEN), BF16),
        pltpu.VMEM((WINLEN, WINLEN), BF16),
        pltpu.VMEM((WINLEN, WINLEN), F32),
        pltpu.VMEM((2, LANES, 5 * LANES), F32),
        pltpu.VMEM((LANES, WINLEN), BF16),
        pltpu.VMEM((2, WINLEN, LANES), BF16),
        pltpu.VMEM((LANES, WINLEN), F32),
        pltpu.VMEM((WINLEN, LANES), BF16),
        pltpu.VMEM((WINLEN, LANES), F32),
        pltpu.VMEM((1, VEC_ROWS * LANES), F32),
        pltpu.VMEM((2 * HEADS, 1, LANES), F32),
        pltpu.VMEM((HEADS, 1, WIDE), F32),
        pltpu.VMEM((NOTE_ROWS, LANES), F32),
        pltpu.VMEM((7, NOTE_ROWS, LANES), F32),
        pltpu.SemaphoreType.DMA((16,)),
        pltpu.SemaphoreType.DMA((2,)),
        pltpu.SemaphoreType.REGULAR((2,)),
        pltpu.SemaphoreType.DMA((2, 2, DEPTH)),
        pltpu.SemaphoreType.DMA((2, 7)),
    ]
    return pl.pallas_call(
        functools.partial(backward_kernel, plan),
        out_shape=[jax.ShapeDtypeStruct((COLUMNS,) + block, F32), positions, positions],
        in_specs=[anywhere] * 16 + [vmem] * 6 + [anywhere],
        out_specs=[vmem, anywhere, anywhere],
        scratch_shapes=scratch + sem_shapes(REDUCE_SEMS),
        compiler_params=pltpu.CompilerParams(
            collective_id=1, has_side_effects=True, vmem_limit_bytes=62 * 2**20
        ),
        name="backward_pass",
    )(*operands)


def fast_shards(hidden_in, cotangent, box_coords, doc_lengths, params, moment_one, moment_two):
    shard_len = params.shape[0]
    plan = Plan(shard_len)
    (proj_qkv, proj_out, proj_in, proj_back, features_t, start_low, queries, keys, values, probs, context_t,
     xhat, normed_low, active, slope, grad_second, vec, rstd, grad_norm_two, output, _, hot_two,
     rest_rows, share) = forward_pass(
        plan, params.reshape(plan.rows, LANES), hidden_in, cotangent,
        jnp.transpose(box_coords, (0, 2, 1)), doc_lengths,
    )
    summed, output_low, grad_hidden = backward_pass(
        Plan(shard_len, carry=5 * LANES),
        (active, slope, proj_back, proj_in, proj_out, proj_qkv, normed_low, start_low, features_t, context_t,
         queries, keys, values, probs, xhat, grad_second, rstd, vec, grad_norm_two, hot_two, rest_rows,
         share, output),
    )
    grad_share = summed.reshape(plan.padded, LANES)[: plan.rows].reshape(-1)
    return finish_step(output_low, grad_hidden, grad_share, params, moment_one, moment_two)


def finish_step(output_low, grad_hidden, grad_share, params, moment_one, moment_two):
    shard_len = params.shape[0]
    index = lax.axis_index("dp") * lax.axis_size("head") + lax.axis_index("head")
    flat_index = index * shard_len + jnp.arange(shard_len, dtype=jnp.int32)
    param_step, new_one = adam_step(params, moment_one, moment_two, grad_share, flat_index)
    return (output_low, grad_hidden, grad_share, param_step, new_one)


def to_windows(shard):
    return lax.all_to_all(shard, "head", split_axis=0, concat_axis=1, tiled=True)


def to_positions(window):
    return lax.all_to_all(window, "head", split_axis=1, concat_axis=0, tiled=True)


def plain_shards(hidden_in, cotangent, box_coords, doc_lengths, params, moment_one, moment_two):
    head_pos = lax.axis_index("head")
    groups = lax.axis_size("head")
    shard_len = params.shape[0]
    flat_params = lax.all_gather(params.astype(BF16), ("dp", "head"), axis=0, tiled=True)
    pieces = unpack(flat_params)
    hidden = to_windows(hidden_in).reshape(WINLEN, D)
    cot = to_windows(cotangent).reshape(WINLEN, D)
    own_box = lax.dynamic_index_in_dim(box_coords, head_pos, 0, keepdims=False)
    own_lengths = lax.dynamic_index_in_dim(doc_lengths, head_pos, 0, keepdims=False)
    chosen, relative, centre_x, centre_y = window_layout(own_lengths, own_box)
    features = box_features(relative).astype(BF16)

    proj_qkv, proj_out, proj_box, proj_in, proj_back = pieces[:5]
    qv_bias, out_bias, norm_one, in_bias, back_bias, norm_two, tables = pieces[5:]
    ops = bias_operands(tables, chosen, centre_x, centre_y)
    start_state = hidden.astype(F32) + matmul(features, proj_box)
    start_low = start_state.astype(BF16)
    qv_float = qv_bias.astype(F32)
    mixed = matmul(start_low, proj_qkv)
    queries = (mixed[:, :D] + qv_float[0]).astype(BF16) * jnp.asarray(HEAD_DIM ** (-0.5), BF16)
    keys = mixed[:, D : 2 * D].astype(BF16)
    values = (mixed[:, 2 * D :] + qv_float[1]).astype(BF16)

    probs, context_t = attention_forward(queries, keys, values, ops)
    first_sum = start_state + rows_inner(context_t, proj_out) + out_bias.astype(F32)
    normed, norm_one_back = jax.vjp(layer_norm, first_sum, norm_one.astype(F32))
    normed_low = normed.astype(BF16)
    inner_act = matmul(normed_low, proj_in) + in_bias.astype(F32)
    active, gelu_back = jax.vjp(gelu_exact, inner_act)
    active_low = active.astype(BF16)
    second_sum = normed + matmul(active_low, proj_back) + back_bias.astype(F32)
    output, norm_two_back = jax.vjp(layer_norm, second_sum, norm_two.astype(F32))
    output_low = to_positions(output.astype(BF16).reshape(1, WINLEN, D))

    grad_second, grad_norm_two = norm_two_back(cot.astype(F32))
    grad_branch = grad_second.astype(BF16)
    grad_proj_back = rows_inner(active_low, grad_branch)
    grad_back_bias = jnp.sum(grad_branch.astype(F32), axis=0)
    (grad_inner_f,) = gelu_back(times_transposed(grad_branch, proj_back))
    grad_inner = grad_inner_f.astype(BF16)
    grad_proj_in = rows_inner(normed_low, grad_inner)
    grad_in_bias = jnp.sum(grad_inner.astype(F32), axis=0)
    grad_first, grad_norm_one = norm_one_back(grad_second + times_transposed(grad_inner, proj_in))
    grad_attn = grad_first.astype(BF16)
    grad_proj_out = matmul(context_t, grad_attn)
    grad_out_bias = jnp.sum(grad_attn.astype(F32), axis=0)
    grad_context = times_transposed(grad_attn, proj_out).astype(BF16)
    grad_queries_t, grad_keys, grad_values, cells, diag = attention_backward(
        queries, keys, values, grad_context, probs, ops
    )
    table_grad = table_grads(cells, diag)
    grad_mixed = jnp.concatenate([grad_queries_t.T, grad_keys, grad_values], axis=1)
    grad_proj_qkv = rows_inner(start_low, grad_mixed)
    summed = jnp.sum(grad_mixed.astype(F32), axis=0)
    grad_qv_bias = jnp.stack([summed[:D], summed[2 * D :]])
    grad_start = grad_first + times_transposed(grad_mixed, proj_qkv)
    grad_start_low = grad_start.astype(BF16)
    grad_hidden = to_positions(grad_start_low.reshape(1, WINLEN, D))
    grad_proj_box = rows_inner(features, grad_start_low)
    grad_list = (
        grad_proj_qkv,
        grad_proj_out,
        grad_proj_box,
        grad_proj_in,
        grad_proj_back,
        grad_qv_bias,
        grad_out_bias,
        grad_norm_one,
        grad_in_bias,
        grad_back_bias,
        grad_norm_two,
        table_grad,
    )
    padding = jnp.zeros((shard_len * groups * lax.axis_size("dp") - USED,), BF16)
    grads_flat = jnp.concatenate([piece.astype(BF16).reshape(-1) for piece in grad_list] + [padding])
    grad_share = lax.psum_scatter(
        grads_flat, ("dp", "head"), scatter_dimension=0, tiled=True
    ).astype(F32)
    return finish_step(output_low, grad_hidden, grad_share, params, moment_one, moment_two)


def solution(mesh):
    placed = (
        P("dp", "head", None),
        P("dp", "head", None),
        P("dp", None, None),
        P("dp", None),
        P(("dp", "head")),
        P(("dp", "head")),
        P(("dp", "head")),
    )
    return jax.shard_map(
        fast_shards if fits(mesh) else plain_shards,
        mesh=mesh,
        in_specs=placed,
        out_specs=(
            P("dp", "head", None),
            P("dp", "head", None),
            P(("dp", "head")),
            P(("dp", "head")),
            P(("dp", "head")),
        ),
        check_vma=False,
    )
```

```python
import functools
import math

import jax
import jax.numpy as jnp
import numpy as np
from jax import lax
from jax.experimental import pallas as pl
from jax.experimental.pallas import tpu as pltpu
from jax.sharding import PartitionSpec as P

D = 768
HEADS = 12
FF = 3072
BUCKETS = 32
WINLEN = 512
HEAD_DIM = 64
PAIRS = HEADS // 2
LANES = 128
BLOCKS = WINLEN // LANES

beta_one = 0.9
beta_two = 0.999
adam_eps = 1e-08
norm_eps = 1e-05
base_rate = 0.001
layer_decay = 0.75
decay_weight = 0.01
adam_count = 100
coord_cell = 32
masked_score = -1e30

F32 = jnp.float32
BF16 = jnp.bfloat16


def layouts_list():
    return (
        (D, 3 * D),
        (D, D),
        (D, D),
        (D, FF),
        (FF, D),
        (2, D),
        (D,),
        (2, D),
        (FF,),
        (D,),
        (2, D),
        (3, HEADS, BUCKETS),
    )


def unpack(flat_params):
    pieces = []
    offset = 0
    for layout in layouts_list():
        elements = math.prod(layout)
        pieces.append(flat_params[offset : offset + elements].reshape(layout))
        offset += elements
    return pieces


def matmul(left_mat, right_mat):
    return jnp.dot(left_mat, right_mat, preferred_element_type=F32)


def rows_inner(left_mat, right_mat):
    return lax.dot_general(left_mat, right_mat, (((0,), (0,)), ((), ())), preferred_element_type=F32)


def times_transposed(left_mat, right_mat):
    return lax.dot_general(left_mat, right_mat, (((1,), (1,)), ((), ())), preferred_element_type=F32)


def layer_norm(values, gain_bias):
    row_mean = jnp.mean(values, axis=-1, keepdims=True)
    centred = values - row_mean
    spread = jnp.mean(centred * centred, axis=-1, keepdims=True)
    return centred * lax.rsqrt(spread + norm_eps) * gain_bias[0] + gain_bias[1]


def gelu_exact(values):
    return jax.nn.gelu(values, approximate=False)


def hot(index, count):
    return (np.asarray(index)[..., None] == np.arange(count)).astype(np.float32)


def clipped(steps):
    return np.clip(steps, -(BUCKETS // 2), BUCKETS // 2 - 1) + BUCKETS // 2


CELLS = np.arange(BUCKETS)
HOT_SAME = hot(clipped(CELLS[:, None] - CELLS[None, :]), BUCKETS)
HOT_LESS = hot(clipped(CELLS[:, None] - CELLS[None, :] - 1), BUCKETS)
WIDE = 6 * LANES
_U = np.arange(WIDE)
BAND_HOT = hot(np.where(_U < 5 * LANES, clipped(_U - 2 * LANES), 0), BUCKETS)
_V = np.arange(4 * LANES)
DIAG_HOT = np.concatenate(
    [
        hot(np.zeros(LANES, np.int64), BUCKETS),
        hot(np.where(_V < 3 * LANES, clipped(_V - LANES), 0), BUCKETS),
        hot(np.full(LANES, BUCKETS - 1), BUCKETS),
    ]
)


def window_layout(doc_lengths, box_coords):
    doc_ends = jnp.cumsum(doc_lengths, dtype=jnp.int32)
    doc_starts = doc_ends - doc_lengths
    places = jnp.arange(WINLEN, dtype=jnp.int32)
    doc_ids = jnp.sum(
        (places[:, None] >= doc_ends[None, :]).astype(jnp.int32), axis=1, dtype=jnp.int32
    )
    docs = jnp.arange(doc_lengths.shape[0], dtype=jnp.int32)
    chosen = doc_ids[:, None] == docs[None, :]
    first_hot = places[:, None] == doc_starts[None, :]
    first_box = jnp.sum(
        jnp.where(first_hot[:, :, None], box_coords[:, None, :], 0), axis=0, dtype=jnp.int32
    )
    anchor = jnp.sum(
        jnp.where(chosen[:, :, None], first_box[None, :, :], 0), axis=1, dtype=jnp.int32
    )
    relative = box_coords - jnp.concatenate([anchor[:, :2], anchor[:, :2]], axis=1)
    centre_x = (box_coords[:, 0] + box_coords[:, 2]) // 2
    centre_y = (box_coords[:, 1] + box_coords[:, 3]) // 2
    return chosen, relative, centre_x, centre_y


def box_features(relative):
    count_freq = D // 8
    steps = jnp.arange(count_freq, dtype=F32)
    frequency = jnp.exp(steps * (-math.log(1000.0) / count_freq))
    angles = relative.astype(F32)[:, :, None] * frequency[None, None, :]
    return jnp.concatenate([jnp.sin(angles), jnp.cos(angles)], axis=2).reshape(relative.shape[0], D)


def bias_operands(tables, chosen, centre_x, centre_y):
    cell_x, cell_y = centre_x // coord_cell, centre_y // coord_cell
    rest_x, rest_y = centre_x % coord_cell, centre_y % coord_cell
    cells = jnp.arange(BUCKETS, dtype=jnp.int32)
    hot_x = (cell_x[:, None] == cells[None, :]).astype(BF16)
    hot_y = (cell_y[:, None] == cells[None, :]).astype(BF16)
    none = jnp.zeros_like(hot_x)
    hot_two = jnp.concatenate([hot_x, hot_y, hot_x, hot_y], axis=1)
    key_x = jnp.stack(
        [
            jnp.concatenate([hot_x, -hot_x, none, none], axis=1),
            jnp.concatenate([none, none, hot_x, -hot_x], axis=1),
        ]
    )
    key_y = jnp.stack(
        [
            jnp.concatenate([hot_y, -hot_y, none, none], axis=1),
            jnp.concatenate([none, none, hot_y, -hot_y], axis=1),
        ]
    )
    same = jnp.einsum("qcb,thb->thqc", HOT_SAME.astype(BF16), tables[1:], preferred_element_type=F32)
    less = jnp.einsum("qcb,thb->thqc", HOT_LESS.astype(BF16), tables[1:], preferred_element_type=F32)
    zero = jnp.zeros_like(same[0])
    base = jnp.concatenate(
        [jnp.concatenate([same[0], zero], axis=2), jnp.concatenate([zero, same[1]], axis=2)], axis=1
    )
    base = base.reshape(PAIRS, 2, 64, 64)[:, ::-1].reshape(HEADS, 64, 64)
    diff_x = jnp.concatenate([jnp.concatenate([less[0], same[0]], axis=2), jnp.zeros((HEADS, 32, 64), F32)], axis=1)
    diff_y = jnp.concatenate([jnp.zeros((HEADS, 32, 64), F32), jnp.concatenate([less[1], same[1]], axis=2)], axis=1)
    rows = jnp.concatenate([base, diff_x, diff_y], axis=0).astype(BF16)
    rows = rows.transpose(1, 0, 2).reshape(64, 3 * D)
    met = matmul(hot_two[:, :64], rows).astype(BF16)
    band = matmul(tables[0], jnp.asarray(BAND_HOT.T, BF16)).reshape(HEADS, 1, WIDE)
    rest_cols = jnp.stack([rest_x, rest_y], axis=1).astype(F32)
    rest_rows = rest_cols.T
    pad = jnp.zeros((WINLEN, LANES - chosen.shape[1]), BF16)
    marks = chosen.astype(BF16)
    mark_keys = jnp.concatenate([marks, pad], axis=1)
    mark_queries = jnp.concatenate([(1 - marks) * jnp.asarray(masked_score, BF16), pad], axis=1)
    return dict(
        hot_two=hot_two,
        key_x=key_x,
        key_y=key_y,
        met=met,
        band=band,
        rest_cols=rest_cols,
        rest_rows=rest_rows,
        mark_keys=mark_keys,
        mark_queries=mark_queries,
    )


def half_masks():
    lane = lax.broadcasted_iota(jnp.int32, (1, LANES), 1)
    low = (lane < HEAD_DIM).astype(F32)
    return low.astype(BF16), (1.0 - low).astype(BF16)


def less_masks(rest_cols, rest_rows, less_x, less_y):
    for part in range(BLOCKS):
        rows = slice(part * LANES, (part + 1) * LANES)
        for axis, less in ((0, less_x), (1, less_y)):
            column = rest_cols[rows, axis : axis + 1]
            row = rest_rows[axis : axis + 1, :]
            less[rows, :] = jnp.where(row < column, 1.0, 0.0).astype(less.dtype)


def attention_forward_kernel(
    q_ref, k_ref, v_ref, hot_ref, keyx_ref, keyy_ref, met_ref, band_ref, cols_ref, rows_ref,
    mkey_ref, mquery_ref, probs_ref, context_ref,
    kaug, qaug, less_x, less_y, wide, scores,
):
    low, high = half_masks()
    less_masks(cols_ref, rows_ref, less_x, less_y)
    kaug[:, LANES:] = mkey_ref[...]
    qaug[:, LANES:] = mquery_ref[...]
    half = 2 * LANES

    def one_pair(pair, carry):
        at = pl.multiple_of(pair * LANES, LANES)
        lanes = pl.ds(at, LANES)
        lanes_x = pl.ds(pl.multiple_of(at + D, LANES), LANES)
        lanes_y = pl.ds(pl.multiple_of(at + 2 * D, LANES), LANES)
        values_t = v_ref[:, lanes].T
        for odd in range(2):
            own, other = (low, high) if odd == 0 else (high, low)
            head = 2 * pair + odd
            kaug[:, :LANES] = k_ref[:, lanes] * own + hot_ref[...] * other
            qaug[:, :LANES] = q_ref[:, lanes] * own + met_ref[:, lanes] * other
            skew_band(band_ref[head], wide)
            for side in range(2):
                cols = slice(side * half, (side + 1) * half)
                top = None
                for part in range(BLOCKS):
                    rows = slice(part * LANES, (part + 1) * LANES)
                    s = times_transposed(kaug[rows, :], qaug[cols, :])
                    dx = times_transposed(keyx_ref[odd, rows, :], met_ref[cols, lanes_x])
                    dy = times_transposed(keyy_ref[odd, rows, :], met_ref[cols, lanes_y])
                    bias = []
                    for block in range(2 * side, 2 * side + 2):
                        step = max(-2, min(2, block - part)) + 2
                        bias.append(wide[:, step * LANES : (step + 1) * LANES])
                    s = s + jnp.concatenate(bias, axis=1)
                    s = s + dx * less_x[rows, cols] + dy * less_y[rows, cols]
                    scores[rows, :] = s
                    best = jnp.max(s, axis=0, keepdims=True)
                    top = best if top is None else jnp.maximum(top, best)
                total = None
                for part in range(BLOCKS):
                    rows = slice(part * LANES, (part + 1) * LANES)
                    e = jnp.exp(scores[rows, :] - top)
                    scores[rows, :] = e
                    add = jnp.sum(e, axis=0, keepdims=True)
                    total = add if total is None else total + add
                share = 1.0 / total
                for part in range(BLOCKS):
                    rows = slice(part * LANES, (part + 1) * LANES)
                    probs_ref[head, rows, cols] = (scores[rows, :] * share).astype(BF16)
                got = matmul(
                    values_t[odd * HEAD_DIM : (odd + 1) * HEAD_DIM, :], probs_ref[head, :, cols]
                )
                context_ref[pl.ds(pl.multiple_of(head * HEAD_DIM, HEAD_DIM), HEAD_DIM), cols] = (
                    got.astype(BF16)
                )
        return carry

    lax.fori_loop(0, PAIRS, one_pair, 0)


def skew_band(row, wide):
    x = jnp.broadcast_to(row, (8, WIDE))
    sub = lax.broadcasted_iota(jnp.int32, (8, WIDE), 0)
    for bit in (1, 2, 4):
        x = jnp.where((sub & bit) != 0, pltpu.roll(x, bit, 1), x)
    for group in range(LANES // 8):
        y = x if group == 0 else pltpu.roll(x, 8 * group, 1)
        wide[8 * group : 8 * group + 8, :] = y[:, : 5 * LANES]


def skew_groups(skewed, wide):
    for group in range(LANES // 8):
        y = skewed if group == 0 else pltpu.roll(skewed, 8 * group, 1)
        wide[8 * group : 8 * group + 8, :] = y[:, : 5 * LANES]


def diagonal_sums(parts):
    total = None
    for group in range(LANES // 8):
        x = jnp.concatenate(
            [parts[8 * group : 8 * group + 8, LANES : 4 * LANES], jnp.zeros((8, LANES), F32)], axis=1
        )
        y = x if group == 0 else pltpu.roll(x, 4 * LANES - 8 * group, 1)
        total = y if total is None else total + y
    sub = lax.broadcasted_iota(jnp.int32, (8, 4 * LANES), 0)
    for bit in (1, 2, 4):
        total = jnp.where((sub & bit) != 0, pltpu.roll(total, 4 * LANES - bit, 1), total)
    return jnp.sum(total, axis=0, keepdims=True)


def attention_backward_kernel(
    q_ref, k_ref, v_ref, dctx_ref, probs_ref, hot_ref, cols_ref, rows_ref,
    dq_ref, dk_ref, dv_ref, cells_ref, diag_ref,
    qaug, less_x, less_y, scores, dscores, band, kept, hot_t,
):
    low, high = half_masks()
    less_masks(cols_ref, rows_ref, less_x, less_y)
    hot_t[...] = hot_ref[...].T
    lane = lax.broadcasted_iota(jnp.int32, (1, LANES), 1)
    scale = HEAD_DIM ** (-0.5)
    of_x = jnp.where((lane // BUCKETS) % 2 == 0, 1.0, 0.0)
    cells_x = hot_ref[...] * of_x.astype(BF16)
    cells_y = hot_ref[...] * (1.0 - of_x).astype(BF16)

    def one_pair(pair, carry):
        at = pl.multiple_of(pair * LANES, LANES)
        lanes = pl.ds(at, LANES)
        keys_t = k_ref[:, lanes].T
        for odd in range(2):
            own, other = (low, high) if odd == 0 else (high, low)
            head = 2 * pair + odd
            qaug[...] = q_ref[:, lanes] * own + hot_ref[...] * other
            dctx = dctx_ref[:, lanes]
            dot = None
            for part in range(BLOCKS):
                rows = slice(part * LANES, (part + 1) * LANES)
                dp = times_transposed(v_ref[rows, lanes] * own, dctx)
                scores[rows, :] = dp
                add = jnp.sum(dp * probs_ref[head, rows, :].astype(F32), axis=0, keepdims=True)
                dot = add if dot is None else dot + add
            band[...] = jnp.zeros_like(band)
            for part in range(BLOCKS):
                rows = slice(part * LANES, (part + 1) * LANES)
                probs = probs_ref[head, rows, :]
                ds = probs.astype(F32) * (scores[rows, :] - dot)
                for block in range(BLOCKS):
                    step = max(-2, min(2, block - part)) + 2
                    where = slice(step * LANES, (step + 1) * LANES)
                    band[:, where] = band[:, where] + ds[:, block * LANES : (block + 1) * LANES]
                ds = ds.astype(BF16)
                dscores[rows, :] = ds
                both = matmul(ds, qaug[...])
                less = matmul(ds * less_x[rows, :], cells_x) + matmul(ds * less_y[rows, :], cells_y)
                dv = matmul(probs, dctx)
                kept[odd, 0, rows, :] = both
                kept[odd, 1, rows, :] = less
                kept[odd, 2, rows, :] = dv
            got = matmul(keys_t[odd * HEAD_DIM : (odd + 1) * HEAD_DIM, :], dscores[...])
            dq_ref[pl.ds(pl.multiple_of(head * HEAD_DIM, HEAD_DIM), HEAD_DIM), :] = (
                got * scale
            ).astype(BF16)
            diag_ref[head, :, LANES : 5 * LANES] = diagonal_sums(band)
            diag_ref[head, :, :LANES] = jnp.sum(band[:, :LANES], axis=0, keepdims=True)
            diag_ref[head, :, 5 * LANES :] = jnp.sum(band[:, 4 * LANES :], axis=0, keepdims=True)
            for which in range(2):
                summed = kept[odd, which]
                first = summed.astype(BF16)
                rest = (summed - first.astype(F32)).astype(BF16)
                cells_ref[head, which] = matmul(hot_t[:64, :], first) + matmul(hot_t[:64, :], rest)
        dk_ref[:, lanes] = jnp.where(lane < HEAD_DIM, kept[0, 0], kept[1, 0]).astype(BF16)
        dv_ref[:, lanes] = jnp.where(lane < HEAD_DIM, kept[0, 2], kept[1, 2]).astype(BF16)
        return carry

    lax.fori_loop(0, PAIRS, one_pair, 0)


def attention_forward(queries, keys, values, ops):
    return pl.pallas_call(
        attention_forward_kernel,
        out_shape=(
            jax.ShapeDtypeStruct((HEADS, WINLEN, WINLEN), BF16),
            jax.ShapeDtypeStruct((D, WINLEN), BF16),
        ),
        scratch_shapes=[
            pltpu.VMEM((WINLEN, 2 * LANES), BF16),
            pltpu.VMEM((WINLEN, 2 * LANES), BF16),
            pltpu.VMEM((WINLEN, WINLEN), F32),
            pltpu.VMEM((WINLEN, WINLEN), F32),
            pltpu.VMEM((LANES, 5 * LANES), F32),
            pltpu.VMEM((WINLEN, 2 * LANES), F32),
        ],
        compiler_params=pltpu.CompilerParams(vmem_limit_bytes=48 * 2**20),
        name="attention_forward",
    )(
        queries, keys, values, ops["hot_two"], ops["key_x"], ops["key_y"], ops["met"], ops["band"],
        ops["rest_cols"], ops["rest_rows"], ops["mark_keys"], ops["mark_queries"],
    )


def attention_backward(queries, keys, values, grad_context, probs, ops):
    return pl.pallas_call(
        attention_backward_kernel,
        out_shape=(
            jax.ShapeDtypeStruct((D, WINLEN), BF16),
            jax.ShapeDtypeStruct((WINLEN, D), BF16),
            jax.ShapeDtypeStruct((WINLEN, D), BF16),
            jax.ShapeDtypeStruct((HEADS, 2, 64, LANES), F32),
            jax.ShapeDtypeStruct((HEADS, 1, WIDE), F32),
        ),
        scratch_shapes=[
            pltpu.VMEM((WINLEN, LANES), BF16),
            pltpu.VMEM((WINLEN, WINLEN), BF16),
            pltpu.VMEM((WINLEN, WINLEN), BF16),
            pltpu.VMEM((WINLEN, WINLEN), F32),
            pltpu.VMEM((WINLEN, WINLEN), BF16),
            pltpu.VMEM((LANES, 5 * LANES), F32),
            pltpu.VMEM((2, 3, WINLEN, LANES), F32),
            pltpu.VMEM((LANES, WINLEN), BF16),
        ],
        compiler_params=pltpu.CompilerParams(vmem_limit_bytes=48 * 2**20),
        name="attention_backward",
    )(
        queries, keys, values, grad_context, probs, ops["hot_two"], ops["rest_cols"],
        ops["rest_rows"],
    )


def table_grads(cells, diag):
    exact = lax.Precision.HIGHEST
    pairs = cells.reshape(PAIRS, 2, 2, 64, LANES)
    every = jnp.stack([pairs[:, 0, 0, :, 64:], pairs[:, 1, 0, :, :64]], axis=1).reshape(HEADS, 64, 64)
    less = cells[:, 1]
    less_x, less_y = less[:, :32, :32], less[:, 32:, 32:64]
    all_x, all_y = every[:, :32, :32], every[:, 32:, 32:]
    same = jnp.stack([all_x - less_x, all_y - less_y]).reshape(2 * HEADS, -1)
    below = jnp.stack([less_x, less_y]).reshape(2 * HEADS, -1)
    same_hot = jnp.asarray(HOT_SAME.transpose(1, 0, 2).reshape(-1, BUCKETS))
    less_hot = jnp.asarray(HOT_LESS.transpose(1, 0, 2).reshape(-1, BUCKETS))
    moved = jnp.dot(same, same_hot, precision=exact) + jnp.dot(below, less_hot, precision=exact)
    along = jnp.dot(diag.reshape(HEADS, WIDE), jnp.asarray(DIAG_HOT), precision=exact)
    return jnp.concatenate([along[None], moved.reshape(2, HEADS, BUCKETS)], axis=0)


COLUMNS = 4
CORES = 2
DEPTH = 4
USED = sum(math.prod(layout) for layout in layouts_list())
MATRICES = layouts_list()[:5]
MISC = sum(math.prod(layout) for layout in layouts_list()[5:])
MISC_ROWS = -(-MISC // (8 * LANES)) * 8


class Plan:
    def __init__(self, shard_len, carry=3 * LANES):
        self.rows = shard_len // LANES
        self.quarter = -(-self.rows // (16 * COLUMNS)) * 16
        self.padded = COLUMNS * self.quarter
        self.per_column = CORES * DEPTH * self.rows
        self.carry = carry
        self.staged = self.carry + self.per_column + 3 * LANES
        starts = []
        offset = 0
        for depth, width in MATRICES:
            starts.append(offset // LANES)
            offset += depth * width
        self.starts = starts
        self.misc_start = offset // LANES


def fits(mesh):
    return mesh.shape["dp"] == COLUMNS * CORES and mesh.shape["head"] == DEPTH


MESH = pl.DeviceIdType.MESH


class Place:
    def __init__(self):
        dp = lax.axis_index("dp")
        self.z = lax.axis_index("head")
        self.core = dp % CORES
        self.column = dp // CORES
        self.x = self.column % 2
        self.y = self.column // 2
        self.col_x = 2 * self.y + (1 - self.x)
        self.col_y = 2 * (1 - self.y) + self.x
        self.col_d = 2 * (1 - self.y) + (1 - self.x)
        self.peer_x = self.at(self.col_x, self.core, self.z)
        self.peer_y = self.at(self.col_y, self.core, self.z)
        self.peer_d = self.at(self.col_d, self.core, self.z)
        self.peer_core = self.at(self.column, 1 - self.core, self.z)
        self.far = [lax.rem(self.z + d, DEPTH) for d in range(1, DEPTH)]
        self.from_far = [lax.rem(self.z + DEPTH - d, DEPTH) for d in range(1, DEPTH)]
        self.peers_z = [self.at(self.column, self.core, f) for f in self.far]

    def at(self, column, core, z):
        return {"dp": column * CORES + core, "head": z}

    def greet(self):
        barrier = pltpu.get_barrier_semaphore()
        peers = [self.peer_x, self.peer_y, self.peer_d, self.peer_core] + self.peers_z
        for peer in peers:
            pl.semaphore_signal(barrier, inc=1, device_id=peer, device_id_type=MESH)
        pl.semaphore_wait(barrier, len(peers))


def remote(src, dst, send_sem, recv_sem, peer):
    return pltpu.make_async_remote_copy(
        src_ref=src, dst_ref=dst, send_sem=send_sem, recv_sem=recv_sem, device_id=peer,
        device_id_type=MESH,
    )


class Gathering:
    def __init__(self, place, flat, sems):
        self.place = place
        self.flat = flat
        self.sems = sems
        self.sent = []

    def send(self, src, dst, kind, index, peer):
        copy = remote(src, dst, self.sems[kind].at[0, index], self.sems[kind].at[1, index], peer)
        copy.start()
        self.sent.append(copy)

    def got(self, dst, kind, index):
        remote(
            dst, dst, self.sems[kind].at[0, index], self.sems[kind].at[1, index], self.place.peer_x
        ).wait_recv()

    def spread(self, own):
        p = self.place
        for index, (column, peer) in enumerate(
            ((p.col_x, p.peer_x), (p.col_y, p.peer_y), (p.col_d, p.peer_d))
        ):
            self.send(
                own.at[column], self.flat.at[p.column, p.core, p.z, column], "spread", index, peer
            )
        self.flat[p.column, p.core, p.z, p.column] = own[p.column]

    def spread_done(self):
        p = self.place
        for index, column in enumerate((p.col_x, p.col_y, p.col_d)):
            self.got(self.flat.at[column, p.core, p.z, p.column], "spread", index)

    def along_z(self, k):
        p = self.place
        piece = self.flat.at[k, p.core, p.z, p.column]
        for d in range(DEPTH - 1):
            self.send(piece, piece, "z", 3 * k + d, p.peers_z[d])

    def first(self, k):
        p = self.place
        for d in range(DEPTH - 1):
            self.got(self.flat.at[k, p.core, p.from_far[d], p.column], "z", 3 * k + d)
        piece = self.flat.at[k, p.core, :, p.column]
        self.send(piece, piece, "one", 2 * k, p.peer_x)
        self.send(piece, piece, "one", 2 * k + 1, p.peer_y)
        self.send(piece, piece, "core", 5 * k, p.peer_core)

    def second(self, k):
        p = self.place
        from_x = self.flat.at[k, p.core, :, p.col_x]
        self.got(from_x, "one", 2 * k)
        part = self.flat.at[k, p.core, 0:2, p.col_x]
        self.send(part, part, "two", 2 * k, p.peer_y)
        self.send(from_x, from_x, "core", 5 * k + 1, p.peer_core)
        from_y = self.flat.at[k, p.core, :, p.col_y]
        self.got(from_y, "one", 2 * k + 1)
        part = self.flat.at[k, p.core, 2:4, p.col_y]
        self.send(part, part, "two", 2 * k + 1, p.peer_x)
        self.send(from_y, from_y, "core", 5 * k + 2, p.peer_core)

    def third(self, k):
        p = self.place
        part = self.flat.at[k, p.core, 0:2, p.col_d]
        self.got(part, "two", 2 * k)
        self.send(part, part, "core", 5 * k + 3, p.peer_core)
        part = self.flat.at[k, p.core, 2:4, p.col_d]
        self.got(part, "two", 2 * k + 1)
        self.send(part, part, "core", 5 * k + 4, p.peer_core)

    def complete(self, k):
        p = self.place
        other = 1 - p.core
        for index, column in enumerate((p.column, p.col_x, p.col_y)):
            self.got(self.flat.at[k, other, :, column], "core", 5 * k + index)
        self.got(self.flat.at[k, other, 0:2, p.col_d], "core", 5 * k + 3)
        self.got(self.flat.at[k, other, 2:4, p.col_d], "core", 5 * k + 4)

    def finish(self):
        for copy in self.sent:
            copy.wait_send()


GATHER_SEMS = {"spread": 3, "z": 12, "one": 8, "two": 8, "core": 20}


def sem_shapes(counts):
    return [pltpu.SemaphoreType.DMA((2, count)) for count in counts.values()]


def stage_column(plan, flat, staged, k):
    def one(shard, carry):
        core, z = shard // DEPTH, shard % DEPTH
        for quarter in range(COLUMNS):
            base = plan.carry + shard * plan.rows + quarter * plan.quarter
            staged[pl.ds(pl.multiple_of(base, 8), plan.quarter), :] = flat[k, core, z, quarter].astype(F32)
        return carry

    lax.fori_loop(0, CORES * DEPTH, one, 0)


def keep_carry(plan, staged):
    end = plan.carry + plan.per_column
    staged[: plan.carry, :] = staged[end - plan.carry : end, :]


ROW_STEP = 48


def column_rows(plan, k, touching):
    low, high = k * plan.per_column, (k + 1) * plan.per_column
    taken = []
    for index, (depth, width) in enumerate(MATRICES):
        group = 16 * (width // LANES)
        from_low, from_high = low - plan.starts[index], high - plan.starts[index]
        begin = max(0, min(depth, from_low // group * 16))
        if touching:
            end = max(0, min(depth, -(-from_high // group) * 16))
        else:
            end = max(0, min(depth, from_high // group * 16))
        if end > begin:
            taken.append((index, begin, end))
    return taken


def staged_at(plan, k, row):
    return plan.carry + row - k * plan.per_column


def row_loops(rows):
    whole = rows // ROW_STEP
    loops = [(ROW_STEP, 0, whole)] if whole else []
    if rows % ROW_STEP:
        loops.append((16, whole * ROW_STEP, (rows % ROW_STEP) // 16))
    return loops


def form_matrices(plan, staged, matrices, k):
    for index, begin, end in column_rows(plan, k, False):
        blocks = MATRICES[index][1] // LANES
        base = staged_at(plan, k, plan.starts[index] + begin * blocks)
        assert 0 <= base
        target = matrices[index]
        for step_rows, first, count in row_loops(end - begin):

            def one(step, carry, step_rows=step_rows, first=first, blocks=blocks, base=base,
                    begin=begin, target=target):
                row = first + step * step_rows
                for block in range(blocks):
                    got = staged[pl.ds(base + row * blocks + block, step_rows, stride=blocks), :]
                    target[
                        pl.ds(pl.multiple_of(begin + row, 16), step_rows),
                        block * LANES : (block + 1) * LANES,
                    ] = got.astype(BF16)
                return carry

            lax.fori_loop(0, count, one, 0)


def adam_step(params, moment_one, moment_two, grads, flat_index):
    box_part = (flat_index >= 4 * D * D) & (flat_index < 5 * D * D)
    step_rate = jnp.where(box_part, base_rate * layer_decay**12, base_rate * layer_decay)
    decay_mask = jnp.where(flat_index < 5 * D * D + 2 * D * FF, decay_weight, 0.0)
    moment_one = beta_one * moment_one + (1.0 - beta_one) * grads
    moment_two = beta_two * moment_two + (1.0 - beta_two) * grads * grads
    first_hat = moment_one / (1.0 - beta_one**adam_count)
    second_hat = moment_two / (1.0 - beta_two**adam_count)
    update = first_hat / (jnp.sqrt(second_hat) + adam_eps) + decay_mask * params
    return (-step_rate * update, moment_one)


VEC = {}
_at = 0
for _name, _rows in (
    ("q_bias", 6), ("v_bias", 6), ("out_bias", 6), ("gain_one", 6), ("shift_one", 6), ("in_bias", 24),
    ("back_bias", 6), ("gain_two", 6), ("shift_two", 6), ("tables", 9),
):
    VEC[_name] = _at * LANES
    _at += _rows
VEC_ROWS = _at
NOTE_ROWS = 96
NBLOCK = 2 * LANES


def note_place(plan):
    row = plan.misc_start - (CORES * DEPTH * COLUMNS - 1) * plan.rows
    quarter, row = row // plan.quarter, row % plan.quarter
    first = row // 16 * 16
    assert first + NOTE_ROWS <= plan.quarter and row - first + VEC_ROWS <= NOTE_ROWS
    return quarter, first, row - first


def spread_notes(place, own, notes, sems, plan):
    quarter, first, _ = note_place(plan)
    source = own.at[quarter, first : first + NOTE_ROWS]
    home = (place.column == COLUMNS - 1) & (place.core == CORES - 1)
    root = home & (place.z == DEPTH - 1)

    def copy(src, index, peer):
        return remote(src, notes, sems.at[0, index], sems.at[1, 0], peer)

    def arrived():
        copy(notes, 0, place.peer_core).wait_recv()

    @pl.when(root)
    def _():
        notes[...] = own[quarter, first : first + NOTE_ROWS]
        for index, peer in enumerate(place.peers_z):
            copy(source, index, peer).start()

    @pl.when(home & (place.z != DEPTH - 1))
    def _():
        arrived()

    @pl.when(home)
    def _():
        for index, peer in enumerate((place.peer_x, place.peer_y, place.peer_d)):
            copy(notes, 3 + index, peer).start()

    @pl.when((place.core == CORES - 1) & (place.column != COLUMNS - 1))
    def _():
        arrived()

    @pl.when(place.core == CORES - 1)
    def _():
        copy(notes, 6, place.peer_core).start()

    @pl.when(place.core != CORES - 1)
    def _():
        arrived()

    def finish():
        @pl.when(root)
        def _():
            for index, peer in enumerate(place.peers_z):
                copy(source, index, peer).wait_send()

        @pl.when(home)
        def _():
            for index, peer in enumerate((place.peer_x, place.peer_y, place.peer_d)):
                copy(notes, 3 + index, peer).wait_send()

        @pl.when(place.core == CORES - 1)
        def _():
            copy(notes, 6, place.peer_core).wait_send()

    return finish


def turns_table():
    count_freq = D // 8
    freq = np.exp(np.arange(count_freq) * (-math.log(1000.0) / count_freq)) / (2 * math.pi)
    per = np.concatenate([freq, freq])
    phase = np.concatenate([np.zeros(count_freq), np.full(count_freq, 0.25)])
    return np.stack([np.tile(per, 4), np.tile(phase, 4)]).astype(np.float32)


def sin_turns(t):
    t = t - jnp.floor(t + 0.5)
    a = jnp.abs(t)
    m = jnp.minimum(a, 0.5 - a) * (2 * math.pi)
    u = m * m
    poly = -1.0 / 39916800.0
    for term in (1.0 / 362880.0, -1.0 / 5040.0, 1.0 / 120.0, -1.0 / 6.0, 1.0):
        poly = poly * u + term
    s = m * poly
    return jnp.where(t < 0, -s, s)


def token_columns(boxes, lengths, window):
    coords = boxes[window].astype(F32)
    place = lax.broadcasted_iota(jnp.int32, (1, WINLEN), 1)
    doc = jnp.zeros((1, WINLEN), F32)
    anchor = jnp.zeros_like(coords)
    begin = 0
    for d in range(4):
        end = begin + lengths[window, d]
        mine = jnp.where((place >= begin) & (place < end), 1.0, 0.0)
        value = jnp.sum(coords * jnp.where(place == begin, 1.0, 0.0), axis=1, keepdims=True)
        anchor = anchor + value * mine
        doc = doc + mine * float(d)
        begin = end
    anchor = jnp.concatenate([anchor[0:2], anchor[0:2]], axis=0)
    relative = coords - anchor
    centre = jnp.floor((coords[0:2] + coords[2:4]) * 0.5)
    cell = jnp.floor(centre * (1.0 / coord_cell))
    rest = centre - cell * coord_cell
    rows = jnp.concatenate(
        [relative, cell, rest, doc, jnp.zeros((LANES - 9, WINLEN), F32)], axis=0
    )
    return rest, rows.T


def form_features(columns, turns_ref, features):
    lane = lax.broadcasted_iota(jnp.int32, (1, LANES), 1)
    for block in range(D // LANES):
        lanes = slice(block * LANES, (block + 1) * LANES)
        low, high = block * LANES // (D // 4), ((block + 1) * LANES - 1) // (D // 4)
        value = columns[:, low : low + 1]
        if high != low:
            value = jnp.where(
                lane + block * LANES < high * (D // 4), value, columns[:, high : high + 1]
            )
        t = value * turns_ref[0:1, lanes] + turns_ref[1:2, lanes]
        features[:, lanes] = sin_turns(t).astype(BF16)


def form_hots(columns, hot_ref, keyx_ref, keyy_ref, mkey, mquery):
    lane = lax.broadcasted_iota(jnp.int32, (1, LANES), 1)
    part = lane // BUCKETS
    cell = (lane % BUCKETS).astype(F32)
    is_x = jnp.where(columns[:, 4:5] == cell, 1.0, 0.0)
    is_y = jnp.where(columns[:, 5:6] == cell, 1.0, 0.0)
    hot_ref[...] = jnp.where(part % 2 == 0, is_x, is_y).astype(BF16)
    sign = jnp.where(part % 2 == 0, 1.0, -1.0)
    for odd in range(2):
        here = jnp.where(part // 2 == odd, sign, 0.0)
        keyx_ref[odd] = (is_x * here).astype(BF16)
        keyy_ref[odd] = (is_y * here).astype(BF16)
    doc = jnp.where(columns[:, 8:9] == lane.astype(F32), 1.0, 0.0)
    mkey[:, LANES:] = doc.astype(BF16)
    mquery[:, LANES:] = (jnp.where(lane < 4, 1.0 - doc, 0.0) * masked_score).astype(BF16)


def form_tables(tables, bands, tilted):
    row = lax.broadcasted_iota(jnp.int32, (LANES, 1), 0)
    half = BUCKETS // 2
    sub = lax.broadcasted_iota(jnp.int32, (8, LANES), 0)
    sub_wide = lax.broadcasted_iota(jnp.int32, (8, WIDE), 0)
    place = lax.broadcasted_iota(jnp.int32, (1, WIDE), 1)
    wanted = jnp.where(place < 5 * LANES, jnp.clip(place - 2 * LANES, -half, half - 1) + half, 0)
    lane = lax.broadcasted_iota(jnp.int32, (1, LANES), 1)
    turned = jnp.clip(64 - lane, -half, half - 1) + half
    for m in range(4):
        hot_band = jnp.where(row == wanted + m * BUCKETS, 1.0, 0.0).astype(BF16)
        got = matmul(tables, hot_band)
        for n in range(3):
            x = jnp.broadcast_to(got[n : n + 1, :], (8, WIDE))
            for bit in (1, 2, 4):
                x = jnp.where((sub_wide & bit) != 0, pltpu.roll(x, bit, 1), x)
            bands[4 * n + m] = x
        hot_turn = jnp.where(row == turned + m * BUCKETS, 1.0, 0.0).astype(BF16)
        got = matmul(tables, hot_turn)
        for t in (1, 2):
            for n in range(3):
                x = jnp.broadcast_to(got[3 * t + n : 3 * t + n + 1, :], (8, LANES))
                for bit in (1, 2, 4):
                    x = jnp.where((sub & bit) != 0, pltpu.roll(x, bit, 1), x)
                for group in range(BUCKETS // 8):
                    y = x if group == 0 else pltpu.roll(x, 8 * group, 1)
                    tilted[(t - 1) * HEADS + 4 * n + m, 8 * group : 8 * group + 8, :] = y


def pair_rows(tilted, pair):
    lane = lax.broadcasted_iota(jnp.int32, (1, LANES), 1)
    part = lane // BUCKETS
    x0, x1 = tilted[2 * pair], tilted[2 * pair + 1]
    y0, y1 = tilted[HEADS + 2 * pair], tilted[HEADS + 2 * pair + 1]

    def same(value, to):
        return value if to == 64 else pltpu.roll(value, (to - 64) % LANES, 1)

    def less(value, to):
        return pltpu.roll(value, (to - 65) % LANES, 1)

    zero = jnp.zeros_like(x0)
    base_x = jnp.where(part == 0, same(x1, 0), jnp.where(part == 2, same(x0, 64), zero))
    base_y = jnp.where(part == 1, same(y1, 32), jnp.where(part == 3, same(y0, 96), zero))

    def steps(even, odd):
        return jnp.where(
            part < 2,
            jnp.where(part == 0, less(even, 0), same(even, 32)),
            jnp.where(part == 2, less(odd, 64), same(odd, 96)),
        )

    rows = [
        jnp.concatenate([base_x, base_y], axis=0),
        jnp.concatenate([steps(x0, x1), zero], axis=0),
        jnp.concatenate([zero, steps(y0, y1)], axis=0),
    ]
    return jnp.concatenate(rows, axis=1).astype(BF16)


def gelu_and_slope(z):
    a = jnp.abs(z)
    t = 1.0 / (1.0 + (0.3275911 / math.sqrt(2.0)) * a)
    poly = 1.061405429 * 0.5
    for term in (-1.453152027, 1.421413741, -0.284496736, 0.254829592):
        poly = poly * t + 0.5 * term
    e = jnp.exp(-0.5 * z * z)
    tail = poly * t * e
    cdf = jnp.where(z < 0, tail, 1.0 - tail)
    return z * cdf, cdf + z * (e * (1.0 / math.sqrt(2.0 * math.pi)))


def forward_kernel(plan, params_in, hidden_in, cot_in, boxes, lengths, turns, *refs):
    (w_qkv_out, w_out_out, w_in_out, w_back_out, features_out, low_out, q_out, k_out, v_out, probs_out,
     context_out, hat_out, normed_out, active_out, slope_out, second_out, vec_out, rstd_out, gain_grads,
     output_ref, cot_ref, hot_out, rest_out, share_out) = refs[:24]
    refs = refs[24:]
    (flat, staged, own, w_qkv, w_out, w_box, w_in, w_back, notes, features, hidden, start, start_low, q_ref,
     k_ref, v_ref, hot_ref, key_x, key_y, bands, tilted, wides, scores, context_t, pair_t, hat, active,
     slope, vec) = refs[:29]
    note_sems, swap_sems, copy_sems, probs_sems = refs[29:33]

    def lend(buffer, slot, lanes):
        return buffer.at[:, slot : slot + lanes]

    less_x, less_y = lend(slope, 0, WINLEN), lend(slope, WINLEN, WINLEN)
    probs = [lend(slope, 2 * WINLEN, WINLEN), lend(slope, 3 * WINLEN, WINLEN)]
    kaugs = [lend(active, 0, 2 * LANES), lend(active, 2 * LANES, 2 * LANES)]
    qaugs = [lend(active, 4 * LANES, 2 * LANES), lend(active, 6 * LANES, 2 * LANES)]
    met = lend(active, 8 * LANES, 3 * LANES)
    place = Place()
    normed_low = hidden
    context = features
    gathering = Gathering(place, flat, dict(zip(GATHER_SEMS, refs[33:])))
    matrices = (w_qkv, w_out, w_box, w_in, w_back)
    written = []

    def write_out(src, dst):
        copy = pltpu.make_async_copy(src, dst, copy_sems.at[len(written)])
        copy.start()
        written.append(copy)

    fetch = pltpu.make_async_copy(params_in, staged.at[: plan.rows], probs_sems.at[0])
    fetch.start()
    place.greet()
    fetch.wait()
    for quarter_at in range(COLUMNS):
        begin = quarter_at * plan.quarter
        own[quarter_at] = staged[begin : begin + plan.quarter, :].astype(BF16)
    gathering.spread(own)

    quarter = WINLEN // DEPTH

    def exchange(source, target, kind):
        rows = pl.ds(pl.multiple_of(place.z * quarter, quarter), quarter)
        for d in range(DEPTH - 1):
            gathering_send(source.at[place.far[d]], target.at[rows], kind, d, place.peers_z[d])

    def gathering_send(src, dst, kind, d, peer):
        copy = remote(src, dst, swap_sems.at[kind, 0, d], swap_sems.at[kind, 1, d], peer)
        copy.start()
        gathering.sent.append(copy)

    def exchanged(target, kind):
        for d in range(DEPTH - 1):
            rows = pl.ds(pl.multiple_of(place.from_far[d] * quarter, quarter), quarter)
            remote(
                target.at[rows], target.at[rows], swap_sems.at[kind, 0, d], swap_sems.at[kind, 1, d],
                place.peer_x,
            ).wait_recv()

    finish_notes = spread_notes(place, own, notes, note_sems, plan)
    own_rows = pl.ds(pl.multiple_of(place.z * quarter, quarter), quarter)
    own_hidden = pltpu.make_async_copy(
        hidden_in.at[place.z], hidden.at[own_rows], swap_sems.at[0, 0, DEPTH - 1]
    )
    own_hidden.start()
    own_cot = pltpu.make_async_copy(
        cot_in.at[place.z], cot_ref.at[own_rows], swap_sems.at[1, 0, DEPTH - 1]
    )
    own_cot.start()
    gathering.spread_done()
    gathering.along_z(0)

    rest, columns = token_columns(boxes, lengths, place.z)
    for part in range(BLOCKS):
        rows = slice(part * LANES, (part + 1) * LANES)
        for axis, less in ((0, less_x), (1, less_y)):
            less[rows, :] = jnp.where(
                rest[axis : axis + 1, :] < columns[rows, 6 + axis : 7 + axis], 1.0, 0.0
            ).astype(BF16)
    rest_out[...] = rest
    form_hots(columns, hot_ref, key_x, key_y, kaugs[0], qaugs[0])
    kaugs[1][:, LANES:] = kaugs[0][:, LANES:]
    qaugs[1][:, LANES:] = qaugs[0][:, LANES:]
    hot_out[...] = hot_ref[...]
    gathering.first(0)
    gathering.along_z(1)
    form_features(columns, turns, features)
    for n in range(D // LANES):
        rows = slice(n * LANES, (n + 1) * LANES)
        context_t[rows, :] = features[:, rows].T
    write_out(context_t, features_out)
    gathering.first(1)
    exchange(hidden_in, hidden, 0)
    gathering.second(0)
    _, _, note_row = note_place(plan)
    for row in range(VEC_ROWS):
        at = note_row + row
        vec[0:1, row * LANES : (row + 1) * LANES] = notes[at // 16 * 16 : at // 16 * 16 + 16, :].astype(
            F32
        )[at % 16 : at % 16 + 1, :]
    vec_out[...] = vec[...]
    table_row = note_row + VEC["tables"] // LANES
    assert table_row % 16 == 0
    form_tables(notes[table_row : table_row + 16, :], bands, tilted)

    gathering.second(1)
    gathering.third(0)
    gathering.complete(0)
    stage_column(plan, flat, staged, 0)
    exchanged(hidden, 0)
    gathering.along_z(2)
    form_matrices(plan, staged, matrices, 0)
    keep_carry(plan, staged)
    gathering.third(1)
    gathering.complete(1)
    stage_column(plan, flat, staged, 1)
    form_matrices(plan, staged, matrices, 1)
    keep_carry(plan, staged)
    write_out(w_qkv, w_qkv_out)
    write_out(w_out, w_out_out)

    own_hidden.wait()
    for n in range(D // NBLOCK):
        lanes = slice(n * NBLOCK, (n + 1) * NBLOCK)
        value = hidden[:, lanes].astype(F32) + matmul(features[...], w_box[:, lanes])
        start[:, lanes] = value
        start_low[:, lanes] = value.astype(BF16)
    write_out(start_low, low_out)
    written[0].wait()

    def project(n, carry):
        at = pl.multiple_of(n * NBLOCK, NBLOCK)
        lanes = pl.ds(at, NBLOCK)
        low = start_low[...]
        bias = vec[0:1, pl.ds(pl.multiple_of(VEC["q_bias"] + at, LANES), NBLOCK)]
        got = matmul(low, w_qkv[:, lanes]) + bias
        q_ref[:, lanes] = (got.astype(BF16).astype(F32) * HEAD_DIM ** (-0.5)).astype(BF16)
        k_ref[:, lanes] = matmul(low, w_qkv[:, pl.ds(pl.multiple_of(at + D, LANES), NBLOCK)]).astype(BF16)
        bias = vec[0:1, pl.ds(pl.multiple_of(VEC["v_bias"] + at, LANES), NBLOCK)]
        got = matmul(low, w_qkv[:, pl.ds(pl.multiple_of(at + 2 * D, LANES), NBLOCK)]) + bias
        v_ref[:, lanes] = got.astype(BF16)
        return carry

    lax.fori_loop(0, D // NBLOCK, project, 0)
    write_out(q_ref, q_out)
    write_out(k_ref, k_out)
    write_out(v_ref, v_out)
    gathering.first(2)
    gathering.along_z(3)

    low, high = half_masks()
    half = 2 * LANES

    def probs_copy(head, odd):
        return pltpu.make_async_copy(probs[odd], probs_out.at[head], probs_sems.at[odd])

    def one_pair(pair, carry):
        at = pl.multiple_of(pair * LANES, LANES)
        lanes = pl.ds(at, LANES)
        values_t = v_ref[:, lanes].T
        met[...] = matmul(hot_ref[:, :64], pair_rows(tilted, pair)).astype(BF16)
        for odd in range(2):
            mine, other = (low, high) if odd == 0 else (high, low)
            kaugs[odd][:, :LANES] = k_ref[:, lanes] * mine + hot_ref[...] * other
            qaugs[odd][:, :LANES] = q_ref[:, lanes] * mine + met[:, :LANES] * other
            skew_groups(bands[2 * pair + odd], wides.at[odd])

            @pl.when(pair > 0)
            def _():
                probs_copy(2 * pair + odd, odd).wait()

        for side in range(2):
            cols = slice(side * half, (side + 1) * half)
            tops = []
            for odd in range(2):
                whole = times_transposed(kaugs[odd][...], qaugs[odd][cols, :])
                steps_x = times_transposed(key_x[odd], met[cols, LANES : 2 * LANES])
                steps_y = times_transposed(key_y[odd], met[cols, 2 * LANES :])
                top = None
                for part in range(BLOCKS):
                    rows = slice(part * LANES, (part + 1) * LANES)
                    bias = []
                    for block in range(2 * side, 2 * side + 2):
                        step = max(-2, min(2, block - part)) + 2
                        bias.append(wides[odd, :, step * LANES : (step + 1) * LANES])
                    s = whole[rows] + jnp.concatenate(bias, axis=1)
                    s = s + steps_x[rows] * less_x[rows, cols].astype(F32)
                    s = s + steps_y[rows] * less_y[rows, cols].astype(F32)
                    scores[odd, rows, :] = s
                    best = jnp.max(s.reshape(LANES // 8, 8, half), axis=0)
                    top = best if top is None else jnp.maximum(top, best)
                tops.append(jnp.max(top, axis=0, keepdims=True))
            for odd in range(2):
                total = None
                for part in range(BLOCKS):
                    rows = slice(part * LANES, (part + 1) * LANES)
                    e = jnp.exp(scores[odd, rows, :] - tops[odd])
                    probs[odd][rows, cols] = e.astype(BF16)
                    add = jnp.sum(e.reshape(LANES // 8, 8, half), axis=0)
                    total = add if total is None else total + add
                share = 1.0 / jnp.sum(total, axis=0, keepdims=True)
                share_out[2 * pair + odd, :, cols] = share
                got = matmul(values_t[odd * HEAD_DIM : (odd + 1) * HEAD_DIM, :], probs[odd][:, cols])
                pair_t[odd * HEAD_DIM : (odd + 1) * HEAD_DIM, cols] = got * share
        for odd in range(2):
            probs_copy(2 * pair + odd, odd).start()
        both = pair_t[...]
        context_t[lanes, :] = both.astype(BF16)
        context[:, lanes] = both.T.astype(BF16)
        return carry

    lax.fori_loop(0, 2, one_pair, 0)
    gathering.first(3)
    exchange(cot_in, cot_ref, 1)
    gathering.second(2)
    lax.fori_loop(2, 4, one_pair, 0)
    gathering.third(2)
    gathering.second(3)
    gathering.complete(2)
    stage_column(plan, flat, staged, 2)
    form_matrices(plan, staged, matrices, 2)
    keep_carry(plan, staged)
    write_out(w_in, w_in_out)
    lax.fori_loop(4, PAIRS, one_pair, 0)
    write_out(context_t, context_out)
    gathering.third(3)

    def vector(name):
        return vec[0:1, VEC[name] : VEC[name] + D]

    for n in range(D // NBLOCK):
        lanes = slice(n * NBLOCK, (n + 1) * NBLOCK)
        bias = vec[0:1, VEC["out_bias"] + n * NBLOCK : VEC["out_bias"] + (n + 1) * NBLOCK]
        start[:, lanes] = start[:, lanes] + matmul(context[...], w_out[:, lanes]) + bias

    step_rows = 64

    def norm_first(n, carry):
        rows = pl.ds(pl.multiple_of(n * step_rows, step_rows), step_rows)
        x = start[rows, :]
        centred = x - jnp.mean(x, axis=1, keepdims=True)
        rstd = lax.rsqrt(jnp.mean(centred * centred, axis=1, keepdims=True) + norm_eps)
        xhat = centred * rstd
        hat[rows, :] = xhat
        rstd_out[rows, :] = jnp.broadcast_to(rstd, (step_rows, LANES))
        normed = xhat * vector("gain_one") + vector("shift_one")
        start[rows, :] = normed
        normed_low[rows, :] = normed.astype(BF16)
        return carry

    lax.fori_loop(0, WINLEN // step_rows, norm_first, 0)
    write_out(hat, hat_out)
    write_out(normed_low, normed_out)

    for odd in range(2):
        probs_copy(0, odd).wait()

    def widen(n, carry):
        at = pl.multiple_of(n * NBLOCK, NBLOCK)
        lanes = pl.ds(at, NBLOCK)
        bias = vec[0:1, pl.ds(pl.multiple_of(VEC["in_bias"] + at, LANES), NBLOCK)]
        value, change = gelu_and_slope(matmul(normed_low[...], w_in[:, lanes]) + bias)
        active[:, lanes] = value.astype(BF16)
        slope[:, lanes] = change.astype(BF16)
        return carry

    lax.fori_loop(0, FF // NBLOCK, widen, 0, unroll=2)
    gathering.complete(3)
    stage_column(plan, flat, staged, 3)
    form_matrices(plan, staged, matrices, 3)
    write_out(w_back, w_back_out)
    write_out(active, active_out)
    write_out(slope, slope_out)
    for n in range(D // NBLOCK):
        lanes = slice(n * NBLOCK, (n + 1) * NBLOCK)
        bias = vec[0:1, VEC["back_bias"] + n * NBLOCK : VEC["back_bias"] + (n + 1) * NBLOCK]
        start[:, lanes] = start[:, lanes] + matmul(active[...], w_back[:, lanes]) + bias

    exchanged(cot_ref, 1)
    own_cot.wait()
    gain_grads[...] = jnp.zeros_like(gain_grads)

    def norm_second(n, carry):
        rows = pl.ds(pl.multiple_of(n * step_rows, step_rows), step_rows)
        x = start[rows, :]
        centred = x - jnp.mean(x, axis=1, keepdims=True)
        rstd = lax.rsqrt(jnp.mean(centred * centred, axis=1, keepdims=True) + norm_eps)
        xhat = centred * rstd
        output_ref[rows, :] = (xhat * vector("gain_two") + vector("shift_two")).astype(BF16)
        cot = cot_ref[rows, :].astype(F32)
        prod = cot * xhat
        gain_grads[0:1, :] = gain_grads[0:1, :] + jnp.sum(prod, axis=0, keepdims=True)
        gain_grads[1:2, :] = gain_grads[1:2, :] + jnp.sum(cot, axis=0, keepdims=True)
        gain = vector("gain_two")
        gc = cot * gain
        mean_one = jnp.mean(gc, axis=1, keepdims=True)
        mean_two = jnp.mean(prod * gain, axis=1, keepdims=True)
        second_out[rows, :] = rstd * (gc - mean_one - xhat * mean_two)
        return carry

    lax.fori_loop(0, WINLEN // step_rows, norm_second, 0)
    for copy in written[1:]:
        copy.wait()
    finish_notes()
    gathering.finish()


def forward_pass(plan, params, hidden_in, cotangent, boxes, lengths):
    anywhere = pl.BlockSpec(memory_space=pl.ANY)
    vmem = pl.BlockSpec(memory_space=pltpu.VMEM)
    token = (WINLEN, D)

    def hbm(shape, dtype=BF16):
        return jax.ShapeDtypeStruct(shape, dtype), anywhere

    def near(shape, dtype=F32):
        return jax.ShapeDtypeStruct(shape, dtype), vmem

    outs = [
        hbm(MATRICES[0]), hbm(MATRICES[1]), hbm(MATRICES[3]), hbm(MATRICES[4]), hbm((D, WINLEN)), hbm(token),
        hbm(token), hbm(token), hbm(token), hbm((HEADS, WINLEN, WINLEN)), hbm((D, WINLEN)),
        hbm(token, F32), hbm(token), hbm((WINLEN, FF)), hbm((WINLEN, FF)), near(token),
        near((1, VEC_ROWS * LANES)), near((WINLEN, LANES)), near((2, D)), near(token, BF16),
        near(token, BF16), near((WINLEN, LANES), BF16), near((2, WINLEN)),
        near((HEADS, 1, WINLEN)),
    ]
    scratch = [
        pltpu.VMEM((COLUMNS, CORES, DEPTH, COLUMNS, plan.quarter, LANES), BF16),
        pltpu.VMEM((plan.staged, LANES), F32),
        pltpu.VMEM((COLUMNS, plan.quarter, LANES), BF16),
    ]
    scratch += [pltpu.VMEM(layout, BF16) for layout in MATRICES]
    scratch += [
        pltpu.VMEM((NOTE_ROWS, LANES), BF16),
        pltpu.VMEM(token, BF16),
        pltpu.VMEM(token, BF16),
        pltpu.VMEM(token, F32),
        pltpu.VMEM(token, BF16),
        pltpu.VMEM(token, BF16),
        pltpu.VMEM(token, BF16),
        pltpu.VMEM(token, BF16),
        pltpu.VMEM((WINLEN, LANES), BF16),
        pltpu.VMEM((2, WINLEN, LANES), BF16),
        pltpu.VMEM((2, WINLEN, LANES), BF16),
        pltpu.VMEM((HEADS, 8, WIDE), F32),
        pltpu.VMEM((2 * HEADS, BUCKETS, LANES), F32),
        pltpu.VMEM((2, LANES, 5 * LANES), F32),
        pltpu.VMEM((2, WINLEN, 2 * LANES), F32),
        pltpu.VMEM((D, WINLEN), BF16),
        pltpu.VMEM((LANES, WINLEN), F32),
        pltpu.VMEM(token, F32),
        pltpu.VMEM((WINLEN, FF), BF16),
        pltpu.VMEM((WINLEN, FF), BF16),
        pltpu.VMEM((1, VEC_ROWS * LANES), F32),
        pltpu.SemaphoreType.DMA((2, 7)),
        pltpu.SemaphoreType.DMA((2, 2, DEPTH)),
        pltpu.SemaphoreType.DMA((16,)),
        pltpu.SemaphoreType.DMA((2,)),
    ]
    return pl.pallas_call(
        functools.partial(forward_kernel, plan),
        out_shape=[shape for shape, _ in outs],
        in_specs=[anywhere] * 3 + [vmem, pl.BlockSpec(memory_space=pltpu.SMEM), vmem],
        out_specs=[spec for _, spec in outs],
        scratch_shapes=scratch + sem_shapes(GATHER_SEMS),
        compiler_params=pltpu.CompilerParams(
            collective_id=0, has_side_effects=True, vmem_limit_bytes=62 * 2**20
        ),
        name="forward_pass",
    )(params, hidden_in, cotangent, boxes, lengths, jnp.asarray(turns_table()))


def token_info(doc_lengths, box_coords):
    places = jnp.arange(WINLEN, dtype=jnp.int32)
    first = places == 0
    doc = jnp.zeros((WINLEN,), jnp.int32)
    end = 0
    for d in range(3):
        end = end + doc_lengths[d]
        doc = doc + (places >= end).astype(jnp.int32)
        first = first | (places == end)
    rows = [box_coords[:, c] for c in range(4)] + [doc, first.astype(jnp.int32)]
    return jnp.stack(rows + [jnp.zeros_like(doc)] * 2).astype(F32)


class Reducing:
    def __init__(self, place, flat, swapped, one, two, deep, piece, result, sems, free):
        self.place = place
        self.flat = flat
        self.swapped = swapped
        self.one = one
        self.two = two
        self.deep = deep
        self.piece = piece
        self.result = result
        self.sems = sems
        self.free = free
        self.sent = {k: [] for k in range(COLUMNS)}

    def send(self, k, src, dst, kind, index, peer):
        copy = remote(src, dst, self.sems[kind].at[0, index], self.sems[kind].at[1, index], peer)
        copy.start()
        self.sent[k].append(copy)

    got = Gathering.got

    def settle(self, k):
        for copy in self.sent.pop(k):
            copy.wait_send()

    def swap(self, k):
        p = self.place
        slot = k % 2
        if k < 2:
            pl.semaphore_wait(self.free.at[slot], 1)
        self.send(k, self.flat.at[slot, 1 - p.core], self.swapped.at[slot], "core", k, p.peer_core)

    def first(self, k):
        p = self.place
        slot = k % 2
        self.got(self.swapped.at[slot], "core", k)

        def one(step, carry):
            z, quarter = step // COLUMNS, step % COLUMNS
            total = self.flat[slot, p.core, z, quarter].astype(F32)
            total = total + self.swapped[slot, z, quarter].astype(F32)
            self.flat[slot, p.core, z, quarter] = total.astype(BF16)
            return carry

        lax.fori_loop(0, DEPTH * COLUMNS, one, 0)
        flat = self.flat
        self.send(k, flat.at[slot, p.core, 0:2, p.col_d], self.one.at[k, 0], "one", 2 * k, p.peer_y)
        self.send(k, flat.at[slot, p.core, 2:4, p.col_d], self.one.at[k, 1], "one", 2 * k + 1, p.peer_x)
        if k >= 2:
            pl.semaphore_signal(
                self.free.at[slot], inc=1, device_id=p.peer_core, device_id_type=MESH
            )

    def second(self, k):
        p = self.place
        slot = k % 2
        for side, column in ((0, p.col_x), (1, p.col_y)):
            self.got(self.one.at[k, side], "one", 2 * k + side)

            def one(step, carry, side=side, column=column):
                z = 2 * side + step
                total = self.flat[slot, p.core, z, column].astype(F32)
                total = total + self.one[k, side, step].astype(F32)
                self.flat[slot, p.core, z, column] = total.astype(BF16)
                return carry

            lax.fori_loop(0, 2, one, 0)
        flat = self.flat
        self.send(k, flat.at[slot, p.core, :, p.col_x], self.two.at[k, 0], "two", 2 * k, p.peer_x)
        self.send(k, flat.at[slot, p.core, :, p.col_y], self.two.at[k, 1], "two", 2 * k + 1, p.peer_y)

    def third(self, k):
        p = self.place
        slot = k % 2
        for side in range(2):
            self.got(self.two.at[k, side], "two", 2 * k + side)

        def one(z, carry):
            total = self.flat[slot, p.core, z, p.column].astype(F32)
            total = total + self.two[k, 0, z].astype(F32) + self.two[k, 1, z].astype(F32)
            self.flat[slot, p.core, z, p.column] = total.astype(BF16)
            return carry

        lax.fori_loop(0, DEPTH, one, 0)
        for d in range(DEPTH - 1):
            self.send(
                k, self.flat.at[slot, p.core, p.far[d], p.column], self.deep.at[k, d], "z", 3 * k + d,
                p.peers_z[d],
            )

    def fourth(self, k):
        p = self.place
        for d in range(DEPTH - 1):
            self.got(self.deep.at[k, d], "z", 3 * k + d)
        total = self.flat[k % 2, p.core, p.z, p.column].astype(F32)
        for d in range(DEPTH - 1):
            total = total + self.deep[k, d].astype(F32)
        self.piece[k] = total.astype(BF16)

    def giving(self, k):
        p = self.place
        sems = self.sems["spread"]
        return remote(
            self.piece.at[k], self.result.at[p.column], sems.at[0, k], sems.at[1, p.column],
            p.at(k, p.core, p.z),
        )

    def give(self, k):
        @pl.when(self.place.column != k)
        def _():
            self.giving(k).start()

    def given(self, k):
        @pl.when(self.place.column != k)
        def _():
            self.giving(k).wait_send()

    def receive(self, out):
        p = self.place
        out[p.column] = self.piece[p.column].astype(F32)
        for column in (p.col_x, p.col_y, p.col_d):
            self.got(self.result.at[column], "spread", column)
            out[column] = self.result[column].astype(F32)


REDUCE_SEMS = {"spread": 4, "z": 12, "one": 8, "two": 8, "core": 4}


def unstage_column(plan, flat, staged, k):
    def one(step, carry):
        shard, quarter = step // COLUMNS, step % COLUMNS
        base = plan.carry + shard * plan.rows + quarter * plan.quarter
        piece = staged[pl.ds(pl.multiple_of(base, 8), plan.quarter), :]
        flat[k % 2, shard // DEPTH, shard % DEPTH, quarter] = piece.astype(BF16)
        return carry

    lax.fori_loop(0, CORES * DEPTH * COLUMNS, one, 0)


class Notes:
    def __init__(self, place, notes, slots, sems):
        self.place, self.notes, self.slots, self.sems = place, notes, slots, sems
        p = place
        self.home = (p.column == COLUMNS - 1) & (p.core == CORES - 1)
        self.root = self.home & (p.z == DEPTH - 1)

    def copy(self, slot, peer):
        return remote(
            self.notes, self.slots.at[slot], self.sems.at[0, 0], self.sems.at[1, slot], peer
        )

    def take(self, slot):
        self.copy(slot, self.place.peer_core).wait_recv()
        self.notes[...] = self.notes[...] + self.slots[slot]

    def start(self):
        p = self.place

        @pl.when(p.core != CORES - 1)
        def _():
            self.copy(0, p.peer_core).start()

    def rise(self):
        p = self.place

        @pl.when(p.core == CORES - 1)
        def _():
            self.take(0)

        @pl.when((p.core == CORES - 1) & (p.column != COLUMNS - 1))
        def _():
            self.copy(1 + p.column, p.at(COLUMNS - 1, p.core, p.z)).start()

    def end(self):
        p = self.place

        @pl.when(self.home)
        def _():
            for slot in range(1, 4):
                self.take(slot)

        @pl.when(self.home & (p.z != DEPTH - 1))
        def _():
            self.copy(4 + p.z, p.at(p.column, p.core, DEPTH - 1)).start()

        @pl.when(self.root)
        def _():
            for slot in range(4, 7):
                self.take(slot)

        @pl.when(jnp.logical_not(self.root))
        def _():
            self.copy(0, p.peer_core).wait_send()


def cell_sums(whole, less, odd):
    lane = lax.broadcasted_iota(jnp.int32, (1, LANES), 1)
    sub = lax.broadcasted_iota(jnp.int32, (8, LANES), 0)
    sums = []
    for axis in range(2):
        rows = slice(axis * BUCKETS, (axis + 1) * BUCKETS)
        start = axis * BUCKETS + (0 if odd else 64)
        every = pltpu.roll(whole[rows], (BUCKETS - start) % LANES, 1)
        below = pltpu.roll(less[rows], (BUCKETS - axis * BUCKETS) % LANES, 1)
        inside = (lane >= BUCKETS) & (lane < 2 * BUCKETS)
        every = jnp.where(inside, every, 0.0)
        below = jnp.where(inside, below, 0.0)
        x = every - below + pltpu.roll(below, LANES - 1, 1)
        total = None
        for group in range(BUCKETS // 8):
            y = x[8 * group : 8 * group + 8]
            y = y if group == 0 else pltpu.roll(y, LANES - 8 * group, 1)
            total = y if total is None else total + y
        for bit in (1, 2, 4):
            total = jnp.where((sub & bit) != 0, pltpu.roll(total, LANES - bit, 1), total)
        sums.append(jnp.sum(total, axis=0, keepdims=True))
    return sums


def exact_dot(a, b):
    return jnp.dot(a, b, preferred_element_type=F32, precision=lax.Precision.HIGHEST)


def bucket_rows(cell_ref, diag_ref):
    half = BUCKETS // 2
    column = lax.broadcasted_iota(jnp.int32, (1, LANES), 1)
    row = lax.broadcasted_iota(jnp.int32, (LANES, 1), 0)
    to = jnp.clip(row - BUCKETS, -half, half - 1) + half
    place = lax.broadcasted_iota(jnp.int32, (WIDE, 1), 0)
    along = place - LANES
    far = jnp.where(place < LANES, 0, jnp.where(place < 5 * LANES, 0, BUCKETS - 1))
    along = jnp.where(
        (place >= LANES) & (place < 4 * LANES),
        jnp.clip(along - LANES, -half, half - 1) + half,
        far,
    )
    first, rest = None, None
    zero = jnp.zeros((5, WIDE), F32)
    for m in range(4):
        hot_along = jnp.where(along + m * BUCKETS == column, 1.0, 0.0)
        got = exact_dot(
            jnp.concatenate([diag_ref[4 * n + m] for n in range(3)] + [zero], axis=0), hot_along
        )
        first = got if first is None else first + got
        hot_cell = jnp.where(to + m * BUCKETS == column, 1.0, 0.0)
        rows = [cell_ref[t * HEADS + 4 * n + m] for t in range(2) for n in range(3)]
        got = exact_dot(jnp.concatenate(rows + [zero[:2, :LANES]], axis=0), hot_cell)
        rest = got if rest is None else rest + got
    return jnp.concatenate([first[:3], rest[:6]], axis=0)


def backward_kernel(
    plan, active_in, slope_in, w_back_in, w_in_in, w_out_in, w_qkv_in, normed_in, low_in, features_in,
    context_in, q_in, k_in, v_in, probs_in, hat_in, second_in, rstd_ref, vec, gain_two, hot_ref, rest_ref,
    share_ref, output_in, *refs,
):
    out, output_pos, hidden_pos = refs[:3]
    (flat, staged, swapped, one_buf, two_buf, deep, piece, result, active, slope, w_back, w_in, w_out,
     turned, context_t, q_ref, k_ref, v_ref, hat, second, branch, dctx, probs, less_x,
     less_y, scores_odd, bands, hot_t, qaugs, pair_t, scaled, share_cols, vecg, cell_rows, diag_rows, notes, slots,
     ) = refs[3:40]
    load_sems, probs_sems, free, pos_sems, note_sems = refs[40:45]
    place = Place()
    reducing = Reducing(
        place, flat, swapped, one_buf, two_buf, deep, piece, result,
        dict(zip(REDUCE_SEMS, refs[45:])), free,
    )
    climbing = Notes(place, notes, slots, note_sems)
    loads = {}

    def load(name, src, dst):
        loads[name] = pltpu.make_async_copy(src, dst, load_sems.at[len(loads)])
        loads[name].start()

    mixed = active.at[:, : 3 * D]
    grad_attn = branch
    w_qkv = w_in.at[:, : 3 * D]
    hidden_low = dctx
    features_t = w_back.at[:D, :WINLEN]
    low_t = w_out.at[:WINLEN]
    scores = [hat.at[:, :WINLEN], scores_odd]
    dscores = [slope.at[:, :WINLEN], slope.at[:, WINLEN : 2 * WINLEN]]
    dscores_x = [slope.at[:, 2 * WINLEN : 3 * WINLEN], slope.at[:, 3 * WINLEN : 4 * WINLEN]]
    dscores_y = [slope.at[:, 4 * WINLEN : 5 * WINLEN], slope.at[:, 5 * WINLEN :]]

    load("second", second_in, second)
    load("active", active_in, active)

    at = staged_at(plan, COLUMNS - 1, plan.misc_start)
    staged[at:, :] = jnp.zeros((plan.staged - at, LANES), F32)
    place.greet()

    quarter = WINLEN // DEPTH
    positions = []

    def to_pos(source, target, kind):
        for d in range(DEPTH - 1):
            rows = pl.ds(pl.multiple_of(place.far[d] * quarter, quarter), quarter)
            copy = remote(
                source.at[rows], target.at[place.z], pos_sems.at[kind, 0, d], pos_sems.at[kind, 1, d],
                place.peers_z[d],
            )
            copy.start()
            positions.append(copy)
        rows = pl.ds(pl.multiple_of(place.z * quarter, quarter), quarter)
        copy = pltpu.make_async_copy(
            source.at[rows], target.at[place.z], pos_sems.at[kind, 0, DEPTH - 1]
        )
        copy.start()
        return copy

    def in_pos(target, kind):
        for d in range(DEPTH - 1):
            there = target.at[place.from_far[d]]
            remote(
                there, there, pos_sems.at[kind, 0, d], pos_sems.at[kind, 1, d], place.peer_x
            ).wait_recv()

    own_output = to_pos(output_in, output_pos, 0)

    def store(k, index, row, value, first_block=0):
        blocks = MATRICES[index][1] // LANES
        base = staged_at(plan, k, plan.starts[index]) + row * blocks + first_block
        for block in range(value.shape[1] // LANES):
            staged[pl.ds(base + block, value.shape[0], stride=blocks), :] = value[
                :, block * LANES : (block + 1) * LANES
            ]

    def column_sum(value):
        return jnp.sum(value, axis=0, keepdims=True)

    def keep_vector(name, lanes_at, value):
        at = pl.multiple_of(VEC[name] + lanes_at, LANES)
        vecg[0:1, pl.ds(at, value.shape[1])] = value

    loads["second"].wait()
    for n in range(D // NBLOCK):
        lanes = slice(n * NBLOCK, (n + 1) * NBLOCK)
        value = second[:, lanes].astype(BF16)
        branch[:, lanes] = value
        keep_vector("back_bias", n * NBLOCK, column_sum(value.astype(F32)))
    loads["active"].wait()
    load("slope", slope_in, slope)
    load("w_back", w_back_in, w_back)
    load("normed", normed_in, dctx)

    def back_rows(k, size, begin, count):
        def body(n, carry):
            row = pl.multiple_of(begin + n * size, LANES)
            turned[:size, :] = active[:, pl.ds(row, size)].T
            store(k, 4, row, matmul(turned[:size, :], branch[...]))
            return carry

        lax.fori_loop(0, count, body, 0)

    back_rows(3, WINLEN, 512, FF // WINLEN - 1)
    unstage_column(plan, flat, staged, 3)
    reducing.swap(3)

    back_rows(2, WINLEN, 0, 1)
    back_rows(2, LANES, 512, 1)
    loads["w_back"].wait()
    loads["slope"].wait()
    load("w_in", w_in_in, w_in)
    load("hat", hat_in, hat)
    load("w_out", w_out_in, w_out)

    def inner(n, carry):
        at = pl.multiple_of(n * NBLOCK, NBLOCK)
        lanes = pl.ds(at, NBLOCK)
        value = times_transposed(branch[...], w_back[lanes, :]) * slope[:, lanes].astype(F32)
        value = value.astype(BF16)
        slope[:, lanes] = value
        keep_vector("in_bias", at, column_sum(value.astype(F32)))
        return carry

    lax.fori_loop(0, FF // NBLOCK, inner, 0, unroll=2)
    grad_inner = slope
    reducing.first(3)

    loads["normed"].wait()
    for n in range(D // NBLOCK):
        rows = slice(n * NBLOCK, (n + 1) * NBLOCK)
        turned[rows, :] = dctx[:, rows].T

    def in_rows(k, begin, end):
        def body(n, carry):
            lanes = pl.ds(pl.multiple_of(n * NBLOCK, NBLOCK), NBLOCK)
            got = matmul(turned[begin:end, :], grad_inner[:, lanes])
            store(k, 3, begin, got, n * (NBLOCK // LANES))
            return carry

        lax.fori_loop(0, FF // NBLOCK, body, 0)

    in_rows(2, 288, D)
    unstage_column(plan, flat, staged, 2)
    reducing.swap(2)
    reducing.second(3)

    loads["w_in"].wait()
    load("context", context_in, context_t)
    load("q", q_in, q_ref)
    load("k", k_in, k_ref)
    load("v", v_in, v_ref)
    for odd in range(2):
        pltpu.make_async_copy(probs_in.at[odd], probs.at[odd], probs_sems.at[odd]).start()
    for n in range(D // NBLOCK):
        lanes = slice(n * NBLOCK, (n + 1) * NBLOCK)
        second[:, lanes] = second[:, lanes] + times_transposed(grad_inner[...], w_in[lanes, :])
    load("w_qkv", w_qkv_in, w_qkv)
    load("features", features_in, features_t)
    reducing.first(2)

    loads["hat"].wait()
    step_rows = 64
    for name in ("gain_one", "shift_one", "out_bias"):
        keep_vector(name, 0, jnp.zeros((1, D), F32))

    def norm_first(n, carry):
        rows = pl.ds(pl.multiple_of(n * step_rows, step_rows), step_rows)
        grad = second[rows, :]
        xhat = hat[rows, :]
        prod = grad * xhat
        gain = vec[0:1, VEC["gain_one"] : VEC["gain_one"] + D]
        gc = grad * gain
        mean_one = jnp.mean(gc, axis=1, keepdims=True)
        mean_two = jnp.mean(prod * gain, axis=1, keepdims=True)
        value = rstd_ref[rows, 0:1] * (gc - mean_one - xhat * mean_two)
        second[rows, :] = value
        value = value.astype(BF16)
        grad_attn[rows, :] = value
        for name, term in (
            ("gain_one", prod), ("shift_one", grad), ("out_bias", value.astype(F32)),
        ):
            lanes = slice(VEC[name], VEC[name] + D)
            vecg[0:1, lanes] = vecg[0:1, lanes] + column_sum(term)
        return carry

    lax.fori_loop(0, WINLEN // step_rows, norm_first, 0)
    reducing.third(3)
    loads["w_out"].wait()
    for n in range(D // NBLOCK):
        lanes = slice(n * NBLOCK, (n + 1) * NBLOCK)
        dctx[:, lanes] = times_transposed(grad_attn[...], w_out[lanes, :]).astype(BF16)
    load("low", low_in, low_t)
    loads["context"].wait()
    in_rows(1, 0, 304)
    reducing.second(2)

    def out_rows(k, begin, end):
        for n in range(D // NBLOCK):
            lanes = slice(n * NBLOCK, (n + 1) * NBLOCK)
            got = matmul(context_t[begin:end, :], grad_attn[:, lanes])
            store(k, 1, begin, got, n * (NBLOCK // LANES))

    out_rows(1, 192, D)
    reducing.fourth(3)
    reducing.give(3)

    low, high = half_masks()
    rest = rest_ref[...]
    columns = jnp.concatenate([rest, jnp.zeros((LANES - 2, WINLEN), F32)], axis=0).T
    for part in range(BLOCKS):
        rows = slice(part * LANES, (part + 1) * LANES)
        for axis, less in ((0, less_x), (1, less_y)):
            less[rows, :] = jnp.where(
                rest[axis : axis + 1, :] < columns[rows, axis : axis + 1], 1.0, 0.0
            ).astype(BF16)
    hot_t[...] = hot_ref[...].T
    lane = lax.broadcasted_iota(jnp.int32, (1, LANES), 1)
    scale = HEAD_DIM ** (-0.5)
    of_x = jnp.where((lane // BUCKETS) % 2 == 0, 1.0, 0.0)
    share_cols[...] = jnp.concatenate(
        [share_ref[head] for head in range(HEADS)] + [jnp.zeros((LANES - HEADS, WINLEN), F32)], axis=0
    ).T
    for name in ("q", "k", "v"):
        loads[name].wait()

    def probs_copy(head, odd):
        return pltpu.make_async_copy(probs_in.at[head], probs.at[odd], probs_sems.at[odd])

    def one_pair(pair, carry):
        at = pl.multiple_of(pair * LANES, LANES)
        lanes = pl.ds(at, LANES)
        keys_t = k_ref[:, lanes].T
        cells_x = hot_ref[...] * of_x.astype(BF16)
        cells_y = hot_ref[...] * (1.0 - of_x).astype(BF16)
        both = pltpu.roll(share_cols[...], lax.rem(LANES - 2 * pair, LANES), 1)
        both = jnp.where(lane < HEAD_DIM, both[:, 0:1], both[:, 1:2])
        scaled[...] = (dctx[:, lanes].astype(F32) * both).astype(BF16)
        grad_context = dctx[:, lanes]
        dots = []
        for odd in range(2):
            mine, other = (low, high) if odd == 0 else (high, low)
            head = 2 * pair + odd
            probs_copy(head, odd).wait()
            qaugs[odd] = q_ref[:, lanes] * mine + hot_ref[...] * other
            products = times_transposed(v_ref[:, lanes] * mine, grad_context)
            dot = None
            for part in range(BLOCKS):
                rows = slice(part * LANES, (part + 1) * LANES)
                dp = products[rows]
                scores[odd][rows, :] = dp
                add = dp * probs[odd, rows, :].astype(F32)
                add = jnp.sum(add.reshape(LANES // 8, 8, WINLEN), axis=0)
                dot = add if dot is None else dot + add
            dots.append(column_sum(dot) * share_ref[head])
            bands[odd] = jnp.zeros_like(bands[odd])
        for odd in range(2):
            head = 2 * pair + odd
            share = share_ref[head]
            for part in range(BLOCKS):
                rows = slice(part * LANES, (part + 1) * LANES)
                ds = probs[odd, rows, :].astype(F32) * ((scores[odd][rows, :] - dots[odd]) * share)
                for block in range(BLOCKS):
                    step = max(-2, min(2, block - part)) + 2
                    where = slice(step * LANES, (step + 1) * LANES)
                    bands[odd, :, where] = (
                        bands[odd, :, where] + ds[:, block * LANES : (block + 1) * LANES]
                    )
                ds = ds.astype(BF16)
                dscores[odd][rows, :] = ds
                dscores_x[odd][rows, :] = ds * less_x[rows, :]
                dscores_y[odd][rows, :] = ds * less_y[rows, :]
        for odd in range(2):
            head = 2 * pair + odd
            keys_cells = matmul(dscores[odd][...], qaugs[odd])
            less = matmul(dscores_x[odd][...], cells_x) + matmul(dscores_y[odd][...], cells_y)
            values_grad = matmul(probs[odd], scaled[...])

            pair_t[odd * HEAD_DIM : (odd + 1) * HEAD_DIM, :] = matmul(
                keys_t[odd * HEAD_DIM : (odd + 1) * HEAD_DIM, :], dscores[odd][...]
            )
            band = bands.at[odd]
            diag_rows[head, :, LANES : 5 * LANES] = diagonal_sums(band)
            diag_rows[head, :, :LANES] = column_sum(band[:, :LANES])
            diag_rows[head, :, 5 * LANES :] = column_sum(band[:, 4 * LANES :])
            sums = []
            for summed in (keys_cells, less):
                first = summed.astype(BF16)
                remainder = (summed - first.astype(F32)).astype(BF16)
                sums.append(matmul(hot_t[:64, :], first) + matmul(hot_t[:64, :], remainder))
            for axis, value in enumerate(cell_sums(sums[0], sums[1], odd)):
                cell_rows[axis * HEADS + head] = value
            for which, value in ((1, keys_cells), (2, values_grad)):
                there = pl.ds(pl.multiple_of(at + which * D, LANES), LANES)
                value = value.astype(BF16)
                if odd:
                    value = mixed[:, there] * low + value * high
                mixed[:, there] = value

        @pl.when(pair < PAIRS - 1)
        def _():
            for odd in range(2):
                probs_copy(2 * pair + odd + 2, odd).start()

        value = (pair_t[...].T * scale).astype(BF16)
        mixed[:, lanes] = value
        keep_vector("q_bias", at, column_sum(value.astype(F32)))
        there = pl.ds(pl.multiple_of(at + 2 * D, LANES), LANES)
        keep_vector("v_bias", at, column_sum(mixed[:, there].astype(F32)))
        return carry

    lax.fori_loop(0, 2, one_pair, 0)
    reducing.third(2)
    lax.fori_loop(2, 4, one_pair, 0)
    reducing.fourth(2)
    reducing.give(2)
    lax.fori_loop(4, PAIRS, one_pair, 0)

    loads["w_qkv"].wait()
    for n in range(D // NBLOCK):
        lanes = slice(n * NBLOCK, (n + 1) * NBLOCK)
        value = second[:, lanes] + times_transposed(mixed[...], w_qkv[lanes, :])
        hidden_low[:, lanes] = value.astype(BF16)
    own_hidden = to_pos(hidden_low, hidden_pos, 1)
    loads["features"].wait()
    for n in range(D // NBLOCK):
        lanes = slice(n * NBLOCK, (n + 1) * NBLOCK)
        store(1, 2, 0, matmul(features_t[...], hidden_low[:, lanes]), n * (NBLOCK // LANES))
    reducing.settle(3)
    unstage_column(plan, flat, staged, 1)
    reducing.swap(1)

    loads["low"].wait()
    for n in range(D // NBLOCK):
        rows = slice(n * NBLOCK, (n + 1) * NBLOCK)
        turned[rows, :] = low_t[:, rows].T

    def qkv_rows(n, carry):
        lanes = pl.ds(pl.multiple_of(n * NBLOCK, NBLOCK), NBLOCK)
        store(0, 0, 0, matmul(turned[...], mixed[:, lanes]), n * (NBLOCK // LANES))
        return carry

    lax.fori_loop(0, 3 * D // NBLOCK, qkv_rows, 0)
    out_rows(0, 0, 208)
    reducing.settle(2)
    unstage_column(plan, flat, staged, 0)
    reducing.swap(0)
    reducing.first(1)
    keep_vector("gain_two", 0, gain_two[0:1, :])
    keep_vector("shift_two", 0, gain_two[1:2, :])
    notes[...] = jnp.zeros_like(notes)
    table = VEC["tables"] // LANES
    for row in range(table):
        notes[row : row + 1, :] = vecg[0:1, row * LANES : (row + 1) * LANES]
    notes[table : table + 9, :] = bucket_rows(cell_rows, diag_rows)
    climbing.start()

    reducing.first(0)
    reducing.second(1)
    climbing.rise()
    reducing.second(0)
    climbing.end()
    reducing.third(1)
    reducing.third(0)
    reducing.fourth(1)
    reducing.give(1)
    reducing.fourth(0)
    reducing.give(0)
    reducing.receive(out)
    note_quarter, note_first, note_row = note_place(plan)
    base = note_first + note_row

    @pl.when(climbing.root)
    def _():
        out[note_quarter, base : base + MISC_ROWS, :] = (
            out[note_quarter, base : base + MISC_ROWS, :] + notes[:MISC_ROWS, :]
        )

    in_pos(output_pos, 0)
    in_pos(hidden_pos, 1)
    own_output.wait()
    own_hidden.wait()
    for copy in positions:
        copy.wait_send()
    for k in range(COLUMNS):
        reducing.given(k)
    reducing.settle(1)
    reducing.settle(0)


def backward_pass(plan, operands):
    anywhere = pl.BlockSpec(memory_space=pl.ANY)
    vmem = pl.BlockSpec(memory_space=pltpu.VMEM)
    token = (WINLEN, D)
    block = (plan.quarter, LANES)
    positions = jax.ShapeDtypeStruct((DEPTH, WINLEN // DEPTH, D), BF16)
    scratch = [
        pltpu.VMEM((2, CORES, DEPTH, COLUMNS) + block, BF16),
        pltpu.VMEM((plan.staged, LANES), F32),
        pltpu.VMEM((2, DEPTH, COLUMNS) + block, BF16),
        pltpu.VMEM((COLUMNS, 2, 2) + block, BF16),
        pltpu.VMEM((COLUMNS, 2, DEPTH) + block, BF16),
        pltpu.VMEM((COLUMNS, DEPTH - 1) + block, BF16),
        pltpu.VMEM((COLUMNS,) + block, BF16),
        pltpu.VMEM((COLUMNS,) + block, BF16),
        pltpu.VMEM((WINLEN, FF), BF16),
        pltpu.VMEM((WINLEN, FF), BF16),
        pltpu.VMEM((FF, D), BF16),
        pltpu.VMEM((D, FF), BF16),
        pltpu.VMEM((D, D), BF16),
        pltpu.VMEM((D, WINLEN), BF16),
        pltpu.VMEM((D, WINLEN), BF16),
        pltpu.VMEM(token, BF16),
        pltpu.VMEM(token, BF16),
        pltpu.VMEM(token, BF16),
        pltpu.VMEM(token, F32),
        pltpu.VMEM(token, F32),
        pltpu.VMEM(token, BF16),
        pltpu.VMEM(token, BF16),
        pltpu.VMEM((2, WINLEN, WINLEN), BF16),
        pltpu.VMEM((WINLEN, WINLEN), BF16),
        pltpu.VMEM((WINLEN, WINLEN), BF16),
        pltpu.VMEM((WINLEN, WINLEN), F32),
        pltpu.VMEM((2, LANES, 5 * LANES), F32),
        pltpu.VMEM((LANES, WINLEN), BF16),
        pltpu.VMEM((2, WINLEN, LANES), BF16),
        pltpu.VMEM((LANES, WINLEN), F32),
        pltpu.VMEM((WINLEN, LANES), BF16),
        pltpu.VMEM((WINLEN, LANES), F32),
        pltpu.VMEM((1, VEC_ROWS * LANES), F32),
        pltpu.VMEM((2 * HEADS, 1, LANES), F32),
        pltpu.VMEM((HEADS, 1, WIDE), F32),
        pltpu.VMEM((NOTE_ROWS, LANES), F32),
        pltpu.VMEM((7, NOTE_ROWS, LANES), F32),
        pltpu.SemaphoreType.DMA((16,)),
        pltpu.SemaphoreType.DMA((2,)),
        pltpu.SemaphoreType.REGULAR((2,)),
        pltpu.SemaphoreType.DMA((2, 2, DEPTH)),
        pltpu.SemaphoreType.DMA((2, 7)),
    ]
    return pl.pallas_call(
        functools.partial(backward_kernel, plan),
        out_shape=[jax.ShapeDtypeStruct((COLUMNS,) + block, F32), positions, positions],
        in_specs=[anywhere] * 16 + [vmem] * 6 + [anywhere],
        out_specs=[vmem, anywhere, anywhere],
        scratch_shapes=scratch + sem_shapes(REDUCE_SEMS),
        compiler_params=pltpu.CompilerParams(
            collective_id=1, has_side_effects=True, vmem_limit_bytes=62 * 2**20
        ),
        name="backward_pass",
    )(*operands)


def fast_shards(hidden_in, cotangent, box_coords, doc_lengths, params, moment_one, moment_two):
    shard_len = params.shape[0]
    plan = Plan(shard_len)
    (proj_qkv, proj_out, proj_in, proj_back, features_t, start_low, queries, keys, values, probs, context_t,
     xhat, normed_low, active, slope, grad_second, vec, rstd, grad_norm_two, output, _, hot_two,
     rest_rows, share) = forward_pass(
        plan, params.reshape(plan.rows, LANES), hidden_in, cotangent,
        jnp.transpose(box_coords, (0, 2, 1)), doc_lengths,
    )
    summed, output_low, grad_hidden = backward_pass(
        Plan(shard_len, carry=5 * LANES),
        (active, slope, proj_back, proj_in, proj_out, proj_qkv, normed_low, start_low, features_t, context_t,
         queries, keys, values, probs, xhat, grad_second, rstd, vec, grad_norm_two, hot_two, rest_rows,
         share, output),
    )
    grad_share = summed.reshape(plan.padded, LANES)[: plan.rows].reshape(-1)
    return finish_step(output_low, grad_hidden, grad_share, params, moment_one, moment_two)


def finish_step(output_low, grad_hidden, grad_share, params, moment_one, moment_two):
    shard_len = params.shape[0]
    index = lax.axis_index("dp") * lax.axis_size("head") + lax.axis_index("head")
    flat_index = index * shard_len + jnp.arange(shard_len, dtype=jnp.int32)
    param_step, new_one = adam_step(params, moment_one, moment_two, grad_share, flat_index)
    return (output_low, grad_hidden, grad_share, param_step, new_one)


def to_windows(shard):
    return lax.all_to_all(shard, "head", split_axis=0, concat_axis=1, tiled=True)


def to_positions(window):
    return lax.all_to_all(window, "head", split_axis=1, concat_axis=0, tiled=True)


def plain_shards(hidden_in, cotangent, box_coords, doc_lengths, params, moment_one, moment_two):
    head_pos = lax.axis_index("head")
    groups = lax.axis_size("head")
    shard_len = params.shape[0]
    flat_params = lax.all_gather(params.astype(BF16), ("dp", "head"), axis=0, tiled=True)
    pieces = unpack(flat_params)
    hidden = to_windows(hidden_in).reshape(WINLEN, D)
    cot = to_windows(cotangent).reshape(WINLEN, D)
    own_box = lax.dynamic_index_in_dim(box_coords, head_pos, 0, keepdims=False)
    own_lengths = lax.dynamic_index_in_dim(doc_lengths, head_pos, 0, keepdims=False)
    chosen, relative, centre_x, centre_y = window_layout(own_lengths, own_box)
    features = box_features(relative).astype(BF16)

    proj_qkv, proj_out, proj_box, proj_in, proj_back = pieces[:5]
    qv_bias, out_bias, norm_one, in_bias, back_bias, norm_two, tables = pieces[5:]
    ops = bias_operands(tables, chosen, centre_x, centre_y)
    start_state = hidden.astype(F32) + matmul(features, proj_box)
    start_low = start_state.astype(BF16)
    qv_float = qv_bias.astype(F32)
    mixed = matmul(start_low, proj_qkv)
    queries = (mixed[:, :D] + qv_float[0]).astype(BF16) * jnp.asarray(HEAD_DIM ** (-0.5), BF16)
    keys = mixed[:, D : 2 * D].astype(BF16)
    values = (mixed[:, 2 * D :] + qv_float[1]).astype(BF16)

    probs, context_t = attention_forward(queries, keys, values, ops)
    first_sum = start_state + rows_inner(context_t, proj_out) + out_bias.astype(F32)
    normed, norm_one_back = jax.vjp(layer_norm, first_sum, norm_one.astype(F32))
    normed_low = normed.astype(BF16)
    inner_act = matmul(normed_low, proj_in) + in_bias.astype(F32)
    active, gelu_back = jax.vjp(gelu_exact, inner_act)
    active_low = active.astype(BF16)
    second_sum = normed + matmul(active_low, proj_back) + back_bias.astype(F32)
    output, norm_two_back = jax.vjp(layer_norm, second_sum, norm_two.astype(F32))
    output_low = to_positions(output.astype(BF16).reshape(1, WINLEN, D))

    grad_second, grad_norm_two = norm_two_back(cot.astype(F32))
    grad_branch = grad_second.astype(BF16)
    grad_proj_back = rows_inner(active_low, grad_branch)
    grad_back_bias = jnp.sum(grad_branch.astype(F32), axis=0)
    (grad_inner_f,) = gelu_back(times_transposed(grad_branch, proj_back))
    grad_inner = grad_inner_f.astype(BF16)
    grad_proj_in = rows_inner(normed_low, grad_inner)
    grad_in_bias = jnp.sum(grad_inner.astype(F32), axis=0)
    grad_first, grad_norm_one = norm_one_back(grad_second + times_transposed(grad_inner, proj_in))
    grad_attn = grad_first.astype(BF16)
    grad_proj_out = matmul(context_t, grad_attn)
    grad_out_bias = jnp.sum(grad_attn.astype(F32), axis=0)
    grad_context = times_transposed(grad_attn, proj_out).astype(BF16)
    grad_queries_t, grad_keys, grad_values, cells, diag = attention_backward(
        queries, keys, values, grad_context, probs, ops
    )
    table_grad = table_grads(cells, diag)
    grad_mixed = jnp.concatenate([grad_queries_t.T, grad_keys, grad_values], axis=1)
    grad_proj_qkv = rows_inner(start_low, grad_mixed)
    summed = jnp.sum(grad_mixed.astype(F32), axis=0)
    grad_qv_bias = jnp.stack([summed[:D], summed[2 * D :]])
    grad_start = grad_first + times_transposed(grad_mixed, proj_qkv)
    grad_start_low = grad_start.astype(BF16)
    grad_hidden = to_positions(grad_start_low.reshape(1, WINLEN, D))
    grad_proj_box = rows_inner(features, grad_start_low)
    grad_list = (
        grad_proj_qkv,
        grad_proj_out,
        grad_proj_box,
        grad_proj_in,
        grad_proj_back,
        grad_qv_bias,
        grad_out_bias,
        grad_norm_one,
        grad_in_bias,
        grad_back_bias,
        grad_norm_two,
        table_grad,
    )
    padding = jnp.zeros((shard_len * groups * lax.axis_size("dp") - USED,), BF16)
    grads_flat = jnp.concatenate([piece.astype(BF16).reshape(-1) for piece in grad_list] + [padding])
    grad_share = lax.psum_scatter(
        grads_flat, ("dp", "head"), scatter_dimension=0, tiled=True
    ).astype(F32)
    return finish_step(output_low, grad_hidden, grad_share, params, moment_one, moment_two)


def solution(mesh):
    placed = (
        P("dp", "head", None),
        P("dp", "head", None),
        P("dp", None, None),
        P("dp", None),
        P(("dp", "head")),
        P(("dp", "head")),
        P(("dp", "head")),
    )
    return jax.shard_map(
        fast_shards if fits(mesh) else plain_shards,
        mesh=mesh,
        in_specs=placed,
        out_specs=(
            P("dp", "head", None),
            P("dp", "head", None),
            P(("dp", "head")),
            P(("dp", "head")),
            P(("dp", "head")),
        ),
        check_vma=False,
    )
```

```python
import functools
import math

import jax
import jax.numpy as jnp
import numpy as np
from jax import lax
from jax.experimental import pallas as pl
from jax.experimental.pallas import tpu as pltpu
from jax.sharding import PartitionSpec as P

D = 768
HEADS = 12
FF = 3072
BUCKETS = 32
WINLEN = 512
HEAD_DIM = 64
PAIRS = HEADS // 2
LANES = 128
BLOCKS = WINLEN // LANES

beta_one = 0.9
beta_two = 0.999
adam_eps = 1e-08
norm_eps = 1e-05
base_rate = 0.001
layer_decay = 0.75
decay_weight = 0.01
adam_count = 100
coord_cell = 32
masked_score = -1e30

F32 = jnp.float32
BF16 = jnp.bfloat16


def layouts_list():
    return (
        (D, 3 * D),
        (D, D),
        (D, D),
        (D, FF),
        (FF, D),
        (2, D),
        (D,),
        (2, D),
        (FF,),
        (D,),
        (2, D),
        (3, HEADS, BUCKETS),
    )


def unpack(flat_params):
    pieces = []
    offset = 0
    for layout in layouts_list():
        elements = math.prod(layout)
        pieces.append(flat_params[offset : offset + elements].reshape(layout))
        offset += elements
    return pieces


def matmul(left_mat, right_mat):
    return jnp.dot(left_mat, right_mat, preferred_element_type=F32)


def rows_inner(left_mat, right_mat):
    return lax.dot_general(left_mat, right_mat, (((0,), (0,)), ((), ())), preferred_element_type=F32)


def times_transposed(left_mat, right_mat):
    return lax.dot_general(left_mat, right_mat, (((1,), (1,)), ((), ())), preferred_element_type=F32)


def layer_norm(values, gain_bias):
    row_mean = jnp.mean(values, axis=-1, keepdims=True)
    centred = values - row_mean
    spread = jnp.mean(centred * centred, axis=-1, keepdims=True)
    return centred * lax.rsqrt(spread + norm_eps) * gain_bias[0] + gain_bias[1]


def gelu_exact(values):
    return jax.nn.gelu(values, approximate=False)


def hot(index, count):
    return (np.asarray(index)[..., None] == np.arange(count)).astype(np.float32)


def clipped(steps):
    return np.clip(steps, -(BUCKETS // 2), BUCKETS // 2 - 1) + BUCKETS // 2


CELLS = np.arange(BUCKETS)
HOT_SAME = hot(clipped(CELLS[:, None] - CELLS[None, :]), BUCKETS)
HOT_LESS = hot(clipped(CELLS[:, None] - CELLS[None, :] - 1), BUCKETS)
WIDE = 6 * LANES
_U = np.arange(WIDE)
BAND_HOT = hot(np.where(_U < 5 * LANES, clipped(_U - 2 * LANES), 0), BUCKETS)
_V = np.arange(4 * LANES)
DIAG_HOT = np.concatenate(
    [
        hot(np.zeros(LANES, np.int64), BUCKETS),
        hot(np.where(_V < 3 * LANES, clipped(_V - LANES), 0), BUCKETS),
        hot(np.full(LANES, BUCKETS - 1), BUCKETS),
    ]
)


def window_layout(doc_lengths, box_coords):
    doc_ends = jnp.cumsum(doc_lengths, dtype=jnp.int32)
    doc_starts = doc_ends - doc_lengths
    places = jnp.arange(WINLEN, dtype=jnp.int32)
    doc_ids = jnp.sum(
        (places[:, None] >= doc_ends[None, :]).astype(jnp.int32), axis=1, dtype=jnp.int32
    )
    docs = jnp.arange(doc_lengths.shape[0], dtype=jnp.int32)
    chosen = doc_ids[:, None] == docs[None, :]
    first_hot = places[:, None] == doc_starts[None, :]
    first_box = jnp.sum(
        jnp.where(first_hot[:, :, None], box_coords[:, None, :], 0), axis=0, dtype=jnp.int32
    )
    anchor = jnp.sum(
        jnp.where(chosen[:, :, None], first_box[None, :, :], 0), axis=1, dtype=jnp.int32
    )
    relative = box_coords - jnp.concatenate([anchor[:, :2], anchor[:, :2]], axis=1)
    centre_x = (box_coords[:, 0] + box_coords[:, 2]) // 2
    centre_y = (box_coords[:, 1] + box_coords[:, 3]) // 2
    return chosen, relative, centre_x, centre_y


def box_features(relative):
    count_freq = D // 8
    steps = jnp.arange(count_freq, dtype=F32)
    frequency = jnp.exp(steps * (-math.log(1000.0) / count_freq))
    angles = relative.astype(F32)[:, :, None] * frequency[None, None, :]
    return jnp.concatenate([jnp.sin(angles), jnp.cos(angles)], axis=2).reshape(relative.shape[0], D)


def bias_operands(tables, chosen, centre_x, centre_y):
    cell_x, cell_y = centre_x // coord_cell, centre_y // coord_cell
    rest_x, rest_y = centre_x % coord_cell, centre_y % coord_cell
    cells = jnp.arange(BUCKETS, dtype=jnp.int32)
    hot_x = (cell_x[:, None] == cells[None, :]).astype(BF16)
    hot_y = (cell_y[:, None] == cells[None, :]).astype(BF16)
    none = jnp.zeros_like(hot_x)
    hot_two = jnp.concatenate([hot_x, hot_y, hot_x, hot_y], axis=1)
    key_x = jnp.stack(
        [
            jnp.concatenate([hot_x, -hot_x, none, none], axis=1),
            jnp.concatenate([none, none, hot_x, -hot_x], axis=1),
        ]
    )
    key_y = jnp.stack(
        [
            jnp.concatenate([hot_y, -hot_y, none, none], axis=1),
            jnp.concatenate([none, none, hot_y, -hot_y], axis=1),
        ]
    )
    same = jnp.einsum("qcb,thb->thqc", HOT_SAME.astype(BF16), tables[1:], preferred_element_type=F32)
    less = jnp.einsum("qcb,thb->thqc", HOT_LESS.astype(BF16), tables[1:], preferred_element_type=F32)
    zero = jnp.zeros_like(same[0])
    base = jnp.concatenate(
        [jnp.concatenate([same[0], zero], axis=2), jnp.concatenate([zero, same[1]], axis=2)], axis=1
    )
    base = base.reshape(PAIRS, 2, 64, 64)[:, ::-1].reshape(HEADS, 64, 64)
    diff_x = jnp.concatenate([jnp.concatenate([less[0], same[0]], axis=2), jnp.zeros((HEADS, 32, 64), F32)], axis=1)
    diff_y = jnp.concatenate([jnp.zeros((HEADS, 32, 64), F32), jnp.concatenate([less[1], same[1]], axis=2)], axis=1)
    rows = jnp.concatenate([base, diff_x, diff_y], axis=0).astype(BF16)
    rows = rows.transpose(1, 0, 2).reshape(64, 3 * D)
    met = matmul(hot_two[:, :64], rows).astype(BF16)
    band = matmul(tables[0], jnp.asarray(BAND_HOT.T, BF16)).reshape(HEADS, 1, WIDE)
    rest_cols = jnp.stack([rest_x, rest_y], axis=1).astype(F32)
    rest_rows = rest_cols.T
    pad = jnp.zeros((WINLEN, LANES - chosen.shape[1]), BF16)
    marks = chosen.astype(BF16)
    mark_keys = jnp.concatenate([marks, pad], axis=1)
    mark_queries = jnp.concatenate([(1 - marks) * jnp.asarray(masked_score, BF16), pad], axis=1)
    return dict(
        hot_two=hot_two,
        key_x=key_x,
        key_y=key_y,
        met=met,
        band=band,
        rest_cols=rest_cols,
        rest_rows=rest_rows,
        mark_keys=mark_keys,
        mark_queries=mark_queries,
    )


def half_masks():
    lane = lax.broadcasted_iota(jnp.int32, (1, LANES), 1)
    low = (lane < HEAD_DIM).astype(F32)
    return low.astype(BF16), (1.0 - low).astype(BF16)


def less_masks(rest_cols, rest_rows, less_x, less_y):
    for part in range(BLOCKS):
        rows = slice(part * LANES, (part + 1) * LANES)
        for axis, less in ((0, less_x), (1, less_y)):
            column = rest_cols[rows, axis : axis + 1]
            row = rest_rows[axis : axis + 1, :]
            less[rows, :] = jnp.where(row < column, 1.0, 0.0).astype(less.dtype)


def attention_forward_kernel(
    q_ref, k_ref, v_ref, hot_ref, keyx_ref, keyy_ref, met_ref, band_ref, cols_ref, rows_ref,
    mkey_ref, mquery_ref, probs_ref, context_ref,
    kaug, qaug, less_x, less_y, wide, scores,
):
    low, high = half_masks()
    less_masks(cols_ref, rows_ref, less_x, less_y)
    kaug[:, LANES:] = mkey_ref[...]
    qaug[:, LANES:] = mquery_ref[...]
    half = 2 * LANES

    def one_pair(pair, carry):
        at = pl.multiple_of(pair * LANES, LANES)
        lanes = pl.ds(at, LANES)
        lanes_x = pl.ds(pl.multiple_of(at + D, LANES), LANES)
        lanes_y = pl.ds(pl.multiple_of(at + 2 * D, LANES), LANES)
        values_t = v_ref[:, lanes].T
        for odd in range(2):
            own, other = (low, high) if odd == 0 else (high, low)
            head = 2 * pair + odd
            kaug[:, :LANES] = k_ref[:, lanes] * own + hot_ref[...] * other
            qaug[:, :LANES] = q_ref[:, lanes] * own + met_ref[:, lanes] * other
            skew_band(band_ref[head], wide)
            for side in range(2):
                cols = slice(side * half, (side + 1) * half)
                top = None
                for part in range(BLOCKS):
                    rows = slice(part * LANES, (part + 1) * LANES)
                    s = times_transposed(kaug[rows, :], qaug[cols, :])
                    dx = times_transposed(keyx_ref[odd, rows, :], met_ref[cols, lanes_x])
                    dy = times_transposed(keyy_ref[odd, rows, :], met_ref[cols, lanes_y])
                    bias = []
                    for block in range(2 * side, 2 * side + 2):
                        step = max(-2, min(2, block - part)) + 2
                        bias.append(wide[:, step * LANES : (step + 1) * LANES])
                    s = s + jnp.concatenate(bias, axis=1)
                    s = s + dx * less_x[rows, cols] + dy * less_y[rows, cols]
                    scores[rows, :] = s
                    best = jnp.max(s, axis=0, keepdims=True)
                    top = best if top is None else jnp.maximum(top, best)
                total = None
                for part in range(BLOCKS):
                    rows = slice(part * LANES, (part + 1) * LANES)
                    e = jnp.exp(scores[rows, :] - top)
                    scores[rows, :] = e
                    add = jnp.sum(e, axis=0, keepdims=True)
                    total = add if total is None else total + add
                share = 1.0 / total
                for part in range(BLOCKS):
                    rows = slice(part * LANES, (part + 1) * LANES)
                    probs_ref[head, rows, cols] = (scores[rows, :] * share).astype(BF16)
                got = matmul(
                    values_t[odd * HEAD_DIM : (odd + 1) * HEAD_DIM, :], probs_ref[head, :, cols]
                )
                context_ref[pl.ds(pl.multiple_of(head * HEAD_DIM, HEAD_DIM), HEAD_DIM), cols] = (
                    got.astype(BF16)
                )
        return carry

    lax.fori_loop(0, PAIRS, one_pair, 0)


def skew_band(row, wide):
    x = jnp.broadcast_to(row, (8, WIDE))
    sub = lax.broadcasted_iota(jnp.int32, (8, WIDE), 0)
    for bit in (1, 2, 4):
        x = jnp.where((sub & bit) != 0, pltpu.roll(x, bit, 1), x)
    for group in range(LANES // 8):
        y = x if group == 0 else pltpu.roll(x, 8 * group, 1)
        wide[8 * group : 8 * group + 8, :] = y[:, : 5 * LANES]


def skew_groups(skewed, wide):
    for group in range(LANES // 8):
        y = skewed if group == 0 else pltpu.roll(skewed, 8 * group, 1)
        wide[8 * group : 8 * group + 8, :] = y[:, : 5 * LANES]


def diagonal_sums(parts):
    total = None
    for group in range(LANES // 8):
        x = jnp.concatenate(
            [parts[8 * group : 8 * group + 8, LANES : 4 * LANES], jnp.zeros((8, LANES), F32)], axis=1
        )
        y = x if group == 0 else pltpu.roll(x, 4 * LANES - 8 * group, 1)
        total = y if total is None else total + y
    sub = lax.broadcasted_iota(jnp.int32, (8, 4 * LANES), 0)
    for bit in (1, 2, 4):
        total = jnp.where((sub & bit) != 0, pltpu.roll(total, 4 * LANES - bit, 1), total)
    return jnp.sum(total, axis=0, keepdims=True)


def attention_backward_kernel(
    q_ref, k_ref, v_ref, dctx_ref, probs_ref, hot_ref, cols_ref, rows_ref,
    dq_ref, dk_ref, dv_ref, cells_ref, diag_ref,
    qaug, less_x, less_y, scores, dscores, band, kept, hot_t,
):
    low, high = half_masks()
    less_masks(cols_ref, rows_ref, less_x, less_y)
    hot_t[...] = hot_ref[...].T
    lane = lax.broadcasted_iota(jnp.int32, (1, LANES), 1)
    scale = HEAD_DIM ** (-0.5)
    of_x = jnp.where((lane // BUCKETS) % 2 == 0, 1.0, 0.0)
    cells_x = hot_ref[...] * of_x.astype(BF16)
    cells_y = hot_ref[...] * (1.0 - of_x).astype(BF16)

    def one_pair(pair, carry):
        at = pl.multiple_of(pair * LANES, LANES)
        lanes = pl.ds(at, LANES)
        keys_t = k_ref[:, lanes].T
        for odd in range(2):
            own, other = (low, high) if odd == 0 else (high, low)
            head = 2 * pair + odd
            qaug[...] = q_ref[:, lanes] * own + hot_ref[...] * other
            dctx = dctx_ref[:, lanes]
            dot = None
            for part in range(BLOCKS):
                rows = slice(part * LANES, (part + 1) * LANES)
                dp = times_transposed(v_ref[rows, lanes] * own, dctx)
                scores[rows, :] = dp
                add = jnp.sum(dp * probs_ref[head, rows, :].astype(F32), axis=0, keepdims=True)
                dot = add if dot is None else dot + add
            band[...] = jnp.zeros_like(band)
            for part in range(BLOCKS):
                rows = slice(part * LANES, (part + 1) * LANES)
                probs = probs_ref[head, rows, :]
                ds = probs.astype(F32) * (scores[rows, :] - dot)
                for block in range(BLOCKS):
                    step = max(-2, min(2, block - part)) + 2
                    where = slice(step * LANES, (step + 1) * LANES)
                    band[:, where] = band[:, where] + ds[:, block * LANES : (block + 1) * LANES]
                ds = ds.astype(BF16)
                dscores[rows, :] = ds
                both = matmul(ds, qaug[...])
                less = matmul(ds * less_x[rows, :], cells_x) + matmul(ds * less_y[rows, :], cells_y)
                dv = matmul(probs, dctx)
                kept[odd, 0, rows, :] = both
                kept[odd, 1, rows, :] = less
                kept[odd, 2, rows, :] = dv
            got = matmul(keys_t[odd * HEAD_DIM : (odd + 1) * HEAD_DIM, :], dscores[...])
            dq_ref[pl.ds(pl.multiple_of(head * HEAD_DIM, HEAD_DIM), HEAD_DIM), :] = (
                got * scale
            ).astype(BF16)
            diag_ref[head, :, LANES : 5 * LANES] = diagonal_sums(band)
            diag_ref[head, :, :LANES] = jnp.sum(band[:, :LANES], axis=0, keepdims=True)
            diag_ref[head, :, 5 * LANES :] = jnp.sum(band[:, 4 * LANES :], axis=0, keepdims=True)
            for which in range(2):
                summed = kept[odd, which]
                first = summed.astype(BF16)
                rest = (summed - first.astype(F32)).astype(BF16)
                cells_ref[head, which] = matmul(hot_t[:64, :], first) + matmul(hot_t[:64, :], rest)
        dk_ref[:, lanes] = jnp.where(lane < HEAD_DIM, kept[0, 0], kept[1, 0]).astype(BF16)
        dv_ref[:, lanes] = jnp.where(lane < HEAD_DIM, kept[0, 2], kept[1, 2]).astype(BF16)
        return carry

    lax.fori_loop(0, PAIRS, one_pair, 0)


def attention_forward(queries, keys, values, ops):
    return pl.pallas_call(
        attention_forward_kernel,
        out_shape=(
            jax.ShapeDtypeStruct((HEADS, WINLEN, WINLEN), BF16),
            jax.ShapeDtypeStruct((D, WINLEN), BF16),
        ),
        scratch_shapes=[
            pltpu.VMEM((WINLEN, 2 * LANES), BF16),
            pltpu.VMEM((WINLEN, 2 * LANES), BF16),
            pltpu.VMEM((WINLEN, WINLEN), F32),
            pltpu.VMEM((WINLEN, WINLEN), F32),
            pltpu.VMEM((LANES, 5 * LANES), F32),
            pltpu.VMEM((WINLEN, 2 * LANES), F32),
        ],
        compiler_params=pltpu.CompilerParams(vmem_limit_bytes=48 * 2**20),
        name="attention_forward",
    )(
        queries, keys, values, ops["hot_two"], ops["key_x"], ops["key_y"], ops["met"], ops["band"],
        ops["rest_cols"], ops["rest_rows"], ops["mark_keys"], ops["mark_queries"],
    )


def attention_backward(queries, keys, values, grad_context, probs, ops):
    return pl.pallas_call(
        attention_backward_kernel,
        out_shape=(
            jax.ShapeDtypeStruct((D, WINLEN), BF16),
            jax.ShapeDtypeStruct((WINLEN, D), BF16),
            jax.ShapeDtypeStruct((WINLEN, D), BF16),
            jax.ShapeDtypeStruct((HEADS, 2, 64, LANES), F32),
            jax.ShapeDtypeStruct((HEADS, 1, WIDE), F32),
        ),
        scratch_shapes=[
            pltpu.VMEM((WINLEN, LANES), BF16),
            pltpu.VMEM((WINLEN, WINLEN), BF16),
            pltpu.VMEM((WINLEN, WINLEN), BF16),
            pltpu.VMEM((WINLEN, WINLEN), F32),
            pltpu.VMEM((WINLEN, WINLEN), BF16),
            pltpu.VMEM((LANES, 5 * LANES), F32),
            pltpu.VMEM((2, 3, WINLEN, LANES), F32),
            pltpu.VMEM((LANES, WINLEN), BF16),
        ],
        compiler_params=pltpu.CompilerParams(vmem_limit_bytes=48 * 2**20),
        name="attention_backward",
    )(
        queries, keys, values, grad_context, probs, ops["hot_two"], ops["rest_cols"],
        ops["rest_rows"],
    )


def table_grads(cells, diag):
    exact = lax.Precision.HIGHEST
    pairs = cells.reshape(PAIRS, 2, 2, 64, LANES)
    every = jnp.stack([pairs[:, 0, 0, :, 64:], pairs[:, 1, 0, :, :64]], axis=1).reshape(HEADS, 64, 64)
    less = cells[:, 1]
    less_x, less_y = less[:, :32, :32], less[:, 32:, 32:64]
    all_x, all_y = every[:, :32, :32], every[:, 32:, 32:]
    same = jnp.stack([all_x - less_x, all_y - less_y]).reshape(2 * HEADS, -1)
    below = jnp.stack([less_x, less_y]).reshape(2 * HEADS, -1)
    same_hot = jnp.asarray(HOT_SAME.transpose(1, 0, 2).reshape(-1, BUCKETS))
    less_hot = jnp.asarray(HOT_LESS.transpose(1, 0, 2).reshape(-1, BUCKETS))
    moved = jnp.dot(same, same_hot, precision=exact) + jnp.dot(below, less_hot, precision=exact)
    along = jnp.dot(diag.reshape(HEADS, WIDE), jnp.asarray(DIAG_HOT), precision=exact)
    return jnp.concatenate([along[None], moved.reshape(2, HEADS, BUCKETS)], axis=0)


COLUMNS = 4
CORES = 2
DEPTH = 4
USED = sum(math.prod(layout) for layout in layouts_list())
MATRICES = layouts_list()[:5]
MISC = sum(math.prod(layout) for layout in layouts_list()[5:])
MISC_ROWS = -(-MISC // (8 * LANES)) * 8


class Plan:
    def __init__(self, shard_len, carry=3 * LANES):
        self.rows = shard_len // LANES
        self.quarter = -(-self.rows // (16 * COLUMNS)) * 16
        self.padded = COLUMNS * self.quarter
        self.per_column = CORES * DEPTH * self.rows
        self.carry = carry
        self.staged = self.carry + self.per_column + 3 * LANES
        starts = []
        offset = 0
        for depth, width in MATRICES:
            starts.append(offset // LANES)
            offset += depth * width
        self.starts = starts
        self.misc_start = offset // LANES


def fits(mesh):
    return mesh.shape["dp"] == COLUMNS * CORES and mesh.shape["head"] == DEPTH


MESH = pl.DeviceIdType.MESH


class Place:
    def __init__(self):
        dp = lax.axis_index("dp")
        self.z = lax.axis_index("head")
        self.core = dp % CORES
        self.column = dp // CORES
        self.x = self.column % 2
        self.y = self.column // 2
        self.col_x = 2 * self.y + (1 - self.x)
        self.col_y = 2 * (1 - self.y) + self.x
        self.col_d = 2 * (1 - self.y) + (1 - self.x)
        self.peer_x = self.at(self.col_x, self.core, self.z)
        self.peer_y = self.at(self.col_y, self.core, self.z)
        self.peer_d = self.at(self.col_d, self.core, self.z)
        self.peer_core = self.at(self.column, 1 - self.core, self.z)
        self.far = [lax.rem(self.z + d, DEPTH) for d in range(1, DEPTH)]
        self.from_far = [lax.rem(self.z + DEPTH - d, DEPTH) for d in range(1, DEPTH)]
        self.peers_z = [self.at(self.column, self.core, f) for f in self.far]

    def at(self, column, core, z):
        return {"dp": column * CORES + core, "head": z}

    def greet(self):
        barrier = pltpu.get_barrier_semaphore()
        peers = [self.peer_x, self.peer_y, self.peer_d, self.peer_core] + self.peers_z
        for peer in peers:
            pl.semaphore_signal(barrier, inc=1, device_id=peer, device_id_type=MESH)
        pl.semaphore_wait(barrier, len(peers))


def remote(src, dst, send_sem, recv_sem, peer):
    return pltpu.make_async_remote_copy(
        src_ref=src, dst_ref=dst, send_sem=send_sem, recv_sem=recv_sem, device_id=peer,
        device_id_type=MESH,
    )


class Gathering:
    def __init__(self, place, flat, sems):
        self.place = place
        self.flat = flat
        self.sems = sems
        self.sent = []

    def send(self, src, dst, kind, index, peer):
        copy = remote(src, dst, self.sems[kind].at[0, index], self.sems[kind].at[1, index], peer)
        copy.start()
        self.sent.append(copy)

    def got(self, dst, kind, index):
        remote(
            dst, dst, self.sems[kind].at[0, index], self.sems[kind].at[1, index], self.place.peer_x
        ).wait_recv()

    def spread(self, own):
        p = self.place
        for index, (column, peer) in enumerate(
            ((p.col_x, p.peer_x), (p.col_y, p.peer_y), (p.col_d, p.peer_d))
        ):
            self.send(
                own.at[column], self.flat.at[p.column, p.core, p.z, column], "spread", index, peer
            )
        self.flat[p.column, p.core, p.z, p.column] = own[p.column]

    def spread_done(self):
        p = self.place
        for index, column in enumerate((p.col_x, p.col_y, p.col_d)):
            self.got(self.flat.at[column, p.core, p.z, p.column], "spread", index)

    def along_z(self, k):
        p = self.place
        piece = self.flat.at[k, p.core, p.z, p.column]
        for d in range(DEPTH - 1):
            self.send(piece, piece, "z", 3 * k + d, p.peers_z[d])

    def first(self, k):
        p = self.place
        for d in range(DEPTH - 1):
            self.got(self.flat.at[k, p.core, p.from_far[d], p.column], "z", 3 * k + d)
        piece = self.flat.at[k, p.core, :, p.column]
        self.send(piece, piece, "one", 2 * k, p.peer_x)
        self.send(piece, piece, "one", 2 * k + 1, p.peer_y)
        self.send(piece, piece, "core", 5 * k, p.peer_core)

    def second(self, k):
        p = self.place
        from_x = self.flat.at[k, p.core, :, p.col_x]
        self.got(from_x, "one", 2 * k)
        part = self.flat.at[k, p.core, 0:2, p.col_x]
        self.send(part, part, "two", 2 * k, p.peer_y)
        self.send(from_x, from_x, "core", 5 * k + 1, p.peer_core)
        from_y = self.flat.at[k, p.core, :, p.col_y]
        self.got(from_y, "one", 2 * k + 1)
        part = self.flat.at[k, p.core, 2:4, p.col_y]
        self.send(part, part, "two", 2 * k + 1, p.peer_x)
        self.send(from_y, from_y, "core", 5 * k + 2, p.peer_core)

    def third(self, k):
        p = self.place
        part = self.flat.at[k, p.core, 0:2, p.col_d]
        self.got(part, "two", 2 * k)
        self.send(part, part, "core", 5 * k + 3, p.peer_core)
        part = self.flat.at[k, p.core, 2:4, p.col_d]
        self.got(part, "two", 2 * k + 1)
        self.send(part, part, "core", 5 * k + 4, p.peer_core)

    def complete(self, k):
        p = self.place
        other = 1 - p.core
        for index, column in enumerate((p.column, p.col_x, p.col_y)):
            self.got(self.flat.at[k, other, :, column], "core", 5 * k + index)
        self.got(self.flat.at[k, other, 0:2, p.col_d], "core", 5 * k + 3)
        self.got(self.flat.at[k, other, 2:4, p.col_d], "core", 5 * k + 4)

    def finish(self):
        for copy in self.sent:
            copy.wait_send()


GATHER_SEMS = {"spread": 3, "z": 12, "one": 8, "two": 8, "core": 20}


def sem_shapes(counts):
    return [pltpu.SemaphoreType.DMA((2, count)) for count in counts.values()]


def stage_column(plan, flat, staged, k):
    def one(shard, carry):
        core, z = shard // DEPTH, shard % DEPTH
        for quarter in range(COLUMNS):
            base = plan.carry + shard * plan.rows + quarter * plan.quarter
            staged[pl.ds(pl.multiple_of(base, 8), plan.quarter), :] = flat[k, core, z, quarter].astype(F32)
        return carry

    lax.fori_loop(0, CORES * DEPTH, one, 0)


def keep_carry(plan, staged):
    end = plan.carry + plan.per_column
    staged[: plan.carry, :] = staged[end - plan.carry : end, :]


ROW_STEP = 48


def column_rows(plan, k, touching):
    low, high = k * plan.per_column, (k + 1) * plan.per_column
    taken = []
    for index, (depth, width) in enumerate(MATRICES):
        group = 16 * (width // LANES)
        from_low, from_high = low - plan.starts[index], high - plan.starts[index]
        begin = max(0, min(depth, from_low // group * 16))
        if touching:
            end = max(0, min(depth, -(-from_high // group) * 16))
        else:
            end = max(0, min(depth, from_high // group * 16))
        if end > begin:
            taken.append((index, begin, end))
    return taken


def staged_at(plan, k, row):
    return plan.carry + row - k * plan.per_column


def row_loops(rows):
    whole = rows // ROW_STEP
    loops = [(ROW_STEP, 0, whole)] if whole else []
    if rows % ROW_STEP:
        loops.append((16, whole * ROW_STEP, (rows % ROW_STEP) // 16))
    return loops


def form_matrices(plan, staged, matrices, k):
    for index, begin, end in column_rows(plan, k, False):
        blocks = MATRICES[index][1] // LANES
        base = staged_at(plan, k, plan.starts[index] + begin * blocks)
        assert 0 <= base
        target = matrices[index]
        for step_rows, first, count in row_loops(end - begin):

            def one(step, carry, step_rows=step_rows, first=first, blocks=blocks, base=base,
                    begin=begin, target=target):
                row = first + step * step_rows
                for block in range(blocks):
                    got = staged[pl.ds(base + row * blocks + block, step_rows, stride=blocks), :]
                    target[
                        pl.ds(pl.multiple_of(begin + row, 16), step_rows),
                        block * LANES : (block + 1) * LANES,
                    ] = got.astype(BF16)
                return carry

            lax.fori_loop(0, count, one, 0)


def adam_step(params, moment_one, moment_two, grads, flat_index):
    box_part = (flat_index >= 4 * D * D) & (flat_index < 5 * D * D)
    step_rate = jnp.where(box_part, base_rate * layer_decay**12, base_rate * layer_decay)
    decay_mask = jnp.where(flat_index < 5 * D * D + 2 * D * FF, decay_weight, 0.0)
    moment_one = beta_one * moment_one + (1.0 - beta_one) * grads
    moment_two = beta_two * moment_two + (1.0 - beta_two) * grads * grads
    first_hat = moment_one / (1.0 - beta_one**adam_count)
    second_hat = moment_two / (1.0 - beta_two**adam_count)
    update = first_hat / (jnp.sqrt(second_hat) + adam_eps) + decay_mask * params
    return (-step_rate * update, moment_one)


VEC = {}
_at = 0
for _name, _rows in (
    ("q_bias", 6), ("v_bias", 6), ("out_bias", 6), ("gain_one", 6), ("shift_one", 6), ("in_bias", 24),
    ("back_bias", 6), ("gain_two", 6), ("shift_two", 6), ("tables", 9),
):
    VEC[_name] = _at * LANES
    _at += _rows
VEC_ROWS = _at
NOTE_ROWS = 96
NBLOCK = 2 * LANES


def note_place(plan):
    row = plan.misc_start - (CORES * DEPTH * COLUMNS - 1) * plan.rows
    quarter, row = row // plan.quarter, row % plan.quarter
    first = row // 16 * 16
    assert first + NOTE_ROWS <= plan.quarter and row - first + VEC_ROWS <= NOTE_ROWS
    return quarter, first, row - first


def spread_notes(place, own, notes, sems, plan):
    quarter, first, _ = note_place(plan)
    source = own.at[quarter, first : first + NOTE_ROWS]
    home = (place.column == COLUMNS - 1) & (place.core == CORES - 1)
    root = home & (place.z == DEPTH - 1)

    def copy(src, index, peer):
        return remote(src, notes, sems.at[0, index], sems.at[1, 0], peer)

    def arrived():
        copy(notes, 0, place.peer_core).wait_recv()

    @pl.when(root)
    def _():
        notes[...] = own[quarter, first : first + NOTE_ROWS]
        for index, peer in enumerate(place.peers_z):
            copy(source, index, peer).start()

    @pl.when(home & (place.z != DEPTH - 1))
    def _():
        arrived()

    @pl.when(home)
    def _():
        for index, peer in enumerate((place.peer_x, place.peer_y, place.peer_d)):
            copy(notes, 3 + index, peer).start()

    @pl.when((place.core == CORES - 1) & (place.column != COLUMNS - 1))
    def _():
        arrived()

    @pl.when(place.core == CORES - 1)
    def _():
        copy(notes, 6, place.peer_core).start()

    @pl.when(place.core != CORES - 1)
    def _():
        arrived()

    def finish():
        @pl.when(root)
        def _():
            for index, peer in enumerate(place.peers_z):
                copy(source, index, peer).wait_send()

        @pl.when(home)
        def _():
            for index, peer in enumerate((place.peer_x, place.peer_y, place.peer_d)):
                copy(notes, 3 + index, peer).wait_send()

        @pl.when(place.core == CORES - 1)
        def _():
            copy(notes, 6, place.peer_core).wait_send()

    return finish


def turns_table():
    count_freq = D // 8
    freq = np.exp(np.arange(count_freq) * (-math.log(1000.0) / count_freq)) / (2 * math.pi)
    per = np.concatenate([freq, freq])
    phase = np.concatenate([np.zeros(count_freq), np.full(count_freq, 0.25)])
    return np.stack([np.tile(per, 4), np.tile(phase, 4)]).astype(np.float32)


def sin_turns(t):
    t = t - jnp.floor(t + 0.5)
    a = jnp.abs(t)
    m = jnp.minimum(a, 0.5 - a) * (2 * math.pi)
    u = m * m
    poly = -1.0 / 39916800.0
    for term in (1.0 / 362880.0, -1.0 / 5040.0, 1.0 / 120.0, -1.0 / 6.0, 1.0):
        poly = poly * u + term
    s = m * poly
    return jnp.where(t < 0, -s, s)


def token_columns(boxes, lengths, window):
    coords = boxes[window].astype(F32)
    place = lax.broadcasted_iota(jnp.int32, (1, WINLEN), 1)
    doc = jnp.zeros((1, WINLEN), F32)
    anchor = jnp.zeros_like(coords)
    begin = 0
    for d in range(4):
        end = begin + lengths[window, d]
        mine = jnp.where((place >= begin) & (place < end), 1.0, 0.0)
        value = jnp.sum(coords * jnp.where(place == begin, 1.0, 0.0), axis=1, keepdims=True)
        anchor = anchor + value * mine
        doc = doc + mine * float(d)
        begin = end
    anchor = jnp.concatenate([anchor[0:2], anchor[0:2]], axis=0)
    relative = coords - anchor
    centre = jnp.floor((coords[0:2] + coords[2:4]) * 0.5)
    cell = jnp.floor(centre * (1.0 / coord_cell))
    rest = centre - cell * coord_cell
    rows = jnp.concatenate(
        [relative, cell, rest, doc, jnp.zeros((LANES - 9, WINLEN), F32)], axis=0
    )
    return rest, rows.T


def form_features(columns, turns_ref, features):
    lane = lax.broadcasted_iota(jnp.int32, (1, LANES), 1)
    for block in range(D // LANES):
        lanes = slice(block * LANES, (block + 1) * LANES)
        low, high = block * LANES // (D // 4), ((block + 1) * LANES - 1) // (D // 4)
        value = columns[:, low : low + 1]
        if high != low:
            value = jnp.where(
                lane + block * LANES < high * (D // 4), value, columns[:, high : high + 1]
            )
        t = value * turns_ref[0:1, lanes] + turns_ref[1:2, lanes]
        features[:, lanes] = sin_turns(t).astype(BF16)


def form_hots(columns, hot_ref, keyx_ref, keyy_ref, mkey, mquery):
    lane = lax.broadcasted_iota(jnp.int32, (1, LANES), 1)
    part = lane // BUCKETS
    cell = (lane % BUCKETS).astype(F32)
    is_x = jnp.where(columns[:, 4:5] == cell, 1.0, 0.0)
    is_y = jnp.where(columns[:, 5:6] == cell, 1.0, 0.0)
    hot_ref[...] = jnp.where(part % 2 == 0, is_x, is_y).astype(BF16)
    sign = jnp.where(part % 2 == 0, 1.0, -1.0)
    for odd in range(2):
        here = jnp.where(part // 2 == odd, sign, 0.0)
        keyx_ref[odd] = (is_x * here).astype(BF16)
        keyy_ref[odd] = (is_y * here).astype(BF16)
    doc = jnp.where(columns[:, 8:9] == lane.astype(F32), 1.0, 0.0)
    mkey[:, LANES:] = doc.astype(BF16)
    mquery[:, LANES:] = (jnp.where(lane < 4, 1.0 - doc, 0.0) * masked_score).astype(BF16)


def form_tables(tables, bands, tilted):
    row = lax.broadcasted_iota(jnp.int32, (LANES, 1), 0)
    half = BUCKETS // 2
    sub = lax.broadcasted_iota(jnp.int32, (8, LANES), 0)
    sub_wide = lax.broadcasted_iota(jnp.int32, (8, WIDE), 0)
    place = lax.broadcasted_iota(jnp.int32, (1, WIDE), 1)
    wanted = jnp.where(place < 5 * LANES, jnp.clip(place - 2 * LANES, -half, half - 1) + half, 0)
    lane = lax.broadcasted_iota(jnp.int32, (1, LANES), 1)
    turned = jnp.clip(64 - lane, -half, half - 1) + half
    for m in range(4):
        hot_band = jnp.where(row == wanted + m * BUCKETS, 1.0, 0.0).astype(BF16)
        got = matmul(tables, hot_band)
        for n in range(3):
            x = jnp.broadcast_to(got[n : n + 1, :], (8, WIDE))
            for bit in (1, 2, 4):
                x = jnp.where((sub_wide & bit) != 0, pltpu.roll(x, bit, 1), x)
            bands[4 * n + m] = x
        hot_turn = jnp.where(row == turned + m * BUCKETS, 1.0, 0.0).astype(BF16)
        got = matmul(tables, hot_turn)
        for t in (1, 2):
            for n in range(3):
                x = jnp.broadcast_to(got[3 * t + n : 3 * t + n + 1, :], (8, LANES))
                for bit in (1, 2, 4):
                    x = jnp.where((sub & bit) != 0, pltpu.roll(x, bit, 1), x)
                for group in range(BUCKETS // 8):
                    y = x if group == 0 else pltpu.roll(x, 8 * group, 1)
                    tilted[(t - 1) * HEADS + 4 * n + m, 8 * group : 8 * group + 8, :] = y


def pair_rows(tilted, pair):
    lane = lax.broadcasted_iota(jnp.int32, (1, LANES), 1)
    part = lane // BUCKETS
    x0, x1 = tilted[2 * pair], tilted[2 * pair + 1]
    y0, y1 = tilted[HEADS + 2 * pair], tilted[HEADS + 2 * pair + 1]

    def same(value, to):
        return value if to == 64 else pltpu.roll(value, (to - 64) % LANES, 1)

    def less(value, to):
        return pltpu.roll(value, (to - 65) % LANES, 1)

    zero = jnp.zeros_like(x0)
    base_x = jnp.where(part == 0, same(x1, 0), jnp.where(part == 2, same(x0, 64), zero))
    base_y = jnp.where(part == 1, same(y1, 32), jnp.where(part == 3, same(y0, 96), zero))

    def steps(even, odd):
        return jnp.where(
            part < 2,
            jnp.where(part == 0, less(even, 0), same(even, 32)),
            jnp.where(part == 2, less(odd, 64), same(odd, 96)),
        )

    rows = [
        jnp.concatenate([base_x, base_y], axis=0),
        jnp.concatenate([steps(x0, x1), zero], axis=0),
        jnp.concatenate([zero, steps(y0, y1)], axis=0),
    ]
    return jnp.concatenate(rows, axis=1).astype(BF16)


def gelu_and_slope(z):
    a = jnp.abs(z)
    t = 1.0 / (1.0 + (0.3275911 / math.sqrt(2.0)) * a)
    poly = 1.061405429 * 0.5
    for term in (-1.453152027, 1.421413741, -0.284496736, 0.254829592):
        poly = poly * t + 0.5 * term
    e = jnp.exp(-0.5 * z * z)
    tail = poly * t * e
    cdf = jnp.where(z < 0, tail, 1.0 - tail)
    return z * cdf, cdf + z * (e * (1.0 / math.sqrt(2.0 * math.pi)))


def forward_kernel(plan, params_in, hidden_in, cot_in, boxes, lengths, turns, *refs):
    (w_qkv_out, w_out_out, w_in_out, w_back_out, features_out, low_out, q_out, k_out, v_out, probs_out,
     context_out, hat_out, normed_out, vec_out, rstd_out, cot_ref, hot_out, rest_out, share_out) = refs[:19]
    refs = refs[19:]
    (flat, staged, own, w_qkv, w_out, w_box, w_in, w_back, notes, features, hidden, start, start_low, q_ref,
     k_ref, v_ref, hot_ref, key_x, key_y, bands, tilted, wides, scores, context_t, pair_t, hat, narrow,
     square, vec) = refs[:29]
    note_sems, swap_sems, copy_sems, probs_sems = refs[29:33]

    def lend(buffer, slot, lanes):
        return buffer.at[:, slot : slot + lanes]

    less_x, less_y = lend(square, 0, WINLEN), lend(square, WINLEN, WINLEN)
    probs = [lend(square, 2 * WINLEN, WINLEN), lend(square, 3 * WINLEN, WINLEN)]
    kaugs = [lend(narrow, 0, 2 * LANES), lend(narrow, 2 * LANES, 2 * LANES)]
    qaugs = [lend(narrow, 4 * LANES, 2 * LANES), lend(narrow, 6 * LANES, 2 * LANES)]
    met = lend(narrow, 8 * LANES, 3 * LANES)
    place = Place()
    normed_low = hidden
    context = features
    gathering = Gathering(place, flat, dict(zip(GATHER_SEMS, refs[33:])))
    matrices = (w_qkv, w_out, w_box, w_in, w_back)
    written = []

    def write_out(src, dst):
        copy = pltpu.make_async_copy(src, dst, copy_sems.at[len(written)])
        copy.start()
        written.append(copy)

    fetch = pltpu.make_async_copy(params_in, staged.at[: plan.rows], probs_sems.at[0])
    fetch.start()
    place.greet()
    fetch.wait()
    for quarter_at in range(COLUMNS):
        begin = quarter_at * plan.quarter
        own[quarter_at] = staged[begin : begin + plan.quarter, :].astype(BF16)
    gathering.spread(own)

    quarter = WINLEN // DEPTH

    def exchange(source, target, kind):
        rows = pl.ds(pl.multiple_of(place.z * quarter, quarter), quarter)
        for d in range(DEPTH - 1):
            gathering_send(source.at[place.far[d]], target.at[rows], kind, d, place.peers_z[d])

    def gathering_send(src, dst, kind, d, peer):
        copy = remote(src, dst, swap_sems.at[kind, 0, d], swap_sems.at[kind, 1, d], peer)
        copy.start()
        gathering.sent.append(copy)

    def exchanged(target, kind):
        for d in range(DEPTH - 1):
            rows = pl.ds(pl.multiple_of(place.from_far[d] * quarter, quarter), quarter)
            remote(
                target.at[rows], target.at[rows], swap_sems.at[kind, 0, d], swap_sems.at[kind, 1, d],
                place.peer_x,
            ).wait_recv()

    finish_notes = spread_notes(place, own, notes, note_sems, plan)
    own_rows = pl.ds(pl.multiple_of(place.z * quarter, quarter), quarter)
    own_hidden = pltpu.make_async_copy(
        hidden_in.at[place.z], hidden.at[own_rows], swap_sems.at[0, 0, DEPTH - 1]
    )
    own_hidden.start()
    own_cot = pltpu.make_async_copy(
        cot_in.at[place.z], cot_ref.at[own_rows], swap_sems.at[1, 0, DEPTH - 1]
    )
    own_cot.start()
    gathering.spread_done()
    gathering.along_z(0)

    rest, columns = token_columns(boxes, lengths, place.z)
    for part in range(BLOCKS):
        rows = slice(part * LANES, (part + 1) * LANES)
        for axis, less in ((0, less_x), (1, less_y)):
            less[rows, :] = jnp.where(
                rest[axis : axis + 1, :] < columns[rows, 6 + axis : 7 + axis], 1.0, 0.0
            ).astype(BF16)
    rest_out[...] = rest
    form_hots(columns, hot_ref, key_x, key_y, kaugs[0], qaugs[0])
    kaugs[1][:, LANES:] = kaugs[0][:, LANES:]
    qaugs[1][:, LANES:] = qaugs[0][:, LANES:]
    hot_out[...] = hot_ref[...]
    gathering.first(0)
    gathering.along_z(1)
    form_features(columns, turns, features)
    for n in range(D // LANES):
        rows = slice(n * LANES, (n + 1) * LANES)
        context_t[rows, :] = features[:, rows].T
    write_out(context_t, features_out)
    gathering.first(1)
    exchange(hidden_in, hidden, 0)
    gathering.second(0)
    _, _, note_row = note_place(plan)
    for row in range(VEC_ROWS):
        at = note_row + row
        vec[0:1, row * LANES : (row + 1) * LANES] = notes[at // 16 * 16 : at // 16 * 16 + 16, :].astype(
            F32
        )[at % 16 : at % 16 + 1, :]
    vec_out[...] = vec[...]
    table_row = note_row + VEC["tables"] // LANES
    assert table_row % 16 == 0
    form_tables(notes[table_row : table_row + 16, :], bands, tilted)

    gathering.second(1)
    gathering.third(0)
    gathering.complete(0)
    stage_column(plan, flat, staged, 0)
    exchanged(hidden, 0)
    gathering.along_z(2)
    form_matrices(plan, staged, matrices, 0)
    keep_carry(plan, staged)
    gathering.third(1)
    gathering.complete(1)
    stage_column(plan, flat, staged, 1)
    form_matrices(plan, staged, matrices, 1)
    keep_carry(plan, staged)
    write_out(w_qkv, w_qkv_out)
    write_out(w_out, w_out_out)

    own_hidden.wait()
    for n in range(D // NBLOCK):
        lanes = slice(n * NBLOCK, (n + 1) * NBLOCK)
        value = hidden[:, lanes].astype(F32) + matmul(features[...], w_box[:, lanes])
        start[:, lanes] = value
        start_low[:, lanes] = value.astype(BF16)
    write_out(start_low, low_out)
    written[0].wait()

    def project(n, carry):
        at = pl.multiple_of(n * NBLOCK, NBLOCK)
        lanes = pl.ds(at, NBLOCK)
        low = start_low[...]
        bias = vec[0:1, pl.ds(pl.multiple_of(VEC["q_bias"] + at, LANES), NBLOCK)]
        got = matmul(low, w_qkv[:, lanes]) + bias
        q_ref[:, lanes] = (got.astype(BF16).astype(F32) * HEAD_DIM ** (-0.5)).astype(BF16)
        k_ref[:, lanes] = matmul(low, w_qkv[:, pl.ds(pl.multiple_of(at + D, LANES), NBLOCK)]).astype(BF16)
        bias = vec[0:1, pl.ds(pl.multiple_of(VEC["v_bias"] + at, LANES), NBLOCK)]
        got = matmul(low, w_qkv[:, pl.ds(pl.multiple_of(at + 2 * D, LANES), NBLOCK)]) + bias
        v_ref[:, lanes] = got.astype(BF16)
        return carry

    lax.fori_loop(0, D // NBLOCK, project, 0)
    write_out(q_ref, q_out)
    write_out(k_ref, k_out)
    write_out(v_ref, v_out)
    gathering.first(2)
    gathering.along_z(3)

    low, high = half_masks()
    half = 2 * LANES

    def probs_copy(head, odd):
        return pltpu.make_async_copy(probs[odd], probs_out.at[head], probs_sems.at[odd])

    def one_pair(pair, carry):
        at = pl.multiple_of(pair * LANES, LANES)
        lanes = pl.ds(at, LANES)
        values_t = v_ref[:, lanes].T
        met[...] = matmul(hot_ref[:, :64], pair_rows(tilted, pair)).astype(BF16)
        for odd in range(2):
            mine, other = (low, high) if odd == 0 else (high, low)
            kaugs[odd][:, :LANES] = k_ref[:, lanes] * mine + hot_ref[...] * other
            qaugs[odd][:, :LANES] = q_ref[:, lanes] * mine + met[:, :LANES] * other
            skew_groups(bands[2 * pair + odd], wides.at[odd])

            @pl.when(pair > 0)
            def _():
                probs_copy(2 * pair + odd, odd).wait()

        for side in range(2):
            cols = slice(side * half, (side + 1) * half)
            tops = []
            for odd in range(2):
                whole = times_transposed(kaugs[odd][...], qaugs[odd][cols, :])
                steps_x = times_transposed(key_x[odd], met[cols, LANES : 2 * LANES])
                steps_y = times_transposed(key_y[odd], met[cols, 2 * LANES :])
                top = None
                for part in range(BLOCKS):
                    rows = slice(part * LANES, (part + 1) * LANES)
                    bias = []
                    for block in range(2 * side, 2 * side + 2):
                        step = max(-2, min(2, block - part)) + 2
                        bias.append(wides[odd, :, step * LANES : (step + 1) * LANES])
                    s = whole[rows] + jnp.concatenate(bias, axis=1)
                    s = s + steps_x[rows] * less_x[rows, cols].astype(F32)
                    s = s + steps_y[rows] * less_y[rows, cols].astype(F32)
                    scores[odd, rows, :] = s
                    best = jnp.max(s.reshape(LANES // 8, 8, half), axis=0)
                    top = best if top is None else jnp.maximum(top, best)
                tops.append(jnp.max(top, axis=0, keepdims=True))
            for odd in range(2):
                total = None
                for part in range(BLOCKS):
                    rows = slice(part * LANES, (part + 1) * LANES)
                    e = jnp.exp(scores[odd, rows, :] - tops[odd])
                    probs[odd][rows, cols] = e.astype(BF16)
                    add = jnp.sum(e.reshape(LANES // 8, 8, half), axis=0)
                    total = add if total is None else total + add
                share = 1.0 / jnp.sum(total, axis=0, keepdims=True)
                share_out[2 * pair + odd, :, cols] = share
                got = matmul(values_t[odd * HEAD_DIM : (odd + 1) * HEAD_DIM, :], probs[odd][:, cols])
                pair_t[odd * HEAD_DIM : (odd + 1) * HEAD_DIM, cols] = got * share
        for odd in range(2):
            probs_copy(2 * pair + odd, odd).start()
        both = pair_t[...]
        context_t[lanes, :] = both.astype(BF16)
        context[:, lanes] = both.T.astype(BF16)
        return carry

    lax.fori_loop(0, 2, one_pair, 0)
    gathering.first(3)
    exchange(cot_in, cot_ref, 1)
    gathering.second(2)
    lax.fori_loop(2, 4, one_pair, 0)
    gathering.third(2)
    gathering.second(3)
    gathering.complete(2)
    stage_column(plan, flat, staged, 2)
    form_matrices(plan, staged, matrices, 2)
    keep_carry(plan, staged)
    write_out(w_in, w_in_out)
    lax.fori_loop(4, PAIRS, one_pair, 0)
    write_out(context_t, context_out)
    gathering.third(3)

    def vector(name):
        return vec[0:1, VEC[name] : VEC[name] + D]

    for n in range(D // NBLOCK):
        lanes = slice(n * NBLOCK, (n + 1) * NBLOCK)
        bias = vec[0:1, VEC["out_bias"] + n * NBLOCK : VEC["out_bias"] + (n + 1) * NBLOCK]
        start[:, lanes] = start[:, lanes] + matmul(context[...], w_out[:, lanes]) + bias

    step_rows = 64

    def norm_first(n, carry):
        rows = pl.ds(pl.multiple_of(n * step_rows, step_rows), step_rows)
        x = start[rows, :]
        centred = x - jnp.mean(x, axis=1, keepdims=True)
        rstd = lax.rsqrt(jnp.mean(centred * centred, axis=1, keepdims=True) + norm_eps)
        xhat = centred * rstd
        hat[rows, :] = xhat
        rstd_out[rows, :] = jnp.broadcast_to(rstd, (step_rows, LANES))
        normed = xhat * vector("gain_one") + vector("shift_one")
        start[rows, :] = normed
        normed_low[rows, :] = normed.astype(BF16)
        return carry

    lax.fori_loop(0, WINLEN // step_rows, norm_first, 0)
    write_out(hat, hat_out)
    write_out(normed_low, normed_out)

    gathering.complete(3)
    stage_column(plan, flat, staged, 3)
    form_matrices(plan, staged, matrices, 3)
    write_out(w_back, w_back_out)
    for odd in range(2):
        probs_copy(0, odd).wait()
    exchanged(cot_ref, 1)
    own_cot.wait()
    for copy in written[1:]:
        copy.wait()
    finish_notes()
    gathering.finish()


def forward_pass(plan, params, hidden_in, cotangent, boxes, lengths):
    anywhere = pl.BlockSpec(memory_space=pl.ANY)
    vmem = pl.BlockSpec(memory_space=pltpu.VMEM)
    token = (WINLEN, D)

    def hbm(shape, dtype=BF16):
        return jax.ShapeDtypeStruct(shape, dtype), anywhere

    def near(shape, dtype=F32):
        return jax.ShapeDtypeStruct(shape, dtype), vmem

    outs = [
        hbm(MATRICES[0]), hbm(MATRICES[1]), hbm(MATRICES[3]), hbm(MATRICES[4]), hbm((D, WINLEN)), hbm(token),
        hbm(token), hbm(token), hbm(token), hbm((HEADS, WINLEN, WINLEN)), hbm((D, WINLEN)),
        hbm(token, F32), hbm(token), near((1, VEC_ROWS * LANES)), near((WINLEN, LANES)),
        near(token, BF16), near((WINLEN, LANES), BF16), near((2, WINLEN)),
        near((HEADS, 1, WINLEN)),
    ]
    scratch = [
        pltpu.VMEM((COLUMNS, CORES, DEPTH, COLUMNS, plan.quarter, LANES), BF16),
        pltpu.VMEM((plan.staged, LANES), F32),
        pltpu.VMEM((COLUMNS, plan.quarter, LANES), BF16),
    ]
    scratch += [pltpu.VMEM(layout, BF16) for layout in MATRICES]
    scratch += [
        pltpu.VMEM((NOTE_ROWS, LANES), BF16),
        pltpu.VMEM(token, BF16),
        pltpu.VMEM(token, BF16),
        pltpu.VMEM(token, F32),
        pltpu.VMEM(token, BF16),
        pltpu.VMEM(token, BF16),
        pltpu.VMEM(token, BF16),
        pltpu.VMEM(token, BF16),
        pltpu.VMEM((WINLEN, LANES), BF16),
        pltpu.VMEM((2, WINLEN, LANES), BF16),
        pltpu.VMEM((2, WINLEN, LANES), BF16),
        pltpu.VMEM((HEADS, 8, WIDE), F32),
        pltpu.VMEM((2 * HEADS, BUCKETS, LANES), F32),
        pltpu.VMEM((2, LANES, 5 * LANES), F32),
        pltpu.VMEM((2, WINLEN, 2 * LANES), F32),
        pltpu.VMEM((D, WINLEN), BF16),
        pltpu.VMEM((LANES, WINLEN), F32),
        pltpu.VMEM(token, F32),
        pltpu.VMEM((WINLEN, 11 * LANES), BF16),
        pltpu.VMEM((WINLEN, 4 * WINLEN), BF16),
        pltpu.VMEM((1, VEC_ROWS * LANES), F32),
        pltpu.SemaphoreType.DMA((2, 7)),
        pltpu.SemaphoreType.DMA((2, 2, DEPTH)),
        pltpu.SemaphoreType.DMA((16,)),
        pltpu.SemaphoreType.DMA((2,)),
    ]
    return pl.pallas_call(
        functools.partial(forward_kernel, plan),
        out_shape=[shape for shape, _ in outs],
        in_specs=[anywhere] * 3 + [vmem, pl.BlockSpec(memory_space=pltpu.SMEM), vmem],
        out_specs=[spec for _, spec in outs],
        scratch_shapes=scratch + sem_shapes(GATHER_SEMS),
        compiler_params=pltpu.CompilerParams(
            collective_id=0, has_side_effects=True, vmem_limit_bytes=62 * 2**20
        ),
        name="forward_pass",
    )(params, hidden_in, cotangent, boxes, lengths, jnp.asarray(turns_table()))


def token_info(doc_lengths, box_coords):
    places = jnp.arange(WINLEN, dtype=jnp.int32)
    first = places == 0
    doc = jnp.zeros((WINLEN,), jnp.int32)
    end = 0
    for d in range(3):
        end = end + doc_lengths[d]
        doc = doc + (places >= end).astype(jnp.int32)
        first = first | (places == end)
    rows = [box_coords[:, c] for c in range(4)] + [doc, first.astype(jnp.int32)]
    return jnp.stack(rows + [jnp.zeros_like(doc)] * 2).astype(F32)


class Reducing:
    def __init__(self, place, flat, swapped, one, two, deep, piece, result, sems, free):
        self.place = place
        self.flat = flat
        self.swapped = swapped
        self.one = one
        self.two = two
        self.deep = deep
        self.piece = piece
        self.result = result
        self.sems = sems
        self.free = free
        self.sent = {k: [] for k in range(COLUMNS)}

    def send(self, k, src, dst, kind, index, peer):
        copy = remote(src, dst, self.sems[kind].at[0, index], self.sems[kind].at[1, index], peer)
        copy.start()
        self.sent[k].append(copy)

    got = Gathering.got

    def settle(self, k):
        for copy in self.sent.pop(k):
            copy.wait_send()

    def swap(self, k):
        p = self.place
        slot = k % 2
        if k < 2:
            pl.semaphore_wait(self.free.at[slot], 1)
        self.send(k, self.flat.at[slot, 1 - p.core], self.swapped.at[slot], "core", k, p.peer_core)

    def first(self, k):
        p = self.place
        slot = k % 2
        self.got(self.swapped.at[slot], "core", k)

        def one(step, carry):
            z, quarter = step // COLUMNS, step % COLUMNS
            total = self.flat[slot, p.core, z, quarter].astype(F32)
            total = total + self.swapped[slot, z, quarter].astype(F32)
            self.flat[slot, p.core, z, quarter] = total.astype(BF16)
            return carry

        lax.fori_loop(0, DEPTH * COLUMNS, one, 0)
        flat = self.flat
        self.send(k, flat.at[slot, p.core, 0:2, p.col_d], self.one.at[k, 0], "one", 2 * k, p.peer_y)
        self.send(k, flat.at[slot, p.core, 2:4, p.col_d], self.one.at[k, 1], "one", 2 * k + 1, p.peer_x)
        if k >= 2:
            pl.semaphore_signal(
                self.free.at[slot], inc=1, device_id=p.peer_core, device_id_type=MESH
            )

    def second(self, k):
        p = self.place
        slot = k % 2
        for side, column in ((0, p.col_x), (1, p.col_y)):
            self.got(self.one.at[k, side], "one", 2 * k + side)

            def one(step, carry, side=side, column=column):
                z = 2 * side + step
                total = self.flat[slot, p.core, z, column].astype(F32)
                total = total + self.one[k, side, step].astype(F32)
                self.flat[slot, p.core, z, column] = total.astype(BF16)
                return carry

            lax.fori_loop(0, 2, one, 0)
        flat = self.flat
        self.send(k, flat.at[slot, p.core, :, p.col_x], self.two.at[k, 0], "two", 2 * k, p.peer_x)
        self.send(k, flat.at[slot, p.core, :, p.col_y], self.two.at[k, 1], "two", 2 * k + 1, p.peer_y)

    def third(self, k):
        p = self.place
        slot = k % 2
        for side in range(2):
            self.got(self.two.at[k, side], "two", 2 * k + side)

        def one(z, carry):
            total = self.flat[slot, p.core, z, p.column].astype(F32)
            total = total + self.two[k, 0, z].astype(F32) + self.two[k, 1, z].astype(F32)
            self.flat[slot, p.core, z, p.column] = total.astype(BF16)
            return carry

        lax.fori_loop(0, DEPTH, one, 0)
        for d in range(DEPTH - 1):
            self.send(
                k, self.flat.at[slot, p.core, p.far[d], p.column], self.deep.at[k, d], "z", 3 * k + d,
                p.peers_z[d],
            )

    def fourth(self, k):
        p = self.place
        for d in range(DEPTH - 1):
            self.got(self.deep.at[k, d], "z", 3 * k + d)
        total = self.flat[k % 2, p.core, p.z, p.column].astype(F32)
        for d in range(DEPTH - 1):
            total = total + self.deep[k, d].astype(F32)
        self.piece[k] = total.astype(BF16)

    def giving(self, k):
        p = self.place
        sems = self.sems["spread"]
        return remote(
            self.piece.at[k], self.result.at[p.column], sems.at[0, k], sems.at[1, p.column],
            p.at(k, p.core, p.z),
        )

    def give(self, k):
        @pl.when(self.place.column != k)
        def _():
            self.giving(k).start()

    def given(self, k):
        @pl.when(self.place.column != k)
        def _():
            self.giving(k).wait_send()

    def receive(self, out):
        p = self.place
        out[p.column] = self.piece[p.column].astype(F32)
        for column in (p.col_x, p.col_y, p.col_d):
            self.got(self.result.at[column], "spread", column)
            out[column] = self.result[column].astype(F32)


REDUCE_SEMS = {"spread": 4, "z": 12, "one": 8, "two": 8, "core": 4}


def unstage_column(plan, flat, staged, k):
    def one(step, carry):
        shard, quarter = step // COLUMNS, step % COLUMNS
        base = plan.carry + shard * plan.rows + quarter * plan.quarter
        piece = staged[pl.ds(pl.multiple_of(base, 8), plan.quarter), :]
        flat[k % 2, shard // DEPTH, shard % DEPTH, quarter] = piece.astype(BF16)
        return carry

    lax.fori_loop(0, CORES * DEPTH * COLUMNS, one, 0)


class Notes:
    def __init__(self, place, notes, slots, sems):
        self.place, self.notes, self.slots, self.sems = place, notes, slots, sems
        p = place
        self.home = (p.column == COLUMNS - 1) & (p.core == CORES - 1)
        self.root = self.home & (p.z == DEPTH - 1)

    def copy(self, slot, peer):
        return remote(
            self.notes, self.slots.at[slot], self.sems.at[0, 0], self.sems.at[1, slot], peer
        )

    def take(self, slot):
        self.copy(slot, self.place.peer_core).wait_recv()
        self.notes[...] = self.notes[...] + self.slots[slot]

    def start(self):
        p = self.place

        @pl.when(p.core != CORES - 1)
        def _():
            self.copy(0, p.peer_core).start()

    def rise(self):
        p = self.place

        @pl.when(p.core == CORES - 1)
        def _():
            self.take(0)

        @pl.when((p.core == CORES - 1) & (p.column != COLUMNS - 1))
        def _():
            self.copy(1 + p.column, p.at(COLUMNS - 1, p.core, p.z)).start()

    def end(self):
        p = self.place

        @pl.when(self.home)
        def _():
            for slot in range(1, 4):
                self.take(slot)

        @pl.when(self.home & (p.z != DEPTH - 1))
        def _():
            self.copy(4 + p.z, p.at(p.column, p.core, DEPTH - 1)).start()

        @pl.when(self.root)
        def _():
            for slot in range(4, 7):
                self.take(slot)

        @pl.when(jnp.logical_not(self.root))
        def _():
            self.copy(0, p.peer_core).wait_send()


def cell_sums(whole, less):
    lane = lax.broadcasted_iota(jnp.int32, (1, LANES), 1)
    sub = lax.broadcasted_iota(jnp.int32, (8, LANES), 0)
    sums = []
    for axis in range(2):
        rows = slice(axis * BUCKETS, (axis + 1) * BUCKETS)
        every = pltpu.roll(whole[rows], (BUCKETS - axis * BUCKETS) % LANES, 1)
        below = pltpu.roll(less[rows], (BUCKETS - axis * BUCKETS) % LANES, 1)
        inside = (lane >= BUCKETS) & (lane < 2 * BUCKETS)
        every = jnp.where(inside, every, 0.0)
        below = jnp.where(inside, below, 0.0)
        x = every - below + pltpu.roll(below, LANES - 1, 1)
        total = None
        for group in range(BUCKETS // 8):
            y = x[8 * group : 8 * group + 8]
            y = y if group == 0 else pltpu.roll(y, LANES - 8 * group, 1)
            total = y if total is None else total + y
        for bit in (1, 2, 4):
            total = jnp.where((sub & bit) != 0, pltpu.roll(total, LANES - bit, 1), total)
        sums.append(jnp.sum(total, axis=0, keepdims=True))
    return sums


def exact_dot(a, b):
    return jnp.dot(a, b, preferred_element_type=F32, precision=lax.Precision.HIGHEST)


def bucket_rows(cell_ref, diag_ref):
    half = BUCKETS // 2
    column = lax.broadcasted_iota(jnp.int32, (1, LANES), 1)
    row = lax.broadcasted_iota(jnp.int32, (LANES, 1), 0)
    to = jnp.clip(row - BUCKETS, -half, half - 1) + half
    place = lax.broadcasted_iota(jnp.int32, (WIDE, 1), 0)
    along = place - LANES
    far = jnp.where(place < LANES, 0, jnp.where(place < 5 * LANES, 0, BUCKETS - 1))
    along = jnp.where(
        (place >= LANES) & (place < 4 * LANES),
        jnp.clip(along - LANES, -half, half - 1) + half,
        far,
    )
    first, rest = None, None
    zero = jnp.zeros((5, WIDE), F32)
    for m in range(4):
        hot_along = jnp.where(along + m * BUCKETS == column, 1.0, 0.0)
        got = exact_dot(
            jnp.concatenate([diag_ref[4 * n + m] for n in range(3)] + [zero], axis=0), hot_along
        )
        first = got if first is None else first + got
        hot_cell = jnp.where(to + m * BUCKETS == column, 1.0, 0.0)
        rows = [cell_ref[t * HEADS + 4 * n + m] for t in range(2) for n in range(3)]
        got = exact_dot(jnp.concatenate(rows + [zero[:2, :LANES]], axis=0), hot_cell)
        rest = got if rest is None else rest + got
    return jnp.concatenate([first[:3], rest[:6]], axis=0)


def backward_kernel(
    plan, w_back_in, w_in_in, w_out_in, w_qkv_in, normed_in, low_in, features_in,
    context_in, q_in, k_in, v_in, probs_in, hat_in, cot_in, rstd_ref, vec, hot_ref, rest_ref, share_ref,
    *refs,
):
    out, output_pos, hidden_pos, spill = refs[:4]
    (flat, staged, swapped, one_buf, two_buf, deep, piece, result, active, slope, w_back, w_in, w_out,
     turned, context_t, q_ref, k_ref, v_ref, hat, second, branch, dctx, probs, less_x,
     less_y, scores_odd, bands, hot_t, pair_t, scaled, share_cols, vecg, cell_rows, diag_rows, notes, slots,
     ) = refs[4:40]
    load_sems, probs_sems, free, pos_sems, note_sems, spill_sems = refs[40:46]
    place = Place()
    reducing = Reducing(
        place, flat, swapped, one_buf, two_buf, deep, piece, result,
        dict(zip(REDUCE_SEMS, refs[46:])), free,
    )
    climbing = Notes(place, notes, slots, note_sems)
    loads = {}

    def load(name, src, dst):
        loads[name] = pltpu.make_async_copy(src, dst, load_sems.at[len(loads)])
        loads[name].start()

    mixed = active.at[:, : 3 * D]
    grad_attn = branch
    w_qkv = w_in.at[:, : 3 * D]
    hidden_low = dctx
    features_t = w_back.at[:D, :WINLEN]
    low_t = w_out.at[:WINLEN]
    scores = [hat.at[:, :WINLEN], scores_odd]
    dscores = [slope.at[:, :WINLEN], slope.at[:, WINLEN : 2 * WINLEN]]
    output_low = w_out.at[:WINLEN]
    output_low = w_out.at[:WINLEN]
    dscores_x = [slope.at[:, 2 * WINLEN : 3 * WINLEN], slope.at[:, 3 * WINLEN : 4 * WINLEN]]
    dscores_y = [slope.at[:, 4 * WINLEN : 5 * WINLEN], slope.at[:, 5 * WINLEN :]]

    load("normed", normed_in, dctx)
    load("w_in", w_in_in, w_in)
    load("hat", hat_in, hat)
    load("w_back", w_back_in, w_back)
    load("cot", cot_in, branch)

    at = staged_at(plan, COLUMNS - 1, plan.misc_start)
    staged[at:, :] = jnp.zeros((plan.staged - at, LANES), F32)
    place.greet()

    quarter = WINLEN // DEPTH
    positions = []

    def to_pos(source, target, kind):
        for d in range(DEPTH - 1):
            rows = pl.ds(pl.multiple_of(place.far[d] * quarter, quarter), quarter)
            copy = remote(
                source.at[rows], target.at[place.z], pos_sems.at[kind, 0, d], pos_sems.at[kind, 1, d],
                place.peers_z[d],
            )
            copy.start()
            positions.append(copy)
        rows = pl.ds(pl.multiple_of(place.z * quarter, quarter), quarter)
        copy = pltpu.make_async_copy(
            source.at[rows], target.at[place.z], pos_sems.at[kind, 0, DEPTH - 1]
        )
        copy.start()
        return copy

    def in_pos(target, kind):
        for d in range(DEPTH - 1):
            there = target.at[place.from_far[d]]
            remote(
                there, there, pos_sems.at[kind, 0, d], pos_sems.at[kind, 1, d], place.peer_x
            ).wait_recv()


    def store(k, index, row, value, first_block=0):
        blocks = MATRICES[index][1] // LANES
        base = staged_at(plan, k, plan.starts[index]) + row * blocks + first_block
        for block in range(value.shape[1] // LANES):
            staged[pl.ds(base + block, value.shape[0], stride=blocks), :] = value[
                :, block * LANES : (block + 1) * LANES
            ]

    def column_sum(value):
        return jnp.sum(value, axis=0, keepdims=True)

    def keep_vector(name, lanes_at, value):
        at = pl.multiple_of(VEC[name] + lanes_at, LANES)
        vecg[0:1, pl.ds(at, value.shape[1])] = value

    def vector(name, at=0, size=D):
        return vec[0:1, pl.ds(pl.multiple_of(VEC[name] + at, LANES), size)]

    loads["normed"].wait()
    loads["w_in"].wait()

    def widen(n, carry):
        at = pl.multiple_of(n * NBLOCK, NBLOCK)
        lanes = pl.ds(at, NBLOCK)
        inner_act = matmul(dctx[...], w_in[:, lanes]) + vector("in_bias", at, NBLOCK)
        value, change = gelu_and_slope(inner_act)
        active[:, lanes] = value.astype(BF16)
        slope[:, lanes] = change.astype(BF16)
        return carry

    lax.fori_loop(0, FF // NBLOCK, widen, 0, unroll=2)
    loads["hat"].wait()
    loads["w_back"].wait()
    for n in range(D // NBLOCK):
        lanes = slice(n * NBLOCK, (n + 1) * NBLOCK)
        normed = hat[:, lanes] * vector("gain_one", n * NBLOCK, NBLOCK) + vector(
            "shift_one", n * NBLOCK, NBLOCK
        )
        second[:, lanes] = (
            normed + matmul(active[...], w_back[:, lanes]) + vector("back_bias", n * NBLOCK, NBLOCK)
        )
    loads["cot"].wait()
    step_rows = 64
    for name in ("gain_two", "shift_two", "back_bias", "gain_one", "shift_one", "out_bias"):
        keep_vector(name, 0, jnp.zeros((1, D), F32))

    def add_vector(name, term):
        lanes = slice(VEC[name], VEC[name] + D)
        vecg[0:1, lanes] = vecg[0:1, lanes] + column_sum(term)

    def norm_second(n, carry):
        rows = pl.ds(pl.multiple_of(n * step_rows, step_rows), step_rows)
        x = second[rows, :]
        centred = x - jnp.mean(x, axis=1, keepdims=True)
        rstd = lax.rsqrt(jnp.mean(centred * centred, axis=1, keepdims=True) + norm_eps)
        xhat = centred * rstd
        gain = vector("gain_two")
        output_low[rows, :] = (xhat * gain + vector("shift_two")).astype(BF16)
        cot = branch[rows, :].astype(F32)
        prod = cot * xhat
        gc = cot * gain
        mean_one = jnp.mean(gc, axis=1, keepdims=True)
        mean_two = jnp.mean(prod * gain, axis=1, keepdims=True)
        value = rstd * (gc - mean_one - xhat * mean_two)
        second[rows, :] = value
        value = value.astype(BF16)
        branch[rows, :] = value
        add_vector("gain_two", prod)
        add_vector("shift_two", cot)
        add_vector("back_bias", value.astype(F32))
        return carry

    lax.fori_loop(0, WINLEN // step_rows, norm_second, 0, unroll=2)
    own_output = to_pos(output_low, output_pos, 0)

    def back_rows(k, size, begin, count):
        def body(n, carry):
            row = pl.multiple_of(begin + n * size, LANES)
            turned[:size, :] = active[:, pl.ds(row, size)].T
            store(k, 4, row, matmul(turned[:size, :], branch[...]))
            return carry

        lax.fori_loop(0, count, body, 0)

    back_rows(3, WINLEN, 512, FF // WINLEN - 1)
    unstage_column(plan, flat, staged, 3)
    reducing.swap(3)

    back_rows(2, WINLEN, 0, 1)
    back_rows(2, LANES, 512, 1)

    def inner(n, carry):
        at = pl.multiple_of(n * NBLOCK, NBLOCK)
        lanes = pl.ds(at, NBLOCK)
        value = times_transposed(branch[...], w_back[lanes, :]) * slope[:, lanes].astype(F32)
        value = value.astype(BF16)
        slope[:, lanes] = value
        keep_vector("in_bias", at, column_sum(value.astype(F32)))
        return carry

    lax.fori_loop(0, FF // NBLOCK, inner, 0, unroll=2)
    grad_inner = slope
    reducing.first(3)

    for n in range(D // NBLOCK):
        rows = slice(n * NBLOCK, (n + 1) * NBLOCK)
        turned[rows, :] = dctx[:, rows].T

    def in_rows(k, begin, end):
        def body(n, carry):
            lanes = pl.ds(pl.multiple_of(n * NBLOCK, NBLOCK), NBLOCK)
            got = matmul(turned[begin:end, :], grad_inner[:, lanes])
            store(k, 3, begin, got, n * (NBLOCK // LANES))
            return carry

        lax.fori_loop(0, FF // NBLOCK, body, 0)

    in_rows(2, 288, D)
    unstage_column(plan, flat, staged, 2)
    reducing.swap(2)
    reducing.second(3)

    load("context", context_in, context_t)
    load("q", q_in, q_ref)
    load("k", k_in, k_ref)
    load("v", v_in, v_ref)
    for odd in range(2):
        pltpu.make_async_copy(probs_in.at[odd], probs.at[odd], probs_sems.at[odd]).start()
    for n in range(D // NBLOCK):
        lanes = slice(n * NBLOCK, (n + 1) * NBLOCK)
        second[:, lanes] = second[:, lanes] + times_transposed(grad_inner[...], w_in[lanes, :])
    load("w_qkv", w_qkv_in, w_qkv)
    load("features", features_in, features_t)
    reducing.first(2)

    for copy in positions:
        copy.wait_send()
    own_output.wait()
    load("w_out", w_out_in, w_out)

    def norm_first(n, carry):
        rows = pl.ds(pl.multiple_of(n * step_rows, step_rows), step_rows)
        grad = second[rows, :]
        xhat = hat[rows, :]
        prod = grad * xhat
        gain = vec[0:1, VEC["gain_one"] : VEC["gain_one"] + D]
        gc = grad * gain
        mean_one = jnp.mean(gc, axis=1, keepdims=True)
        mean_two = jnp.mean(prod * gain, axis=1, keepdims=True)
        value = rstd_ref[rows, 0:1] * (gc - mean_one - xhat * mean_two)
        second[rows, :] = value
        value = value.astype(BF16)
        grad_attn[rows, :] = value
        add_vector("gain_one", prod)
        add_vector("shift_one", grad)
        add_vector("out_bias", value.astype(F32))
        return carry

    lax.fori_loop(0, WINLEN // step_rows, norm_first, 0, unroll=2)
    reducing.third(3)
    loads["w_out"].wait()
    for n in range(D // NBLOCK):
        lanes = slice(n * NBLOCK, (n + 1) * NBLOCK)
        dctx[:, lanes] = times_transposed(grad_attn[...], w_out[lanes, :]).astype(BF16)
    load("low", low_in, low_t)
    loads["context"].wait()
    in_rows(1, 0, 304)
    reducing.second(2)

    def out_rows(k, begin, end):
        for n in range(D // NBLOCK):
            lanes = slice(n * NBLOCK, (n + 1) * NBLOCK)
            got = matmul(context_t[begin:end, :], grad_attn[:, lanes])
            store(k, 1, begin, got, n * (NBLOCK // LANES))

    out_rows(1, 192, D)
    reducing.fourth(3)
    reducing.give(3)

    low, high = half_masks()
    rest = rest_ref[...]
    columns = jnp.concatenate([rest, jnp.zeros((LANES - 2, WINLEN), F32)], axis=0).T
    for part in range(BLOCKS):
        rows = slice(part * LANES, (part + 1) * LANES)
        for axis, less in ((0, less_x), (1, less_y)):
            less[rows, :] = jnp.where(
                rest[axis : axis + 1, :] < columns[rows, axis : axis + 1], 1.0, 0.0
            ).astype(BF16)
    hot_t[...] = hot_ref[...].T
    lane = lax.broadcasted_iota(jnp.int32, (1, LANES), 1)
    scale = HEAD_DIM ** (-0.5)
    of_x = jnp.where((lane // BUCKETS) % 2 == 0, 1.0, 0.0)
    share_cols[...] = jnp.concatenate(
        [share_ref[head] for head in range(HEADS)] + [jnp.zeros((LANES - HEADS, WINLEN), F32)], axis=0
    ).T
    for name in ("q", "k", "v"):
        loads[name].wait()

    def probs_copy(head, odd):
        return pltpu.make_async_copy(probs_in.at[head], probs.at[odd], probs_sems.at[odd])

    def spill_copy(head, odd):
        return pltpu.make_async_copy(dscores[odd], spill.at[head], spill_sems.at[odd])

    def one_pair(pair, carry):
        at = pl.multiple_of(pair * LANES, LANES)
        lanes = pl.ds(at, LANES)
        keys_t = k_ref[:, lanes].T
        both = pltpu.roll(share_cols[...], lax.rem(LANES - 2 * pair, LANES), 1)
        both = jnp.where(lane < HEAD_DIM, both[:, 0:1], both[:, 1:2])
        scaled[...] = (dctx[:, lanes].astype(F32) * both).astype(BF16)
        grad_context = dctx[:, lanes]
        dots = []
        for odd in range(2):
            mine, other = (low, high) if odd == 0 else (high, low)
            head = 2 * pair + odd
            probs_copy(head, odd).wait()
            products = times_transposed(v_ref[:, lanes] * mine, grad_context)
            dot = None
            for part in range(BLOCKS):
                rows = slice(part * LANES, (part + 1) * LANES)
                dp = products[rows]
                scores[odd][rows, :] = dp
                add = dp * probs[odd, rows, :].astype(F32)
                add = jnp.sum(add.reshape(LANES // 8, 8, WINLEN), axis=0)
                dot = add if dot is None else dot + add
            dots.append(column_sum(dot) * share_ref[head])
        for odd in range(2):
            head = 2 * pair + odd
            share = share_ref[head]

            @pl.when(pair > 0)
            def _():
                spill_copy(head, odd).wait()

            for part in range(BLOCKS):
                rows = slice(part * LANES, (part + 1) * LANES)
                ds = probs[odd, rows, :].astype(F32) * ((scores[odd][rows, :] - dots[odd]) * share)
                dscores[odd][rows, :] = ds.astype(BF16)
            spill_copy(head, odd).start()
        for odd in range(2):
            head = 2 * pair + odd
            keys_grad = matmul(dscores[odd][...], q_ref[:, lanes])
            values_grad = matmul(probs[odd], scaled[...])

            pair_t[odd * HEAD_DIM : (odd + 1) * HEAD_DIM, :] = matmul(
                keys_t[odd * HEAD_DIM : (odd + 1) * HEAD_DIM, :], dscores[odd][...]
            )
            for which, value in ((1, keys_grad), (2, values_grad)):
                there = pl.ds(pl.multiple_of(at + which * D, LANES), LANES)
                value = value.astype(BF16)
                if odd:
                    value = mixed[:, there] * low + value * high
                mixed[:, there] = value

        @pl.when(pair < PAIRS - 1)
        def _():
            for odd in range(2):
                probs_copy(2 * pair + odd + 2, odd).start()

        value = (pair_t[...].T * scale).astype(BF16)
        mixed[:, lanes] = value
        keep_vector("q_bias", at, column_sum(value.astype(F32)))
        there = pl.ds(pl.multiple_of(at + 2 * D, LANES), LANES)
        keep_vector("v_bias", at, column_sum(mixed[:, there].astype(F32)))
        return carry

    lax.fori_loop(0, 2, one_pair, 0)
    reducing.third(2)
    lax.fori_loop(2, 4, one_pair, 0)
    reducing.fourth(2)
    reducing.give(2)
    lax.fori_loop(4, PAIRS, one_pair, 0)

    for odd in range(2):
        spill_copy(0, odd).wait()
    loads["w_qkv"].wait()
    for n in range(D // NBLOCK):
        lanes = slice(n * NBLOCK, (n + 1) * NBLOCK)
        value = second[:, lanes] + times_transposed(mixed[...], w_qkv[lanes, :])
        hidden_low[:, lanes] = value.astype(BF16)
    own_hidden = to_pos(hidden_low, hidden_pos, 1)
    loads["features"].wait()
    for n in range(D // NBLOCK):
        lanes = slice(n * NBLOCK, (n + 1) * NBLOCK)
        store(1, 2, 0, matmul(features_t[...], hidden_low[:, lanes]), n * (NBLOCK // LANES))
    reducing.settle(3)
    unstage_column(plan, flat, staged, 1)
    reducing.swap(1)

    loads["low"].wait()
    for n in range(D // NBLOCK):
        rows = slice(n * NBLOCK, (n + 1) * NBLOCK)
        turned[rows, :] = low_t[:, rows].T

    def qkv_rows(n, carry):
        lanes = pl.ds(pl.multiple_of(n * NBLOCK, NBLOCK), NBLOCK)
        store(0, 0, 0, matmul(turned[...], mixed[:, lanes]), n * (NBLOCK // LANES))
        return carry

    lax.fori_loop(0, 3 * D // NBLOCK, qkv_rows, 0)
    out_rows(0, 0, 208)
    reducing.settle(2)
    unstage_column(plan, flat, staged, 0)
    reducing.swap(0)

    def fetch_scores(head):
        there = slope.at[:, pl.ds(pl.multiple_of(lax.rem(head, 2) * WINLEN, WINLEN), WINLEN)]
        return pltpu.make_async_copy(spill.at[head], there, spill_sems.at[lax.rem(head, 2)])

    cells = [hot_ref[...] * of_x.astype(BF16), hot_ref[...] * (1.0 - of_x).astype(BF16)]
    band = bands.at[0]
    parts_x = slope.at[:, 2 * WINLEN : 3 * WINLEN]
    parts_y = slope.at[:, 3 * WINLEN : 4 * WINLEN]

    def one_table(head, carry):
        fetch_scores(head).wait()

        @pl.when(head < HEADS - 1)
        def _():
            fetch_scores(head + 1).start()

        here = slope.at[:, pl.ds(pl.multiple_of(lax.rem(head, 2) * WINLEN, WINLEN), WINLEN)]
        band[...] = jnp.zeros_like(band)
        for part in range(BLOCKS):
            rows = slice(part * LANES, (part + 1) * LANES)
            low_ds = here[rows, :]
            parts_x[rows, :] = low_ds * less_x[rows, :]
            parts_y[rows, :] = low_ds * less_y[rows, :]
            ds = low_ds.astype(F32)
            for block in range(BLOCKS):
                step = max(-2, min(2, block - part)) + 2
                where = slice(step * LANES, (step + 1) * LANES)
                band[:, where] = band[:, where] + ds[:, block * LANES : (block + 1) * LANES]
        whole = matmul(here[...], hot_ref[...])
        less = matmul(parts_x[...], cells[0]) + matmul(parts_y[...], cells[1])
        diag_rows[head, :, LANES : 5 * LANES] = diagonal_sums(band)
        diag_rows[head, :, :LANES] = column_sum(band[:, :LANES])
        diag_rows[head, :, 5 * LANES :] = column_sum(band[:, 4 * LANES :])
        sums = []
        for summed in (whole, less):
            first = summed.astype(BF16)
            remainder = (summed - first.astype(F32)).astype(BF16)
            sums.append(matmul(hot_t[:64, :], first) + matmul(hot_t[:64, :], remainder))
        for axis, value in enumerate(cell_sums(sums[0], sums[1])):
            cell_rows[axis * HEADS + head] = value
        return carry

    fetch_scores(0).start()
    reducing.first(1)
    lax.fori_loop(0, 4, one_table, 0)
    reducing.first(0)
    reducing.second(1)
    lax.fori_loop(4, 8, one_table, 0)
    reducing.second(0)
    lax.fori_loop(8, HEADS, one_table, 0)
    notes[...] = jnp.zeros_like(notes)
    table = VEC["tables"] // LANES
    for row in range(table):
        notes[row : row + 1, :] = vecg[0:1, row * LANES : (row + 1) * LANES]
    notes[table : table + 9, :] = bucket_rows(cell_rows, diag_rows)
    climbing.start()
    reducing.third(1)
    climbing.rise()
    reducing.third(0)
    reducing.fourth(1)
    reducing.give(1)
    climbing.end()
    reducing.fourth(0)
    reducing.give(0)
    reducing.receive(out)
    note_quarter, note_first, note_row = note_place(plan)
    base = note_first + note_row

    @pl.when(climbing.root)
    def _():
        out[note_quarter, base : base + MISC_ROWS, :] = (
            out[note_quarter, base : base + MISC_ROWS, :] + notes[:MISC_ROWS, :]
        )

    in_pos(output_pos, 0)
    in_pos(hidden_pos, 1)
    own_hidden.wait()
    for copy in positions[DEPTH - 1 :]:
        copy.wait_send()
    for k in range(COLUMNS):
        reducing.given(k)
    reducing.settle(1)
    reducing.settle(0)


def backward_pass(plan, operands):
    anywhere = pl.BlockSpec(memory_space=pl.ANY)
    vmem = pl.BlockSpec(memory_space=pltpu.VMEM)
    token = (WINLEN, D)
    block = (plan.quarter, LANES)
    positions = jax.ShapeDtypeStruct((DEPTH, WINLEN // DEPTH, D), BF16)
    scratch = [
        pltpu.VMEM((2, CORES, DEPTH, COLUMNS) + block, BF16),
        pltpu.VMEM((plan.staged, LANES), F32),
        pltpu.VMEM((2, DEPTH, COLUMNS) + block, BF16),
        pltpu.VMEM((COLUMNS, 2, 2) + block, BF16),
        pltpu.VMEM((COLUMNS, 2, DEPTH) + block, BF16),
        pltpu.VMEM((COLUMNS, DEPTH - 1) + block, BF16),
        pltpu.VMEM((COLUMNS,) + block, BF16),
        pltpu.VMEM((COLUMNS,) + block, BF16),
        pltpu.VMEM((WINLEN, FF), BF16),
        pltpu.VMEM((WINLEN, FF), BF16),
        pltpu.VMEM((FF, D), BF16),
        pltpu.VMEM((D, FF), BF16),
        pltpu.VMEM((D, D), BF16),
        pltpu.VMEM((D, WINLEN), BF16),
        pltpu.VMEM((D, WINLEN), BF16),
        pltpu.VMEM(token, BF16),
        pltpu.VMEM(token, BF16),
        pltpu.VMEM(token, BF16),
        pltpu.VMEM(token, F32),
        pltpu.VMEM(token, F32),
        pltpu.VMEM(token, BF16),
        pltpu.VMEM(token, BF16),
        pltpu.VMEM((2, WINLEN, WINLEN), BF16),
        pltpu.VMEM((WINLEN, WINLEN), BF16),
        pltpu.VMEM((WINLEN, WINLEN), BF16),
        pltpu.VMEM((WINLEN, WINLEN), F32),
        pltpu.VMEM((1, LANES, 5 * LANES), F32),
        pltpu.VMEM((LANES, WINLEN), BF16),
        pltpu.VMEM((LANES, WINLEN), F32),
        pltpu.VMEM((WINLEN, LANES), BF16),
        pltpu.VMEM((WINLEN, LANES), F32),
        pltpu.VMEM((1, VEC_ROWS * LANES), F32),
        pltpu.VMEM((2 * HEADS, 1, LANES), F32),
        pltpu.VMEM((HEADS, 1, WIDE), F32),
        pltpu.VMEM((NOTE_ROWS, LANES), F32),
        pltpu.VMEM((7, NOTE_ROWS, LANES), F32),
        pltpu.SemaphoreType.DMA((16,)),
        pltpu.SemaphoreType.DMA((2,)),
        pltpu.SemaphoreType.REGULAR((2,)),
        pltpu.SemaphoreType.DMA((2, 2, DEPTH)),
        pltpu.SemaphoreType.DMA((2, 7)),
        pltpu.SemaphoreType.DMA((2,)),
    ]
    return pl.pallas_call(
        functools.partial(backward_kernel, plan),
        out_shape=[
            jax.ShapeDtypeStruct((COLUMNS,) + block, F32), positions, positions,
            jax.ShapeDtypeStruct((HEADS, WINLEN, WINLEN), BF16),
        ],
        in_specs=[anywhere] * 14 + [vmem] * 5,
        out_specs=[vmem] + [anywhere] * 3,
        scratch_shapes=scratch + sem_shapes(REDUCE_SEMS),
        compiler_params=pltpu.CompilerParams(
            collective_id=1, has_side_effects=True, vmem_limit_bytes=62 * 2**20
        ),
        name="backward_pass",
    )(*operands)


def fast_shards(hidden_in, cotangent, box_coords, doc_lengths, params, moment_one, moment_two):
    shard_len = params.shape[0]
    plan = Plan(shard_len)
    (proj_qkv, proj_out, proj_in, proj_back, features_t, start_low, queries, keys, values, probs, context_t,
     xhat, normed_low, vec, rstd, cot, hot_two,
     rest_rows, share) = forward_pass(
        plan, params.reshape(plan.rows, LANES), hidden_in, cotangent,
        jnp.transpose(box_coords, (0, 2, 1)), doc_lengths,
    )
    summed, output_low, grad_hidden, _ = backward_pass(
        Plan(shard_len, carry=5 * LANES),
        (proj_back, proj_in, proj_out, proj_qkv, normed_low, start_low, features_t, context_t, queries, keys,
         values, probs, xhat, cot, rstd, vec, hot_two, rest_rows, share),
    )
    grad_share = summed.reshape(plan.padded, LANES)[: plan.rows].reshape(-1)
    return finish_step(output_low, grad_hidden, grad_share, params, moment_one, moment_two)


def finish_step(output_low, grad_hidden, grad_share, params, moment_one, moment_two):
    shard_len = params.shape[0]
    index = lax.axis_index("dp") * lax.axis_size("head") + lax.axis_index("head")
    flat_index = index * shard_len + jnp.arange(shard_len, dtype=jnp.int32)
    param_step, new_one = adam_step(params, moment_one, moment_two, grad_share, flat_index)
    return (output_low, grad_hidden, grad_share, param_step, new_one)


def to_windows(shard):
    return lax.all_to_all(shard, "head", split_axis=0, concat_axis=1, tiled=True)


def to_positions(window):
    return lax.all_to_all(window, "head", split_axis=1, concat_axis=0, tiled=True)


def plain_shards(hidden_in, cotangent, box_coords, doc_lengths, params, moment_one, moment_two):
    head_pos = lax.axis_index("head")
    groups = lax.axis_size("head")
    shard_len = params.shape[0]
    flat_params = lax.all_gather(params.astype(BF16), ("dp", "head"), axis=0, tiled=True)
    pieces = unpack(flat_params)
    hidden = to_windows(hidden_in).reshape(WINLEN, D)
    cot = to_windows(cotangent).reshape(WINLEN, D)
    own_box = lax.dynamic_index_in_dim(box_coords, head_pos, 0, keepdims=False)
    own_lengths = lax.dynamic_index_in_dim(doc_lengths, head_pos, 0, keepdims=False)
    chosen, relative, centre_x, centre_y = window_layout(own_lengths, own_box)
    features = box_features(relative).astype(BF16)

    proj_qkv, proj_out, proj_box, proj_in, proj_back = pieces[:5]
    qv_bias, out_bias, norm_one, in_bias, back_bias, norm_two, tables = pieces[5:]
    ops = bias_operands(tables, chosen, centre_x, centre_y)
    start_state = hidden.astype(F32) + matmul(features, proj_box)
    start_low = start_state.astype(BF16)
    qv_float = qv_bias.astype(F32)
    mixed = matmul(start_low, proj_qkv)
    queries = (mixed[:, :D] + qv_float[0]).astype(BF16) * jnp.asarray(HEAD_DIM ** (-0.5), BF16)
    keys = mixed[:, D : 2 * D].astype(BF16)
    values = (mixed[:, 2 * D :] + qv_float[1]).astype(BF16)

    probs, context_t = attention_forward(queries, keys, values, ops)
    first_sum = start_state + rows_inner(context_t, proj_out) + out_bias.astype(F32)
    normed, norm_one_back = jax.vjp(layer_norm, first_sum, norm_one.astype(F32))
    normed_low = normed.astype(BF16)
    inner_act = matmul(normed_low, proj_in) + in_bias.astype(F32)
    active, gelu_back = jax.vjp(gelu_exact, inner_act)
    active_low = active.astype(BF16)
    second_sum = normed + matmul(active_low, proj_back) + back_bias.astype(F32)
    output, norm_two_back = jax.vjp(layer_norm, second_sum, norm_two.astype(F32))
    output_low = to_positions(output.astype(BF16).reshape(1, WINLEN, D))

    grad_second, grad_norm_two = norm_two_back(cot.astype(F32))
    grad_branch = grad_second.astype(BF16)
    grad_proj_back = rows_inner(active_low, grad_branch)
    grad_back_bias = jnp.sum(grad_branch.astype(F32), axis=0)
    (grad_inner_f,) = gelu_back(times_transposed(grad_branch, proj_back))
    grad_inner = grad_inner_f.astype(BF16)
    grad_proj_in = rows_inner(normed_low, grad_inner)
    grad_in_bias = jnp.sum(grad_inner.astype(F32), axis=0)
    grad_first, grad_norm_one = norm_one_back(grad_second + times_transposed(grad_inner, proj_in))
    grad_attn = grad_first.astype(BF16)
    grad_proj_out = matmul(context_t, grad_attn)
    grad_out_bias = jnp.sum(grad_attn.astype(F32), axis=0)
    grad_context = times_transposed(grad_attn, proj_out).astype(BF16)
    grad_queries_t, grad_keys, grad_values, cells, diag = attention_backward(
        queries, keys, values, grad_context, probs, ops
    )
    table_grad = table_grads(cells, diag)
    grad_mixed = jnp.concatenate([grad_queries_t.T, grad_keys, grad_values], axis=1)
    grad_proj_qkv = rows_inner(start_low, grad_mixed)
    summed = jnp.sum(grad_mixed.astype(F32), axis=0)
    grad_qv_bias = jnp.stack([summed[:D], summed[2 * D :]])
    grad_start = grad_first + times_transposed(grad_mixed, proj_qkv)
    grad_start_low = grad_start.astype(BF16)
    grad_hidden = to_positions(grad_start_low.reshape(1, WINLEN, D))
    grad_proj_box = rows_inner(features, grad_start_low)
    grad_list = (
        grad_proj_qkv,
        grad_proj_out,
        grad_proj_box,
        grad_proj_in,
        grad_proj_back,
        grad_qv_bias,
        grad_out_bias,
        grad_norm_one,
        grad_in_bias,
        grad_back_bias,
        grad_norm_two,
        table_grad,
    )
    padding = jnp.zeros((shard_len * groups * lax.axis_size("dp") - USED,), BF16)
    grads_flat = jnp.concatenate([piece.astype(BF16).reshape(-1) for piece in grad_list] + [padding])
    grad_share = lax.psum_scatter(
        grads_flat, ("dp", "head"), scatter_dimension=0, tiled=True
    ).astype(F32)
    return finish_step(output_low, grad_hidden, grad_share, params, moment_one, moment_two)


def solution(mesh):
    placed = (
        P("dp", "head", None),
        P("dp", "head", None),
        P("dp", None, None),
        P("dp", None),
        P(("dp", "head")),
        P(("dp", "head")),
        P(("dp", "head")),
    )
    return jax.shard_map(
        fast_shards if fits(mesh) else plain_shards,
        mesh=mesh,
        in_specs=placed,
        out_specs=(
            P("dp", "head", None),
            P("dp", "head", None),
            P(("dp", "head")),
            P(("dp", "head")),
            P(("dp", "head")),
        ),
        check_vma=False,
    )
```

```python
import functools
import math

import jax
import jax.numpy as jnp
import numpy as np
from jax import lax
from jax.experimental import pallas as pl
from jax.experimental.pallas import tpu as pltpu
from jax.sharding import PartitionSpec as P

D = 768
HEADS = 12
FF = 3072
BUCKETS = 32
WINLEN = 512
HEAD_DIM = 64
PAIRS = HEADS // 2
LANES = 128
BLOCKS = WINLEN // LANES

beta_one = 0.9
beta_two = 0.999
adam_eps = 1e-08
norm_eps = 1e-05
base_rate = 0.001
layer_decay = 0.75
decay_weight = 0.01
adam_count = 100
coord_cell = 32
masked_score = -1e30

F32 = jnp.float32
BF16 = jnp.bfloat16


def layouts_list():
    return (
        (D, 3 * D),
        (D, D),
        (D, D),
        (D, FF),
        (FF, D),
        (2, D),
        (D,),
        (2, D),
        (FF,),
        (D,),
        (2, D),
        (3, HEADS, BUCKETS),
    )


def unpack(flat_params):
    pieces = []
    offset = 0
    for layout in layouts_list():
        elements = math.prod(layout)
        pieces.append(flat_params[offset : offset + elements].reshape(layout))
        offset += elements
    return pieces


def matmul(left_mat, right_mat):
    return jnp.dot(left_mat, right_mat, preferred_element_type=F32)


def rows_inner(left_mat, right_mat):
    return lax.dot_general(left_mat, right_mat, (((0,), (0,)), ((), ())), preferred_element_type=F32)


def times_transposed(left_mat, right_mat):
    return lax.dot_general(left_mat, right_mat, (((1,), (1,)), ((), ())), preferred_element_type=F32)


def layer_norm(values, gain_bias):
    row_mean = jnp.mean(values, axis=-1, keepdims=True)
    centred = values - row_mean
    spread = jnp.mean(centred * centred, axis=-1, keepdims=True)
    return centred * lax.rsqrt(spread + norm_eps) * gain_bias[0] + gain_bias[1]


def gelu_exact(values):
    return jax.nn.gelu(values, approximate=False)


def hot(index, count):
    return (np.asarray(index)[..., None] == np.arange(count)).astype(np.float32)


def clipped(steps):
    return np.clip(steps, -(BUCKETS // 2), BUCKETS // 2 - 1) + BUCKETS // 2


CELLS = np.arange(BUCKETS)
HOT_SAME = hot(clipped(CELLS[:, None] - CELLS[None, :]), BUCKETS)
HOT_LESS = hot(clipped(CELLS[:, None] - CELLS[None, :] - 1), BUCKETS)
WIDE = 6 * LANES
_U = np.arange(WIDE)
BAND_HOT = hot(np.where(_U < 5 * LANES, clipped(_U - 2 * LANES), 0), BUCKETS)
_V = np.arange(4 * LANES)
DIAG_HOT = np.concatenate(
    [
        hot(np.zeros(LANES, np.int64), BUCKETS),
        hot(np.where(_V < 3 * LANES, clipped(_V - LANES), 0), BUCKETS),
        hot(np.full(LANES, BUCKETS - 1), BUCKETS),
    ]
)


def window_layout(doc_lengths, box_coords):
    doc_ends = jnp.cumsum(doc_lengths, dtype=jnp.int32)
    doc_starts = doc_ends - doc_lengths
    places = jnp.arange(WINLEN, dtype=jnp.int32)
    doc_ids = jnp.sum(
        (places[:, None] >= doc_ends[None, :]).astype(jnp.int32), axis=1, dtype=jnp.int32
    )
    docs = jnp.arange(doc_lengths.shape[0], dtype=jnp.int32)
    chosen = doc_ids[:, None] == docs[None, :]
    first_hot = places[:, None] == doc_starts[None, :]
    first_box = jnp.sum(
        jnp.where(first_hot[:, :, None], box_coords[:, None, :], 0), axis=0, dtype=jnp.int32
    )
    anchor = jnp.sum(
        jnp.where(chosen[:, :, None], first_box[None, :, :], 0), axis=1, dtype=jnp.int32
    )
    relative = box_coords - jnp.concatenate([anchor[:, :2], anchor[:, :2]], axis=1)
    centre_x = (box_coords[:, 0] + box_coords[:, 2]) // 2
    centre_y = (box_coords[:, 1] + box_coords[:, 3]) // 2
    return chosen, relative, centre_x, centre_y


def box_features(relative):
    count_freq = D // 8
    steps = jnp.arange(count_freq, dtype=F32)
    frequency = jnp.exp(steps * (-math.log(1000.0) / count_freq))
    angles = relative.astype(F32)[:, :, None] * frequency[None, None, :]
    return jnp.concatenate([jnp.sin(angles), jnp.cos(angles)], axis=2).reshape(relative.shape[0], D)


def bias_operands(tables, chosen, centre_x, centre_y):
    cell_x, cell_y = centre_x // coord_cell, centre_y // coord_cell
    rest_x, rest_y = centre_x % coord_cell, centre_y % coord_cell
    cells = jnp.arange(BUCKETS, dtype=jnp.int32)
    hot_x = (cell_x[:, None] == cells[None, :]).astype(BF16)
    hot_y = (cell_y[:, None] == cells[None, :]).astype(BF16)
    none = jnp.zeros_like(hot_x)
    hot_two = jnp.concatenate([hot_x, hot_y, hot_x, hot_y], axis=1)
    key_x = jnp.stack(
        [
            jnp.concatenate([hot_x, -hot_x, none, none], axis=1),
            jnp.concatenate([none, none, hot_x, -hot_x], axis=1),
        ]
    )
    key_y = jnp.stack(
        [
            jnp.concatenate([hot_y, -hot_y, none, none], axis=1),
            jnp.concatenate([none, none, hot_y, -hot_y], axis=1),
        ]
    )
    same = jnp.einsum("qcb,thb->thqc", HOT_SAME.astype(BF16), tables[1:], preferred_element_type=F32)
    less = jnp.einsum("qcb,thb->thqc", HOT_LESS.astype(BF16), tables[1:], preferred_element_type=F32)
    zero = jnp.zeros_like(same[0])
    base = jnp.concatenate(
        [jnp.concatenate([same[0], zero], axis=2), jnp.concatenate([zero, same[1]], axis=2)], axis=1
    )
    base = base.reshape(PAIRS, 2, 64, 64)[:, ::-1].reshape(HEADS, 64, 64)
    diff_x = jnp.concatenate([jnp.concatenate([less[0], same[0]], axis=2), jnp.zeros((HEADS, 32, 64), F32)], axis=1)
    diff_y = jnp.concatenate([jnp.zeros((HEADS, 32, 64), F32), jnp.concatenate([less[1], same[1]], axis=2)], axis=1)
    rows = jnp.concatenate([base, diff_x, diff_y], axis=0).astype(BF16)
    rows = rows.transpose(1, 0, 2).reshape(64, 3 * D)
    met = matmul(hot_two[:, :64], rows).astype(BF16)
    band = matmul(tables[0], jnp.asarray(BAND_HOT.T, BF16)).reshape(HEADS, 1, WIDE)
    rest_cols = jnp.stack([rest_x, rest_y], axis=1).astype(F32)
    rest_rows = rest_cols.T
    pad = jnp.zeros((WINLEN, LANES - chosen.shape[1]), BF16)
    marks = chosen.astype(BF16)
    mark_keys = jnp.concatenate([marks, pad], axis=1)
    mark_queries = jnp.concatenate([(1 - marks) * jnp.asarray(masked_score, BF16), pad], axis=1)
    return dict(
        hot_two=hot_two,
        key_x=key_x,
        key_y=key_y,
        met=met,
        band=band,
        rest_cols=rest_cols,
        rest_rows=rest_rows,
        mark_keys=mark_keys,
        mark_queries=mark_queries,
    )


def half_masks():
    lane = lax.broadcasted_iota(jnp.int32, (1, LANES), 1)
    low = (lane < HEAD_DIM).astype(F32)
    return low.astype(BF16), (1.0 - low).astype(BF16)


def less_masks(rest_cols, rest_rows, less_x, less_y):
    for part in range(BLOCKS):
        rows = slice(part * LANES, (part + 1) * LANES)
        for axis, less in ((0, less_x), (1, less_y)):
            column = rest_cols[rows, axis : axis + 1]
            row = rest_rows[axis : axis + 1, :]
            less[rows, :] = jnp.where(row < column, 1.0, 0.0).astype(less.dtype)


def attention_forward_kernel(
    q_ref, k_ref, v_ref, hot_ref, keyx_ref, keyy_ref, met_ref, band_ref, cols_ref, rows_ref,
    mkey_ref, mquery_ref, probs_ref, context_ref,
    kaug, qaug, less_x, less_y, wide, scores,
):
    low, high = half_masks()
    less_masks(cols_ref, rows_ref, less_x, less_y)
    kaug[:, LANES:] = mkey_ref[...]
    qaug[:, LANES:] = mquery_ref[...]
    half = 2 * LANES

    def one_pair(pair, carry):
        at = pl.multiple_of(pair * LANES, LANES)
        lanes = pl.ds(at, LANES)
        lanes_x = pl.ds(pl.multiple_of(at + D, LANES), LANES)
        lanes_y = pl.ds(pl.multiple_of(at + 2 * D, LANES), LANES)
        values_t = v_ref[:, lanes].T
        for odd in range(2):
            own, other = (low, high) if odd == 0 else (high, low)
            head = 2 * pair + odd
            kaug[:, :LANES] = k_ref[:, lanes] * own + hot_ref[...] * other
            qaug[:, :LANES] = q_ref[:, lanes] * own + met_ref[:, lanes] * other
            skew_band(band_ref[head], wide)
            for side in range(2):
                cols = slice(side * half, (side + 1) * half)
                top = None
                for part in range(BLOCKS):
                    rows = slice(part * LANES, (part + 1) * LANES)
                    s = times_transposed(kaug[rows, :], qaug[cols, :])
                    dx = times_transposed(keyx_ref[odd, rows, :], met_ref[cols, lanes_x])
                    dy = times_transposed(keyy_ref[odd, rows, :], met_ref[cols, lanes_y])
                    bias = []
                    for block in range(2 * side, 2 * side + 2):
                        step = max(-2, min(2, block - part)) + 2
                        bias.append(wide[:, step * LANES : (step + 1) * LANES])
                    s = s + jnp.concatenate(bias, axis=1)
                    s = s + dx * less_x[rows, cols] + dy * less_y[rows, cols]
                    scores[rows, :] = s
                    best = jnp.max(s, axis=0, keepdims=True)
                    top = best if top is None else jnp.maximum(top, best)
                total = None
                for part in range(BLOCKS):
                    rows = slice(part * LANES, (part + 1) * LANES)
                    e = jnp.exp(scores[rows, :] - top)
                    scores[rows, :] = e
                    add = jnp.sum(e, axis=0, keepdims=True)
                    total = add if total is None else total + add
                share = 1.0 / total
                for part in range(BLOCKS):
                    rows = slice(part * LANES, (part + 1) * LANES)
                    probs_ref[head, rows, cols] = (scores[rows, :] * share).astype(BF16)
                got = matmul(
                    values_t[odd * HEAD_DIM : (odd + 1) * HEAD_DIM, :], probs_ref[head, :, cols]
                )
                context_ref[pl.ds(pl.multiple_of(head * HEAD_DIM, HEAD_DIM), HEAD_DIM), cols] = (
                    got.astype(BF16)
                )
        return carry

    lax.fori_loop(0, PAIRS, one_pair, 0)


def skew_band(row, wide):
    x = jnp.broadcast_to(row, (8, WIDE))
    sub = lax.broadcasted_iota(jnp.int32, (8, WIDE), 0)
    for bit in (1, 2, 4):
        x = jnp.where((sub & bit) != 0, pltpu.roll(x, bit, 1), x)
    for group in range(LANES // 8):
        y = x if group == 0 else pltpu.roll(x, 8 * group, 1)
        wide[8 * group : 8 * group + 8, :] = y[:, : 5 * LANES]


def skew_groups(skewed, wide):
    for group in range(LANES // 8):
        y = skewed if group == 0 else pltpu.roll(skewed, 8 * group, 1)
        wide[8 * group : 8 * group + 8, :] = y[:, : 5 * LANES]


def diagonal_sums(parts):
    total = None
    for group in range(LANES // 8):
        x = jnp.concatenate(
            [parts[8 * group : 8 * group + 8, LANES : 4 * LANES], jnp.zeros((8, LANES), F32)], axis=1
        )
        y = x if group == 0 else pltpu.roll(x, 4 * LANES - 8 * group, 1)
        total = y if total is None else total + y
    sub = lax.broadcasted_iota(jnp.int32, (8, 4 * LANES), 0)
    for bit in (1, 2, 4):
        total = jnp.where((sub & bit) != 0, pltpu.roll(total, 4 * LANES - bit, 1), total)
    return jnp.sum(total, axis=0, keepdims=True)


def attention_backward_kernel(
    q_ref, k_ref, v_ref, dctx_ref, probs_ref, hot_ref, cols_ref, rows_ref,
    dq_ref, dk_ref, dv_ref, cells_ref, diag_ref,
    qaug, less_x, less_y, scores, dscores, band, kept, hot_t,
):
    low, high = half_masks()
    less_masks(cols_ref, rows_ref, less_x, less_y)
    hot_t[...] = hot_ref[...].T
    lane = lax.broadcasted_iota(jnp.int32, (1, LANES), 1)
    scale = HEAD_DIM ** (-0.5)
    of_x = jnp.where((lane // BUCKETS) % 2 == 0, 1.0, 0.0)
    cells_x = hot_ref[...] * of_x.astype(BF16)
    cells_y = hot_ref[...] * (1.0 - of_x).astype(BF16)

    def one_pair(pair, carry):
        at = pl.multiple_of(pair * LANES, LANES)
        lanes = pl.ds(at, LANES)
        keys_t = k_ref[:, lanes].T
        for odd in range(2):
            own, other = (low, high) if odd == 0 else (high, low)
            head = 2 * pair + odd
            qaug[...] = q_ref[:, lanes] * own + hot_ref[...] * other
            dctx = dctx_ref[:, lanes]
            dot = None
            for part in range(BLOCKS):
                rows = slice(part * LANES, (part + 1) * LANES)
                dp = times_transposed(v_ref[rows, lanes] * own, dctx)
                scores[rows, :] = dp
                add = jnp.sum(dp * probs_ref[head, rows, :].astype(F32), axis=0, keepdims=True)
                dot = add if dot is None else dot + add
            band[...] = jnp.zeros_like(band)
            for part in range(BLOCKS):
                rows = slice(part * LANES, (part + 1) * LANES)
                probs = probs_ref[head, rows, :]
                ds = probs.astype(F32) * (scores[rows, :] - dot)
                for block in range(BLOCKS):
                    step = max(-2, min(2, block - part)) + 2
                    where = slice(step * LANES, (step + 1) * LANES)
                    band[:, where] = band[:, where] + ds[:, block * LANES : (block + 1) * LANES]
                ds = ds.astype(BF16)
                dscores[rows, :] = ds
                both = matmul(ds, qaug[...])
                less = matmul(ds * less_x[rows, :], cells_x) + matmul(ds * less_y[rows, :], cells_y)
                dv = matmul(probs, dctx)
                kept[odd, 0, rows, :] = both
                kept[odd, 1, rows, :] = less
                kept[odd, 2, rows, :] = dv
            got = matmul(keys_t[odd * HEAD_DIM : (odd + 1) * HEAD_DIM, :], dscores[...])
            dq_ref[pl.ds(pl.multiple_of(head * HEAD_DIM, HEAD_DIM), HEAD_DIM), :] = (
                got * scale
            ).astype(BF16)
            diag_ref[head, :, LANES : 5 * LANES] = diagonal_sums(band)
            diag_ref[head, :, :LANES] = jnp.sum(band[:, :LANES], axis=0, keepdims=True)
            diag_ref[head, :, 5 * LANES :] = jnp.sum(band[:, 4 * LANES :], axis=0, keepdims=True)
            for which in range(2):
                summed = kept[odd, which]
                first = summed.astype(BF16)
                rest = (summed - first.astype(F32)).astype(BF16)
                cells_ref[head, which] = matmul(hot_t[:64, :], first) + matmul(hot_t[:64, :], rest)
        dk_ref[:, lanes] = jnp.where(lane < HEAD_DIM, kept[0, 0], kept[1, 0]).astype(BF16)
        dv_ref[:, lanes] = jnp.where(lane < HEAD_DIM, kept[0, 2], kept[1, 2]).astype(BF16)
        return carry

    lax.fori_loop(0, PAIRS, one_pair, 0)


def attention_forward(queries, keys, values, ops):
    return pl.pallas_call(
        attention_forward_kernel,
        out_shape=(
            jax.ShapeDtypeStruct((HEADS, WINLEN, WINLEN), BF16),
            jax.ShapeDtypeStruct((D, WINLEN), BF16),
        ),
        scratch_shapes=[
            pltpu.VMEM((WINLEN, 2 * LANES), BF16),
            pltpu.VMEM((WINLEN, 2 * LANES), BF16),
            pltpu.VMEM((WINLEN, WINLEN), F32),
            pltpu.VMEM((WINLEN, WINLEN), F32),
            pltpu.VMEM((LANES, 5 * LANES), F32),
            pltpu.VMEM((WINLEN, 2 * LANES), F32),
        ],
        compiler_params=pltpu.CompilerParams(vmem_limit_bytes=48 * 2**20),
        name="attention_forward",
    )(
        queries, keys, values, ops["hot_two"], ops["key_x"], ops["key_y"], ops["met"], ops["band"],
        ops["rest_cols"], ops["rest_rows"], ops["mark_keys"], ops["mark_queries"],
    )


def attention_backward(queries, keys, values, grad_context, probs, ops):
    return pl.pallas_call(
        attention_backward_kernel,
        out_shape=(
            jax.ShapeDtypeStruct((D, WINLEN), BF16),
            jax.ShapeDtypeStruct((WINLEN, D), BF16),
            jax.ShapeDtypeStruct((WINLEN, D), BF16),
            jax.ShapeDtypeStruct((HEADS, 2, 64, LANES), F32),
            jax.ShapeDtypeStruct((HEADS, 1, WIDE), F32),
        ),
        scratch_shapes=[
            pltpu.VMEM((WINLEN, LANES), BF16),
            pltpu.VMEM((WINLEN, WINLEN), BF16),
            pltpu.VMEM((WINLEN, WINLEN), BF16),
            pltpu.VMEM((WINLEN, WINLEN), F32),
            pltpu.VMEM((WINLEN, WINLEN), BF16),
            pltpu.VMEM((LANES, 5 * LANES), F32),
            pltpu.VMEM((2, 3, WINLEN, LANES), F32),
            pltpu.VMEM((LANES, WINLEN), BF16),
        ],
        compiler_params=pltpu.CompilerParams(vmem_limit_bytes=48 * 2**20),
        name="attention_backward",
    )(
        queries, keys, values, grad_context, probs, ops["hot_two"], ops["rest_cols"],
        ops["rest_rows"],
    )


def table_grads(cells, diag):
    exact = lax.Precision.HIGHEST
    pairs = cells.reshape(PAIRS, 2, 2, 64, LANES)
    every = jnp.stack([pairs[:, 0, 0, :, 64:], pairs[:, 1, 0, :, :64]], axis=1).reshape(HEADS, 64, 64)
    less = cells[:, 1]
    less_x, less_y = less[:, :32, :32], less[:, 32:, 32:64]
    all_x, all_y = every[:, :32, :32], every[:, 32:, 32:]
    same = jnp.stack([all_x - less_x, all_y - less_y]).reshape(2 * HEADS, -1)
    below = jnp.stack([less_x, less_y]).reshape(2 * HEADS, -1)
    same_hot = jnp.asarray(HOT_SAME.transpose(1, 0, 2).reshape(-1, BUCKETS))
    less_hot = jnp.asarray(HOT_LESS.transpose(1, 0, 2).reshape(-1, BUCKETS))
    moved = jnp.dot(same, same_hot, precision=exact) + jnp.dot(below, less_hot, precision=exact)
    along = jnp.dot(diag.reshape(HEADS, WIDE), jnp.asarray(DIAG_HOT), precision=exact)
    return jnp.concatenate([along[None], moved.reshape(2, HEADS, BUCKETS)], axis=0)


COLUMNS = 4
CORES = 2
DEPTH = 4
USED = sum(math.prod(layout) for layout in layouts_list())
MATRICES = layouts_list()[:5]
MISC = sum(math.prod(layout) for layout in layouts_list()[5:])
MISC_ROWS = -(-MISC // (8 * LANES)) * 8


class Plan:
    def __init__(self, shard_len, carry=3 * LANES):
        self.rows = shard_len // LANES
        self.quarter = -(-self.rows // (16 * COLUMNS)) * 16
        self.padded = COLUMNS * self.quarter
        self.per_column = CORES * DEPTH * self.rows
        self.carry = carry
        self.staged = self.carry + self.per_column + 3 * LANES
        starts = []
        offset = 0
        for depth, width in MATRICES:
            starts.append(offset // LANES)
            offset += depth * width
        self.starts = starts
        self.misc_start = offset // LANES


def fits(mesh):
    return mesh.shape["dp"] == COLUMNS * CORES and mesh.shape["head"] == DEPTH


MESH = pl.DeviceIdType.MESH


class Place:
    def __init__(self):
        dp = lax.axis_index("dp")
        self.z = lax.axis_index("head")
        self.core = dp % CORES
        self.column = dp // CORES
        self.x = self.column % 2
        self.y = self.column // 2
        self.col_x = 2 * self.y + (1 - self.x)
        self.col_y = 2 * (1 - self.y) + self.x
        self.col_d = 2 * (1 - self.y) + (1 - self.x)
        self.peer_x = self.at(self.col_x, self.core, self.z)
        self.peer_y = self.at(self.col_y, self.core, self.z)
        self.peer_d = self.at(self.col_d, self.core, self.z)
        self.peer_core = self.at(self.column, 1 - self.core, self.z)
        self.far = [lax.rem(self.z + d, DEPTH) for d in range(1, DEPTH)]
        self.from_far = [lax.rem(self.z + DEPTH - d, DEPTH) for d in range(1, DEPTH)]
        self.peers_z = [self.at(self.column, self.core, f) for f in self.far]

    def at(self, column, core, z):
        return {"dp": column * CORES + core, "head": z}

    def greet(self):
        barrier = pltpu.get_barrier_semaphore()
        peers = [self.peer_x, self.peer_y, self.peer_d, self.peer_core] + self.peers_z
        for peer in peers:
            pl.semaphore_signal(barrier, inc=1, device_id=peer, device_id_type=MESH)
        pl.semaphore_wait(barrier, len(peers))


def remote(src, dst, send_sem, recv_sem, peer):
    return pltpu.make_async_remote_copy(
        src_ref=src, dst_ref=dst, send_sem=send_sem, recv_sem=recv_sem, device_id=peer,
        device_id_type=MESH,
    )


class Gathering:
    def __init__(self, place, flat, sems):
        self.place = place
        self.flat = flat
        self.sems = sems
        self.sent = []

    def send(self, src, dst, kind, index, peer):
        copy = remote(src, dst, self.sems[kind].at[0, index], self.sems[kind].at[1, index], peer)
        copy.start()
        self.sent.append(copy)

    def got(self, dst, kind, index):
        remote(
            dst, dst, self.sems[kind].at[0, index], self.sems[kind].at[1, index], self.place.peer_x
        ).wait_recv()

    def rows(self, h):
        half = self.flat.shape[-2] // 2
        return slice(h * half, (h + 1) * half)

    def spread(self, own, h):
        p = self.place
        rows = self.rows(h)
        for index, (column, peer) in enumerate(
            ((p.col_x, p.peer_x), (p.col_y, p.peer_y), (p.col_d, p.peer_d))
        ):
            self.send(
                own.at[column, rows], self.flat.at[p.column, p.core, p.z, column, rows], "spread",
                2 * index + h, peer,
            )
        self.flat[p.column, p.core, p.z, p.column, rows] = own[p.column, rows]

    def spread_done(self, h):
        p = self.place
        for index, column in enumerate((p.col_x, p.col_y, p.col_d)):
            self.got(self.flat.at[column, p.core, p.z, p.column, self.rows(h)], "spread", 2 * index + h)

    def along_z(self, k, h):
        p = self.place
        piece = self.flat.at[k, p.core, p.z, p.column, self.rows(h)]
        for d in range(DEPTH - 1):
            self.send(piece, piece, "z", 3 * (2 * k + h) + d, p.peers_z[d])

    def first(self, k, h):
        p = self.place
        n = 2 * k + h
        for d in range(DEPTH - 1):
            self.got(
                self.flat.at[k, p.core, p.from_far[d], p.column, self.rows(h)], "z", 3 * n + d
            )
        piece = self.flat.at[k, p.core, :, p.column, self.rows(h)]
        self.send(piece, piece, "one", 2 * n, p.peer_x)
        self.send(piece, piece, "one", 2 * n + 1, p.peer_y)
        self.send(piece, piece, "core", 5 * n, p.peer_core)

    def second(self, k, h):
        p = self.place
        n = 2 * k + h
        rows = self.rows(h)
        from_x = self.flat.at[k, p.core, :, p.col_x, rows]
        self.got(from_x, "one", 2 * n)
        part = self.flat.at[k, p.core, 0:2, p.col_x, rows]
        self.send(part, part, "two", 2 * n, p.peer_y)
        self.send(from_x, from_x, "core", 5 * n + 1, p.peer_core)
        from_y = self.flat.at[k, p.core, :, p.col_y, rows]
        self.got(from_y, "one", 2 * n + 1)
        part = self.flat.at[k, p.core, 2:4, p.col_y, rows]
        self.send(part, part, "two", 2 * n + 1, p.peer_x)
        self.send(from_y, from_y, "core", 5 * n + 2, p.peer_core)

    def third(self, k, h):
        p = self.place
        n = 2 * k + h
        for side in range(2):
            part = self.flat.at[k, p.core, 2 * side : 2 * side + 2, p.col_d, self.rows(h)]
            self.got(part, "two", 2 * n + side)
            self.send(part, part, "core", 5 * n + 3 + side, p.peer_core)

    def complete(self, k):
        p = self.place
        other = 1 - p.core
        for h in range(2):
            n = 2 * k + h
            rows = self.rows(h)
            for index, column in enumerate((p.column, p.col_x, p.col_y)):
                self.got(self.flat.at[k, other, :, column, rows], "core", 5 * n + index)
            for side in range(2):
                self.got(
                    self.flat.at[k, other, 2 * side : 2 * side + 2, p.col_d, rows], "core",
                    5 * n + 3 + side,
                )

    def finish(self):
        for copy in self.sent:
            copy.wait_send()


GATHER_SEMS = {"spread": 6, "z": 24, "one": 16, "two": 16, "core": 40}


def sem_shapes(counts):
    return [pltpu.SemaphoreType.DMA((2, count)) for count in counts.values()]


def stage_column(plan, flat, staged, k):
    def one(shard, carry):
        core, z = shard // DEPTH, shard % DEPTH
        for quarter in range(COLUMNS):
            base = plan.carry + shard * plan.rows + quarter * plan.quarter
            staged[pl.ds(pl.multiple_of(base, 8), plan.quarter), :] = flat[k, core, z, quarter].astype(F32)
        return carry

    lax.fori_loop(0, CORES * DEPTH, one, 0)


def keep_carry(plan, staged):
    end = plan.carry + plan.per_column
    staged[: plan.carry, :] = staged[end - plan.carry : end, :]


ROW_STEP = 48


def column_rows(plan, k, touching):
    low, high = k * plan.per_column, (k + 1) * plan.per_column
    taken = []
    for index, (depth, width) in enumerate(MATRICES):
        group = 16 * (width // LANES)
        from_low, from_high = low - plan.starts[index], high - plan.starts[index]
        begin = max(0, min(depth, from_low // group * 16))
        if touching:
            end = max(0, min(depth, -(-from_high // group) * 16))
        else:
            end = max(0, min(depth, from_high // group * 16))
        if end > begin:
            taken.append((index, begin, end))
    return taken


def staged_at(plan, k, row):
    return plan.carry + row - k * plan.per_column


def row_loops(rows):
    whole = rows // ROW_STEP
    loops = [(ROW_STEP, 0, whole)] if whole else []
    if rows % ROW_STEP:
        loops.append((16, whole * ROW_STEP, (rows % ROW_STEP) // 16))
    return loops


def form_matrices(plan, staged, matrices, k):
    for index, begin, end in column_rows(plan, k, False):
        blocks = MATRICES[index][1] // LANES
        base = staged_at(plan, k, plan.starts[index] + begin * blocks)
        assert 0 <= base
        target = matrices[index]
        for step_rows, first, count in row_loops(end - begin):

            def one(step, carry, step_rows=step_rows, first=first, blocks=blocks, base=base,
                    begin=begin, target=target):
                row = first + step * step_rows
                for block in range(blocks):
                    got = staged[pl.ds(base + row * blocks + block, step_rows, stride=blocks), :]
                    target[
                        pl.ds(pl.multiple_of(begin + row, 16), step_rows),
                        block * LANES : (block + 1) * LANES,
                    ] = got.astype(BF16)
                return carry

            lax.fori_loop(0, count, one, 0)


def adam_step(params, moment_one, moment_two, grads, flat_index):
    box_part = (flat_index >= 4 * D * D) & (flat_index < 5 * D * D)
    step_rate = jnp.where(box_part, base_rate * layer_decay**12, base_rate * layer_decay)
    decay_mask = jnp.where(flat_index < 5 * D * D + 2 * D * FF, decay_weight, 0.0)
    moment_one = beta_one * moment_one + (1.0 - beta_one) * grads
    moment_two = beta_two * moment_two + (1.0 - beta_two) * grads * grads
    first_hat = moment_one / (1.0 - beta_one**adam_count)
    second_hat = moment_two / (1.0 - beta_two**adam_count)
    update = first_hat / (jnp.sqrt(second_hat) + adam_eps) + decay_mask * params
    return (-step_rate * update, moment_one)


VEC = {}
_at = 0
for _name, _rows in (
    ("q_bias", 6), ("v_bias", 6), ("out_bias", 6), ("gain_one", 6), ("shift_one", 6), ("in_bias", 24),
    ("back_bias", 6), ("gain_two", 6), ("shift_two", 6), ("tables", 9),
):
    VEC[_name] = _at * LANES
    _at += _rows
VEC_ROWS = _at
NOTE_ROWS = 96
NBLOCK = 2 * LANES


def note_place(plan):
    row = plan.misc_start - (CORES * DEPTH * COLUMNS - 1) * plan.rows
    quarter, row = row // plan.quarter, row % plan.quarter
    first = row // 16 * 16
    assert first + NOTE_ROWS <= plan.quarter and row - first + VEC_ROWS <= NOTE_ROWS
    return quarter, first, row - first


def spread_notes(place, own, notes, sems, plan):
    quarter, first, _ = note_place(plan)
    source = own.at[quarter, first : first + NOTE_ROWS]
    home = (place.column == COLUMNS - 1) & (place.core == CORES - 1)
    root = home & (place.z == DEPTH - 1)

    def copy(src, index, peer):
        return remote(src, notes, sems.at[0, index], sems.at[1, 0], peer)

    def arrived():
        copy(notes, 0, place.peer_core).wait_recv()

    @pl.when(root)
    def _():
        notes[...] = own[quarter, first : first + NOTE_ROWS]
        for index, peer in enumerate(place.peers_z):
            copy(source, index, peer).start()

    @pl.when(home & (place.z != DEPTH - 1))
    def _():
        arrived()

    @pl.when(home)
    def _():
        for index, peer in enumerate((place.peer_x, place.peer_y, place.peer_d)):
            copy(notes, 3 + index, peer).start()

    @pl.when((place.core == CORES - 1) & (place.column != COLUMNS - 1))
    def _():
        arrived()

    @pl.when(place.core == CORES - 1)
    def _():
        copy(notes, 6, place.peer_core).start()

    @pl.when(place.core != CORES - 1)
    def _():
        arrived()

    def finish():
        @pl.when(root)
        def _():
            for index, peer in enumerate(place.peers_z):
                copy(source, index, peer).wait_send()

        @pl.when(home)
        def _():
            for index, peer in enumerate((place.peer_x, place.peer_y, place.peer_d)):
                copy(notes, 3 + index, peer).wait_send()

        @pl.when(place.core == CORES - 1)
        def _():
            copy(notes, 6, place.peer_core).wait_send()

    return finish


def turns_table():
    count_freq = D // 8
    freq = np.exp(np.arange(count_freq) * (-math.log(1000.0) / count_freq)) / (2 * math.pi)
    per = np.concatenate([freq, freq])
    phase = np.concatenate([np.zeros(count_freq), np.full(count_freq, 0.25)])
    return np.stack([np.tile(per, 4), np.tile(phase, 4)]).astype(np.float32)


def sin_turns(t):
    t = t - jnp.floor(t + 0.5)
    a = jnp.abs(t)
    m = jnp.minimum(a, 0.5 - a) * (2 * math.pi)
    u = m * m
    poly = -1.0 / 39916800.0
    for term in (1.0 / 362880.0, -1.0 / 5040.0, 1.0 / 120.0, -1.0 / 6.0, 1.0):
        poly = poly * u + term
    s = m * poly
    return jnp.where(t < 0, -s, s)


def token_columns(boxes, lengths, window):
    coords = boxes[window].astype(F32)
    place = lax.broadcasted_iota(jnp.int32, (1, WINLEN), 1)
    doc = jnp.zeros((1, WINLEN), F32)
    anchor = jnp.zeros_like(coords)
    begin = 0
    for d in range(4):
        end = begin + lengths[window, d]
        mine = jnp.where((place >= begin) & (place < end), 1.0, 0.0)
        value = jnp.sum(coords * jnp.where(place == begin, 1.0, 0.0), axis=1, keepdims=True)
        anchor = anchor + value * mine
        doc = doc + mine * float(d)
        begin = end
    anchor = jnp.concatenate([anchor[0:2], anchor[0:2]], axis=0)
    relative = coords - anchor
    centre = jnp.floor((coords[0:2] + coords[2:4]) * 0.5)
    cell = jnp.floor(centre * (1.0 / coord_cell))
    rest = centre - cell * coord_cell
    rows = jnp.concatenate(
        [relative, cell, rest, doc, jnp.zeros((LANES - 9, WINLEN), F32)], axis=0
    )
    return rest, rows.T


def form_features(columns, turns_ref, features):
    lane = lax.broadcasted_iota(jnp.int32, (1, LANES), 1)
    for block in range(D // LANES):
        lanes = slice(block * LANES, (block + 1) * LANES)
        low, high = block * LANES // (D // 4), ((block + 1) * LANES - 1) // (D // 4)
        value = columns[:, low : low + 1]
        if high != low:
            value = jnp.where(
                lane + block * LANES < high * (D // 4), value, columns[:, high : high + 1]
            )
        t = value * turns_ref[0:1, lanes] + turns_ref[1:2, lanes]
        features[:, lanes] = sin_turns(t).astype(BF16)


def form_hots(columns, hot_ref, keyx_ref, keyy_ref, mkey, mquery):
    lane = lax.broadcasted_iota(jnp.int32, (1, LANES), 1)
    part = lane // BUCKETS
    cell = (lane % BUCKETS).astype(F32)
    is_x = jnp.where(columns[:, 4:5] == cell, 1.0, 0.0)
    is_y = jnp.where(columns[:, 5:6] == cell, 1.0, 0.0)
    hot_ref[...] = jnp.where(part % 2 == 0, is_x, is_y).astype(BF16)
    sign = jnp.where(part % 2 == 0, 1.0, -1.0)
    for odd in range(2):
        here = jnp.where(part // 2 == odd, sign, 0.0)
        keyx_ref[odd] = (is_x * here).astype(BF16)
        keyy_ref[odd] = (is_y * here).astype(BF16)
    doc = jnp.where(columns[:, 8:9] == lane.astype(F32), 1.0, 0.0)
    mkey[:, LANES:] = doc.astype(BF16)
    mquery[:, LANES:] = (jnp.where(lane < 4, 1.0 - doc, 0.0) * masked_score).astype(BF16)


def form_tables(tables, bands, tilted):
    row = lax.broadcasted_iota(jnp.int32, (LANES, 1), 0)
    half = BUCKETS // 2
    sub = lax.broadcasted_iota(jnp.int32, (8, LANES), 0)
    sub_wide = lax.broadcasted_iota(jnp.int32, (8, WIDE), 0)
    place = lax.broadcasted_iota(jnp.int32, (1, WIDE), 1)
    wanted = jnp.where(place < 5 * LANES, jnp.clip(place - 2 * LANES, -half, half - 1) + half, 0)
    lane = lax.broadcasted_iota(jnp.int32, (1, LANES), 1)
    turned = jnp.clip(64 - lane, -half, half - 1) + half
    for m in range(4):
        hot_band = jnp.where(row == wanted + m * BUCKETS, 1.0, 0.0).astype(BF16)
        got = matmul(tables, hot_band)
        for n in range(3):
            x = jnp.broadcast_to(got[n : n + 1, :], (8, WIDE))
            for bit in (1, 2, 4):
                x = jnp.where((sub_wide & bit) != 0, pltpu.roll(x, bit, 1), x)
            bands[4 * n + m] = x
        hot_turn = jnp.where(row == turned + m * BUCKETS, 1.0, 0.0).astype(BF16)
        got = matmul(tables, hot_turn)
        for t in (1, 2):
            for n in range(3):
                x = jnp.broadcast_to(got[3 * t + n : 3 * t + n + 1, :], (8, LANES))
                for bit in (1, 2, 4):
                    x = jnp.where((sub & bit) != 0, pltpu.roll(x, bit, 1), x)
                for group in range(BUCKETS // 8):
                    y = x if group == 0 else pltpu.roll(x, 8 * group, 1)
                    tilted[(t - 1) * HEADS + 4 * n + m, 8 * group : 8 * group + 8, :] = y


def pair_rows(tilted, pair):
    lane = lax.broadcasted_iota(jnp.int32, (1, LANES), 1)
    part = lane // BUCKETS
    x0, x1 = tilted[2 * pair], tilted[2 * pair + 1]
    y0, y1 = tilted[HEADS + 2 * pair], tilted[HEADS + 2 * pair + 1]

    def same(value, to):
        return value if to == 64 else pltpu.roll(value, (to - 64) % LANES, 1)

    def less(value, to):
        return pltpu.roll(value, (to - 65) % LANES, 1)

    zero = jnp.zeros_like(x0)
    base_x = jnp.where(part == 0, same(x1, 0), jnp.where(part == 2, same(x0, 64), zero))
    base_y = jnp.where(part == 1, same(y1, 32), jnp.where(part == 3, same(y0, 96), zero))

    def steps(even, odd):
        return jnp.where(
            part < 2,
            jnp.where(part == 0, less(even, 0), same(even, 32)),
            jnp.where(part == 2, less(odd, 64), same(odd, 96)),
        )

    rows = [
        jnp.concatenate([base_x, base_y], axis=0),
        jnp.concatenate([steps(x0, x1), zero], axis=0),
        jnp.concatenate([zero, steps(y0, y1)], axis=0),
    ]
    return jnp.concatenate(rows, axis=1).astype(BF16)


def gelu_and_slope(z):
    a = jnp.abs(z)
    t = 1.0 / (1.0 + (0.3275911 / math.sqrt(2.0)) * a)
    poly = 1.061405429 * 0.5
    for term in (-1.453152027, 1.421413741, -0.284496736, 0.254829592):
        poly = poly * t + 0.5 * term
    e = jnp.exp(-0.5 * z * z)
    tail = poly * t * e
    cdf = jnp.where(z < 0, tail, 1.0 - tail)
    return z * cdf, cdf + z * (e * (1.0 / math.sqrt(2.0 * math.pi)))


def forward_kernel(plan, params_in, hidden_in, cot_in, boxes, lengths, turns, *refs):
    (w_qkv_out, w_out_out, w_in_out, w_back_out, features_out, low_out, q_out, k_out, v_out, probs_out,
     context_out, hat_out, normed_out, vec_out, rstd_out, cot_ref, hot_out, rest_out, share_out) = refs[:19]
    refs = refs[19:]
    (flat, staged, own, w_qkv, w_out, w_box, w_in, w_back, notes, features, hidden, start, start_low, q_ref,
     k_ref, v_ref, hot_ref, key_x, key_y, bands, tilted, wides, scores, context_t, pair_t, hat, narrow,
     square, vec) = refs[:29]
    note_sems, swap_sems, copy_sems, probs_sems = refs[29:33]

    def lend(buffer, slot, lanes):
        return buffer.at[:, slot : slot + lanes]

    less_x, less_y = lend(square, 0, WINLEN), lend(square, WINLEN, WINLEN)
    probs = [lend(square, 2 * WINLEN, WINLEN), lend(square, 3 * WINLEN, WINLEN)]
    kaugs = [lend(narrow, 0, 2 * LANES), lend(narrow, 2 * LANES, 2 * LANES)]
    qaugs = [lend(narrow, 4 * LANES, 2 * LANES), lend(narrow, 6 * LANES, 2 * LANES)]
    met = lend(narrow, 8 * LANES, 3 * LANES)
    place = Place()
    normed_low = hidden
    context = features
    gathering = Gathering(place, flat, dict(zip(GATHER_SEMS, refs[33:])))
    matrices = (w_qkv, w_out, w_box, w_in, w_back)
    written = []

    def write_out(src, dst):
        copy = pltpu.make_async_copy(src, dst, copy_sems.at[len(written)])
        copy.start()
        written.append(copy)

    fetch = pltpu.make_async_copy(params_in, staged.at[: plan.rows], probs_sems.at[0])
    fetch.start()
    place.greet()
    fetch.wait()
    for quarter_at in range(COLUMNS):
        begin = quarter_at * plan.quarter
        own[quarter_at] = staged[begin : begin + plan.quarter, :].astype(BF16)
    gathering.spread(own, 0)
    gathering.spread(own, 1)

    quarter = WINLEN // DEPTH

    def exchange(source, target, kind):
        rows = pl.ds(pl.multiple_of(place.z * quarter, quarter), quarter)
        for d in range(DEPTH - 1):
            gathering_send(source.at[place.far[d]], target.at[rows], kind, d, place.peers_z[d])

    def gathering_send(src, dst, kind, d, peer):
        copy = remote(src, dst, swap_sems.at[kind, 0, d], swap_sems.at[kind, 1, d], peer)
        copy.start()
        gathering.sent.append(copy)

    def exchanged(target, kind):
        for d in range(DEPTH - 1):
            rows = pl.ds(pl.multiple_of(place.from_far[d] * quarter, quarter), quarter)
            remote(
                target.at[rows], target.at[rows], swap_sems.at[kind, 0, d], swap_sems.at[kind, 1, d],
                place.peer_x,
            ).wait_recv()

    finish_notes = spread_notes(place, own, notes, note_sems, plan)
    own_rows = pl.ds(pl.multiple_of(place.z * quarter, quarter), quarter)
    own_hidden = pltpu.make_async_copy(
        hidden_in.at[place.z], hidden.at[own_rows], swap_sems.at[0, 0, DEPTH - 1]
    )
    own_hidden.start()
    own_cot = pltpu.make_async_copy(
        cot_in.at[place.z], cot_ref.at[own_rows], swap_sems.at[1, 0, DEPTH - 1]
    )
    own_cot.start()
    gathering.spread_done(0)
    gathering.along_z(0, 0)
    gathering.spread_done(1)
    gathering.along_z(0, 1)

    rest, columns = token_columns(boxes, lengths, place.z)
    for part in range(BLOCKS):
        rows = slice(part * LANES, (part + 1) * LANES)
        for axis, less in ((0, less_x), (1, less_y)):
            less[rows, :] = jnp.where(
                rest[axis : axis + 1, :] < columns[rows, 6 + axis : 7 + axis], 1.0, 0.0
            ).astype(BF16)
    rest_out[...] = rest
    form_hots(columns, hot_ref, key_x, key_y, kaugs[0], qaugs[0])
    kaugs[1][:, LANES:] = kaugs[0][:, LANES:]
    qaugs[1][:, LANES:] = qaugs[0][:, LANES:]
    hot_out[...] = hot_ref[...]
    gathering.first(0, 0)
    gathering.along_z(1, 0)
    gathering.first(0, 1)
    gathering.along_z(1, 1)
    form_features(columns, turns, features)
    for n in range(D // LANES):
        rows = slice(n * LANES, (n + 1) * LANES)
        context_t[rows, :] = features[:, rows].T
    write_out(context_t, features_out)
    gathering.first(1, 0)
    exchange(hidden_in, hidden, 0)
    gathering.second(0, 0)
    gathering.first(1, 1)
    gathering.second(0, 1)
    _, _, note_row = note_place(plan)
    for row in range(VEC_ROWS):
        at = note_row + row
        vec[0:1, row * LANES : (row + 1) * LANES] = notes[at // 16 * 16 : at // 16 * 16 + 16, :].astype(
            F32
        )[at % 16 : at % 16 + 1, :]
    vec_out[...] = vec[...]
    table_row = note_row + VEC["tables"] // LANES
    assert table_row % 16 == 0
    form_tables(notes[table_row : table_row + 16, :], bands, tilted)

    gathering.third(0, 0)
    gathering.second(1, 0)
    gathering.third(0, 1)
    gathering.second(1, 1)
    gathering.complete(0)
    stage_column(plan, flat, staged, 0)
    exchanged(hidden, 0)
    gathering.along_z(2, 0)
    gathering.along_z(2, 1)
    form_matrices(plan, staged, matrices, 0)
    keep_carry(plan, staged)
    gathering.third(1, 0)
    gathering.third(1, 1)
    gathering.complete(1)
    stage_column(plan, flat, staged, 1)
    form_matrices(plan, staged, matrices, 1)
    keep_carry(plan, staged)
    write_out(w_qkv, w_qkv_out)
    write_out(w_out, w_out_out)

    own_hidden.wait()
    for n in range(D // NBLOCK):
        lanes = slice(n * NBLOCK, (n + 1) * NBLOCK)
        value = hidden[:, lanes].astype(F32) + matmul(features[...], w_box[:, lanes])
        start[:, lanes] = value
        start_low[:, lanes] = value.astype(BF16)
    write_out(start_low, low_out)
    written[0].wait()

    def project(n, carry):
        at = pl.multiple_of(n * NBLOCK, NBLOCK)
        lanes = pl.ds(at, NBLOCK)
        low = start_low[...]
        bias = vec[0:1, pl.ds(pl.multiple_of(VEC["q_bias"] + at, LANES), NBLOCK)]
        got = matmul(low, w_qkv[:, lanes]) + bias
        q_ref[:, lanes] = (got.astype(BF16).astype(F32) * HEAD_DIM ** (-0.5)).astype(BF16)
        k_ref[:, lanes] = matmul(low, w_qkv[:, pl.ds(pl.multiple_of(at + D, LANES), NBLOCK)]).astype(BF16)
        bias = vec[0:1, pl.ds(pl.multiple_of(VEC["v_bias"] + at, LANES), NBLOCK)]
        got = matmul(low, w_qkv[:, pl.ds(pl.multiple_of(at + 2 * D, LANES), NBLOCK)]) + bias
        v_ref[:, lanes] = got.astype(BF16)
        return carry

    lax.fori_loop(0, D // NBLOCK, project, 0)
    write_out(q_ref, q_out)
    write_out(k_ref, k_out)
    write_out(v_ref, v_out)
    gathering.first(2, 0)
    gathering.along_z(3, 0)
    gathering.first(2, 1)
    gathering.along_z(3, 1)

    low, high = half_masks()
    half = 2 * LANES

    def probs_copy(head, odd):
        return pltpu.make_async_copy(probs[odd], probs_out.at[head], probs_sems.at[odd])

    def one_pair(pair, carry):
        at = pl.multiple_of(pair * LANES, LANES)
        lanes = pl.ds(at, LANES)
        values_t = v_ref[:, lanes].T
        met[...] = matmul(hot_ref[:, :64], pair_rows(tilted, pair)).astype(BF16)
        for odd in range(2):
            mine, other = (low, high) if odd == 0 else (high, low)
            kaugs[odd][:, :LANES] = k_ref[:, lanes] * mine + hot_ref[...] * other
            qaugs[odd][:, :LANES] = q_ref[:, lanes] * mine + met[:, :LANES] * other
            skew_groups(bands[2 * pair + odd], wides.at[odd])

            @pl.when(pair > 0)
            def _():
                probs_copy(2 * pair + odd, odd).wait()

        for side in range(2):
            cols = slice(side * half, (side + 1) * half)
            tops = []
            for odd in range(2):
                whole = times_transposed(kaugs[odd][...], qaugs[odd][cols, :])
                steps_x = times_transposed(key_x[odd], met[cols, LANES : 2 * LANES])
                steps_y = times_transposed(key_y[odd], met[cols, 2 * LANES :])
                top = None
                for part in range(BLOCKS):
                    rows = slice(part * LANES, (part + 1) * LANES)
                    bias = []
                    for block in range(2 * side, 2 * side + 2):
                        step = max(-2, min(2, block - part)) + 2
                        bias.append(wides[odd, :, step * LANES : (step + 1) * LANES])
                    s = whole[rows] + jnp.concatenate(bias, axis=1)
                    s = s + steps_x[rows] * less_x[rows, cols].astype(F32)
                    s = s + steps_y[rows] * less_y[rows, cols].astype(F32)
                    scores[odd, rows, :] = s
                    best = jnp.max(s.reshape(LANES // 8, 8, half), axis=0)
                    top = best if top is None else jnp.maximum(top, best)
                tops.append(jnp.max(top, axis=0, keepdims=True))
            for odd in range(2):
                total = None
                for part in range(BLOCKS):
                    rows = slice(part * LANES, (part + 1) * LANES)
                    e = jnp.exp(scores[odd, rows, :] - tops[odd])
                    probs[odd][rows, cols] = e.astype(BF16)
                    add = jnp.sum(e.reshape(LANES // 8, 8, half), axis=0)
                    total = add if total is None else total + add
                share = 1.0 / jnp.sum(total, axis=0, keepdims=True)
                share_out[2 * pair + odd, :, cols] = share
                got = matmul(values_t[odd * HEAD_DIM : (odd + 1) * HEAD_DIM, :], probs[odd][:, cols])
                pair_t[odd * HEAD_DIM : (odd + 1) * HEAD_DIM, cols] = got * share
        for odd in range(2):
            probs_copy(2 * pair + odd, odd).start()
        both = pair_t[...]
        context_t[lanes, :] = both.astype(BF16)
        context[:, lanes] = both.T.astype(BF16)
        return carry

    lax.fori_loop(0, 2, one_pair, 0)
    gathering.second(2, 0)
    gathering.first(3, 0)
    gathering.second(2, 1)
    gathering.first(3, 1)
    exchange(cot_in, cot_ref, 1)
    lax.fori_loop(2, 4, one_pair, 0)
    for h in range(2):
        gathering.third(2, h)
        gathering.second(3, h)
    gathering.complete(2)
    stage_column(plan, flat, staged, 2)
    form_matrices(plan, staged, matrices, 2)
    keep_carry(plan, staged)
    write_out(w_in, w_in_out)
    lax.fori_loop(4, PAIRS, one_pair, 0)
    write_out(context_t, context_out)
    for h in range(2):
        gathering.third(3, h)

    def vector(name):
        return vec[0:1, VEC[name] : VEC[name] + D]

    for n in range(D // NBLOCK):
        lanes = slice(n * NBLOCK, (n + 1) * NBLOCK)
        bias = vec[0:1, VEC["out_bias"] + n * NBLOCK : VEC["out_bias"] + (n + 1) * NBLOCK]
        start[:, lanes] = start[:, lanes] + matmul(context[...], w_out[:, lanes]) + bias

    step_rows = 64

    def norm_first(n, carry):
        rows = pl.ds(pl.multiple_of(n * step_rows, step_rows), step_rows)
        x = start[rows, :]
        centred = x - jnp.mean(x, axis=1, keepdims=True)
        rstd = lax.rsqrt(jnp.mean(centred * centred, axis=1, keepdims=True) + norm_eps)
        xhat = centred * rstd
        hat[rows, :] = xhat
        rstd_out[rows, :] = jnp.broadcast_to(rstd, (step_rows, LANES))
        normed = xhat * vector("gain_one") + vector("shift_one")
        start[rows, :] = normed
        normed_low[rows, :] = normed.astype(BF16)
        return carry

    lax.fori_loop(0, WINLEN // step_rows, norm_first, 0)
    write_out(hat, hat_out)
    write_out(normed_low, normed_out)

    gathering.complete(3)
    stage_column(plan, flat, staged, 3)
    form_matrices(plan, staged, matrices, 3)
    write_out(w_back, w_back_out)
    for odd in range(2):
        probs_copy(0, odd).wait()
    exchanged(cot_ref, 1)
    own_cot.wait()
    for copy in written[1:]:
        copy.wait()
    finish_notes()
    gathering.finish()


def forward_pass(plan, params, hidden_in, cotangent, boxes, lengths):
    anywhere = pl.BlockSpec(memory_space=pl.ANY)
    vmem = pl.BlockSpec(memory_space=pltpu.VMEM)
    token = (WINLEN, D)

    def hbm(shape, dtype=BF16):
        return jax.ShapeDtypeStruct(shape, dtype), anywhere

    def near(shape, dtype=F32):
        return jax.ShapeDtypeStruct(shape, dtype), vmem

    outs = [
        hbm(MATRICES[0]), hbm(MATRICES[1]), hbm(MATRICES[3]), hbm(MATRICES[4]), hbm((D, WINLEN)), hbm(token),
        hbm(token), hbm(token), hbm(token), hbm((HEADS, WINLEN, WINLEN)), hbm((D, WINLEN)),
        hbm(token, F32), hbm(token), near((1, VEC_ROWS * LANES)), near((WINLEN, LANES)),
        near(token, BF16), near((WINLEN, LANES), BF16), near((2, WINLEN)),
        near((HEADS, 1, WINLEN)),
    ]
    scratch = [
        pltpu.VMEM((COLUMNS, CORES, DEPTH, COLUMNS, plan.quarter, LANES), BF16),
        pltpu.VMEM((plan.staged, LANES), F32),
        pltpu.VMEM((COLUMNS, plan.quarter, LANES), BF16),
    ]
    scratch += [pltpu.VMEM(layout, BF16) for layout in MATRICES]
    scratch += [
        pltpu.VMEM((NOTE_ROWS, LANES), BF16),
        pltpu.VMEM(token, BF16),
        pltpu.VMEM(token, BF16),
        pltpu.VMEM(token, F32),
        pltpu.VMEM(token, BF16),
        pltpu.VMEM(token, BF16),
        pltpu.VMEM(token, BF16),
        pltpu.VMEM(token, BF16),
        pltpu.VMEM((WINLEN, LANES), BF16),
        pltpu.VMEM((2, WINLEN, LANES), BF16),
        pltpu.VMEM((2, WINLEN, LANES), BF16),
        pltpu.VMEM((HEADS, 8, WIDE), F32),
        pltpu.VMEM((2 * HEADS, BUCKETS, LANES), F32),
        pltpu.VMEM((2, LANES, 5 * LANES), F32),
        pltpu.VMEM((2, WINLEN, 2 * LANES), F32),
        pltpu.VMEM((D, WINLEN), BF16),
        pltpu.VMEM((LANES, WINLEN), F32),
        pltpu.VMEM(token, F32),
        pltpu.VMEM((WINLEN, 11 * LANES), BF16),
        pltpu.VMEM((WINLEN, 4 * WINLEN), BF16),
        pltpu.VMEM((1, VEC_ROWS * LANES), F32),
        pltpu.SemaphoreType.DMA((2, 7)),
        pltpu.SemaphoreType.DMA((2, 2, DEPTH)),
        pltpu.SemaphoreType.DMA((16,)),
        pltpu.SemaphoreType.DMA((2,)),
    ]
    return pl.pallas_call(
        functools.partial(forward_kernel, plan),
        out_shape=[shape for shape, _ in outs],
        in_specs=[anywhere] * 3 + [vmem, pl.BlockSpec(memory_space=pltpu.SMEM), vmem],
        out_specs=[spec for _, spec in outs],
        scratch_shapes=scratch + sem_shapes(GATHER_SEMS),
        compiler_params=pltpu.CompilerParams(
            collective_id=0, has_side_effects=True, vmem_limit_bytes=62 * 2**20
        ),
        name="forward_pass",
    )(params, hidden_in, cotangent, boxes, lengths, jnp.asarray(turns_table()))


def token_info(doc_lengths, box_coords):
    places = jnp.arange(WINLEN, dtype=jnp.int32)
    first = places == 0
    doc = jnp.zeros((WINLEN,), jnp.int32)
    end = 0
    for d in range(3):
        end = end + doc_lengths[d]
        doc = doc + (places >= end).astype(jnp.int32)
        first = first | (places == end)
    rows = [box_coords[:, c] for c in range(4)] + [doc, first.astype(jnp.int32)]
    return jnp.stack(rows + [jnp.zeros_like(doc)] * 2).astype(F32)


class Reducing:
    def __init__(self, place, flat, swapped, one, two, deep, piece, result, sems, free):
        self.place = place
        self.flat = flat
        self.swapped = swapped
        self.one = one
        self.two = two
        self.deep = deep
        self.piece = piece
        self.result = result
        self.sems = sems
        self.free = free
        self.sent = {k: [] for k in range(COLUMNS)}

    def send(self, k, src, dst, kind, index, peer):
        copy = remote(src, dst, self.sems[kind].at[0, index], self.sems[kind].at[1, index], peer)
        copy.start()
        self.sent[k].append(copy)

    got = Gathering.got

    def settle(self, k):
        for copy in self.sent.pop(k):
            copy.wait_send()

    rows = Gathering.rows

    def swap(self, k, h):
        p = self.place
        slot = k % 2
        if k < 2 and h == 0:
            pl.semaphore_wait(self.free.at[slot], 1)
        self.send(
            k, self.flat.at[slot, 1 - p.core, :, :, self.rows(h)],
            self.swapped.at[slot, :, :, self.rows(h)], "core", 2 * k + h, p.peer_core,
        )

    def first(self, k, h):
        p = self.place
        slot = k % 2
        n, rows = 2 * k + h, self.rows(h)
        self.got(self.swapped.at[slot, :, :, rows], "core", n)

        def one(step, carry):
            z, quarter = step // COLUMNS, step % COLUMNS
            total = self.flat[slot, p.core, z, quarter, rows].astype(F32)
            total = total + self.swapped[slot, z, quarter, rows].astype(F32)
            self.flat[slot, p.core, z, quarter, rows] = total.astype(BF16)
            return carry

        lax.fori_loop(0, DEPTH * COLUMNS, one, 0)
        flat = self.flat
        for side, peer in ((0, p.peer_y), (1, p.peer_x)):
            self.send(
                k, flat.at[slot, p.core, 2 * side : 2 * side + 2, p.col_d, rows],
                self.one.at[k, side, :, rows], "one", 2 * n + side, peer,
            )
        if k >= 2 and h == 1:
            pl.semaphore_signal(
                self.free.at[slot], inc=1, device_id=p.peer_core, device_id_type=MESH
            )

    def second(self, k, h):
        p = self.place
        slot = k % 2
        n, rows = 2 * k + h, self.rows(h)
        for side, column in ((0, p.col_x), (1, p.col_y)):
            self.got(self.one.at[k, side, :, rows], "one", 2 * n + side)

            def one(step, carry, side=side, column=column):
                z = 2 * side + step
                total = self.flat[slot, p.core, z, column, rows].astype(F32)
                total = total + self.one[k, side, step, rows].astype(F32)
                self.flat[slot, p.core, z, column, rows] = total.astype(BF16)
                return carry

            lax.fori_loop(0, 2, one, 0)
        for side, column, peer in ((0, p.col_x, p.peer_x), (1, p.col_y, p.peer_y)):
            self.send(
                k, self.flat.at[slot, p.core, :, column, rows], self.two.at[k, side, :, rows], "two",
                2 * n + side, peer,
            )

    def third(self, k, h):
        p = self.place
        slot = k % 2
        n, rows = 2 * k + h, self.rows(h)
        for side in range(2):
            self.got(self.two.at[k, side, :, rows], "two", 2 * n + side)

        def one(z, carry):
            total = self.flat[slot, p.core, z, p.column, rows].astype(F32)
            total = total + self.two[k, 0, z, rows].astype(F32) + self.two[k, 1, z, rows].astype(F32)
            self.flat[slot, p.core, z, p.column, rows] = total.astype(BF16)
            return carry

        lax.fori_loop(0, DEPTH, one, 0)
        for d in range(DEPTH - 1):
            self.send(
                k, self.flat.at[slot, p.core, p.far[d], p.column, rows], self.deep.at[k, d, rows], "z",
                3 * n + d, p.peers_z[d],
            )

    def fourth(self, k, h):
        p = self.place
        n, rows = 2 * k + h, self.rows(h)
        for d in range(DEPTH - 1):
            self.got(self.deep.at[k, d, rows], "z", 3 * n + d)
        total = self.flat[k % 2, p.core, p.z, p.column, rows].astype(F32)
        for d in range(DEPTH - 1):
            total = total + self.deep[k, d, rows].astype(F32)
        self.piece[k, rows] = total.astype(BF16)

    def giving(self, k, h):
        p = self.place
        sems = self.sems["spread"]
        return remote(
            self.piece.at[k, self.rows(h)], self.result.at[p.column, self.rows(h)],
            sems.at[0, 2 * k + h], sems.at[1, 2 * p.column + h], p.at(k, p.core, p.z),
        )

    def give(self, k, h):
        @pl.when(self.place.column != k)
        def _():
            self.giving(k, h).start()

    def given(self, k, h):
        @pl.when(self.place.column != k)
        def _():
            self.giving(k, h).wait_send()

    def receive(self, out):
        p = self.place
        out[p.column] = self.piece[p.column].astype(F32)
        for column in (p.col_x, p.col_y, p.col_d):
            for h in range(2):
                self.got(self.result.at[column, self.rows(h)], "spread", 2 * column + h)
            out[column] = self.result[column].astype(F32)


REDUCE_SEMS = {"spread": 8, "z": 24, "one": 16, "two": 16, "core": 8}


def unstage_column(plan, flat, staged, k):
    def one(step, carry):
        shard, quarter = step // COLUMNS, step % COLUMNS
        base = plan.carry + shard * plan.rows + quarter * plan.quarter
        piece = staged[pl.ds(pl.multiple_of(base, 8), plan.quarter), :]
        flat[k % 2, shard // DEPTH, shard % DEPTH, quarter] = piece.astype(BF16)
        return carry

    lax.fori_loop(0, CORES * DEPTH * COLUMNS, one, 0)


class Notes:
    def __init__(self, place, notes, slots, sems):
        self.place, self.notes, self.slots, self.sems = place, notes, slots, sems
        p = place
        self.home = (p.column == COLUMNS - 1) & (p.core == CORES - 1)
        self.root = self.home & (p.z == DEPTH - 1)

    def copy(self, slot, peer):
        return remote(
            self.notes, self.slots.at[slot], self.sems.at[0, 0], self.sems.at[1, slot], peer
        )

    def take(self, slot):
        self.copy(slot, self.place.peer_core).wait_recv()
        self.notes[...] = self.notes[...] + self.slots[slot]

    def start(self):
        p = self.place

        @pl.when(p.core != CORES - 1)
        def _():
            self.copy(0, p.peer_core).start()

    def rise(self):
        p = self.place

        @pl.when(p.core == CORES - 1)
        def _():
            self.take(0)

        @pl.when((p.core == CORES - 1) & (p.column != COLUMNS - 1))
        def _():
            self.copy(1 + p.column, p.at(COLUMNS - 1, p.core, p.z)).start()

    def end(self):
        p = self.place

        @pl.when(self.home)
        def _():
            for slot in range(1, 4):
                self.take(slot)

        @pl.when(self.home & (p.z != DEPTH - 1))
        def _():
            self.copy(4 + p.z, p.at(p.column, p.core, DEPTH - 1)).start()

        @pl.when(self.root)
        def _():
            for slot in range(4, 7):
                self.take(slot)

        @pl.when(jnp.logical_not(self.root))
        def _():
            self.copy(0, p.peer_core).wait_send()


def cell_sums(whole, less):
    lane = lax.broadcasted_iota(jnp.int32, (1, LANES), 1)
    sub = lax.broadcasted_iota(jnp.int32, (8, LANES), 0)
    sums = []
    for axis in range(2):
        rows = slice(axis * BUCKETS, (axis + 1) * BUCKETS)
        every = pltpu.roll(whole[rows], (BUCKETS - axis * BUCKETS) % LANES, 1)
        below = pltpu.roll(less[rows], (BUCKETS - axis * BUCKETS) % LANES, 1)
        inside = (lane >= BUCKETS) & (lane < 2 * BUCKETS)
        every = jnp.where(inside, every, 0.0)
        below = jnp.where(inside, below, 0.0)
        x = every - below + pltpu.roll(below, LANES - 1, 1)
        total = None
        for group in range(BUCKETS // 8):
            y = x[8 * group : 8 * group + 8]
            y = y if group == 0 else pltpu.roll(y, LANES - 8 * group, 1)
            total = y if total is None else total + y
        for bit in (1, 2, 4):
            total = jnp.where((sub & bit) != 0, pltpu.roll(total, LANES - bit, 1), total)
        sums.append(jnp.sum(total, axis=0, keepdims=True))
    return sums


def exact_dot(a, b):
    return jnp.dot(a, b, preferred_element_type=F32, precision=lax.Precision.HIGHEST)


def bucket_rows(cell_ref, diag_ref):
    half = BUCKETS // 2
    column = lax.broadcasted_iota(jnp.int32, (1, LANES), 1)
    row = lax.broadcasted_iota(jnp.int32, (LANES, 1), 0)
    to = jnp.clip(row - BUCKETS, -half, half - 1) + half
    place = lax.broadcasted_iota(jnp.int32, (WIDE, 1), 0)
    along = place - LANES
    far = jnp.where(place < LANES, 0, jnp.where(place < 5 * LANES, 0, BUCKETS - 1))
    along = jnp.where(
        (place >= LANES) & (place < 4 * LANES),
        jnp.clip(along - LANES, -half, half - 1) + half,
        far,
    )
    first, rest = None, None
    zero = jnp.zeros((5, WIDE), F32)
    for m in range(4):
        hot_along = jnp.where(along + m * BUCKETS == column, 1.0, 0.0)
        got = exact_dot(
            jnp.concatenate([diag_ref[4 * n + m] for n in range(3)] + [zero], axis=0), hot_along
        )
        first = got if first is None else first + got
        hot_cell = jnp.where(to + m * BUCKETS == column, 1.0, 0.0)
        rows = [cell_ref[t * HEADS + 4 * n + m] for t in range(2) for n in range(3)]
        got = exact_dot(jnp.concatenate(rows + [zero[:2, :LANES]], axis=0), hot_cell)
        rest = got if rest is None else rest + got
    return jnp.concatenate([first[:3], rest[:6]], axis=0)


def backward_kernel(
    plan, w_back_in, w_in_in, w_out_in, w_qkv_in, normed_in, low_in, features_in,
    context_in, q_in, k_in, v_in, probs_in, hat_in, cot_in, rstd_ref, vec, hot_ref, rest_ref, share_ref,
    *refs,
):
    out, output_pos, hidden_pos, spill = refs[:4]
    (flat, staged, swapped, one_buf, two_buf, deep, piece, result, active, slope, w_back, w_in, w_out,
     turned, context_t, q_ref, k_ref, v_ref, hat, second, branch, dctx, probs, less_x,
     less_y, scores_odd, bands, hot_t, pair_t, scaled, share_cols, vecg, cell_rows, diag_rows, notes, slots,
     ) = refs[4:40]
    load_sems, probs_sems, free, pos_sems, note_sems, spill_sems = refs[40:46]
    place = Place()
    reducing = Reducing(
        place, flat, swapped, one_buf, two_buf, deep, piece, result,
        dict(zip(REDUCE_SEMS, refs[46:])), free,
    )
    climbing = Notes(place, notes, slots, note_sems)
    loads = {}

    def load(name, src, dst):
        loads[name] = pltpu.make_async_copy(src, dst, load_sems.at[len(loads)])
        loads[name].start()

    mixed = active.at[:, : 3 * D]
    grad_attn = branch
    w_qkv = w_in.at[:, : 3 * D]
    hidden_low = dctx
    features_t = w_back.at[:D, :WINLEN]
    low_t = w_out.at[:WINLEN]
    scores = [hat.at[:, :WINLEN], scores_odd]
    dscores = [slope.at[:, :WINLEN], slope.at[:, WINLEN : 2 * WINLEN]]
    output_low = w_out.at[:WINLEN]
    output_low = w_out.at[:WINLEN]
    dscores_x = [slope.at[:, 2 * WINLEN : 3 * WINLEN], slope.at[:, 3 * WINLEN : 4 * WINLEN]]
    dscores_y = [slope.at[:, 4 * WINLEN : 5 * WINLEN], slope.at[:, 5 * WINLEN :]]

    load("normed", normed_in, dctx)
    load("w_in", w_in_in, w_in)
    load("hat", hat_in, hat)
    load("w_back", w_back_in, w_back)
    load("cot", cot_in, branch)

    at = staged_at(plan, COLUMNS - 1, plan.misc_start)
    staged[at:, :] = jnp.zeros((plan.staged - at, LANES), F32)
    place.greet()

    quarter = WINLEN // DEPTH
    positions = []

    def to_pos(source, target, kind):
        for d in range(DEPTH - 1):
            rows = pl.ds(pl.multiple_of(place.far[d] * quarter, quarter), quarter)
            copy = remote(
                source.at[rows], target.at[place.z], pos_sems.at[kind, 0, d], pos_sems.at[kind, 1, d],
                place.peers_z[d],
            )
            copy.start()
            positions.append(copy)
        rows = pl.ds(pl.multiple_of(place.z * quarter, quarter), quarter)
        copy = pltpu.make_async_copy(
            source.at[rows], target.at[place.z], pos_sems.at[kind, 0, DEPTH - 1]
        )
        copy.start()
        return copy

    def in_pos(target, kind):
        for d in range(DEPTH - 1):
            there = target.at[place.from_far[d]]
            remote(
                there, there, pos_sems.at[kind, 0, d], pos_sems.at[kind, 1, d], place.peer_x
            ).wait_recv()


    def store(k, index, row, value, first_block=0):
        blocks = MATRICES[index][1] // LANES
        base = staged_at(plan, k, plan.starts[index]) + row * blocks + first_block
        for block in range(value.shape[1] // LANES):
            staged[pl.ds(base + block, value.shape[0], stride=blocks), :] = value[
                :, block * LANES : (block + 1) * LANES
            ]

    def column_sum(value):
        return jnp.sum(value, axis=0, keepdims=True)

    def keep_vector(name, lanes_at, value):
        at = pl.multiple_of(VEC[name] + lanes_at, LANES)
        vecg[0:1, pl.ds(at, value.shape[1])] = value

    def vector(name, at=0, size=D):
        return vec[0:1, pl.ds(pl.multiple_of(VEC[name] + at, LANES), size)]

    loads["normed"].wait()
    loads["w_in"].wait()

    def widen(n, carry):
        at = pl.multiple_of(n * NBLOCK, NBLOCK)
        lanes = pl.ds(at, NBLOCK)
        inner_act = matmul(dctx[...], w_in[:, lanes]) + vector("in_bias", at, NBLOCK)
        value, change = gelu_and_slope(inner_act)
        active[:, lanes] = value.astype(BF16)
        slope[:, lanes] = change.astype(BF16)
        return carry

    lax.fori_loop(0, FF // NBLOCK, widen, 0, unroll=2)
    loads["hat"].wait()
    loads["w_back"].wait()
    for n in range(D // NBLOCK):
        lanes = slice(n * NBLOCK, (n + 1) * NBLOCK)
        normed = hat[:, lanes] * vector("gain_one", n * NBLOCK, NBLOCK) + vector(
            "shift_one", n * NBLOCK, NBLOCK
        )
        second[:, lanes] = (
            normed + matmul(active[...], w_back[:, lanes]) + vector("back_bias", n * NBLOCK, NBLOCK)
        )
    loads["cot"].wait()
    step_rows = 64
    for name in ("gain_two", "shift_two", "back_bias", "gain_one", "shift_one", "out_bias"):
        keep_vector(name, 0, jnp.zeros((1, D), F32))

    def add_vector(name, term):
        lanes = slice(VEC[name], VEC[name] + D)
        vecg[0:1, lanes] = vecg[0:1, lanes] + column_sum(term)

    def norm_second(n, carry):
        rows = pl.ds(pl.multiple_of(n * step_rows, step_rows), step_rows)
        x = second[rows, :]
        centred = x - jnp.mean(x, axis=1, keepdims=True)
        rstd = lax.rsqrt(jnp.mean(centred * centred, axis=1, keepdims=True) + norm_eps)
        xhat = centred * rstd
        gain = vector("gain_two")
        output_low[rows, :] = (xhat * gain + vector("shift_two")).astype(BF16)
        cot = branch[rows, :].astype(F32)
        prod = cot * xhat
        gc = cot * gain
        mean_one = jnp.mean(gc, axis=1, keepdims=True)
        mean_two = jnp.mean(prod * gain, axis=1, keepdims=True)
        value = rstd * (gc - mean_one - xhat * mean_two)
        second[rows, :] = value
        value = value.astype(BF16)
        branch[rows, :] = value
        add_vector("gain_two", prod)
        add_vector("shift_two", cot)
        add_vector("back_bias", value.astype(F32))
        return carry

    lax.fori_loop(0, WINLEN // step_rows, norm_second, 0, unroll=2)
    own_output = to_pos(output_low, output_pos, 0)

    def back_rows(k, size, begin, count):
        def body(n, carry):
            row = pl.multiple_of(begin + n * size, LANES)
            turned[:size, :] = active[:, pl.ds(row, size)].T
            store(k, 4, row, matmul(turned[:size, :], branch[...]))
            return carry

        lax.fori_loop(0, count, body, 0)

    back_rows(3, WINLEN, 512, FF // WINLEN - 1)
    unstage_column(plan, flat, staged, 3)
    reducing.swap(3, 0)
    reducing.swap(3, 1)

    back_rows(2, WINLEN, 0, 1)
    back_rows(2, LANES, 512, 1)

    def inner(n, carry):
        at = pl.multiple_of(n * NBLOCK, NBLOCK)
        lanes = pl.ds(at, NBLOCK)
        value = times_transposed(branch[...], w_back[lanes, :]) * slope[:, lanes].astype(F32)
        value = value.astype(BF16)
        slope[:, lanes] = value
        keep_vector("in_bias", at, column_sum(value.astype(F32)))
        return carry

    lax.fori_loop(0, FF // NBLOCK, inner, 0, unroll=2)
    grad_inner = slope
    reducing.first(3, 0)
    reducing.first(3, 1)

    for n in range(D // NBLOCK):
        rows = slice(n * NBLOCK, (n + 1) * NBLOCK)
        turned[rows, :] = dctx[:, rows].T

    def in_rows(k, begin, end):
        def body(n, carry):
            lanes = pl.ds(pl.multiple_of(n * NBLOCK, NBLOCK), NBLOCK)
            got = matmul(turned[begin:end, :], grad_inner[:, lanes])
            store(k, 3, begin, got, n * (NBLOCK // LANES))
            return carry

        lax.fori_loop(0, FF // NBLOCK, body, 0)

    in_rows(2, 288, D)
    unstage_column(plan, flat, staged, 2)
    reducing.swap(2, 0)
    reducing.swap(2, 1)
    reducing.second(3, 0)
    reducing.second(3, 1)

    load("context", context_in, context_t)
    load("q", q_in, q_ref)
    load("k", k_in, k_ref)
    load("v", v_in, v_ref)
    for odd in range(2):
        pltpu.make_async_copy(probs_in.at[odd], probs.at[odd], probs_sems.at[odd]).start()
    for n in range(D // NBLOCK):
        lanes = slice(n * NBLOCK, (n + 1) * NBLOCK)
        second[:, lanes] = second[:, lanes] + times_transposed(grad_inner[...], w_in[lanes, :])
    load("w_qkv", w_qkv_in, w_qkv)
    load("features", features_in, features_t)
    reducing.first(2, 0)
    reducing.first(2, 1)

    for copy in positions:
        copy.wait_send()
    own_output.wait()
    load("w_out", w_out_in, w_out)

    def norm_first(n, carry):
        rows = pl.ds(pl.multiple_of(n * step_rows, step_rows), step_rows)
        grad = second[rows, :]
        xhat = hat[rows, :]
        prod = grad * xhat
        gain = vec[0:1, VEC["gain_one"] : VEC["gain_one"] + D]
        gc = grad * gain
        mean_one = jnp.mean(gc, axis=1, keepdims=True)
        mean_two = jnp.mean(prod * gain, axis=1, keepdims=True)
        value = rstd_ref[rows, 0:1] * (gc - mean_one - xhat * mean_two)
        second[rows, :] = value
        value = value.astype(BF16)
        grad_attn[rows, :] = value
        add_vector("gain_one", prod)
        add_vector("shift_one", grad)
        add_vector("out_bias", value.astype(F32))
        return carry

    lax.fori_loop(0, WINLEN // step_rows, norm_first, 0, unroll=2)
    reducing.third(3, 0)
    reducing.third(3, 1)
    loads["w_out"].wait()
    for n in range(D // NBLOCK):
        lanes = slice(n * NBLOCK, (n + 1) * NBLOCK)
        dctx[:, lanes] = times_transposed(grad_attn[...], w_out[lanes, :]).astype(BF16)
    load("low", low_in, low_t)
    loads["context"].wait()
    in_rows(1, 0, 304)
    reducing.second(2, 0)
    reducing.second(2, 1)

    def out_rows(k, begin, end):
        for n in range(D // NBLOCK):
            lanes = slice(n * NBLOCK, (n + 1) * NBLOCK)
            got = matmul(context_t[begin:end, :], grad_attn[:, lanes])
            store(k, 1, begin, got, n * (NBLOCK // LANES))

    out_rows(1, 192, D)
    reducing.fourth(3, 0)
    reducing.fourth(3, 1)
    reducing.give(3, 0)
    reducing.give(3, 1)

    low, high = half_masks()
    rest = rest_ref[...]
    columns = jnp.concatenate([rest, jnp.zeros((LANES - 2, WINLEN), F32)], axis=0).T
    for part in range(BLOCKS):
        rows = slice(part * LANES, (part + 1) * LANES)
        for axis, less in ((0, less_x), (1, less_y)):
            less[rows, :] = jnp.where(
                rest[axis : axis + 1, :] < columns[rows, axis : axis + 1], 1.0, 0.0
            ).astype(BF16)
    hot_t[...] = hot_ref[...].T
    lane = lax.broadcasted_iota(jnp.int32, (1, LANES), 1)
    scale = HEAD_DIM ** (-0.5)
    of_x = jnp.where((lane // BUCKETS) % 2 == 0, 1.0, 0.0)
    share_cols[...] = jnp.concatenate(
        [share_ref[head] for head in range(HEADS)] + [jnp.zeros((LANES - HEADS, WINLEN), F32)], axis=0
    ).T
    for name in ("q", "k", "v"):
        loads[name].wait()

    def probs_copy(head, odd):
        return pltpu.make_async_copy(probs_in.at[head], probs.at[odd], probs_sems.at[odd])

    def spill_copy(head, odd):
        return pltpu.make_async_copy(dscores[odd], spill.at[head], spill_sems.at[odd])

    def one_pair(pair, carry):
        at = pl.multiple_of(pair * LANES, LANES)
        lanes = pl.ds(at, LANES)
        keys_t = k_ref[:, lanes].T
        both = pltpu.roll(share_cols[...], lax.rem(LANES - 2 * pair, LANES), 1)
        both = jnp.where(lane < HEAD_DIM, both[:, 0:1], both[:, 1:2])
        scaled[...] = (dctx[:, lanes].astype(F32) * both).astype(BF16)
        grad_context = dctx[:, lanes]
        dots = []
        for odd in range(2):
            mine, other = (low, high) if odd == 0 else (high, low)
            head = 2 * pair + odd
            probs_copy(head, odd).wait()
            products = times_transposed(v_ref[:, lanes] * mine, grad_context)
            dot = None
            for part in range(BLOCKS):
                rows = slice(part * LANES, (part + 1) * LANES)
                dp = products[rows]
                scores[odd][rows, :] = dp
                add = dp * probs[odd, rows, :].astype(F32)
                add = jnp.sum(add.reshape(LANES // 8, 8, WINLEN), axis=0)
                dot = add if dot is None else dot + add
            dots.append(column_sum(dot) * share_ref[head])
        for odd in range(2):
            head = 2 * pair + odd
            share = share_ref[head]

            @pl.when(pair > 0)
            def _():
                spill_copy(head, odd).wait()

            for part in range(BLOCKS):
                rows = slice(part * LANES, (part + 1) * LANES)
                ds = probs[odd, rows, :].astype(F32) * ((scores[odd][rows, :] - dots[odd]) * share)
                dscores[odd][rows, :] = ds.astype(BF16)
            spill_copy(head, odd).start()
        for odd in range(2):
            head = 2 * pair + odd
            keys_grad = matmul(dscores[odd][...], q_ref[:, lanes])
            values_grad = matmul(probs[odd], scaled[...])

            pair_t[odd * HEAD_DIM : (odd + 1) * HEAD_DIM, :] = matmul(
                keys_t[odd * HEAD_DIM : (odd + 1) * HEAD_DIM, :], dscores[odd][...]
            )
            for which, value in ((1, keys_grad), (2, values_grad)):
                there = pl.ds(pl.multiple_of(at + which * D, LANES), LANES)
                value = value.astype(BF16)
                if odd:
                    value = mixed[:, there] * low + value * high
                mixed[:, there] = value

        @pl.when(pair < PAIRS - 1)
        def _():
            for odd in range(2):
                probs_copy(2 * pair + odd + 2, odd).start()

        value = (pair_t[...].T * scale).astype(BF16)
        mixed[:, lanes] = value
        keep_vector("q_bias", at, column_sum(value.astype(F32)))
        there = pl.ds(pl.multiple_of(at + 2 * D, LANES), LANES)
        keep_vector("v_bias", at, column_sum(mixed[:, there].astype(F32)))
        return carry

    lax.fori_loop(0, 2, one_pair, 0)
    reducing.third(2, 0)
    reducing.third(2, 1)
    lax.fori_loop(2, 4, one_pair, 0)
    reducing.fourth(2, 0)
    reducing.fourth(2, 1)
    reducing.give(2, 0)
    reducing.give(2, 1)
    lax.fori_loop(4, PAIRS, one_pair, 0)

    for odd in range(2):
        spill_copy(0, odd).wait()
    loads["w_qkv"].wait()
    for n in range(D // NBLOCK):
        lanes = slice(n * NBLOCK, (n + 1) * NBLOCK)
        value = second[:, lanes] + times_transposed(mixed[...], w_qkv[lanes, :])
        hidden_low[:, lanes] = value.astype(BF16)
    own_hidden = to_pos(hidden_low, hidden_pos, 1)
    loads["features"].wait()
    for n in range(D // NBLOCK):
        lanes = slice(n * NBLOCK, (n + 1) * NBLOCK)
        store(1, 2, 0, matmul(features_t[...], hidden_low[:, lanes]), n * (NBLOCK // LANES))
    reducing.settle(3)
    unstage_column(plan, flat, staged, 1)
    reducing.swap(1, 0)
    reducing.swap(1, 1)

    loads["low"].wait()
    for n in range(D // NBLOCK):
        rows = slice(n * NBLOCK, (n + 1) * NBLOCK)
        turned[rows, :] = low_t[:, rows].T

    def qkv_rows(n, carry):
        lanes = pl.ds(pl.multiple_of(n * NBLOCK, NBLOCK), NBLOCK)
        store(0, 0, 0, matmul(turned[...], mixed[:, lanes]), n * (NBLOCK // LANES))
        return carry

    lax.fori_loop(0, 3 * D // NBLOCK, qkv_rows, 0)
    out_rows(0, 0, 208)
    reducing.settle(2)
    unstage_column(plan, flat, staged, 0)
    reducing.swap(0, 0)
    reducing.swap(0, 1)

    def fetch_scores(head):
        there = slope.at[:, pl.ds(pl.multiple_of(lax.rem(head, 2) * WINLEN, WINLEN), WINLEN)]
        return pltpu.make_async_copy(spill.at[head], there, spill_sems.at[lax.rem(head, 2)])

    cells = [hot_ref[...] * of_x.astype(BF16), hot_ref[...] * (1.0 - of_x).astype(BF16)]
    band = bands.at[0]
    parts_x = slope.at[:, 2 * WINLEN : 3 * WINLEN]
    parts_y = slope.at[:, 3 * WINLEN : 4 * WINLEN]

    def one_table(head, carry):
        fetch_scores(head).wait()

        @pl.when(head < HEADS - 1)
        def _():
            fetch_scores(head + 1).start()

        here = slope.at[:, pl.ds(pl.multiple_of(lax.rem(head, 2) * WINLEN, WINLEN), WINLEN)]
        band[...] = jnp.zeros_like(band)
        for part in range(BLOCKS):
            rows = slice(part * LANES, (part + 1) * LANES)
            low_ds = here[rows, :]
            parts_x[rows, :] = low_ds * less_x[rows, :]
            parts_y[rows, :] = low_ds * less_y[rows, :]
            ds = low_ds.astype(F32)
            for block in range(BLOCKS):
                step = max(-2, min(2, block - part)) + 2
                where = slice(step * LANES, (step + 1) * LANES)
                band[:, where] = band[:, where] + ds[:, block * LANES : (block + 1) * LANES]
        whole = matmul(here[...], hot_ref[...])
        less = matmul(parts_x[...], cells[0]) + matmul(parts_y[...], cells[1])
        diag_rows[head, :, LANES : 5 * LANES] = diagonal_sums(band)
        diag_rows[head, :, :LANES] = column_sum(band[:, :LANES])
        diag_rows[head, :, 5 * LANES :] = column_sum(band[:, 4 * LANES :])
        sums = []
        for summed in (whole, less):
            first = summed.astype(BF16)
            remainder = (summed - first.astype(F32)).astype(BF16)
            sums.append(matmul(hot_t[:64, :], first) + matmul(hot_t[:64, :], remainder))
        for axis, value in enumerate(cell_sums(sums[0], sums[1])):
            cell_rows[axis * HEADS + head] = value
        return carry

    fetch_scores(0).start()
    reducing.first(1, 0)
    reducing.first(1, 1)
    lax.fori_loop(0, 4, one_table, 0)
    reducing.first(0, 0)
    reducing.second(1, 0)
    reducing.first(0, 1)
    reducing.second(1, 1)
    lax.fori_loop(4, 8, one_table, 0)
    reducing.second(0, 0)
    reducing.third(1, 0)
    reducing.second(0, 1)
    reducing.third(1, 1)
    lax.fori_loop(8, HEADS, one_table, 0)
    notes[...] = jnp.zeros_like(notes)
    table = VEC["tables"] // LANES
    for row in range(table):
        notes[row : row + 1, :] = vecg[0:1, row * LANES : (row + 1) * LANES]
    notes[table : table + 9, :] = bucket_rows(cell_rows, diag_rows)
    climbing.start()
    reducing.third(0, 0)
    reducing.fourth(1, 0)
    reducing.give(1, 0)
    climbing.rise()
    reducing.third(0, 1)
    reducing.fourth(1, 1)
    reducing.give(1, 1)
    reducing.fourth(0, 0)
    reducing.give(0, 0)
    climbing.end()
    reducing.fourth(0, 1)
    reducing.give(0, 1)
    reducing.receive(out)
    note_quarter, note_first, note_row = note_place(plan)
    base = note_first + note_row

    @pl.when(climbing.root)
    def _():
        out[note_quarter, base : base + MISC_ROWS, :] = (
            out[note_quarter, base : base + MISC_ROWS, :] + notes[:MISC_ROWS, :]
        )

    in_pos(output_pos, 0)
    in_pos(hidden_pos, 1)
    own_hidden.wait()
    for copy in positions[DEPTH - 1 :]:
        copy.wait_send()
    for k in range(COLUMNS):
        for h in range(2):
            reducing.given(k, h)
    reducing.settle(1)
    reducing.settle(0)


def backward_pass(plan, operands):
    anywhere = pl.BlockSpec(memory_space=pl.ANY)
    vmem = pl.BlockSpec(memory_space=pltpu.VMEM)
    token = (WINLEN, D)
    block = (plan.quarter, LANES)
    positions = jax.ShapeDtypeStruct((DEPTH, WINLEN // DEPTH, D), BF16)
    scratch = [
        pltpu.VMEM((2, CORES, DEPTH, COLUMNS) + block, BF16),
        pltpu.VMEM((plan.staged, LANES), F32),
        pltpu.VMEM((2, DEPTH, COLUMNS) + block, BF16),
        pltpu.VMEM((COLUMNS, 2, 2) + block, BF16),
        pltpu.VMEM((COLUMNS, 2, DEPTH) + block, BF16),
        pltpu.VMEM((COLUMNS, DEPTH - 1) + block, BF16),
        pltpu.VMEM((COLUMNS,) + block, BF16),
        pltpu.VMEM((COLUMNS,) + block, BF16),
        pltpu.VMEM((WINLEN, FF), BF16),
        pltpu.VMEM((WINLEN, FF), BF16),
        pltpu.VMEM((FF, D), BF16),
        pltpu.VMEM((D, FF), BF16),
        pltpu.VMEM((D, D), BF16),
        pltpu.VMEM((D, WINLEN), BF16),
        pltpu.VMEM((D, WINLEN), BF16),
        pltpu.VMEM(token, BF16),
        pltpu.VMEM(token, BF16),
        pltpu.VMEM(token, BF16),
        pltpu.VMEM(token, F32),
        pltpu.VMEM(token, F32),
        pltpu.VMEM(token, BF16),
        pltpu.VMEM(token, BF16),
        pltpu.VMEM((2, WINLEN, WINLEN), BF16),
        pltpu.VMEM((WINLEN, WINLEN), BF16),
        pltpu.VMEM((WINLEN, WINLEN), BF16),
        pltpu.VMEM((WINLEN, WINLEN), F32),
        pltpu.VMEM((1, LANES, 5 * LANES), F32),
        pltpu.VMEM((LANES, WINLEN), BF16),
        pltpu.VMEM((LANES, WINLEN), F32),
        pltpu.VMEM((WINLEN, LANES), BF16),
        pltpu.VMEM((WINLEN, LANES), F32),
        pltpu.VMEM((1, VEC_ROWS * LANES), F32),
        pltpu.VMEM((2 * HEADS, 1, LANES), F32),
        pltpu.VMEM((HEADS, 1, WIDE), F32),
        pltpu.VMEM((NOTE_ROWS, LANES), F32),
        pltpu.VMEM((7, NOTE_ROWS, LANES), F32),
        pltpu.SemaphoreType.DMA((16,)),
        pltpu.SemaphoreType.DMA((2,)),
        pltpu.SemaphoreType.REGULAR((2,)),
        pltpu.SemaphoreType.DMA((2, 2, DEPTH)),
        pltpu.SemaphoreType.DMA((2, 7)),
        pltpu.SemaphoreType.DMA((2,)),
    ]
    return pl.pallas_call(
        functools.partial(backward_kernel, plan),
        out_shape=[
            jax.ShapeDtypeStruct((COLUMNS,) + block, F32), positions, positions,
            jax.ShapeDtypeStruct((HEADS, WINLEN, WINLEN), BF16),
        ],
        in_specs=[anywhere] * 14 + [vmem] * 5,
        out_specs=[vmem] + [anywhere] * 3,
        scratch_shapes=scratch + sem_shapes(REDUCE_SEMS),
        compiler_params=pltpu.CompilerParams(
            collective_id=1, has_side_effects=True, vmem_limit_bytes=62 * 2**20
        ),
        name="backward_pass",
    )(*operands)


def fast_shards(hidden_in, cotangent, box_coords, doc_lengths, params, moment_one, moment_two):
    shard_len = params.shape[0]
    plan = Plan(shard_len)
    (proj_qkv, proj_out, proj_in, proj_back, features_t, start_low, queries, keys, values, probs, context_t,
     xhat, normed_low, vec, rstd, cot, hot_two,
     rest_rows, share) = forward_pass(
        plan, params.reshape(plan.rows, LANES), hidden_in, cotangent,
        jnp.transpose(box_coords, (0, 2, 1)), doc_lengths,
    )
    summed, output_low, grad_hidden, _ = backward_pass(
        Plan(shard_len, carry=5 * LANES),
        (proj_back, proj_in, proj_out, proj_qkv, normed_low, start_low, features_t, context_t, queries, keys,
         values, probs, xhat, cot, rstd, vec, hot_two, rest_rows, share),
    )
    grad_share = summed.reshape(plan.padded, LANES)[: plan.rows].reshape(-1)
    return finish_step(output_low, grad_hidden, grad_share, params, moment_one, moment_two)


def finish_step(output_low, grad_hidden, grad_share, params, moment_one, moment_two):
    shard_len = params.shape[0]
    index = lax.axis_index("dp") * lax.axis_size("head") + lax.axis_index("head")
    flat_index = index * shard_len + jnp.arange(shard_len, dtype=jnp.int32)
    param_step, new_one = adam_step(params, moment_one, moment_two, grad_share, flat_index)
    return (output_low, grad_hidden, grad_share, param_step, new_one)


def to_windows(shard):
    return lax.all_to_all(shard, "head", split_axis=0, concat_axis=1, tiled=True)


def to_positions(window):
    return lax.all_to_all(window, "head", split_axis=1, concat_axis=0, tiled=True)


def plain_shards(hidden_in, cotangent, box_coords, doc_lengths, params, moment_one, moment_two):
    head_pos = lax.axis_index("head")
    groups = lax.axis_size("head")
    shard_len = params.shape[0]
    flat_params = lax.all_gather(params.astype(BF16), ("dp", "head"), axis=0, tiled=True)
    pieces = unpack(flat_params)
    hidden = to_windows(hidden_in).reshape(WINLEN, D)
    cot = to_windows(cotangent).reshape(WINLEN, D)
    own_box = lax.dynamic_index_in_dim(box_coords, head_pos, 0, keepdims=False)
    own_lengths = lax.dynamic_index_in_dim(doc_lengths, head_pos, 0, keepdims=False)
    chosen, relative, centre_x, centre_y = window_layout(own_lengths, own_box)
    features = box_features(relative).astype(BF16)

    proj_qkv, proj_out, proj_box, proj_in, proj_back = pieces[:5]
    qv_bias, out_bias, norm_one, in_bias, back_bias, norm_two, tables = pieces[5:]
    ops = bias_operands(tables, chosen, centre_x, centre_y)
    start_state = hidden.astype(F32) + matmul(features, proj_box)
    start_low = start_state.astype(BF16)
    qv_float = qv_bias.astype(F32)
    mixed = matmul(start_low, proj_qkv)
    queries = (mixed[:, :D] + qv_float[0]).astype(BF16) * jnp.asarray(HEAD_DIM ** (-0.5), BF16)
    keys = mixed[:, D : 2 * D].astype(BF16)
    values = (mixed[:, 2 * D :] + qv_float[1]).astype(BF16)

    probs, context_t = attention_forward(queries, keys, values, ops)
    first_sum = start_state + rows_inner(context_t, proj_out) + out_bias.astype(F32)
    normed, norm_one_back = jax.vjp(layer_norm, first_sum, norm_one.astype(F32))
    normed_low = normed.astype(BF16)
    inner_act = matmul(normed_low, proj_in) + in_bias.astype(F32)
    active, gelu_back = jax.vjp(gelu_exact, inner_act)
    active_low = active.astype(BF16)
    second_sum = normed + matmul(active_low, proj_back) + back_bias.astype(F32)
    output, norm_two_back = jax.vjp(layer_norm, second_sum, norm_two.astype(F32))
    output_low = to_positions(output.astype(BF16).reshape(1, WINLEN, D))

    grad_second, grad_norm_two = norm_two_back(cot.astype(F32))
    grad_branch = grad_second.astype(BF16)
    grad_proj_back = rows_inner(active_low, grad_branch)
    grad_back_bias = jnp.sum(grad_branch.astype(F32), axis=0)
    (grad_inner_f,) = gelu_back(times_transposed(grad_branch, proj_back))
    grad_inner = grad_inner_f.astype(BF16)
    grad_proj_in = rows_inner(normed_low, grad_inner)
    grad_in_bias = jnp.sum(grad_inner.astype(F32), axis=0)
    grad_first, grad_norm_one = norm_one_back(grad_second + times_transposed(grad_inner, proj_in))
    grad_attn = grad_first.astype(BF16)
    grad_proj_out = matmul(context_t, grad_attn)
    grad_out_bias = jnp.sum(grad_attn.astype(F32), axis=0)
    grad_context = times_transposed(grad_attn, proj_out).astype(BF16)
    grad_queries_t, grad_keys, grad_values, cells, diag = attention_backward(
        queries, keys, values, grad_context, probs, ops
    )
    table_grad = table_grads(cells, diag)
    grad_mixed = jnp.concatenate([grad_queries_t.T, grad_keys, grad_values], axis=1)
    grad_proj_qkv = rows_inner(start_low, grad_mixed)
    summed = jnp.sum(grad_mixed.astype(F32), axis=0)
    grad_qv_bias = jnp.stack([summed[:D], summed[2 * D :]])
    grad_start = grad_first + times_transposed(grad_mixed, proj_qkv)
    grad_start_low = grad_start.astype(BF16)
    grad_hidden = to_positions(grad_start_low.reshape(1, WINLEN, D))
    grad_proj_box = rows_inner(features, grad_start_low)
    grad_list = (
        grad_proj_qkv,
        grad_proj_out,
        grad_proj_box,
        grad_proj_in,
        grad_proj_back,
        grad_qv_bias,
        grad_out_bias,
        grad_norm_one,
        grad_in_bias,
        grad_back_bias,
        grad_norm_two,
        table_grad,
    )
    padding = jnp.zeros((shard_len * groups * lax.axis_size("dp") - USED,), BF16)
    grads_flat = jnp.concatenate([piece.astype(BF16).reshape(-1) for piece in grad_list] + [padding])
    grad_share = lax.psum_scatter(
        grads_flat, ("dp", "head"), scatter_dimension=0, tiled=True
    ).astype(F32)
    return finish_step(output_low, grad_hidden, grad_share, params, moment_one, moment_two)


def solution(mesh):
    placed = (
        P("dp", "head", None),
        P("dp", "head", None),
        P("dp", None, None),
        P("dp", None),
        P(("dp", "head")),
        P(("dp", "head")),
        P(("dp", "head")),
    )
    return jax.shard_map(
        fast_shards if fits(mesh) else plain_shards,
        mesh=mesh,
        in_specs=placed,
        out_specs=(
            P("dp", "head", None),
            P("dp", "head", None),
            P(("dp", "head")),
            P(("dp", "head")),
            P(("dp", "head")),
        ),
        check_vma=False,
    )
```

```python
import functools
import math

import jax
import jax.numpy as jnp
import numpy as np
from jax import lax
from jax.experimental import pallas as pl
from jax.experimental.pallas import tpu as pltpu
from jax.sharding import PartitionSpec as P

D = 768
HEADS = 12
FF = 3072
BUCKETS = 32
WINLEN = 512
HEAD_DIM = 64
PAIRS = HEADS // 2
LANES = 128
BLOCKS = WINLEN // LANES

beta_one = 0.9
beta_two = 0.999
adam_eps = 1e-08
norm_eps = 1e-05
base_rate = 0.001
layer_decay = 0.75
decay_weight = 0.01
adam_count = 100
coord_cell = 32
masked_score = -1e30

F32 = jnp.float32
BF16 = jnp.bfloat16


def layouts_list():
    return (
        (D, 3 * D),
        (D, D),
        (D, D),
        (D, FF),
        (FF, D),
        (2, D),
        (D,),
        (2, D),
        (FF,),
        (D,),
        (2, D),
        (3, HEADS, BUCKETS),
    )


def unpack(flat_params):
    pieces = []
    offset = 0
    for layout in layouts_list():
        elements = math.prod(layout)
        pieces.append(flat_params[offset : offset + elements].reshape(layout))
        offset += elements
    return pieces


def matmul(left_mat, right_mat):
    return jnp.dot(left_mat, right_mat, preferred_element_type=F32)


def rows_inner(left_mat, right_mat):
    return lax.dot_general(left_mat, right_mat, (((0,), (0,)), ((), ())), preferred_element_type=F32)


def times_transposed(left_mat, right_mat):
    return lax.dot_general(left_mat, right_mat, (((1,), (1,)), ((), ())), preferred_element_type=F32)


def layer_norm(values, gain_bias):
    row_mean = jnp.mean(values, axis=-1, keepdims=True)
    centred = values - row_mean
    spread = jnp.mean(centred * centred, axis=-1, keepdims=True)
    return centred * lax.rsqrt(spread + norm_eps) * gain_bias[0] + gain_bias[1]


def gelu_exact(values):
    return jax.nn.gelu(values, approximate=False)


def hot(index, count):
    return (np.asarray(index)[..., None] == np.arange(count)).astype(np.float32)


def clipped(steps):
    return np.clip(steps, -(BUCKETS // 2), BUCKETS // 2 - 1) + BUCKETS // 2


CELLS = np.arange(BUCKETS)
HOT_SAME = hot(clipped(CELLS[:, None] - CELLS[None, :]), BUCKETS)
HOT_LESS = hot(clipped(CELLS[:, None] - CELLS[None, :] - 1), BUCKETS)
WIDE = 6 * LANES
_U = np.arange(WIDE)
BAND_HOT = hot(np.where(_U < 5 * LANES, clipped(_U - 2 * LANES), 0), BUCKETS)
_V = np.arange(4 * LANES)
DIAG_HOT = np.concatenate(
    [
        hot(np.zeros(LANES, np.int64), BUCKETS),
        hot(np.where(_V < 3 * LANES, clipped(_V - LANES), 0), BUCKETS),
        hot(np.full(LANES, BUCKETS - 1), BUCKETS),
    ]
)


def window_layout(doc_lengths, box_coords):
    doc_ends = jnp.cumsum(doc_lengths, dtype=jnp.int32)
    doc_starts = doc_ends - doc_lengths
    places = jnp.arange(WINLEN, dtype=jnp.int32)
    doc_ids = jnp.sum(
        (places[:, None] >= doc_ends[None, :]).astype(jnp.int32), axis=1, dtype=jnp.int32
    )
    docs = jnp.arange(doc_lengths.shape[0], dtype=jnp.int32)
    chosen = doc_ids[:, None] == docs[None, :]
    first_hot = places[:, None] == doc_starts[None, :]
    first_box = jnp.sum(
        jnp.where(first_hot[:, :, None], box_coords[:, None, :], 0), axis=0, dtype=jnp.int32
    )
    anchor = jnp.sum(
        jnp.where(chosen[:, :, None], first_box[None, :, :], 0), axis=1, dtype=jnp.int32
    )
    relative = box_coords - jnp.concatenate([anchor[:, :2], anchor[:, :2]], axis=1)
    centre_x = (box_coords[:, 0] + box_coords[:, 2]) // 2
    centre_y = (box_coords[:, 1] + box_coords[:, 3]) // 2
    return chosen, relative, centre_x, centre_y


def box_features(relative):
    count_freq = D // 8
    steps = jnp.arange(count_freq, dtype=F32)
    frequency = jnp.exp(steps * (-math.log(1000.0) / count_freq))
    angles = relative.astype(F32)[:, :, None] * frequency[None, None, :]
    return jnp.concatenate([jnp.sin(angles), jnp.cos(angles)], axis=2).reshape(relative.shape[0], D)


def bias_operands(tables, chosen, centre_x, centre_y):
    cell_x, cell_y = centre_x // coord_cell, centre_y // coord_cell
    rest_x, rest_y = centre_x % coord_cell, centre_y % coord_cell
    cells = jnp.arange(BUCKETS, dtype=jnp.int32)
    hot_x = (cell_x[:, None] == cells[None, :]).astype(BF16)
    hot_y = (cell_y[:, None] == cells[None, :]).astype(BF16)
    none = jnp.zeros_like(hot_x)
    hot_two = jnp.concatenate([hot_x, hot_y, hot_x, hot_y], axis=1)
    key_x = jnp.stack(
        [
            jnp.concatenate([hot_x, -hot_x, none, none], axis=1),
            jnp.concatenate([none, none, hot_x, -hot_x], axis=1),
        ]
    )
    key_y = jnp.stack(
        [
            jnp.concatenate([hot_y, -hot_y, none, none], axis=1),
            jnp.concatenate([none, none, hot_y, -hot_y], axis=1),
        ]
    )
    same = jnp.einsum("qcb,thb->thqc", HOT_SAME.astype(BF16), tables[1:], preferred_element_type=F32)
    less = jnp.einsum("qcb,thb->thqc", HOT_LESS.astype(BF16), tables[1:], preferred_element_type=F32)
    zero = jnp.zeros_like(same[0])
    base = jnp.concatenate(
        [jnp.concatenate([same[0], zero], axis=2), jnp.concatenate([zero, same[1]], axis=2)], axis=1
    )
    base = base.reshape(PAIRS, 2, 64, 64)[:, ::-1].reshape(HEADS, 64, 64)
    diff_x = jnp.concatenate([jnp.concatenate([less[0], same[0]], axis=2), jnp.zeros((HEADS, 32, 64), F32)], axis=1)
    diff_y = jnp.concatenate([jnp.zeros((HEADS, 32, 64), F32), jnp.concatenate([less[1], same[1]], axis=2)], axis=1)
    rows = jnp.concatenate([base, diff_x, diff_y], axis=0).astype(BF16)
    rows = rows.transpose(1, 0, 2).reshape(64, 3 * D)
    met = matmul(hot_two[:, :64], rows).astype(BF16)
    band = matmul(tables[0], jnp.asarray(BAND_HOT.T, BF16)).reshape(HEADS, 1, WIDE)
    rest_cols = jnp.stack([rest_x, rest_y], axis=1).astype(F32)
    rest_rows = rest_cols.T
    pad = jnp.zeros((WINLEN, LANES - chosen.shape[1]), BF16)
    marks = chosen.astype(BF16)
    mark_keys = jnp.concatenate([marks, pad], axis=1)
    mark_queries = jnp.concatenate([(1 - marks) * jnp.asarray(masked_score, BF16), pad], axis=1)
    return dict(
        hot_two=hot_two,
        key_x=key_x,
        key_y=key_y,
        met=met,
        band=band,
        rest_cols=rest_cols,
        rest_rows=rest_rows,
        mark_keys=mark_keys,
        mark_queries=mark_queries,
    )


def half_masks():
    lane = lax.broadcasted_iota(jnp.int32, (1, LANES), 1)
    low = (lane < HEAD_DIM).astype(F32)
    return low.astype(BF16), (1.0 - low).astype(BF16)


def less_masks(rest_cols, rest_rows, less_x, less_y):
    for part in range(BLOCKS):
        rows = slice(part * LANES, (part + 1) * LANES)
        for axis, less in ((0, less_x), (1, less_y)):
            column = rest_cols[rows, axis : axis + 1]
            row = rest_rows[axis : axis + 1, :]
            less[rows, :] = jnp.where(row < column, 1.0, 0.0).astype(less.dtype)


def attention_forward_kernel(
    q_ref, k_ref, v_ref, hot_ref, keyx_ref, keyy_ref, met_ref, band_ref, cols_ref, rows_ref,
    mkey_ref, mquery_ref, probs_ref, context_ref,
    kaug, qaug, less_x, less_y, wide, scores,
):
    low, high = half_masks()
    less_masks(cols_ref, rows_ref, less_x, less_y)
    kaug[:, LANES:] = mkey_ref[...]
    qaug[:, LANES:] = mquery_ref[...]
    half = 2 * LANES

    def one_pair(pair, carry):
        at = pl.multiple_of(pair * LANES, LANES)
        lanes = pl.ds(at, LANES)
        lanes_x = pl.ds(pl.multiple_of(at + D, LANES), LANES)
        lanes_y = pl.ds(pl.multiple_of(at + 2 * D, LANES), LANES)
        values_t = v_ref[:, lanes].T
        for odd in range(2):
            own, other = (low, high) if odd == 0 else (high, low)
            head = 2 * pair + odd
            kaug[:, :LANES] = k_ref[:, lanes] * own + hot_ref[...] * other
            qaug[:, :LANES] = q_ref[:, lanes] * own + met_ref[:, lanes] * other
            skew_band(band_ref[head], wide)
            for side in range(2):
                cols = slice(side * half, (side + 1) * half)
                top = None
                for part in range(BLOCKS):
                    rows = slice(part * LANES, (part + 1) * LANES)
                    s = times_transposed(kaug[rows, :], qaug[cols, :])
                    dx = times_transposed(keyx_ref[odd, rows, :], met_ref[cols, lanes_x])
                    dy = times_transposed(keyy_ref[odd, rows, :], met_ref[cols, lanes_y])
                    bias = []
                    for block in range(2 * side, 2 * side + 2):
                        step = max(-2, min(2, block - part)) + 2
                        bias.append(wide[:, step * LANES : (step + 1) * LANES])
                    s = s + jnp.concatenate(bias, axis=1)
                    s = s + dx * less_x[rows, cols] + dy * less_y[rows, cols]
                    scores[rows, :] = s
                    best = jnp.max(s, axis=0, keepdims=True)
                    top = best if top is None else jnp.maximum(top, best)
                total = None
                for part in range(BLOCKS):
                    rows = slice(part * LANES, (part + 1) * LANES)
                    e = jnp.exp(scores[rows, :] - top)
                    scores[rows, :] = e
                    add = jnp.sum(e, axis=0, keepdims=True)
                    total = add if total is None else total + add
                share = 1.0 / total
                for part in range(BLOCKS):
                    rows = slice(part * LANES, (part + 1) * LANES)
                    probs_ref[head, rows, cols] = (scores[rows, :] * share).astype(BF16)
                got = matmul(
                    values_t[odd * HEAD_DIM : (odd + 1) * HEAD_DIM, :], probs_ref[head, :, cols]
                )
                context_ref[pl.ds(pl.multiple_of(head * HEAD_DIM, HEAD_DIM), HEAD_DIM), cols] = (
                    got.astype(BF16)
                )
        return carry

    lax.fori_loop(0, PAIRS, one_pair, 0)


def skew_band(row, wide):
    x = jnp.broadcast_to(row, (8, WIDE))
    sub = lax.broadcasted_iota(jnp.int32, (8, WIDE), 0)
    for bit in (1, 2, 4):
        x = jnp.where((sub & bit) != 0, pltpu.roll(x, bit, 1), x)
    for group in range(LANES // 8):
        y = x if group == 0 else pltpu.roll(x, 8 * group, 1)
        wide[8 * group : 8 * group + 8, :] = y[:, : 5 * LANES]


def skew_groups(skewed, wide):
    for group in range(LANES // 8):
        y = skewed if group == 0 else pltpu.roll(skewed, 8 * group, 1)
        wide[8 * group : 8 * group + 8, :] = y[:, : 5 * LANES]


def diagonal_sums(parts):
    total = None
    for group in range(LANES // 8):
        x = jnp.concatenate(
            [parts[8 * group : 8 * group + 8, LANES : 4 * LANES], jnp.zeros((8, LANES), F32)], axis=1
        )
        y = x if group == 0 else pltpu.roll(x, 4 * LANES - 8 * group, 1)
        total = y if total is None else total + y
    sub = lax.broadcasted_iota(jnp.int32, (8, 4 * LANES), 0)
    for bit in (1, 2, 4):
        total = jnp.where((sub & bit) != 0, pltpu.roll(total, 4 * LANES - bit, 1), total)
    return jnp.sum(total, axis=0, keepdims=True)


def attention_backward_kernel(
    q_ref, k_ref, v_ref, dctx_ref, probs_ref, hot_ref, cols_ref, rows_ref,
    dq_ref, dk_ref, dv_ref, cells_ref, diag_ref,
    qaug, less_x, less_y, scores, dscores, band, kept, hot_t,
):
    low, high = half_masks()
    less_masks(cols_ref, rows_ref, less_x, less_y)
    hot_t[...] = hot_ref[...].T
    lane = lax.broadcasted_iota(jnp.int32, (1, LANES), 1)
    scale = HEAD_DIM ** (-0.5)
    of_x = jnp.where((lane // BUCKETS) % 2 == 0, 1.0, 0.0)
    cells_x = hot_ref[...] * of_x.astype(BF16)
    cells_y = hot_ref[...] * (1.0 - of_x).astype(BF16)

    def one_pair(pair, carry):
        at = pl.multiple_of(pair * LANES, LANES)
        lanes = pl.ds(at, LANES)
        keys_t = k_ref[:, lanes].T
        for odd in range(2):
            own, other = (low, high) if odd == 0 else (high, low)
            head = 2 * pair + odd
            qaug[...] = q_ref[:, lanes] * own + hot_ref[...] * other
            dctx = dctx_ref[:, lanes]
            dot = None
            for part in range(BLOCKS):
                rows = slice(part * LANES, (part + 1) * LANES)
                dp = times_transposed(v_ref[rows, lanes] * own, dctx)
                scores[rows, :] = dp
                add = jnp.sum(dp * probs_ref[head, rows, :].astype(F32), axis=0, keepdims=True)
                dot = add if dot is None else dot + add
            band[...] = jnp.zeros_like(band)
            for part in range(BLOCKS):
                rows = slice(part * LANES, (part + 1) * LANES)
                probs = probs_ref[head, rows, :]
                ds = probs.astype(F32) * (scores[rows, :] - dot)
                for block in range(BLOCKS):
                    step = max(-2, min(2, block - part)) + 2
                    where = slice(step * LANES, (step + 1) * LANES)
                    band[:, where] = band[:, where] + ds[:, block * LANES : (block + 1) * LANES]
                ds = ds.astype(BF16)
                dscores[rows, :] = ds
                both = matmul(ds, qaug[...])
                less = matmul(ds * less_x[rows, :], cells_x) + matmul(ds * less_y[rows, :], cells_y)
                dv = matmul(probs, dctx)
                kept[odd, 0, rows, :] = both
                kept[odd, 1, rows, :] = less
                kept[odd, 2, rows, :] = dv
            got = matmul(keys_t[odd * HEAD_DIM : (odd + 1) * HEAD_DIM, :], dscores[...])
            dq_ref[pl.ds(pl.multiple_of(head * HEAD_DIM, HEAD_DIM), HEAD_DIM), :] = (
                got * scale
            ).astype(BF16)
            diag_ref[head, :, LANES : 5 * LANES] = diagonal_sums(band)
            diag_ref[head, :, :LANES] = jnp.sum(band[:, :LANES], axis=0, keepdims=True)
            diag_ref[head, :, 5 * LANES :] = jnp.sum(band[:, 4 * LANES :], axis=0, keepdims=True)
            for which in range(2):
                summed = kept[odd, which]
                first = summed.astype(BF16)
                rest = (summed - first.astype(F32)).astype(BF16)
                cells_ref[head, which] = matmul(hot_t[:64, :], first) + matmul(hot_t[:64, :], rest)
        dk_ref[:, lanes] = jnp.where(lane < HEAD_DIM, kept[0, 0], kept[1, 0]).astype(BF16)
        dv_ref[:, lanes] = jnp.where(lane < HEAD_DIM, kept[0, 2], kept[1, 2]).astype(BF16)
        return carry

    lax.fori_loop(0, PAIRS, one_pair, 0)


def attention_forward(queries, keys, values, ops):
    return pl.pallas_call(
        attention_forward_kernel,
        out_shape=(
            jax.ShapeDtypeStruct((HEADS, WINLEN, WINLEN), BF16),
            jax.ShapeDtypeStruct((D, WINLEN), BF16),
        ),
        scratch_shapes=[
            pltpu.VMEM((WINLEN, 2 * LANES), BF16),
            pltpu.VMEM((WINLEN, 2 * LANES), BF16),
            pltpu.VMEM((WINLEN, WINLEN), F32),
            pltpu.VMEM((WINLEN, WINLEN), F32),
            pltpu.VMEM((LANES, 5 * LANES), F32),
            pltpu.VMEM((WINLEN, 2 * LANES), F32),
        ],
        compiler_params=pltpu.CompilerParams(vmem_limit_bytes=48 * 2**20),
        name="attention_forward",
    )(
        queries, keys, values, ops["hot_two"], ops["key_x"], ops["key_y"], ops["met"], ops["band"],
        ops["rest_cols"], ops["rest_rows"], ops["mark_keys"], ops["mark_queries"],
    )


def attention_backward(queries, keys, values, grad_context, probs, ops):
    return pl.pallas_call(
        attention_backward_kernel,
        out_shape=(
            jax.ShapeDtypeStruct((D, WINLEN), BF16),
            jax.ShapeDtypeStruct((WINLEN, D), BF16),
            jax.ShapeDtypeStruct((WINLEN, D), BF16),
            jax.ShapeDtypeStruct((HEADS, 2, 64, LANES), F32),
            jax.ShapeDtypeStruct((HEADS, 1, WIDE), F32),
        ),
        scratch_shapes=[
            pltpu.VMEM((WINLEN, LANES), BF16),
            pltpu.VMEM((WINLEN, WINLEN), BF16),
            pltpu.VMEM((WINLEN, WINLEN), BF16),
            pltpu.VMEM((WINLEN, WINLEN), F32),
            pltpu.VMEM((WINLEN, WINLEN), BF16),
            pltpu.VMEM((LANES, 5 * LANES), F32),
            pltpu.VMEM((2, 3, WINLEN, LANES), F32),
            pltpu.VMEM((LANES, WINLEN), BF16),
        ],
        compiler_params=pltpu.CompilerParams(vmem_limit_bytes=48 * 2**20),
        name="attention_backward",
    )(
        queries, keys, values, grad_context, probs, ops["hot_two"], ops["rest_cols"],
        ops["rest_rows"],
    )


def table_grads(cells, diag):
    exact = lax.Precision.HIGHEST
    pairs = cells.reshape(PAIRS, 2, 2, 64, LANES)
    every = jnp.stack([pairs[:, 0, 0, :, 64:], pairs[:, 1, 0, :, :64]], axis=1).reshape(HEADS, 64, 64)
    less = cells[:, 1]
    less_x, less_y = less[:, :32, :32], less[:, 32:, 32:64]
    all_x, all_y = every[:, :32, :32], every[:, 32:, 32:]
    same = jnp.stack([all_x - less_x, all_y - less_y]).reshape(2 * HEADS, -1)
    below = jnp.stack([less_x, less_y]).reshape(2 * HEADS, -1)
    same_hot = jnp.asarray(HOT_SAME.transpose(1, 0, 2).reshape(-1, BUCKETS))
    less_hot = jnp.asarray(HOT_LESS.transpose(1, 0, 2).reshape(-1, BUCKETS))
    moved = jnp.dot(same, same_hot, precision=exact) + jnp.dot(below, less_hot, precision=exact)
    along = jnp.dot(diag.reshape(HEADS, WIDE), jnp.asarray(DIAG_HOT), precision=exact)
    return jnp.concatenate([along[None], moved.reshape(2, HEADS, BUCKETS)], axis=0)


COLUMNS = 4
CORES = 2
DEPTH = 4
USED = sum(math.prod(layout) for layout in layouts_list())
MATRICES = layouts_list()[:5]
MISC = sum(math.prod(layout) for layout in layouts_list()[5:])
MISC_ROWS = -(-MISC // (8 * LANES)) * 8


class Plan:
    def __init__(self, shard_len, carry=3 * LANES):
        self.rows = shard_len // LANES
        self.quarter = -(-self.rows // (16 * COLUMNS)) * 16
        self.padded = COLUMNS * self.quarter
        self.per_column = CORES * DEPTH * self.rows
        self.carry = carry
        self.staged = self.carry + self.per_column + 3 * LANES
        starts = []
        offset = 0
        for depth, width in MATRICES:
            starts.append(offset // LANES)
            offset += depth * width
        self.starts = starts
        self.misc_start = offset // LANES


def fits(mesh):
    return mesh.shape["dp"] == COLUMNS * CORES and mesh.shape["head"] == DEPTH


MESH = pl.DeviceIdType.MESH


class Place:
    def __init__(self):
        dp = lax.axis_index("dp")
        self.z = lax.axis_index("head")
        self.core = dp % CORES
        self.column = dp // CORES
        self.x = self.column % 2
        self.y = self.column // 2
        self.col_x = 2 * self.y + (1 - self.x)
        self.col_y = 2 * (1 - self.y) + self.x
        self.col_d = 2 * (1 - self.y) + (1 - self.x)
        self.peer_x = self.at(self.col_x, self.core, self.z)
        self.peer_y = self.at(self.col_y, self.core, self.z)
        self.peer_d = self.at(self.col_d, self.core, self.z)
        self.peer_core = self.at(self.column, 1 - self.core, self.z)
        self.far = [lax.rem(self.z + d, DEPTH) for d in range(1, DEPTH)]
        self.from_far = [lax.rem(self.z + DEPTH - d, DEPTH) for d in range(1, DEPTH)]
        self.peers_z = [self.at(self.column, self.core, f) for f in self.far]

    def at(self, column, core, z):
        return {"dp": column * CORES + core, "head": z}

    def greet(self):
        barrier = pltpu.get_barrier_semaphore()
        peers = [self.peer_x, self.peer_y, self.peer_d, self.peer_core] + self.peers_z
        for peer in peers:
            pl.semaphore_signal(barrier, inc=1, device_id=peer, device_id_type=MESH)
        pl.semaphore_wait(barrier, len(peers))


def remote(src, dst, send_sem, recv_sem, peer):
    return pltpu.make_async_remote_copy(
        src_ref=src, dst_ref=dst, send_sem=send_sem, recv_sem=recv_sem, device_id=peer,
        device_id_type=MESH,
    )


class Gathering:
    def __init__(self, place, flat, sems):
        self.place = place
        self.flat = flat
        self.sems = sems
        self.sent = []

    def send(self, src, dst, kind, index, peer):
        copy = remote(src, dst, self.sems[kind].at[0, index], self.sems[kind].at[1, index], peer)
        copy.start()
        self.sent.append(copy)

    def got(self, dst, kind, index):
        remote(
            dst, dst, self.sems[kind].at[0, index], self.sems[kind].at[1, index], self.place.peer_x
        ).wait_recv()

    def rows(self, h):
        half = self.flat.shape[-2] // 2
        return slice(h * half, (h + 1) * half)

    def spread(self, own, h):
        p = self.place
        rows = self.rows(h)
        for index, (column, peer) in enumerate(
            ((p.col_x, p.peer_x), (p.col_y, p.peer_y), (p.col_d, p.peer_d))
        ):
            self.send(
                own.at[column, rows], self.flat.at[p.column, p.core, p.z, column, rows], "spread",
                2 * index + h, peer,
            )
        self.flat[p.column, p.core, p.z, p.column, rows] = own[p.column, rows]

    def spread_done(self, h):
        p = self.place
        for index, column in enumerate((p.col_x, p.col_y, p.col_d)):
            self.got(self.flat.at[column, p.core, p.z, p.column, self.rows(h)], "spread", 2 * index + h)

    def along_z(self, k, h):
        p = self.place
        piece = self.flat.at[k, p.core, p.z, p.column, self.rows(h)]
        for d in range(DEPTH - 1):
            self.send(piece, piece, "z", 3 * (2 * k + h) + d, p.peers_z[d])

    def first(self, k, h):
        p = self.place
        n = 2 * k + h
        for d in range(DEPTH - 1):
            self.got(
                self.flat.at[k, p.core, p.from_far[d], p.column, self.rows(h)], "z", 3 * n + d
            )
        piece = self.flat.at[k, p.core, :, p.column, self.rows(h)]
        self.send(piece, piece, "one", 2 * n, p.peer_x)
        self.send(piece, piece, "one", 2 * n + 1, p.peer_y)
        self.send(piece, piece, "core", 5 * n, p.peer_core)

    def second(self, k, h):
        p = self.place
        n = 2 * k + h
        rows = self.rows(h)
        from_x = self.flat.at[k, p.core, :, p.col_x, rows]
        self.got(from_x, "one", 2 * n)
        part = self.flat.at[k, p.core, 0:2, p.col_x, rows]
        self.send(part, part, "two", 2 * n, p.peer_y)
        self.send(from_x, from_x, "core", 5 * n + 1, p.peer_core)
        from_y = self.flat.at[k, p.core, :, p.col_y, rows]
        self.got(from_y, "one", 2 * n + 1)
        part = self.flat.at[k, p.core, 2:4, p.col_y, rows]
        self.send(part, part, "two", 2 * n + 1, p.peer_x)
        self.send(from_y, from_y, "core", 5 * n + 2, p.peer_core)

    def third(self, k, h):
        p = self.place
        n = 2 * k + h
        for side in range(2):
            part = self.flat.at[k, p.core, 2 * side : 2 * side + 2, p.col_d, self.rows(h)]
            self.got(part, "two", 2 * n + side)
            self.send(part, part, "core", 5 * n + 3 + side, p.peer_core)

    def complete(self, k):
        p = self.place
        other = 1 - p.core
        for h in range(2):
            n = 2 * k + h
            rows = self.rows(h)
            for index, column in enumerate((p.column, p.col_x, p.col_y)):
                self.got(self.flat.at[k, other, :, column, rows], "core", 5 * n + index)
            for side in range(2):
                self.got(
                    self.flat.at[k, other, 2 * side : 2 * side + 2, p.col_d, rows], "core",
                    5 * n + 3 + side,
                )

    def finish(self):
        for copy in self.sent:
            copy.wait_send()


GATHER_SEMS = {"spread": 6, "z": 24, "one": 16, "two": 16, "core": 40}


def sem_shapes(counts):
    return [pltpu.SemaphoreType.DMA((2, count)) for count in counts.values()]


def stage_column(plan, flat, staged, k):
    def one(shard, carry):
        core, z = shard // DEPTH, shard % DEPTH
        for quarter in range(COLUMNS):
            base = plan.carry + shard * plan.rows + quarter * plan.quarter
            staged[pl.ds(pl.multiple_of(base, 8), plan.quarter), :] = flat[k, core, z, quarter].astype(F32)
        return carry

    lax.fori_loop(0, CORES * DEPTH, one, 0)


def keep_carry(plan, staged):
    end = plan.carry + plan.per_column
    staged[: plan.carry, :] = staged[end - plan.carry : end, :]


ROW_STEP = 48


def column_rows(plan, k, touching):
    low, high = k * plan.per_column, (k + 1) * plan.per_column
    taken = []
    for index, (depth, width) in enumerate(MATRICES):
        group = 16 * (width // LANES)
        from_low, from_high = low - plan.starts[index], high - plan.starts[index]
        begin = max(0, min(depth, from_low // group * 16))
        if touching:
            end = max(0, min(depth, -(-from_high // group) * 16))
        else:
            end = max(0, min(depth, from_high // group * 16))
        if end > begin:
            taken.append((index, begin, end))
    return taken


def staged_at(plan, k, row):
    return plan.carry + row - k * plan.per_column


def row_loops(rows):
    whole = rows // ROW_STEP
    loops = [(ROW_STEP, 0, whole)] if whole else []
    if rows % ROW_STEP:
        loops.append((16, whole * ROW_STEP, (rows % ROW_STEP) // 16))
    return loops


def form_matrices(plan, staged, matrices, k):
    for index, begin, end in column_rows(plan, k, False):
        blocks = MATRICES[index][1] // LANES
        base = staged_at(plan, k, plan.starts[index] + begin * blocks)
        assert 0 <= base
        target = matrices[index]
        for step_rows, first, count in row_loops(end - begin):

            def one(step, carry, step_rows=step_rows, first=first, blocks=blocks, base=base,
                    begin=begin, target=target):
                row = first + step * step_rows
                for block in range(blocks):
                    got = staged[pl.ds(base + row * blocks + block, step_rows, stride=blocks), :]
                    target[
                        pl.ds(pl.multiple_of(begin + row, 16), step_rows),
                        block * LANES : (block + 1) * LANES,
                    ] = got.astype(BF16)
                return carry

            lax.fori_loop(0, count, one, 0)


def adam_step(params, moment_one, moment_two, grads, flat_index):
    box_part = (flat_index >= 4 * D * D) & (flat_index < 5 * D * D)
    step_rate = jnp.where(box_part, base_rate * layer_decay**12, base_rate * layer_decay)
    decay_mask = jnp.where(flat_index < 5 * D * D + 2 * D * FF, decay_weight, 0.0)
    moment_one = beta_one * moment_one + (1.0 - beta_one) * grads
    moment_two = beta_two * moment_two + (1.0 - beta_two) * grads * grads
    first_hat = moment_one / (1.0 - beta_one**adam_count)
    second_hat = moment_two / (1.0 - beta_two**adam_count)
    update = first_hat / (jnp.sqrt(second_hat) + adam_eps) + decay_mask * params
    return (-step_rate * update, moment_one)


VEC = {}
_at = 0
for _name, _rows in (
    ("q_bias", 6), ("v_bias", 6), ("out_bias", 6), ("gain_one", 6), ("shift_one", 6), ("in_bias", 24),
    ("back_bias", 6), ("gain_two", 6), ("shift_two", 6), ("tables", 9),
):
    VEC[_name] = _at * LANES
    _at += _rows
VEC_ROWS = _at
NOTE_ROWS = 96
NBLOCK = 2 * LANES


def note_place(plan):
    row = plan.misc_start - (CORES * DEPTH * COLUMNS - 1) * plan.rows
    quarter, row = row // plan.quarter, row % plan.quarter
    first = row // 16 * 16
    assert first + NOTE_ROWS <= plan.quarter and row - first + VEC_ROWS <= NOTE_ROWS
    return quarter, first, row - first


def spread_notes(place, own, notes, sems, plan):
    quarter, first, _ = note_place(plan)
    source = own.at[quarter, first : first + NOTE_ROWS]
    home = (place.column == COLUMNS - 1) & (place.core == CORES - 1)
    root = home & (place.z == DEPTH - 1)

    def copy(src, index, peer):
        return remote(src, notes, sems.at[0, index], sems.at[1, 0], peer)

    def arrived():
        copy(notes, 0, place.peer_core).wait_recv()

    @pl.when(root)
    def _():
        notes[...] = own[quarter, first : first + NOTE_ROWS]
        for index, peer in enumerate(place.peers_z):
            copy(source, index, peer).start()

    @pl.when(home & (place.z != DEPTH - 1))
    def _():
        arrived()

    @pl.when(home)
    def _():
        for index, peer in enumerate((place.peer_x, place.peer_y, place.peer_d)):
            copy(notes, 3 + index, peer).start()

    @pl.when((place.core == CORES - 1) & (place.column != COLUMNS - 1))
    def _():
        arrived()

    @pl.when(place.core == CORES - 1)
    def _():
        copy(notes, 6, place.peer_core).start()

    @pl.when(place.core != CORES - 1)
    def _():
        arrived()

    def finish():
        @pl.when(root)
        def _():
            for index, peer in enumerate(place.peers_z):
                copy(source, index, peer).wait_send()

        @pl.when(home)
        def _():
            for index, peer in enumerate((place.peer_x, place.peer_y, place.peer_d)):
                copy(notes, 3 + index, peer).wait_send()

        @pl.when(place.core == CORES - 1)
        def _():
            copy(notes, 6, place.peer_core).wait_send()

    return finish


def turns_table():
    count_freq = D // 8
    freq = np.exp(np.arange(count_freq) * (-math.log(1000.0) / count_freq)) / (2 * math.pi)
    per = np.concatenate([freq, freq])
    phase = np.concatenate([np.zeros(count_freq), np.full(count_freq, 0.25)])
    return np.stack([np.tile(per, 4), np.tile(phase, 4)]).astype(np.float32)


def sin_turns(t):
    t = t - jnp.floor(t + 0.5)
    a = jnp.abs(t)
    m = jnp.minimum(a, 0.5 - a) * (2 * math.pi)
    u = m * m
    poly = -1.0 / 39916800.0
    for term in (1.0 / 362880.0, -1.0 / 5040.0, 1.0 / 120.0, -1.0 / 6.0, 1.0):
        poly = poly * u + term
    s = m * poly
    return jnp.where(t < 0, -s, s)


def token_columns(boxes, lengths, window):
    coords = boxes[window].astype(F32)
    place = lax.broadcasted_iota(jnp.int32, (1, WINLEN), 1)
    doc = jnp.zeros((1, WINLEN), F32)
    anchor = jnp.zeros_like(coords)
    begin = 0
    for d in range(4):
        end = begin + lengths[window, d]
        mine = jnp.where((place >= begin) & (place < end), 1.0, 0.0)
        value = jnp.sum(coords * jnp.where(place == begin, 1.0, 0.0), axis=1, keepdims=True)
        anchor = anchor + value * mine
        doc = doc + mine * float(d)
        begin = end
    anchor = jnp.concatenate([anchor[0:2], anchor[0:2]], axis=0)
    relative = coords - anchor
    centre = jnp.floor((coords[0:2] + coords[2:4]) * 0.5)
    cell = jnp.floor(centre * (1.0 / coord_cell))
    rest = centre - cell * coord_cell
    rows = jnp.concatenate(
        [relative, cell, rest, doc, jnp.zeros((LANES - 9, WINLEN), F32)], axis=0
    )
    return rest, rows.T


def form_features(columns, turns_ref, features):
    lane = lax.broadcasted_iota(jnp.int32, (1, LANES), 1)
    for block in range(D // LANES):
        lanes = slice(block * LANES, (block + 1) * LANES)
        low, high = block * LANES // (D // 4), ((block + 1) * LANES - 1) // (D // 4)
        value = columns[:, low : low + 1]
        if high != low:
            value = jnp.where(
                lane + block * LANES < high * (D // 4), value, columns[:, high : high + 1]
            )
        t = value * turns_ref[0:1, lanes] + turns_ref[1:2, lanes]
        features[:, lanes] = sin_turns(t).astype(BF16)


def form_hots(columns, hot_ref, keyx_ref, keyy_ref, mkey, mquery):
    lane = lax.broadcasted_iota(jnp.int32, (1, LANES), 1)
    part = lane // BUCKETS
    cell = (lane % BUCKETS).astype(F32)
    is_x = jnp.where(columns[:, 4:5] == cell, 1.0, 0.0)
    is_y = jnp.where(columns[:, 5:6] == cell, 1.0, 0.0)
    hot_ref[...] = jnp.where(part % 2 == 0, is_x, is_y).astype(BF16)
    sign = jnp.where(part % 2 == 0, 1.0, -1.0)
    for odd in range(2):
        here = jnp.where(part // 2 == odd, sign, 0.0)
        keyx_ref[odd] = (is_x * here).astype(BF16)
        keyy_ref[odd] = (is_y * here).astype(BF16)
    doc = jnp.where(columns[:, 8:9] == lane.astype(F32), 1.0, 0.0)
    mkey[:, LANES:] = doc.astype(BF16)
    mquery[:, LANES:] = (jnp.where(lane < 4, 1.0 - doc, 0.0) * masked_score).astype(BF16)


def form_tables(tables, bands, tilted):
    row = lax.broadcasted_iota(jnp.int32, (LANES, 1), 0)
    half = BUCKETS // 2
    sub = lax.broadcasted_iota(jnp.int32, (8, LANES), 0)
    sub_wide = lax.broadcasted_iota(jnp.int32, (8, WIDE), 0)
    place = lax.broadcasted_iota(jnp.int32, (1, WIDE), 1)
    wanted = jnp.where(place < 5 * LANES, jnp.clip(place - 2 * LANES, -half, half - 1) + half, 0)
    lane = lax.broadcasted_iota(jnp.int32, (1, LANES), 1)
    turned = jnp.clip(64 - lane, -half, half - 1) + half
    for m in range(4):
        hot_band = jnp.where(row == wanted + m * BUCKETS, 1.0, 0.0).astype(BF16)
        got = matmul(tables, hot_band)
        for n in range(3):
            x = jnp.broadcast_to(got[n : n + 1, :], (8, WIDE))
            for bit in (1, 2, 4):
                x = jnp.where((sub_wide & bit) != 0, pltpu.roll(x, bit, 1), x)
            bands[4 * n + m] = x
        hot_turn = jnp.where(row == turned + m * BUCKETS, 1.0, 0.0).astype(BF16)
        got = matmul(tables, hot_turn)
        for t in (1, 2):
            for n in range(3):
                x = jnp.broadcast_to(got[3 * t + n : 3 * t + n + 1, :], (8, LANES))
                for bit in (1, 2, 4):
                    x = jnp.where((sub & bit) != 0, pltpu.roll(x, bit, 1), x)
                for group in range(BUCKETS // 8):
                    y = x if group == 0 else pltpu.roll(x, 8 * group, 1)
                    tilted[(t - 1) * HEADS + 4 * n + m, 8 * group : 8 * group + 8, :] = y


def pair_rows(tilted, pair):
    lane = lax.broadcasted_iota(jnp.int32, (1, LANES), 1)
    part = lane // BUCKETS
    x0, x1 = tilted[2 * pair], tilted[2 * pair + 1]
    y0, y1 = tilted[HEADS + 2 * pair], tilted[HEADS + 2 * pair + 1]

    def same(value, to):
        return value if to == 64 else pltpu.roll(value, (to - 64) % LANES, 1)

    def less(value, to):
        return pltpu.roll(value, (to - 65) % LANES, 1)

    zero = jnp.zeros_like(x0)
    base_x = jnp.where(part == 0, same(x1, 0), jnp.where(part == 2, same(x0, 64), zero))
    base_y = jnp.where(part == 1, same(y1, 32), jnp.where(part == 3, same(y0, 96), zero))

    def steps(even, odd):
        return jnp.where(
            part < 2,
            jnp.where(part == 0, less(even, 0), same(even, 32)),
            jnp.where(part == 2, less(odd, 64), same(odd, 96)),
        )

    rows = [
        jnp.concatenate([base_x, base_y], axis=0),
        jnp.concatenate([steps(x0, x1), zero], axis=0),
        jnp.concatenate([zero, steps(y0, y1)], axis=0),
    ]
    return jnp.concatenate(rows, axis=1).astype(BF16)


def gelu_and_slope(z):
    a = jnp.abs(z)
    t = 1.0 / (1.0 + (0.3275911 / math.sqrt(2.0)) * a)
    poly = 1.061405429 * 0.5
    for term in (-1.453152027, 1.421413741, -0.284496736, 0.254829592):
        poly = poly * t + 0.5 * term
    e = jnp.exp(-0.5 * z * z)
    tail = poly * t * e
    cdf = jnp.where(z < 0, tail, 1.0 - tail)
    return z * cdf, cdf + z * (e * (1.0 / math.sqrt(2.0 * math.pi)))


def forward_kernel(plan, params_in, hidden_in, cot_in, boxes, lengths, turns, *refs):
    (w_qkv_out, w_out_out, w_in_out, w_back_out, features_out, low_out, q_out, k_out, v_out, probs_out,
     context_out, hat_out, normed_out, vec_out, rstd_out, cot_ref, hot_out, rest_out, share_out) = refs[:19]
    refs = refs[19:]
    (flat, staged, own, w_qkv, w_out, w_box, w_in, w_back, notes, features, hidden, start, start_low, q_ref,
     k_ref, v_ref, hot_ref, key_x, key_y, bands, tilted, wides, scores, context_t, pair_t, hat, narrow,
     square, vec) = refs[:29]
    note_sems, swap_sems, copy_sems, probs_sems = refs[29:33]

    def lend(buffer, slot, lanes):
        return buffer.at[:, slot : slot + lanes]

    less_x, less_y = lend(square, 0, WINLEN), lend(square, WINLEN, WINLEN)
    probs = [lend(square, 2 * WINLEN, WINLEN), lend(square, 3 * WINLEN, WINLEN)]
    kaugs = [lend(narrow, 0, 2 * LANES), lend(narrow, 2 * LANES, 2 * LANES)]
    qaugs = [lend(narrow, 4 * LANES, 2 * LANES), lend(narrow, 6 * LANES, 2 * LANES)]
    met = lend(narrow, 8 * LANES, 3 * LANES)
    place = Place()
    normed_low = hidden
    context = features
    gathering = Gathering(place, flat, dict(zip(GATHER_SEMS, refs[33:])))
    matrices = (w_qkv, w_out, w_box, w_in, w_back)
    written = []

    def write_out(src, dst):
        copy = pltpu.make_async_copy(src, dst, copy_sems.at[len(written)])
        copy.start()
        written.append(copy)

    fetch = pltpu.make_async_copy(params_in, staged.at[: plan.rows], probs_sems.at[0])
    fetch.start()
    place.greet()
    fetch.wait()
    for quarter_at in range(COLUMNS):
        begin = quarter_at * plan.quarter
        own[quarter_at] = staged[begin : begin + plan.quarter, :].astype(BF16)
    gathering.spread(own, 0)
    gathering.spread(own, 1)

    quarter = WINLEN // DEPTH

    def exchange(source, target, kind):
        rows = pl.ds(pl.multiple_of(place.z * quarter, quarter), quarter)
        for d in range(DEPTH - 1):
            gathering_send(source.at[place.far[d]], target.at[rows], kind, d, place.peers_z[d])

    def gathering_send(src, dst, kind, d, peer):
        copy = remote(src, dst, swap_sems.at[kind, 0, d], swap_sems.at[kind, 1, d], peer)
        copy.start()
        gathering.sent.append(copy)

    def exchanged(target, kind):
        for d in range(DEPTH - 1):
            rows = pl.ds(pl.multiple_of(place.from_far[d] * quarter, quarter), quarter)
            remote(
                target.at[rows], target.at[rows], swap_sems.at[kind, 0, d], swap_sems.at[kind, 1, d],
                place.peer_x,
            ).wait_recv()

    finish_notes = spread_notes(place, own, notes, note_sems, plan)
    own_rows = pl.ds(pl.multiple_of(place.z * quarter, quarter), quarter)
    own_hidden = pltpu.make_async_copy(
        hidden_in.at[place.z], hidden.at[own_rows], swap_sems.at[0, 0, DEPTH - 1]
    )
    own_hidden.start()
    own_cot = pltpu.make_async_copy(
        cot_in.at[place.z], cot_ref.at[own_rows], swap_sems.at[1, 0, DEPTH - 1]
    )
    own_cot.start()
    gathering.spread_done(0)
    gathering.along_z(0, 0)
    gathering.spread_done(1)
    gathering.along_z(0, 1)

    rest, columns = token_columns(boxes, lengths, place.z)
    for part in range(BLOCKS):
        rows = slice(part * LANES, (part + 1) * LANES)
        for axis, less in ((0, less_x), (1, less_y)):
            less[rows, :] = jnp.where(
                rest[axis : axis + 1, :] < columns[rows, 6 + axis : 7 + axis], 1.0, 0.0
            ).astype(BF16)
    rest_out[...] = rest
    form_hots(columns, hot_ref, key_x, key_y, kaugs[0], qaugs[0])
    kaugs[1][:, LANES:] = kaugs[0][:, LANES:]
    qaugs[1][:, LANES:] = qaugs[0][:, LANES:]
    hot_out[...] = hot_ref[...]
    gathering.first(0, 0)
    gathering.along_z(1, 0)
    gathering.first(0, 1)
    gathering.along_z(1, 1)
    form_features(columns, turns, features)
    for n in range(D // LANES):
        rows = slice(n * LANES, (n + 1) * LANES)
        context_t[rows, :] = features[:, rows].T
    write_out(context_t, features_out)
    gathering.first(1, 0)
    exchange(hidden_in, hidden, 0)
    gathering.second(0, 0)
    gathering.first(1, 1)
    gathering.second(0, 1)
    _, _, note_row = note_place(plan)
    for row in range(VEC_ROWS):
        at = note_row + row
        vec[0:1, row * LANES : (row + 1) * LANES] = notes[at // 16 * 16 : at // 16 * 16 + 16, :].astype(
            F32
        )[at % 16 : at % 16 + 1, :]
    vec_out[...] = vec[...]
    table_row = note_row + VEC["tables"] // LANES
    assert table_row % 16 == 0
    form_tables(notes[table_row : table_row + 16, :], bands, tilted)

    gathering.third(0, 0)
    gathering.second(1, 0)
    gathering.third(0, 1)
    gathering.second(1, 1)
    gathering.complete(0)
    stage_column(plan, flat, staged, 0)
    exchanged(hidden, 0)
    gathering.along_z(2, 0)
    gathering.along_z(2, 1)
    form_matrices(plan, staged, matrices, 0)
    keep_carry(plan, staged)
    gathering.third(1, 0)
    gathering.third(1, 1)
    gathering.complete(1)
    stage_column(plan, flat, staged, 1)
    form_matrices(plan, staged, matrices, 1)
    keep_carry(plan, staged)
    write_out(w_qkv, w_qkv_out)
    write_out(w_out, w_out_out)

    own_hidden.wait()
    for n in range(D // NBLOCK):
        lanes = slice(n * NBLOCK, (n + 1) * NBLOCK)
        value = hidden[:, lanes].astype(F32) + matmul(features[...], w_box[:, lanes])
        start[:, lanes] = value
        start_low[:, lanes] = value.astype(BF16)
    write_out(start_low, low_out)
    written[0].wait()

    def project(n, carry):
        at = pl.multiple_of(n * NBLOCK, NBLOCK)
        lanes = pl.ds(at, NBLOCK)
        low = start_low[...]
        bias = vec[0:1, pl.ds(pl.multiple_of(VEC["q_bias"] + at, LANES), NBLOCK)]
        got = matmul(low, w_qkv[:, lanes]) + bias
        q_ref[:, lanes] = (got.astype(BF16).astype(F32) * HEAD_DIM ** (-0.5)).astype(BF16)
        k_ref[:, lanes] = matmul(low, w_qkv[:, pl.ds(pl.multiple_of(at + D, LANES), NBLOCK)]).astype(BF16)
        bias = vec[0:1, pl.ds(pl.multiple_of(VEC["v_bias"] + at, LANES), NBLOCK)]
        got = matmul(low, w_qkv[:, pl.ds(pl.multiple_of(at + 2 * D, LANES), NBLOCK)]) + bias
        v_ref[:, lanes] = got.astype(BF16)
        return carry

    lax.fori_loop(0, D // NBLOCK, project, 0)
    write_out(q_ref, q_out)
    write_out(k_ref, k_out)
    write_out(v_ref, v_out)
    gathering.first(2, 0)
    gathering.along_z(3, 0)
    gathering.first(2, 1)
    gathering.along_z(3, 1)

    low, high = half_masks()
    half = 2 * LANES

    def probs_copy(head, odd):
        return pltpu.make_async_copy(probs[odd], probs_out.at[head], probs_sems.at[odd])

    def one_pair(pair, carry):
        at = pl.multiple_of(pair * LANES, LANES)
        lanes = pl.ds(at, LANES)
        values_t = v_ref[:, lanes].T
        met[...] = matmul(hot_ref[:, :64], pair_rows(tilted, pair)).astype(BF16)
        for odd in range(2):
            mine, other = (low, high) if odd == 0 else (high, low)
            kaugs[odd][:, :LANES] = k_ref[:, lanes] * mine + hot_ref[...] * other
            qaugs[odd][:, :LANES] = q_ref[:, lanes] * mine + met[:, :LANES] * other
            skew_groups(bands[2 * pair + odd], wides.at[odd])

            @pl.when(pair > 0)
            def _():
                probs_copy(2 * pair + odd, odd).wait()

        for side in range(2):
            cols = slice(side * half, (side + 1) * half)
            tops = []
            for odd in range(2):
                whole = times_transposed(kaugs[odd][...], qaugs[odd][cols, :])
                steps_x = times_transposed(key_x[odd], met[cols, LANES : 2 * LANES])
                steps_y = times_transposed(key_y[odd], met[cols, 2 * LANES :])
                top = None
                for part in range(BLOCKS):
                    rows = slice(part * LANES, (part + 1) * LANES)
                    bias = []
                    for block in range(2 * side, 2 * side + 2):
                        step = max(-2, min(2, block - part)) + 2
                        bias.append(wides[odd, :, step * LANES : (step + 1) * LANES])
                    s = whole[rows] + jnp.concatenate(bias, axis=1)
                    s = s + steps_x[rows] * less_x[rows, cols].astype(F32)
                    s = s + steps_y[rows] * less_y[rows, cols].astype(F32)
                    scores[odd, rows, :] = s
                    best = jnp.max(s.reshape(LANES // 8, 8, half), axis=0)
                    top = best if top is None else jnp.maximum(top, best)
                tops.append(jnp.max(top, axis=0, keepdims=True))
            for odd in range(2):
                total = None
                for part in range(BLOCKS):
                    rows = slice(part * LANES, (part + 1) * LANES)
                    e = jnp.exp(scores[odd, rows, :] - tops[odd])
                    probs[odd][rows, cols] = e.astype(BF16)
                    add = jnp.sum(e.reshape(LANES // 8, 8, half), axis=0)
                    total = add if total is None else total + add
                share = 1.0 / jnp.sum(total, axis=0, keepdims=True)
                share_out[2 * pair + odd, :, cols] = share
                got = matmul(values_t[odd * HEAD_DIM : (odd + 1) * HEAD_DIM, :], probs[odd][:, cols])
                pair_t[odd * HEAD_DIM : (odd + 1) * HEAD_DIM, cols] = got * share
        for odd in range(2):
            probs_copy(2 * pair + odd, odd).start()
        both = pair_t[...]
        context_t[lanes, :] = both.astype(BF16)
        context[:, lanes] = both.T.astype(BF16)
        return carry

    lax.fori_loop(0, 2, one_pair, 0)
    gathering.second(2, 0)
    gathering.first(3, 0)
    gathering.second(2, 1)
    gathering.first(3, 1)
    exchange(cot_in, cot_ref, 1)
    lax.fori_loop(2, 4, one_pair, 0)
    for h in range(2):
        gathering.third(2, h)
        gathering.second(3, h)
    gathering.complete(2)
    stage_column(plan, flat, staged, 2)
    form_matrices(plan, staged, matrices, 2)
    keep_carry(plan, staged)
    write_out(w_in, w_in_out)
    lax.fori_loop(4, PAIRS, one_pair, 0)
    write_out(context_t, context_out)
    for h in range(2):
        gathering.third(3, h)

    def vector(name):
        return vec[0:1, VEC[name] : VEC[name] + D]

    for n in range(D // NBLOCK):
        lanes = slice(n * NBLOCK, (n + 1) * NBLOCK)
        bias = vec[0:1, VEC["out_bias"] + n * NBLOCK : VEC["out_bias"] + (n + 1) * NBLOCK]
        start[:, lanes] = start[:, lanes] + matmul(context[...], w_out[:, lanes]) + bias

    step_rows = 64

    def norm_first(n, carry):
        rows = pl.ds(pl.multiple_of(n * step_rows, step_rows), step_rows)
        x = start[rows, :]
        centred = x - jnp.mean(x, axis=1, keepdims=True)
        rstd = lax.rsqrt(jnp.mean(centred * centred, axis=1, keepdims=True) + norm_eps)
        xhat = centred * rstd
        hat[rows, :] = xhat
        rstd_out[rows, :] = jnp.broadcast_to(rstd, (step_rows, LANES))
        normed = xhat * vector("gain_one") + vector("shift_one")
        start[rows, :] = normed
        normed_low[rows, :] = normed.astype(BF16)
        return carry

    lax.fori_loop(0, WINLEN // step_rows, norm_first, 0)
    write_out(hat, hat_out)
    write_out(normed_low, normed_out)

    gathering.complete(3)
    stage_column(plan, flat, staged, 3)
    form_matrices(plan, staged, matrices, 3)
    write_out(w_back, w_back_out)
    for odd in range(2):
        probs_copy(0, odd).wait()
    exchanged(cot_ref, 1)
    own_cot.wait()
    for copy in written[1:]:
        copy.wait()
    finish_notes()
    gathering.finish()


def forward_pass(plan, params, hidden_in, cotangent, boxes, lengths):
    anywhere = pl.BlockSpec(memory_space=pl.ANY)
    vmem = pl.BlockSpec(memory_space=pltpu.VMEM)
    token = (WINLEN, D)

    def hbm(shape, dtype=BF16):
        return jax.ShapeDtypeStruct(shape, dtype), anywhere

    def near(shape, dtype=F32):
        return jax.ShapeDtypeStruct(shape, dtype), vmem

    outs = [
        hbm(MATRICES[0]), hbm(MATRICES[1]), hbm(MATRICES[3]), hbm(MATRICES[4]), hbm((D, WINLEN)), hbm(token),
        hbm(token), hbm(token), hbm(token), hbm((HEADS, WINLEN, WINLEN)), hbm((D, WINLEN)),
        hbm(token, F32), hbm(token), near((1, VEC_ROWS * LANES)), near((WINLEN, LANES)),
        near(token, BF16), near((WINLEN, LANES), BF16), near((2, WINLEN)),
        near((HEADS, 1, WINLEN)),
    ]
    scratch = [
        pltpu.VMEM((COLUMNS, CORES, DEPTH, COLUMNS, plan.quarter, LANES), BF16),
        pltpu.VMEM((plan.staged, LANES), F32),
        pltpu.VMEM((COLUMNS, plan.quarter, LANES), BF16),
    ]
    scratch += [pltpu.VMEM(layout, BF16) for layout in MATRICES]
    scratch += [
        pltpu.VMEM((NOTE_ROWS, LANES), BF16),
        pltpu.VMEM(token, BF16),
        pltpu.VMEM(token, BF16),
        pltpu.VMEM(token, F32),
        pltpu.VMEM(token, BF16),
        pltpu.VMEM(token, BF16),
        pltpu.VMEM(token, BF16),
        pltpu.VMEM(token, BF16),
        pltpu.VMEM((WINLEN, LANES), BF16),
        pltpu.VMEM((2, WINLEN, LANES), BF16),
        pltpu.VMEM((2, WINLEN, LANES), BF16),
        pltpu.VMEM((HEADS, 8, WIDE), F32),
        pltpu.VMEM((2 * HEADS, BUCKETS, LANES), F32),
        pltpu.VMEM((2, LANES, 5 * LANES), F32),
        pltpu.VMEM((2, WINLEN, 2 * LANES), F32),
        pltpu.VMEM((D, WINLEN), BF16),
        pltpu.VMEM((LANES, WINLEN), F32),
        pltpu.VMEM(token, F32),
        pltpu.VMEM((WINLEN, 11 * LANES), BF16),
        pltpu.VMEM((WINLEN, 4 * WINLEN), BF16),
        pltpu.VMEM((1, VEC_ROWS * LANES), F32),
        pltpu.SemaphoreType.DMA((2, 7)),
        pltpu.SemaphoreType.DMA((2, 2, DEPTH)),
        pltpu.SemaphoreType.DMA((16,)),
        pltpu.SemaphoreType.DMA((2,)),
    ]
    return pl.pallas_call(
        functools.partial(forward_kernel, plan),
        out_shape=[shape for shape, _ in outs],
        in_specs=[anywhere] * 3 + [vmem, pl.BlockSpec(memory_space=pltpu.SMEM), vmem],
        out_specs=[spec for _, spec in outs],
        scratch_shapes=scratch + sem_shapes(GATHER_SEMS),
        compiler_params=pltpu.CompilerParams(
            collective_id=0, has_side_effects=True, vmem_limit_bytes=62 * 2**20
        ),
        name="forward_pass",
    )(params, hidden_in, cotangent, boxes, lengths, jnp.asarray(turns_table()))


def token_info(doc_lengths, box_coords):
    places = jnp.arange(WINLEN, dtype=jnp.int32)
    first = places == 0
    doc = jnp.zeros((WINLEN,), jnp.int32)
    end = 0
    for d in range(3):
        end = end + doc_lengths[d]
        doc = doc + (places >= end).astype(jnp.int32)
        first = first | (places == end)
    rows = [box_coords[:, c] for c in range(4)] + [doc, first.astype(jnp.int32)]
    return jnp.stack(rows + [jnp.zeros_like(doc)] * 2).astype(F32)


class Reducing:
    def __init__(self, place, flat, swapped, one, two, deep, piece, result, sems, free):
        self.place = place
        self.flat = flat
        self.swapped = swapped
        self.one = one
        self.two = two
        self.deep = deep
        self.piece = piece
        self.result = result
        self.sems = sems
        self.free = free
        self.sent = {k: [] for k in range(COLUMNS)}

    def send(self, k, src, dst, kind, index, peer):
        copy = remote(src, dst, self.sems[kind].at[0, index], self.sems[kind].at[1, index], peer)
        copy.start()
        self.sent[k].append(copy)

    got = Gathering.got

    def settle(self, k):
        for copy in self.sent.pop(k):
            copy.wait_send()

    rows = Gathering.rows

    def swap(self, k, h):
        p = self.place
        slot = k % 2
        if k < 2 and h == 0:
            pl.semaphore_wait(self.free.at[slot], 1)
        self.send(
            k, self.flat.at[slot, 1 - p.core, :, :, self.rows(h)],
            self.swapped.at[slot, :, :, self.rows(h)], "core", 2 * k + h, p.peer_core,
        )

    def first(self, k, h):
        p = self.place
        slot = k % 2
        n, rows = 2 * k + h, self.rows(h)
        self.got(self.swapped.at[slot, :, :, rows], "core", n)

        def one(step, carry):
            z, quarter = step // COLUMNS, step % COLUMNS
            total = self.flat[slot, p.core, z, quarter, rows].astype(F32)
            total = total + self.swapped[slot, z, quarter, rows].astype(F32)
            self.flat[slot, p.core, z, quarter, rows] = total.astype(BF16)
            return carry

        lax.fori_loop(0, DEPTH * COLUMNS, one, 0)
        flat = self.flat
        for side, peer in ((0, p.peer_y), (1, p.peer_x)):
            self.send(
                k, flat.at[slot, p.core, 2 * side : 2 * side + 2, p.col_d, rows],
                self.one.at[k, side, :, rows], "one", 2 * n + side, peer,
            )
        if k >= 2 and h == 1:
            pl.semaphore_signal(
                self.free.at[slot], inc=1, device_id=p.peer_core, device_id_type=MESH
            )

    def second(self, k, h):
        p = self.place
        slot = k % 2
        n, rows = 2 * k + h, self.rows(h)
        for side, column in ((0, p.col_x), (1, p.col_y)):
            self.got(self.one.at[k, side, :, rows], "one", 2 * n + side)

            def one(step, carry, side=side, column=column):
                z = 2 * side + step
                total = self.flat[slot, p.core, z, column, rows].astype(F32)
                total = total + self.one[k, side, step, rows].astype(F32)
                self.flat[slot, p.core, z, column, rows] = total.astype(BF16)
                return carry

            lax.fori_loop(0, 2, one, 0)
        for side, column, peer in ((0, p.col_x, p.peer_x), (1, p.col_y, p.peer_y)):
            self.send(
                k, self.flat.at[slot, p.core, :, column, rows], self.two.at[k, side, :, rows], "two",
                2 * n + side, peer,
            )

    def third(self, k, h):
        p = self.place
        slot = k % 2
        n, rows = 2 * k + h, self.rows(h)
        for side in range(2):
            self.got(self.two.at[k, side, :, rows], "two", 2 * n + side)

        def one(z, carry):
            total = self.flat[slot, p.core, z, p.column, rows].astype(F32)
            total = total + self.two[k, 0, z, rows].astype(F32) + self.two[k, 1, z, rows].astype(F32)
            self.flat[slot, p.core, z, p.column, rows] = total.astype(BF16)
            return carry

        lax.fori_loop(0, DEPTH, one, 0)
        for d in range(DEPTH - 1):
            self.send(
                k, self.flat.at[slot, p.core, p.far[d], p.column, rows], self.deep.at[k, d, rows], "z",
                3 * n + d, p.peers_z[d],
            )

    def fourth(self, k, h):
        p = self.place
        n, rows = 2 * k + h, self.rows(h)
        for d in range(DEPTH - 1):
            self.got(self.deep.at[k, d, rows], "z", 3 * n + d)
        total = self.flat[k % 2, p.core, p.z, p.column, rows].astype(F32)
        for d in range(DEPTH - 1):
            total = total + self.deep[k, d, rows].astype(F32)
        self.piece[k, rows] = total.astype(BF16)

    def giving(self, k, h):
        p = self.place
        sems = self.sems["spread"]
        return remote(
            self.piece.at[k, self.rows(h)], self.result.at[p.column, self.rows(h)],
            sems.at[0, 2 * k + h], sems.at[1, 2 * p.column + h], p.at(k, p.core, p.z),
        )

    def give(self, k, h):
        @pl.when(self.place.column != k)
        def _():
            self.giving(k, h).start()

    def given(self, k, h):
        @pl.when(self.place.column != k)
        def _():
            self.giving(k, h).wait_send()

    def receive(self, out):
        p = self.place
        out[p.column] = self.piece[p.column].astype(F32)
        for column in (p.col_x, p.col_y, p.col_d):
            for h in range(2):
                self.got(self.result.at[column, self.rows(h)], "spread", 2 * column + h)
            out[column] = self.result[column].astype(F32)


REDUCE_SEMS = {"spread": 8, "z": 24, "one": 16, "two": 16, "core": 8}


def unstage_column(plan, flat, staged, k):
    def one(step, carry):
        shard, quarter = step // COLUMNS, step % COLUMNS
        base = plan.carry + shard * plan.rows + quarter * plan.quarter
        piece = staged[pl.ds(pl.multiple_of(base, 8), plan.quarter), :]
        flat[k % 2, shard // DEPTH, shard % DEPTH, quarter] = piece.astype(BF16)
        return carry

    lax.fori_loop(0, CORES * DEPTH * COLUMNS, one, 0)


class Notes:
    def __init__(self, place, notes, slots, sems):
        self.place, self.notes, self.slots, self.sems = place, notes, slots, sems
        p = place
        self.home = (p.column == COLUMNS - 1) & (p.core == CORES - 1)
        self.root = self.home & (p.z == DEPTH - 1)

    def copy(self, slot, peer):
        return remote(
            self.notes, self.slots.at[slot], self.sems.at[0, 0], self.sems.at[1, slot], peer
        )

    def take(self, slot):
        self.copy(slot, self.place.peer_core).wait_recv()
        self.notes[...] = self.notes[...] + self.slots[slot]

    def start(self):
        p = self.place

        @pl.when(p.core != CORES - 1)
        def _():
            self.copy(0, p.peer_core).start()

    def rise(self):
        p = self.place

        @pl.when(p.core == CORES - 1)
        def _():
            self.take(0)

        @pl.when((p.core == CORES - 1) & (p.column != COLUMNS - 1))
        def _():
            self.copy(1 + p.column, p.at(COLUMNS - 1, p.core, p.z)).start()

    def end(self):
        p = self.place

        @pl.when(self.home)
        def _():
            for slot in range(1, 4):
                self.take(slot)

        @pl.when(self.home & (p.z != DEPTH - 1))
        def _():
            self.copy(4 + p.z, p.at(p.column, p.core, DEPTH - 1)).start()

        @pl.when(self.root)
        def _():
            for slot in range(4, 7):
                self.take(slot)

        @pl.when(jnp.logical_not(self.root))
        def _():
            self.copy(0, p.peer_core).wait_send()


def cell_sums(whole, less):
    lane = lax.broadcasted_iota(jnp.int32, (1, LANES), 1)
    sub = lax.broadcasted_iota(jnp.int32, (8, LANES), 0)
    sums = []
    for axis in range(2):
        rows = slice(axis * BUCKETS, (axis + 1) * BUCKETS)
        every = pltpu.roll(whole[rows], (BUCKETS - axis * BUCKETS) % LANES, 1)
        below = pltpu.roll(less[rows], (BUCKETS - axis * BUCKETS) % LANES, 1)
        inside = (lane >= BUCKETS) & (lane < 2 * BUCKETS)
        every = jnp.where(inside, every, 0.0)
        below = jnp.where(inside, below, 0.0)
        x = every - below + pltpu.roll(below, LANES - 1, 1)
        total = None
        for group in range(BUCKETS // 8):
            y = x[8 * group : 8 * group + 8]
            y = y if group == 0 else pltpu.roll(y, LANES - 8 * group, 1)
            total = y if total is None else total + y
        for bit in (1, 2, 4):
            total = jnp.where((sub & bit) != 0, pltpu.roll(total, LANES - bit, 1), total)
        sums.append(jnp.sum(total, axis=0, keepdims=True))
    return sums


def exact_dot(a, b):
    return jnp.dot(a, b, preferred_element_type=F32, precision=lax.Precision.HIGHEST)


def bucket_rows(cell_ref, diag_ref):
    half = BUCKETS // 2
    column = lax.broadcasted_iota(jnp.int32, (1, LANES), 1)
    row = lax.broadcasted_iota(jnp.int32, (LANES, 1), 0)
    to = jnp.clip(row - BUCKETS, -half, half - 1) + half
    place = lax.broadcasted_iota(jnp.int32, (WIDE, 1), 0)
    along = place - LANES
    far = jnp.where(place < LANES, 0, jnp.where(place < 5 * LANES, 0, BUCKETS - 1))
    along = jnp.where(
        (place >= LANES) & (place < 4 * LANES),
        jnp.clip(along - LANES, -half, half - 1) + half,
        far,
    )
    first, rest = None, None
    zero = jnp.zeros((5, WIDE), F32)
    for m in range(4):
        hot_along = jnp.where(along + m * BUCKETS == column, 1.0, 0.0)
        got = exact_dot(
            jnp.concatenate([diag_ref[4 * n + m] for n in range(3)] + [zero], axis=0), hot_along
        )
        first = got if first is None else first + got
        hot_cell = jnp.where(to + m * BUCKETS == column, 1.0, 0.0)
        rows = [cell_ref[t * HEADS + 4 * n + m] for t in range(2) for n in range(3)]
        got = exact_dot(jnp.concatenate(rows + [zero[:2, :LANES]], axis=0), hot_cell)
        rest = got if rest is None else rest + got
    return jnp.concatenate([first[:3], rest[:6]], axis=0)


def backward_kernel(
    plan, w_back_in, w_in_in, w_out_in, w_qkv_in, normed_in, low_in, features_in,
    context_in, q_in, k_in, v_in, probs_in, hat_in, cot_in, rstd_ref, vec, hot_ref, rest_ref, share_ref,
    *refs,
):
    out, output_pos, hidden_pos, spill = refs[:4]
    (flat, staged, swapped, one_buf, two_buf, deep, piece, result, active, slope, w_back, w_in, w_out,
     turned, context_t, q_ref, k_ref, v_ref, hat, second, branch, dctx, probs, less_x,
     less_y, scores_odd, bands, hot_t, pair_t, scaled, share_cols, vecg, cell_rows, diag_rows, notes, slots,
     ) = refs[4:40]
    load_sems, probs_sems, free, pos_sems, note_sems, spill_sems = refs[40:46]
    place = Place()
    reducing = Reducing(
        place, flat, swapped, one_buf, two_buf, deep, piece, result,
        dict(zip(REDUCE_SEMS, refs[46:])), free,
    )
    climbing = Notes(place, notes, slots, note_sems)
    loads = {}

    def load(name, src, dst):
        loads[name] = pltpu.make_async_copy(src, dst, load_sems.at[len(loads)])
        loads[name].start()

    mixed = active.at[:, : 3 * D]
    grad_attn = branch
    w_qkv = w_in.at[:, : 3 * D]
    hidden_low = dctx
    features_t = w_back.at[:D, :WINLEN]
    low_t = w_out.at[:WINLEN]
    scores = [hat.at[:, :WINLEN], scores_odd]
    dscores = [w_back.at[2 * WINLEN : 3 * WINLEN, :WINLEN], w_back.at[3 * WINLEN : 4 * WINLEN, :WINLEN]]
    low_turned = w_back.at[4 * WINLEN : 4 * WINLEN + D, :WINLEN]
    output_low = w_out.at[:WINLEN]
    output_low = w_out.at[:WINLEN]
    dscores_x = [slope.at[:, 2 * WINLEN : 3 * WINLEN], slope.at[:, 3 * WINLEN : 4 * WINLEN]]
    dscores_y = [slope.at[:, 4 * WINLEN : 5 * WINLEN], slope.at[:, 5 * WINLEN :]]

    load("normed", normed_in, dctx)
    load("w_in", w_in_in, w_in)
    load("hat", hat_in, hat)
    load("w_back", w_back_in, w_back)
    load("cot", cot_in, branch)

    at = staged_at(plan, COLUMNS - 1, plan.misc_start)
    staged[at:, :] = jnp.zeros((plan.staged - at, LANES), F32)
    place.greet()

    quarter = WINLEN // DEPTH
    positions = []

    def to_pos(source, target, kind):
        for d in range(DEPTH - 1):
            rows = pl.ds(pl.multiple_of(place.far[d] * quarter, quarter), quarter)
            copy = remote(
                source.at[rows], target.at[place.z], pos_sems.at[kind, 0, d], pos_sems.at[kind, 1, d],
                place.peers_z[d],
            )
            copy.start()
            positions.append(copy)
        rows = pl.ds(pl.multiple_of(place.z * quarter, quarter), quarter)
        copy = pltpu.make_async_copy(
            source.at[rows], target.at[place.z], pos_sems.at[kind, 0, DEPTH - 1]
        )
        copy.start()
        return copy

    def in_pos(target, kind):
        for d in range(DEPTH - 1):
            there = target.at[place.from_far[d]]
            remote(
                there, there, pos_sems.at[kind, 0, d], pos_sems.at[kind, 1, d], place.peer_x
            ).wait_recv()


    def store(k, index, row, value, first_block=0):
        blocks = MATRICES[index][1] // LANES
        base = staged_at(plan, k, plan.starts[index]) + row * blocks + first_block
        for block in range(value.shape[1] // LANES):
            staged[pl.ds(base + block, value.shape[0], stride=blocks), :] = value[
                :, block * LANES : (block + 1) * LANES
            ]

    def column_sum(value):
        return jnp.sum(value, axis=0, keepdims=True)

    def keep_vector(name, lanes_at, value):
        at = pl.multiple_of(VEC[name] + lanes_at, LANES)
        vecg[0:1, pl.ds(at, value.shape[1])] = value

    def vector(name, at=0, size=D):
        return vec[0:1, pl.ds(pl.multiple_of(VEC[name] + at, LANES), size)]

    loads["normed"].wait()
    loads["w_in"].wait()

    def widen(n, carry):
        at = pl.multiple_of(n * NBLOCK, NBLOCK)
        lanes = pl.ds(at, NBLOCK)
        inner_act = matmul(dctx[...], w_in[:, lanes]) + vector("in_bias", at, NBLOCK)
        value, change = gelu_and_slope(inner_act)
        active[:, lanes] = value.astype(BF16)
        slope[:, lanes] = change.astype(BF16)
        return carry

    lax.fori_loop(0, FF // NBLOCK, widen, 0, unroll=2)
    loads["hat"].wait()
    loads["w_back"].wait()
    for n in range(D // NBLOCK):
        lanes = slice(n * NBLOCK, (n + 1) * NBLOCK)
        normed = hat[:, lanes] * vector("gain_one", n * NBLOCK, NBLOCK) + vector(
            "shift_one", n * NBLOCK, NBLOCK
        )
        second[:, lanes] = (
            normed + matmul(active[...], w_back[:, lanes]) + vector("back_bias", n * NBLOCK, NBLOCK)
        )
    loads["cot"].wait()
    step_rows = 64
    for name in ("gain_two", "shift_two", "back_bias", "gain_one", "shift_one", "out_bias"):
        keep_vector(name, 0, jnp.zeros((1, D), F32))

    def add_vector(name, term):
        lanes = slice(VEC[name], VEC[name] + D)
        vecg[0:1, lanes] = vecg[0:1, lanes] + column_sum(term)

    def norm_second(n, carry):
        rows = pl.ds(pl.multiple_of(n * step_rows, step_rows), step_rows)
        x = second[rows, :]
        centred = x - jnp.mean(x, axis=1, keepdims=True)
        rstd = lax.rsqrt(jnp.mean(centred * centred, axis=1, keepdims=True) + norm_eps)
        xhat = centred * rstd
        gain = vector("gain_two")
        output_low[rows, :] = (xhat * gain + vector("shift_two")).astype(BF16)
        cot = branch[rows, :].astype(F32)
        prod = cot * xhat
        gc = cot * gain
        mean_one = jnp.mean(gc, axis=1, keepdims=True)
        mean_two = jnp.mean(prod * gain, axis=1, keepdims=True)
        value = rstd * (gc - mean_one - xhat * mean_two)
        second[rows, :] = value
        value = value.astype(BF16)
        branch[rows, :] = value
        add_vector("gain_two", prod)
        add_vector("shift_two", cot)
        add_vector("back_bias", value.astype(F32))
        return carry

    lax.fori_loop(0, WINLEN // step_rows, norm_second, 0, unroll=2)
    own_output = to_pos(output_low, output_pos, 0)

    def back_rows(k, size, begin, count):
        def body(n, carry):
            row = pl.multiple_of(begin + n * size, LANES)
            turned[:size, :] = active[:, pl.ds(row, size)].T
            store(k, 4, row, matmul(turned[:size, :], branch[...]))
            return carry

        lax.fori_loop(0, count, body, 0)

    back_rows(3, WINLEN, 512, FF // WINLEN - 1)
    unstage_column(plan, flat, staged, 3)
    reducing.swap(3, 0)
    reducing.swap(3, 1)

    back_rows(2, WINLEN, 0, 1)
    back_rows(2, LANES, 512, 1)

    def inner(n, carry):
        at = pl.multiple_of(n * NBLOCK, NBLOCK)
        lanes = pl.ds(at, NBLOCK)
        value = times_transposed(branch[...], w_back[lanes, :]) * slope[:, lanes].astype(F32)
        value = value.astype(BF16)
        slope[:, lanes] = value
        keep_vector("in_bias", at, column_sum(value.astype(F32)))
        return carry

    lax.fori_loop(0, FF // NBLOCK, inner, 0, unroll=2)
    grad_inner = slope
    reducing.first(3, 0)
    reducing.first(3, 1)

    for n in range(D // NBLOCK):
        rows = slice(n * NBLOCK, (n + 1) * NBLOCK)
        turned[rows, :] = dctx[:, rows].T

    def in_rows(k, begin, end):
        def body(n, carry):
            lanes = pl.ds(pl.multiple_of(n * NBLOCK, NBLOCK), NBLOCK)
            got = matmul(turned[begin:end, :], grad_inner[:, lanes])
            store(k, 3, begin, got, n * (NBLOCK // LANES))
            return carry

        lax.fori_loop(0, FF // NBLOCK, body, 0)

    in_rows(2, 288, D)
    unstage_column(plan, flat, staged, 2)
    reducing.swap(2, 0)
    reducing.swap(2, 1)
    reducing.second(3, 0)
    reducing.second(3, 1)

    load("context", context_in, context_t)
    load("q", q_in, q_ref)
    load("k", k_in, k_ref)
    load("v", v_in, v_ref)
    for odd in range(2):
        pltpu.make_async_copy(probs_in.at[odd], probs.at[odd], probs_sems.at[odd]).start()
    for n in range(D // NBLOCK):
        lanes = slice(n * NBLOCK, (n + 1) * NBLOCK)
        second[:, lanes] = second[:, lanes] + times_transposed(grad_inner[...], w_in[lanes, :])
    load("w_qkv", w_qkv_in, w_qkv)
    load("features", features_in, features_t)
    reducing.first(2, 0)
    reducing.first(2, 1)

    for copy in positions:
        copy.wait_send()
    own_output.wait()
    load("w_out", w_out_in, w_out)

    def norm_first(n, carry):
        rows = pl.ds(pl.multiple_of(n * step_rows, step_rows), step_rows)
        grad = second[rows, :]
        xhat = hat[rows, :]
        prod = grad * xhat
        gain = vec[0:1, VEC["gain_one"] : VEC["gain_one"] + D]
        gc = grad * gain
        mean_one = jnp.mean(gc, axis=1, keepdims=True)
        mean_two = jnp.mean(prod * gain, axis=1, keepdims=True)
        value = rstd_ref[rows, 0:1] * (gc - mean_one - xhat * mean_two)
        second[rows, :] = value
        value = value.astype(BF16)
        grad_attn[rows, :] = value
        add_vector("gain_one", prod)
        add_vector("shift_one", grad)
        add_vector("out_bias", value.astype(F32))
        return carry

    lax.fori_loop(0, WINLEN // step_rows, norm_first, 0, unroll=2)
    reducing.third(3, 0)
    reducing.third(3, 1)
    loads["w_out"].wait()
    for n in range(D // NBLOCK):
        lanes = slice(n * NBLOCK, (n + 1) * NBLOCK)
        dctx[:, lanes] = times_transposed(grad_attn[...], w_out[lanes, :]).astype(BF16)
    load("low", low_in, low_t)
    loads["context"].wait()
    reducing.second(2, 0)
    reducing.second(2, 1)

    def out_rows(k, begin, end):
        for n in range(D // NBLOCK):
            lanes = slice(n * NBLOCK, (n + 1) * NBLOCK)
            got = matmul(context_t[begin:end, :], grad_attn[:, lanes])
            store(k, 1, begin, got, n * (NBLOCK // LANES))

    reducing.fourth(3, 0)
    reducing.fourth(3, 1)
    reducing.give(3, 0)
    reducing.give(3, 1)

    low, high = half_masks()
    rest = rest_ref[...]
    columns = jnp.concatenate([rest, jnp.zeros((LANES - 2, WINLEN), F32)], axis=0).T
    for part in range(BLOCKS):
        rows = slice(part * LANES, (part + 1) * LANES)
        for axis, less in ((0, less_x), (1, less_y)):
            less[rows, :] = jnp.where(
                rest[axis : axis + 1, :] < columns[rows, axis : axis + 1], 1.0, 0.0
            ).astype(BF16)
    hot_t[...] = hot_ref[...].T
    lane = lax.broadcasted_iota(jnp.int32, (1, LANES), 1)
    scale = HEAD_DIM ** (-0.5)
    of_x = jnp.where((lane // BUCKETS) % 2 == 0, 1.0, 0.0)
    share_cols[...] = jnp.concatenate(
        [share_ref[head] for head in range(HEADS)] + [jnp.zeros((LANES - HEADS, WINLEN), F32)], axis=0
    ).T
    for name in ("q", "k", "v"):
        loads[name].wait()

    def probs_copy(head, odd):
        return pltpu.make_async_copy(probs_in.at[head], probs.at[odd], probs_sems.at[odd])

    def spill_copy(head, odd):
        return pltpu.make_async_copy(dscores[odd], spill.at[head], spill_sems.at[odd])

    def one_pair(pair, carry):
        at = pl.multiple_of(pair * LANES, LANES)
        lanes = pl.ds(at, LANES)
        keys_t = k_ref[:, lanes].T
        both = pltpu.roll(share_cols[...], lax.rem(LANES - 2 * pair, LANES), 1)
        both = jnp.where(lane < HEAD_DIM, both[:, 0:1], both[:, 1:2])
        scaled[...] = (dctx[:, lanes].astype(F32) * both).astype(BF16)
        grad_context = dctx[:, lanes]
        dots = []
        for odd in range(2):
            mine, other = (low, high) if odd == 0 else (high, low)
            head = 2 * pair + odd
            probs_copy(head, odd).wait()
            products = times_transposed(v_ref[:, lanes] * mine, grad_context)
            dot = None
            for part in range(BLOCKS):
                rows = slice(part * LANES, (part + 1) * LANES)
                dp = products[rows]
                scores[odd][rows, :] = dp
                add = dp * probs[odd, rows, :].astype(F32)
                add = jnp.sum(add.reshape(LANES // 8, 8, WINLEN), axis=0)
                dot = add if dot is None else dot + add
            dots.append(column_sum(dot) * share_ref[head])
        for odd in range(2):
            head = 2 * pair + odd
            share = share_ref[head]

            @pl.when(pair > 0)
            def _():
                spill_copy(head, odd).wait()

            for part in range(BLOCKS):
                rows = slice(part * LANES, (part + 1) * LANES)
                ds = probs[odd, rows, :].astype(F32) * ((scores[odd][rows, :] - dots[odd]) * share)
                dscores[odd][rows, :] = ds.astype(BF16)
            spill_copy(head, odd).start()
        for odd in range(2):
            head = 2 * pair + odd
            keys_grad = matmul(dscores[odd][...], q_ref[:, lanes])
            values_grad = matmul(probs[odd], scaled[...])

            pair_t[odd * HEAD_DIM : (odd + 1) * HEAD_DIM, :] = matmul(
                keys_t[odd * HEAD_DIM : (odd + 1) * HEAD_DIM, :], dscores[odd][...]
            )
            for which, value in ((1, keys_grad), (2, values_grad)):
                there = pl.ds(pl.multiple_of(at + which * D, LANES), LANES)
                value = value.astype(BF16)
                if odd:
                    value = mixed[:, there] * low + value * high
                mixed[:, there] = value

        @pl.when(pair < PAIRS - 1)
        def _():
            for odd in range(2):
                probs_copy(2 * pair + odd + 2, odd).start()

        value = (pair_t[...].T * scale).astype(BF16)
        mixed[:, lanes] = value
        keep_vector("q_bias", at, column_sum(value.astype(F32)))
        there = pl.ds(pl.multiple_of(at + 2 * D, LANES), LANES)
        keep_vector("v_bias", at, column_sum(mixed[:, there].astype(F32)))
        return carry

    lax.fori_loop(0, 2, one_pair, 0)
    reducing.third(2, 0)
    reducing.third(2, 1)
    lax.fori_loop(2, 4, one_pair, 0)
    reducing.fourth(2, 0)
    reducing.fourth(2, 1)
    reducing.give(2, 0)
    reducing.give(2, 1)
    lax.fori_loop(4, PAIRS, one_pair, 0)

    for odd in range(2):
        spill_copy(0, odd).wait()
    loads["low"].wait()
    for n in range(D // NBLOCK):
        rows = slice(n * NBLOCK, (n + 1) * NBLOCK)
        low_turned[rows, :] = low_t[:, rows].T

    def qkv_rows(n, carry):
        lanes = pl.ds(pl.multiple_of(n * NBLOCK, NBLOCK), NBLOCK)
        store(0, 0, 0, matmul(low_turned[...], mixed[:, lanes]), n * (NBLOCK // LANES))
        return carry

    lax.fori_loop(0, 3 * D // NBLOCK, qkv_rows, 0)
    out_rows(0, 0, 208)
    reducing.settle(2)
    unstage_column(plan, flat, staged, 0)
    reducing.swap(0, 0)
    reducing.swap(0, 1)

    loads["w_qkv"].wait()
    for n in range(D // NBLOCK):
        lanes = slice(n * NBLOCK, (n + 1) * NBLOCK)
        value = second[:, lanes] + times_transposed(mixed[...], w_qkv[lanes, :])
        hidden_low[:, lanes] = value.astype(BF16)
    own_hidden = to_pos(hidden_low, hidden_pos, 1)
    reducing.first(0, 0)
    reducing.first(0, 1)
    loads["features"].wait()
    for n in range(D // NBLOCK):
        lanes = slice(n * NBLOCK, (n + 1) * NBLOCK)
        store(1, 2, 0, matmul(features_t[...], hidden_low[:, lanes]), n * (NBLOCK // LANES))
    in_rows(1, 0, 304)
    out_rows(1, 192, D)
    reducing.settle(3)
    unstage_column(plan, flat, staged, 1)
    reducing.swap(1, 0)
    reducing.swap(1, 1)
    reducing.second(0, 0)
    reducing.second(0, 1)

    def fetch_scores(head):
        there = slope.at[:, pl.ds(pl.multiple_of(lax.rem(head, 2) * WINLEN, WINLEN), WINLEN)]
        return pltpu.make_async_copy(spill.at[head], there, spill_sems.at[lax.rem(head, 2)])

    cells = [hot_ref[...] * of_x.astype(BF16), hot_ref[...] * (1.0 - of_x).astype(BF16)]
    band = bands.at[0]
    parts_x = slope.at[:, 2 * WINLEN : 3 * WINLEN]
    parts_y = slope.at[:, 3 * WINLEN : 4 * WINLEN]

    def one_table(head, carry):
        fetch_scores(head).wait()

        @pl.when(head < HEADS - 1)
        def _():
            fetch_scores(head + 1).start()

        here = slope.at[:, pl.ds(pl.multiple_of(lax.rem(head, 2) * WINLEN, WINLEN), WINLEN)]
        band[...] = jnp.zeros_like(band)
        for part in range(BLOCKS):
            rows = slice(part * LANES, (part + 1) * LANES)
            low_ds = here[rows, :]
            parts_x[rows, :] = low_ds * less_x[rows, :]
            parts_y[rows, :] = low_ds * less_y[rows, :]
            ds = low_ds.astype(F32)
            for block in range(BLOCKS):
                step = max(-2, min(2, block - part)) + 2
                where = slice(step * LANES, (step + 1) * LANES)
                band[:, where] = band[:, where] + ds[:, block * LANES : (block + 1) * LANES]
        whole = matmul(here[...], hot_ref[...])
        less = matmul(parts_x[...], cells[0]) + matmul(parts_y[...], cells[1])
        diag_rows[head, :, LANES : 5 * LANES] = diagonal_sums(band)
        diag_rows[head, :, :LANES] = column_sum(band[:, :LANES])
        diag_rows[head, :, 5 * LANES :] = column_sum(band[:, 4 * LANES :])
        sums = []
        for summed in (whole, less):
            first = summed.astype(BF16)
            remainder = (summed - first.astype(F32)).astype(BF16)
            sums.append(matmul(hot_t[:64, :], first) + matmul(hot_t[:64, :], remainder))
        for axis, value in enumerate(cell_sums(sums[0], sums[1])):
            cell_rows[axis * HEADS + head] = value
        return carry

    fetch_scores(0).start()
    reducing.first(1, 0)
    reducing.first(1, 1)
    lax.fori_loop(0, 4, one_table, 0)
    reducing.third(0, 0)
    reducing.second(1, 0)
    reducing.third(0, 1)
    reducing.second(1, 1)
    lax.fori_loop(4, 8, one_table, 0)
    reducing.fourth(0, 0)
    reducing.give(0, 0)
    reducing.third(1, 0)
    reducing.fourth(0, 1)
    reducing.give(0, 1)
    lax.fori_loop(8, HEADS, one_table, 0)
    notes[...] = jnp.zeros_like(notes)
    table = VEC["tables"] // LANES
    for row in range(table):
        notes[row : row + 1, :] = vecg[0:1, row * LANES : (row + 1) * LANES]
    notes[table : table + 9, :] = bucket_rows(cell_rows, diag_rows)
    climbing.start()
    reducing.third(1, 1)
    climbing.rise()
    reducing.fourth(1, 0)
    reducing.give(1, 0)
    climbing.end()
    reducing.fourth(1, 1)
    reducing.give(1, 1)
    reducing.receive(out)
    note_quarter, note_first, note_row = note_place(plan)
    base = note_first + note_row

    @pl.when(climbing.root)
    def _():
        out[note_quarter, base : base + MISC_ROWS, :] = (
            out[note_quarter, base : base + MISC_ROWS, :] + notes[:MISC_ROWS, :]
        )

    in_pos(output_pos, 0)
    in_pos(hidden_pos, 1)
    own_hidden.wait()
    for copy in positions[DEPTH - 1 :]:
        copy.wait_send()
    for k in range(COLUMNS):
        for h in range(2):
            reducing.given(k, h)
    reducing.settle(1)
    reducing.settle(0)


def backward_pass(plan, operands):
    anywhere = pl.BlockSpec(memory_space=pl.ANY)
    vmem = pl.BlockSpec(memory_space=pltpu.VMEM)
    token = (WINLEN, D)
    block = (plan.quarter, LANES)
    positions = jax.ShapeDtypeStruct((DEPTH, WINLEN // DEPTH, D), BF16)
    scratch = [
        pltpu.VMEM((2, CORES, DEPTH, COLUMNS) + block, BF16),
        pltpu.VMEM((plan.staged, LANES), F32),
        pltpu.VMEM((2, DEPTH, COLUMNS) + block, BF16),
        pltpu.VMEM((COLUMNS, 2, 2) + block, BF16),
        pltpu.VMEM((COLUMNS, 2, DEPTH) + block, BF16),
        pltpu.VMEM((COLUMNS, DEPTH - 1) + block, BF16),
        pltpu.VMEM((COLUMNS,) + block, BF16),
        pltpu.VMEM((COLUMNS,) + block, BF16),
        pltpu.VMEM((WINLEN, FF), BF16),
        pltpu.VMEM((WINLEN, FF), BF16),
        pltpu.VMEM((FF, D), BF16),
        pltpu.VMEM((D, FF), BF16),
        pltpu.VMEM((D, D), BF16),
        pltpu.VMEM((D, WINLEN), BF16),
        pltpu.VMEM((D, WINLEN), BF16),
        pltpu.VMEM(token, BF16),
        pltpu.VMEM(token, BF16),
        pltpu.VMEM(token, BF16),
        pltpu.VMEM(token, F32),
        pltpu.VMEM(token, F32),
        pltpu.VMEM(token, BF16),
        pltpu.VMEM(token, BF16),
        pltpu.VMEM((2, WINLEN, WINLEN), BF16),
        pltpu.VMEM((WINLEN, WINLEN), BF16),
        pltpu.VMEM((WINLEN, WINLEN), BF16),
        pltpu.VMEM((WINLEN, WINLEN), F32),
        pltpu.VMEM((1, LANES, 5 * LANES), F32),
        pltpu.VMEM((LANES, WINLEN), BF16),
        pltpu.VMEM((LANES, WINLEN), F32),
        pltpu.VMEM((WINLEN, LANES), BF16),
        pltpu.VMEM((WINLEN, LANES), F32),
        pltpu.VMEM((1, VEC_ROWS * LANES), F32),
        pltpu.VMEM((2 * HEADS, 1, LANES), F32),
        pltpu.VMEM((HEADS, 1, WIDE), F32),
        pltpu.VMEM((NOTE_ROWS, LANES), F32),
        pltpu.VMEM((7, NOTE_ROWS, LANES), F32),
        pltpu.SemaphoreType.DMA((16,)),
        pltpu.SemaphoreType.DMA((2,)),
        pltpu.SemaphoreType.REGULAR((2,)),
        pltpu.SemaphoreType.DMA((2, 2, DEPTH)),
        pltpu.SemaphoreType.DMA((2, 7)),
        pltpu.SemaphoreType.DMA((2,)),
    ]
    return pl.pallas_call(
        functools.partial(backward_kernel, plan),
        out_shape=[
            jax.ShapeDtypeStruct((COLUMNS,) + block, F32), positions, positions,
            jax.ShapeDtypeStruct((HEADS, WINLEN, WINLEN), BF16),
        ],
        in_specs=[anywhere] * 14 + [vmem] * 5,
        out_specs=[vmem] + [anywhere] * 3,
        scratch_shapes=scratch + sem_shapes(REDUCE_SEMS),
        compiler_params=pltpu.CompilerParams(
            collective_id=1, has_side_effects=True, vmem_limit_bytes=62 * 2**20
        ),
        name="backward_pass",
    )(*operands)


def fast_shards(hidden_in, cotangent, box_coords, doc_lengths, params, moment_one, moment_two):
    shard_len = params.shape[0]
    plan = Plan(shard_len)
    (proj_qkv, proj_out, proj_in, proj_back, features_t, start_low, queries, keys, values, probs, context_t,
     xhat, normed_low, vec, rstd, cot, hot_two,
     rest_rows, share) = forward_pass(
        plan, params.reshape(plan.rows, LANES), hidden_in, cotangent,
        jnp.transpose(box_coords, (0, 2, 1)), doc_lengths,
    )
    summed, output_low, grad_hidden, _ = backward_pass(
        Plan(shard_len, carry=5 * LANES),
        (proj_back, proj_in, proj_out, proj_qkv, normed_low, start_low, features_t, context_t, queries, keys,
         values, probs, xhat, cot, rstd, vec, hot_two, rest_rows, share),
    )
    grad_share = summed.reshape(plan.padded, LANES)[: plan.rows].reshape(-1)
    return finish_step(output_low, grad_hidden, grad_share, params, moment_one, moment_two)


def finish_step(output_low, grad_hidden, grad_share, params, moment_one, moment_two):
    shard_len = params.shape[0]
    index = lax.axis_index("dp") * lax.axis_size("head") + lax.axis_index("head")
    flat_index = index * shard_len + jnp.arange(shard_len, dtype=jnp.int32)
    param_step, new_one = adam_step(params, moment_one, moment_two, grad_share, flat_index)
    return (output_low, grad_hidden, grad_share, param_step, new_one)


def to_windows(shard):
    return lax.all_to_all(shard, "head", split_axis=0, concat_axis=1, tiled=True)


def to_positions(window):
    return lax.all_to_all(window, "head", split_axis=1, concat_axis=0, tiled=True)


def plain_shards(hidden_in, cotangent, box_coords, doc_lengths, params, moment_one, moment_two):
    head_pos = lax.axis_index("head")
    groups = lax.axis_size("head")
    shard_len = params.shape[0]
    flat_params = lax.all_gather(params.astype(BF16), ("dp", "head"), axis=0, tiled=True)
    pieces = unpack(flat_params)
    hidden = to_windows(hidden_in).reshape(WINLEN, D)
    cot = to_windows(cotangent).reshape(WINLEN, D)
    own_box = lax.dynamic_index_in_dim(box_coords, head_pos, 0, keepdims=False)
    own_lengths = lax.dynamic_index_in_dim(doc_lengths, head_pos, 0, keepdims=False)
    chosen, relative, centre_x, centre_y = window_layout(own_lengths, own_box)
    features = box_features(relative).astype(BF16)

    proj_qkv, proj_out, proj_box, proj_in, proj_back = pieces[:5]
    qv_bias, out_bias, norm_one, in_bias, back_bias, norm_two, tables = pieces[5:]
    ops = bias_operands(tables, chosen, centre_x, centre_y)
    start_state = hidden.astype(F32) + matmul(features, proj_box)
    start_low = start_state.astype(BF16)
    qv_float = qv_bias.astype(F32)
    mixed = matmul(start_low, proj_qkv)
    queries = (mixed[:, :D] + qv_float[0]).astype(BF16) * jnp.asarray(HEAD_DIM ** (-0.5), BF16)
    keys = mixed[:, D : 2 * D].astype(BF16)
    values = (mixed[:, 2 * D :] + qv_float[1]).astype(BF16)

    probs, context_t = attention_forward(queries, keys, values, ops)
    first_sum = start_state + rows_inner(context_t, proj_out) + out_bias.astype(F32)
    normed, norm_one_back = jax.vjp(layer_norm, first_sum, norm_one.astype(F32))
    normed_low = normed.astype(BF16)
    inner_act = matmul(normed_low, proj_in) + in_bias.astype(F32)
    active, gelu_back = jax.vjp(gelu_exact, inner_act)
    active_low = active.astype(BF16)
    second_sum = normed + matmul(active_low, proj_back) + back_bias.astype(F32)
    output, norm_two_back = jax.vjp(layer_norm, second_sum, norm_two.astype(F32))
    output_low = to_positions(output.astype(BF16).reshape(1, WINLEN, D))

    grad_second, grad_norm_two = norm_two_back(cot.astype(F32))
    grad_branch = grad_second.astype(BF16)
    grad_proj_back = rows_inner(active_low, grad_branch)
    grad_back_bias = jnp.sum(grad_branch.astype(F32), axis=0)
    (grad_inner_f,) = gelu_back(times_transposed(grad_branch, proj_back))
    grad_inner = grad_inner_f.astype(BF16)
    grad_proj_in = rows_inner(normed_low, grad_inner)
    grad_in_bias = jnp.sum(grad_inner.astype(F32), axis=0)
    grad_first, grad_norm_one = norm_one_back(grad_second + times_transposed(grad_inner, proj_in))
    grad_attn = grad_first.astype(BF16)
    grad_proj_out = matmul(context_t, grad_attn)
    grad_out_bias = jnp.sum(grad_attn.astype(F32), axis=0)
    grad_context = times_transposed(grad_attn, proj_out).astype(BF16)
    grad_queries_t, grad_keys, grad_values, cells, diag = attention_backward(
        queries, keys, values, grad_context, probs, ops
    )
    table_grad = table_grads(cells, diag)
    grad_mixed = jnp.concatenate([grad_queries_t.T, grad_keys, grad_values], axis=1)
    grad_proj_qkv = rows_inner(start_low, grad_mixed)
    summed = jnp.sum(grad_mixed.astype(F32), axis=0)
    grad_qv_bias = jnp.stack([summed[:D], summed[2 * D :]])
    grad_start = grad_first + times_transposed(grad_mixed, proj_qkv)
    grad_start_low = grad_start.astype(BF16)
    grad_hidden = to_positions(grad_start_low.reshape(1, WINLEN, D))
    grad_proj_box = rows_inner(features, grad_start_low)
    grad_list = (
        grad_proj_qkv,
        grad_proj_out,
        grad_proj_box,
        grad_proj_in,
        grad_proj_back,
        grad_qv_bias,
        grad_out_bias,
        grad_norm_one,
        grad_in_bias,
        grad_back_bias,
        grad_norm_two,
        table_grad,
    )
    padding = jnp.zeros((shard_len * groups * lax.axis_size("dp") - USED,), BF16)
    grads_flat = jnp.concatenate([piece.astype(BF16).reshape(-1) for piece in grad_list] + [padding])
    grad_share = lax.psum_scatter(
        grads_flat, ("dp", "head"), scatter_dimension=0, tiled=True
    ).astype(F32)
    return finish_step(output_low, grad_hidden, grad_share, params, moment_one, moment_two)


def solution(mesh):
    placed = (
        P("dp", "head", None),
        P("dp", "head", None),
        P("dp", None, None),
        P("dp", None),
        P(("dp", "head")),
        P(("dp", "head")),
        P(("dp", "head")),
    )
    return jax.shard_map(
        fast_shards if fits(mesh) else plain_shards,
        mesh=mesh,
        in_specs=placed,
        out_specs=(
            P("dp", "head", None),
            P("dp", "head", None),
            P(("dp", "head")),
            P(("dp", "head")),
            P(("dp", "head")),
        ),
        check_vma=False,
    )
```

```python
import functools
import math

import jax
import jax.numpy as jnp
import numpy as np
from jax import lax
from jax.experimental import pallas as pl
from jax.experimental.pallas import tpu as pltpu
from jax.sharding import PartitionSpec as P

D = 768
HEADS = 12
FF = 3072
BUCKETS = 32
WINLEN = 512
HEAD_DIM = 64
PAIRS = HEADS // 2
LANES = 128
BLOCKS = WINLEN // LANES

beta_one = 0.9
beta_two = 0.999
adam_eps = 1e-08
norm_eps = 1e-05
base_rate = 0.001
layer_decay = 0.75
decay_weight = 0.01
adam_count = 100
coord_cell = 32
masked_score = -1e30

F32 = jnp.float32
BF16 = jnp.bfloat16


def layouts_list():
    return (
        (D, 3 * D),
        (D, D),
        (D, D),
        (D, FF),
        (FF, D),
        (2, D),
        (D,),
        (2, D),
        (FF,),
        (D,),
        (2, D),
        (3, HEADS, BUCKETS),
    )


def unpack(flat_params):
    pieces = []
    offset = 0
    for layout in layouts_list():
        elements = math.prod(layout)
        pieces.append(flat_params[offset : offset + elements].reshape(layout))
        offset += elements
    return pieces


def matmul(left_mat, right_mat):
    return jnp.dot(left_mat, right_mat, preferred_element_type=F32)


def rows_inner(left_mat, right_mat):
    return lax.dot_general(left_mat, right_mat, (((0,), (0,)), ((), ())), preferred_element_type=F32)


def times_transposed(left_mat, right_mat):
    return lax.dot_general(left_mat, right_mat, (((1,), (1,)), ((), ())), preferred_element_type=F32)


def layer_norm(values, gain_bias):
    row_mean = jnp.mean(values, axis=-1, keepdims=True)
    centred = values - row_mean
    spread = jnp.mean(centred * centred, axis=-1, keepdims=True)
    return centred * lax.rsqrt(spread + norm_eps) * gain_bias[0] + gain_bias[1]


def gelu_exact(values):
    return jax.nn.gelu(values, approximate=False)


def hot(index, count):
    return (np.asarray(index)[..., None] == np.arange(count)).astype(np.float32)


def clipped(steps):
    return np.clip(steps, -(BUCKETS // 2), BUCKETS // 2 - 1) + BUCKETS // 2


CELLS = np.arange(BUCKETS)
HOT_SAME = hot(clipped(CELLS[:, None] - CELLS[None, :]), BUCKETS)
HOT_LESS = hot(clipped(CELLS[:, None] - CELLS[None, :] - 1), BUCKETS)
WIDE = 6 * LANES
_U = np.arange(WIDE)
BAND_HOT = hot(np.where(_U < 5 * LANES, clipped(_U - 2 * LANES), 0), BUCKETS)
_V = np.arange(4 * LANES)
DIAG_HOT = np.concatenate(
    [
        hot(np.zeros(LANES, np.int64), BUCKETS),
        hot(np.where(_V < 3 * LANES, clipped(_V - LANES), 0), BUCKETS),
        hot(np.full(LANES, BUCKETS - 1), BUCKETS),
    ]
)


def window_layout(doc_lengths, box_coords):
    doc_ends = jnp.cumsum(doc_lengths, dtype=jnp.int32)
    doc_starts = doc_ends - doc_lengths
    places = jnp.arange(WINLEN, dtype=jnp.int32)
    doc_ids = jnp.sum(
        (places[:, None] >= doc_ends[None, :]).astype(jnp.int32), axis=1, dtype=jnp.int32
    )
    docs = jnp.arange(doc_lengths.shape[0], dtype=jnp.int32)
    chosen = doc_ids[:, None] == docs[None, :]
    first_hot = places[:, None] == doc_starts[None, :]
    first_box = jnp.sum(
        jnp.where(first_hot[:, :, None], box_coords[:, None, :], 0), axis=0, dtype=jnp.int32
    )
    anchor = jnp.sum(
        jnp.where(chosen[:, :, None], first_box[None, :, :], 0), axis=1, dtype=jnp.int32
    )
    relative = box_coords - jnp.concatenate([anchor[:, :2], anchor[:, :2]], axis=1)
    centre_x = (box_coords[:, 0] + box_coords[:, 2]) // 2
    centre_y = (box_coords[:, 1] + box_coords[:, 3]) // 2
    return chosen, relative, centre_x, centre_y


def box_features(relative):
    count_freq = D // 8
    steps = jnp.arange(count_freq, dtype=F32)
    frequency = jnp.exp(steps * (-math.log(1000.0) / count_freq))
    angles = relative.astype(F32)[:, :, None] * frequency[None, None, :]
    return jnp.concatenate([jnp.sin(angles), jnp.cos(angles)], axis=2).reshape(relative.shape[0], D)


def bias_operands(tables, chosen, centre_x, centre_y):
    cell_x, cell_y = centre_x // coord_cell, centre_y // coord_cell
    rest_x, rest_y = centre_x % coord_cell, centre_y % coord_cell
    cells = jnp.arange(BUCKETS, dtype=jnp.int32)
    hot_x = (cell_x[:, None] == cells[None, :]).astype(BF16)
    hot_y = (cell_y[:, None] == cells[None, :]).astype(BF16)
    none = jnp.zeros_like(hot_x)
    hot_two = jnp.concatenate([hot_x, hot_y, hot_x, hot_y], axis=1)
    key_x = jnp.stack(
        [
            jnp.concatenate([hot_x, -hot_x, none, none], axis=1),
            jnp.concatenate([none, none, hot_x, -hot_x], axis=1),
        ]
    )
    key_y = jnp.stack(
        [
            jnp.concatenate([hot_y, -hot_y, none, none], axis=1),
            jnp.concatenate([none, none, hot_y, -hot_y], axis=1),
        ]
    )
    same = jnp.einsum("qcb,thb->thqc", HOT_SAME.astype(BF16), tables[1:], preferred_element_type=F32)
    less = jnp.einsum("qcb,thb->thqc", HOT_LESS.astype(BF16), tables[1:], preferred_element_type=F32)
    zero = jnp.zeros_like(same[0])
    base = jnp.concatenate(
        [jnp.concatenate([same[0], zero], axis=2), jnp.concatenate([zero, same[1]], axis=2)], axis=1
    )
    base = base.reshape(PAIRS, 2, 64, 64)[:, ::-1].reshape(HEADS, 64, 64)
    diff_x = jnp.concatenate([jnp.concatenate([less[0], same[0]], axis=2), jnp.zeros((HEADS, 32, 64), F32)], axis=1)
    diff_y = jnp.concatenate([jnp.zeros((HEADS, 32, 64), F32), jnp.concatenate([less[1], same[1]], axis=2)], axis=1)
    rows = jnp.concatenate([base, diff_x, diff_y], axis=0).astype(BF16)
    rows = rows.transpose(1, 0, 2).reshape(64, 3 * D)
    met = matmul(hot_two[:, :64], rows).astype(BF16)
    band = matmul(tables[0], jnp.asarray(BAND_HOT.T, BF16)).reshape(HEADS, 1, WIDE)
    rest_cols = jnp.stack([rest_x, rest_y], axis=1).astype(F32)
    rest_rows = rest_cols.T
    pad = jnp.zeros((WINLEN, LANES - chosen.shape[1]), BF16)
    marks = chosen.astype(BF16)
    mark_keys = jnp.concatenate([marks, pad], axis=1)
    mark_queries = jnp.concatenate([(1 - marks) * jnp.asarray(masked_score, BF16), pad], axis=1)
    return dict(
        hot_two=hot_two,
        key_x=key_x,
        key_y=key_y,
        met=met,
        band=band,
        rest_cols=rest_cols,
        rest_rows=rest_rows,
        mark_keys=mark_keys,
        mark_queries=mark_queries,
    )


def half_masks():
    lane = lax.broadcasted_iota(jnp.int32, (1, LANES), 1)
    low = (lane < HEAD_DIM).astype(F32)
    return low.astype(BF16), (1.0 - low).astype(BF16)


def less_masks(rest_cols, rest_rows, less_x, less_y):
    for part in range(BLOCKS):
        rows = slice(part * LANES, (part + 1) * LANES)
        for axis, less in ((0, less_x), (1, less_y)):
            column = rest_cols[rows, axis : axis + 1]
            row = rest_rows[axis : axis + 1, :]
            less[rows, :] = jnp.where(row < column, 1.0, 0.0).astype(less.dtype)


def attention_forward_kernel(
    q_ref, k_ref, v_ref, hot_ref, keyx_ref, keyy_ref, met_ref, band_ref, cols_ref, rows_ref,
    mkey_ref, mquery_ref, probs_ref, context_ref,
    kaug, qaug, less_x, less_y, wide, scores,
):
    low, high = half_masks()
    less_masks(cols_ref, rows_ref, less_x, less_y)
    kaug[:, LANES:] = mkey_ref[...]
    qaug[:, LANES:] = mquery_ref[...]
    half = 2 * LANES

    def one_pair(pair, carry):
        at = pl.multiple_of(pair * LANES, LANES)
        lanes = pl.ds(at, LANES)
        lanes_x = pl.ds(pl.multiple_of(at + D, LANES), LANES)
        lanes_y = pl.ds(pl.multiple_of(at + 2 * D, LANES), LANES)
        values_t = v_ref[:, lanes].T
        for odd in range(2):
            own, other = (low, high) if odd == 0 else (high, low)
            head = 2 * pair + odd
            kaug[:, :LANES] = k_ref[:, lanes] * own + hot_ref[...] * other
            qaug[:, :LANES] = q_ref[:, lanes] * own + met_ref[:, lanes] * other
            skew_band(band_ref[head], wide)
            for side in range(2):
                cols = slice(side * half, (side + 1) * half)
                top = None
                for part in range(BLOCKS):
                    rows = slice(part * LANES, (part + 1) * LANES)
                    s = times_transposed(kaug[rows, :], qaug[cols, :])
                    dx = times_transposed(keyx_ref[odd, rows, :], met_ref[cols, lanes_x])
                    dy = times_transposed(keyy_ref[odd, rows, :], met_ref[cols, lanes_y])
                    bias = []
                    for block in range(2 * side, 2 * side + 2):
                        step = max(-2, min(2, block - part)) + 2
                        bias.append(wide[:, step * LANES : (step + 1) * LANES])
                    s = s + jnp.concatenate(bias, axis=1)
                    s = s + dx * less_x[rows, cols] + dy * less_y[rows, cols]
                    scores[rows, :] = s
                    best = jnp.max(s, axis=0, keepdims=True)
                    top = best if top is None else jnp.maximum(top, best)
                total = None
                for part in range(BLOCKS):
                    rows = slice(part * LANES, (part + 1) * LANES)
                    e = jnp.exp(scores[rows, :] - top)
                    scores[rows, :] = e
                    add = jnp.sum(e, axis=0, keepdims=True)
                    total = add if total is None else total + add
                share = 1.0 / total
                for part in range(BLOCKS):
                    rows = slice(part * LANES, (part + 1) * LANES)
                    probs_ref[head, rows, cols] = (scores[rows, :] * share).astype(BF16)
                got = matmul(
                    values_t[odd * HEAD_DIM : (odd + 1) * HEAD_DIM, :], probs_ref[head, :, cols]
                )
                context_ref[pl.ds(pl.multiple_of(head * HEAD_DIM, HEAD_DIM), HEAD_DIM), cols] = (
                    got.astype(BF16)
                )
        return carry

    lax.fori_loop(0, PAIRS, one_pair, 0)


def skew_band(row, wide):
    x = jnp.broadcast_to(row, (8, WIDE))
    sub = lax.broadcasted_iota(jnp.int32, (8, WIDE), 0)
    for bit in (1, 2, 4):
        x = jnp.where((sub & bit) != 0, pltpu.roll(x, bit, 1), x)
    for group in range(LANES // 8):
        y = x if group == 0 else pltpu.roll(x, 8 * group, 1)
        wide[8 * group : 8 * group + 8, :] = y[:, : 5 * LANES]


def skew_groups(skewed, wide):
    for group in range(LANES // 8):
        y = skewed if group == 0 else pltpu.roll(skewed, 8 * group, 1)
        wide[8 * group : 8 * group + 8, :] = y[:, : 5 * LANES]


def diagonal_sums(parts):
    total = None
    for group in range(LANES // 8):
        x = jnp.concatenate(
            [parts[8 * group : 8 * group + 8, LANES : 4 * LANES], jnp.zeros((8, LANES), F32)], axis=1
        )
        y = x if group == 0 else pltpu.roll(x, 4 * LANES - 8 * group, 1)
        total = y if total is None else total + y
    sub = lax.broadcasted_iota(jnp.int32, (8, 4 * LANES), 0)
    for bit in (1, 2, 4):
        total = jnp.where((sub & bit) != 0, pltpu.roll(total, 4 * LANES - bit, 1), total)
    return jnp.sum(total, axis=0, keepdims=True)


def attention_backward_kernel(
    q_ref, k_ref, v_ref, dctx_ref, probs_ref, hot_ref, cols_ref, rows_ref,
    dq_ref, dk_ref, dv_ref, cells_ref, diag_ref,
    qaug, less_x, less_y, scores, dscores, band, kept, hot_t,
):
    low, high = half_masks()
    less_masks(cols_ref, rows_ref, less_x, less_y)
    hot_t[...] = hot_ref[...].T
    lane = lax.broadcasted_iota(jnp.int32, (1, LANES), 1)
    scale = HEAD_DIM ** (-0.5)
    of_x = jnp.where((lane // BUCKETS) % 2 == 0, 1.0, 0.0)
    cells_x = hot_ref[...] * of_x.astype(BF16)
    cells_y = hot_ref[...] * (1.0 - of_x).astype(BF16)

    def one_pair(pair, carry):
        at = pl.multiple_of(pair * LANES, LANES)
        lanes = pl.ds(at, LANES)
        keys_t = k_ref[:, lanes].T
        for odd in range(2):
            own, other = (low, high) if odd == 0 else (high, low)
            head = 2 * pair + odd
            qaug[...] = q_ref[:, lanes] * own + hot_ref[...] * other
            dctx = dctx_ref[:, lanes]
            dot = None
            for part in range(BLOCKS):
                rows = slice(part * LANES, (part + 1) * LANES)
                dp = times_transposed(v_ref[rows, lanes] * own, dctx)
                scores[rows, :] = dp
                add = jnp.sum(dp * probs_ref[head, rows, :].astype(F32), axis=0, keepdims=True)
                dot = add if dot is None else dot + add
            band[...] = jnp.zeros_like(band)
            for part in range(BLOCKS):
                rows = slice(part * LANES, (part + 1) * LANES)
                probs = probs_ref[head, rows, :]
                ds = probs.astype(F32) * (scores[rows, :] - dot)
                for block in range(BLOCKS):
                    step = max(-2, min(2, block - part)) + 2
                    where = slice(step * LANES, (step + 1) * LANES)
                    band[:, where] = band[:, where] + ds[:, block * LANES : (block + 1) * LANES]
                ds = ds.astype(BF16)
                dscores[rows, :] = ds
                both = matmul(ds, qaug[...])
                less = matmul(ds * less_x[rows, :], cells_x) + matmul(ds * less_y[rows, :], cells_y)
                dv = matmul(probs, dctx)
                kept[odd, 0, rows, :] = both
                kept[odd, 1, rows, :] = less
                kept[odd, 2, rows, :] = dv
            got = matmul(keys_t[odd * HEAD_DIM : (odd + 1) * HEAD_DIM, :], dscores[...])
            dq_ref[pl.ds(pl.multiple_of(head * HEAD_DIM, HEAD_DIM), HEAD_DIM), :] = (
                got * scale
            ).astype(BF16)
            diag_ref[head, :, LANES : 5 * LANES] = diagonal_sums(band)
            diag_ref[head, :, :LANES] = jnp.sum(band[:, :LANES], axis=0, keepdims=True)
            diag_ref[head, :, 5 * LANES :] = jnp.sum(band[:, 4 * LANES :], axis=0, keepdims=True)
            for which in range(2):
                summed = kept[odd, which]
                first = summed.astype(BF16)
                rest = (summed - first.astype(F32)).astype(BF16)
                cells_ref[head, which] = matmul(hot_t[:64, :], first) + matmul(hot_t[:64, :], rest)
        dk_ref[:, lanes] = jnp.where(lane < HEAD_DIM, kept[0, 0], kept[1, 0]).astype(BF16)
        dv_ref[:, lanes] = jnp.where(lane < HEAD_DIM, kept[0, 2], kept[1, 2]).astype(BF16)
        return carry

    lax.fori_loop(0, PAIRS, one_pair, 0)


def attention_forward(queries, keys, values, ops):
    return pl.pallas_call(
        attention_forward_kernel,
        out_shape=(
            jax.ShapeDtypeStruct((HEADS, WINLEN, WINLEN), BF16),
            jax.ShapeDtypeStruct((D, WINLEN), BF16),
        ),
        scratch_shapes=[
            pltpu.VMEM((WINLEN, 2 * LANES), BF16),
            pltpu.VMEM((WINLEN, 2 * LANES), BF16),
            pltpu.VMEM((WINLEN, WINLEN), F32),
            pltpu.VMEM((WINLEN, WINLEN), F32),
            pltpu.VMEM((LANES, 5 * LANES), F32),
            pltpu.VMEM((WINLEN, 2 * LANES), F32),
        ],
        compiler_params=pltpu.CompilerParams(vmem_limit_bytes=48 * 2**20),
        name="attention_forward",
    )(
        queries, keys, values, ops["hot_two"], ops["key_x"], ops["key_y"], ops["met"], ops["band"],
        ops["rest_cols"], ops["rest_rows"], ops["mark_keys"], ops["mark_queries"],
    )


def attention_backward(queries, keys, values, grad_context, probs, ops):
    return pl.pallas_call(
        attention_backward_kernel,
        out_shape=(
            jax.ShapeDtypeStruct((D, WINLEN), BF16),
            jax.ShapeDtypeStruct((WINLEN, D), BF16),
            jax.ShapeDtypeStruct((WINLEN, D), BF16),
            jax.ShapeDtypeStruct((HEADS, 2, 64, LANES), F32),
            jax.ShapeDtypeStruct((HEADS, 1, WIDE), F32),
        ),
        scratch_shapes=[
            pltpu.VMEM((WINLEN, LANES), BF16),
            pltpu.VMEM((WINLEN, WINLEN), BF16),
            pltpu.VMEM((WINLEN, WINLEN), BF16),
            pltpu.VMEM((WINLEN, WINLEN), F32),
            pltpu.VMEM((WINLEN, WINLEN), BF16),
            pltpu.VMEM((LANES, 5 * LANES), F32),
            pltpu.VMEM((2, 3, WINLEN, LANES), F32),
            pltpu.VMEM((LANES, WINLEN), BF16),
        ],
        compiler_params=pltpu.CompilerParams(vmem_limit_bytes=48 * 2**20),
        name="attention_backward",
    )(
        queries, keys, values, grad_context, probs, ops["hot_two"], ops["rest_cols"],
        ops["rest_rows"],
    )


def table_grads(cells, diag):
    exact = lax.Precision.HIGHEST
    pairs = cells.reshape(PAIRS, 2, 2, 64, LANES)
    every = jnp.stack([pairs[:, 0, 0, :, 64:], pairs[:, 1, 0, :, :64]], axis=1).reshape(HEADS, 64, 64)
    less = cells[:, 1]
    less_x, less_y = less[:, :32, :32], less[:, 32:, 32:64]
    all_x, all_y = every[:, :32, :32], every[:, 32:, 32:]
    same = jnp.stack([all_x - less_x, all_y - less_y]).reshape(2 * HEADS, -1)
    below = jnp.stack([less_x, less_y]).reshape(2 * HEADS, -1)
    same_hot = jnp.asarray(HOT_SAME.transpose(1, 0, 2).reshape(-1, BUCKETS))
    less_hot = jnp.asarray(HOT_LESS.transpose(1, 0, 2).reshape(-1, BUCKETS))
    moved = jnp.dot(same, same_hot, precision=exact) + jnp.dot(below, less_hot, precision=exact)
    along = jnp.dot(diag.reshape(HEADS, WIDE), jnp.asarray(DIAG_HOT), precision=exact)
    return jnp.concatenate([along[None], moved.reshape(2, HEADS, BUCKETS)], axis=0)


COLUMNS = 4
CORES = 2
DEPTH = 4
USED = sum(math.prod(layout) for layout in layouts_list())
MATRICES = layouts_list()[:5]
MISC = sum(math.prod(layout) for layout in layouts_list()[5:])
MISC_ROWS = -(-MISC // (8 * LANES)) * 8


class Plan:
    def __init__(self, shard_len, carry=3 * LANES):
        self.rows = shard_len // LANES
        self.quarter = -(-self.rows // (16 * COLUMNS)) * 16
        self.padded = COLUMNS * self.quarter
        self.per_column = CORES * DEPTH * self.rows
        self.carry = carry
        self.staged = self.carry + self.per_column + 3 * LANES
        starts = []
        offset = 0
        for depth, width in MATRICES:
            starts.append(offset // LANES)
            offset += depth * width
        self.starts = starts
        self.misc_start = offset // LANES


def fits(mesh):
    return mesh.shape["dp"] == COLUMNS * CORES and mesh.shape["head"] == DEPTH


MESH = pl.DeviceIdType.MESH


class Place:
    def __init__(self):
        dp = lax.axis_index("dp")
        self.z = lax.axis_index("head")
        self.core = dp % CORES
        self.column = dp // CORES
        self.x = self.column % 2
        self.y = self.column // 2
        self.col_x = 2 * self.y + (1 - self.x)
        self.col_y = 2 * (1 - self.y) + self.x
        self.col_d = 2 * (1 - self.y) + (1 - self.x)
        self.peer_x = self.at(self.col_x, self.core, self.z)
        self.peer_y = self.at(self.col_y, self.core, self.z)
        self.peer_d = self.at(self.col_d, self.core, self.z)
        self.peer_core = self.at(self.column, 1 - self.core, self.z)
        self.far = [lax.rem(self.z + d, DEPTH) for d in range(1, DEPTH)]
        self.from_far = [lax.rem(self.z + DEPTH - d, DEPTH) for d in range(1, DEPTH)]
        self.peers_z = [self.at(self.column, self.core, f) for f in self.far]

    def at(self, column, core, z):
        return {"dp": column * CORES + core, "head": z}

    def greet(self):
        barrier = pltpu.get_barrier_semaphore()
        peers = [self.peer_x, self.peer_y, self.peer_d, self.peer_core] + self.peers_z
        for peer in peers:
            pl.semaphore_signal(barrier, inc=1, device_id=peer, device_id_type=MESH)
        pl.semaphore_wait(barrier, len(peers))


def remote(src, dst, send_sem, recv_sem, peer):
    return pltpu.make_async_remote_copy(
        src_ref=src, dst_ref=dst, send_sem=send_sem, recv_sem=recv_sem, device_id=peer,
        device_id_type=MESH,
    )


class Gathering:
    def __init__(self, place, flat, sems):
        self.place = place
        self.flat = flat
        self.sems = sems
        self.sent = []

    def send(self, src, dst, kind, index, peer):
        copy = remote(src, dst, self.sems[kind].at[0, index], self.sems[kind].at[1, index], peer)
        copy.start()
        self.sent.append(copy)

    def got(self, dst, kind, index):
        remote(
            dst, dst, self.sems[kind].at[0, index], self.sems[kind].at[1, index], self.place.peer_x
        ).wait_recv()

    def rows(self, h):
        half = self.flat.shape[-2] // 2
        return slice(h * half, (h + 1) * half)

    def spread(self, own, h):
        p = self.place
        rows = self.rows(h)
        for index, (column, peer) in enumerate(
            ((p.col_x, p.peer_x), (p.col_y, p.peer_y), (p.col_d, p.peer_d))
        ):
            self.send(
                own.at[column, rows], self.flat.at[p.column, p.core, p.z, column, rows], "spread",
                2 * index + h, peer,
            )
        self.flat[p.column, p.core, p.z, p.column, rows] = own[p.column, rows]

    def spread_done(self, h):
        p = self.place
        for index, column in enumerate((p.col_x, p.col_y, p.col_d)):
            self.got(self.flat.at[column, p.core, p.z, p.column, self.rows(h)], "spread", 2 * index + h)

    def along_z(self, k, h):
        p = self.place
        piece = self.flat.at[k, p.core, p.z, p.column, self.rows(h)]
        for d in range(DEPTH - 1):
            self.send(piece, piece, "z", 3 * (2 * k + h) + d, p.peers_z[d])

    def first(self, k, h):
        p = self.place
        n = 2 * k + h
        for d in range(DEPTH - 1):
            self.got(
                self.flat.at[k, p.core, p.from_far[d], p.column, self.rows(h)], "z", 3 * n + d
            )
        piece = self.flat.at[k, p.core, :, p.column, self.rows(h)]
        self.send(piece, piece, "one", 2 * n, p.peer_x)
        self.send(piece, piece, "one", 2 * n + 1, p.peer_y)
        self.send(piece, piece, "core", 5 * n, p.peer_core)

    def second(self, k, h):
        p = self.place
        n = 2 * k + h
        rows = self.rows(h)
        from_x = self.flat.at[k, p.core, :, p.col_x, rows]
        self.got(from_x, "one", 2 * n)
        part = self.flat.at[k, p.core, 0:2, p.col_x, rows]
        self.send(part, part, "two", 2 * n, p.peer_y)
        self.send(from_x, from_x, "core", 5 * n + 1, p.peer_core)
        from_y = self.flat.at[k, p.core, :, p.col_y, rows]
        self.got(from_y, "one", 2 * n + 1)
        part = self.flat.at[k, p.core, 2:4, p.col_y, rows]
        self.send(part, part, "two", 2 * n + 1, p.peer_x)
        self.send(from_y, from_y, "core", 5 * n + 2, p.peer_core)

    def third(self, k, h):
        p = self.place
        n = 2 * k + h
        for side in range(2):
            part = self.flat.at[k, p.core, 2 * side : 2 * side + 2, p.col_d, self.rows(h)]
            self.got(part, "two", 2 * n + side)
            self.send(part, part, "core", 5 * n + 3 + side, p.peer_core)

    def complete(self, k):
        p = self.place
        other = 1 - p.core
        for h in range(2):
            n = 2 * k + h
            rows = self.rows(h)
            for index, column in enumerate((p.column, p.col_x, p.col_y)):
                self.got(self.flat.at[k, other, :, column, rows], "core", 5 * n + index)
            for side in range(2):
                self.got(
                    self.flat.at[k, other, 2 * side : 2 * side + 2, p.col_d, rows], "core",
                    5 * n + 3 + side,
                )

    def finish(self):
        for copy in self.sent:
            copy.wait_send()


GATHER_SEMS = {"spread": 6, "z": 24, "one": 16, "two": 16, "core": 40}


def sem_shapes(counts):
    return [pltpu.SemaphoreType.DMA((2, count)) for count in counts.values()]


def stage_column(plan, flat, staged, k):
    def one(shard, carry):
        core, z = shard // DEPTH, shard % DEPTH
        for quarter in range(COLUMNS):
            base = plan.carry + shard * plan.rows + quarter * plan.quarter
            staged[pl.ds(pl.multiple_of(base, 8), plan.quarter), :] = flat[k, core, z, quarter].astype(F32)
        return carry

    lax.fori_loop(0, CORES * DEPTH, one, 0)


def keep_carry(plan, staged):
    end = plan.carry + plan.per_column
    staged[: plan.carry, :] = staged[end - plan.carry : end, :]


ROW_STEP = 48


def column_rows(plan, k, touching):
    low, high = k * plan.per_column, (k + 1) * plan.per_column
    taken = []
    for index, (depth, width) in enumerate(MATRICES):
        group = 16 * (width // LANES)
        from_low, from_high = low - plan.starts[index], high - plan.starts[index]
        begin = max(0, min(depth, from_low // group * 16))
        if touching:
            end = max(0, min(depth, -(-from_high // group) * 16))
        else:
            end = max(0, min(depth, from_high // group * 16))
        if end > begin:
            taken.append((index, begin, end))
    return taken


def staged_at(plan, k, row):
    return plan.carry + row - k * plan.per_column


def row_loops(rows):
    whole = rows // ROW_STEP
    loops = [(ROW_STEP, 0, whole)] if whole else []
    if rows % ROW_STEP:
        loops.append((16, whole * ROW_STEP, (rows % ROW_STEP) // 16))
    return loops


def form_matrices(plan, staged, matrices, k):
    for index, begin, end in column_rows(plan, k, False):
        blocks = MATRICES[index][1] // LANES
        base = staged_at(plan, k, plan.starts[index] + begin * blocks)
        assert 0 <= base
        target = matrices[index]
        for step_rows, first, count in row_loops(end - begin):

            def one(step, carry, step_rows=step_rows, first=first, blocks=blocks, base=base,
                    begin=begin, target=target):
                row = first + step * step_rows
                for block in range(blocks):
                    got = staged[pl.ds(base + row * blocks + block, step_rows, stride=blocks), :]
                    target[
                        pl.ds(pl.multiple_of(begin + row, 16), step_rows),
                        block * LANES : (block + 1) * LANES,
                    ] = got.astype(BF16)
                return carry

            lax.fori_loop(0, count, one, 0)


def adam_step(params, moment_one, moment_two, grads, flat_index):
    box_part = (flat_index >= 4 * D * D) & (flat_index < 5 * D * D)
    step_rate = jnp.where(box_part, base_rate * layer_decay**12, base_rate * layer_decay)
    decay_mask = jnp.where(flat_index < 5 * D * D + 2 * D * FF, decay_weight, 0.0)
    moment_one = beta_one * moment_one + (1.0 - beta_one) * grads
    moment_two = beta_two * moment_two + (1.0 - beta_two) * grads * grads
    first_hat = moment_one / (1.0 - beta_one**adam_count)
    second_hat = moment_two / (1.0 - beta_two**adam_count)
    update = first_hat / (jnp.sqrt(second_hat) + adam_eps) + decay_mask * params
    return (-step_rate * update, moment_one)


VEC = {}
_at = 0
for _name, _rows in (
    ("q_bias", 6), ("v_bias", 6), ("out_bias", 6), ("gain_one", 6), ("shift_one", 6), ("in_bias", 24),
    ("back_bias", 6), ("gain_two", 6), ("shift_two", 6), ("tables", 9),
):
    VEC[_name] = _at * LANES
    _at += _rows
VEC_ROWS = _at
NOTE_ROWS = 96
NBLOCK = 2 * LANES


def note_place(plan):
    row = plan.misc_start - (CORES * DEPTH * COLUMNS - 1) * plan.rows
    quarter, row = row // plan.quarter, row % plan.quarter
    first = row // 16 * 16
    assert first + NOTE_ROWS <= plan.quarter and row - first + VEC_ROWS <= NOTE_ROWS
    return quarter, first, row - first


def spread_notes(place, own, notes, sems, plan):
    quarter, first, _ = note_place(plan)
    source = own.at[quarter, first : first + NOTE_ROWS]
    home = (place.column == COLUMNS - 1) & (place.core == CORES - 1)
    root = home & (place.z == DEPTH - 1)

    def copy(src, index, peer):
        return remote(src, notes, sems.at[0, index], sems.at[1, 0], peer)

    def arrived():
        copy(notes, 0, place.peer_core).wait_recv()

    @pl.when(root)
    def _():
        notes[...] = own[quarter, first : first + NOTE_ROWS]
        for index, peer in enumerate(place.peers_z):
            copy(source, index, peer).start()

    @pl.when(home & (place.z != DEPTH - 1))
    def _():
        arrived()

    @pl.when(home)
    def _():
        for index, peer in enumerate((place.peer_x, place.peer_y, place.peer_d)):
            copy(notes, 3 + index, peer).start()

    @pl.when((place.core == CORES - 1) & (place.column != COLUMNS - 1))
    def _():
        arrived()

    @pl.when(place.core == CORES - 1)
    def _():
        copy(notes, 6, place.peer_core).start()

    @pl.when(place.core != CORES - 1)
    def _():
        arrived()

    def finish():
        @pl.when(root)
        def _():
            for index, peer in enumerate(place.peers_z):
                copy(source, index, peer).wait_send()

        @pl.when(home)
        def _():
            for index, peer in enumerate((place.peer_x, place.peer_y, place.peer_d)):
                copy(notes, 3 + index, peer).wait_send()

        @pl.when(place.core == CORES - 1)
        def _():
            copy(notes, 6, place.peer_core).wait_send()

    return finish


def turns_table():
    count_freq = D // 8
    freq = np.exp(np.arange(count_freq) * (-math.log(1000.0) / count_freq)) / (2 * math.pi)
    per = np.concatenate([freq, freq])
    phase = np.concatenate([np.zeros(count_freq), np.full(count_freq, 0.25)])
    return np.stack([np.tile(per, 4), np.tile(phase, 4)]).astype(np.float32)


def sin_turns(t):
    t = t - jnp.floor(t + 0.5)
    a = jnp.abs(t)
    m = jnp.minimum(a, 0.5 - a) * (2 * math.pi)
    u = m * m
    poly = -1.0 / 39916800.0
    for term in (1.0 / 362880.0, -1.0 / 5040.0, 1.0 / 120.0, -1.0 / 6.0, 1.0):
        poly = poly * u + term
    s = m * poly
    return jnp.where(t < 0, -s, s)


def token_columns(boxes, lengths, window):
    coords = boxes[window].astype(F32)
    place = lax.broadcasted_iota(jnp.int32, (1, WINLEN), 1)
    doc = jnp.zeros((1, WINLEN), F32)
    anchor = jnp.zeros_like(coords)
    begin = 0
    for d in range(4):
        end = begin + lengths[window, d]
        mine = jnp.where((place >= begin) & (place < end), 1.0, 0.0)
        value = jnp.sum(coords * jnp.where(place == begin, 1.0, 0.0), axis=1, keepdims=True)
        anchor = anchor + value * mine
        doc = doc + mine * float(d)
        begin = end
    anchor = jnp.concatenate([anchor[0:2], anchor[0:2]], axis=0)
    relative = coords - anchor
    centre = jnp.floor((coords[0:2] + coords[2:4]) * 0.5)
    cell = jnp.floor(centre * (1.0 / coord_cell))
    rest = centre - cell * coord_cell
    rows = jnp.concatenate(
        [relative, cell, rest, doc, jnp.zeros((LANES - 9, WINLEN), F32)], axis=0
    )
    return rest, rows.T


def form_features(columns, turns_ref, features):
    lane = lax.broadcasted_iota(jnp.int32, (1, LANES), 1)
    for block in range(D // LANES):
        lanes = slice(block * LANES, (block + 1) * LANES)
        low, high = block * LANES // (D // 4), ((block + 1) * LANES - 1) // (D // 4)
        value = columns[:, low : low + 1]
        if high != low:
            value = jnp.where(
                lane + block * LANES < high * (D // 4), value, columns[:, high : high + 1]
            )
        t = value * turns_ref[0:1, lanes] + turns_ref[1:2, lanes]
        features[:, lanes] = sin_turns(t).astype(BF16)


def form_hots(columns, hot_ref, keyx_ref, keyy_ref, mkey, mquery):
    lane = lax.broadcasted_iota(jnp.int32, (1, LANES), 1)
    part = lane // BUCKETS
    cell = (lane % BUCKETS).astype(F32)
    is_x = jnp.where(columns[:, 4:5] == cell, 1.0, 0.0)
    is_y = jnp.where(columns[:, 5:6] == cell, 1.0, 0.0)
    hot_ref[...] = jnp.where(part % 2 == 0, is_x, is_y).astype(BF16)
    sign = jnp.where(part % 2 == 0, 1.0, -1.0)
    for odd in range(2):
        here = jnp.where(part // 2 == odd, sign, 0.0)
        keyx_ref[odd] = (is_x * here).astype(BF16)
        keyy_ref[odd] = (is_y * here).astype(BF16)
    doc = jnp.where(columns[:, 8:9] == lane.astype(F32), 1.0, 0.0)
    mkey[:, LANES:] = doc.astype(BF16)
    mquery[:, LANES:] = (jnp.where(lane < 4, 1.0 - doc, 0.0) * masked_score).astype(BF16)


def form_tables(tables, bands, tilted):
    row = lax.broadcasted_iota(jnp.int32, (LANES, 1), 0)
    half = BUCKETS // 2
    sub = lax.broadcasted_iota(jnp.int32, (8, LANES), 0)
    sub_wide = lax.broadcasted_iota(jnp.int32, (8, WIDE), 0)
    place = lax.broadcasted_iota(jnp.int32, (1, WIDE), 1)
    wanted = jnp.where(place < 5 * LANES, jnp.clip(place - 2 * LANES, -half, half - 1) + half, 0)
    lane = lax.broadcasted_iota(jnp.int32, (1, LANES), 1)
    turned = jnp.clip(64 - lane, -half, half - 1) + half
    for m in range(4):
        hot_band = jnp.where(row == wanted + m * BUCKETS, 1.0, 0.0).astype(BF16)
        got = matmul(tables, hot_band)
        for n in range(3):
            x = jnp.broadcast_to(got[n : n + 1, :], (8, WIDE))
            for bit in (1, 2, 4):
                x = jnp.where((sub_wide & bit) != 0, pltpu.roll(x, bit, 1), x)
            bands[4 * n + m] = x
        hot_turn = jnp.where(row == turned + m * BUCKETS, 1.0, 0.0).astype(BF16)
        got = matmul(tables, hot_turn)
        for t in (1, 2):
            for n in range(3):
                x = jnp.broadcast_to(got[3 * t + n : 3 * t + n + 1, :], (8, LANES))
                for bit in (1, 2, 4):
                    x = jnp.where((sub & bit) != 0, pltpu.roll(x, bit, 1), x)
                for group in range(BUCKETS // 8):
                    y = x if group == 0 else pltpu.roll(x, 8 * group, 1)
                    tilted[(t - 1) * HEADS + 4 * n + m, 8 * group : 8 * group + 8, :] = y


def pair_rows(tilted, pair):
    lane = lax.broadcasted_iota(jnp.int32, (1, LANES), 1)
    part = lane // BUCKETS
    x0, x1 = tilted[2 * pair], tilted[2 * pair + 1]
    y0, y1 = tilted[HEADS + 2 * pair], tilted[HEADS + 2 * pair + 1]

    def same(value, to):
        return value if to == 64 else pltpu.roll(value, (to - 64) % LANES, 1)

    def less(value, to):
        return pltpu.roll(value, (to - 65) % LANES, 1)

    zero = jnp.zeros_like(x0)
    base_x = jnp.where(part == 0, same(x1, 0), jnp.where(part == 2, same(x0, 64), zero))
    base_y = jnp.where(part == 1, same(y1, 32), jnp.where(part == 3, same(y0, 96), zero))

    def steps(even, odd):
        return jnp.where(
            part < 2,
            jnp.where(part == 0, less(even, 0), same(even, 32)),
            jnp.where(part == 2, less(odd, 64), same(odd, 96)),
        )

    rows = [
        jnp.concatenate([base_x, base_y], axis=0),
        jnp.concatenate([steps(x0, x1), zero], axis=0),
        jnp.concatenate([zero, steps(y0, y1)], axis=0),
    ]
    return jnp.concatenate(rows, axis=1).astype(BF16)


def gelu_and_slope(z):
    a = jnp.abs(z)
    t = 1.0 / (1.0 + (0.3275911 / math.sqrt(2.0)) * a)
    poly = 1.061405429 * 0.5
    for term in (-1.453152027, 1.421413741, -0.284496736, 0.254829592):
        poly = poly * t + 0.5 * term
    e = jnp.exp(-0.5 * z * z)
    tail = poly * t * e
    cdf = jnp.where(z < 0, tail, 1.0 - tail)
    return z * cdf, cdf + z * (e * (1.0 / math.sqrt(2.0 * math.pi)))


def forward_kernel(plan, params_in, hidden_in, cot_in, boxes, lengths, turns, *refs):
    (w_qkv_out, w_out_out, w_in_out, w_back_out, features_out, low_out, q_out, k_out, v_out, probs_out,
     context_out, hat_out, normed_out, vec_out, rstd_out, cot_ref, hot_out, rest_out, share_out) = refs[:19]
    refs = refs[19:]
    (flat, staged, own, w_qkv, w_out, w_box, w_in, w_back, notes, features, hidden, start, start_low, q_ref,
     k_ref, v_ref, hot_ref, key_x, key_y, bands, tilted, wides, scores, context_t, pair_t, hat, narrow,
     square, vec) = refs[:29]
    note_sems, swap_sems, copy_sems, probs_sems = refs[29:33]

    def lend(buffer, slot, lanes):
        return buffer.at[:, slot : slot + lanes]

    less_x, less_y = lend(square, 0, WINLEN), lend(square, WINLEN, WINLEN)
    probs = [lend(square, 2 * WINLEN, WINLEN), lend(square, 3 * WINLEN, WINLEN)]
    kaugs = [lend(narrow, 0, 2 * LANES), lend(narrow, 2 * LANES, 2 * LANES)]
    qaugs = [lend(narrow, 4 * LANES, 2 * LANES), lend(narrow, 6 * LANES, 2 * LANES)]
    met = lend(narrow, 8 * LANES, 3 * LANES)
    place = Place()
    normed_low = hidden
    context = features
    gathering = Gathering(place, flat, dict(zip(GATHER_SEMS, refs[33:])))
    matrices = (w_qkv, w_out, w_box, w_in, w_back)
    written = []

    def write_out(src, dst):
        copy = pltpu.make_async_copy(src, dst, copy_sems.at[len(written)])
        copy.start()
        written.append(copy)

    fetch = pltpu.make_async_copy(params_in, staged.at[: plan.rows], probs_sems.at[0])
    fetch.start()
    place.greet()
    fetch.wait()
    for quarter_at in range(COLUMNS):
        begin = quarter_at * plan.quarter
        own[quarter_at] = staged[begin : begin + plan.quarter, :].astype(BF16)
    gathering.spread(own, 0)
    gathering.spread(own, 1)

    quarter = WINLEN // DEPTH

    def exchange(source, target, kind):
        rows = pl.ds(pl.multiple_of(place.z * quarter, quarter), quarter)
        for d in range(DEPTH - 1):
            gathering_send(source.at[place.far[d]], target.at[rows], kind, d, place.peers_z[d])

    def gathering_send(src, dst, kind, d, peer):
        copy = remote(src, dst, swap_sems.at[kind, 0, d], swap_sems.at[kind, 1, d], peer)
        copy.start()
        gathering.sent.append(copy)

    def exchanged(target, kind):
        for d in range(DEPTH - 1):
            rows = pl.ds(pl.multiple_of(place.from_far[d] * quarter, quarter), quarter)
            remote(
                target.at[rows], target.at[rows], swap_sems.at[kind, 0, d], swap_sems.at[kind, 1, d],
                place.peer_x,
            ).wait_recv()

    finish_notes = spread_notes(place, own, notes, note_sems, plan)
    own_rows = pl.ds(pl.multiple_of(place.z * quarter, quarter), quarter)
    own_hidden = pltpu.make_async_copy(
        hidden_in.at[place.z], hidden.at[own_rows], swap_sems.at[0, 0, DEPTH - 1]
    )
    own_hidden.start()
    own_cot = pltpu.make_async_copy(
        cot_in.at[place.z], cot_ref.at[own_rows], swap_sems.at[1, 0, DEPTH - 1]
    )
    own_cot.start()
    gathering.spread_done(0)
    gathering.along_z(0, 0)
    gathering.spread_done(1)
    gathering.along_z(0, 1)

    rest, columns = token_columns(boxes, lengths, place.z)
    for part in range(BLOCKS):
        rows = slice(part * LANES, (part + 1) * LANES)
        for axis, less in ((0, less_x), (1, less_y)):
            less[rows, :] = jnp.where(
                rest[axis : axis + 1, :] < columns[rows, 6 + axis : 7 + axis], 1.0, 0.0
            ).astype(BF16)
    rest_out[...] = rest
    form_hots(columns, hot_ref, key_x, key_y, kaugs[0], qaugs[0])
    kaugs[1][:, LANES:] = kaugs[0][:, LANES:]
    qaugs[1][:, LANES:] = qaugs[0][:, LANES:]
    hot_out[...] = hot_ref[...]
    gathering.first(0, 0)
    gathering.along_z(1, 0)
    gathering.first(0, 1)
    gathering.along_z(1, 1)
    form_features(columns, turns, features)
    for n in range(D // LANES):
        rows = slice(n * LANES, (n + 1) * LANES)
        context_t[rows, :] = features[:, rows].T
    write_out(context_t, features_out)
    gathering.first(1, 0)
    exchange(hidden_in, hidden, 0)
    gathering.second(0, 0)
    gathering.first(1, 1)
    gathering.second(0, 1)
    _, _, note_row = note_place(plan)
    for row in range(VEC_ROWS):
        at = note_row + row
        vec[0:1, row * LANES : (row + 1) * LANES] = notes[at // 16 * 16 : at // 16 * 16 + 16, :].astype(
            F32
        )[at % 16 : at % 16 + 1, :]
    vec_out[...] = vec[...]
    table_row = note_row + VEC["tables"] // LANES
    assert table_row % 16 == 0
    form_tables(notes[table_row : table_row + 16, :], bands, tilted)

    gathering.third(0, 0)
    gathering.second(1, 0)
    gathering.third(0, 1)
    gathering.second(1, 1)
    gathering.complete(0)
    stage_column(plan, flat, staged, 0)
    exchanged(hidden, 0)
    gathering.along_z(2, 0)
    gathering.along_z(2, 1)
    form_matrices(plan, staged, matrices, 0)
    keep_carry(plan, staged)
    gathering.third(1, 0)
    gathering.third(1, 1)
    gathering.complete(1)
    stage_column(plan, flat, staged, 1)
    form_matrices(plan, staged, matrices, 1)
    keep_carry(plan, staged)
    write_out(w_qkv, w_qkv_out)
    write_out(w_out, w_out_out)

    own_hidden.wait()
    for n in range(D // NBLOCK):
        lanes = slice(n * NBLOCK, (n + 1) * NBLOCK)
        value = hidden[:, lanes].astype(F32) + matmul(features[...], w_box[:, lanes])
        start[:, lanes] = value
        start_low[:, lanes] = value.astype(BF16)
    write_out(start_low, low_out)
    written[0].wait()

    def project(n, carry):
        at = pl.multiple_of(n * NBLOCK, NBLOCK)
        lanes = pl.ds(at, NBLOCK)
        low = start_low[...]
        bias = vec[0:1, pl.ds(pl.multiple_of(VEC["q_bias"] + at, LANES), NBLOCK)]
        got = matmul(low, w_qkv[:, lanes]) + bias
        q_ref[:, lanes] = (got.astype(BF16).astype(F32) * HEAD_DIM ** (-0.5)).astype(BF16)
        k_ref[:, lanes] = matmul(low, w_qkv[:, pl.ds(pl.multiple_of(at + D, LANES), NBLOCK)]).astype(BF16)
        bias = vec[0:1, pl.ds(pl.multiple_of(VEC["v_bias"] + at, LANES), NBLOCK)]
        got = matmul(low, w_qkv[:, pl.ds(pl.multiple_of(at + 2 * D, LANES), NBLOCK)]) + bias
        v_ref[:, lanes] = got.astype(BF16)
        return carry

    lax.fori_loop(0, D // NBLOCK, project, 0)
    write_out(q_ref, q_out)
    write_out(k_ref, k_out)
    write_out(v_ref, v_out)
    gathering.first(2, 0)
    gathering.along_z(3, 0)
    gathering.first(2, 1)
    gathering.along_z(3, 1)

    low, high = half_masks()
    half = 2 * LANES

    def probs_copy(head, odd):
        return pltpu.make_async_copy(probs[odd], probs_out.at[head], probs_sems.at[odd])

    def one_pair(pair, carry):
        at = pl.multiple_of(pair * LANES, LANES)
        lanes = pl.ds(at, LANES)
        values_t = v_ref[:, lanes].T
        met[...] = matmul(hot_ref[:, :64], pair_rows(tilted, pair)).astype(BF16)
        for odd in range(2):
            mine, other = (low, high) if odd == 0 else (high, low)
            kaugs[odd][:, :LANES] = k_ref[:, lanes] * mine + hot_ref[...] * other
            qaugs[odd][:, :LANES] = q_ref[:, lanes] * mine + met[:, :LANES] * other
            skew_groups(bands[2 * pair + odd], wides.at[odd])

            @pl.when(pair > 0)
            def _():
                probs_copy(2 * pair + odd, odd).wait()

        for side in range(2):
            cols = slice(side * half, (side + 1) * half)
            tops = []
            for odd in range(2):
                top = None
                for part in range(BLOCKS):
                    rows = slice(part * LANES, (part + 1) * LANES)
                    bias = []
                    for block in range(2 * side, 2 * side + 2):
                        step = max(-2, min(2, block - part)) + 2
                        bias.append(wides[odd, :, step * LANES : (step + 1) * LANES])
                    s = times_transposed(kaugs[odd][rows, :], qaugs[odd][cols, :])
                    s = s + jnp.concatenate(bias, axis=1)
                    steps = times_transposed(key_x[odd, rows, :], met[cols, LANES : 2 * LANES])
                    s = s + steps * less_x[rows, cols].astype(F32)
                    steps = times_transposed(key_y[odd, rows, :], met[cols, 2 * LANES :])
                    s = s + steps * less_y[rows, cols].astype(F32)
                    scores[odd, rows, :] = s
                    best = jnp.max(s.reshape(LANES // 8, 8, half), axis=0)
                    top = best if top is None else jnp.maximum(top, best)
                tops.append(jnp.max(top, axis=0, keepdims=True))
            for odd in range(2):
                total = None
                for part in range(BLOCKS):
                    rows = slice(part * LANES, (part + 1) * LANES)
                    e = jnp.exp(scores[odd, rows, :] - tops[odd])
                    probs[odd][rows, cols] = e.astype(BF16)
                    add = jnp.sum(e.reshape(LANES // 8, 8, half), axis=0)
                    total = add if total is None else total + add
                share = 1.0 / jnp.sum(total, axis=0, keepdims=True)
                share_out[2 * pair + odd, :, cols] = share
                got = matmul(values_t[odd * HEAD_DIM : (odd + 1) * HEAD_DIM, :], probs[odd][:, cols])
                pair_t[odd * HEAD_DIM : (odd + 1) * HEAD_DIM, cols] = got * share
        for odd in range(2):
            probs_copy(2 * pair + odd, odd).start()
        both = pair_t[...]
        context_t[lanes, :] = both.astype(BF16)
        context[:, lanes] = both.T.astype(BF16)
        return carry

    lax.fori_loop(0, 2, one_pair, 0)
    gathering.second(2, 0)
    gathering.first(3, 0)
    gathering.second(2, 1)
    gathering.first(3, 1)
    exchange(cot_in, cot_ref, 1)
    lax.fori_loop(2, 4, one_pair, 0)
    for h in range(2):
        gathering.third(2, h)
        gathering.second(3, h)
    gathering.complete(2)
    stage_column(plan, flat, staged, 2)
    form_matrices(plan, staged, matrices, 2)
    keep_carry(plan, staged)
    write_out(w_in, w_in_out)
    lax.fori_loop(4, PAIRS, one_pair, 0)
    write_out(context_t, context_out)
    for h in range(2):
        gathering.third(3, h)

    def vector(name):
        return vec[0:1, VEC[name] : VEC[name] + D]

    for n in range(D // NBLOCK):
        lanes = slice(n * NBLOCK, (n + 1) * NBLOCK)
        bias = vec[0:1, VEC["out_bias"] + n * NBLOCK : VEC["out_bias"] + (n + 1) * NBLOCK]
        start[:, lanes] = start[:, lanes] + matmul(context[...], w_out[:, lanes]) + bias

    step_rows = 64

    def norm_first(n, carry):
        rows = pl.ds(pl.multiple_of(n * step_rows, step_rows), step_rows)
        x = start[rows, :]
        centred = x - jnp.mean(x, axis=1, keepdims=True)
        rstd = lax.rsqrt(jnp.mean(centred * centred, axis=1, keepdims=True) + norm_eps)
        xhat = centred * rstd
        hat[rows, :] = xhat
        rstd_out[rows, :] = jnp.broadcast_to(rstd, (step_rows, LANES))
        normed = xhat * vector("gain_one") + vector("shift_one")
        start[rows, :] = normed
        normed_low[rows, :] = normed.astype(BF16)
        return carry

    lax.fori_loop(0, WINLEN // step_rows, norm_first, 0)
    write_out(hat, hat_out)
    write_out(normed_low, normed_out)

    gathering.complete(3)
    stage_column(plan, flat, staged, 3)
    form_matrices(plan, staged, matrices, 3)
    write_out(w_back, w_back_out)
    for odd in range(2):
        probs_copy(0, odd).wait()
    exchanged(cot_ref, 1)
    own_cot.wait()
    for copy in written[1:]:
        copy.wait()
    finish_notes()
    gathering.finish()


def forward_pass(plan, params, hidden_in, cotangent, boxes, lengths):
    anywhere = pl.BlockSpec(memory_space=pl.ANY)
    vmem = pl.BlockSpec(memory_space=pltpu.VMEM)
    token = (WINLEN, D)

    def hbm(shape, dtype=BF16):
        return jax.ShapeDtypeStruct(shape, dtype), anywhere

    def near(shape, dtype=F32):
        return jax.ShapeDtypeStruct(shape, dtype), vmem

    outs = [
        hbm(MATRICES[0]), hbm(MATRICES[1]), hbm(MATRICES[3]), hbm(MATRICES[4]), hbm((D, WINLEN)), hbm(token),
        hbm(token), hbm(token), hbm(token), hbm((HEADS, WINLEN, WINLEN)), hbm((D, WINLEN)),
        hbm(token, F32), hbm(token), near((1, VEC_ROWS * LANES)), near((WINLEN, LANES)),
        near(token, BF16), near((WINLEN, LANES), BF16), near((2, WINLEN)),
        near((HEADS, 1, WINLEN)),
    ]
    scratch = [
        pltpu.VMEM((COLUMNS, CORES, DEPTH, COLUMNS, plan.quarter, LANES), BF16),
        pltpu.VMEM((plan.staged, LANES), F32),
        pltpu.VMEM((COLUMNS, plan.quarter, LANES), BF16),
    ]
    scratch += [pltpu.VMEM(layout, BF16) for layout in MATRICES]
    scratch += [
        pltpu.VMEM((NOTE_ROWS, LANES), BF16),
        pltpu.VMEM(token, BF16),
        pltpu.VMEM(token, BF16),
        pltpu.VMEM(token, F32),
        pltpu.VMEM(token, BF16),
        pltpu.VMEM(token, BF16),
        pltpu.VMEM(token, BF16),
        pltpu.VMEM(token, BF16),
        pltpu.VMEM((WINLEN, LANES), BF16),
        pltpu.VMEM((2, WINLEN, LANES), BF16),
        pltpu.VMEM((2, WINLEN, LANES), BF16),
        pltpu.VMEM((HEADS, 8, WIDE), F32),
        pltpu.VMEM((2 * HEADS, BUCKETS, LANES), F32),
        pltpu.VMEM((2, LANES, 5 * LANES), F32),
        pltpu.VMEM((2, WINLEN, 2 * LANES), F32),
        pltpu.VMEM((D, WINLEN), BF16),
        pltpu.VMEM((LANES, WINLEN), F32),
        pltpu.VMEM(token, F32),
        pltpu.VMEM((WINLEN, 11 * LANES), BF16),
        pltpu.VMEM((WINLEN, 4 * WINLEN), BF16),
        pltpu.VMEM((1, VEC_ROWS * LANES), F32),
        pltpu.SemaphoreType.DMA((2, 7)),
        pltpu.SemaphoreType.DMA((2, 2, DEPTH)),
        pltpu.SemaphoreType.DMA((16,)),
        pltpu.SemaphoreType.DMA((2,)),
    ]
    return pl.pallas_call(
        functools.partial(forward_kernel, plan),
        out_shape=[shape for shape, _ in outs],
        in_specs=[anywhere] * 3 + [vmem, pl.BlockSpec(memory_space=pltpu.SMEM), vmem],
        out_specs=[spec for _, spec in outs],
        scratch_shapes=scratch + sem_shapes(GATHER_SEMS),
        compiler_params=pltpu.CompilerParams(
            collective_id=0, has_side_effects=True, vmem_limit_bytes=62 * 2**20
        ),
        name="forward_pass",
    )(params, hidden_in, cotangent, boxes, lengths, jnp.asarray(turns_table()))


def token_info(doc_lengths, box_coords):
    places = jnp.arange(WINLEN, dtype=jnp.int32)
    first = places == 0
    doc = jnp.zeros((WINLEN,), jnp.int32)
    end = 0
    for d in range(3):
        end = end + doc_lengths[d]
        doc = doc + (places >= end).astype(jnp.int32)
        first = first | (places == end)
    rows = [box_coords[:, c] for c in range(4)] + [doc, first.astype(jnp.int32)]
    return jnp.stack(rows + [jnp.zeros_like(doc)] * 2).astype(F32)


class Reducing:
    def __init__(self, place, flat, swapped, one, two, deep, piece, result, sems, free):
        self.place = place
        self.flat = flat
        self.swapped = swapped
        self.one = one
        self.two = two
        self.deep = deep
        self.piece = piece
        self.result = result
        self.sems = sems
        self.free = free
        self.sent = {k: [] for k in range(COLUMNS)}

    def send(self, k, src, dst, kind, index, peer):
        copy = remote(src, dst, self.sems[kind].at[0, index], self.sems[kind].at[1, index], peer)
        copy.start()
        self.sent[k].append(copy)

    got = Gathering.got

    def settle(self, k):
        for copy in self.sent.pop(k):
            copy.wait_send()

    rows = Gathering.rows

    def swap(self, k, h):
        p = self.place
        slot = k % 2
        if k < 2 and h == 0:
            pl.semaphore_wait(self.free.at[slot], 1)
        self.send(
            k, self.flat.at[slot, 1 - p.core, :, :, self.rows(h)],
            self.swapped.at[slot, :, :, self.rows(h)], "core", 2 * k + h, p.peer_core,
        )

    def first(self, k, h):
        p = self.place
        slot = k % 2
        n, rows = 2 * k + h, self.rows(h)
        self.got(self.swapped.at[slot, :, :, rows], "core", n)

        def one(step, carry):
            z, quarter = step // COLUMNS, step % COLUMNS
            total = self.flat[slot, p.core, z, quarter, rows].astype(F32)
            total = total + self.swapped[slot, z, quarter, rows].astype(F32)
            self.flat[slot, p.core, z, quarter, rows] = total.astype(BF16)
            return carry

        lax.fori_loop(0, DEPTH * COLUMNS, one, 0)
        flat = self.flat
        for side, peer in ((0, p.peer_y), (1, p.peer_x)):
            self.send(
                k, flat.at[slot, p.core, 2 * side : 2 * side + 2, p.col_d, rows],
                self.one.at[k, side, :, rows], "one", 2 * n + side, peer,
            )
        if k >= 2 and h == 1:
            pl.semaphore_signal(
                self.free.at[slot], inc=1, device_id=p.peer_core, device_id_type=MESH
            )

    def second(self, k, h):
        p = self.place
        slot = k % 2
        n, rows = 2 * k + h, self.rows(h)
        for side, column in ((0, p.col_x), (1, p.col_y)):
            self.got(self.one.at[k, side, :, rows], "one", 2 * n + side)

            def one(step, carry, side=side, column=column):
                z = 2 * side + step
                total = self.flat[slot, p.core, z, column, rows].astype(F32)
                total = total + self.one[k, side, step, rows].astype(F32)
                self.flat[slot, p.core, z, column, rows] = total.astype(BF16)
                return carry

            lax.fori_loop(0, 2, one, 0)
        for side, column, peer in ((0, p.col_x, p.peer_x), (1, p.col_y, p.peer_y)):
            self.send(
                k, self.flat.at[slot, p.core, :, column, rows], self.two.at[k, side, :, rows], "two",
                2 * n + side, peer,
            )

    def third(self, k, h):
        p = self.place
        slot = k % 2
        n, rows = 2 * k + h, self.rows(h)
        for side in range(2):
            self.got(self.two.at[k, side, :, rows], "two", 2 * n + side)

        def one(z, carry):
            total = self.flat[slot, p.core, z, p.column, rows].astype(F32)
            total = total + self.two[k, 0, z, rows].astype(F32) + self.two[k, 1, z, rows].astype(F32)
            self.flat[slot, p.core, z, p.column, rows] = total.astype(BF16)
            return carry

        lax.fori_loop(0, DEPTH, one, 0)
        for d in range(DEPTH - 1):
            self.send(
                k, self.flat.at[slot, p.core, p.far[d], p.column, rows], self.deep.at[k, d, rows], "z",
                3 * n + d, p.peers_z[d],
            )

    def fourth(self, k, h):
        p = self.place
        n, rows = 2 * k + h, self.rows(h)
        for d in range(DEPTH - 1):
            self.got(self.deep.at[k, d, rows], "z", 3 * n + d)
        total = self.flat[k % 2, p.core, p.z, p.column, rows].astype(F32)
        for d in range(DEPTH - 1):
            total = total + self.deep[k, d, rows].astype(F32)
        self.piece[k, rows] = total.astype(BF16)

    def giving(self, k, h):
        p = self.place
        sems = self.sems["spread"]
        return remote(
            self.piece.at[k, self.rows(h)], self.result.at[p.column, self.rows(h)],
            sems.at[0, 2 * k + h], sems.at[1, 2 * p.column + h], p.at(k, p.core, p.z),
        )

    def give(self, k, h):
        @pl.when(self.place.column != k)
        def _():
            self.giving(k, h).start()

    def given(self, k, h):
        @pl.when(self.place.column != k)
        def _():
            self.giving(k, h).wait_send()

    def receive(self, out):
        p = self.place
        out[p.column] = self.piece[p.column].astype(F32)
        for column in (p.col_x, p.col_y, p.col_d):
            for h in range(2):
                self.got(self.result.at[column, self.rows(h)], "spread", 2 * column + h)
            out[column] = self.result[column].astype(F32)


REDUCE_SEMS = {"spread": 8, "z": 24, "one": 16, "two": 16, "core": 8}


def unstage_column(plan, flat, staged, k):
    def one(step, carry):
        shard, quarter = step // COLUMNS, step % COLUMNS
        base = plan.carry + shard * plan.rows + quarter * plan.quarter
        piece = staged[pl.ds(pl.multiple_of(base, 8), plan.quarter), :]
        flat[k % 2, shard // DEPTH, shard % DEPTH, quarter] = piece.astype(BF16)
        return carry

    lax.fori_loop(0, CORES * DEPTH * COLUMNS, one, 0)


class Notes:
    def __init__(self, place, notes, slots, sems):
        self.place, self.notes, self.slots, self.sems = place, notes, slots, sems
        p = place
        self.home = (p.column == COLUMNS - 1) & (p.core == CORES - 1)
        self.root = self.home & (p.z == DEPTH - 1)

    def copy(self, slot, peer):
        return remote(
            self.notes, self.slots.at[slot], self.sems.at[0, 0], self.sems.at[1, slot], peer
        )

    def take(self, slot):
        self.copy(slot, self.place.peer_core).wait_recv()
        self.notes[...] = self.notes[...] + self.slots[slot]

    def start(self):
        p = self.place

        @pl.when(p.core != CORES - 1)
        def _():
            self.copy(0, p.peer_core).start()

    def rise(self):
        p = self.place

        @pl.when(p.core == CORES - 1)
        def _():
            self.take(0)

        @pl.when((p.core == CORES - 1) & (p.column != COLUMNS - 1))
        def _():
            self.copy(1 + p.column, p.at(COLUMNS - 1, p.core, p.z)).start()

    def end(self):
        p = self.place

        @pl.when(self.home)
        def _():
            for slot in range(1, 4):
                self.take(slot)

        @pl.when(self.home & (p.z != DEPTH - 1))
        def _():
            self.copy(4 + p.z, p.at(p.column, p.core, DEPTH - 1)).start()

        @pl.when(self.root)
        def _():
            for slot in range(4, 7):
                self.take(slot)

        @pl.when(jnp.logical_not(self.root))
        def _():
            self.copy(0, p.peer_core).wait_send()


def cell_sums(whole, less):
    lane = lax.broadcasted_iota(jnp.int32, (1, LANES), 1)
    sub = lax.broadcasted_iota(jnp.int32, (8, LANES), 0)
    sums = []
    for axis in range(2):
        rows = slice(axis * BUCKETS, (axis + 1) * BUCKETS)
        every = pltpu.roll(whole[rows], (BUCKETS - axis * BUCKETS) % LANES, 1)
        below = pltpu.roll(less[rows], (BUCKETS - axis * BUCKETS) % LANES, 1)
        inside = (lane >= BUCKETS) & (lane < 2 * BUCKETS)
        every = jnp.where(inside, every, 0.0)
        below = jnp.where(inside, below, 0.0)
        x = every - below + pltpu.roll(below, LANES - 1, 1)
        total = None
        for group in range(BUCKETS // 8):
            y = x[8 * group : 8 * group + 8]
            y = y if group == 0 else pltpu.roll(y, LANES - 8 * group, 1)
            total = y if total is None else total + y
        for bit in (1, 2, 4):
            total = jnp.where((sub & bit) != 0, pltpu.roll(total, LANES - bit, 1), total)
        sums.append(jnp.sum(total, axis=0, keepdims=True))
    return sums


def exact_dot(a, b):
    return jnp.dot(a, b, preferred_element_type=F32, precision=lax.Precision.HIGHEST)


def bucket_rows(cell_ref, diag_ref):
    half = BUCKETS // 2
    column = lax.broadcasted_iota(jnp.int32, (1, LANES), 1)
    row = lax.broadcasted_iota(jnp.int32, (LANES, 1), 0)
    to = jnp.clip(row - BUCKETS, -half, half - 1) + half
    place = lax.broadcasted_iota(jnp.int32, (WIDE, 1), 0)
    along = place - LANES
    far = jnp.where(place < LANES, 0, jnp.where(place < 5 * LANES, 0, BUCKETS - 1))
    along = jnp.where(
        (place >= LANES) & (place < 4 * LANES),
        jnp.clip(along - LANES, -half, half - 1) + half,
        far,
    )
    first, rest = None, None
    zero = jnp.zeros((5, WIDE), F32)
    for m in range(4):
        hot_along = jnp.where(along + m * BUCKETS == column, 1.0, 0.0)
        got = exact_dot(
            jnp.concatenate([diag_ref[4 * n + m] for n in range(3)] + [zero], axis=0), hot_along
        )
        first = got if first is None else first + got
        hot_cell = jnp.where(to + m * BUCKETS == column, 1.0, 0.0)
        rows = [cell_ref[t * HEADS + 4 * n + m] for t in range(2) for n in range(3)]
        got = exact_dot(jnp.concatenate(rows + [zero[:2, :LANES]], axis=0), hot_cell)
        rest = got if rest is None else rest + got
    return jnp.concatenate([first[:3], rest[:6]], axis=0)


def backward_kernel(
    plan, w_back_in, w_in_in, w_out_in, w_qkv_in, normed_in, low_in, features_in,
    context_in, q_in, k_in, v_in, probs_in, hat_in, cot_in, rstd_ref, vec, hot_ref, rest_ref, share_ref,
    *refs,
):
    out, output_pos, hidden_pos, spill = refs[:4]
    (flat, staged, swapped, one_buf, two_buf, deep, piece, result, active, slope, w_back, w_in, w_out,
     turned, context_t, q_ref, k_ref, v_ref, hat, second, branch, dctx, probs, less_x,
     less_y, scores_odd, bands, hot_t, pair_t, scaled, share_cols, vecg, cell_rows, diag_rows, notes, slots,
     ) = refs[4:40]
    load_sems, probs_sems, free, pos_sems, note_sems, spill_sems = refs[40:46]
    place = Place()
    reducing = Reducing(
        place, flat, swapped, one_buf, two_buf, deep, piece, result,
        dict(zip(REDUCE_SEMS, refs[46:])), free,
    )
    climbing = Notes(place, notes, slots, note_sems)
    loads = {}

    def load(name, src, dst):
        loads[name] = pltpu.make_async_copy(src, dst, load_sems.at[len(loads)])
        loads[name].start()

    mixed = active.at[:, : 3 * D]
    grad_attn = branch
    w_qkv = w_in.at[:, : 3 * D]
    hidden_low = dctx
    features_t = w_back.at[:D, :WINLEN]
    low_t = w_out.at[:WINLEN]
    scores = [hat.at[:, :WINLEN], scores_odd]
    dscores = [w_back.at[2 * WINLEN : 3 * WINLEN, :WINLEN], w_back.at[3 * WINLEN : 4 * WINLEN, :WINLEN]]
    low_turned = w_back.at[4 * WINLEN : 4 * WINLEN + D, :WINLEN]
    output_low = w_out.at[:WINLEN]
    output_low = w_out.at[:WINLEN]
    dscores_x = [slope.at[:, 2 * WINLEN : 3 * WINLEN], slope.at[:, 3 * WINLEN : 4 * WINLEN]]
    dscores_y = [slope.at[:, 4 * WINLEN : 5 * WINLEN], slope.at[:, 5 * WINLEN :]]

    load("normed", normed_in, dctx)
    load("w_in", w_in_in, w_in)

    at = staged_at(plan, COLUMNS - 1, plan.misc_start)
    staged[at:, :] = jnp.zeros((plan.staged - at, LANES), F32)
    place.greet()

    quarter = WINLEN // DEPTH
    positions = []

    def to_pos(source, target, kind):
        for d in range(DEPTH - 1):
            rows = pl.ds(pl.multiple_of(place.far[d] * quarter, quarter), quarter)
            copy = remote(
                source.at[rows], target.at[place.z], pos_sems.at[kind, 0, d], pos_sems.at[kind, 1, d],
                place.peers_z[d],
            )
            copy.start()
            positions.append(copy)
        rows = pl.ds(pl.multiple_of(place.z * quarter, quarter), quarter)
        copy = pltpu.make_async_copy(
            source.at[rows], target.at[place.z], pos_sems.at[kind, 0, DEPTH - 1]
        )
        copy.start()
        return copy

    def in_pos(target, kind):
        for d in range(DEPTH - 1):
            there = target.at[place.from_far[d]]
            remote(
                there, there, pos_sems.at[kind, 0, d], pos_sems.at[kind, 1, d], place.peer_x
            ).wait_recv()


    def store(k, index, row, value, first_block=0):
        blocks = MATRICES[index][1] // LANES
        base = staged_at(plan, k, plan.starts[index]) + row * blocks + first_block
        for block in range(value.shape[1] // LANES):
            staged[pl.ds(base + block, value.shape[0], stride=blocks), :] = value[
                :, block * LANES : (block + 1) * LANES
            ]

    def column_sum(value):
        return jnp.sum(value, axis=0, keepdims=True)

    def keep_vector(name, lanes_at, value):
        at = pl.multiple_of(VEC[name] + lanes_at, LANES)
        vecg[0:1, pl.ds(at, value.shape[1])] = value

    def vector(name, at=0, size=D):
        return vec[0:1, pl.ds(pl.multiple_of(VEC[name] + at, LANES), size)]

    loads["normed"].wait()
    loads["w_in"].wait()
    load("w_back", w_back_in, w_back)
    load("hat", hat_in, hat)
    load("cot", cot_in, branch)

    def widen(n, carry):
        at = pl.multiple_of(n * NBLOCK, NBLOCK)
        lanes = pl.ds(at, NBLOCK)
        inner_act = matmul(dctx[...], w_in[:, lanes]) + vector("in_bias", at, NBLOCK)
        value, change = gelu_and_slope(inner_act)
        active[:, lanes] = value.astype(BF16)
        slope[:, lanes] = change.astype(BF16)
        return carry

    lax.fori_loop(0, FF // NBLOCK, widen, 0, unroll=2)
    loads["hat"].wait()
    loads["w_back"].wait()
    for n in range(D // NBLOCK):
        lanes = slice(n * NBLOCK, (n + 1) * NBLOCK)
        normed = hat[:, lanes] * vector("gain_one", n * NBLOCK, NBLOCK) + vector(
            "shift_one", n * NBLOCK, NBLOCK
        )
        second[:, lanes] = (
            normed + matmul(active[...], w_back[:, lanes]) + vector("back_bias", n * NBLOCK, NBLOCK)
        )
    loads["cot"].wait()
    step_rows = 64
    for name in ("gain_two", "shift_two", "back_bias", "gain_one", "shift_one", "out_bias"):
        keep_vector(name, 0, jnp.zeros((1, D), F32))

    def add_vector(name, term):
        lanes = slice(VEC[name], VEC[name] + D)
        vecg[0:1, lanes] = vecg[0:1, lanes] + column_sum(term)

    def norm_second(n, carry):
        rows = pl.ds(pl.multiple_of(n * step_rows, step_rows), step_rows)
        x = second[rows, :]
        centred = x - jnp.mean(x, axis=1, keepdims=True)
        rstd = lax.rsqrt(jnp.mean(centred * centred, axis=1, keepdims=True) + norm_eps)
        xhat = centred * rstd
        gain = vector("gain_two")
        output_low[rows, :] = (xhat * gain + vector("shift_two")).astype(BF16)
        cot = branch[rows, :].astype(F32)
        prod = cot * xhat
        gc = cot * gain
        mean_one = jnp.mean(gc, axis=1, keepdims=True)
        mean_two = jnp.mean(prod * gain, axis=1, keepdims=True)
        value = rstd * (gc - mean_one - xhat * mean_two)
        second[rows, :] = value
        value = value.astype(BF16)
        branch[rows, :] = value
        add_vector("gain_two", prod)
        add_vector("shift_two", cot)
        add_vector("back_bias", value.astype(F32))
        return carry

    lax.fori_loop(0, WINLEN // step_rows, norm_second, 0, unroll=2)
    own_output = to_pos(output_low, output_pos, 0)

    def back_rows(k, size, begin, count):
        def body(n, carry):
            row = pl.multiple_of(begin + n * size, LANES)
            turned[:size, :] = active[:, pl.ds(row, size)].T
            store(k, 4, row, matmul(turned[:size, :], branch[...]))
            return carry

        lax.fori_loop(0, count, body, 0)

    back_rows(3, WINLEN, 512, FF // WINLEN - 1)
    unstage_column(plan, flat, staged, 3)
    reducing.swap(3, 0)
    reducing.swap(3, 1)

    back_rows(2, WINLEN, 0, 1)
    back_rows(2, LANES, 512, 1)

    def inner(n, carry):
        at = pl.multiple_of(n * NBLOCK, NBLOCK)
        lanes = pl.ds(at, NBLOCK)
        value = times_transposed(branch[...], w_back[lanes, :]) * slope[:, lanes].astype(F32)
        value = value.astype(BF16)
        slope[:, lanes] = value
        keep_vector("in_bias", at, column_sum(value.astype(F32)))
        return carry

    lax.fori_loop(0, FF // NBLOCK, inner, 0, unroll=2)
    grad_inner = slope
    reducing.first(3, 0)
    reducing.first(3, 1)

    for n in range(D // NBLOCK):
        rows = slice(n * NBLOCK, (n + 1) * NBLOCK)
        turned[rows, :] = dctx[:, rows].T

    def in_rows(k, begin, end):
        def body(n, carry):
            lanes = pl.ds(pl.multiple_of(n * NBLOCK, NBLOCK), NBLOCK)
            got = matmul(turned[begin:end, :], grad_inner[:, lanes])
            store(k, 3, begin, got, n * (NBLOCK // LANES))
            return carry

        lax.fori_loop(0, FF // NBLOCK, body, 0)

    in_rows(2, 288, D)
    unstage_column(plan, flat, staged, 2)
    reducing.swap(2, 0)
    reducing.swap(2, 1)
    reducing.second(3, 0)
    reducing.second(3, 1)

    load("context", context_in, context_t)
    load("q", q_in, q_ref)
    load("k", k_in, k_ref)
    load("v", v_in, v_ref)
    for odd in range(2):
        pltpu.make_async_copy(probs_in.at[odd], probs.at[odd], probs_sems.at[odd]).start()
    for n in range(D // NBLOCK):
        lanes = slice(n * NBLOCK, (n + 1) * NBLOCK)
        second[:, lanes] = second[:, lanes] + times_transposed(grad_inner[...], w_in[lanes, :])
    load("w_qkv", w_qkv_in, w_qkv)
    load("features", features_in, features_t)
    reducing.first(2, 0)
    reducing.first(2, 1)

    for copy in positions:
        copy.wait_send()
    own_output.wait()
    load("w_out", w_out_in, w_out)

    def norm_first(n, carry):
        rows = pl.ds(pl.multiple_of(n * step_rows, step_rows), step_rows)
        grad = second[rows, :]
        xhat = hat[rows, :]
        prod = grad * xhat
        gain = vec[0:1, VEC["gain_one"] : VEC["gain_one"] + D]
        gc = grad * gain
        mean_one = jnp.mean(gc, axis=1, keepdims=True)
        mean_two = jnp.mean(prod * gain, axis=1, keepdims=True)
        value = rstd_ref[rows, 0:1] * (gc - mean_one - xhat * mean_two)
        second[rows, :] = value
        value = value.astype(BF16)
        grad_attn[rows, :] = value
        add_vector("gain_one", prod)
        add_vector("shift_one", grad)
        add_vector("out_bias", value.astype(F32))
        return carry

    lax.fori_loop(0, WINLEN // step_rows, norm_first, 0, unroll=2)
    reducing.third(3, 0)
    reducing.third(3, 1)
    loads["w_out"].wait()
    for n in range(D // NBLOCK):
        lanes = slice(n * NBLOCK, (n + 1) * NBLOCK)
        dctx[:, lanes] = times_transposed(grad_attn[...], w_out[lanes, :]).astype(BF16)
    load("low", low_in, low_t)
    loads["context"].wait()
    reducing.second(2, 0)
    reducing.second(2, 1)

    def out_rows(k, begin, end):
        for n in range(D // NBLOCK):
            lanes = slice(n * NBLOCK, (n + 1) * NBLOCK)
            got = matmul(context_t[begin:end, :], grad_attn[:, lanes])
            store(k, 1, begin, got, n * (NBLOCK // LANES))

    reducing.fourth(3, 0)
    reducing.fourth(3, 1)
    reducing.give(3, 0)
    reducing.give(3, 1)

    low, high = half_masks()
    rest = rest_ref[...]
    columns = jnp.concatenate([rest, jnp.zeros((LANES - 2, WINLEN), F32)], axis=0).T
    for part in range(BLOCKS):
        rows = slice(part * LANES, (part + 1) * LANES)
        for axis, less in ((0, less_x), (1, less_y)):
            less[rows, :] = jnp.where(
                rest[axis : axis + 1, :] < columns[rows, axis : axis + 1], 1.0, 0.0
            ).astype(BF16)
    hot_t[...] = hot_ref[...].T
    lane = lax.broadcasted_iota(jnp.int32, (1, LANES), 1)
    scale = HEAD_DIM ** (-0.5)
    of_x = jnp.where((lane // BUCKETS) % 2 == 0, 1.0, 0.0)
    share_cols[...] = jnp.concatenate(
        [share_ref[head] for head in range(HEADS)] + [jnp.zeros((LANES - HEADS, WINLEN), F32)], axis=0
    ).T
    for name in ("q", "k", "v"):
        loads[name].wait()

    def probs_copy(head, odd):
        return pltpu.make_async_copy(probs_in.at[head], probs.at[odd], probs_sems.at[odd])

    def spill_copy(head, odd):
        return pltpu.make_async_copy(dscores[odd], spill.at[head], spill_sems.at[odd])

    def one_pair(pair, carry):
        at = pl.multiple_of(pair * LANES, LANES)
        lanes = pl.ds(at, LANES)
        keys_t = k_ref[:, lanes].T
        both = pltpu.roll(share_cols[...], lax.rem(LANES - 2 * pair, LANES), 1)
        both = jnp.where(lane < HEAD_DIM, both[:, 0:1], both[:, 1:2])
        scaled[...] = (dctx[:, lanes].astype(F32) * both).astype(BF16)
        grad_context = dctx[:, lanes]
        dots = []
        for odd in range(2):
            mine, other = (low, high) if odd == 0 else (high, low)
            head = 2 * pair + odd
            probs_copy(head, odd).wait()
            dot = None
            for part in range(BLOCKS):
                rows = slice(part * LANES, (part + 1) * LANES)
                dp = times_transposed(v_ref[rows, lanes] * mine, grad_context)
                scores[odd][rows, :] = dp
                add = dp * probs[odd, rows, :].astype(F32)
                add = jnp.sum(add.reshape(LANES // 8, 8, WINLEN), axis=0)
                dot = add if dot is None else dot + add
            dots.append(column_sum(dot) * share_ref[head])
        for odd in range(2):
            head = 2 * pair + odd
            share = share_ref[head]

            @pl.when(pair > 0)
            def _():
                spill_copy(head, odd).wait()

            for part in range(BLOCKS):
                rows = slice(part * LANES, (part + 1) * LANES)
                ds = probs[odd, rows, :].astype(F32) * ((scores[odd][rows, :] - dots[odd]) * share)
                dscores[odd][rows, :] = ds.astype(BF16)
            spill_copy(head, odd).start()
        for odd in range(2):
            head = 2 * pair + odd
            keys_grad = matmul(dscores[odd][...], q_ref[:, lanes])
            values_grad = matmul(probs[odd], scaled[...])

            pair_t[odd * HEAD_DIM : (odd + 1) * HEAD_DIM, :] = matmul(
                keys_t[odd * HEAD_DIM : (odd + 1) * HEAD_DIM, :], dscores[odd][...]
            )
            for which, value in ((1, keys_grad), (2, values_grad)):
                there = pl.ds(pl.multiple_of(at + which * D, LANES), LANES)
                value = value.astype(BF16)
                if odd:
                    value = mixed[:, there] * low + value * high
                mixed[:, there] = value

        @pl.when(pair < PAIRS - 1)
        def _():
            for odd in range(2):
                probs_copy(2 * pair + odd + 2, odd).start()

        value = (pair_t[...].T * scale).astype(BF16)
        mixed[:, lanes] = value
        keep_vector("q_bias", at, column_sum(value.astype(F32)))
        there = pl.ds(pl.multiple_of(at + 2 * D, LANES), LANES)
        keep_vector("v_bias", at, column_sum(mixed[:, there].astype(F32)))
        return carry

    lax.fori_loop(0, 2, one_pair, 0)
    reducing.third(2, 0)
    reducing.third(2, 1)
    lax.fori_loop(2, 4, one_pair, 0)
    reducing.fourth(2, 0)
    reducing.fourth(2, 1)
    reducing.give(2, 0)
    reducing.give(2, 1)
    lax.fori_loop(4, PAIRS, one_pair, 0)

    for odd in range(2):
        spill_copy(0, odd).wait()
    loads["low"].wait()
    for n in range(D // NBLOCK):
        rows = slice(n * NBLOCK, (n + 1) * NBLOCK)
        low_turned[rows, :] = low_t[:, rows].T

    def qkv_rows(n, carry):
        lanes = pl.ds(pl.multiple_of(n * NBLOCK, NBLOCK), NBLOCK)
        store(0, 0, 0, matmul(low_turned[...], mixed[:, lanes]), n * (NBLOCK // LANES))
        return carry

    lax.fori_loop(0, 3 * D // NBLOCK, qkv_rows, 0)
    out_rows(0, 0, 208)
    reducing.settle(2)
    unstage_column(plan, flat, staged, 0)
    reducing.swap(0, 0)
    reducing.swap(0, 1)

    loads["w_qkv"].wait()
    for n in range(D // NBLOCK):
        lanes = slice(n * NBLOCK, (n + 1) * NBLOCK)
        value = second[:, lanes] + times_transposed(mixed[...], w_qkv[lanes, :])
        hidden_low[:, lanes] = value.astype(BF16)
    own_hidden = to_pos(hidden_low, hidden_pos, 1)
    reducing.first(0, 0)
    reducing.first(0, 1)
    loads["features"].wait()
    for n in range(D // NBLOCK):
        lanes = slice(n * NBLOCK, (n + 1) * NBLOCK)
        store(1, 2, 0, matmul(features_t[...], hidden_low[:, lanes]), n * (NBLOCK // LANES))
    in_rows(1, 0, 304)
    out_rows(1, 192, D)
    reducing.settle(3)
    unstage_column(plan, flat, staged, 1)
    reducing.swap(1, 0)
    reducing.swap(1, 1)
    reducing.second(0, 0)
    reducing.second(0, 1)

    def fetch_scores(head):
        there = slope.at[:, pl.ds(pl.multiple_of(lax.rem(head, 2) * WINLEN, WINLEN), WINLEN)]
        return pltpu.make_async_copy(spill.at[head], there, spill_sems.at[lax.rem(head, 2)])

    cells = [hot_ref[...] * of_x.astype(BF16), hot_ref[...] * (1.0 - of_x).astype(BF16)]
    band = bands.at[0]
    parts_x = slope.at[:, 2 * WINLEN : 3 * WINLEN]
    parts_y = slope.at[:, 3 * WINLEN : 4 * WINLEN]

    def one_table(head, carry):
        fetch_scores(head).wait()

        @pl.when(head < HEADS - 1)
        def _():
            fetch_scores(head + 1).start()

        here = slope.at[:, pl.ds(pl.multiple_of(lax.rem(head, 2) * WINLEN, WINLEN), WINLEN)]
        band[...] = jnp.zeros_like(band)
        for part in range(BLOCKS):
            rows = slice(part * LANES, (part + 1) * LANES)
            low_ds = here[rows, :]
            parts_x[rows, :] = low_ds * less_x[rows, :]
            parts_y[rows, :] = low_ds * less_y[rows, :]
            ds = low_ds.astype(F32)
            for block in range(BLOCKS):
                step = max(-2, min(2, block - part)) + 2
                where = slice(step * LANES, (step + 1) * LANES)
                band[:, where] = band[:, where] + ds[:, block * LANES : (block + 1) * LANES]
        whole = matmul(here[...], hot_ref[...])
        less = matmul(parts_x[...], cells[0]) + matmul(parts_y[...], cells[1])
        diag_rows[head, :, LANES : 5 * LANES] = diagonal_sums(band)
        diag_rows[head, :, :LANES] = column_sum(band[:, :LANES])
        diag_rows[head, :, 5 * LANES :] = column_sum(band[:, 4 * LANES :])
        sums = []
        for summed in (whole, less):
            first = summed.astype(BF16)
            remainder = (summed - first.astype(F32)).astype(BF16)
            sums.append(matmul(hot_t[:64, :], first) + matmul(hot_t[:64, :], remainder))
        for axis, value in enumerate(cell_sums(sums[0], sums[1])):
            cell_rows[axis * HEADS + head] = value
        return carry

    fetch_scores(0).start()
    reducing.first(1, 0)
    reducing.first(1, 1)
    lax.fori_loop(0, 4, one_table, 0)
    reducing.third(0, 0)
    reducing.second(1, 0)
    reducing.third(0, 1)
    reducing.second(1, 1)
    lax.fori_loop(4, 8, one_table, 0)
    reducing.fourth(0, 0)
    reducing.give(0, 0)
    reducing.third(1, 0)
    reducing.fourth(0, 1)
    reducing.give(0, 1)
    lax.fori_loop(8, HEADS, one_table, 0)
    notes[...] = jnp.zeros_like(notes)
    table = VEC["tables"] // LANES
    for row in range(table):
        notes[row : row + 1, :] = vecg[0:1, row * LANES : (row + 1) * LANES]
    notes[table : table + 9, :] = bucket_rows(cell_rows, diag_rows)
    climbing.start()
    reducing.third(1, 1)
    climbing.rise()
    reducing.fourth(1, 0)
    reducing.give(1, 0)
    climbing.end()
    reducing.fourth(1, 1)
    reducing.give(1, 1)
    reducing.receive(out)
    note_quarter, note_first, note_row = note_place(plan)
    base = note_first + note_row

    @pl.when(climbing.root)
    def _():
        out[note_quarter, base : base + MISC_ROWS, :] = (
            out[note_quarter, base : base + MISC_ROWS, :] + notes[:MISC_ROWS, :]
        )

    in_pos(output_pos, 0)
    in_pos(hidden_pos, 1)
    own_hidden.wait()
    for copy in positions[DEPTH - 1 :]:
        copy.wait_send()
    for k in range(COLUMNS):
        for h in range(2):
            reducing.given(k, h)
    reducing.settle(1)
    reducing.settle(0)


def backward_pass(plan, operands):
    anywhere = pl.BlockSpec(memory_space=pl.ANY)
    vmem = pl.BlockSpec(memory_space=pltpu.VMEM)
    token = (WINLEN, D)
    block = (plan.quarter, LANES)
    positions = jax.ShapeDtypeStruct((DEPTH, WINLEN // DEPTH, D), BF16)
    scratch = [
        pltpu.VMEM((2, CORES, DEPTH, COLUMNS) + block, BF16),
        pltpu.VMEM((plan.staged, LANES), F32),
        pltpu.VMEM((2, DEPTH, COLUMNS) + block, BF16),
        pltpu.VMEM((COLUMNS, 2, 2) + block, BF16),
        pltpu.VMEM((COLUMNS, 2, DEPTH) + block, BF16),
        pltpu.VMEM((COLUMNS, DEPTH - 1) + block, BF16),
        pltpu.VMEM((COLUMNS,) + block, BF16),
        pltpu.VMEM((COLUMNS,) + block, BF16),
        pltpu.VMEM((WINLEN, FF), BF16),
        pltpu.VMEM((WINLEN, FF), BF16),
        pltpu.VMEM((FF, D), BF16),
        pltpu.VMEM((D, FF), BF16),
        pltpu.VMEM((D, D), BF16),
        pltpu.VMEM((D, WINLEN), BF16),
        pltpu.VMEM((D, WINLEN), BF16),
        pltpu.VMEM(token, BF16),
        pltpu.VMEM(token, BF16),
        pltpu.VMEM(token, BF16),
        pltpu.VMEM(token, F32),
        pltpu.VMEM(token, F32),
        pltpu.VMEM(token, BF16),
        pltpu.VMEM(token, BF16),
        pltpu.VMEM((2, WINLEN, WINLEN), BF16),
        pltpu.VMEM((WINLEN, WINLEN), BF16),
        pltpu.VMEM((WINLEN, WINLEN), BF16),
        pltpu.VMEM((WINLEN, WINLEN), F32),
        pltpu.VMEM((1, LANES, 5 * LANES), F32),
        pltpu.VMEM((LANES, WINLEN), BF16),
        pltpu.VMEM((LANES, WINLEN), F32),
        pltpu.VMEM((WINLEN, LANES), BF16),
        pltpu.VMEM((WINLEN, LANES), F32),
        pltpu.VMEM((1, VEC_ROWS * LANES), F32),
        pltpu.VMEM((2 * HEADS, 1, LANES), F32),
        pltpu.VMEM((HEADS, 1, WIDE), F32),
        pltpu.VMEM((NOTE_ROWS, LANES), F32),
        pltpu.VMEM((7, NOTE_ROWS, LANES), F32),
        pltpu.SemaphoreType.DMA((16,)),
        pltpu.SemaphoreType.DMA((2,)),
        pltpu.SemaphoreType.REGULAR((2,)),
        pltpu.SemaphoreType.DMA((2, 2, DEPTH)),
        pltpu.SemaphoreType.DMA((2, 7)),
        pltpu.SemaphoreType.DMA((2,)),
    ]
    return pl.pallas_call(
        functools.partial(backward_kernel, plan),
        out_shape=[
            jax.ShapeDtypeStruct((COLUMNS,) + block, F32), positions, positions,
            jax.ShapeDtypeStruct((HEADS, WINLEN, WINLEN), BF16),
        ],
        in_specs=[anywhere] * 14 + [vmem] * 5,
        out_specs=[vmem] + [anywhere] * 3,
        scratch_shapes=scratch + sem_shapes(REDUCE_SEMS),
        compiler_params=pltpu.CompilerParams(
            collective_id=1, has_side_effects=True, vmem_limit_bytes=62 * 2**20
        ),
        name="backward_pass",
    )(*operands)


def fast_shards(hidden_in, cotangent, box_coords, doc_lengths, params, moment_one, moment_two):
    shard_len = params.shape[0]
    plan = Plan(shard_len)
    (proj_qkv, proj_out, proj_in, proj_back, features_t, start_low, queries, keys, values, probs, context_t,
     xhat, normed_low, vec, rstd, cot, hot_two,
     rest_rows, share) = forward_pass(
        plan, params.reshape(plan.rows, LANES), hidden_in, cotangent,
        jnp.transpose(box_coords, (0, 2, 1)), doc_lengths,
    )
    summed, output_low, grad_hidden, _ = backward_pass(
        Plan(shard_len, carry=5 * LANES),
        (proj_back, proj_in, proj_out, proj_qkv, normed_low, start_low, features_t, context_t, queries, keys,
         values, probs, xhat, cot, rstd, vec, hot_two, rest_rows, share),
    )
    grad_share = summed.reshape(plan.padded, LANES)[: plan.rows].reshape(-1)
    return finish_step(output_low, grad_hidden, grad_share, params, moment_one, moment_two)


def finish_step(output_low, grad_hidden, grad_share, params, moment_one, moment_two):
    shard_len = params.shape[0]
    index = lax.axis_index("dp") * lax.axis_size("head") + lax.axis_index("head")
    flat_index = index * shard_len + jnp.arange(shard_len, dtype=jnp.int32)
    param_step, new_one = adam_step(params, moment_one, moment_two, grad_share, flat_index)
    return (output_low, grad_hidden, grad_share, param_step, new_one)


def to_windows(shard):
    return lax.all_to_all(shard, "head", split_axis=0, concat_axis=1, tiled=True)


def to_positions(window):
    return lax.all_to_all(window, "head", split_axis=1, concat_axis=0, tiled=True)


def plain_shards(hidden_in, cotangent, box_coords, doc_lengths, params, moment_one, moment_two):
    head_pos = lax.axis_index("head")
    groups = lax.axis_size("head")
    shard_len = params.shape[0]
    flat_params = lax.all_gather(params.astype(BF16), ("dp", "head"), axis=0, tiled=True)
    pieces = unpack(flat_params)
    hidden = to_windows(hidden_in).reshape(WINLEN, D)
    cot = to_windows(cotangent).reshape(WINLEN, D)
    own_box = lax.dynamic_index_in_dim(box_coords, head_pos, 0, keepdims=False)
    own_lengths = lax.dynamic_index_in_dim(doc_lengths, head_pos, 0, keepdims=False)
    chosen, relative, centre_x, centre_y = window_layout(own_lengths, own_box)
    features = box_features(relative).astype(BF16)

    proj_qkv, proj_out, proj_box, proj_in, proj_back = pieces[:5]
    qv_bias, out_bias, norm_one, in_bias, back_bias, norm_two, tables = pieces[5:]
    ops = bias_operands(tables, chosen, centre_x, centre_y)
    start_state = hidden.astype(F32) + matmul(features, proj_box)
    start_low = start_state.astype(BF16)
    qv_float = qv_bias.astype(F32)
    mixed = matmul(start_low, proj_qkv)
    queries = (mixed[:, :D] + qv_float[0]).astype(BF16) * jnp.asarray(HEAD_DIM ** (-0.5), BF16)
    keys = mixed[:, D : 2 * D].astype(BF16)
    values = (mixed[:, 2 * D :] + qv_float[1]).astype(BF16)

    probs, context_t = attention_forward(queries, keys, values, ops)
    first_sum = start_state + rows_inner(context_t, proj_out) + out_bias.astype(F32)
    normed, norm_one_back = jax.vjp(layer_norm, first_sum, norm_one.astype(F32))
    normed_low = normed.astype(BF16)
    inner_act = matmul(normed_low, proj_in) + in_bias.astype(F32)
    active, gelu_back = jax.vjp(gelu_exact, inner_act)
    active_low = active.astype(BF16)
    second_sum = normed + matmul(active_low, proj_back) + back_bias.astype(F32)
    output, norm_two_back = jax.vjp(layer_norm, second_sum, norm_two.astype(F32))
    output_low = to_positions(output.astype(BF16).reshape(1, WINLEN, D))

    grad_second, grad_norm_two = norm_two_back(cot.astype(F32))
    grad_branch = grad_second.astype(BF16)
    grad_proj_back = rows_inner(active_low, grad_branch)
    grad_back_bias = jnp.sum(grad_branch.astype(F32), axis=0)
    (grad_inner_f,) = gelu_back(times_transposed(grad_branch, proj_back))
    grad_inner = grad_inner_f.astype(BF16)
    grad_proj_in = rows_inner(normed_low, grad_inner)
    grad_in_bias = jnp.sum(grad_inner.astype(F32), axis=0)
    grad_first, grad_norm_one = norm_one_back(grad_second + times_transposed(grad_inner, proj_in))
    grad_attn = grad_first.astype(BF16)
    grad_proj_out = matmul(context_t, grad_attn)
    grad_out_bias = jnp.sum(grad_attn.astype(F32), axis=0)
    grad_context = times_transposed(grad_attn, proj_out).astype(BF16)
    grad_queries_t, grad_keys, grad_values, cells, diag = attention_backward(
        queries, keys, values, grad_context, probs, ops
    )
    table_grad = table_grads(cells, diag)
    grad_mixed = jnp.concatenate([grad_queries_t.T, grad_keys, grad_values], axis=1)
    grad_proj_qkv = rows_inner(start_low, grad_mixed)
    summed = jnp.sum(grad_mixed.astype(F32), axis=0)
    grad_qv_bias = jnp.stack([summed[:D], summed[2 * D :]])
    grad_start = grad_first + times_transposed(grad_mixed, proj_qkv)
    grad_start_low = grad_start.astype(BF16)
    grad_hidden = to_positions(grad_start_low.reshape(1, WINLEN, D))
    grad_proj_box = rows_inner(features, grad_start_low)
    grad_list = (
        grad_proj_qkv,
        grad_proj_out,
        grad_proj_box,
        grad_proj_in,
        grad_proj_back,
        grad_qv_bias,
        grad_out_bias,
        grad_norm_one,
        grad_in_bias,
        grad_back_bias,
        grad_norm_two,
        table_grad,
    )
    padding = jnp.zeros((shard_len * groups * lax.axis_size("dp") - USED,), BF16)
    grads_flat = jnp.concatenate([piece.astype(BF16).reshape(-1) for piece in grad_list] + [padding])
    grad_share = lax.psum_scatter(
        grads_flat, ("dp", "head"), scatter_dimension=0, tiled=True
    ).astype(F32)
    return finish_step(output_low, grad_hidden, grad_share, params, moment_one, moment_two)


def solution(mesh):
    placed = (
        P("dp", "head", None),
        P("dp", "head", None),
        P("dp", None, None),
        P("dp", None),
        P(("dp", "head")),
        P(("dp", "head")),
        P(("dp", "head")),
    )
    return jax.shard_map(
        fast_shards if fits(mesh) else plain_shards,
        mesh=mesh,
        in_specs=placed,
        out_specs=(
            P("dp", "head", None),
            P("dp", "head", None),
            P(("dp", "head")),
            P(("dp", "head")),
            P(("dp", "head")),
        ),
        check_vma=False,
    )
```

```python
import functools
import math

import jax
import jax.numpy as jnp
import numpy as np
from jax import lax
from jax.experimental import pallas as pl
from jax.experimental.pallas import tpu as pltpu
from jax.sharding import PartitionSpec as P

D = 768
HEADS = 12
FF = 3072
BUCKETS = 32
WINLEN = 512
HEAD_DIM = 64
PAIRS = HEADS // 2
LANES = 128
BLOCKS = WINLEN // LANES

beta_one = 0.9
beta_two = 0.999
adam_eps = 1e-08
norm_eps = 1e-05
base_rate = 0.001
layer_decay = 0.75
decay_weight = 0.01
adam_count = 100
coord_cell = 32
masked_score = -1e30

F32 = jnp.float32
BF16 = jnp.bfloat16


def layouts_list():
    return (
        (D, 3 * D),
        (D, D),
        (D, D),
        (D, FF),
        (FF, D),
        (2, D),
        (D,),
        (2, D),
        (FF,),
        (D,),
        (2, D),
        (3, HEADS, BUCKETS),
    )


def unpack(flat_params):
    pieces = []
    offset = 0
    for layout in layouts_list():
        elements = math.prod(layout)
        pieces.append(flat_params[offset : offset + elements].reshape(layout))
        offset += elements
    return pieces


def matmul(left_mat, right_mat):
    return jnp.dot(left_mat, right_mat, preferred_element_type=F32)


def rows_inner(left_mat, right_mat):
    return lax.dot_general(left_mat, right_mat, (((0,), (0,)), ((), ())), preferred_element_type=F32)


def times_transposed(left_mat, right_mat):
    return lax.dot_general(left_mat, right_mat, (((1,), (1,)), ((), ())), preferred_element_type=F32)


def layer_norm(values, gain_bias):
    row_mean = jnp.mean(values, axis=-1, keepdims=True)
    centred = values - row_mean
    spread = jnp.mean(centred * centred, axis=-1, keepdims=True)
    return centred * lax.rsqrt(spread + norm_eps) * gain_bias[0] + gain_bias[1]


def gelu_exact(values):
    return jax.nn.gelu(values, approximate=False)


def hot(index, count):
    return (np.asarray(index)[..., None] == np.arange(count)).astype(np.float32)


def clipped(steps):
    return np.clip(steps, -(BUCKETS // 2), BUCKETS // 2 - 1) + BUCKETS // 2


CELLS = np.arange(BUCKETS)
HOT_SAME = hot(clipped(CELLS[:, None] - CELLS[None, :]), BUCKETS)
HOT_LESS = hot(clipped(CELLS[:, None] - CELLS[None, :] - 1), BUCKETS)
WIDE = 6 * LANES
_U = np.arange(WIDE)
BAND_HOT = hot(np.where(_U < 5 * LANES, clipped(_U - 2 * LANES), 0), BUCKETS)
_V = np.arange(4 * LANES)
DIAG_HOT = np.concatenate(
    [
        hot(np.zeros(LANES, np.int64), BUCKETS),
        hot(np.where(_V < 3 * LANES, clipped(_V - LANES), 0), BUCKETS),
        hot(np.full(LANES, BUCKETS - 1), BUCKETS),
    ]
)


def window_layout(doc_lengths, box_coords):
    doc_ends = jnp.cumsum(doc_lengths, dtype=jnp.int32)
    doc_starts = doc_ends - doc_lengths
    places = jnp.arange(WINLEN, dtype=jnp.int32)
    doc_ids = jnp.sum(
        (places[:, None] >= doc_ends[None, :]).astype(jnp.int32), axis=1, dtype=jnp.int32
    )
    docs = jnp.arange(doc_lengths.shape[0], dtype=jnp.int32)
    chosen = doc_ids[:, None] == docs[None, :]
    first_hot = places[:, None] == doc_starts[None, :]
    first_box = jnp.sum(
        jnp.where(first_hot[:, :, None], box_coords[:, None, :], 0), axis=0, dtype=jnp.int32
    )
    anchor = jnp.sum(
        jnp.where(chosen[:, :, None], first_box[None, :, :], 0), axis=1, dtype=jnp.int32
    )
    relative = box_coords - jnp.concatenate([anchor[:, :2], anchor[:, :2]], axis=1)
    centre_x = (box_coords[:, 0] + box_coords[:, 2]) // 2
    centre_y = (box_coords[:, 1] + box_coords[:, 3]) // 2
    return chosen, relative, centre_x, centre_y


def box_features(relative):
    count_freq = D // 8
    steps = jnp.arange(count_freq, dtype=F32)
    frequency = jnp.exp(steps * (-math.log(1000.0) / count_freq))
    angles = relative.astype(F32)[:, :, None] * frequency[None, None, :]
    return jnp.concatenate([jnp.sin(angles), jnp.cos(angles)], axis=2).reshape(relative.shape[0], D)


def bias_operands(tables, chosen, centre_x, centre_y):
    cell_x, cell_y = centre_x // coord_cell, centre_y // coord_cell
    rest_x, rest_y = centre_x % coord_cell, centre_y % coord_cell
    cells = jnp.arange(BUCKETS, dtype=jnp.int32)
    hot_x = (cell_x[:, None] == cells[None, :]).astype(BF16)
    hot_y = (cell_y[:, None] == cells[None, :]).astype(BF16)
    none = jnp.zeros_like(hot_x)
    hot_two = jnp.concatenate([hot_x, hot_y, hot_x, hot_y], axis=1)
    key_x = jnp.stack(
        [
            jnp.concatenate([hot_x, -hot_x, none, none], axis=1),
            jnp.concatenate([none, none, hot_x, -hot_x], axis=1),
        ]
    )
    key_y = jnp.stack(
        [
            jnp.concatenate([hot_y, -hot_y, none, none], axis=1),
            jnp.concatenate([none, none, hot_y, -hot_y], axis=1),
        ]
    )
    same = jnp.einsum("qcb,thb->thqc", HOT_SAME.astype(BF16), tables[1:], preferred_element_type=F32)
    less = jnp.einsum("qcb,thb->thqc", HOT_LESS.astype(BF16), tables[1:], preferred_element_type=F32)
    zero = jnp.zeros_like(same[0])
    base = jnp.concatenate(
        [jnp.concatenate([same[0], zero], axis=2), jnp.concatenate([zero, same[1]], axis=2)], axis=1
    )
    base = base.reshape(PAIRS, 2, 64, 64)[:, ::-1].reshape(HEADS, 64, 64)
    diff_x = jnp.concatenate([jnp.concatenate([less[0], same[0]], axis=2), jnp.zeros((HEADS, 32, 64), F32)], axis=1)
    diff_y = jnp.concatenate([jnp.zeros((HEADS, 32, 64), F32), jnp.concatenate([less[1], same[1]], axis=2)], axis=1)
    rows = jnp.concatenate([base, diff_x, diff_y], axis=0).astype(BF16)
    rows = rows.transpose(1, 0, 2).reshape(64, 3 * D)
    met = matmul(hot_two[:, :64], rows).astype(BF16)
    band = matmul(tables[0], jnp.asarray(BAND_HOT.T, BF16)).reshape(HEADS, 1, WIDE)
    rest_cols = jnp.stack([rest_x, rest_y], axis=1).astype(F32)
    rest_rows = rest_cols.T
    pad = jnp.zeros((WINLEN, LANES - chosen.shape[1]), BF16)
    marks = chosen.astype(BF16)
    mark_keys = jnp.concatenate([marks, pad], axis=1)
    mark_queries = jnp.concatenate([(1 - marks) * jnp.asarray(masked_score, BF16), pad], axis=1)
    return dict(
        hot_two=hot_two,
        key_x=key_x,
        key_y=key_y,
        met=met,
        band=band,
        rest_cols=rest_cols,
        rest_rows=rest_rows,
        mark_keys=mark_keys,
        mark_queries=mark_queries,
    )


def half_masks():
    lane = lax.broadcasted_iota(jnp.int32, (1, LANES), 1)
    low = (lane < HEAD_DIM).astype(F32)
    return low.astype(BF16), (1.0 - low).astype(BF16)


def less_masks(rest_cols, rest_rows, less_x, less_y):
    for part in range(BLOCKS):
        rows = slice(part * LANES, (part + 1) * LANES)
        for axis, less in ((0, less_x), (1, less_y)):
            column = rest_cols[rows, axis : axis + 1]
            row = rest_rows[axis : axis + 1, :]
            less[rows, :] = jnp.where(row < column, 1.0, 0.0).astype(less.dtype)


def attention_forward_kernel(
    q_ref, k_ref, v_ref, hot_ref, keyx_ref, keyy_ref, met_ref, band_ref, cols_ref, rows_ref,
    mkey_ref, mquery_ref, probs_ref, context_ref,
    kaug, qaug, less_x, less_y, wide, scores,
):
    low, high = half_masks()
    less_masks(cols_ref, rows_ref, less_x, less_y)
    kaug[:, LANES:] = mkey_ref[...]
    qaug[:, LANES:] = mquery_ref[...]
    half = 2 * LANES

    def one_pair(pair, carry):
        at = pl.multiple_of(pair * LANES, LANES)
        lanes = pl.ds(at, LANES)
        lanes_x = pl.ds(pl.multiple_of(at + D, LANES), LANES)
        lanes_y = pl.ds(pl.multiple_of(at + 2 * D, LANES), LANES)
        values_t = v_ref[:, lanes].T
        for odd in range(2):
            own, other = (low, high) if odd == 0 else (high, low)
            head = 2 * pair + odd
            kaug[:, :LANES] = k_ref[:, lanes] * own + hot_ref[...] * other
            qaug[:, :LANES] = q_ref[:, lanes] * own + met_ref[:, lanes] * other
            skew_band(band_ref[head], wide)
            for side in range(2):
                cols = slice(side * half, (side + 1) * half)
                top = None
                for part in range(BLOCKS):
                    rows = slice(part * LANES, (part + 1) * LANES)
                    s = times_transposed(kaug[rows, :], qaug[cols, :])
                    dx = times_transposed(keyx_ref[odd, rows, :], met_ref[cols, lanes_x])
                    dy = times_transposed(keyy_ref[odd, rows, :], met_ref[cols, lanes_y])
                    bias = []
                    for block in range(2 * side, 2 * side + 2):
                        step = max(-2, min(2, block - part)) + 2
                        bias.append(wide[:, step * LANES : (step + 1) * LANES])
                    s = s + jnp.concatenate(bias, axis=1)
                    s = s + dx * less_x[rows, cols] + dy * less_y[rows, cols]
                    scores[rows, :] = s
                    best = jnp.max(s, axis=0, keepdims=True)
                    top = best if top is None else jnp.maximum(top, best)
                total = None
                for part in range(BLOCKS):
                    rows = slice(part * LANES, (part + 1) * LANES)
                    e = jnp.exp(scores[rows, :] - top)
                    scores[rows, :] = e
                    add = jnp.sum(e, axis=0, keepdims=True)
                    total = add if total is None else total + add
                share = 1.0 / total
                for part in range(BLOCKS):
                    rows = slice(part * LANES, (part + 1) * LANES)
                    probs_ref[head, rows, cols] = (scores[rows, :] * share).astype(BF16)
                got = matmul(
                    values_t[odd * HEAD_DIM : (odd + 1) * HEAD_DIM, :], probs_ref[head, :, cols]
                )
                context_ref[pl.ds(pl.multiple_of(head * HEAD_DIM, HEAD_DIM), HEAD_DIM), cols] = (
                    got.astype(BF16)
                )
        return carry

    lax.fori_loop(0, PAIRS, one_pair, 0)


def skew_band(row, wide):
    x = jnp.broadcast_to(row, (8, WIDE))
    sub = lax.broadcasted_iota(jnp.int32, (8, WIDE), 0)
    for bit in (1, 2, 4):
        x = jnp.where((sub & bit) != 0, pltpu.roll(x, bit, 1), x)
    for group in range(LANES // 8):
        y = x if group == 0 else pltpu.roll(x, 8 * group, 1)
        wide[8 * group : 8 * group + 8, :] = y[:, : 5 * LANES]


def skew_groups(skewed, wide):
    for group in range(LANES // 8):
        y = skewed if group == 0 else pltpu.roll(skewed, 8 * group, 1)
        wide[8 * group : 8 * group + 8, :] = y[:, : 5 * LANES]


def diagonal_sums(parts):
    total = None
    for group in range(LANES // 8):
        x = jnp.concatenate(
            [parts[8 * group : 8 * group + 8, LANES : 4 * LANES], jnp.zeros((8, LANES), F32)], axis=1
        )
        y = x if group == 0 else pltpu.roll(x, 4 * LANES - 8 * group, 1)
        total = y if total is None else total + y
    sub = lax.broadcasted_iota(jnp.int32, (8, 4 * LANES), 0)
    for bit in (1, 2, 4):
        total = jnp.where((sub & bit) != 0, pltpu.roll(total, 4 * LANES - bit, 1), total)
    return jnp.sum(total, axis=0, keepdims=True)


def attention_backward_kernel(
    q_ref, k_ref, v_ref, dctx_ref, probs_ref, hot_ref, cols_ref, rows_ref,
    dq_ref, dk_ref, dv_ref, cells_ref, diag_ref,
    qaug, less_x, less_y, scores, dscores, band, kept, hot_t,
):
    low, high = half_masks()
    less_masks(cols_ref, rows_ref, less_x, less_y)
    hot_t[...] = hot_ref[...].T
    lane = lax.broadcasted_iota(jnp.int32, (1, LANES), 1)
    scale = HEAD_DIM ** (-0.5)
    of_x = jnp.where((lane // BUCKETS) % 2 == 0, 1.0, 0.0)
    cells_x = hot_ref[...] * of_x.astype(BF16)
    cells_y = hot_ref[...] * (1.0 - of_x).astype(BF16)

    def one_pair(pair, carry):
        at = pl.multiple_of(pair * LANES, LANES)
        lanes = pl.ds(at, LANES)
        keys_t = k_ref[:, lanes].T
        for odd in range(2):
            own, other = (low, high) if odd == 0 else (high, low)
            head = 2 * pair + odd
            qaug[...] = q_ref[:, lanes] * own + hot_ref[...] * other
            dctx = dctx_ref[:, lanes]
            dot = None
            for part in range(BLOCKS):
                rows = slice(part * LANES, (part + 1) * LANES)
                dp = times_transposed(v_ref[rows, lanes] * own, dctx)
                scores[rows, :] = dp
                add = jnp.sum(dp * probs_ref[head, rows, :].astype(F32), axis=0, keepdims=True)
                dot = add if dot is None else dot + add
            band[...] = jnp.zeros_like(band)
            for part in range(BLOCKS):
                rows = slice(part * LANES, (part + 1) * LANES)
                probs = probs_ref[head, rows, :]
                ds = probs.astype(F32) * (scores[rows, :] - dot)
                for block in range(BLOCKS):
                    step = max(-2, min(2, block - part)) + 2
                    where = slice(step * LANES, (step + 1) * LANES)
                    band[:, where] = band[:, where] + ds[:, block * LANES : (block + 1) * LANES]
                ds = ds.astype(BF16)
                dscores[rows, :] = ds
                both = matmul(ds, qaug[...])
                less = matmul(ds * less_x[rows, :], cells_x) + matmul(ds * less_y[rows, :], cells_y)
                dv = matmul(probs, dctx)
                kept[odd, 0, rows, :] = both
                kept[odd, 1, rows, :] = less
                kept[odd, 2, rows, :] = dv
            got = matmul(keys_t[odd * HEAD_DIM : (odd + 1) * HEAD_DIM, :], dscores[...])
            dq_ref[pl.ds(pl.multiple_of(head * HEAD_DIM, HEAD_DIM), HEAD_DIM), :] = (
                got * scale
            ).astype(BF16)
            diag_ref[head, :, LANES : 5 * LANES] = diagonal_sums(band)
            diag_ref[head, :, :LANES] = jnp.sum(band[:, :LANES], axis=0, keepdims=True)
            diag_ref[head, :, 5 * LANES :] = jnp.sum(band[:, 4 * LANES :], axis=0, keepdims=True)
            for which in range(2):
                summed = kept[odd, which]
                first = summed.astype(BF16)
                rest = (summed - first.astype(F32)).astype(BF16)
                cells_ref[head, which] = matmul(hot_t[:64, :], first) + matmul(hot_t[:64, :], rest)
        dk_ref[:, lanes] = jnp.where(lane < HEAD_DIM, kept[0, 0], kept[1, 0]).astype(BF16)
        dv_ref[:, lanes] = jnp.where(lane < HEAD_DIM, kept[0, 2], kept[1, 2]).astype(BF16)
        return carry

    lax.fori_loop(0, PAIRS, one_pair, 0)


def attention_forward(queries, keys, values, ops):
    return pl.pallas_call(
        attention_forward_kernel,
        out_shape=(
            jax.ShapeDtypeStruct((HEADS, WINLEN, WINLEN), BF16),
            jax.ShapeDtypeStruct((D, WINLEN), BF16),
        ),
        scratch_shapes=[
            pltpu.VMEM((WINLEN, 2 * LANES), BF16),
            pltpu.VMEM((WINLEN, 2 * LANES), BF16),
            pltpu.VMEM((WINLEN, WINLEN), F32),
            pltpu.VMEM((WINLEN, WINLEN), F32),
            pltpu.VMEM((LANES, 5 * LANES), F32),
            pltpu.VMEM((WINLEN, 2 * LANES), F32),
        ],
        compiler_params=pltpu.CompilerParams(vmem_limit_bytes=48 * 2**20),
        name="attention_forward",
    )(
        queries, keys, values, ops["hot_two"], ops["key_x"], ops["key_y"], ops["met"], ops["band"],
        ops["rest_cols"], ops["rest_rows"], ops["mark_keys"], ops["mark_queries"],
    )


def attention_backward(queries, keys, values, grad_context, probs, ops):
    return pl.pallas_call(
        attention_backward_kernel,
        out_shape=(
            jax.ShapeDtypeStruct((D, WINLEN), BF16),
            jax.ShapeDtypeStruct((WINLEN, D), BF16),
            jax.ShapeDtypeStruct((WINLEN, D), BF16),
            jax.ShapeDtypeStruct((HEADS, 2, 64, LANES), F32),
            jax.ShapeDtypeStruct((HEADS, 1, WIDE), F32),
        ),
        scratch_shapes=[
            pltpu.VMEM((WINLEN, LANES), BF16),
            pltpu.VMEM((WINLEN, WINLEN), BF16),
            pltpu.VMEM((WINLEN, WINLEN), BF16),
            pltpu.VMEM((WINLEN, WINLEN), F32),
            pltpu.VMEM((WINLEN, WINLEN), BF16),
            pltpu.VMEM((LANES, 5 * LANES), F32),
            pltpu.VMEM((2, 3, WINLEN, LANES), F32),
            pltpu.VMEM((LANES, WINLEN), BF16),
        ],
        compiler_params=pltpu.CompilerParams(vmem_limit_bytes=48 * 2**20),
        name="attention_backward",
    )(
        queries, keys, values, grad_context, probs, ops["hot_two"], ops["rest_cols"],
        ops["rest_rows"],
    )


def table_grads(cells, diag):
    exact = lax.Precision.HIGHEST
    pairs = cells.reshape(PAIRS, 2, 2, 64, LANES)
    every = jnp.stack([pairs[:, 0, 0, :, 64:], pairs[:, 1, 0, :, :64]], axis=1).reshape(HEADS, 64, 64)
    less = cells[:, 1]
    less_x, less_y = less[:, :32, :32], less[:, 32:, 32:64]
    all_x, all_y = every[:, :32, :32], every[:, 32:, 32:]
    same = jnp.stack([all_x - less_x, all_y - less_y]).reshape(2 * HEADS, -1)
    below = jnp.stack([less_x, less_y]).reshape(2 * HEADS, -1)
    same_hot = jnp.asarray(HOT_SAME.transpose(1, 0, 2).reshape(-1, BUCKETS))
    less_hot = jnp.asarray(HOT_LESS.transpose(1, 0, 2).reshape(-1, BUCKETS))
    moved = jnp.dot(same, same_hot, precision=exact) + jnp.dot(below, less_hot, precision=exact)
    along = jnp.dot(diag.reshape(HEADS, WIDE), jnp.asarray(DIAG_HOT), precision=exact)
    return jnp.concatenate([along[None], moved.reshape(2, HEADS, BUCKETS)], axis=0)


COLUMNS = 4
CORES = 2
DEPTH = 4
USED = sum(math.prod(layout) for layout in layouts_list())
MATRICES = layouts_list()[:5]
MISC = sum(math.prod(layout) for layout in layouts_list()[5:])
MISC_ROWS = -(-MISC // (8 * LANES)) * 8


class Plan:
    def __init__(self, shard_len, carry=3 * LANES):
        self.rows = shard_len // LANES
        self.quarter = -(-self.rows // (16 * COLUMNS)) * 16
        self.padded = COLUMNS * self.quarter
        self.per_column = CORES * DEPTH * self.rows
        self.carry = carry
        self.staged = self.carry + self.per_column + 3 * LANES
        starts = []
        offset = 0
        for depth, width in MATRICES:
            starts.append(offset // LANES)
            offset += depth * width
        self.starts = starts
        self.misc_start = offset // LANES


def fits(mesh):
    return mesh.shape["dp"] == COLUMNS * CORES and mesh.shape["head"] == DEPTH


MESH = pl.DeviceIdType.MESH


class Place:
    def __init__(self):
        dp = lax.axis_index("dp")
        self.z = lax.axis_index("head")
        self.core = dp % CORES
        self.column = dp // CORES
        self.x = self.column % 2
        self.y = self.column // 2
        self.col_x = 2 * self.y + (1 - self.x)
        self.col_y = 2 * (1 - self.y) + self.x
        self.col_d = 2 * (1 - self.y) + (1 - self.x)
        self.peer_x = self.at(self.col_x, self.core, self.z)
        self.peer_y = self.at(self.col_y, self.core, self.z)
        self.peer_d = self.at(self.col_d, self.core, self.z)
        self.peer_core = self.at(self.column, 1 - self.core, self.z)
        self.far = [lax.rem(self.z + d, DEPTH) for d in range(1, DEPTH)]
        self.from_far = [lax.rem(self.z + DEPTH - d, DEPTH) for d in range(1, DEPTH)]
        self.peers_z = [self.at(self.column, self.core, f) for f in self.far]

    def at(self, column, core, z):
        return {"dp": column * CORES + core, "head": z}

    def greet(self):
        barrier = pltpu.get_barrier_semaphore()
        peers = [self.peer_x, self.peer_y, self.peer_d, self.peer_core] + self.peers_z
        for peer in peers:
            pl.semaphore_signal(barrier, inc=1, device_id=peer, device_id_type=MESH)
        pl.semaphore_wait(barrier, len(peers))


def remote(src, dst, send_sem, recv_sem, peer):
    return pltpu.make_async_remote_copy(
        src_ref=src, dst_ref=dst, send_sem=send_sem, recv_sem=recv_sem, device_id=peer,
        device_id_type=MESH,
    )


class Gathering:
    def __init__(self, place, flat, sems):
        self.place = place
        self.flat = flat
        self.sems = sems
        self.sent = []

    def send(self, src, dst, kind, index, peer):
        copy = remote(src, dst, self.sems[kind].at[0, index], self.sems[kind].at[1, index], peer)
        copy.start()
        self.sent.append(copy)

    def got(self, dst, kind, index):
        remote(
            dst, dst, self.sems[kind].at[0, index], self.sems[kind].at[1, index], self.place.peer_x
        ).wait_recv()

    def rows(self, h):
        half = self.flat.shape[-2] // 2
        return slice(h * half, (h + 1) * half)

    def spread(self, own, h):
        p = self.place
        rows = self.rows(h)
        for index, (column, peer) in enumerate(
            ((p.col_x, p.peer_x), (p.col_y, p.peer_y), (p.col_d, p.peer_d))
        ):
            self.send(
                own.at[column, rows], self.flat.at[p.column, p.core, p.z, column, rows], "spread",
                2 * index + h, peer,
            )
        self.flat[p.column, p.core, p.z, p.column, rows] = own[p.column, rows]

    def spread_done(self, h):
        p = self.place
        for index, column in enumerate((p.col_x, p.col_y, p.col_d)):
            self.got(self.flat.at[column, p.core, p.z, p.column, self.rows(h)], "spread", 2 * index + h)

    def along_z(self, k, h):
        p = self.place
        piece = self.flat.at[k, p.core, p.z, p.column, self.rows(h)]
        for d in range(DEPTH - 1):
            self.send(piece, piece, "z", 3 * (2 * k + h) + d, p.peers_z[d])

    def first(self, k, h):
        p = self.place
        n = 2 * k + h
        for d in range(DEPTH - 1):
            self.got(
                self.flat.at[k, p.core, p.from_far[d], p.column, self.rows(h)], "z", 3 * n + d
            )
        piece = self.flat.at[k, p.core, :, p.column, self.rows(h)]
        self.send(piece, piece, "one", 2 * n, p.peer_x)
        self.send(piece, piece, "one", 2 * n + 1, p.peer_y)
        self.send(piece, piece, "core", 5 * n, p.peer_core)

    def second(self, k, h):
        p = self.place
        n = 2 * k + h
        rows = self.rows(h)
        from_x = self.flat.at[k, p.core, :, p.col_x, rows]
        self.got(from_x, "one", 2 * n)
        part = self.flat.at[k, p.core, 0:2, p.col_x, rows]
        self.send(part, part, "two", 2 * n, p.peer_y)
        self.send(from_x, from_x, "core", 5 * n + 1, p.peer_core)
        from_y = self.flat.at[k, p.core, :, p.col_y, rows]
        self.got(from_y, "one", 2 * n + 1)
        part = self.flat.at[k, p.core, 2:4, p.col_y, rows]
        self.send(part, part, "two", 2 * n + 1, p.peer_x)
        self.send(from_y, from_y, "core", 5 * n + 2, p.peer_core)

    def third(self, k, h):
        p = self.place
        n = 2 * k + h
        for side in range(2):
            part = self.flat.at[k, p.core, 2 * side : 2 * side + 2, p.col_d, self.rows(h)]
            self.got(part, "two", 2 * n + side)
            self.send(part, part, "core", 5 * n + 3 + side, p.peer_core)

    def complete(self, k):
        p = self.place
        other = 1 - p.core
        for h in range(2):
            n = 2 * k + h
            rows = self.rows(h)
            for index, column in enumerate((p.column, p.col_x, p.col_y)):
                self.got(self.flat.at[k, other, :, column, rows], "core", 5 * n + index)
            for side in range(2):
                self.got(
                    self.flat.at[k, other, 2 * side : 2 * side + 2, p.col_d, rows], "core",
                    5 * n + 3 + side,
                )

    def finish(self):
        for copy in self.sent:
            copy.wait_send()


GATHER_SEMS = {"spread": 6, "z": 24, "one": 16, "two": 16, "core": 40}


def sem_shapes(counts):
    return [pltpu.SemaphoreType.DMA((2, count)) for count in counts.values()]


def stage_column(plan, flat, staged, k):
    def one(shard, carry):
        core, z = shard // DEPTH, shard % DEPTH
        for quarter in range(COLUMNS):
            base = plan.carry + shard * plan.rows + quarter * plan.quarter
            staged[pl.ds(pl.multiple_of(base, 8), plan.quarter), :] = flat[k, core, z, quarter].astype(F32)
        return carry

    lax.fori_loop(0, CORES * DEPTH, one, 0)


def keep_carry(plan, staged):
    end = plan.carry + plan.per_column
    staged[: plan.carry, :] = staged[end - plan.carry : end, :]


ROW_STEP = 48


def column_rows(plan, k, touching):
    low, high = k * plan.per_column, (k + 1) * plan.per_column
    taken = []
    for index, (depth, width) in enumerate(MATRICES):
        group = 16 * (width // LANES)
        from_low, from_high = low - plan.starts[index], high - plan.starts[index]
        begin = max(0, min(depth, from_low // group * 16))
        if touching:
            end = max(0, min(depth, -(-from_high // group) * 16))
        else:
            end = max(0, min(depth, from_high // group * 16))
        if end > begin:
            taken.append((index, begin, end))
    return taken


def staged_at(plan, k, row):
    return plan.carry + row - k * plan.per_column


def row_loops(rows):
    whole = rows // ROW_STEP
    loops = [(ROW_STEP, 0, whole)] if whole else []
    if rows % ROW_STEP:
        loops.append((16, whole * ROW_STEP, (rows % ROW_STEP) // 16))
    return loops


def form_matrices(plan, staged, matrices, k):
    for index, begin, end in column_rows(plan, k, False):
        blocks = MATRICES[index][1] // LANES
        base = staged_at(plan, k, plan.starts[index] + begin * blocks)
        assert 0 <= base
        target = matrices[index]
        for step_rows, first, count in row_loops(end - begin):

            def one(step, carry, step_rows=step_rows, first=first, blocks=blocks, base=base,
                    begin=begin, target=target):
                row = first + step * step_rows
                for block in range(blocks):
                    got = staged[pl.ds(base + row * blocks + block, step_rows, stride=blocks), :]
                    target[
                        pl.ds(pl.multiple_of(begin + row, 16), step_rows),
                        block * LANES : (block + 1) * LANES,
                    ] = got.astype(BF16)
                return carry

            lax.fori_loop(0, count, one, 0)


def adam_step(params, moment_one, moment_two, grads, flat_index):
    box_part = (flat_index >= 4 * D * D) & (flat_index < 5 * D * D)
    step_rate = jnp.where(box_part, base_rate * layer_decay**12, base_rate * layer_decay)
    decay_mask = jnp.where(flat_index < 5 * D * D + 2 * D * FF, decay_weight, 0.0)
    moment_one = beta_one * moment_one + (1.0 - beta_one) * grads
    moment_two = beta_two * moment_two + (1.0 - beta_two) * grads * grads
    first_hat = moment_one / (1.0 - beta_one**adam_count)
    second_hat = moment_two / (1.0 - beta_two**adam_count)
    update = first_hat / (jnp.sqrt(second_hat) + adam_eps) + decay_mask * params
    return (-step_rate * update, moment_one)


VEC = {}
_at = 0
for _name, _rows in (
    ("q_bias", 6), ("v_bias", 6), ("out_bias", 6), ("gain_one", 6), ("shift_one", 6), ("in_bias", 24),
    ("back_bias", 6), ("gain_two", 6), ("shift_two", 6), ("tables", 9),
):
    VEC[_name] = _at * LANES
    _at += _rows
VEC_ROWS = _at
NOTE_ROWS = 96
NBLOCK = 2 * LANES


def note_place(plan):
    row = plan.misc_start - (CORES * DEPTH * COLUMNS - 1) * plan.rows
    quarter, row = row // plan.quarter, row % plan.quarter
    first = row // 16 * 16
    assert first + NOTE_ROWS <= plan.quarter and row - first + VEC_ROWS <= NOTE_ROWS
    return quarter, first, row - first


def spread_notes(place, own, notes, sems, plan):
    quarter, first, _ = note_place(plan)
    source = own.at[quarter, first : first + NOTE_ROWS]
    home = (place.column == COLUMNS - 1) & (place.core == CORES - 1)
    root = home & (place.z == DEPTH - 1)

    def copy(src, index, peer):
        return remote(src, notes, sems.at[0, index], sems.at[1, 0], peer)

    def arrived():
        copy(notes, 0, place.peer_core).wait_recv()

    @pl.when(root)
    def _():
        notes[...] = own[quarter, first : first + NOTE_ROWS]
        for index, peer in enumerate(place.peers_z):
            copy(source, index, peer).start()

    @pl.when(home & (place.z != DEPTH - 1))
    def _():
        arrived()

    @pl.when(home)
    def _():
        for index, peer in enumerate((place.peer_x, place.peer_y, place.peer_d)):
            copy(notes, 3 + index, peer).start()

    @pl.when((place.core == CORES - 1) & (place.column != COLUMNS - 1))
    def _():
        arrived()

    @pl.when(place.core == CORES - 1)
    def _():
        copy(notes, 6, place.peer_core).start()

    @pl.when(place.core != CORES - 1)
    def _():
        arrived()

    def finish():
        @pl.when(root)
        def _():
            for index, peer in enumerate(place.peers_z):
                copy(source, index, peer).wait_send()

        @pl.when(home)
        def _():
            for index, peer in enumerate((place.peer_x, place.peer_y, place.peer_d)):
                copy(notes, 3 + index, peer).wait_send()

        @pl.when(place.core == CORES - 1)
        def _():
            copy(notes, 6, place.peer_core).wait_send()

    return finish


def turns_table():
    count_freq = D // 8
    freq = np.exp(np.arange(count_freq) * (-math.log(1000.0) / count_freq)) / (2 * math.pi)
    per = np.concatenate([freq, freq])
    phase = np.concatenate([np.zeros(count_freq), np.full(count_freq, 0.25)])
    return np.stack([np.tile(per, 4), np.tile(phase, 4)]).astype(np.float32)


def sin_turns(t):
    t = t - jnp.floor(t + 0.5)
    a = jnp.abs(t)
    m = jnp.minimum(a, 0.5 - a) * (2 * math.pi)
    u = m * m
    poly = -1.0 / 39916800.0
    for term in (1.0 / 362880.0, -1.0 / 5040.0, 1.0 / 120.0, -1.0 / 6.0, 1.0):
        poly = poly * u + term
    s = m * poly
    return jnp.where(t < 0, -s, s)


def token_columns(boxes, lengths, window):
    coords = boxes[window].astype(F32)
    place = lax.broadcasted_iota(jnp.int32, (1, WINLEN), 1)
    doc = jnp.zeros((1, WINLEN), F32)
    anchor = jnp.zeros_like(coords)
    begin = 0
    for d in range(4):
        end = begin + lengths[window, d]
        mine = jnp.where((place >= begin) & (place < end), 1.0, 0.0)
        value = jnp.sum(coords * jnp.where(place == begin, 1.0, 0.0), axis=1, keepdims=True)
        anchor = anchor + value * mine
        doc = doc + mine * float(d)
        begin = end
    anchor = jnp.concatenate([anchor[0:2], anchor[0:2]], axis=0)
    relative = coords - anchor
    centre = jnp.floor((coords[0:2] + coords[2:4]) * 0.5)
    cell = jnp.floor(centre * (1.0 / coord_cell))
    rest = centre - cell * coord_cell
    rows = jnp.concatenate(
        [relative, cell, rest, doc, jnp.zeros((LANES - 9, WINLEN), F32)], axis=0
    )
    return rest, rows.T


def form_features(columns, turns_ref, features):
    lane = lax.broadcasted_iota(jnp.int32, (1, LANES), 1)
    for block in range(D // LANES):
        lanes = slice(block * LANES, (block + 1) * LANES)
        low, high = block * LANES // (D // 4), ((block + 1) * LANES - 1) // (D // 4)
        value = columns[:, low : low + 1]
        if high != low:
            value = jnp.where(
                lane + block * LANES < high * (D // 4), value, columns[:, high : high + 1]
            )
        t = value * turns_ref[0:1, lanes] + turns_ref[1:2, lanes]
        features[:, lanes] = sin_turns(t).astype(BF16)


def form_hots(columns, hot_ref, keyx_ref, keyy_ref, mkey, mquery):
    lane = lax.broadcasted_iota(jnp.int32, (1, LANES), 1)
    part = lane // BUCKETS
    cell = (lane % BUCKETS).astype(F32)
    is_x = jnp.where(columns[:, 4:5] == cell, 1.0, 0.0)
    is_y = jnp.where(columns[:, 5:6] == cell, 1.0, 0.0)
    hot_ref[...] = jnp.where(part % 2 == 0, is_x, is_y).astype(BF16)
    sign = jnp.where(part % 2 == 0, 1.0, -1.0)
    for odd in range(2):
        here = jnp.where(part // 2 == odd, sign, 0.0)
        keyx_ref[odd] = (is_x * here).astype(BF16)
        keyy_ref[odd] = (is_y * here).astype(BF16)
    doc = jnp.where(columns[:, 8:9] == lane.astype(F32), 1.0, 0.0)
    mkey[:, LANES:] = doc.astype(BF16)
    mquery[:, LANES:] = (jnp.where(lane < 4, 1.0 - doc, 0.0) * masked_score).astype(BF16)


def form_tables(tables, bands, tilted):
    row = lax.broadcasted_iota(jnp.int32, (LANES, 1), 0)
    half = BUCKETS // 2
    sub = lax.broadcasted_iota(jnp.int32, (8, LANES), 0)
    sub_wide = lax.broadcasted_iota(jnp.int32, (8, WIDE), 0)
    place = lax.broadcasted_iota(jnp.int32, (1, WIDE), 1)
    wanted = jnp.where(place < 5 * LANES, jnp.clip(place - 2 * LANES, -half, half - 1) + half, 0)
    lane = lax.broadcasted_iota(jnp.int32, (1, LANES), 1)
    turned = jnp.clip(64 - lane, -half, half - 1) + half
    for m in range(4):
        hot_band = jnp.where(row == wanted + m * BUCKETS, 1.0, 0.0).astype(BF16)
        got = matmul(tables, hot_band)
        for n in range(3):
            x = jnp.broadcast_to(got[n : n + 1, :], (8, WIDE))
            for bit in (1, 2, 4):
                x = jnp.where((sub_wide & bit) != 0, pltpu.roll(x, bit, 1), x)
            bands[4 * n + m] = x
        hot_turn = jnp.where(row == turned + m * BUCKETS, 1.0, 0.0).astype(BF16)
        got = matmul(tables, hot_turn)
        for t in (1, 2):
            for n in range(3):
                x = jnp.broadcast_to(got[3 * t + n : 3 * t + n + 1, :], (8, LANES))
                for bit in (1, 2, 4):
                    x = jnp.where((sub & bit) != 0, pltpu.roll(x, bit, 1), x)
                for group in range(BUCKETS // 8):
                    y = x if group == 0 else pltpu.roll(x, 8 * group, 1)
                    tilted[(t - 1) * HEADS + 4 * n + m, 8 * group : 8 * group + 8, :] = y


def pair_rows(tilted, pair):
    lane = lax.broadcasted_iota(jnp.int32, (1, LANES), 1)
    part = lane // BUCKETS
    x0, x1 = tilted[2 * pair], tilted[2 * pair + 1]
    y0, y1 = tilted[HEADS + 2 * pair], tilted[HEADS + 2 * pair + 1]

    def same(value, to):
        return value if to == 64 else pltpu.roll(value, (to - 64) % LANES, 1)

    def less(value, to):
        return pltpu.roll(value, (to - 65) % LANES, 1)

    zero = jnp.zeros_like(x0)
    base_x = jnp.where(part == 0, same(x1, 0), jnp.where(part == 2, same(x0, 64), zero))
    base_y = jnp.where(part == 1, same(y1, 32), jnp.where(part == 3, same(y0, 96), zero))

    def steps(even, odd):
        return jnp.where(
            part < 2,
            jnp.where(part == 0, less(even, 0), same(even, 32)),
            jnp.where(part == 2, less(odd, 64), same(odd, 96)),
        )

    rows = [
        jnp.concatenate([base_x, base_y], axis=0),
        jnp.concatenate([steps(x0, x1), zero], axis=0),
        jnp.concatenate([zero, steps(y0, y1)], axis=0),
    ]
    return jnp.concatenate(rows, axis=1).astype(BF16)


def gelu_and_slope(z):
    a = jnp.abs(z)
    t = 1.0 / (1.0 + (0.3275911 / math.sqrt(2.0)) * a)
    poly = 1.061405429 * 0.5
    for term in (-1.453152027, 1.421413741, -0.284496736, 0.254829592):
        poly = poly * t + 0.5 * term
    e = jnp.exp(-0.5 * z * z)
    tail = poly * t * e
    cdf = jnp.where(z < 0, tail, 1.0 - tail)
    return z * cdf, cdf + z * (e * (1.0 / math.sqrt(2.0 * math.pi)))


def forward_kernel(plan, params_in, hidden_in, cot_in, boxes, lengths, turns, *refs):
    (w_qkv_out, w_out_out, w_in_out, w_back_out, features_out, low_out, q_out, k_out, v_out, probs_out,
     context_out, hat_out, normed_out, vec_out, rstd_out, cot_ref, hot_out, rest_out, share_out) = refs[:19]
    refs = refs[19:]
    (flat, staged, own, w_qkv, w_out, w_box, w_in, w_back, notes, features, hidden, start, start_low, q_ref,
     k_ref, v_ref, hot_ref, key_x, key_y, bands, tilted, wides, scores, context_t, pair_t, hat, narrow,
     square, vec) = refs[:29]
    note_sems, swap_sems, copy_sems, probs_sems = refs[29:33]

    def lend(buffer, slot, lanes):
        return buffer.at[:, slot : slot + lanes]

    less_x, less_y = lend(square, 0, WINLEN), lend(square, WINLEN, WINLEN)
    probs = [lend(square, 2 * WINLEN, WINLEN), lend(square, 3 * WINLEN, WINLEN)]
    kaugs = [lend(narrow, 0, 2 * LANES), lend(narrow, 2 * LANES, 2 * LANES)]
    qaugs = [lend(narrow, 4 * LANES, 2 * LANES), lend(narrow, 6 * LANES, 2 * LANES)]
    met = lend(narrow, 8 * LANES, 3 * LANES)
    place = Place()
    normed_low = hidden
    context = features
    gathering = Gathering(place, flat, dict(zip(GATHER_SEMS, refs[33:])))
    matrices = (w_qkv, w_out, w_box, w_in, w_back)
    written = []

    def write_out(src, dst):
        copy = pltpu.make_async_copy(src, dst, copy_sems.at[len(written)])
        copy.start()
        written.append(copy)

    fetch = pltpu.make_async_copy(params_in, staged.at[: plan.rows], probs_sems.at[0])
    fetch.start()
    place.greet()
    fetch.wait()
    for quarter_at in range(COLUMNS):
        begin = quarter_at * plan.quarter
        own[quarter_at] = staged[begin : begin + plan.quarter, :].astype(BF16)
    gathering.spread(own, 0)
    gathering.spread(own, 1)

    quarter = WINLEN // DEPTH

    def exchange(source, target, kind):
        rows = pl.ds(pl.multiple_of(place.z * quarter, quarter), quarter)
        for d in range(DEPTH - 1):
            gathering_send(source.at[place.far[d]], target.at[rows], kind, d, place.peers_z[d])

    def gathering_send(src, dst, kind, d, peer):
        copy = remote(src, dst, swap_sems.at[kind, 0, d], swap_sems.at[kind, 1, d], peer)
        copy.start()
        gathering.sent.append(copy)

    def exchanged(target, kind):
        for d in range(DEPTH - 1):
            rows = pl.ds(pl.multiple_of(place.from_far[d] * quarter, quarter), quarter)
            remote(
                target.at[rows], target.at[rows], swap_sems.at[kind, 0, d], swap_sems.at[kind, 1, d],
                place.peer_x,
            ).wait_recv()

    finish_notes = spread_notes(place, own, notes, note_sems, plan)
    own_rows = pl.ds(pl.multiple_of(place.z * quarter, quarter), quarter)
    own_hidden = pltpu.make_async_copy(
        hidden_in.at[place.z], hidden.at[own_rows], swap_sems.at[0, 0, DEPTH - 1]
    )
    own_hidden.start()
    own_cot = pltpu.make_async_copy(
        cot_in.at[place.z], cot_ref.at[own_rows], swap_sems.at[1, 0, DEPTH - 1]
    )
    own_cot.start()
    gathering.spread_done(0)
    gathering.along_z(0, 0)
    gathering.spread_done(1)
    gathering.along_z(0, 1)

    rest, columns = token_columns(boxes, lengths, place.z)
    for part in range(BLOCKS):
        rows = slice(part * LANES, (part + 1) * LANES)
        for axis, less in ((0, less_x), (1, less_y)):
            less[rows, :] = jnp.where(
                rest[axis : axis + 1, :] < columns[rows, 6 + axis : 7 + axis], 1.0, 0.0
            ).astype(BF16)
    rest_out[...] = rest
    form_hots(columns, hot_ref, key_x, key_y, kaugs[0], qaugs[0])
    kaugs[1][:, LANES:] = kaugs[0][:, LANES:]
    qaugs[1][:, LANES:] = qaugs[0][:, LANES:]
    hot_out[...] = hot_ref[...]
    gathering.first(0, 0)
    gathering.along_z(1, 0)
    gathering.first(0, 1)
    gathering.along_z(1, 1)
    form_features(columns, turns, features)
    for n in range(D // LANES):
        rows = slice(n * LANES, (n + 1) * LANES)
        context_t[rows, :] = features[:, rows].T
    write_out(context_t, features_out)
    gathering.first(1, 0)
    exchange(hidden_in, hidden, 0)
    gathering.second(0, 0)
    gathering.first(1, 1)
    gathering.second(0, 1)
    _, _, note_row = note_place(plan)
    for row in range(VEC_ROWS):
        at = note_row + row
        vec[0:1, row * LANES : (row + 1) * LANES] = notes[at // 16 * 16 : at // 16 * 16 + 16, :].astype(
            F32
        )[at % 16 : at % 16 + 1, :]
    vec_out[...] = vec[...]
    table_row = note_row + VEC["tables"] // LANES
    assert table_row % 16 == 0
    form_tables(notes[table_row : table_row + 16, :], bands, tilted)

    gathering.third(0, 0)
    gathering.second(1, 0)
    gathering.third(0, 1)
    gathering.second(1, 1)
    gathering.complete(0)
    stage_column(plan, flat, staged, 0)
    exchanged(hidden, 0)
    gathering.along_z(2, 0)
    gathering.along_z(2, 1)
    form_matrices(plan, staged, matrices, 0)
    keep_carry(plan, staged)
    gathering.third(1, 0)
    gathering.third(1, 1)
    gathering.complete(1)
    stage_column(plan, flat, staged, 1)
    form_matrices(plan, staged, matrices, 1)
    keep_carry(plan, staged)
    write_out(w_qkv, w_qkv_out)
    write_out(w_out, w_out_out)

    own_hidden.wait()
    for n in range(D // NBLOCK):
        lanes = slice(n * NBLOCK, (n + 1) * NBLOCK)
        value = hidden[:, lanes].astype(F32) + matmul(features[...], w_box[:, lanes])
        start[:, lanes] = value
        start_low[:, lanes] = value.astype(BF16)
    write_out(start_low, low_out)
    written[0].wait()

    def project(n, carry):
        at = pl.multiple_of(n * NBLOCK, NBLOCK)
        lanes = pl.ds(at, NBLOCK)
        low = start_low[...]
        bias = vec[0:1, pl.ds(pl.multiple_of(VEC["q_bias"] + at, LANES), NBLOCK)]
        got = matmul(low, w_qkv[:, lanes]) + bias
        q_ref[:, lanes] = (got.astype(BF16).astype(F32) * HEAD_DIM ** (-0.5)).astype(BF16)
        k_ref[:, lanes] = matmul(low, w_qkv[:, pl.ds(pl.multiple_of(at + D, LANES), NBLOCK)]).astype(BF16)
        bias = vec[0:1, pl.ds(pl.multiple_of(VEC["v_bias"] + at, LANES), NBLOCK)]
        got = matmul(low, w_qkv[:, pl.ds(pl.multiple_of(at + 2 * D, LANES), NBLOCK)]) + bias
        v_ref[:, lanes] = got.astype(BF16)
        return carry

    lax.fori_loop(0, D // NBLOCK, project, 0)
    write_out(q_ref, q_out)
    write_out(k_ref, k_out)
    write_out(v_ref, v_out)
    gathering.first(2, 0)
    gathering.along_z(3, 0)
    gathering.first(2, 1)
    gathering.along_z(3, 1)

    low, high = half_masks()
    half = 2 * LANES

    def probs_copy(head, odd):
        return pltpu.make_async_copy(probs[odd], probs_out.at[head], probs_sems.at[odd])

    def one_pair(pair, carry):
        at = pl.multiple_of(pair * LANES, LANES)
        lanes = pl.ds(at, LANES)
        values_t = v_ref[:, lanes].T
        met[...] = matmul(hot_ref[:, :64], pair_rows(tilted, pair)).astype(BF16)
        for odd in range(2):
            mine, other = (low, high) if odd == 0 else (high, low)
            kaugs[odd][:, :LANES] = k_ref[:, lanes] * mine + hot_ref[...] * other
            qaugs[odd][:, :LANES] = q_ref[:, lanes] * mine + met[:, :LANES] * other
            skew_groups(bands[2 * pair + odd], wides.at[odd])

            @pl.when(pair > 0)
            def _():
                probs_copy(2 * pair + odd, odd).wait()

        for side in range(2):
            cols = slice(side * half, (side + 1) * half)
            tops = []
            for odd in range(2):
                whole = times_transposed(kaugs[odd][...], qaugs[odd][cols, :])
                steps_x = times_transposed(key_x[odd], met[cols, LANES : 2 * LANES])
                steps_y = times_transposed(key_y[odd], met[cols, 2 * LANES :])
                top = None
                for part in range(BLOCKS):
                    rows = slice(part * LANES, (part + 1) * LANES)
                    bias = []
                    for block in range(2 * side, 2 * side + 2):
                        step = max(-2, min(2, block - part)) + 2
                        bias.append(wides[odd, :, step * LANES : (step + 1) * LANES])
                    s = whole[rows] + jnp.concatenate(bias, axis=1)
                    s = s + steps_x[rows] * less_x[rows, cols].astype(F32)
                    s = s + steps_y[rows] * less_y[rows, cols].astype(F32)
                    scores[odd, rows, :] = s
                    best = jnp.max(s.reshape(LANES // 8, 8, half), axis=0)
                    top = best if top is None else jnp.maximum(top, best)
                tops.append(jnp.max(top, axis=0, keepdims=True))
            for odd in range(2):
                total = None
                for part in range(BLOCKS):
                    rows = slice(part * LANES, (part + 1) * LANES)
                    e = jnp.exp(scores[odd, rows, :] - tops[odd])
                    probs[odd][rows, cols] = e.astype(BF16)
                    add = jnp.sum(e.reshape(LANES // 8, 8, half), axis=0)
                    total = add if total is None else total + add
                share = 1.0 / jnp.sum(total, axis=0, keepdims=True)
                share_out[2 * pair + odd, :, cols] = share
                got = matmul(values_t[odd * HEAD_DIM : (odd + 1) * HEAD_DIM, :], probs[odd][:, cols])
                pair_t[odd * HEAD_DIM : (odd + 1) * HEAD_DIM, cols] = got * share
        for odd in range(2):
            probs_copy(2 * pair + odd, odd).start()
        both = pair_t[...]
        context_t[lanes, :] = both.astype(BF16)
        context[:, lanes] = both.T.astype(BF16)
        return carry

    lax.fori_loop(0, 2, one_pair, 0)
    exchange(cot_in, cot_ref, 1)
    gathering.second(2, 0)
    gathering.first(3, 0)
    gathering.second(2, 1)
    gathering.first(3, 1)
    lax.fori_loop(2, 4, one_pair, 0)
    for h in range(2):
        gathering.third(2, h)
        gathering.second(3, h)
    gathering.complete(2)
    stage_column(plan, flat, staged, 2)
    form_matrices(plan, staged, matrices, 2)
    keep_carry(plan, staged)
    write_out(w_in, w_in_out)
    lax.fori_loop(4, PAIRS, one_pair, 0)
    write_out(context_t, context_out)
    for h in range(2):
        gathering.third(3, h)

    def vector(name):
        return vec[0:1, VEC[name] : VEC[name] + D]

    for n in range(D // NBLOCK):
        lanes = slice(n * NBLOCK, (n + 1) * NBLOCK)
        bias = vec[0:1, VEC["out_bias"] + n * NBLOCK : VEC["out_bias"] + (n + 1) * NBLOCK]
        start[:, lanes] = start[:, lanes] + matmul(context[...], w_out[:, lanes]) + bias

    step_rows = 64

    def norm_first(n, carry):
        rows = pl.ds(pl.multiple_of(n * step_rows, step_rows), step_rows)
        x = start[rows, :]
        centred = x - jnp.mean(x, axis=1, keepdims=True)
        rstd = lax.rsqrt(jnp.mean(centred * centred, axis=1, keepdims=True) + norm_eps)
        xhat = centred * rstd
        hat[rows, :] = xhat
        rstd_out[rows, :] = jnp.broadcast_to(rstd, (step_rows, LANES))
        normed = xhat * vector("gain_one") + vector("shift_one")
        start[rows, :] = normed
        normed_low[rows, :] = normed.astype(BF16)
        return carry

    lax.fori_loop(0, WINLEN // step_rows, norm_first, 0)
    write_out(hat, hat_out)
    write_out(normed_low, normed_out)

    gathering.complete(3)
    stage_column(plan, flat, staged, 3)
    form_matrices(plan, staged, matrices, 3)
    write_out(w_back, w_back_out)
    for odd in range(2):
        probs_copy(0, odd).wait()
    exchanged(cot_ref, 1)
    own_cot.wait()
    for copy in written[1:]:
        copy.wait()
    finish_notes()
    gathering.finish()


def forward_pass(plan, params, hidden_in, cotangent, boxes, lengths):
    anywhere = pl.BlockSpec(memory_space=pl.ANY)
    vmem = pl.BlockSpec(memory_space=pltpu.VMEM)
    token = (WINLEN, D)

    def hbm(shape, dtype=BF16):
        return jax.ShapeDtypeStruct(shape, dtype), anywhere

    def near(shape, dtype=F32):
        return jax.ShapeDtypeStruct(shape, dtype), vmem

    outs = [
        hbm(MATRICES[0]), hbm(MATRICES[1]), hbm(MATRICES[3]), hbm(MATRICES[4]), hbm((D, WINLEN)), hbm(token),
        hbm(token), hbm(token), hbm(token), hbm((HEADS, WINLEN, WINLEN)), hbm((D, WINLEN)),
        hbm(token, F32), hbm(token), near((1, VEC_ROWS * LANES)), near((WINLEN, LANES)),
        near(token, BF16), near((WINLEN, LANES), BF16), near((2, WINLEN)),
        near((HEADS, 1, WINLEN)),
    ]
    scratch = [
        pltpu.VMEM((COLUMNS, CORES, DEPTH, COLUMNS, plan.quarter, LANES), BF16),
        pltpu.VMEM((plan.staged, LANES), F32),
        pltpu.VMEM((COLUMNS, plan.quarter, LANES), BF16),
    ]
    scratch += [pltpu.VMEM(layout, BF16) for layout in MATRICES]
    scratch += [
        pltpu.VMEM((NOTE_ROWS, LANES), BF16),
        pltpu.VMEM(token, BF16),
        pltpu.VMEM(token, BF16),
        pltpu.VMEM(token, F32),
        pltpu.VMEM(token, BF16),
        pltpu.VMEM(token, BF16),
        pltpu.VMEM(token, BF16),
        pltpu.VMEM(token, BF16),
        pltpu.VMEM((WINLEN, LANES), BF16),
        pltpu.VMEM((2, WINLEN, LANES), BF16),
        pltpu.VMEM((2, WINLEN, LANES), BF16),
        pltpu.VMEM((HEADS, 8, WIDE), F32),
        pltpu.VMEM((2 * HEADS, BUCKETS, LANES), F32),
        pltpu.VMEM((2, LANES, 5 * LANES), F32),
        pltpu.VMEM((2, WINLEN, 2 * LANES), F32),
        pltpu.VMEM((D, WINLEN), BF16),
        pltpu.VMEM((LANES, WINLEN), F32),
        pltpu.VMEM(token, F32),
        pltpu.VMEM((WINLEN, 11 * LANES), BF16),
        pltpu.VMEM((WINLEN, 4 * WINLEN), BF16),
        pltpu.VMEM((1, VEC_ROWS * LANES), F32),
        pltpu.SemaphoreType.DMA((2, 7)),
        pltpu.SemaphoreType.DMA((2, 2, DEPTH)),
        pltpu.SemaphoreType.DMA((16,)),
        pltpu.SemaphoreType.DMA((2,)),
    ]
    return pl.pallas_call(
        functools.partial(forward_kernel, plan),
        out_shape=[shape for shape, _ in outs],
        in_specs=[anywhere] * 3 + [vmem, pl.BlockSpec(memory_space=pltpu.SMEM), vmem],
        out_specs=[spec for _, spec in outs],
        scratch_shapes=scratch + sem_shapes(GATHER_SEMS),
        compiler_params=pltpu.CompilerParams(
            collective_id=0, has_side_effects=True, vmem_limit_bytes=62 * 2**20
        ),
        name="forward_pass",
    )(params, hidden_in, cotangent, boxes, lengths, jnp.asarray(turns_table()))


def token_info(doc_lengths, box_coords):
    places = jnp.arange(WINLEN, dtype=jnp.int32)
    first = places == 0
    doc = jnp.zeros((WINLEN,), jnp.int32)
    end = 0
    for d in range(3):
        end = end + doc_lengths[d]
        doc = doc + (places >= end).astype(jnp.int32)
        first = first | (places == end)
    rows = [box_coords[:, c] for c in range(4)] + [doc, first.astype(jnp.int32)]
    return jnp.stack(rows + [jnp.zeros_like(doc)] * 2).astype(F32)


class Reducing:
    def __init__(self, place, flat, swapped, one, two, deep, piece, result, sems, free):
        self.place = place
        self.flat = flat
        self.swapped = swapped
        self.one = one
        self.two = two
        self.deep = deep
        self.piece = piece
        self.result = result
        self.sems = sems
        self.free = free
        self.sent = {k: [] for k in range(COLUMNS)}

    def send(self, k, src, dst, kind, index, peer):
        copy = remote(src, dst, self.sems[kind].at[0, index], self.sems[kind].at[1, index], peer)
        copy.start()
        self.sent[k].append(copy)

    got = Gathering.got

    def settle(self, k):
        for copy in self.sent.pop(k):
            copy.wait_send()

    rows = Gathering.rows

    def swap(self, k, h):
        p = self.place
        slot = k % 2
        if k < 2 and h == 0:
            pl.semaphore_wait(self.free.at[slot], 1)
        self.send(
            k, self.flat.at[slot, 1 - p.core, :, :, self.rows(h)],
            self.swapped.at[slot, :, :, self.rows(h)], "core", 2 * k + h, p.peer_core,
        )

    def first(self, k, h):
        p = self.place
        slot = k % 2
        n, rows = 2 * k + h, self.rows(h)
        self.got(self.swapped.at[slot, :, :, rows], "core", n)

        def one(step, carry):
            z, quarter = step // COLUMNS, step % COLUMNS
            total = self.flat[slot, p.core, z, quarter, rows].astype(F32)
            total = total + self.swapped[slot, z, quarter, rows].astype(F32)
            self.flat[slot, p.core, z, quarter, rows] = total.astype(BF16)
            return carry

        lax.fori_loop(0, DEPTH * COLUMNS, one, 0)
        flat = self.flat
        for side, peer in ((0, p.peer_y), (1, p.peer_x)):
            self.send(
                k, flat.at[slot, p.core, 2 * side : 2 * side + 2, p.col_d, rows],
                self.one.at[k, side, :, rows], "one", 2 * n + side, peer,
            )
        if k >= 2 and h == 1:
            pl.semaphore_signal(
                self.free.at[slot], inc=1, device_id=p.peer_core, device_id_type=MESH
            )

    def second(self, k, h):
        p = self.place
        slot = k % 2
        n, rows = 2 * k + h, self.rows(h)
        for side, column in ((0, p.col_x), (1, p.col_y)):
            self.got(self.one.at[k, side, :, rows], "one", 2 * n + side)

            def one(step, carry, side=side, column=column):
                z = 2 * side + step
                total = self.flat[slot, p.core, z, column, rows].astype(F32)
                total = total + self.one[k, side, step, rows].astype(F32)
                self.flat[slot, p.core, z, column, rows] = total.astype(BF16)
                return carry

            lax.fori_loop(0, 2, one, 0)
        for side, column, peer in ((0, p.col_x, p.peer_x), (1, p.col_y, p.peer_y)):
            self.send(
                k, self.flat.at[slot, p.core, :, column, rows], self.two.at[k, side, :, rows], "two",
                2 * n + side, peer,
            )

    def third(self, k, h):
        p = self.place
        slot = k % 2
        n, rows = 2 * k + h, self.rows(h)
        for side in range(2):
            self.got(self.two.at[k, side, :, rows], "two", 2 * n + side)

        def one(z, carry):
            total = self.flat[slot, p.core, z, p.column, rows].astype(F32)
            total = total + self.two[k, 0, z, rows].astype(F32) + self.two[k, 1, z, rows].astype(F32)
            self.flat[slot, p.core, z, p.column, rows] = total.astype(BF16)
            return carry

        lax.fori_loop(0, DEPTH, one, 0)
        for d in range(DEPTH - 1):
            self.send(
                k, self.flat.at[slot, p.core, p.far[d], p.column, rows], self.deep.at[k, d, rows], "z",
                3 * n + d, p.peers_z[d],
            )

    def fourth(self, k, h):
        p = self.place
        n, rows = 2 * k + h, self.rows(h)
        for d in range(DEPTH - 1):
            self.got(self.deep.at[k, d, rows], "z", 3 * n + d)
        total = self.flat[k % 2, p.core, p.z, p.column, rows].astype(F32)
        for d in range(DEPTH - 1):
            total = total + self.deep[k, d, rows].astype(F32)
        self.piece[k, rows] = total.astype(BF16)

    def giving(self, k, h):
        p = self.place
        sems = self.sems["spread"]
        return remote(
            self.piece.at[k, self.rows(h)], self.result.at[p.column, self.rows(h)],
            sems.at[0, 2 * k + h], sems.at[1, 2 * p.column + h], p.at(k, p.core, p.z),
        )

    def give(self, k, h):
        @pl.when(self.place.column != k)
        def _():
            self.giving(k, h).start()

    def given(self, k, h):
        @pl.when(self.place.column != k)
        def _():
            self.giving(k, h).wait_send()

    def receive(self, out):
        p = self.place
        out[p.column] = self.piece[p.column].astype(F32)
        for column in (p.col_x, p.col_y, p.col_d):
            for h in range(2):
                self.got(self.result.at[column, self.rows(h)], "spread", 2 * column + h)
            out[column] = self.result[column].astype(F32)


REDUCE_SEMS = {"spread": 8, "z": 24, "one": 16, "two": 16, "core": 8}


def unstage_column(plan, flat, staged, k):
    def one(step, carry):
        shard, quarter = step // COLUMNS, step % COLUMNS
        base = plan.carry + shard * plan.rows + quarter * plan.quarter
        piece = staged[pl.ds(pl.multiple_of(base, 8), plan.quarter), :]
        flat[k % 2, shard // DEPTH, shard % DEPTH, quarter] = piece.astype(BF16)
        return carry

    lax.fori_loop(0, CORES * DEPTH * COLUMNS, one, 0)


class Notes:
    def __init__(self, place, notes, slots, sems):
        self.place, self.notes, self.slots, self.sems = place, notes, slots, sems
        p = place
        self.home = (p.column == COLUMNS - 1) & (p.core == CORES - 1)
        self.root = self.home & (p.z == DEPTH - 1)

    def copy(self, slot, peer):
        return remote(
            self.notes, self.slots.at[slot], self.sems.at[0, 0], self.sems.at[1, slot], peer
        )

    def take(self, slot):
        self.copy(slot, self.place.peer_core).wait_recv()
        self.notes[...] = self.notes[...] + self.slots[slot]

    def start(self):
        p = self.place

        @pl.when(p.core != CORES - 1)
        def _():
            self.copy(0, p.peer_core).start()

    def rise(self):
        p = self.place

        @pl.when(p.core == CORES - 1)
        def _():
            self.take(0)

        @pl.when((p.core == CORES - 1) & (p.column != COLUMNS - 1))
        def _():
            self.copy(1 + p.column, p.at(COLUMNS - 1, p.core, p.z)).start()

    def end(self):
        p = self.place

        @pl.when(self.home)
        def _():
            for slot in range(1, 4):
                self.take(slot)

        @pl.when(self.home & (p.z != DEPTH - 1))
        def _():
            self.copy(4 + p.z, p.at(p.column, p.core, DEPTH - 1)).start()

        @pl.when(self.root)
        def _():
            for slot in range(4, 7):
                self.take(slot)

        @pl.when(jnp.logical_not(self.root))
        def _():
            self.copy(0, p.peer_core).wait_send()


def cell_sums(whole, less):
    lane = lax.broadcasted_iota(jnp.int32, (1, LANES), 1)
    sub = lax.broadcasted_iota(jnp.int32, (8, LANES), 0)
    sums = []
    for axis in range(2):
        rows = slice(axis * BUCKETS, (axis + 1) * BUCKETS)
        every = pltpu.roll(whole[rows], (BUCKETS - axis * BUCKETS) % LANES, 1)
        below = pltpu.roll(less[rows], (BUCKETS - axis * BUCKETS) % LANES, 1)
        inside = (lane >= BUCKETS) & (lane < 2 * BUCKETS)
        every = jnp.where(inside, every, 0.0)
        below = jnp.where(inside, below, 0.0)
        x = every - below + pltpu.roll(below, LANES - 1, 1)
        total = None
        for group in range(BUCKETS // 8):
            y = x[8 * group : 8 * group + 8]
            y = y if group == 0 else pltpu.roll(y, LANES - 8 * group, 1)
            total = y if total is None else total + y
        for bit in (1, 2, 4):
            total = jnp.where((sub & bit) != 0, pltpu.roll(total, LANES - bit, 1), total)
        sums.append(jnp.sum(total, axis=0, keepdims=True))
    return sums


def exact_dot(a, b):
    return jnp.dot(a, b, preferred_element_type=F32, precision=lax.Precision.HIGHEST)


def bucket_rows(cell_ref, diag_ref):
    half = BUCKETS // 2
    column = lax.broadcasted_iota(jnp.int32, (1, LANES), 1)
    row = lax.broadcasted_iota(jnp.int32, (LANES, 1), 0)
    to = jnp.clip(row - BUCKETS, -half, half - 1) + half
    place = lax.broadcasted_iota(jnp.int32, (WIDE, 1), 0)
    along = place - LANES
    far = jnp.where(place < LANES, 0, jnp.where(place < 5 * LANES, 0, BUCKETS - 1))
    along = jnp.where(
        (place >= LANES) & (place < 4 * LANES),
        jnp.clip(along - LANES, -half, half - 1) + half,
        far,
    )
    first, rest = None, None
    zero = jnp.zeros((5, WIDE), F32)
    for m in range(4):
        hot_along = jnp.where(along + m * BUCKETS == column, 1.0, 0.0)
        got = exact_dot(
            jnp.concatenate([diag_ref[4 * n + m] for n in range(3)] + [zero], axis=0), hot_along
        )
        first = got if first is None else first + got
        hot_cell = jnp.where(to + m * BUCKETS == column, 1.0, 0.0)
        rows = [cell_ref[t * HEADS + 4 * n + m] for t in range(2) for n in range(3)]
        got = exact_dot(jnp.concatenate(rows + [zero[:2, :LANES]], axis=0), hot_cell)
        rest = got if rest is None else rest + got
    return jnp.concatenate([first[:3], rest[:6]], axis=0)


def backward_kernel(
    plan, w_back_in, w_in_in, w_out_in, w_qkv_in, normed_in, low_in, features_in,
    context_in, q_in, k_in, v_in, probs_in, hat_in, cot_in, rstd_ref, vec, hot_ref, rest_ref, share_ref,
    *refs,
):
    out, output_pos, hidden_pos, spill = refs[:4]
    (flat, staged, swapped, one_buf, two_buf, deep, piece, result, active, slope, w_back, w_in, w_out,
     turned, context_t, q_ref, k_ref, v_ref, hat, second, branch, dctx, probs, less_x,
     less_y, scores_odd, bands, hot_t, pair_t, scaled, share_cols, vecg, cell_rows, diag_rows, notes, slots,
     ) = refs[4:40]
    load_sems, probs_sems, free, pos_sems, note_sems, spill_sems = refs[40:46]
    place = Place()
    reducing = Reducing(
        place, flat, swapped, one_buf, two_buf, deep, piece, result,
        dict(zip(REDUCE_SEMS, refs[46:])), free,
    )
    climbing = Notes(place, notes, slots, note_sems)
    loads = {}

    def load(name, src, dst):
        loads[name] = pltpu.make_async_copy(src, dst, load_sems.at[len(loads)])
        loads[name].start()

    mixed = active.at[:, : 3 * D]
    grad_attn = branch
    w_qkv = w_in.at[:, : 3 * D]
    hidden_low = dctx
    features_t = w_back.at[:D, :WINLEN]
    low_t = w_out.at[:WINLEN]
    scores = [hat.at[:, :WINLEN], scores_odd]
    dscores = [w_back.at[2 * WINLEN : 3 * WINLEN, :WINLEN], w_back.at[3 * WINLEN : 4 * WINLEN, :WINLEN]]
    low_turned = w_back.at[4 * WINLEN : 4 * WINLEN + D, :WINLEN]
    output_low = w_out.at[:WINLEN]
    output_low = w_out.at[:WINLEN]
    dscores_x = [slope.at[:, 2 * WINLEN : 3 * WINLEN], slope.at[:, 3 * WINLEN : 4 * WINLEN]]
    dscores_y = [slope.at[:, 4 * WINLEN : 5 * WINLEN], slope.at[:, 5 * WINLEN :]]

    load("normed", normed_in, dctx)
    load("w_in", w_in_in, w_in)
    load("hat", hat_in, hat)
    load("w_back", w_back_in, w_back)
    load("cot", cot_in, branch)

    at = staged_at(plan, COLUMNS - 1, plan.misc_start)
    staged[at:, :] = jnp.zeros((plan.staged - at, LANES), F32)
    place.greet()

    quarter = WINLEN // DEPTH
    positions = []

    def to_pos(source, target, kind):
        for d in range(DEPTH - 1):
            rows = pl.ds(pl.multiple_of(place.far[d] * quarter, quarter), quarter)
            copy = remote(
                source.at[rows], target.at[place.z], pos_sems.at[kind, 0, d], pos_sems.at[kind, 1, d],
                place.peers_z[d],
            )
            copy.start()
            positions.append(copy)
        rows = pl.ds(pl.multiple_of(place.z * quarter, quarter), quarter)
        copy = pltpu.make_async_copy(
            source.at[rows], target.at[place.z], pos_sems.at[kind, 0, DEPTH - 1]
        )
        copy.start()
        return copy

    def in_pos(target, kind):
        for d in range(DEPTH - 1):
            there = target.at[place.from_far[d]]
            remote(
                there, there, pos_sems.at[kind, 0, d], pos_sems.at[kind, 1, d], place.peer_x
            ).wait_recv()


    def store(k, index, row, value, first_block=0):
        blocks = MATRICES[index][1] // LANES
        base = staged_at(plan, k, plan.starts[index]) + row * blocks + first_block
        for block in range(value.shape[1] // LANES):
            staged[pl.ds(base + block, value.shape[0], stride=blocks), :] = value[
                :, block * LANES : (block + 1) * LANES
            ]

    def column_sum(value):
        return jnp.sum(value, axis=0, keepdims=True)

    def keep_vector(name, lanes_at, value):
        at = pl.multiple_of(VEC[name] + lanes_at, LANES)
        vecg[0:1, pl.ds(at, value.shape[1])] = value

    def vector(name, at=0, size=D):
        return vec[0:1, pl.ds(pl.multiple_of(VEC[name] + at, LANES), size)]

    loads["normed"].wait()
    loads["w_in"].wait()

    def widen(n, carry):
        at = pl.multiple_of(n * NBLOCK, NBLOCK)
        lanes = pl.ds(at, NBLOCK)
        inner_act = matmul(dctx[...], w_in[:, lanes]) + vector("in_bias", at, NBLOCK)
        value, change = gelu_and_slope(inner_act)
        active[:, lanes] = value.astype(BF16)
        slope[:, lanes] = change.astype(BF16)
        return carry

    lax.fori_loop(0, FF // NBLOCK, widen, 0, unroll=2)
    loads["hat"].wait()
    loads["w_back"].wait()
    for n in range(D // NBLOCK):
        lanes = slice(n * NBLOCK, (n + 1) * NBLOCK)
        normed = hat[:, lanes] * vector("gain_one", n * NBLOCK, NBLOCK) + vector(
            "shift_one", n * NBLOCK, NBLOCK
        )
        second[:, lanes] = (
            normed + matmul(active[...], w_back[:, lanes]) + vector("back_bias", n * NBLOCK, NBLOCK)
        )
    loads["cot"].wait()
    step_rows = 64
    for name in ("gain_two", "shift_two", "back_bias", "gain_one", "shift_one", "out_bias"):
        keep_vector(name, 0, jnp.zeros((1, D), F32))

    def add_vector(name, term):
        lanes = slice(VEC[name], VEC[name] + D)
        vecg[0:1, lanes] = vecg[0:1, lanes] + column_sum(term)

    def norm_second(n, carry):
        rows = pl.ds(pl.multiple_of(n * step_rows, step_rows), step_rows)
        x = second[rows, :]
        centred = x - jnp.mean(x, axis=1, keepdims=True)
        rstd = lax.rsqrt(jnp.mean(centred * centred, axis=1, keepdims=True) + norm_eps)
        xhat = centred * rstd
        gain = vector("gain_two")
        output_low[rows, :] = (xhat * gain + vector("shift_two")).astype(BF16)
        cot = branch[rows, :].astype(F32)
        prod = cot * xhat
        gc = cot * gain
        mean_one = jnp.mean(gc, axis=1, keepdims=True)
        mean_two = jnp.mean(prod * gain, axis=1, keepdims=True)
        value = rstd * (gc - mean_one - xhat * mean_two)
        second[rows, :] = value
        value = value.astype(BF16)
        branch[rows, :] = value
        add_vector("gain_two", prod)
        add_vector("shift_two", cot)
        add_vector("back_bias", value.astype(F32))
        return carry

    lax.fori_loop(0, WINLEN // step_rows, norm_second, 0, unroll=2)
    own_output = to_pos(output_low, output_pos, 0)

    def back_rows(k, size, begin, count):
        def body(n, carry):
            row = pl.multiple_of(begin + n * size, LANES)
            turned[:size, :] = active[:, pl.ds(row, size)].T
            store(k, 4, row, matmul(turned[:size, :], branch[...]))
            return carry

        lax.fori_loop(0, count, body, 0)

    back_rows(3, WINLEN, 512, FF // WINLEN - 1)
    unstage_column(plan, flat, staged, 3)
    reducing.swap(3, 0)
    reducing.swap(3, 1)

    back_rows(2, WINLEN, 0, 1)
    back_rows(2, LANES, 512, 1)

    def inner(n, carry):
        at = pl.multiple_of(n * NBLOCK, NBLOCK)
        lanes = pl.ds(at, NBLOCK)
        value = times_transposed(branch[...], w_back[lanes, :]) * slope[:, lanes].astype(F32)
        value = value.astype(BF16)
        slope[:, lanes] = value
        keep_vector("in_bias", at, column_sum(value.astype(F32)))
        return carry

    lax.fori_loop(0, FF // NBLOCK, inner, 0, unroll=2)
    grad_inner = slope
    reducing.first(3, 0)
    reducing.first(3, 1)

    for n in range(D // NBLOCK):
        rows = slice(n * NBLOCK, (n + 1) * NBLOCK)
        turned[rows, :] = dctx[:, rows].T

    def in_rows(k, begin, end):
        def body(n, carry):
            lanes = pl.ds(pl.multiple_of(n * NBLOCK, NBLOCK), NBLOCK)
            got = matmul(turned[begin:end, :], grad_inner[:, lanes])
            store(k, 3, begin, got, n * (NBLOCK // LANES))
            return carry

        lax.fori_loop(0, FF // NBLOCK, body, 0)

    in_rows(2, 288, D)
    unstage_column(plan, flat, staged, 2)
    reducing.swap(2, 0)
    reducing.swap(2, 1)
    reducing.second(3, 0)
    reducing.second(3, 1)

    load("context", context_in, context_t)
    load("q", q_in, q_ref)
    load("k", k_in, k_ref)
    load("v", v_in, v_ref)
    for odd in range(2):
        pltpu.make_async_copy(probs_in.at[odd], probs.at[odd], probs_sems.at[odd]).start()
    for n in range(D // NBLOCK):
        lanes = slice(n * NBLOCK, (n + 1) * NBLOCK)
        second[:, lanes] = second[:, lanes] + times_transposed(grad_inner[...], w_in[lanes, :])
    load("w_qkv", w_qkv_in, w_qkv)
    load("features", features_in, features_t)
    reducing.first(2, 0)
    reducing.first(2, 1)

    for copy in positions:
        copy.wait_send()
    own_output.wait()
    load("w_out", w_out_in, w_out)

    def norm_first(n, carry):
        rows = pl.ds(pl.multiple_of(n * step_rows, step_rows), step_rows)
        grad = second[rows, :]
        xhat = hat[rows, :]
        prod = grad * xhat
        gain = vec[0:1, VEC["gain_one"] : VEC["gain_one"] + D]
        gc = grad * gain
        mean_one = jnp.mean(gc, axis=1, keepdims=True)
        mean_two = jnp.mean(prod * gain, axis=1, keepdims=True)
        value = rstd_ref[rows, 0:1] * (gc - mean_one - xhat * mean_two)
        second[rows, :] = value
        value = value.astype(BF16)
        grad_attn[rows, :] = value
        add_vector("gain_one", prod)
        add_vector("shift_one", grad)
        add_vector("out_bias", value.astype(F32))
        return carry

    lax.fori_loop(0, WINLEN // step_rows, norm_first, 0, unroll=2)
    reducing.third(3, 0)
    reducing.third(3, 1)
    loads["w_out"].wait()
    for n in range(D // NBLOCK):
        lanes = slice(n * NBLOCK, (n + 1) * NBLOCK)
        dctx[:, lanes] = times_transposed(grad_attn[...], w_out[lanes, :]).astype(BF16)
    load("low", low_in, low_t)
    loads["context"].wait()
    reducing.second(2, 0)
    reducing.second(2, 1)

    def out_rows(k, begin, end):
        for n in range(D // NBLOCK):
            lanes = slice(n * NBLOCK, (n + 1) * NBLOCK)
            got = matmul(context_t[begin:end, :], grad_attn[:, lanes])
            store(k, 1, begin, got, n * (NBLOCK // LANES))

    reducing.fourth(3, 0)
    reducing.fourth(3, 1)
    reducing.give(3, 0)
    reducing.give(3, 1)

    low, high = half_masks()
    rest = rest_ref[...]
    columns = jnp.concatenate([rest, jnp.zeros((LANES - 2, WINLEN), F32)], axis=0).T
    for part in range(BLOCKS):
        rows = slice(part * LANES, (part + 1) * LANES)
        for axis, less in ((0, less_x), (1, less_y)):
            less[rows, :] = jnp.where(
                rest[axis : axis + 1, :] < columns[rows, axis : axis + 1], 1.0, 0.0
            ).astype(BF16)
    hot_t[...] = hot_ref[...].T
    lane = lax.broadcasted_iota(jnp.int32, (1, LANES), 1)
    scale = HEAD_DIM ** (-0.5)
    of_x = jnp.where((lane // BUCKETS) % 2 == 0, 1.0, 0.0)
    share_cols[...] = jnp.concatenate(
        [share_ref[head] for head in range(HEADS)] + [jnp.zeros((LANES - HEADS, WINLEN), F32)], axis=0
    ).T
    for name in ("q", "k", "v"):
        loads[name].wait()

    def probs_copy(head, odd):
        return pltpu.make_async_copy(probs_in.at[head], probs.at[odd], probs_sems.at[odd])

    def spill_copy(head, odd):
        return pltpu.make_async_copy(dscores[odd], spill.at[head], spill_sems.at[odd])

    def one_pair(pair, carry):
        at = pl.multiple_of(pair * LANES, LANES)
        lanes = pl.ds(at, LANES)
        keys_t = k_ref[:, lanes].T
        both = pltpu.roll(share_cols[...], lax.rem(LANES - 2 * pair, LANES), 1)
        both = jnp.where(lane < HEAD_DIM, both[:, 0:1], both[:, 1:2])
        scaled[...] = (dctx[:, lanes].astype(F32) * both).astype(BF16)
        grad_context = dctx[:, lanes]
        dots = []
        for odd in range(2):
            mine, other = (low, high) if odd == 0 else (high, low)
            head = 2 * pair + odd
            probs_copy(head, odd).wait()
            products = times_transposed(v_ref[:, lanes] * mine, grad_context)
            dot = None
            for part in range(BLOCKS):
                rows = slice(part * LANES, (part + 1) * LANES)
                dp = products[rows]
                scores[odd][rows, :] = dp
                add = dp * probs[odd, rows, :].astype(F32)
                add = jnp.sum(add.reshape(LANES // 8, 8, WINLEN), axis=0)
                dot = add if dot is None else dot + add
            dots.append(column_sum(dot) * share_ref[head])
        for odd in range(2):
            head = 2 * pair + odd
            share = share_ref[head]

            @pl.when(pair > 0)
            def _():
                spill_copy(head, odd).wait()

            for part in range(BLOCKS):
                rows = slice(part * LANES, (part + 1) * LANES)
                ds = probs[odd, rows, :].astype(F32) * ((scores[odd][rows, :] - dots[odd]) * share)
                dscores[odd][rows, :] = ds.astype(BF16)
            spill_copy(head, odd).start()
        for odd in range(2):
            head = 2 * pair + odd
            keys_grad = matmul(dscores[odd][...], q_ref[:, lanes])
            values_grad = matmul(probs[odd], scaled[...])

            pair_t[odd * HEAD_DIM : (odd + 1) * HEAD_DIM, :] = matmul(
                keys_t[odd * HEAD_DIM : (odd + 1) * HEAD_DIM, :], dscores[odd][...]
            )
            for which, value in ((1, keys_grad), (2, values_grad)):
                there = pl.ds(pl.multiple_of(at + which * D, LANES), LANES)
                value = value.astype(BF16)
                if odd:
                    value = mixed[:, there] * low + value * high
                mixed[:, there] = value

        @pl.when(pair < PAIRS - 1)
        def _():
            for odd in range(2):
                probs_copy(2 * pair + odd + 2, odd).start()

        value = (pair_t[...].T * scale).astype(BF16)
        mixed[:, lanes] = value
        keep_vector("q_bias", at, column_sum(value.astype(F32)))
        there = pl.ds(pl.multiple_of(at + 2 * D, LANES), LANES)
        keep_vector("v_bias", at, column_sum(mixed[:, there].astype(F32)))
        return carry

    lax.fori_loop(0, 2, one_pair, 0)
    reducing.third(2, 0)
    reducing.third(2, 1)
    lax.fori_loop(2, 4, one_pair, 0)
    reducing.fourth(2, 0)
    reducing.fourth(2, 1)
    reducing.give(2, 0)
    reducing.give(2, 1)
    lax.fori_loop(4, PAIRS, one_pair, 0)

    for odd in range(2):
        spill_copy(0, odd).wait()
    loads["low"].wait()
    for n in range(D // NBLOCK):
        rows = slice(n * NBLOCK, (n + 1) * NBLOCK)
        low_turned[rows, :] = low_t[:, rows].T

    def qkv_rows(n, carry):
        lanes = pl.ds(pl.multiple_of(n * NBLOCK, NBLOCK), NBLOCK)
        store(0, 0, 0, matmul(low_turned[...], mixed[:, lanes]), n * (NBLOCK // LANES))
        return carry

    lax.fori_loop(0, 3 * D // NBLOCK, qkv_rows, 0)
    out_rows(0, 0, 208)
    reducing.settle(2)
    unstage_column(plan, flat, staged, 0)
    reducing.swap(0, 0)
    reducing.swap(0, 1)

    loads["w_qkv"].wait()
    for n in range(D // NBLOCK):
        lanes = slice(n * NBLOCK, (n + 1) * NBLOCK)
        value = second[:, lanes] + times_transposed(mixed[...], w_qkv[lanes, :])
        hidden_low[:, lanes] = value.astype(BF16)
    own_hidden = to_pos(hidden_low, hidden_pos, 1)
    reducing.first(0, 0)
    reducing.first(0, 1)
    loads["features"].wait()
    for n in range(D // NBLOCK):
        lanes = slice(n * NBLOCK, (n + 1) * NBLOCK)
        store(1, 2, 0, matmul(features_t[...], hidden_low[:, lanes]), n * (NBLOCK // LANES))
    in_rows(1, 0, 304)
    out_rows(1, 192, D)
    reducing.settle(3)
    unstage_column(plan, flat, staged, 1)
    reducing.swap(1, 0)
    reducing.swap(1, 1)
    reducing.second(0, 0)
    reducing.second(0, 1)

    def fetch_scores(head):
        there = slope.at[:, pl.ds(pl.multiple_of(lax.rem(head, 2) * WINLEN, WINLEN), WINLEN)]
        return pltpu.make_async_copy(spill.at[head], there, spill_sems.at[lax.rem(head, 2)])

    cells = [hot_ref[...] * of_x.astype(BF16), hot_ref[...] * (1.0 - of_x).astype(BF16)]
    band = bands.at[0]
    parts_x = slope.at[:, 2 * WINLEN : 3 * WINLEN]
    parts_y = slope.at[:, 3 * WINLEN : 4 * WINLEN]

    def one_table(head, carry):
        fetch_scores(head).wait()

        @pl.when(head < HEADS - 1)
        def _():
            fetch_scores(head + 1).start()

        here = slope.at[:, pl.ds(pl.multiple_of(lax.rem(head, 2) * WINLEN, WINLEN), WINLEN)]
        band[...] = jnp.zeros_like(band)
        for part in range(BLOCKS):
            rows = slice(part * LANES, (part + 1) * LANES)
            low_ds = here[rows, :]
            parts_x[rows, :] = low_ds * less_x[rows, :]
            parts_y[rows, :] = low_ds * less_y[rows, :]
            ds = low_ds.astype(F32)
            for block in range(BLOCKS):
                step = max(-2, min(2, block - part)) + 2
                where = slice(step * LANES, (step + 1) * LANES)
                band[:, where] = band[:, where] + ds[:, block * LANES : (block + 1) * LANES]
        whole = matmul(here[...], hot_ref[...])
        less = matmul(parts_x[...], cells[0]) + matmul(parts_y[...], cells[1])
        diag_rows[head, :, LANES : 5 * LANES] = diagonal_sums(band)
        diag_rows[head, :, :LANES] = column_sum(band[:, :LANES])
        diag_rows[head, :, 5 * LANES :] = column_sum(band[:, 4 * LANES :])
        sums = []
        for summed in (whole, less):
            first = summed.astype(BF16)
            remainder = (summed - first.astype(F32)).astype(BF16)
            sums.append(matmul(hot_t[:64, :], first) + matmul(hot_t[:64, :], remainder))
        for axis, value in enumerate(cell_sums(sums[0], sums[1])):
            cell_rows[axis * HEADS + head] = value
        return carry

    fetch_scores(0).start()
    reducing.first(1, 0)
    reducing.first(1, 1)
    lax.fori_loop(0, 4, one_table, 0)
    reducing.third(0, 0)
    reducing.second(1, 0)
    reducing.third(0, 1)
    reducing.second(1, 1)
    lax.fori_loop(4, 8, one_table, 0)
    reducing.fourth(0, 0)
    reducing.give(0, 0)
    reducing.third(1, 0)
    reducing.fourth(0, 1)
    reducing.give(0, 1)
    lax.fori_loop(8, HEADS, one_table, 0)
    notes[...] = jnp.zeros_like(notes)
    table = VEC["tables"] // LANES
    for row in range(table):
        notes[row : row + 1, :] = vecg[0:1, row * LANES : (row + 1) * LANES]
    notes[table : table + 9, :] = bucket_rows(cell_rows, diag_rows)
    climbing.start()
    reducing.third(1, 1)
    climbing.rise()
    reducing.fourth(1, 0)
    reducing.give(1, 0)
    climbing.end()
    reducing.fourth(1, 1)
    reducing.give(1, 1)
    reducing.receive(out)
    note_quarter, note_first, note_row = note_place(plan)
    base = note_first + note_row

    @pl.when(climbing.root)
    def _():
        out[note_quarter, base : base + MISC_ROWS, :] = (
            out[note_quarter, base : base + MISC_ROWS, :] + notes[:MISC_ROWS, :]
        )

    in_pos(output_pos, 0)
    in_pos(hidden_pos, 1)
    own_hidden.wait()
    for copy in positions[DEPTH - 1 :]:
        copy.wait_send()
    for k in range(COLUMNS):
        for h in range(2):
            reducing.given(k, h)
    reducing.settle(1)
    reducing.settle(0)


def backward_pass(plan, operands):
    anywhere = pl.BlockSpec(memory_space=pl.ANY)
    vmem = pl.BlockSpec(memory_space=pltpu.VMEM)
    token = (WINLEN, D)
    block = (plan.quarter, LANES)
    positions = jax.ShapeDtypeStruct((DEPTH, WINLEN // DEPTH, D), BF16)
    scratch = [
        pltpu.VMEM((2, CORES, DEPTH, COLUMNS) + block, BF16),
        pltpu.VMEM((plan.staged, LANES), F32),
        pltpu.VMEM((2, DEPTH, COLUMNS) + block, BF16),
        pltpu.VMEM((COLUMNS, 2, 2) + block, BF16),
        pltpu.VMEM((COLUMNS, 2, DEPTH) + block, BF16),
        pltpu.VMEM((COLUMNS, DEPTH - 1) + block, BF16),
        pltpu.VMEM((COLUMNS,) + block, BF16),
        pltpu.VMEM((COLUMNS,) + block, BF16),
        pltpu.VMEM((WINLEN, FF), BF16),
        pltpu.VMEM((WINLEN, FF), BF16),
        pltpu.VMEM((FF, D), BF16),
        pltpu.VMEM((D, FF), BF16),
        pltpu.VMEM((D, D), BF16),
        pltpu.VMEM((D, WINLEN), BF16),
        pltpu.VMEM((D, WINLEN), BF16),
        pltpu.VMEM(token, BF16),
        pltpu.VMEM(token, BF16),
        pltpu.VMEM(token, BF16),
        pltpu.VMEM(token, F32),
        pltpu.VMEM(token, F32),
        pltpu.VMEM(token, BF16),
        pltpu.VMEM(token, BF16),
        pltpu.VMEM((2, WINLEN, WINLEN), BF16),
        pltpu.VMEM((WINLEN, WINLEN), BF16),
        pltpu.VMEM((WINLEN, WINLEN), BF16),
        pltpu.VMEM((WINLEN, WINLEN), F32),
        pltpu.VMEM((1, LANES, 5 * LANES), F32),
        pltpu.VMEM((LANES, WINLEN), BF16),
        pltpu.VMEM((LANES, WINLEN), F32),
        pltpu.VMEM((WINLEN, LANES), BF16),
        pltpu.VMEM((WINLEN, LANES), F32),
        pltpu.VMEM((1, VEC_ROWS * LANES), F32),
        pltpu.VMEM((2 * HEADS, 1, LANES), F32),
        pltpu.VMEM((HEADS, 1, WIDE), F32),
        pltpu.VMEM((NOTE_ROWS, LANES), F32),
        pltpu.VMEM((7, NOTE_ROWS, LANES), F32),
        pltpu.SemaphoreType.DMA((16,)),
        pltpu.SemaphoreType.DMA((2,)),
        pltpu.SemaphoreType.REGULAR((2,)),
        pltpu.SemaphoreType.DMA((2, 2, DEPTH)),
        pltpu.SemaphoreType.DMA((2, 7)),
        pltpu.SemaphoreType.DMA((2,)),
    ]
    return pl.pallas_call(
        functools.partial(backward_kernel, plan),
        out_shape=[
            jax.ShapeDtypeStruct((COLUMNS,) + block, F32), positions, positions,
            jax.ShapeDtypeStruct((HEADS, WINLEN, WINLEN), BF16),
        ],
        in_specs=[anywhere] * 14 + [vmem] * 5,
        out_specs=[vmem] + [anywhere] * 3,
        scratch_shapes=scratch + sem_shapes(REDUCE_SEMS),
        compiler_params=pltpu.CompilerParams(
            collective_id=1, has_side_effects=True, vmem_limit_bytes=62 * 2**20
        ),
        name="backward_pass",
    )(*operands)


def fast_shards(hidden_in, cotangent, box_coords, doc_lengths, params, moment_one, moment_two):
    shard_len = params.shape[0]
    plan = Plan(shard_len)
    (proj_qkv, proj_out, proj_in, proj_back, features_t, start_low, queries, keys, values, probs, context_t,
     xhat, normed_low, vec, rstd, cot, hot_two,
     rest_rows, share) = forward_pass(
        plan, params.reshape(plan.rows, LANES), hidden_in, cotangent,
        jnp.transpose(box_coords, (0, 2, 1)), doc_lengths,
    )
    summed, output_low, grad_hidden, _ = backward_pass(
        Plan(shard_len, carry=5 * LANES),
        (proj_back, proj_in, proj_out, proj_qkv, normed_low, start_low, features_t, context_t, queries, keys,
         values, probs, xhat, cot, rstd, vec, hot_two, rest_rows, share),
    )
    grad_share = summed.reshape(plan.padded, LANES)[: plan.rows].reshape(-1)
    return finish_step(output_low, grad_hidden, grad_share, params, moment_one, moment_two)


def finish_step(output_low, grad_hidden, grad_share, params, moment_one, moment_two):
    shard_len = params.shape[0]
    index = lax.axis_index("dp") * lax.axis_size("head") + lax.axis_index("head")
    flat_index = index * shard_len + jnp.arange(shard_len, dtype=jnp.int32)
    param_step, new_one = adam_step(params, moment_one, moment_two, grad_share, flat_index)
    return (output_low, grad_hidden, grad_share, param_step, new_one)


def to_windows(shard):
    return lax.all_to_all(shard, "head", split_axis=0, concat_axis=1, tiled=True)


def to_positions(window):
    return lax.all_to_all(window, "head", split_axis=1, concat_axis=0, tiled=True)


def plain_shards(hidden_in, cotangent, box_coords, doc_lengths, params, moment_one, moment_two):
    head_pos = lax.axis_index("head")
    groups = lax.axis_size("head")
    shard_len = params.shape[0]
    flat_params = lax.all_gather(params.astype(BF16), ("dp", "head"), axis=0, tiled=True)
    pieces = unpack(flat_params)
    hidden = to_windows(hidden_in).reshape(WINLEN, D)
    cot = to_windows(cotangent).reshape(WINLEN, D)
    own_box = lax.dynamic_index_in_dim(box_coords, head_pos, 0, keepdims=False)
    own_lengths = lax.dynamic_index_in_dim(doc_lengths, head_pos, 0, keepdims=False)
    chosen, relative, centre_x, centre_y = window_layout(own_lengths, own_box)
    features = box_features(relative).astype(BF16)

    proj_qkv, proj_out, proj_box, proj_in, proj_back = pieces[:5]
    qv_bias, out_bias, norm_one, in_bias, back_bias, norm_two, tables = pieces[5:]
    ops = bias_operands(tables, chosen, centre_x, centre_y)
    start_state = hidden.astype(F32) + matmul(features, proj_box)
    start_low = start_state.astype(BF16)
    qv_float = qv_bias.astype(F32)
    mixed = matmul(start_low, proj_qkv)
    queries = (mixed[:, :D] + qv_float[0]).astype(BF16) * jnp.asarray(HEAD_DIM ** (-0.5), BF16)
    keys = mixed[:, D : 2 * D].astype(BF16)
    values = (mixed[:, 2 * D :] + qv_float[1]).astype(BF16)

    probs, context_t = attention_forward(queries, keys, values, ops)
    first_sum = start_state + rows_inner(context_t, proj_out) + out_bias.astype(F32)
    normed, norm_one_back = jax.vjp(layer_norm, first_sum, norm_one.astype(F32))
    normed_low = normed.astype(BF16)
    inner_act = matmul(normed_low, proj_in) + in_bias.astype(F32)
    active, gelu_back = jax.vjp(gelu_exact, inner_act)
    active_low = active.astype(BF16)
    second_sum = normed + matmul(active_low, proj_back) + back_bias.astype(F32)
    output, norm_two_back = jax.vjp(layer_norm, second_sum, norm_two.astype(F32))
    output_low = to_positions(output.astype(BF16).reshape(1, WINLEN, D))

    grad_second, grad_norm_two = norm_two_back(cot.astype(F32))
    grad_branch = grad_second.astype(BF16)
    grad_proj_back = rows_inner(active_low, grad_branch)
    grad_back_bias = jnp.sum(grad_branch.astype(F32), axis=0)
    (grad_inner_f,) = gelu_back(times_transposed(grad_branch, proj_back))
    grad_inner = grad_inner_f.astype(BF16)
    grad_proj_in = rows_inner(normed_low, grad_inner)
    grad_in_bias = jnp.sum(grad_inner.astype(F32), axis=0)
    grad_first, grad_norm_one = norm_one_back(grad_second + times_transposed(grad_inner, proj_in))
    grad_attn = grad_first.astype(BF16)
    grad_proj_out = matmul(context_t, grad_attn)
    grad_out_bias = jnp.sum(grad_attn.astype(F32), axis=0)
    grad_context = times_transposed(grad_attn, proj_out).astype(BF16)
    grad_queries_t, grad_keys, grad_values, cells, diag = attention_backward(
        queries, keys, values, grad_context, probs, ops
    )
    table_grad = table_grads(cells, diag)
    grad_mixed = jnp.concatenate([grad_queries_t.T, grad_keys, grad_values], axis=1)
    grad_proj_qkv = rows_inner(start_low, grad_mixed)
    summed = jnp.sum(grad_mixed.astype(F32), axis=0)
    grad_qv_bias = jnp.stack([summed[:D], summed[2 * D :]])
    grad_start = grad_first + times_transposed(grad_mixed, proj_qkv)
    grad_start_low = grad_start.astype(BF16)
    grad_hidden = to_positions(grad_start_low.reshape(1, WINLEN, D))
    grad_proj_box = rows_inner(features, grad_start_low)
    grad_list = (
        grad_proj_qkv,
        grad_proj_out,
        grad_proj_box,
        grad_proj_in,
        grad_proj_back,
        grad_qv_bias,
        grad_out_bias,
        grad_norm_one,
        grad_in_bias,
        grad_back_bias,
        grad_norm_two,
        table_grad,
    )
    padding = jnp.zeros((shard_len * groups * lax.axis_size("dp") - USED,), BF16)
    grads_flat = jnp.concatenate([piece.astype(BF16).reshape(-1) for piece in grad_list] + [padding])
    grad_share = lax.psum_scatter(
        grads_flat, ("dp", "head"), scatter_dimension=0, tiled=True
    ).astype(F32)
    return finish_step(output_low, grad_hidden, grad_share, params, moment_one, moment_two)


def solution(mesh):
    placed = (
        P("dp", "head", None),
        P("dp", "head", None),
        P("dp", None, None),
        P("dp", None),
        P(("dp", "head")),
        P(("dp", "head")),
        P(("dp", "head")),
    )
    return jax.shard_map(
        fast_shards if fits(mesh) else plain_shards,
        mesh=mesh,
        in_specs=placed,
        out_specs=(
            P("dp", "head", None),
            P("dp", "head", None),
            P(("dp", "head")),
            P(("dp", "head")),
            P(("dp", "head")),
        ),
        check_vma=False,
    )
```
